32 devices in a mesh: gx: 4 (over y, x), gy: 2 (over core), gz: 4 (over z).
Axes of the slice: x: 2, y: 2, z: 4, core: 2. Of those that a mesh axis runs over, the one named last changes fastest.
Arguments:
- activations: bfloat16 [64, 32, 16, 512], P(None, 'gx', 'gy', 'gz'), may hold values from -6 to 6
- preact: bfloat16 [64, 32, 16, 512], P(None, 'gx', 'gy', 'gz'), may hold values from -6 to 6
- upstream: bfloat16 [64, 32, 16, 512], P(None, 'gx', 'gy', 'gz'), may hold values from -6 to 6
- master: float32 [110592], P(('gx', 'gy', 'gz')), may hold values from -0.15625 to 0.15625
- first_moment: float32 [110592], P(('gx', 'gy', 'gz')), may hold values from -4 to 4
- second_moment: float32 [110592], P(('gx', 'gy', 'gz')), may hold values from 0.05 to 2
Outputs:
- grad_input: bfloat16 [64, 32, 16, 512], P(None, 'gx', 'gy', 'gz')
- weight_grad: float32 [110592], P(('gx', 'gy', 'gz'))
- new_master: float32 [110592], P(('gx', 'gy', 'gz'))
- new_first: float32 [110592], P(('gx', 'gy', 'gz'))
- new_second: float32 [110592], P(('gx', 'gy', 'gz'))
The draws below stay inside these ranges and needn't reach their ends.
All inputs are finite; a program needn't handle non-finite values.
Results may differ from the reference program's by a relative error of at most 0.0049.
Values may be sent and summed in bfloat16 or wider, within the bound.
No kernel may reach another device: no remote copies, remote signals or barrier semaphores. Data moves between devices by JAX's collectives and lax.ppermute only.
A program may use at most 64 MiB of HBM per device.

```python
import math
import jax
import jax.numpy as jnp
from jax import lax

C = 64
NX = 32
NY = 16
NZ = 512
PARAMS = 110592


def level_of(key, shape, cuts, low, high):
    def one(position, parts):
        draws = jax.random.uniform(jax.random.fold_in(jax.random.fold_in(key, 6), position), (parts,), jnp.float32, low / len(cuts), high / len(cuts))
        return jnp.repeat(jnp.exp(draws), shape[position] // parts).reshape((-1,) + (1,) * (len(shape) - position - 1))

    gain = one(*cuts[0])
    for cut in cuts[1:]:
        gain = gain * one(*cut)
    return gain


def noise(rng, shape, spread, most, pieces=(), held_as=jnp.bfloat16):
    result = spread * jax.random.normal(rng, shape, jnp.float32)
    if pieces:
        result = result * level_of(rng, shape, pieces, -0.22, 0.18)
    return jnp.clip(result, -most, most).astype(held_as)


def setup_inputs(seed: int = 0) -> dict:
    splits = jax.random.split(jax.random.key(seed), 7)
    activations = noise(splits[0], (C, NX, NY, NZ), 1.0, 6.0, ((1, 4), (2, 2), (3, 4)))
    preact = noise(splits[1], (C, NX, NY, NZ), 1.0, 6.0, ((1, 4), (2, 2), (3, 4)))
    upstream = noise(splits[2], (C, NX, NY, NZ), 1.0, 6.0, ((1, 4), (2, 2), (3, 4)))
    master = noise(splits[3], (PARAMS,), (C * 27) ** -0.5, 0.15625, ((0, 32),), jnp.float32)
    first_moment = noise(splits[4], (PARAMS,), 0.5, 4.0, ((0, 32),), jnp.float32)
    second_moment = jnp.clip(jnp.exp(math.log(2.0) - 3.6888794 * jax.random.uniform(splits[5], (PARAMS,), jnp.float32) ** level_of(splits[5], (PARAMS,), ((0, 32),), -0.2, 0.2)), 0.05, 2.0)
    return dict(activations=activations, preact=preact, upstream=upstream, master=master, first_moment=first_moment, second_moment=second_moment)


def reference(activations, preact, upstream, master, first_moment, second_moment):
    pre_grad = jnp.where(preact > 0, upstream, jnp.zeros_like(upstream))
    kernel = master.astype(jnp.bfloat16).reshape(C, C, 27).astype(jnp.float32)
    widths = ((0, 0), (1, 1), (1, 1), (1, 1))
    padded_grad = jnp.pad(pre_grad, widths)
    padded_input = jnp.pad(activations, widths)

    def plane_step(carry, index):
        grad_slab = lax.dynamic_slice_in_dim(padded_grad, index, 3, 1).astype(jnp.float32)
        input_slab = lax.dynamic_slice_in_dim(padded_input, index, 3, 1).astype(jnp.float32)
        center = lax.dynamic_slice_in_dim(pre_grad, index, 1, 1)[:, 0].astype(jnp.float32)
        plane = jnp.zeros((C, NY, NZ), jnp.float32)
        taps = []
        for shift_x in range(3):
            for shift_y in range(3):
                for shift_z in range(3):
                    tap = shift_x * 9 + shift_y * 3 + shift_z
                    source = grad_slab[:, 2 - shift_x, 2 - shift_y:2 - shift_y + NY, 2 - shift_z:2 - shift_z + NZ]
                    plane = plane + jnp.einsum('oi,oyz->iyz', kernel[:, :, tap], source)
                    window = input_slab[:, shift_x, shift_y:shift_y + NY, shift_z:shift_z + NZ]
                    taps.append(jnp.einsum('oyz,iyz->oi', center, window))
        return (carry + jnp.stack(taps, axis=-1), plane)
    start = jnp.zeros((C, C, 27), jnp.float32)
    total, planes = lax.scan(plane_step, start, jnp.arange(NX, dtype=jnp.int32))
    grad_input = jnp.transpose(planes, (1, 0, 2, 3)).astype(jnp.bfloat16)
    weight_grad = total.reshape(-1) / jnp.sqrt(jnp.float32(NX * NY * NZ))
    new_first = 0.9 * first_moment + 0.1 * weight_grad
    new_second = 0.999 * second_moment + 0.001 * weight_grad * weight_grad
    corr_first = 1.0 - (0.9 ** 10) ** 10
    corr_second = 1.0 - (0.999 ** 10) ** 10
    update = new_first / corr_first / (jnp.sqrt(new_second / corr_second) + 1e-08) + 0.01 * master
    new_master = master - 0.05 * update
    return (grad_input, weight_grad, new_master, new_first, new_second)
```

```python
import math

import jax
import jax.numpy as jnp
from jax import lax
from jax.sharding import PartitionSpec as P

AXES = ("gx", "gy", "gz")


def padded_2(block, sides, width):
    for axis, dim in sides:
        count = lax.axis_size(axis)
        forward = [(i, i + 1) for i in range(count - 1)]
        backward = [(target, source) for source, target in forward]
        low = lax.ppermute(
            lax.slice_in_dim(block, block.shape[dim] - width, None, axis=dim), axis, forward
        )
        high = lax.ppermute(lax.slice_in_dim(block, 0, width, axis=dim), axis, backward)
        block = jnp.concatenate([low, block, high], axis=dim)
    return block


def local(activations, preact, upstream, master, first_moment, second_moment):
    channels = activations.shape[0]
    size_x, size_y, size_z = activations.shape[1:]
    devices = math.prod(lax.axis_size(a) for a in AXES)
    share = master.shape[0]
    sent = jnp.broadcast_to(master.astype(jnp.bfloat16)[None], (devices, share))
    kernel_flat = lax.all_to_all(sent, AXES, 0, 0, tiled=True)
    pre_grad = jnp.where(preact > 0, upstream, jnp.zeros_like(upstream))
    padded_grad = padded_2(pre_grad, (("gx", 1), ("gy", 2), ("gz", 3)), 1)
    tap_terms = []
    for shift_x in range(3):
        for shift_y in range(3):
            for shift_z in range(3):
                window = padded_grad[
                    :,
                    2 - shift_x : 2 - shift_x + size_x,
                    2 - shift_y : 2 - shift_y + size_y,
                    2 - shift_z : 2 - shift_z + size_z,
                ]
                tap_terms.append(
                    lax.dot_general(
                        window,
                        activations,
                        (((1, 2, 3), (1, 2, 3)), ((), ())),
                        preferred_element_type=jnp.float32,
                    )
                )
    voxels = size_x * size_y * size_z * devices
    partial = (jnp.stack(tap_terms, axis=-1) / math.sqrt(voxels)).astype(jnp.bfloat16)
    parts = lax.all_to_all(partial.reshape(devices, share), AXES, 0, 0, tiled=True)
    weight_grad = jnp.sum(parts.astype(jnp.float32), axis=0)
    kernel = kernel_flat.reshape(channels, channels, 3, 3, 3)
    flipped = jnp.transpose(kernel, (1, 0, 2, 3, 4))[:, :, ::-1, ::-1, ::-1]
    conv_out = lax.conv_general_dilated(
        padded_grad[None],
        flipped,
        (1, 1, 1),
        "VALID",
        dimension_numbers=("NCDHW", "OIDHW", "NCDHW"),
        preferred_element_type=jnp.float32,
    )
    grad_input = conv_out[0].astype(jnp.bfloat16)
    new_first = 0.9 * first_moment + 0.1 * weight_grad
    new_second = 0.999 * second_moment + 0.001 * weight_grad * weight_grad
    corr_first = 1.0 - (0.9**10) ** 10
    corr_second = 1.0 - (0.999**10) ** 10
    update = new_first / corr_first / (jnp.sqrt(new_second / corr_second) + 1e-08) + 0.01 * master
    new_master = master - 0.05 * update
    return (grad_input, weight_grad, new_master, new_first, new_second)


def solution(mesh):
    volume = P(None, "gx", "gy", "gz")
    flat = P(AXES)
    return jax.shard_map(
        local,
        mesh=mesh,
        in_specs=(volume, volume, volume, flat, flat, flat),
        out_specs=(volume, flat, flat, flat, flat),
        check_vma=False,
    )
```

```python
import functools
import math

import jax
import jax.numpy as jnp
from jax import lax
from jax.experimental import pallas as pl
from jax.experimental.pallas import tpu as pltpu
from jax.sharding import PartitionSpec as P

AXES = ("gx", "gy", "gz")
LANES = 128
VMEM = pl.BlockSpec(memory_space=pltpu.VMEM)
F32 = jnp.float32
BF16 = jnp.bfloat16


def params(mib=40):
    return pltpu.CompilerParams(vmem_limit_bytes=mib * 2**20)


def prep_kernel(both, p_ref, u_ref, g_ref, xlo_ref, xhi_ref, *refs):
    outs, scratch = refs[:-1], refs[-1]
    step = pl.program_id(0)
    channels, _, size_y, size_z = p_ref.shape
    grad = jnp.where(p_ref[:, 0] > 0, u_ref[:, 0], jnp.zeros_like(u_ref[:, 0]))
    scratch[...] = grad.astype(F32).reshape(channels * size_y, size_z)
    rows = [scratch[pl.ds(y, channels, stride=size_y), :].astype(BF16) for y in range(size_y)]
    for y in range(size_y):
        g_ref[0, :, y * size_z : (y + 1) * size_z] = rows[y]
    if both:
        faces = (rows[0], rows[-1])
    else:
        first = lax.axis_index("gy") == 0
        faces = (jnp.where(first, rows[-1].astype(F32), rows[0].astype(F32)).astype(BF16),)
    for face, (face_ref, low_ref, high_ref) in zip(
        faces, (outs[3 * k : 3 * k + 3] for k in range(len(faces)))
    ):
        face_ref[0] = face

        @pl.when(step == 0)
        def _():
            low_ref[...] = face

        @pl.when(step == pl.num_programs(0) - 1)
        def _():
            high_ref[...] = face

    @pl.when(step == 0)
    def _():
        xlo_ref[...] = g_ref[0]

    @pl.when(step == pl.num_programs(0) - 1)
    def _():
        xhi_ref[...] = g_ref[0]


def prep(preact, upstream, both):
    channels, size_x, size_y, size_z = preact.shape
    plane = size_y * size_z
    block = pl.BlockSpec((channels, 1, size_y, size_z), lambda x: (0, x, 0, 0))
    out_shape = [
        jax.ShapeDtypeStruct((size_x, channels, plane), BF16),
        jax.ShapeDtypeStruct((channels, plane), BF16),
        jax.ShapeDtypeStruct((channels, plane), BF16),
    ]
    out_specs = [
        pl.BlockSpec((1, channels, plane), lambda x: (x, 0, 0)),
        pl.BlockSpec((channels, plane), lambda x: (0, 0)),
        pl.BlockSpec((channels, plane), lambda x: (0, 0)),
    ]
    for _ in range(2 if both else 1):
        out_shape += [
            jax.ShapeDtypeStruct((size_x, channels, size_z), BF16),
            jax.ShapeDtypeStruct((channels, size_z), BF16),
            jax.ShapeDtypeStruct((channels, size_z), BF16),
        ]
        out_specs += [
            pl.BlockSpec((1, channels, size_z), lambda x: (x, 0, 0)),
            pl.BlockSpec((channels, size_z), lambda x: (0, 0)),
            pl.BlockSpec((channels, size_z), lambda x: (0, 0)),
        ]
    return pl.pallas_call(
        functools.partial(prep_kernel, both),
        grid=(size_x,),
        in_specs=[block, block],
        out_specs=out_specs,
        out_shape=out_shape,
        scratch_shapes=[pltpu.VMEM((channels * size_y, size_z), F32)],
        compiler_params=params(),
        name="prep",
    )(preact, upstream)


def y_masks():
    me = lax.axis_index("gy")
    return me > 0, me < lax.axis_size("gy") - 1


def masked(keep, value):
    return jnp.where(keep, value.astype(F32), 0.0).astype(BF16)


def extended_plane(index, size_x, masks, g_ref, xlo_ref, xhi_ref, y_refs, edge_refs):
    if index == 0:
        body, low, high = xlo_ref[...], edge_refs[0][...], edge_refs[1][...]
    elif index == size_x + 1:
        body, low, high = xhi_ref[...], edge_refs[2][...], edge_refs[3][...]
    else:
        body, low, high = g_ref[index - 1], y_refs[0][index - 1], y_refs[1][index - 1]
    return masked(masks[0], low), body, masked(masks[1], high)


def pack_kernel(g_ref, xlo_ref, xhi_ref, ylo_ref, yhi_ref, e0, e1, e2, e3, *refs):
    ext_ref, zlo_ref, zhi_ref = refs
    size_x, channels, plane = g_ref.shape
    size_z = ylo_ref.shape[-1]
    rows_y = plane // size_z + 2
    masks = y_masks()
    for index in range(size_x + 2):
        low, body, high = extended_plane(
            index, size_x, masks, g_ref, xlo_ref, xhi_ref, (ylo_ref, yhi_ref), (e0, e1, e2, e3)
        )
        ext_ref[index, :, :size_z] = low
        ext_ref[index, :, size_z : size_z + plane] = body
        ext_ref[index, :, size_z + plane :] = high
    voxel = lax.broadcasted_iota(jnp.int32, (rows_y * size_z, 2 * LANES), 0)
    lane = lax.broadcasted_iota(jnp.int32, (rows_y * size_z, 2 * LANES), 1)
    wanted = jnp.where(lane < LANES, lane * size_z, (lane - LANES) * size_z + size_z - 1)
    pick = (voxel == wanted).astype(F32).astype(BF16)
    columns = jnp.dot(
        ext_ref[...].reshape((size_x + 2) * channels, rows_y * size_z),
        pick,
        preferred_element_type=F32,
    )
    zlo = jnp.zeros((channels, LANES), F32)
    zhi = jnp.zeros((channels, LANES), F32)
    for index in range(size_x + 2):
        rows = columns[index * channels : (index + 1) * channels]
        zlo = zlo + pltpu.roll(rows[:, :LANES], index * rows_y, 1)
        zhi = zhi + pltpu.roll(rows[:, LANES:], index * rows_y, 1)
    zlo_ref[...] = zlo.astype(BF16)
    zhi_ref[...] = zhi.astype(BF16)


def pack(g, x_halos, y_halos, edges):
    size_x, channels, plane = g.shape
    size_z = y_halos[0].shape[-1]
    ext = jax.ShapeDtypeStruct((size_x + 2, channels, plane + 2 * size_z), BF16)
    face = jax.ShapeDtypeStruct((channels, LANES), BF16)
    return pl.pallas_call(
        pack_kernel,
        in_specs=[VMEM] * 9,
        out_specs=[VMEM] * 3,
        out_shape=[ext, face, face],
        compiler_params=params(),
        name="pack",
    )(g, *x_halos, *y_halos, *edges)


def wgrad_kernel(scale, ext_ref, zlo_ref, zhi_ref, act_ref, g3_ref, part_ref, x3, acc, tile, flat):
    planes, channels, ext = ext_ref.shape
    size_x, size_y, size_z = act_ref.shape[1:]
    rows_y = size_y + 2
    group = 3 * channels
    low, high = zlo_ref[...].astype(F32), zhi_ref[...].astype(F32)
    turned = []
    for index in range(planes):
        shift = (LANES - index * rows_y) % LANES
        turned.append(
            jnp.concatenate([pltpu.roll(low, shift, 1), pltpu.roll(high, shift, 1)], axis=1)
        )
    source = lax.broadcasted_iota(jnp.int32, (2 * LANES, ext), 0)
    voxel = lax.broadcasted_iota(jnp.int32, (2 * LANES, ext), 1)
    place = jnp.where(source < LANES, source * size_z, (source - LANES) * size_z + size_z - 1)
    place = jnp.where(source % LANES < rows_y, place, -1)
    put = (voxel == place).astype(F32).astype(BF16)
    halo = jnp.dot(
        jnp.concatenate(turned, axis=0).astype(BF16), put, preferred_element_type=F32
    )
    lane = lax.broadcasted_iota(jnp.int32, (channels, size_z), 1)
    for index in range(planes):
        base = index * group
        for row in range(rows_y):
            cols = slice(row * size_z, (row + 1) * size_z)
            value = ext_ref[index, :, cols]
            wide = value.astype(F32)
            edge = halo[index * channels : (index + 1) * channels, cols]
            before = jnp.where(lane == 0, edge, pltpu.roll(wide, 1, 1))
            after = jnp.where(lane == size_z - 1, edge, pltpu.roll(wide, size_z - 1, 1))
            g3_ref[base : base + channels, cols] = before.astype(BF16)
            g3_ref[base + channels : base + 2 * channels, cols] = value
            g3_ref[base + 2 * channels : base + group, cols] = after.astype(BF16)
    zero = jnp.zeros((channels, size_z), BF16)
    for x in range(size_x):
        tile[...] = act_ref[:, x].astype(F32).reshape(channels * size_y, size_z)
        for y in range(size_y):
            value = tile[pl.ds(y, channels, stride=size_y), :].astype(BF16)
            for b in range(3):
                row = y + 2 - b
                x3[x, b * channels : (b + 1) * channels, row * size_z : (row + 1) * size_z] = value
        for b, row in ((0, 0), (0, 1), (1, 0), (1, rows_y - 1), (2, rows_y - 2), (2, rows_y - 1)):
            x3[x, b * channels : (b + 1) * channels, row * size_z : (row + 1) * size_z] = zero
    for x in range(size_x):
        product = lax.dot_general(
            g3_ref[x * group : (x + 3) * group, :],
            x3[x],
            (((1,), (1,)), ((), ())),
            preferred_element_type=F32,
        )
        if x == 0:
            acc[...] = product
        else:
            acc[...] += product
    wide = jnp.concatenate([acc[...] * scale, jnp.zeros((channels, group), F32)], axis=0)
    turned = jnp.concatenate(
        [wide, jnp.zeros((wide.shape[0], -group % LANES), F32)], axis=1
    ).T
    for b in range(3):
        rows = turned[b * channels : (b + 1) * channels]
        for pair in range(5):
            cell = rows[:, pair * LANES : (pair + 1) * LANES]
            for half in range(2):
                block = 2 * pair + half
                if block < 9:
                    tap = (2 - block // 3) * 9 + b * 3 + 2 - block % 3
                    moved = cell if half == 0 else pltpu.roll(cell, LANES - channels, 1)
                    flat[pl.ds(tap, channels, stride=27), :] = moved
    part_ref[...] = flat[...].T[:channels, : part_ref.shape[1]].astype(BF16)


def wgrad(ext, zlo, zhi, activations, scale):
    channels, size_x, size_y, size_z = activations.shape
    width = (size_y + 2) * size_z
    taps = 27 * channels
    flops = 2 * 9 * channels * 3 * channels * size_x * width
    return pl.pallas_call(
        functools.partial(wgrad_kernel, scale),
        in_specs=[VMEM] * 4,
        out_specs=[VMEM] * 2,
        out_shape=[
            jax.ShapeDtypeStruct(((size_x + 2) * 3 * channels, width), BF16),
            jax.ShapeDtypeStruct((channels, taps), BF16),
        ],
        scratch_shapes=[
            pltpu.VMEM((size_x, 3 * channels, width), BF16),
            pltpu.VMEM((9 * channels, 3 * channels), F32),
            pltpu.VMEM((channels * size_y, size_z), F32),
            pltpu.VMEM((-(-taps // LANES) * LANES, LANES), F32),
        ],
        compiler_params=params(),
        cost_estimate=pl.CostEstimate(
            flops=flops, bytes_accessed=8 * 2**20, transcendentals=0
        ),
        name="wgrad",
    )(ext, zlo, zhi, activations)


def dgrad_kernel(size_y, w_ref, g3_ref, out_ref, turned, weights, tile):
    channels, size_x, _, size_z = out_ref.shape
    group = 3 * channels
    plane = size_y * size_z
    taps = w_ref.shape[1]
    wide = w_ref[...].astype(F32)
    wide = jnp.concatenate([wide, jnp.zeros((LANES - channels, taps), F32)], axis=0)
    wide = jnp.concatenate([wide, jnp.zeros((LANES, -taps % LANES), F32)], axis=1)
    turned[...] = wide.T
    for b in range(3):
        blocks = []
        for a in range(3):
            for c in range(3):
                tap = (2 - a) * 9 + (2 - b) * 3 + 2 - c
                blocks.append(turned[pl.ds(tap, channels, stride=27), :][:, :channels])
        zero = jnp.zeros((channels, group), F32)
        weights[b, :channels] = jnp.concatenate(blocks + [zero], axis=1).astype(BF16)
        weights[b, channels:] = jnp.concatenate([zero] + blocks, axis=1).astype(BF16)
    for pair in range(size_x // 2):
        rows = slice(2 * pair * group, (2 * pair + 4) * group)
        total = None
        for b in range(3):
            product = jnp.dot(
                weights[b],
                g3_ref[rows, b * size_z : b * size_z + plane],
                preferred_element_type=F32,
            )
            total = product if total is None else total + product
        for half in range(2):
            for y in range(size_y):
                tile[pl.ds(y, channels, stride=size_y), :] = total[
                    half * channels : (half + 1) * channels, y * size_z : (y + 1) * size_z
                ]
            out_ref[:, 2 * pair + half] = (
                tile[...].reshape(channels, size_y, size_z).astype(BF16)
            )


def dgrad(kernel, g3, shape):
    channels, size_x, size_y, size_z = shape
    taps = kernel.shape[1]
    flops = 2 * 12 * channels * 3 * channels * size_x * size_y * size_z
    return pl.pallas_call(
        functools.partial(dgrad_kernel, size_y),
        in_specs=[VMEM] * 2,
        out_specs=VMEM,
        out_shape=jax.ShapeDtypeStruct(shape, BF16),
        scratch_shapes=[
            pltpu.VMEM((-(-taps // LANES) * LANES, LANES), F32),
            pltpu.VMEM((3, 2 * channels, 12 * channels), BF16),
            pltpu.VMEM((channels * size_y, size_z), F32),
        ],
        compiler_params=params(),
        cost_estimate=pl.CostEstimate(
            flops=flops, bytes_accessed=8 * 2**20, transcendentals=0
        ),
        name="dgrad",
    )(kernel, g3)


def shifted(value, moves):
    names = tuple(moves)
    sizes = [lax.axis_size(name) for name in names]
    pairs = []
    for source in range(math.prod(sizes)):
        rest, coords = source, []
        for size in reversed(sizes):
            coords.insert(0, rest % size)
            rest //= size
        coords = [
            (at + moves[name]) if moves[name] != "swap" else 1 - at
            for at, name in zip(coords, names)
        ]
        if all(0 <= at < size for at, size in zip(coords, sizes)):
            target = 0
            for at, size in zip(coords, sizes):
                target = target * size + at
            pairs.append((source, target))
    return lax.ppermute(value, names if len(names) > 1 else names[0], pairs)


def local(activations, preact, upstream, master, first_moment, second_moment):
    channels, size_x, size_y, size_z = activations.shape
    devices = math.prod(lax.axis_size(a) for a in AXES)
    share = master.shape[0]
    taps = 27 * channels
    span = min(share, taps)
    sent = jnp.broadcast_to(
        master.astype(BF16).reshape(1, share // span, span), (devices, share // span, span)
    )
    kernel = lax.all_to_all(sent, AXES, 0, 0, tiled=True).reshape(channels, taps)

    both = lax.axis_size("gy") != 2
    g, xlo, xhi, *faces = prep(preact, upstream, both)
    if both:
        y_halos = (shifted(faces[3], {"gy": 1}), shifted(faces[0], {"gy": -1}))
        edges = (
            shifted(faces[5], {"gx": 1, "gy": 1}),
            shifted(faces[2], {"gx": 1, "gy": -1}),
            shifted(faces[4], {"gx": -1, "gy": 1}),
            shifted(faces[1], {"gx": -1, "gy": -1}),
        )
    else:
        y_halos = (shifted(faces[0], {"gy": "swap"}),) * 2
        edges = (shifted(faces[2], {"gx": 1, "gy": "swap"}),) * 2
        edges += (shifted(faces[1], {"gx": -1, "gy": "swap"}),) * 2
    x_halos = (shifted(xhi, {"gx": 1}), shifted(xlo, {"gx": -1}))
    ext, zlo, zhi = pack(g, x_halos, y_halos, edges)
    zlo, zhi = shifted(zhi, {"gz": 1}), shifted(zlo, {"gz": -1})

    voxels = size_x * size_y * size_z * devices
    g3, part = wgrad(ext, zlo, zhi, activations, 1.0 / math.sqrt(voxels))
    parts = lax.all_to_all(
        part.reshape(devices, share // span, span), AXES, 0, 0, tiled=True
    )
    grad_input = dgrad(kernel, g3, activations.shape)
    weight_grad = jnp.sum(parts.astype(F32), axis=0).reshape(share)
    new_first = 0.9 * first_moment + 0.1 * weight_grad
    new_second = 0.999 * second_moment + 0.001 * weight_grad * weight_grad
    corr_first = 1.0 - (0.9**10) ** 10
    corr_second = 1.0 - (0.999**10) ** 10
    update = new_first / corr_first / (jnp.sqrt(new_second / corr_second) + 1e-08) + 0.01 * master
    new_master = master - 0.05 * update
    return (grad_input, weight_grad, new_master, new_first, new_second)


def solution(mesh):
    volume = P(None, "gx", "gy", "gz")
    flat = P(AXES)
    return jax.shard_map(
        local,
        mesh=mesh,
        in_specs=(volume, volume, volume, flat, flat, flat),
        out_specs=(volume, flat, flat, flat, flat),
        check_vma=False,
    )
```

```python
import functools
import math

import jax
import jax.numpy as jnp
from jax import lax
from jax.experimental import pallas as pl
from jax.experimental.pallas import tpu as pltpu
from jax.sharding import PartitionSpec as P

AXES = ("gx", "gy", "gz")
LANES = 128
VMEM = pl.BlockSpec(memory_space=pltpu.VMEM)
HBM = pl.BlockSpec(memory_space=pltpu.HBM)
F32 = jnp.float32
BF16 = jnp.bfloat16


def params(mib=24):
    return pltpu.CompilerParams(vmem_limit_bytes=mib * 2**20)


def masked_plane(p, u, tile, write):
    channels, size_y, size_z = p.shape
    tile[...] = jnp.where(p > 0, u, jnp.zeros_like(u)).astype(F32).reshape(-1, size_z)
    for y in range(size_y):
        write(y, tile[pl.ds(y, channels, stride=size_y), :].astype(BF16))


def face_kernel(p_ref, u_ref, m_ref, low_ref, high_ref, sent_ref, p_buf, u_buf, tile, sems):
    size_x, size_z = p_ref.shape[1], p_ref.shape[3]
    copies = []
    for k, x in enumerate((0, size_x - 1)):
        pair = (
            pltpu.make_async_copy(p_ref.at[:, x], p_buf.at[k], sems.at[2 * k]),
            pltpu.make_async_copy(u_ref.at[:, x], u_buf.at[k], sems.at[2 * k + 1]),
        )
        for copy in pair:
            copy.start()
        copies.append(pair)
    sent_ref[...] = jnp.broadcast_to(m_ref[...].astype(BF16)[None], sent_ref.shape)
    for k, out_ref in enumerate((low_ref, high_ref)):
        for copy in copies[k]:
            copy.wait()

        def write(y, value):
            out_ref[:, y * size_z : (y + 1) * size_z] = value

        masked_plane(p_buf[k], u_buf[k], tile.at[k], write)


def faces(preact, upstream, share, devices):
    channels, size_x, size_y, size_z = preact.shape
    face = jax.ShapeDtypeStruct((channels, size_y * size_z), BF16)
    buffer = pltpu.VMEM((2, channels, size_y, size_z), BF16)
    return pl.pallas_call(
        face_kernel,
        in_specs=[HBM, HBM, VMEM],
        out_specs=[VMEM] * 3,
        out_shape=[face, face, jax.ShapeDtypeStruct((devices, *share.shape), BF16)],
        scratch_shapes=[
            buffer,
            buffer,
            pltpu.VMEM((2, channels * size_y, size_z), F32),
            pltpu.SemaphoreType.DMA((4,)),
        ],
        compiler_params=params(),
        name="faces",
    )(preact, upstream, share)


def inner_kernel(p_ref, u_ref, a_ref, g_ref, x3_ref, p_buf, u_buf, a_buf, tile, sems):
    channels, size_x, size_y, size_z = a_ref.shape
    inner = size_x - 2
    copies = []
    for x in range(inner):
        copies.append(
            (
                pltpu.make_async_copy(p_ref.at[:, x + 1], p_buf.at[x], sems.at[x]),
                pltpu.make_async_copy(u_ref.at[:, x + 1], u_buf.at[x], sems.at[inner + x]),
            )
        )
    for x in range(size_x):
        copies.append(
            (pltpu.make_async_copy(a_ref.at[:, x], a_buf.at[x], sems.at[2 * inner + x]),)
        )
    for group in copies:
        for copy in group:
            copy.start()
    for x in range(inner):
        for copy in copies[x]:
            copy.wait()

        def write(y, value):
            g_ref[x, :, y * size_z : (y + 1) * size_z] = value

        masked_plane(p_buf[x], u_buf[x], tile.at[x % 2], write)
    zero = jnp.zeros((channels, size_z), BF16)
    last = size_y + 1
    for x in range(size_x):
        copies[inner + x][0].wait()
        tile[x % 2] = a_buf[x].astype(F32).reshape(channels * size_y, size_z)
        for y in range(size_y):
            value = tile[x % 2, pl.ds(y, channels, stride=size_y), :].astype(BF16)
            for b in range(3):
                row = y + 2 - b
                x3_ref[x, b * channels : (b + 1) * channels, row * size_z : (row + 1) * size_z] = value
        for b, row in ((0, 0), (0, 1), (1, 0), (1, last), (2, last - 1), (2, last)):
            x3_ref[x, b * channels : (b + 1) * channels, row * size_z : (row + 1) * size_z] = zero


def inner_planes(preact, upstream, activations):
    channels, size_x, size_y, size_z = preact.shape
    plane = size_y * size_z
    return pl.pallas_call(
        inner_kernel,
        in_specs=[HBM] * 3,
        out_specs=[VMEM] * 2,
        out_shape=[
            jax.ShapeDtypeStruct((size_x - 2, channels, plane), BF16),
            jax.ShapeDtypeStruct((size_x, 3 * channels, plane + 2 * size_z), BF16),
        ],
        scratch_shapes=[
            pltpu.VMEM((size_x - 2, channels, size_y, size_z), BF16),
            pltpu.VMEM((size_x - 2, channels, size_y, size_z), BF16),
            pltpu.VMEM((size_x, channels, size_y, size_z), BF16),
            pltpu.VMEM((2, channels * size_y, size_z), F32),
            pltpu.SemaphoreType.DMA((3 * size_x - 4,)),
        ],
        compiler_params=params(),
        cost_estimate=pl.CostEstimate(flops=0, bytes_accessed=10 * 2**20, transcendentals=0),
        name="inner",
    )(preact, upstream, activations)


def pack_kernel(both, spots, xlo_ref, first_ref, g_ref, last_ref, xhi_ref, *refs):
    y_refs, tiles_ref = refs[:-1], refs[-1]
    inner, channels, plane = g_ref.shape
    size_z = y_refs[0].shape[-1]
    size_y = plane // size_z
    planes = [xlo_ref[...], first_ref[...]]
    planes += [g_ref[x] for x in range(inner)]
    planes += [last_ref[...], xhi_ref[...]]
    is_first = lax.axis_index("gy") == 0
    for index, value in enumerate(planes):
        low, high = value[:, :size_z], value[:, plane - size_z :]
        if both:
            y_refs[0][index] = low
            y_refs[1][index] = high
        else:
            y_refs[0][index] = jnp.where(
                is_first, high.astype(F32), low.astype(F32)
            ).astype(BF16)
    voxel = lax.broadcasted_iota(jnp.int32, (plane, 2 * LANES), 0)
    lane = lax.broadcasted_iota(jnp.int32, (plane, 2 * LANES), 1)
    wanted = jnp.where(lane < LANES, lane * size_z, (lane - LANES) * size_z + size_z - 1)
    pick = (voxel == wanted).astype(F32).astype(BF16)
    columns = jnp.dot(
        jnp.concatenate(planes, axis=0), pick, preferred_element_type=F32
    )
    zlo = jnp.zeros((channels, LANES), F32)
    zhi = jnp.zeros((channels, LANES), F32)
    for index in range(len(planes)):
        rows = columns[index * channels : (index + 1) * channels]
        zlo = zlo + pltpu.roll(rows[:, :LANES], index * size_y, 1)
        zhi = zhi + pltpu.roll(rows[:, LANES:], index * size_y, 1)
    me = lax.axis_index("gz")
    zlo, zhi = zlo.astype(BF16), zhi.astype(BF16)
    for spot in range(spots[0] * spots[1]):
        at = spot % spots[1]

        @pl.when(at > me)
        def _():
            tiles_ref[spot] = zhi

        @pl.when(at <= me)
        def _():
            tiles_ref[spot] = zlo


def pack(planes, size_z, both):
    inner, channels, plane = planes[2].shape
    spots = (lax.axis_size("gy"), lax.axis_size("gz"))
    count = 2 if both else 1
    face = jax.ShapeDtypeStruct((inner + 4, channels, size_z), BF16)
    tiles = jax.ShapeDtypeStruct((spots[0] * spots[1], channels, LANES), BF16)
    return pl.pallas_call(
        functools.partial(pack_kernel, both, spots),
        in_specs=[VMEM] * 5,
        out_specs=[VMEM] * (count + 1),
        out_shape=[face] * count + [tiles],
        compiler_params=params(),
        name="pack",
    )(*planes)


def z_columns(tiles_ref, spots, planes, size_y, side):
    me_y, me_z = lax.axis_index("gy"), lax.axis_index("gz")
    at_z = jnp.clip(me_z + side, 0, spots[1] - 1)
    inside = (me_z + side >= 0) & (me_z + side < spots[1])
    found = []
    for move in (-1, 0, 1):
        at_y = jnp.clip(me_y + move, 0, spots[0] - 1)
        keep = inside & (me_y + move >= 0) & (me_y + move < spots[0])
        found.append(jnp.where(keep, tiles_ref[at_y * spots[1] + at_z].astype(F32), 0.0))
    lane = lax.broadcasted_iota(jnp.int32, found[0].shape, 1)
    columns = []
    for index in range(planes):
        start = index * size_y
        before = pltpu.roll(found[0], (size_y - (start + size_y - 1)) % LANES, 1)
        own = pltpu.roll(found[1], -start % LANES, 1)
        after = pltpu.roll(found[2], (size_y + 1 - start) % LANES, 1)
        value = jnp.where(lane < size_y, own, jnp.where(lane == size_y, before, after))
        columns.append(jnp.where(lane < size_y + 2, value, 0.0))
    return columns


def wgrad_kernel(scale, spots, *refs):
    xlo_ref, first_ref, g_ref, last_ref, xhi_ref, ylo_ref, yhi_ref, tiles_ref, x3_ref = refs[:9]
    g3_ref, part_ref, acc, flat = refs[9:]
    inner, channels, plane = g_ref.shape
    planes, size_x = inner + 4, inner + 2
    size_z = ylo_ref.shape[-1]
    size_y = plane // size_z
    rows_y = size_y + 2
    ext = rows_y * size_z
    group = 3 * channels
    low = z_columns(tiles_ref, spots, planes, size_y, -1)
    high = z_columns(tiles_ref, spots, planes, size_y, 1)
    columns = jnp.concatenate(
        [jnp.concatenate(pair, axis=1) for pair in zip(low, high)], axis=0
    ).astype(BF16)
    source = lax.broadcasted_iota(jnp.int32, (2 * LANES, ext), 0)
    voxel = lax.broadcasted_iota(jnp.int32, (2 * LANES, ext), 1)
    number = source % LANES
    row = jnp.where(number < size_y, number + 1, jnp.where(number == size_y, 0, size_y + 1))
    place = row * size_z + jnp.where(source < LANES, 0, size_z - 1)
    place = jnp.where(number < rows_y, place, -1)
    put = (voxel == place).astype(F32).astype(BF16)
    halo = jnp.dot(columns, put, preferred_element_type=F32)
    lane = lax.broadcasted_iota(jnp.int32, (channels, size_z), 1)
    me, count = lax.axis_index("gy"), spots[0]
    for index in range(planes):
        base = index * group
        body = {0: xlo_ref, 1: first_ref, planes - 2: last_ref, planes - 1: xhi_ref}.get(index)
        for row in range(rows_y):
            cols = slice(row * size_z, (row + 1) * size_z)
            if row == 0:
                wide = jnp.where(me > 0, ylo_ref[index].astype(F32), 0.0)
            elif row == rows_y - 1:
                wide = jnp.where(me < count - 1, yhi_ref[index].astype(F32), 0.0)
            else:
                at = slice((row - 1) * size_z, row * size_z)
                wide = (g_ref[index - 2, :, at] if body is None else body[:, at]).astype(F32)
            edge = halo[index * channels : (index + 1) * channels, cols]
            before = jnp.where(lane == 0, edge, pltpu.roll(wide, 1, 1))
            after = jnp.where(lane == size_z - 1, edge, pltpu.roll(wide, size_z - 1, 1))
            g3_ref[base : base + channels, cols] = before.astype(BF16)
            g3_ref[base + channels : base + 2 * channels, cols] = wide.astype(BF16)
            g3_ref[base + 2 * channels : base + group, cols] = after.astype(BF16)
    for x in range(size_x):
        product = lax.dot_general(
            g3_ref[x * group : (x + 3) * group, :],
            x3_ref[x],
            (((1,), (1,)), ((), ())),
            preferred_element_type=F32,
        )
        if x == 0:
            acc[...] = product
        else:
            acc[...] += product
    wide = jnp.concatenate([acc[...] * scale, jnp.zeros((channels, group), F32)], axis=0)
    turned = jnp.concatenate(
        [wide, jnp.zeros((wide.shape[0], -group % LANES), F32)], axis=1
    ).T
    for b in range(3):
        rows = turned[b * channels : (b + 1) * channels]
        for pair in range(5):
            cell = rows[:, pair * LANES : (pair + 1) * LANES]
            for half in range(2):
                block = 2 * pair + half
                if block < 9:
                    tap = (2 - block // 3) * 9 + b * 3 + 2 - block % 3
                    moved = cell if half == 0 else pltpu.roll(cell, LANES - channels, 1)
                    flat[pl.ds(tap, channels, stride=27), :] = moved
    part_ref[...] = flat[...].T[:channels, : part_ref.shape[1]].astype(BF16)


def wgrad(planes, y_halos, tiles, x3, scale):
    size_x, group, width = x3.shape
    channels = group // 3
    taps = 27 * channels
    spots = (lax.axis_size("gy"), lax.axis_size("gz"))
    flops = 2 * 3 * group * group * size_x * width
    return pl.pallas_call(
        functools.partial(wgrad_kernel, scale, spots),
        in_specs=[VMEM] * 9,
        out_specs=[VMEM] * 2,
        out_shape=[
            jax.ShapeDtypeStruct(((size_x + 2) * group, width), BF16),
            jax.ShapeDtypeStruct((channels, taps), BF16),
        ],
        scratch_shapes=[
            pltpu.VMEM((3 * group, group), F32),
            pltpu.VMEM((-(-taps // LANES) * LANES, LANES), F32),
        ],
        compiler_params=params(),
        cost_estimate=pl.CostEstimate(
            flops=flops, bytes_accessed=8 * 2**20, transcendentals=0
        ),
        name="wgrad",
    )(*planes, *y_halos, tiles, x3)


def dgrad_kernel(size_y, w_ref, g3_ref, out_ref, turned, weights, tile):
    channels, size_x, _, size_z = out_ref.shape
    group = 3 * channels
    plane = size_y * size_z
    taps = w_ref.shape[1]
    wide = w_ref[...].astype(F32)
    wide = jnp.concatenate([wide, jnp.zeros((LANES - channels, taps), F32)], axis=0)
    wide = jnp.concatenate([wide, jnp.zeros((LANES, -taps % LANES), F32)], axis=1)
    turned[...] = wide.T
    for b in range(3):
        blocks = []
        for a in range(3):
            for c in range(3):
                tap = (2 - a) * 9 + (2 - b) * 3 + 2 - c
                blocks.append(turned[pl.ds(tap, channels, stride=27), :][:, :channels])
        zero = jnp.zeros((channels, group), F32)
        weights[b, :channels] = jnp.concatenate(blocks + [zero], axis=1).astype(BF16)
        weights[b, channels:] = jnp.concatenate([zero] + blocks, axis=1).astype(BF16)
    for pair in range(size_x // 2):
        rows = slice(2 * pair * group, (2 * pair + 4) * group)
        total = None
        for b in range(3):
            product = jnp.dot(
                weights[b],
                g3_ref[rows, b * size_z : b * size_z + plane],
                preferred_element_type=F32,
            )
            total = product if total is None else total + product
        for half in range(2):
            for y in range(size_y):
                tile[pl.ds(y, channels, stride=size_y), :] = total[
                    half * channels : (half + 1) * channels, y * size_z : (y + 1) * size_z
                ]
            out_ref[:, 2 * pair + half] = (
                tile[...].reshape(channels, size_y, size_z).astype(BF16)
            )


def dgrad(kernel, g3, shape):
    channels, size_x, size_y, size_z = shape
    taps = kernel.shape[1]
    flops = 2 * 12 * channels * 3 * channels * size_x * size_y * size_z
    return pl.pallas_call(
        functools.partial(dgrad_kernel, size_y),
        in_specs=[VMEM] * 2,
        out_specs=VMEM,
        out_shape=jax.ShapeDtypeStruct(shape, BF16),
        scratch_shapes=[
            pltpu.VMEM((-(-taps // LANES) * LANES, LANES), F32),
            pltpu.VMEM((3, 2 * channels, 12 * channels), BF16),
            pltpu.VMEM((channels * size_y, size_z), F32),
        ],
        compiler_params=params(),
        cost_estimate=pl.CostEstimate(
            flops=flops, bytes_accessed=8 * 2**20, transcendentals=0
        ),
        name="dgrad",
    )(kernel, g3)


def shifted(value, moves):
    names = tuple(moves)
    sizes = [lax.axis_size(name) for name in names]
    pairs = []
    for source in range(math.prod(sizes)):
        rest, coords = source, []
        for size in reversed(sizes):
            coords.insert(0, rest % size)
            rest //= size
        coords = [
            (at + moves[name]) if moves[name] != "swap" else 1 - at
            for at, name in zip(coords, names)
        ]
        if all(0 <= at < size for at, size in zip(coords, sizes)):
            target = 0
            for at, size in zip(coords, sizes):
                target = target * size + at
            pairs.append((source, target))
    return lax.ppermute(value, names if len(names) > 1 else names[0], pairs)


def local(activations, preact, upstream, master, first_moment, second_moment):
    channels, size_x, size_y, size_z = activations.shape
    devices = math.prod(lax.axis_size(a) for a in AXES)
    share = master.shape[0]
    taps = 27 * channels
    span = min(share, taps)
    first, last, sent = faces(preact, upstream, master.reshape(share // span, span), devices)
    x_halos = (shifted(last, {"gx": 1}), shifted(first, {"gx": -1}))
    kernel = lax.all_to_all(sent, AXES, 0, 0, tiled=True).reshape(channels, taps)
    inner, x3 = inner_planes(preact, upstream, activations)
    planes = (x_halos[0], first, inner, last, x_halos[1])
    both = lax.axis_size("gy") != 2
    *y_faces, tiles = pack(planes, size_z, both)
    if both:
        y_halos = (shifted(y_faces[1], {"gy": 1}), shifted(y_faces[0], {"gy": -1}))
    else:
        y_halos = (shifted(y_faces[0], {"gy": "swap"}),) * 2
    tiles = lax.all_to_all(tiles, ("gy", "gz"), 0, 0, tiled=True)
    tiles, kernel = lax.optimization_barrier((tiles, kernel))

    voxels = size_x * size_y * size_z * devices
    g3, part = wgrad(planes, y_halos, tiles, x3, 1.0 / math.sqrt(voxels))
    parts = lax.all_to_all(
        part.reshape(devices, share // span, span), AXES, 0, 0, tiled=True
    )
    grad_input = dgrad(kernel, g3, activations.shape)
    weight_grad = jnp.sum(parts.astype(F32), axis=0).reshape(share)
    new_first = 0.9 * first_moment + 0.1 * weight_grad
    new_second = 0.999 * second_moment + 0.001 * weight_grad * weight_grad
    corr_first = 1.0 - (0.9**10) ** 10
    corr_second = 1.0 - (0.999**10) ** 10
    update = new_first / corr_first / (jnp.sqrt(new_second / corr_second) + 1e-08) + 0.01 * master
    new_master = master - 0.05 * update
    return (grad_input, weight_grad, new_master, new_first, new_second)


def solution(mesh):
    volume = P(None, "gx", "gy", "gz")
    flat = P(AXES)
    return jax.shard_map(
        local,
        mesh=mesh,
        in_specs=(volume, volume, volume, flat, flat, flat),
        out_specs=(volume, flat, flat, flat, flat),
        check_vma=False,
    )
```

```python
import functools
import math

import jax
import jax.numpy as jnp
from jax import lax
from jax.experimental import pallas as pl
from jax.experimental.pallas import tpu as pltpu
from jax.sharding import PartitionSpec as P

AXES = ("gx", "gy", "gz")
LANES = 128
VMEM = pl.BlockSpec(memory_space=pltpu.VMEM)
HBM = pl.BlockSpec(memory_space=pltpu.HBM)
F32 = jnp.float32
BF16 = jnp.bfloat16
ALL_VMEM = 64 * 2**20


def params(limit=24 * 2**20):
    return pltpu.CompilerParams(vmem_limit_bytes=limit)


def cost(flops, moved):
    return pl.CostEstimate(flops=flops, bytes_accessed=moved, transcendentals=0)


def to_planes(value, tile, rows, write):
    channels, size_y, size_z = value.shape
    tile[...] = value.astype(F32).reshape(channels * size_y, size_z)
    count = channels // rows
    for y in range(size_y):
        for r in range(rows):
            picked = tile[pl.ds(r * size_y + y, count, stride=rows * size_y), :]
            write(slice(r * count, (r + 1) * count), y, picked.astype(BF16))


def masked(p, u):
    return jnp.where(p > 0, u, jnp.zeros_like(u))


def face_kernel(rows, p_ref, u_ref, low_ref, high_ref, p_buf, u_buf, tile, sems):
    size_x, size_z = p_ref.shape[1], p_ref.shape[3]
    copies = []
    for k, x in enumerate((0, size_x - 1)):
        pair = (
            pltpu.make_async_copy(p_ref.at[:, x], p_buf.at[k], sems.at[2 * k]),
            pltpu.make_async_copy(u_ref.at[:, x], u_buf.at[k], sems.at[2 * k + 1]),
        )
        for copy in pair:
            copy.start()
        copies.append(pair)
    for k, out_ref in enumerate((low_ref, high_ref)):
        for copy in copies[k]:
            copy.wait()

        def write(at, y, value):
            out_ref[at, y * size_z : (y + 1) * size_z] = value

        to_planes(masked(p_buf[k], u_buf[k]), tile.at[k], rows, write)


def faces(preact, upstream, rows):
    channels, size_x, size_y, size_z = preact.shape
    face = jax.ShapeDtypeStruct((channels, size_y * size_z), BF16)
    buffer = pltpu.VMEM((2, channels, size_y, size_z), BF16)
    return pl.pallas_call(
        functools.partial(face_kernel, rows),
        in_specs=[HBM, HBM],
        out_specs=[VMEM] * 2,
        out_shape=[face, face],
        scratch_shapes=[
            buffer,
            buffer,
            pltpu.VMEM((2, channels * size_y, size_z), F32),
            pltpu.SemaphoreType.DMA((4,)),
        ],
        compiler_params=params(ALL_VMEM - 900_000),
        cost_estimate=cost(0, 2**20),
        name="faces",
    )(preact, upstream)


def inner_kernel(rows, p_ref, u_ref, a_ref, g_ref, x_ref, p_buf, u_buf, a_buf, tile, sems):
    channels, size_x, size_y, size_z = a_ref.shape
    inner = size_x - 2
    copies = []
    for x in range(inner):
        copies.append(
            (
                pltpu.make_async_copy(p_ref.at[:, x + 1], p_buf.at[x], sems.at[x]),
                pltpu.make_async_copy(u_ref.at[:, x + 1], u_buf.at[x], sems.at[inner + x]),
            )
        )
    for x in range(size_x):
        copies.append(
            (pltpu.make_async_copy(a_ref.at[:, x], a_buf.at[x], sems.at[2 * inner + x]),)
        )
    for group in copies:
        for copy in group:
            copy.start()
    for x in range(inner):
        for copy in copies[x]:
            copy.wait()

        def write(at, y, value):
            g_ref[x, at, y * size_z : (y + 1) * size_z] = value

        to_planes(masked(p_buf[x], u_buf[x]), tile.at[x % 2], rows, write)
    for x in range(size_x):
        copies[inner + x][0].wait()

        def write(at, y, value):
            x_ref[x, at, y * size_z : (y + 1) * size_z] = value

        to_planes(a_buf[x], tile.at[x % 2], 1, write)


def inner_planes(preact, upstream, activations, rows):
    channels, size_x, size_y, size_z = preact.shape
    plane = size_y * size_z
    return pl.pallas_call(
        functools.partial(inner_kernel, rows),
        in_specs=[HBM] * 3,
        out_specs=[VMEM] * 2,
        out_shape=[
            jax.ShapeDtypeStruct((size_x - 2, channels, plane), BF16),
            jax.ShapeDtypeStruct((size_x, channels, plane), BF16),
        ],
        scratch_shapes=[
            pltpu.VMEM((size_x - 2, channels, size_y, size_z), BF16),
            pltpu.VMEM((size_x - 2, channels, size_y, size_z), BF16),
            pltpu.VMEM((size_x, channels, size_y, size_z), BF16),
            pltpu.VMEM((2, channels * size_y, size_z), F32),
            pltpu.SemaphoreType.DMA((3 * size_x - 4,)),
        ],
        compiler_params=params(ALL_VMEM - 2_900_000),
        cost_estimate=cost(0, 6 * 2**20),
        name="inner",
    )(preact, upstream, activations)


def body_of(refs, index):
    planes = refs[2].shape[0] + 4
    if 2 <= index < planes - 2:
        return refs[2].at[index - 2]
    return refs[{0: 0, 1: 1, planes - 2: 3, planes - 1: 4}[index]]


def yface_kernel(both, *refs):
    y_refs = refs[5:]
    size_z = y_refs[0].shape[-1]
    is_first = lax.axis_index("gy") == 0
    for index in range(y_refs[0].shape[0]):
        body = body_of(refs[:5], index)
        plane = body.shape[-1]
        low, high = body[:, :size_z], body[:, plane - size_z :]
        if both:
            y_refs[0][index] = low
            y_refs[1][index] = high
        else:
            picked = jnp.where(is_first, high.astype(F32), low.astype(F32))
            y_refs[0][index] = picked.astype(BF16)


def y_faces(planes, size_z, both):
    inner, channels, _ = planes[2].shape
    count = 2 if both else 1
    face = jax.ShapeDtypeStruct((inner + 4, channels, size_z), BF16)
    return pl.pallas_call(
        functools.partial(yface_kernel, both),
        in_specs=[VMEM] * 5,
        out_specs=[VMEM] * count,
        out_shape=[face] * count,
        compiler_params=params(),
        cost_estimate=cost(0, 2**19),
        name="yfaces",
    )(*planes)


def y_halo(refs, index):
    me = lax.axis_index("gy")
    low = jnp.where(me > 0, refs[0][index].astype(F32), 0.0)
    high = jnp.where(me < lax.axis_size("gy") - 1, refs[1][index].astype(F32), 0.0)
    return low, high


def zface_kernel(*refs):
    m_ref, zlo_ref, zhi_ref, sent_ref = refs[7:]
    planes, channels, size_z = refs[5].shape
    plane = refs[0].shape[-1]
    rows_y = plane // size_z + 2
    ext = rows_y * size_z
    voxel = lax.broadcasted_iota(jnp.int32, (ext, 2 * LANES), 0)
    lane = lax.broadcasted_iota(jnp.int32, (ext, 2 * LANES), 1)
    wanted = jnp.where(lane < LANES, lane * size_z, (lane - LANES) * size_z + size_z - 1)
    pick = (voxel == wanted).astype(F32).astype(BF16)
    whole = []
    for index in range(planes):
        low, high = y_halo(refs[5:7], index)
        body = body_of(refs[:5], index)[...]
        whole.append(jnp.concatenate([low.astype(BF16), body, high.astype(BF16)], axis=1))
    columns = jnp.dot(jnp.concatenate(whole, axis=0), pick, preferred_element_type=F32)
    zlo = jnp.zeros((channels, LANES), F32)
    zhi = jnp.zeros((channels, LANES), F32)
    for index in range(planes):
        rows = columns[index * channels : (index + 1) * channels]
        zlo = zlo + pltpu.roll(rows[:, :LANES], index * rows_y, 1)
        zhi = zhi + pltpu.roll(rows[:, LANES:], index * rows_y, 1)
    zlo_ref[...] = zlo.astype(BF16)
    zhi_ref[...] = zhi.astype(BF16)
    count, height, width = sent_ref.shape
    share = m_ref[...]
    if height > share.shape[0]:
        share = jnp.concatenate([share, jnp.zeros((height - share.shape[0], width), F32)], axis=0)
    sent_ref[...] = jnp.broadcast_to(share.astype(BF16)[None], sent_ref.shape)


def z_faces(planes, y_halos, share, sent_shape):
    channels = planes[0].shape[0]
    face = jax.ShapeDtypeStruct((channels, LANES), BF16)
    return pl.pallas_call(
        zface_kernel,
        in_specs=[VMEM] * 8,
        out_specs=[VMEM] * 3,
        out_shape=[face, face, jax.ShapeDtypeStruct(sent_shape, BF16)],
        compiler_params=params(),
        cost_estimate=cost(2**27, 2**21),
        name="zfaces",
    )(*planes, *y_halos, share)


def z_halo(zlo_ref, zhi_ref, planes, rows_y, size_z):
    ext = rows_y * size_z
    low, high = zlo_ref[...].astype(F32), zhi_ref[...].astype(F32)
    turned = []
    for index in range(planes):
        shift = -index * rows_y % LANES
        turned.append(
            jnp.concatenate([pltpu.roll(low, shift, 1), pltpu.roll(high, shift, 1)], axis=1)
        )
    source = lax.broadcasted_iota(jnp.int32, (2 * LANES, ext), 0)
    voxel = lax.broadcasted_iota(jnp.int32, (2 * LANES, ext), 1)
    place = jnp.where(source < LANES, source * size_z, (source - LANES) * size_z + size_z - 1)
    place = jnp.where(source % LANES < rows_y, place, -1)
    put = (voxel == place).astype(F32).astype(BF16)
    return jnp.dot(jnp.concatenate(turned, axis=0).astype(BF16), put, preferred_element_type=F32)


def shifted_plane(index, refs, halo, g3):
    planes, channels, size_z = refs[5].shape
    rows_y = refs[0].shape[-1] // size_z + 2
    base = 3 * channels * index
    lane = lax.broadcasted_iota(jnp.int32, (channels, size_z), 1)
    low, high = y_halo(refs[5:7], index)
    body = body_of(refs[:5], index)
    for row in range(rows_y):
        cols = slice(row * size_z, (row + 1) * size_z)
        if row == 0:
            wide = low
        elif row == rows_y - 1:
            wide = high
        else:
            wide = body[:, (row - 1) * size_z : row * size_z].astype(F32)
        edge = halo[index * channels : (index + 1) * channels, cols]
        before = jnp.where(lane == 0, edge, pltpu.roll(wide, 1, 1))
        after = jnp.where(lane == size_z - 1, edge, pltpu.roll(wide, size_z - 1, 1))
        g3[base : base + channels, cols] = before.astype(BF16)
        g3[base + channels : base + 2 * channels, cols] = wide.astype(BF16)
        g3[base + 2 * channels : base + 3 * channels, cols] = after.astype(BF16)


def wgrad_kernel(scale, rows, *refs):
    x_ref, part_ref, g3, x3, acc, flat, chunks = refs[9:]
    planes, channels, size_z = refs[5].shape
    size_x = planes - 2
    plane = refs[0].shape[-1]
    rows_y = plane // size_z + 2
    group = 3 * channels
    halo = z_halo(refs[7], refs[8], planes, rows_y, size_z)
    zero = jnp.zeros((channels, 2 * size_z), BF16)
    done = 0
    for x in range(size_x):
        while done < x + 3:
            shifted_plane(done, refs, halo, g3)
            done += 1
        value = x_ref[x]
        for b in range(3):
            at = slice(b * channels, (b + 1) * channels)
            start = (2 - b) * size_z
            x3[x, at, start : start + plane] = value
            if start:
                x3[x, at, :start] = zero[:, :start]
            if start < 2 * size_z:
                x3[x, at, start + plane :] = zero[:, start:]
        product = lax.dot_general(
            g3[x * group : (x + 3) * group, :],
            x3[x],
            (((1,), (1,)), ((), ())),
            preferred_element_type=F32,
        )
        if x == 0:
            acc[...] = product
        else:
            acc[...] += product
    wide = jnp.concatenate([acc[...] * scale, jnp.zeros((channels, group), F32)], axis=0)
    turned = jnp.concatenate(
        [wide, jnp.zeros((wide.shape[0], -group % LANES), F32)], axis=1
    ).T
    for b in range(3):
        block_rows = turned[b * channels : (b + 1) * channels]
        for block in range(9):
            pair, half = block // 2, block % 2
            cell = block_rows[:, pair * LANES : (pair + 1) * LANES]
            tap = (2 - block // 3) * 9 + b * 3 + 2 - block % 3
            moved = pltpu.roll(cell, LANES - channels, 1) if half else cell
            flat[pl.ds(tap, channels, stride=27), :] = moved
    whole = flat[...].T[:channels, : 27 * channels]
    if rows is None:
        part_ref[...] = whole.astype(BF16)
        return
    count, height, width = part_ref.shape
    line = jnp.concatenate([whole[r * count : (r + 1) * count] for r in range(rows)], axis=1)
    used = line.shape[1] // width
    chunks[...] = jnp.zeros_like(chunks)
    for k in range(used):
        chunks[pl.ds(k, count, stride=height), :] = line[:, k * width : (k + 1) * width]
    part_ref[...] = chunks[...].reshape(part_ref.shape).astype(BF16)


def wgrad(sources, planes_x, scale, rows, part_shape):
    size_x, channels, plane = planes_x.shape
    size_z = sources[5].shape[-1]
    width = plane + 2 * size_z
    group = 3 * channels
    taps = 27 * channels
    return pl.pallas_call(
        functools.partial(wgrad_kernel, scale, rows),
        in_specs=[VMEM] * 10,
        out_specs=VMEM,
        out_shape=jax.ShapeDtypeStruct(part_shape, BF16),
        scratch_shapes=[
            pltpu.VMEM(((size_x + 2) * group, width), BF16),
            pltpu.VMEM((size_x, group, width), BF16),
            pltpu.VMEM((3 * group, group), F32),
            pltpu.VMEM((-(-taps // LANES) * LANES, LANES), F32),
            pltpu.VMEM((math.prod(part_shape[:-1]), part_shape[-1]), F32),
        ],
        compiler_params=params(32 * 2**20),
        cost_estimate=cost(2 * 3 * group * group * size_x * width, 4 * 2**20),
        name="wgrad",
    )(*sources, planes_x)


def dgrad_kernel(rows, *refs):
    w_ref, out_ref, g3, turned, weights, tile, chunks = refs[9:]
    planes, channels, size_z = refs[5].shape
    size_x = planes - 2
    plane = refs[0].shape[-1]
    size_y = plane // size_z
    group = 3 * channels
    taps = 27 * channels
    if rows is None:
        whole = w_ref[...].astype(F32)
    else:
        count, height, width = w_ref.shape
        chunks[...] = w_ref[...].astype(F32).reshape(chunks.shape)
        used = rows * taps // width
        line = jnp.concatenate(
            [chunks[pl.ds(k, count, stride=height), :] for k in range(used)], axis=1
        )
        whole = jnp.concatenate([line[:, r * taps : (r + 1) * taps] for r in range(rows)], axis=0)
    whole = jnp.concatenate([whole, jnp.zeros((LANES - channels, taps), F32)], axis=0)
    whole = jnp.concatenate([whole, jnp.zeros((LANES, -taps % LANES), F32)], axis=1)
    turned[...] = whole.T
    for b in range(3):
        blocks = []
        for a in range(3):
            for c in range(3):
                tap = (2 - a) * 9 + (2 - b) * 3 + 2 - c
                blocks.append(turned[pl.ds(tap, channels, stride=27), :][:, :channels])
        zero = jnp.zeros((channels, group), F32)
        weights[b, :channels] = jnp.concatenate(blocks + [zero], axis=1).astype(BF16)
        weights[b, channels:] = jnp.concatenate([zero] + blocks, axis=1).astype(BF16)
    halo = z_halo(refs[7], refs[8], planes, size_y + 2, size_z)
    done = 0
    for pair in range(size_x // 2):
        while done < 2 * pair + 4:
            shifted_plane(done, refs, halo, g3)
            done += 1
        at = slice(2 * pair * group, (2 * pair + 4) * group)
        total = None
        for b in range(3):
            product = jnp.dot(
                weights[b],
                g3[at, b * size_z : b * size_z + plane],
                preferred_element_type=F32,
            )
            total = product if total is None else total + product
        for half in range(2):
            for y in range(size_y):
                tile[half, pl.ds(y, channels, stride=size_y), :] = total[
                    half * channels : (half + 1) * channels, y * size_z : (y + 1) * size_z
                ]
            out_ref[:, 2 * pair + half] = (
                tile[half].reshape(channels, size_y, size_z).astype(BF16)
            )


def dgrad(sources, kernel, shape, rows):
    channels, size_x, size_y, size_z = shape
    taps = 27 * channels
    group = 3 * channels
    return pl.pallas_call(
        functools.partial(dgrad_kernel, rows),
        in_specs=[VMEM] * 10,
        out_specs=VMEM,
        out_shape=jax.ShapeDtypeStruct(shape, BF16),
        scratch_shapes=[
            pltpu.VMEM(((size_x + 2) * group, (size_y + 2) * size_z), BF16),
            pltpu.VMEM((-(-taps // LANES) * LANES, LANES), F32),
            pltpu.VMEM((3, 2 * channels, 4 * group), BF16),
            pltpu.VMEM((2, channels * size_y, size_z), F32),
            pltpu.VMEM((math.prod(kernel.shape[:-1]), kernel.shape[-1]), F32),
        ],
        compiler_params=params(32 * 2**20),
        cost_estimate=cost(2 * 12 * channels * group * size_x * size_y * size_z, 4 * 2**20),
        name="dgrad",
    )(*sources, kernel)


def shifted(value, moves):
    names = tuple(moves)
    sizes = [lax.axis_size(name) for name in names]
    pairs = []
    for source in range(math.prod(sizes)):
        rest, coords = source, []
        for size in reversed(sizes):
            coords.insert(0, rest % size)
            rest //= size
        coords = [
            (at + moves[name]) if moves[name] != "swap" else 1 - at
            for at, name in zip(coords, names)
        ]
        if all(0 <= at < size for at, size in zip(coords, sizes)):
            target = 0
            for at, size in zip(coords, sizes):
                target = target * size + at
            pairs.append((source, target))
    return lax.ppermute(value, names if len(names) > 1 else names[0], pairs)


def local(activations, preact, upstream, master, first_moment, second_moment):
    channels, size_x, size_y, size_z = activations.shape
    devices = math.prod(lax.axis_size(a) for a in AXES)
    share = master.shape[0]
    taps = 27 * channels
    tiled = share % taps == 0 and share % LANES == 0
    rows = share // taps if tiled else None
    both = lax.axis_size("gy") != 2

    first, last = faces(preact, upstream, rows or 1)
    x_halos = (shifted(last, {"gx": 1}), shifted(first, {"gx": -1}))
    inner, planes_x = inner_planes(preact, upstream, activations, rows or 1)
    planes = (x_halos[0], first, inner, last, x_halos[1])
    y_sent = y_faces(planes, size_z, both)
    if both:
        y_halos = (shifted(y_sent[1], {"gy": 1}), shifted(y_sent[0], {"gy": -1}))
    else:
        y_halos = (shifted(y_sent[0], {"gy": "swap"}),) * 2
    if tiled:
        used = share // LANES
        block = (-(-used // 16) * 16, LANES)
        own = master.reshape(used, LANES)
    else:
        block = (1, share)
        own = master.reshape(block)
    zlo, zhi, sent = z_faces(planes, y_halos, own, (devices, *block))
    z_halos = (shifted(zhi, {"gz": 1}), shifted(zlo, {"gz": -1}))
    kernel = lax.all_to_all(sent, AXES, 0, 0, tiled=True)
    if not tiled:
        kernel = kernel.reshape(channels, taps)

    voxels = size_x * size_y * size_z * devices
    sources = (*planes, *y_halos, *z_halos)
    part = wgrad(
        sources,
        planes_x,
        1.0 / math.sqrt(voxels),
        rows,
        (devices, *block) if tiled else (channels, taps),
    )
    part, kernel = lax.optimization_barrier((part, kernel))
    parts = lax.all_to_all(part.reshape(devices, *block), AXES, 0, 0, tiled=True)
    grad_input = dgrad(sources, kernel, activations.shape, rows)
    total = jnp.sum(parts.astype(F32), axis=0)
    weight_grad = total.reshape(-1)[:share]
    new_first = 0.9 * first_moment + 0.1 * weight_grad
    new_second = 0.999 * second_moment + 0.001 * weight_grad * weight_grad
    corr_first = 1.0 - (0.9**10) ** 10
    corr_second = 1.0 - (0.999**10) ** 10
    update = new_first / corr_first / (jnp.sqrt(new_second / corr_second) + 1e-08) + 0.01 * master
    new_master = master - 0.05 * update
    return (grad_input, weight_grad, new_master, new_first, new_second)


def solution(mesh):
    volume = P(None, "gx", "gy", "gz")
    flat = P(AXES)
    return jax.shard_map(
        local,
        mesh=mesh,
        in_specs=(volume, volume, volume, flat, flat, flat),
        out_specs=(volume, flat, flat, flat, flat),
        check_vma=False,
    )
```

```python
import functools
import math

import jax
import jax.numpy as jnp
from jax import lax
from jax.experimental import pallas as pl
from jax.experimental.pallas import tpu as pltpu
from jax.sharding import PartitionSpec as P

AXES = ("gx", "gy", "gz")
LANES = 128
VMEM = pl.BlockSpec(memory_space=pltpu.VMEM)
HBM = pl.BlockSpec(memory_space=pltpu.HBM)
F32 = jnp.float32
BF16 = jnp.bfloat16
ALL_VMEM = 64 * 2**20


def params(limit=24 * 2**20):
    return pltpu.CompilerParams(vmem_limit_bytes=limit)


def cost(flops, moved):
    return pl.CostEstimate(flops=flops, bytes_accessed=moved, transcendentals=0)


def to_planes(value, tile, rows, write):
    channels, size_y, size_z = value.shape
    tile[...] = value.astype(F32).reshape(channels * size_y, size_z)
    count = channels // rows
    for y in range(size_y):
        for r in range(rows):
            picked = tile[pl.ds(r * size_y + y, count, stride=rows * size_y), :]
            write(slice(r * count, (r + 1) * count), y, picked.astype(BF16))


def masked(p, u):
    return jnp.where(p > 0, u, jnp.zeros_like(u))


def padded_share(m_ref, height):
    share = m_ref[...]
    if height > share.shape[0]:
        rest = jnp.zeros((height - share.shape[0], share.shape[1]), F32)
        share = jnp.concatenate([share, rest], axis=0)
    return share.astype(BF16)


def face_kernel(rows, p_ref, u_ref, m_ref, low_ref, high_ref, sent_ref, p_buf, u_buf, tile, sems):
    sent_ref[...] = padded_share(m_ref, sent_ref.shape[0])
    size_x, size_z = p_ref.shape[1], p_ref.shape[3]
    copies = []
    for k, x in enumerate((0, size_x - 1)):
        pair = (
            pltpu.make_async_copy(p_ref.at[:, x], p_buf.at[k], sems.at[2 * k]),
            pltpu.make_async_copy(u_ref.at[:, x], u_buf.at[k], sems.at[2 * k + 1]),
        )
        for copy in pair:
            copy.start()
        copies.append(pair)
    for k, out_ref in enumerate((low_ref, high_ref)):
        for copy in copies[k]:
            copy.wait()

        def write(at, y, value):
            out_ref[at, y * size_z : (y + 1) * size_z] = value

        to_planes(masked(p_buf[k], u_buf[k]), tile.at[k], rows, write)


def faces(preact, upstream, share, rows, block):
    channels, size_x, size_y, size_z = preact.shape
    face = jax.ShapeDtypeStruct((channels, size_y * size_z), BF16)
    buffer = pltpu.VMEM((2, channels, size_y, size_z), BF16)
    return pl.pallas_call(
        functools.partial(face_kernel, rows),
        in_specs=[HBM, HBM, VMEM],
        out_specs=[VMEM] * 3,
        out_shape=[face, face, jax.ShapeDtypeStruct(block, BF16)],
        scratch_shapes=[
            buffer,
            buffer,
            pltpu.VMEM((2, channels * size_y, size_z), F32),
            pltpu.SemaphoreType.DMA((4,)),
        ],
        compiler_params=params(ALL_VMEM - 900_000),
        cost_estimate=cost(0, 2**20),
        name="faces",
    )(preact, upstream, share)


def inner_kernel(rows, p_ref, u_ref, a_ref, g_ref, x_ref, p_buf, u_buf, a_buf, tile, sems):
    channels, size_x, size_y, size_z = a_ref.shape
    inner = size_x - 2
    copies = []
    for x in range(inner):
        copies.append(
            (
                pltpu.make_async_copy(p_ref.at[:, x + 1], p_buf.at[x], sems.at[x]),
                pltpu.make_async_copy(u_ref.at[:, x + 1], u_buf.at[x], sems.at[inner + x]),
            )
        )
    for x in range(size_x):
        copies.append(
            (pltpu.make_async_copy(a_ref.at[:, x], a_buf.at[x], sems.at[2 * inner + x]),)
        )
    for group in copies:
        for copy in group:
            copy.start()
    for x in range(inner):
        for copy in copies[x]:
            copy.wait()

        def write(at, y, value):
            g_ref[x, at, y * size_z : (y + 1) * size_z] = value

        to_planes(masked(p_buf[x], u_buf[x]), tile.at[x % 2], rows, write)
    for x in range(size_x):
        copies[inner + x][0].wait()

        def write(at, y, value):
            x_ref[x, at, y * size_z : (y + 1) * size_z] = value

        to_planes(a_buf[x], tile.at[x % 2], 1, write)


def inner_planes(preact, upstream, activations, rows):
    channels, size_x, size_y, size_z = preact.shape
    plane = size_y * size_z
    return pl.pallas_call(
        functools.partial(inner_kernel, rows),
        in_specs=[HBM] * 3,
        out_specs=[VMEM] * 2,
        out_shape=[
            jax.ShapeDtypeStruct((size_x - 2, channels, plane), BF16),
            jax.ShapeDtypeStruct((size_x, channels, plane), BF16),
        ],
        scratch_shapes=[
            pltpu.VMEM((size_x - 2, channels, size_y, size_z), BF16),
            pltpu.VMEM((size_x - 2, channels, size_y, size_z), BF16),
            pltpu.VMEM((size_x, channels, size_y, size_z), BF16),
            pltpu.VMEM((2, channels * size_y, size_z), F32),
            pltpu.SemaphoreType.DMA((3 * size_x - 4,)),
        ],
        compiler_params=params(ALL_VMEM - 2_900_000),
        cost_estimate=cost(0, 6 * 2**20),
        name="inner",
    )(preact, upstream, activations)


def body_of(refs, index):
    planes = refs[2].shape[0] + 4
    if 2 <= index < planes - 2:
        return refs[2].at[index - 2]
    return refs[{0: 0, 1: 1, planes - 2: 3, planes - 1: 4}[index]]


def yface_kernel(both, *refs):
    y_refs = refs[5:]
    size_z = y_refs[0].shape[-1]
    is_first = lax.axis_index("gy") == 0
    for index in range(y_refs[0].shape[0]):
        body = body_of(refs[:5], index)
        plane = body.shape[-1]
        low, high = body[:, :size_z], body[:, plane - size_z :]
        if both:
            y_refs[0][index] = low
            y_refs[1][index] = high
        else:
            picked = jnp.where(is_first, high.astype(F32), low.astype(F32))
            y_refs[0][index] = picked.astype(BF16)


def y_faces(planes, size_z, both):
    inner, channels, _ = planes[2].shape
    count = 2 if both else 1
    face = jax.ShapeDtypeStruct((inner + 4, channels, size_z), BF16)
    return pl.pallas_call(
        functools.partial(yface_kernel, both),
        in_specs=[VMEM] * 5,
        out_specs=[VMEM] * count,
        out_shape=[face] * count,
        compiler_params=params(),
        cost_estimate=cost(0, 2**19),
        name="yfaces",
    )(*planes)


def y_halo(refs, index):
    me = lax.axis_index("gy")
    low = jnp.where(me > 0, refs[0][index].astype(F32), 0.0)
    high = jnp.where(me < lax.axis_size("gy") - 1, refs[1][index].astype(F32), 0.0)
    return low, high


def zface_kernel(*refs):
    zlo_ref, zhi_ref = refs[7:]
    planes, channels, size_z = refs[5].shape
    plane = refs[0].shape[-1]
    rows_y = plane // size_z + 2
    ext = rows_y * size_z
    voxel = lax.broadcasted_iota(jnp.int32, (ext, 2 * LANES), 0)
    lane = lax.broadcasted_iota(jnp.int32, (ext, 2 * LANES), 1)
    wanted = jnp.where(lane < LANES, lane * size_z, (lane - LANES) * size_z + size_z - 1)
    pick = (voxel == wanted).astype(F32).astype(BF16)
    whole = []
    for index in range(planes):
        low, high = y_halo(refs[5:7], index)
        body = body_of(refs[:5], index)[...]
        whole.append(jnp.concatenate([low.astype(BF16), body, high.astype(BF16)], axis=1))
    columns = jnp.dot(jnp.concatenate(whole, axis=0), pick, preferred_element_type=F32)
    zlo = jnp.zeros((channels, LANES), F32)
    zhi = jnp.zeros((channels, LANES), F32)
    for index in range(planes):
        rows = columns[index * channels : (index + 1) * channels]
        zlo = zlo + pltpu.roll(rows[:, :LANES], index * rows_y, 1)
        zhi = zhi + pltpu.roll(rows[:, LANES:], index * rows_y, 1)
    zlo_ref[...] = zlo.astype(BF16)
    zhi_ref[...] = zhi.astype(BF16)


def z_faces(planes, y_halos):
    channels = planes[0].shape[0]
    face = jax.ShapeDtypeStruct((channels, LANES), BF16)
    return pl.pallas_call(
        zface_kernel,
        in_specs=[VMEM] * 7,
        out_specs=[VMEM] * 2,
        out_shape=[face, face],
        compiler_params=params(),
        cost_estimate=cost(2**27, 2**21),
        name="zfaces",
    )(*planes, *y_halos)


def z_halo(zlo_ref, zhi_ref, planes, rows_y, size_z):
    ext = rows_y * size_z
    low, high = zlo_ref[...].astype(F32), zhi_ref[...].astype(F32)
    turned = []
    for index in range(planes):
        shift = -index * rows_y % LANES
        turned.append(
            jnp.concatenate([pltpu.roll(low, shift, 1), pltpu.roll(high, shift, 1)], axis=1)
        )
    source = lax.broadcasted_iota(jnp.int32, (2 * LANES, ext), 0)
    voxel = lax.broadcasted_iota(jnp.int32, (2 * LANES, ext), 1)
    place = jnp.where(source < LANES, source * size_z, (source - LANES) * size_z + size_z - 1)
    place = jnp.where(source % LANES < rows_y, place, -1)
    put = (voxel == place).astype(F32).astype(BF16)
    return jnp.dot(jnp.concatenate(turned, axis=0).astype(BF16), put, preferred_element_type=F32)


def shifted_plane(index, refs, halo, g3):
    planes, channels, size_z = refs[5].shape
    rows_y = refs[0].shape[-1] // size_z + 2
    base = 3 * channels * index
    lane = lax.broadcasted_iota(jnp.int32, (channels, size_z), 1)
    low, high = y_halo(refs[5:7], index)
    body = body_of(refs[:5], index)
    for row in range(rows_y):
        cols = slice(row * size_z, (row + 1) * size_z)
        if row == 0:
            wide = low
        elif row == rows_y - 1:
            wide = high
        else:
            wide = body[:, (row - 1) * size_z : row * size_z].astype(F32)
        edge = halo[index * channels : (index + 1) * channels, cols]
        before = jnp.where(lane == 0, edge, pltpu.roll(wide, 1, 1))
        after = jnp.where(lane == size_z - 1, edge, pltpu.roll(wide, size_z - 1, 1))
        g3[base : base + channels, cols] = before.astype(BF16)
        g3[base + channels : base + 2 * channels, cols] = wide.astype(BF16)
        g3[base + 2 * channels : base + 3 * channels, cols] = after.astype(BF16)


def wgrad_kernel(scale, rows, *refs):
    x_ref, part_ref, g3, x3, acc, flat, chunks = refs[9:]
    planes, channels, size_z = refs[5].shape
    size_x = planes - 2
    plane = refs[0].shape[-1]
    rows_y = plane // size_z + 2
    group = 3 * channels
    halo = z_halo(refs[7], refs[8], planes, rows_y, size_z)
    zero = jnp.zeros((channels, 2 * size_z), BF16)
    done = 0
    for x in range(size_x):
        while done < x + 3:
            shifted_plane(done, refs, halo, g3)
            done += 1
        value = x_ref[x]
        for b in range(3):
            at = slice(b * channels, (b + 1) * channels)
            start = (2 - b) * size_z
            x3[x, at, start : start + plane] = value
            if start:
                x3[x, at, :start] = zero[:, :start]
            if start < 2 * size_z:
                x3[x, at, start + plane :] = zero[:, start:]
        product = lax.dot_general(
            g3[x * group : (x + 3) * group, :],
            x3[x],
            (((1,), (1,)), ((), ())),
            preferred_element_type=F32,
        )
        if x == 0:
            acc[...] = product
        else:
            acc[...] += product
    wide = jnp.concatenate([acc[...] * scale, jnp.zeros((channels, group), F32)], axis=0)
    turned = jnp.concatenate(
        [wide, jnp.zeros((wide.shape[0], -group % LANES), F32)], axis=1
    ).T
    for b in range(3):
        block_rows = turned[b * channels : (b + 1) * channels]
        for block in range(9):
            pair, half = block // 2, block % 2
            cell = block_rows[:, pair * LANES : (pair + 1) * LANES]
            tap = (2 - block // 3) * 9 + b * 3 + 2 - block % 3
            moved = pltpu.roll(cell, LANES - channels, 1) if half else cell
            flat[pl.ds(tap, channels, stride=27), :] = moved
    whole = flat[...].T[:channels, : 27 * channels]
    if rows is None:
        part_ref[...] = whole.astype(BF16)
        return
    count, height, width = part_ref.shape
    line = jnp.concatenate([whole[r * count : (r + 1) * count] for r in range(rows)], axis=1)
    used = line.shape[1] // width
    chunks[...] = jnp.zeros_like(chunks)
    for k in range(used):
        chunks[pl.ds(k, count, stride=height), :] = line[:, k * width : (k + 1) * width]
    part_ref[...] = chunks[...].reshape(part_ref.shape).astype(BF16)


def wgrad(sources, planes_x, scale, rows, part_shape):
    size_x, channels, plane = planes_x.shape
    size_z = sources[5].shape[-1]
    width = plane + 2 * size_z
    group = 3 * channels
    taps = 27 * channels
    return pl.pallas_call(
        functools.partial(wgrad_kernel, scale, rows),
        in_specs=[VMEM] * 10,
        out_specs=VMEM,
        out_shape=jax.ShapeDtypeStruct(part_shape, BF16),
        scratch_shapes=[
            pltpu.VMEM(((size_x + 2) * group, width), BF16),
            pltpu.VMEM((size_x, group, width), BF16),
            pltpu.VMEM((3 * group, group), F32),
            pltpu.VMEM((-(-taps // LANES) * LANES, LANES), F32),
            pltpu.VMEM((math.prod(part_shape[:-1]), part_shape[-1]), F32),
        ],
        compiler_params=params(32 * 2**20),
        cost_estimate=cost(2 * 3 * group * group * size_x * width, 4 * 2**20),
        name="wgrad",
    )(*sources, planes_x)


def dgrad_kernel(rows, *refs):
    w_ref, out_ref, g3, turned, weights, tile, chunks = refs[9:]
    planes, channels, size_z = refs[5].shape
    size_x = planes - 2
    plane = refs[0].shape[-1]
    size_y = plane // size_z
    group = 3 * channels
    taps = 27 * channels
    if rows is None:
        whole = w_ref[...].astype(F32)
    else:
        count, height, width = w_ref.shape
        chunks[...] = w_ref[...].astype(F32).reshape(chunks.shape)
        used = rows * taps // width
        line = jnp.concatenate(
            [chunks[pl.ds(k, count, stride=height), :] for k in range(used)], axis=1
        )
        whole = jnp.concatenate([line[:, r * taps : (r + 1) * taps] for r in range(rows)], axis=0)
    whole = jnp.concatenate([whole, jnp.zeros((LANES - channels, taps), F32)], axis=0)
    whole = jnp.concatenate([whole, jnp.zeros((LANES, -taps % LANES), F32)], axis=1)
    turned[...] = whole.T
    for b in range(3):
        blocks = []
        for a in range(3):
            for c in range(3):
                tap = (2 - a) * 9 + (2 - b) * 3 + 2 - c
                blocks.append(turned[pl.ds(tap, channels, stride=27), :][:, :channels])
        zero = jnp.zeros((channels, group), F32)
        weights[b, :channels] = jnp.concatenate(blocks + [zero], axis=1).astype(BF16)
        weights[b, channels:] = jnp.concatenate([zero] + blocks, axis=1).astype(BF16)
    halo = z_halo(refs[7], refs[8], planes, size_y + 2, size_z)
    done = 0
    for pair in range(size_x // 2):
        while done < 2 * pair + 4:
            shifted_plane(done, refs, halo, g3)
            done += 1
        at = slice(2 * pair * group, (2 * pair + 4) * group)
        total = None
        for b in range(3):
            product = jnp.dot(
                weights[b],
                g3[at, b * size_z : b * size_z + plane],
                preferred_element_type=F32,
            )
            total = product if total is None else total + product
        for half in range(2):
            for y in range(size_y):
                tile[half, pl.ds(y, channels, stride=size_y), :] = total[
                    half * channels : (half + 1) * channels, y * size_z : (y + 1) * size_z
                ]
            out_ref[:, 2 * pair + half] = (
                tile[half].reshape(channels, size_y, size_z).astype(BF16)
            )


def dgrad(sources, kernel, shape, rows):
    channels, size_x, size_y, size_z = shape
    taps = 27 * channels
    group = 3 * channels
    return pl.pallas_call(
        functools.partial(dgrad_kernel, rows),
        in_specs=[VMEM] * 10,
        out_specs=VMEM,
        out_shape=jax.ShapeDtypeStruct(shape, BF16),
        scratch_shapes=[
            pltpu.VMEM(((size_x + 2) * group, (size_y + 2) * size_z), BF16),
            pltpu.VMEM((-(-taps // LANES) * LANES, LANES), F32),
            pltpu.VMEM((3, 2 * channels, 4 * group), BF16),
            pltpu.VMEM((2, channels * size_y, size_z), F32),
            pltpu.VMEM((math.prod(kernel.shape[:-1]), kernel.shape[-1]), F32),
        ],
        compiler_params=params(32 * 2**20),
        cost_estimate=cost(2 * 12 * channels * group * size_x * size_y * size_z, 4 * 2**20),
        name="dgrad",
    )(*sources, kernel)


def shifted(value, moves):
    names = tuple(moves)
    sizes = [lax.axis_size(name) for name in names]
    pairs = []
    for source in range(math.prod(sizes)):
        rest, coords = source, []
        for size in reversed(sizes):
            coords.insert(0, rest % size)
            rest //= size
        coords = [
            (at + moves[name]) if moves[name] != "swap" else 1 - at
            for at, name in zip(coords, names)
        ]
        if all(0 <= at < size for at, size in zip(coords, sizes)):
            target = 0
            for at, size in zip(coords, sizes):
                target = target * size + at
            pairs.append((source, target))
    return lax.ppermute(value, names if len(names) > 1 else names[0], pairs)


def local(activations, preact, upstream, master, first_moment, second_moment):
    channels, size_x, size_y, size_z = activations.shape
    devices = math.prod(lax.axis_size(a) for a in AXES)
    share = master.shape[0]
    taps = 27 * channels
    tiled = share % taps == 0 and share % LANES == 0
    rows = share // taps if tiled else None
    both = lax.axis_size("gy") != 2

    if tiled:
        used = share // LANES
        block = (-(-used // 16) * 16, LANES)
        own = master.reshape(used, LANES)
    else:
        block = (1, share)
        own = master.reshape(block)
    first, last, sent = faces(preact, upstream, own, rows or 1, block)
    kernel = lax.all_gather(sent, AXES, axis=0)
    if not tiled:
        kernel = kernel.reshape(channels, taps)
    x_halos = (shifted(last, {"gx": 1}), shifted(first, {"gx": -1}))
    inner, planes_x = inner_planes(preact, upstream, activations, rows or 1)
    planes = (x_halos[0], first, inner, last, x_halos[1])
    y_sent = y_faces(planes, size_z, both)
    if both:
        y_halos = (shifted(y_sent[1], {"gy": 1}), shifted(y_sent[0], {"gy": -1}))
    else:
        y_halos = (shifted(y_sent[0], {"gy": "swap"}),) * 2
    zlo, zhi = z_faces(planes, y_halos)
    z_halos = (shifted(zhi, {"gz": 1}), shifted(zlo, {"gz": -1}))

    voxels = size_x * size_y * size_z * devices
    sources = (*planes, *y_halos, *z_halos)
    part = wgrad(
        sources,
        planes_x,
        1.0 / math.sqrt(voxels),
        rows,
        (devices, *block) if tiled else (channels, taps),
    )
    parts = lax.all_to_all(part.reshape(devices, *block), AXES, 0, 0, tiled=True)
    grad_input = dgrad(sources, kernel, activations.shape, rows)
    total = jnp.sum(parts.astype(F32), axis=0)
    weight_grad = total.reshape(-1)[:share]
    new_first = 0.9 * first_moment + 0.1 * weight_grad
    new_second = 0.999 * second_moment + 0.001 * weight_grad * weight_grad
    corr_first = 1.0 - (0.9**10) ** 10
    corr_second = 1.0 - (0.999**10) ** 10
    update = new_first / corr_first / (jnp.sqrt(new_second / corr_second) + 1e-08) + 0.01 * master
    new_master = master - 0.05 * update
    return (grad_input, weight_grad, new_master, new_first, new_second)


def solution(mesh):
    volume = P(None, "gx", "gy", "gz")
    flat = P(AXES)
    return jax.shard_map(
        local,
        mesh=mesh,
        in_specs=(volume, volume, volume, flat, flat, flat),
        out_specs=(volume, flat, flat, flat, flat),
        check_vma=False,
    )
```

```python
import functools
import math

import jax
import jax.numpy as jnp
from jax import lax
from jax.experimental import pallas as pl
from jax.experimental.pallas import tpu as pltpu
from jax.sharding import PartitionSpec as P

AXES = ("gx", "gy", "gz")
LANES = 128
VMEM = pl.BlockSpec(memory_space=pltpu.VMEM)
HBM = pl.BlockSpec(memory_space=pltpu.HBM)
F32 = jnp.float32
BF16 = jnp.bfloat16
ALL_VMEM = 64 * 2**20


def params(limit=24 * 2**20):
    return pltpu.CompilerParams(vmem_limit_bytes=limit)


def cost(flops, moved):
    return pl.CostEstimate(flops=flops, bytes_accessed=moved, transcendentals=0)


def to_planes(value, tile, write):
    channels, size_y, size_z = value.shape
    tile[...] = value.astype(F32).reshape(channels * size_y, size_z)
    for y in range(size_y):
        write(y, tile[pl.ds(y, channels, stride=size_y), :].astype(BF16))


def masked(p, u):
    return jnp.where(p > 0, u, jnp.zeros_like(u))


def face_kernel(p_ref, u_ref, low_ref, high_ref, p_buf, u_buf, tile, sems):
    size_x, size_z = p_ref.shape[1], p_ref.shape[3]
    copies = []
    for k, x in enumerate((0, size_x - 1)):
        pair = (
            pltpu.make_async_copy(p_ref.at[:, x], p_buf.at[k], sems.at[2 * k]),
            pltpu.make_async_copy(u_ref.at[:, x], u_buf.at[k], sems.at[2 * k + 1]),
        )
        for copy in pair:
            copy.start()
        copies.append(pair)
    for k, out_ref in enumerate((low_ref, high_ref)):
        for copy in copies[k]:
            copy.wait()

        def write(y, value):
            out_ref[:, y * size_z : (y + 1) * size_z] = value

        to_planes(masked(p_buf[k], u_buf[k]), tile.at[k], write)


def faces(preact, upstream):
    channels, size_x, size_y, size_z = preact.shape
    face = jax.ShapeDtypeStruct((channels, size_y * size_z), BF16)
    buffer = pltpu.VMEM((2, channels, size_y, size_z), BF16)
    return pl.pallas_call(
        face_kernel,
        in_specs=[HBM, HBM],
        out_specs=[VMEM] * 2,
        out_shape=[face, face],
        scratch_shapes=[
            buffer,
            buffer,
            pltpu.VMEM((2, channels * size_y, size_z), F32),
            pltpu.SemaphoreType.DMA((4,)),
        ],
        compiler_params=params(ALL_VMEM - 900_000),
        cost_estimate=cost(0, 2**20),
        name="faces",
    )(preact, upstream)


def inner_kernel(p_ref, u_ref, a_ref, m_ref, g_ref, x_ref, sent_ref, p_buf, u_buf, a_buf, tile, sems):
    channels, size_x, size_y, size_z = a_ref.shape
    inner = size_x - 2
    copies = []
    for x in range(inner):
        copies.append(
            (
                pltpu.make_async_copy(p_ref.at[:, x + 1], p_buf.at[x], sems.at[x]),
                pltpu.make_async_copy(u_ref.at[:, x + 1], u_buf.at[x], sems.at[inner + x]),
            )
        )
    for x in range(size_x):
        copies.append(
            (pltpu.make_async_copy(a_ref.at[:, x], a_buf.at[x], sems.at[2 * inner + x]),)
        )
    for group in copies:
        for copy in group:
            copy.start()
    share = m_ref[...]
    count, height, width = sent_ref.shape
    if height > share.shape[0]:
        share = jnp.concatenate([share, jnp.zeros((height - share.shape[0], width), F32)], axis=0)
    sent_ref[...] = jnp.broadcast_to(share.astype(BF16)[None], sent_ref.shape)
    for x in range(inner):
        for copy in copies[x]:
            copy.wait()

        def write(y, value):
            g_ref[x, :, y * size_z : (y + 1) * size_z] = value

        to_planes(masked(p_buf[x], u_buf[x]), tile.at[x % 2], write)
    for x in range(size_x):
        copies[inner + x][0].wait()

        def write(y, value):
            x_ref[x, :, y * size_z : (y + 1) * size_z] = value

        to_planes(a_buf[x], tile.at[x % 2], write)


def inner_planes(preact, upstream, activations, share, sent_shape):
    channels, size_x, size_y, size_z = preact.shape
    plane = size_y * size_z
    return pl.pallas_call(
        inner_kernel,
        in_specs=[HBM] * 3 + [VMEM],
        out_specs=[VMEM] * 3,
        out_shape=[
            jax.ShapeDtypeStruct((size_x - 2, channels, plane), BF16),
            jax.ShapeDtypeStruct((size_x, channels, plane), BF16),
            jax.ShapeDtypeStruct(sent_shape, BF16),
        ],
        scratch_shapes=[
            pltpu.VMEM((size_x - 2, channels, size_y, size_z), BF16),
            pltpu.VMEM((size_x - 2, channels, size_y, size_z), BF16),
            pltpu.VMEM((size_x, channels, size_y, size_z), BF16),
            pltpu.VMEM((2, channels * size_y, size_z), F32),
            pltpu.SemaphoreType.DMA((3 * size_x - 4,)),
        ],
        compiler_params=params(ALL_VMEM - 3_600_000),
        cost_estimate=cost(0, 6 * 2**20),
        name="inner",
    )(preact, upstream, activations, share)


def body_of(refs, index):
    planes = refs[2].shape[0] + 4
    if 2 <= index < planes - 2:
        return refs[2].at[index - 2]
    return refs[{0: 0, 1: 1, planes - 2: 3, planes - 1: 4}[index]]


def y_halo(refs, index):
    me = lax.axis_index("gy")
    low = jnp.where(me > 0, refs[0][index].astype(F32), 0.0)
    high = jnp.where(me < lax.axis_size("gy") - 1, refs[1][index].astype(F32), 0.0)
    return low, high


def z_picker(rows_y, size_z):
    shape = (rows_y * size_z, 2 * LANES)
    voxel = lax.broadcasted_iota(jnp.int32, shape, 0)
    lane = lax.broadcasted_iota(jnp.int32, shape, 1)
    wanted = jnp.where(lane < LANES, lane * size_z, (lane - LANES) * size_z + size_z - 1)
    return (voxel == wanted).astype(F32).astype(BF16)


def z_tiles(planes, rows_y, size_z):
    channels = planes[0].shape[0]
    columns = jnp.dot(
        jnp.concatenate(planes, axis=0), z_picker(rows_y, size_z), preferred_element_type=F32
    )
    low = jnp.zeros((channels, LANES), F32)
    high = jnp.zeros((channels, LANES), F32)
    for index in range(len(planes)):
        rows = columns[index * channels : (index + 1) * channels]
        low = low + pltpu.roll(rows[:, :LANES], index * rows_y, 1)
        high = high + pltpu.roll(rows[:, LANES:], index * rows_y, 1)
    return low, high


def put_columns(columns, row_of, rows_y, size_z):
    shape = (2 * LANES, rows_y * size_z)
    source = lax.broadcasted_iota(jnp.int32, shape, 0)
    voxel = lax.broadcasted_iota(jnp.int32, shape, 1)
    number = source % LANES
    place = row_of(number) * size_z + jnp.where(source < LANES, 0, size_z - 1)
    place = jnp.where(number < rows_y, place, -1)
    put = (voxel == place).astype(F32).astype(BF16)
    rows = [jnp.concatenate(pair, axis=1) for pair in columns]
    return jnp.dot(
        jnp.concatenate(rows, axis=0).astype(BF16), put, preferred_element_type=F32
    )


def z_halo(low_ref, high_ref, planes, rows_y, size_z):
    columns = []
    for index in range(planes):
        shift = -index * rows_y % LANES
        columns.append(
            [pltpu.roll(ref[...].astype(F32), shift, 1) for ref in (low_ref, high_ref)]
        )
    return put_columns(columns, lambda number: number, rows_y, size_z)


def pair_z_halo(low_ref, high_ref, planes, size_y, size_z):
    me = lax.axis_index("gy")
    sides = []
    for ref in (low_ref, high_ref):
        first, second = ref[0].astype(F32), ref[1].astype(F32)
        lane = lax.broadcasted_iota(jnp.int32, first.shape, 1)
        own = jnp.where(me == 0, first, second)
        before = jnp.where(me == 0, 0.0, first)
        after = jnp.where(me == 0, second, 0.0)
        columns = []
        for index in range(planes):
            start = index * size_y
            columns.append(
                jnp.where(
                    lane < size_y,
                    pltpu.roll(own, -start % LANES, 1),
                    jnp.where(
                        lane == size_y,
                        pltpu.roll(before, (1 - start) % LANES, 1),
                        pltpu.roll(after, (size_y + 1 - start) % LANES, 1),
                    ),
                )
            )
        sides.append(columns)

    def row_of(number):
        return jnp.where(number < size_y, number + 1, jnp.where(number == size_y, 0, size_y + 1))

    return put_columns(list(zip(*sides)), row_of, size_y + 2, size_z)


def shifted_plane(index, refs, halo, g3):
    channels, plane = refs[0].shape
    size_z = refs[5].shape[-1]
    rows_y = plane // size_z + 2
    base = 3 * channels * index
    lane = lax.broadcasted_iota(jnp.int32, (channels, size_z), 1)
    low, high = y_halo(refs[5:7], index)
    body = body_of(refs[:5], index)
    for row in range(rows_y):
        cols = slice(row * size_z, (row + 1) * size_z)
        if row == 0:
            wide = low
        elif row == rows_y - 1:
            wide = high
        else:
            wide = body[:, (row - 1) * size_z : row * size_z].astype(F32)
        edge = 0.0 if halo is None else halo[index * channels : (index + 1) * channels, cols]
        before = jnp.where(lane == 0, edge, pltpu.roll(wide, 1, 1))
        after = jnp.where(lane == size_z - 1, edge, pltpu.roll(wide, size_z - 1, 1))
        g3[base : base + channels, cols] = before.astype(BF16)
        g3[base + channels : base + 2 * channels, cols] = wide.astype(BF16)
        g3[base + 2 * channels : base + 3 * channels, cols] = after.astype(BF16)


def weight_products(refs, halo, x_ref, g3, x3, acc):
    size_x, channels, plane = x_ref.shape
    size_z = refs[5].shape[-1]
    group = 3 * channels
    zero = jnp.zeros((channels, 2 * size_z), BF16)
    done = 0
    for x in range(size_x):
        while done < x + 3:
            shifted_plane(done, refs, halo, g3)
            done += 1
        value = x_ref[x]
        for b in range(3):
            at = slice(b * channels, (b + 1) * channels)
            start = (2 - b) * size_z
            x3[x, at, start : start + plane] = value
            if start:
                x3[x, at, :start] = zero[:, :start]
            if start < 2 * size_z:
                x3[x, at, start + plane :] = zero[:, start:]
        product = lax.dot_general(
            g3[x * group : (x + 3) * group, :],
            x3[x],
            (((1,), (1,)), ((), ())),
            preferred_element_type=F32,
        )
        if x == 0:
            acc[...] = product
        else:
            acc[...] += product


def to_flat(value, count, channels, flat):
    height, width = value.shape
    wide = jnp.concatenate([value, jnp.zeros((-height % LANES, width), F32)], axis=0)
    wide = jnp.concatenate([wide, jnp.zeros((wide.shape[0], -width % LANES), F32)], axis=1)
    turned = wide.T
    for b in range(3):
        rows = turned[b * channels : (b + 1) * channels]
        for block in range(9):
            start = block * count
            cell = rows[:, start // LANES * LANES : (start // LANES + 1) * LANES]
            tap = (2 - block // 3) * 9 + b * 3 + 2 - block % 3
            shift = -start % LANES
            flat[pl.ds(tap, channels, stride=27), :] = pltpu.roll(cell, shift, 1) if shift else cell
    return flat[...].T[:count]


def spread_weights(whole, turned, weights):
    channels, taps = whole.shape
    group = 3 * channels
    whole = jnp.concatenate([whole, jnp.zeros((LANES - channels, taps), F32)], axis=0)
    whole = jnp.concatenate([whole, jnp.zeros((LANES, -taps % LANES), F32)], axis=1)
    turned[...] = whole.T
    for b in range(3):
        blocks = []
        for a in range(3):
            for c in range(3):
                tap = (2 - a) * 9 + (2 - b) * 3 + 2 - c
                blocks.append(turned[pl.ds(tap, channels, stride=27), :][:, :channels])
        zero = jnp.zeros((channels, group), F32)
        weights[b, :channels] = jnp.concatenate(blocks + [zero], axis=1).astype(BF16)
        weights[b, channels:] = jnp.concatenate([zero] + blocks, axis=1).astype(BF16)


def input_products(refs, halo, g3, weights, tile, out_ref):
    channels, size_x, size_y, size_z = out_ref.shape
    group = 3 * channels
    plane = size_y * size_z
    done = 0
    for pair in range(size_x // 2):
        while done < 2 * pair + 4:
            shifted_plane(done, refs, halo, g3)
            done += 1
        at = slice(2 * pair * group, (2 * pair + 4) * group)
        total = None
        for b in range(3):
            product = jnp.dot(
                weights[b],
                g3[at, b * size_z : b * size_z + plane],
                preferred_element_type=F32,
            )
            total = product if total is None else total + product
        for half in range(2):
            for y in range(size_y):
                tile[half, pl.ds(y, channels, stride=size_y), :] = total[
                    half * channels : (half + 1) * channels, y * size_z : (y + 1) * size_z
                ]
            out_ref[:, 2 * pair + half] = (
                tile[half].reshape(channels, size_y, size_z).astype(BF16)
            )


def g3_scratch(channels, size_x, size_y, size_z):
    return pltpu.VMEM(((size_x + 2) * 3 * channels, (size_y + 2) * size_z), BF16)


def x3_scratch(channels, size_x, size_y, size_z):
    return pltpu.VMEM((size_x, 3 * channels, (size_y + 2) * size_z), BF16)


def acc_scratch(channels):
    return pltpu.VMEM((9 * channels, 3 * channels), F32)


def flat_scratch(channels):
    return pltpu.VMEM((-(-27 * channels // LANES) * LANES, LANES), F32)


def dgrad_scratch(channels, size_x, size_y, size_z):
    return [
        g3_scratch(channels, size_x, size_y, size_z),
        flat_scratch(channels),
        pltpu.VMEM((3, 2 * channels, 12 * channels), BF16),
        pltpu.VMEM((2, channels * size_y, size_z), F32),
    ]


def wgrad_cost(channels, size_x, size_y, size_z):
    return cost(54 * channels * channels * size_x * (size_y + 2) * size_z, 4 * 2**20)


def dgrad_cost(channels, size_x, size_y, size_z):
    return cost(72 * channels * channels * size_x * size_y * size_z, 4 * 2**20)


def side_kernel(*refs):
    sent_ref = refs[5]
    planes = refs[2].shape[0] + 4
    plane = refs[0].shape[-1]
    size_z = sent_ref.shape[-1]
    is_first = lax.axis_index("gy") == 0
    whole = []
    for index in range(planes):
        body = body_of(refs[:5], index)[...]
        whole.append(body)
        low, high = body[:, :size_z], body[:, plane - size_z :]
        picked = jnp.where(is_first, high.astype(F32), low.astype(F32))
        sent_ref[index] = picked.astype(BF16)
    low, high = z_tiles(whole, plane // size_z, size_z)
    sent_ref[planes] = low.astype(BF16)
    sent_ref[planes + 1] = high.astype(BF16)


def side(planes, size_z):
    inner, channels, _ = planes[2].shape
    return pl.pallas_call(
        side_kernel,
        in_specs=[VMEM] * 5,
        out_specs=VMEM,
        out_shape=jax.ShapeDtypeStruct((inner + 6, channels, size_z), BF16),
        compiler_params=params(),
        cost_estimate=cost(2**27, 2**21),
        name="side",
    )(*planes)


def join_kernel(own_ref, other_ref, low_ref, high_ref):
    at = own_ref.shape[0] - 2
    me = lax.axis_index("gy")
    for k, out_ref in enumerate((low_ref, high_ref)):
        out_ref[me] = own_ref[at + k]
        out_ref[1 - me] = other_ref[at + k]


def join(own, other):
    tiles = jax.ShapeDtypeStruct((2, *own.shape[1:]), BF16)
    return pl.pallas_call(
        join_kernel,
        in_specs=[VMEM] * 2,
        out_specs=[VMEM] * 2,
        out_shape=[tiles, tiles],
        compiler_params=params(),
        cost_estimate=cost(0, 2**17),
        name="join",
    )(own, other)


def pair_wgrad_kernel(span, *refs):
    x_ref, mine_ref, theirs_ref, g3, x3, acc = refs[7:]
    size_x, channels, plane = x_ref.shape
    size_z = refs[5].shape[-1]
    weight_products(refs, None, x_ref, g3, x3, acc)
    me = lax.axis_index("gy")
    rows = 9 * channels // 2
    width = 3 * channels
    spare = jnp.zeros((rows, mine_ref.shape[1] - width), F32)
    halves = []
    for half in range(2):
        at = range(half * span, 9 * channels, 2 * span)
        halves.append(jnp.concatenate([acc[start : start + span, :] for start in at], axis=0))
    low, high = z_tiles([x_ref[x] for x in range(size_x)], plane // size_z, size_z)
    for ref, own in ((mine_ref, True), (theirs_ref, False)):
        picked = jnp.where((me == 0) == own, halves[0], halves[1])
        ref[:rows, :] = jnp.concatenate([picked, spare], axis=1)
        ref[rows:, :LANES] = low
        ref[rows:, LANES:] = high


def pair_wgrad(sources, planes_x, shape, span):
    channels = shape[0]
    part = jax.ShapeDtypeStruct((9 * channels // 2 + channels, 2 * LANES), F32)
    return pl.pallas_call(
        functools.partial(pair_wgrad_kernel, span),
        in_specs=[VMEM] * 8,
        out_specs=[VMEM] * 2,
        out_shape=[part, part],
        scratch_shapes=[g3_scratch(*shape), x3_scratch(*shape), acc_scratch(channels)],
        compiler_params=params(32 * 2**20),
        cost_estimate=wgrad_cost(*shape),
        name="wgrad",
    )(*sources, planes_x)


def finish_kernel(scale, span, rows, sizes, *refs):
    mine_ref, other_ref, zlo_ref, zhi_ref, part_ref, flat, lines, chunks = refs
    size_x, size_y = sizes
    channels = zlo_ref.shape[1]
    count = channels // 2
    height = 9 * count
    area = size_x * size_y
    me = lax.axis_index("gy")
    total = (mine_ref[:height, :] + other_ref[:height, :])[:, : 3 * channels]
    own, other = mine_ref[height:, :], other_ref[height:, :]
    inputs = (jnp.where(me == 0, own, other), jnp.where(me == 0, other, own))
    lane = lax.broadcasted_iota(jnp.int32, (channels, LANES), 1)
    row = lane % size_y
    few = lax.broadcasted_iota(jnp.int32, (count, LANES), 1)
    edge = {}
    for side_z, tile_ref in ((0, zlo_ref), (2, zhi_ref)):
        cols = slice(0, LANES) if side_z == 0 else slice(LANES, 2 * LANES)
        value = jnp.where(
            lane < area, inputs[0][:, cols], pltpu.roll(inputs[1][:, cols], area, 1)
        )
        jump = area - size_y + 1
        below = jnp.where(lane >= area, pltpu.roll(value, jump, 1), 0.0)
        above = jnp.where(lane < area, pltpu.roll(value, LANES - jump, 1), 0.0)
        right = jnp.concatenate(
            [
                jnp.where(row > 0, pltpu.roll(value, 1, 1), below),
                value,
                jnp.where(row < size_y - 1, pltpu.roll(value, LANES - 1, 1), above),
            ],
            axis=0,
        )
        tiles = []
        for device in range(2):
            tile = tile_ref[device].astype(F32)
            halves = [
                jnp.concatenate(
                    [tile[at : at + span] for at in range(half * span, channels, 2 * span)], axis=0
                )
                for half in range(2)
            ]
            tiles.append(jnp.where(me == 0, halves[0], halves[1]))
        left = []
        for a in range(3):
            first = pltpu.roll(tiles[0], -a * size_y % LANES, 1)
            second = pltpu.roll(tiles[1], (area - a * size_y) % LANES, 1)
            left.append(jnp.where(few < area, first, jnp.where(few < 2 * area, second, 0.0)))
        edge[side_z] = lax.dot_general(
            jnp.concatenate(left, axis=0).astype(BF16),
            right.astype(BF16),
            (((1,), (1,)), ((), ())),
            preferred_element_type=F32,
        )
    blocks = []
    for a in range(3):
        for c in range(3):
            block = total[(3 * a + c) * count : (3 * a + c + 1) * count]
            blocks.append(block if c == 1 else block + edge[c][a * count : (a + 1) * count])
    taps = 27 * channels
    whole = to_flat(jnp.concatenate(blocks, axis=0) * scale, count, channels, flat)
    pieces = whole.shape[1] // LANES
    for k in range(pieces):
        lines[k * count : (k + 1) * count, :] = whole[:, k * LANES : (k + 1) * LANES]
    number, tall, width = part_ref.shape
    parts = []
    for r in range(rows):
        found = [lines[pl.ds(k * count + r, number, stride=rows), :] for k in range(pieces)]
        parts.append(jnp.concatenate(found, axis=1)[:, :taps])
    line = jnp.concatenate(parts, axis=1)
    chunks[...] = jnp.zeros_like(chunks)
    for k in range(line.shape[1] // width):
        chunks[pl.ds(k, number, stride=tall), :] = line[:, k * width : (k + 1) * width]
    part_ref[...] = chunks[...].reshape(part_ref.shape).astype(BF16)


def finish(mine, other, z_halos, scale, span, rows, sizes, part_shape):
    channels = z_halos[0].shape[1]
    return pl.pallas_call(
        functools.partial(finish_kernel, scale, span, rows, sizes),
        in_specs=[VMEM] * 4,
        out_specs=VMEM,
        out_shape=jax.ShapeDtypeStruct(part_shape, BF16),
        scratch_shapes=[
            flat_scratch(channels),
            pltpu.VMEM((-(-27 * channels // LANES) * channels // 2, LANES), F32),
            pltpu.VMEM((part_shape[0] * part_shape[1], part_shape[2]), F32),
        ],
        compiler_params=params(),
        cost_estimate=cost(2**24, 2**20),
        name="finish",
    )(mine, other, *z_halos)


def pair_dgrad_kernel(rows, *refs):
    w_ref, out_ref, g3, turned, weights, tile, chunks, lines = refs[9:]
    channels, size_x, size_y, size_z = out_ref.shape
    taps = 27 * channels
    count, height, width = w_ref.shape
    chunks[...] = w_ref[...].astype(F32).reshape(chunks.shape)
    line = jnp.concatenate(
        [chunks[pl.ds(k, count, stride=height), :] for k in range(rows * taps // width)], axis=1
    )
    pieces = lines.shape[0] // channels
    spare = jnp.zeros((count, pieces * LANES - taps), F32)
    for r in range(rows):
        found = jnp.concatenate([line[:, r * taps : (r + 1) * taps], spare], axis=1)
        for k in range(pieces):
            lines[pl.ds(k * channels + r, count, stride=rows), :] = found[
                :, k * LANES : (k + 1) * LANES
            ]
    whole = [lines[k * channels : (k + 1) * channels, :] for k in range(pieces)]
    spread_weights(jnp.concatenate(whole, axis=1)[:, :taps], turned, weights)
    halo = pair_z_halo(refs[7], refs[8], size_x + 2, size_y, size_z)
    input_products(refs, halo, g3, weights, tile, out_ref)


def pair_dgrad(sources, kernel, shape, rows):
    channels = shape[0]
    return pl.pallas_call(
        functools.partial(pair_dgrad_kernel, rows),
        in_specs=[VMEM] * 10,
        out_specs=VMEM,
        out_shape=jax.ShapeDtypeStruct(shape, BF16),
        scratch_shapes=dgrad_scratch(*shape)
        + [
            pltpu.VMEM((kernel.shape[0] * kernel.shape[1], kernel.shape[2]), F32),
            pltpu.VMEM((-(-27 * channels // LANES) * channels, LANES), F32),
        ],
        compiler_params=params(32 * 2**20),
        cost_estimate=dgrad_cost(*shape),
        name="dgrad",
    )(*sources, kernel)


def pair_gradients(activations, preact, upstream, master, scale):
    shape = activations.shape
    channels, size_x, size_y, size_z = shape
    devices = math.prod(lax.axis_size(a) for a in AXES)
    rows = channels // devices
    span = lax.axis_size("gz") * rows
    used = master.shape[0] // LANES
    tall = -(-used // 16) * 16
    first, last = faces(preact, upstream)
    x_halos = (shifted(last, {"gx": 1}), shifted(first, {"gx": -1}))
    inner, planes_x, sent = inner_planes(
        preact, upstream, activations, master.reshape(used, LANES), (devices, tall, LANES)
    )
    kernel = lax.all_to_all(sent, AXES, 0, 0, tiled=True)
    planes = (x_halos[0], first, inner, last, x_halos[1])
    own = side(planes, size_z)
    other = shifted(own, {"gy": "swap"})
    zlo, zhi = join(own, other)
    z_halos = (shifted(zhi, {"gz": 1}), shifted(zlo, {"gz": -1}))
    sources = (*planes, other, other)
    mine, theirs = pair_wgrad(sources, planes_x, shape, span)
    theirs = shifted(theirs, {"gy": "swap"})
    part = finish(
        mine,
        theirs,
        z_halos,
        scale,
        span,
        rows,
        (size_x, size_y),
        (devices // 2, tall, LANES),
    )
    part, kernel = lax.optimization_barrier((part, kernel))
    parts = lax.all_to_all(part, ("gx", "gz"), 0, 0, tiled=True)
    grad_input = pair_dgrad((*sources, *z_halos), kernel, shape, rows)
    return grad_input, parts


def yface_kernel(*refs):
    low_ref, high_ref = refs[5:]
    size_z = low_ref.shape[-1]
    for index in range(low_ref.shape[0]):
        body = body_of(refs[:5], index)
        plane = body.shape[-1]
        low_ref[index] = body[:, :size_z]
        high_ref[index] = body[:, plane - size_z :]


def y_faces(planes, size_z):
    inner, channels, _ = planes[2].shape
    face = jax.ShapeDtypeStruct((inner + 4, channels, size_z), BF16)
    return pl.pallas_call(
        yface_kernel,
        in_specs=[VMEM] * 5,
        out_specs=[VMEM] * 2,
        out_shape=[face] * 2,
        compiler_params=params(),
        cost_estimate=cost(0, 2**19),
        name="yfaces",
    )(*planes)


def zface_kernel(*refs):
    zlo_ref, zhi_ref = refs[7:]
    size_z = refs[5].shape[-1]
    whole = []
    for index in range(refs[5].shape[0]):
        low, high = y_halo(refs[5:7], index)
        body = body_of(refs[:5], index)[...]
        whole.append(jnp.concatenate([low.astype(BF16), body, high.astype(BF16)], axis=1))
    low, high = z_tiles(whole, whole[0].shape[1] // size_z, size_z)
    zlo_ref[...] = low.astype(BF16)
    zhi_ref[...] = high.astype(BF16)


def z_faces(planes, y_halos):
    face = jax.ShapeDtypeStruct((planes[0].shape[0], LANES), BF16)
    return pl.pallas_call(
        zface_kernel,
        in_specs=[VMEM] * 7,
        out_specs=[VMEM] * 2,
        out_shape=[face, face],
        compiler_params=params(),
        cost_estimate=cost(2**27, 2**21),
        name="zfaces",
    )(*planes, *y_halos)


def wgrad_kernel(scale, *refs):
    x_ref, part_ref, g3, x3, acc, flat = refs[9:]
    size_x, channels, plane = x_ref.shape
    size_z = refs[5].shape[-1]
    halo = z_halo(refs[7], refs[8], size_x + 2, plane // size_z + 2, size_z)
    weight_products(refs, halo, x_ref, g3, x3, acc)
    whole = to_flat(acc[...] * scale, channels, channels, flat)
    part_ref[...] = whole[:, : part_ref.shape[1]].astype(BF16)


def wgrad(sources, planes_x, shape, scale):
    channels = shape[0]
    return pl.pallas_call(
        functools.partial(wgrad_kernel, scale),
        in_specs=[VMEM] * 10,
        out_specs=VMEM,
        out_shape=jax.ShapeDtypeStruct((channels, 27 * channels), BF16),
        scratch_shapes=[
            g3_scratch(*shape),
            x3_scratch(*shape),
            acc_scratch(channels),
            flat_scratch(channels),
        ],
        compiler_params=params(32 * 2**20),
        cost_estimate=wgrad_cost(*shape),
        name="wgrad",
    )(*sources, planes_x)


def dgrad_kernel(*refs):
    w_ref, out_ref, g3, turned, weights, tile = refs[9:]
    _, size_x, size_y, size_z = out_ref.shape
    spread_weights(w_ref[...].astype(F32), turned, weights)
    halo = z_halo(refs[7], refs[8], size_x + 2, size_y + 2, size_z)
    input_products(refs, halo, g3, weights, tile, out_ref)


def dgrad(sources, kernel, shape):
    return pl.pallas_call(
        dgrad_kernel,
        in_specs=[VMEM] * 10,
        out_specs=VMEM,
        out_shape=jax.ShapeDtypeStruct(shape, BF16),
        scratch_shapes=dgrad_scratch(*shape),
        compiler_params=params(32 * 2**20),
        cost_estimate=dgrad_cost(*shape),
        name="dgrad",
    )(*sources, kernel)


def general_gradients(activations, preact, upstream, master, scale):
    shape = activations.shape
    channels, _, _, size_z = shape
    devices = math.prod(lax.axis_size(a) for a in AXES)
    share = master.shape[0]
    first, last = faces(preact, upstream)
    x_halos = (shifted(last, {"gx": 1}), shifted(first, {"gx": -1}))
    inner, planes_x, sent = inner_planes(
        preact, upstream, activations, master.reshape(1, share), (devices, 1, share)
    )
    kernel = lax.all_to_all(sent, AXES, 0, 0, tiled=True).reshape(channels, 27 * channels)
    planes = (x_halos[0], first, inner, last, x_halos[1])
    y_sent = y_faces(planes, size_z)
    y_halos = (shifted(y_sent[1], {"gy": 1}), shifted(y_sent[0], {"gy": -1}))
    zlo, zhi = z_faces(planes, y_halos)
    z_halos = (shifted(zhi, {"gz": 1}), shifted(zlo, {"gz": -1}))
    sources = (*planes, *y_halos, *z_halos)
    part = wgrad(sources, planes_x, shape, scale)
    part, kernel = lax.optimization_barrier((part, kernel))
    parts = lax.all_to_all(part.reshape(devices, 1, share), AXES, 0, 0, tiled=True)
    grad_input = dgrad(sources, kernel, shape)
    return grad_input, parts


def shifted(value, moves):
    names = tuple(moves)
    sizes = [lax.axis_size(name) for name in names]
    pairs = []
    for source in range(math.prod(sizes)):
        rest, coords = source, []
        for size in reversed(sizes):
            coords.insert(0, rest % size)
            rest //= size
        coords = [
            (at + moves[name]) if moves[name] != "swap" else 1 - at
            for at, name in zip(coords, names)
        ]
        if all(0 <= at < size for at, size in zip(coords, sizes)):
            target = 0
            for at, size in zip(coords, sizes):
                target = target * size + at
            pairs.append((source, target))
    return lax.ppermute(value, names if len(names) > 1 else names[0], pairs)


def local(activations, preact, upstream, master, first_moment, second_moment):
    channels, size_x, size_y, size_z = activations.shape
    devices = math.prod(lax.axis_size(a) for a in AXES)
    share = master.shape[0]
    scale = 1.0 / math.sqrt(size_x * size_y * size_z * devices)
    in_pairs = (
        lax.axis_size("gy") == 2
        and channels % devices == 0
        and share % LANES == 0
        and channels // devices * lax.axis_size("gz") % 8 == 0
        and 2 * size_x * size_y <= LANES
        and (size_x + 2) * size_y <= LANES
    )
    gradients = pair_gradients if in_pairs else general_gradients
    grad_input, parts = gradients(activations, preact, upstream, master, scale)
    weight_grad = jnp.sum(parts.astype(F32), axis=0).reshape(-1)[:share]
    new_first = 0.9 * first_moment + 0.1 * weight_grad
    new_second = 0.999 * second_moment + 0.001 * weight_grad * weight_grad
    corr_first = 1.0 - (0.9**10) ** 10
    corr_second = 1.0 - (0.999**10) ** 10
    update = new_first / corr_first / (jnp.sqrt(new_second / corr_second) + 1e-08) + 0.01 * master
    new_master = master - 0.05 * update
    return (grad_input, weight_grad, new_master, new_first, new_second)


def solution(mesh):
    volume = P(None, "gx", "gy", "gz")
    flat = P(AXES)
    return jax.shard_map(
        local,
        mesh=mesh,
        in_specs=(volume, volume, volume, flat, flat, flat),
        out_specs=(volume, flat, flat, flat, flat),
        check_vma=False,
    )
```

```python
import functools
import math

import jax
import jax.numpy as jnp
from jax import lax
from jax.experimental import pallas as pl
from jax.experimental.pallas import tpu as pltpu
from jax.sharding import PartitionSpec as P

AXES = ("gx", "gy", "gz")
LANES = 128
VMEM = pl.BlockSpec(memory_space=pltpu.VMEM)
HBM = pl.BlockSpec(memory_space=pltpu.HBM)
F32 = jnp.float32
BF16 = jnp.bfloat16
ALL_VMEM = 64 * 2**20


def params(limit=24 * 2**20):
    return pltpu.CompilerParams(vmem_limit_bytes=limit)


def cost(flops, moved):
    return pl.CostEstimate(flops=flops, bytes_accessed=moved, transcendentals=0)


def to_planes(value, tile, write):
    channels, size_y, size_z = value.shape
    tile[...] = value.astype(F32).reshape(channels * size_y, size_z)
    for y in range(size_y):
        write(y, tile[pl.ds(y, channels, stride=size_y), :].astype(BF16))


def masked(p, u):
    return jnp.where(p > 0, u, jnp.zeros_like(u))


def face_kernel(p_ref, u_ref, low_ref, high_ref, p_buf, u_buf, tile, sems):
    size_x, size_z = p_ref.shape[1], p_ref.shape[3]
    copies = []
    for k, x in enumerate((0, size_x - 1)):
        pair = (
            pltpu.make_async_copy(p_ref.at[:, x], p_buf.at[k], sems.at[2 * k]),
            pltpu.make_async_copy(u_ref.at[:, x], u_buf.at[k], sems.at[2 * k + 1]),
        )
        for copy in pair:
            copy.start()
        copies.append(pair)
    for k, out_ref in enumerate((low_ref, high_ref)):
        for copy in copies[k]:
            copy.wait()

        def write(y, value):
            out_ref[:, y * size_z : (y + 1) * size_z] = value

        to_planes(masked(p_buf[k], u_buf[k]), tile.at[k], write)


def faces(preact, upstream):
    channels, size_x, size_y, size_z = preact.shape
    face = jax.ShapeDtypeStruct((channels, size_y * size_z), BF16)
    buffer = pltpu.VMEM((2, channels, size_y, size_z), BF16)
    return pl.pallas_call(
        face_kernel,
        in_specs=[HBM, HBM],
        out_specs=[VMEM] * 2,
        out_shape=[face, face],
        scratch_shapes=[
            buffer,
            buffer,
            pltpu.VMEM((2, channels * size_y, size_z), F32),
            pltpu.SemaphoreType.DMA((4,)),
        ],
        compiler_params=params(ALL_VMEM - 900_000),
        cost_estimate=cost(0, 2**20),
        name="faces",
    )(preact, upstream)


def read_inner(p_ref, u_ref, a_ref, g_ref, x_ref, p_buf, u_buf, a_buf, tile, sems):
    channels, size_x, size_y, size_z = a_ref.shape
    inner = size_x - 2
    copies = []
    for x in range(inner):
        copies.append(
            (
                pltpu.make_async_copy(p_ref.at[:, x + 1], p_buf.at[x], sems.at[x]),
                pltpu.make_async_copy(u_ref.at[:, x + 1], u_buf.at[x], sems.at[inner + x]),
            )
        )
    for x in range(size_x):
        copies.append(
            (pltpu.make_async_copy(a_ref.at[:, x], a_buf.at[x], sems.at[2 * inner + x]),)
        )
    for group in copies:
        for copy in group:
            copy.start()
    for x in range(inner):
        for copy in copies[x]:
            copy.wait()

        def write(y, value):
            g_ref[x, :, y * size_z : (y + 1) * size_z] = value

        to_planes(masked(p_buf[x], u_buf[x]), tile.at[x % 2], write)
    for x in range(size_x):
        copies[inner + x][0].wait()

        def write(y, value):
            x_ref[x, :, y * size_z : (y + 1) * size_z] = value

        to_planes(a_buf[x], tile.at[x % 2], write)


def inner_kernel(*refs):
    read_inner(*refs)


def inner_outputs(channels, size_x, size_y, size_z):
    plane = size_y * size_z
    return [
        jax.ShapeDtypeStruct((size_x - 2, channels, plane), BF16),
        jax.ShapeDtypeStruct((size_x, channels, plane), BF16),
    ]


def inner_scratch(channels, size_x, size_y, size_z):
    return [
        pltpu.VMEM((size_x - 2, channels, size_y, size_z), BF16),
        pltpu.VMEM((size_x - 2, channels, size_y, size_z), BF16),
        pltpu.VMEM((size_x, channels, size_y, size_z), BF16),
        pltpu.VMEM((2, channels * size_y, size_z), F32),
        pltpu.SemaphoreType.DMA((3 * size_x - 4,)),
    ]


def inner_planes(preact, upstream, activations):
    shape = preact.shape
    return pl.pallas_call(
        inner_kernel,
        in_specs=[HBM] * 3,
        out_specs=[VMEM] * 2,
        out_shape=inner_outputs(*shape),
        scratch_shapes=inner_scratch(*shape),
        compiler_params=params(ALL_VMEM - 3_600_000),
        cost_estimate=cost(0, 6 * 2**20),
        name="inner",
    )(preact, upstream, activations)


def body_of(refs, index):
    planes = refs[2].shape[0] + 4
    if 2 <= index < planes - 2:
        return refs[2].at[index - 2]
    return refs[{0: 0, 1: 1, planes - 2: 3, planes - 1: 4}[index]]


def y_halo(refs, index):
    me = lax.axis_index("gy")
    low = jnp.where(me > 0, refs[0][index].astype(F32), 0.0)
    high = jnp.where(me < lax.axis_size("gy") - 1, refs[1][index].astype(F32), 0.0)
    return low, high


def z_picker(rows_y, size_z):
    shape = (rows_y * size_z, 2 * LANES)
    voxel = lax.broadcasted_iota(jnp.int32, shape, 0)
    lane = lax.broadcasted_iota(jnp.int32, shape, 1)
    wanted = jnp.where(lane < LANES, lane * size_z, (lane - LANES) * size_z + size_z - 1)
    return (voxel == wanted).astype(F32).astype(BF16)


def z_tiles(planes, rows_y, size_z, numbers):
    channels = planes[0].shape[0]
    columns = jnp.dot(
        jnp.concatenate(planes, axis=0), z_picker(rows_y, size_z), preferred_element_type=F32
    )
    low = jnp.zeros((channels, LANES), F32)
    high = jnp.zeros((channels, LANES), F32)
    for index, number in enumerate(numbers):
        rows = columns[index * channels : (index + 1) * channels]
        low = low + pltpu.roll(rows[:, :LANES], number * rows_y, 1)
        high = high + pltpu.roll(rows[:, LANES:], number * rows_y, 1)
    return low, high


def put_columns(columns, row_of, rows_y, size_z):
    shape = (2 * LANES, rows_y * size_z)
    source = lax.broadcasted_iota(jnp.int32, shape, 0)
    voxel = lax.broadcasted_iota(jnp.int32, shape, 1)
    number = source % LANES
    place = row_of(number) * size_z + jnp.where(source < LANES, 0, size_z - 1)
    place = jnp.where(number < rows_y, place, -1)
    put = (voxel == place).astype(F32).astype(BF16)
    rows = [jnp.concatenate(pair, axis=1) for pair in columns]
    return jnp.dot(
        jnp.concatenate(rows, axis=0).astype(BF16), put, preferred_element_type=F32
    )


def z_halo(low_ref, high_ref, planes, rows_y, size_z):
    columns = []
    for index in range(planes):
        shift = -index * rows_y % LANES
        columns.append(
            [pltpu.roll(ref[...].astype(F32), shift, 1) for ref in (low_ref, high_ref)]
        )
    return put_columns(columns, lambda number: number, rows_y, size_z)


def pair_z_halo(low_ref, high_ref, planes, size_y, size_z):
    me = lax.axis_index("gy")
    sides = []
    for ref in (low_ref, high_ref):
        first, second = ref[0].astype(F32), ref[1].astype(F32)
        lane = lax.broadcasted_iota(jnp.int32, first.shape, 1)
        own = jnp.where(me == 0, first, second)
        before = jnp.where(me == 0, 0.0, first)
        after = jnp.where(me == 0, second, 0.0)
        columns = []
        for index in range(planes):
            start = index * size_y
            columns.append(
                jnp.where(
                    lane < size_y,
                    pltpu.roll(own, -start % LANES, 1),
                    jnp.where(
                        lane == size_y,
                        pltpu.roll(before, (1 - start) % LANES, 1),
                        pltpu.roll(after, (size_y + 1 - start) % LANES, 1),
                    ),
                )
            )
        sides.append(columns)

    def row_of(number):
        return jnp.where(number < size_y, number + 1, jnp.where(number == size_y, 0, size_y + 1))

    return put_columns(list(zip(*sides)), row_of, size_y + 2, size_z)


def shifted_plane(index, refs, halo, g3):
    channels, plane = refs[0].shape
    size_z = refs[5].shape[-1]
    rows_y = plane // size_z + 2
    base = 3 * channels * index
    lane = lax.broadcasted_iota(jnp.int32, (channels, size_z), 1)
    low, high = y_halo(refs[5:7], index)
    body = body_of(refs[:5], index)
    for row in range(rows_y):
        cols = slice(row * size_z, (row + 1) * size_z)
        if row == 0:
            wide = low
        elif row == rows_y - 1:
            wide = high
        else:
            wide = body[:, (row - 1) * size_z : row * size_z].astype(F32)
        edge = 0.0 if halo is None else halo[index * channels : (index + 1) * channels, cols]
        before = jnp.where(lane == 0, edge, pltpu.roll(wide, 1, 1))
        after = jnp.where(lane == size_z - 1, edge, pltpu.roll(wide, size_z - 1, 1))
        g3[base : base + channels, cols] = before.astype(BF16)
        g3[base + channels : base + 2 * channels, cols] = wide.astype(BF16)
        g3[base + 2 * channels : base + 3 * channels, cols] = after.astype(BF16)


def weight_products(refs, halo, x_ref, g3, x3, acc):
    size_x, channels, plane = x_ref.shape
    size_z = refs[5].shape[-1]
    group = 3 * channels
    zero = jnp.zeros((channels, 2 * size_z), BF16)
    done = 0
    for x in range(size_x):
        while done < x + 3:
            shifted_plane(done, refs, halo, g3)
            done += 1
        value = x_ref[x]
        for b in range(3):
            at = slice(b * channels, (b + 1) * channels)
            start = (2 - b) * size_z
            x3[x, at, start : start + plane] = value
            if start:
                x3[x, at, :start] = zero[:, :start]
            if start < 2 * size_z:
                x3[x, at, start + plane :] = zero[:, start:]
        product = lax.dot_general(
            g3[x * group : (x + 3) * group, :],
            x3[x],
            (((1,), (1,)), ((), ())),
            preferred_element_type=F32,
        )
        if x == 0:
            acc[...] = product
        else:
            acc[...] += product


def to_flat(value, count, channels, flat):
    height, width = value.shape
    wide = value
    if height % LANES:
        wide = jnp.concatenate([wide, jnp.zeros((-height % LANES, width), F32)], axis=0)
    if width % LANES:
        wide = jnp.concatenate([wide, jnp.zeros((wide.shape[0], -width % LANES), F32)], axis=1)
    turned = wide.T
    for b in range(3):
        rows = turned[b * channels : (b + 1) * channels]
        for block in range(9):
            start = block * count
            cell = rows[:, start // LANES * LANES : (start // LANES + 1) * LANES]
            tap = (2 - block // 3) * 9 + b * 3 + 2 - block % 3
            shift = -start % LANES
            flat[pl.ds(tap, channels, stride=27), :] = pltpu.roll(cell, shift, 1) if shift else cell
    return flat[...].T[:count]


def spread_weights(whole, turned, weights):
    channels, taps = whole.shape
    group = 3 * channels
    whole = jnp.concatenate([whole, jnp.zeros((LANES - channels, taps), F32)], axis=0)
    whole = jnp.concatenate([whole, jnp.zeros((LANES, -taps % LANES), F32)], axis=1)
    turned[...] = whole.T
    for b in range(3):
        blocks = []
        for a in range(3):
            for c in range(3):
                tap = (2 - a) * 9 + (2 - b) * 3 + 2 - c
                blocks.append(turned[pl.ds(tap, channels, stride=27), :][:, :channels])
        zero = jnp.zeros((channels, group), F32)
        weights[b, :channels] = jnp.concatenate(blocks + [zero], axis=1).astype(BF16)
        weights[b, channels:] = jnp.concatenate([zero] + blocks, axis=1).astype(BF16)


def input_products(refs, halo, g3, weights, tile, out_ref):
    channels, size_x, size_y, size_z = out_ref.shape
    group = 3 * channels
    plane = size_y * size_z
    done = 0
    for pair in range(size_x // 2):
        while done < 2 * pair + 4:
            shifted_plane(done, refs, halo, g3)
            done += 1
        at = slice(2 * pair * group, (2 * pair + 4) * group)
        total = None
        for b in range(3):
            product = jnp.dot(
                weights[b],
                g3[at, b * size_z : b * size_z + plane],
                preferred_element_type=F32,
            )
            total = product if total is None else total + product
        for half in range(2):
            for y in range(size_y):
                tile[half, pl.ds(y, channels, stride=size_y), :] = total[
                    half * channels : (half + 1) * channels, y * size_z : (y + 1) * size_z
                ]
            out_ref[:, 2 * pair + half] = (
                tile[half].reshape(channels, size_y, size_z).astype(BF16)
            )


def g3_scratch(channels, size_x, size_y, size_z):
    return pltpu.VMEM(((size_x + 2) * 3 * channels, (size_y + 2) * size_z), BF16)


def x3_scratch(channels, size_x, size_y, size_z):
    return pltpu.VMEM((size_x, 3 * channels, (size_y + 2) * size_z), BF16)


def acc_scratch(channels):
    return pltpu.VMEM((9 * channels, 3 * channels), F32)


def flat_scratch(channels):
    return pltpu.VMEM((-(-27 * channels // LANES) * LANES, LANES), F32)


def dgrad_scratch(channels, size_x, size_y, size_z):
    return [
        g3_scratch(channels, size_x, size_y, size_z),
        flat_scratch(channels),
        pltpu.VMEM((3, 2 * channels, 12 * channels), BF16),
        pltpu.VMEM((2, channels * size_y, size_z), F32),
    ]


def wgrad_cost(channels, size_x, size_y, size_z):
    return cost(54 * channels * channels * size_x * (size_y + 2) * size_z, 4 * 2**20)


def dgrad_cost(channels, size_x, size_y, size_z):
    return cost(72 * channels * channels * size_x * size_y * size_z, 4 * 2**20)


def row_for_other(body, size_z):
    plane = body.shape[-1]
    low, high = body[:, :size_z].astype(F32), body[:, plane - size_z :].astype(F32)
    return jnp.where(lax.axis_index("gy") == 0, high, low).astype(BF16)


def pair_inner_kernel(*refs):
    first_ref, last_ref = refs[3:5]
    g_ref, x_ref, side_ref = refs[5:8]
    read_inner(*refs[:3], g_ref, x_ref, *refs[8:])
    size_z = side_ref.shape[-1]
    size_x, channels, plane = x_ref.shape
    size_y = plane // size_z
    bodies = [first_ref] + [g_ref.at[x] for x in range(size_x - 2)] + [last_ref]
    for x, body in enumerate(bodies):
        side_ref[x] = row_for_other(body, size_z)
    low, high = z_tiles([body[...] for body in bodies], size_y, size_z, range(1, size_x + 1))
    side_ref[size_x] = low.astype(BF16)
    side_ref[size_x + 1] = high.astype(BF16)
    low, high = z_tiles([x_ref[x] for x in range(size_x)], size_y, size_z, range(size_x))
    side_ref[size_x + 2] = (low + pltpu.roll(high, size_x * size_y, 1)).astype(BF16)


def pair_inner(preact, upstream, activations, first, last):
    shape = preact.shape
    channels, size_x, _, size_z = shape
    return pl.pallas_call(
        pair_inner_kernel,
        in_specs=[HBM] * 3 + [VMEM] * 2,
        out_specs=[VMEM] * 3,
        out_shape=inner_outputs(*shape)
        + [jax.ShapeDtypeStruct((size_x + 3, channels, size_z), BF16)],
        scratch_shapes=inner_scratch(*shape),
        compiler_params=params(ALL_VMEM - 3_600_000),
        cost_estimate=cost(0, 6 * 2**20),
        name="inner",
    )(preact, upstream, activations, first, last)


def side_kernel(xlo_ref, xhi_ref, own_ref, sent_ref):
    size_x = own_ref.shape[0] - 3
    size_z = own_ref.shape[-1]
    size_y = xlo_ref.shape[-1] // size_z
    sent_ref[0] = row_for_other(xlo_ref, size_z)
    for x in range(size_x):
        sent_ref[x + 1] = own_ref[x]
    sent_ref[size_x + 1] = row_for_other(xhi_ref, size_z)
    tiles = z_tiles([xlo_ref[...], xhi_ref[...]], size_y, size_z, (0, size_x + 1))
    for k in range(2):
        sent_ref[size_x + 2 + k] = (own_ref[size_x + k].astype(F32) + tiles[k]).astype(BF16)
    sent_ref[size_x + 4] = own_ref[size_x + 2]


def side(x_halos, own):
    return pl.pallas_call(
        side_kernel,
        in_specs=[VMEM] * 3,
        out_specs=VMEM,
        out_shape=jax.ShapeDtypeStruct((own.shape[0] + 2, *own.shape[1:]), BF16),
        compiler_params=params(),
        cost_estimate=cost(2**25, 2**19),
        name="side",
    )(*x_halos, own)


def join_kernel(own_ref, other_ref, low_ref, high_ref):
    at = own_ref.shape[0] - 3
    me = lax.axis_index("gy")
    for k, out_ref in enumerate((low_ref, high_ref)):
        out_ref[me] = own_ref[at + k]
        out_ref[1 - me] = other_ref[at + k]


def join(own, other):
    tiles = jax.ShapeDtypeStruct((2, *own.shape[1:]), BF16)
    return pl.pallas_call(
        join_kernel,
        in_specs=[VMEM] * 2,
        out_specs=[VMEM] * 2,
        out_shape=[tiles, tiles],
        compiler_params=params(),
        cost_estimate=cost(0, 2**17),
        name="join",
    )(own, other)


def pair_wgrad_kernel(span, *refs):
    x_ref, mine_ref, theirs_ref, g3, x3, acc = refs[7:]
    channels = x_ref.shape[1]
    weight_products(refs, None, x_ref, g3, x3, acc)
    is_first = lax.axis_index("gy") == 0
    width = 3 * channels
    halves = []
    for half in range(2):
        at = range(half * span, 9 * channels, 2 * span)
        halves.append(jnp.concatenate([acc[start : start + span, :] for start in at], axis=0))
    spare = jnp.zeros((halves[0].shape[0], mine_ref.shape[1] - width), F32)
    for ref, order in ((mine_ref, halves), (theirs_ref, halves[::-1])):
        picked = jnp.where(is_first, order[0], order[1])
        ref[...] = jnp.concatenate([picked, spare], axis=1)


def pair_wgrad(sources, planes_x, shape, span):
    channels = shape[0]
    width = -(-3 * channels // LANES) * LANES
    part = jax.ShapeDtypeStruct((9 * channels // 2, width), F32)
    return pl.pallas_call(
        functools.partial(pair_wgrad_kernel, span),
        in_specs=[VMEM] * 8,
        out_specs=[VMEM] * 2,
        out_shape=[part, part],
        scratch_shapes=[g3_scratch(*shape), x3_scratch(*shape), acc_scratch(channels)],
        compiler_params=params(32 * 2**20),
        cost_estimate=wgrad_cost(*shape),
        name="wgrad",
    )(*sources, planes_x)


def edge_kernel(span, sizes, own_ref, other_ref, zlo_ref, zhi_ref, edge_ref):
    size_x, size_y = sizes
    channels = zlo_ref.shape[1]
    count = channels // 2
    area = size_x * size_y
    is_first = lax.axis_index("gy") == 0
    at = own_ref.shape[0] - 1
    own, other = own_ref[at].astype(F32), other_ref[at].astype(F32)
    inputs = (jnp.where(is_first, own, other), jnp.where(is_first, other, own))
    lane = lax.broadcasted_iota(jnp.int32, (channels, LANES), 1)
    row = lane % size_y
    few = lax.broadcasted_iota(jnp.int32, (count, LANES), 1)
    for number, tile_ref in enumerate((zlo_ref, zhi_ref)):
        value = jnp.where(
            lane < area,
            pltpu.roll(inputs[0], -number * area % LANES, 1),
            pltpu.roll(inputs[1], (1 - number) * area % LANES, 1),
        )
        jump = area - size_y + 1
        below = jnp.where(lane >= area, pltpu.roll(value, jump, 1), 0.0)
        above = jnp.where(lane < area, pltpu.roll(value, LANES - jump, 1), 0.0)
        right = jnp.concatenate(
            [
                jnp.where(row > 0, pltpu.roll(value, 1, 1), below),
                value,
                jnp.where(row < size_y - 1, pltpu.roll(value, LANES - 1, 1), above),
            ],
            axis=0,
        )
        tiles = []
        for device in range(2):
            tile = tile_ref[device].astype(F32)
            halves = [
                jnp.concatenate(
                    [tile[s : s + span] for s in range(half * span, channels, 2 * span)], axis=0
                )
                for half in range(2)
            ]
            tiles.append(jnp.where(is_first, halves[0], halves[1]))
        left = []
        for a in range(3):
            first = pltpu.roll(tiles[0], -a * size_y % LANES, 1)
            second = pltpu.roll(tiles[1], (area - a * size_y) % LANES, 1)
            left.append(jnp.where(few < area, first, jnp.where(few < 2 * area, second, 0.0)))
        product = lax.dot_general(
            jnp.concatenate(left, axis=0).astype(BF16),
            right.astype(BF16),
            (((1,), (1,)), ((), ())),
            preferred_element_type=F32,
        )
        spare = jnp.zeros((3 * count, edge_ref.shape[2] - 3 * channels), F32)
        edge_ref[number] = jnp.concatenate([product, spare], axis=1)


def z_edges(own, other, z_halos, span, sizes, width):
    channels = own.shape[1]
    return pl.pallas_call(
        functools.partial(edge_kernel, span, sizes),
        in_specs=[VMEM] * 4,
        out_specs=VMEM,
        out_shape=jax.ShapeDtypeStruct((2, 3 * channels // 2, width), F32),
        compiler_params=params(),
        cost_estimate=cost(2**27, 2**20),
        name="edges",
    )(own, other, *z_halos)


def finish_kernel(scale, rows, channels, mine_ref, other_ref, edge_ref, part_ref, flat, lines, chunks):
    count = channels // 2
    taps = 27 * channels
    total = mine_ref[...] + other_ref[...]
    blocks = []
    for a in range(3):
        for c in range(3):
            block = total[(3 * a + c) * count : (3 * a + c + 1) * count]
            if c != 1:
                block = block + edge_ref[c // 2, a * count : (a + 1) * count, :]
            blocks.append(block)
    whole = to_flat(jnp.concatenate(blocks, axis=0) * scale, count, channels, flat)
    pieces = whole.shape[1] // LANES
    for k in range(pieces):
        lines[k * count : (k + 1) * count, :] = whole[:, k * LANES : (k + 1) * LANES]
    number, tall, width = part_ref.shape
    parts = []
    for r in range(rows):
        found = [lines[pl.ds(k * count + r, number, stride=rows), :] for k in range(pieces)]
        parts.append(jnp.concatenate(found, axis=1)[:, :taps])
    line = jnp.concatenate(parts, axis=1)
    chunks[...] = jnp.zeros_like(chunks)
    for k in range(line.shape[1] // width):
        chunks[pl.ds(k, number, stride=tall), :] = line[:, k * width : (k + 1) * width]
    part_ref[...] = chunks[...].reshape(part_ref.shape).astype(BF16)


def finish(mine, other, edge, scale, rows, channels, part_shape):
    return pl.pallas_call(
        functools.partial(finish_kernel, scale, rows, channels),
        in_specs=[VMEM] * 3,
        out_specs=VMEM,
        out_shape=jax.ShapeDtypeStruct(part_shape, BF16),
        scratch_shapes=[
            flat_scratch(channels),
            pltpu.VMEM((-(-27 * channels // LANES) * channels // 2, LANES), F32),
            pltpu.VMEM((part_shape[0] * part_shape[1], part_shape[2]), F32),
        ],
        compiler_params=params(),
        cost_estimate=cost(2**24, 2**20),
        name="finish",
    )(mine, other, edge)


def adam_step(master, first, second, weight_grad):
    new_first = 0.9 * first + 0.1 * weight_grad
    new_second = 0.999 * second + 0.001 * weight_grad * weight_grad
    corr_first = 1.0 - (0.9**10) ** 10
    corr_second = 1.0 - (0.999**10) ** 10
    update = new_first / corr_first / (jnp.sqrt(new_second / corr_second) + 1e-08) + 0.01 * master
    return master - 0.05 * update, new_first, new_second


def adam_kernel(parts_ref, master_ref, first_ref, second_ref, *out_refs):
    weight_grad = parts_ref[0].astype(F32)
    for source in range(1, parts_ref.shape[0]):
        weight_grad = weight_grad + parts_ref[source].astype(F32)
    weight_grad = weight_grad[: master_ref.shape[0]]
    results = adam_step(master_ref[...], first_ref[...], second_ref[...], weight_grad)
    for out_ref, result in zip(out_refs, (weight_grad, *results)):
        out_ref[...] = result


def adam(parts, *states):
    share = states[0].shape[0]
    tiled = [state.reshape(share // LANES, LANES) for state in states]
    result = jax.ShapeDtypeStruct(tiled[0].shape, F32)
    outs = pl.pallas_call(
        adam_kernel,
        in_specs=[VMEM] * 4,
        out_specs=[VMEM] * 4,
        out_shape=[result] * 4,
        compiler_params=params(),
        cost_estimate=cost(2**18, 2**18),
        name="adam",
    )(parts, *tiled)
    return tuple(out.reshape(share) for out in outs)


def pair_dgrad_kernel(rows, *refs):
    w_ref, out_ref, g3, turned, weights, tile, chunks, lines = refs[9:]
    channels, size_x, size_y, size_z = out_ref.shape
    taps = 27 * channels
    count, height, width = w_ref.shape
    chunks[...] = w_ref[...].astype(F32).reshape(chunks.shape)
    line = jnp.concatenate(
        [chunks[pl.ds(k, count, stride=height), :] for k in range(rows * taps // width)], axis=1
    )
    pieces = lines.shape[0] // channels
    spare = jnp.zeros((count, pieces * LANES - taps), F32)
    for r in range(rows):
        found = jnp.concatenate([line[:, r * taps : (r + 1) * taps], spare], axis=1)
        for k in range(pieces):
            lines[pl.ds(k * channels + r, count, stride=rows), :] = found[
                :, k * LANES : (k + 1) * LANES
            ]
    whole = [lines[k * channels : (k + 1) * channels, :] for k in range(pieces)]
    spread_weights(jnp.concatenate(whole, axis=1)[:, :taps], turned, weights)
    halo = pair_z_halo(refs[7], refs[8], size_x + 2, size_y, size_z)
    input_products(refs, halo, g3, weights, tile, out_ref)


def pair_dgrad(sources, kernel, shape, rows):
    channels = shape[0]
    return pl.pallas_call(
        functools.partial(pair_dgrad_kernel, rows),
        in_specs=[VMEM] * 10,
        out_specs=VMEM,
        out_shape=jax.ShapeDtypeStruct(shape, BF16),
        scratch_shapes=dgrad_scratch(*shape)
        + [
            pltpu.VMEM((kernel.shape[0] * kernel.shape[1], kernel.shape[2]), F32),
            pltpu.VMEM((-(-27 * channels // LANES) * channels, LANES), F32),
        ],
        compiler_params=params(32 * 2**20),
        cost_estimate=dgrad_cost(*shape),
        name="dgrad",
    )(*sources, kernel)


def pair_program(activations, preact, upstream, master, first_moment, second_moment, scale):
    shape = activations.shape
    channels, size_x, size_y, _ = shape
    devices = math.prod(lax.axis_size(a) for a in AXES)
    rows = channels // devices
    span = lax.axis_size("gz") * rows
    used = master.shape[0] // LANES
    tall = -(-used // 16) * 16
    first, last = faces(preact, upstream)
    x_halos = (shifted(last, {"gx": 1}), shifted(first, {"gx": -1}))
    inner, planes_x, own = pair_inner(preact, upstream, activations, first, last)
    sent = jnp.pad(master.astype(BF16).reshape(used, LANES), ((0, tall - used), (0, 0)))
    kernel = lax.all_to_all(
        jnp.broadcast_to(sent[None], (devices, tall, LANES)), AXES, 0, 0, tiled=True
    )
    planes = (x_halos[0], first, inner, last, x_halos[1])
    own = side(x_halos, own)
    other = shifted(own, {"gy": "swap"})
    zlo, zhi = join(own, other)
    z_halos = (shifted(zhi, {"gz": 1}), shifted(zlo, {"gz": -1}))
    sources = (*planes, other, other)
    mine, theirs = pair_wgrad(sources, planes_x, shape, span)
    theirs, *z_halos = lax.optimization_barrier((theirs, *z_halos))
    theirs = shifted(theirs, {"gy": "swap"})
    edge = z_edges(own, other, z_halos, span, (size_x, size_y), mine.shape[1])
    part = finish(mine, theirs, edge, scale, rows, channels, (devices // 2, tall, LANES))
    part, kernel = lax.optimization_barrier((part, kernel))
    parts = lax.all_to_all(part, ("gx", "gz"), 0, 0, tiled=True)
    grad_input = pair_dgrad((*sources, *z_halos), kernel, shape, rows)
    return grad_input, *adam(parts, master, first_moment, second_moment)


def yface_kernel(*refs):
    low_ref, high_ref = refs[5:]
    size_z = low_ref.shape[-1]
    for index in range(low_ref.shape[0]):
        body = body_of(refs[:5], index)
        plane = body.shape[-1]
        low_ref[index] = body[:, :size_z]
        high_ref[index] = body[:, plane - size_z :]


def y_faces(planes, size_z):
    inner, channels, _ = planes[2].shape
    face = jax.ShapeDtypeStruct((inner + 4, channels, size_z), BF16)
    return pl.pallas_call(
        yface_kernel,
        in_specs=[VMEM] * 5,
        out_specs=[VMEM] * 2,
        out_shape=[face] * 2,
        compiler_params=params(),
        cost_estimate=cost(0, 2**19),
        name="yfaces",
    )(*planes)


def zface_kernel(*refs):
    zlo_ref, zhi_ref = refs[7:]
    size_z = refs[5].shape[-1]
    whole = []
    for index in range(refs[5].shape[0]):
        low, high = y_halo(refs[5:7], index)
        body = body_of(refs[:5], index)[...]
        whole.append(jnp.concatenate([low.astype(BF16), body, high.astype(BF16)], axis=1))
    low, high = z_tiles(whole, whole[0].shape[1] // size_z, size_z, range(len(whole)))
    zlo_ref[...] = low.astype(BF16)
    zhi_ref[...] = high.astype(BF16)


def z_faces(planes, y_halos):
    face = jax.ShapeDtypeStruct((planes[0].shape[0], LANES), BF16)
    return pl.pallas_call(
        zface_kernel,
        in_specs=[VMEM] * 7,
        out_specs=[VMEM] * 2,
        out_shape=[face, face],
        compiler_params=params(),
        cost_estimate=cost(2**27, 2**21),
        name="zfaces",
    )(*planes, *y_halos)


def wgrad_kernel(scale, *refs):
    x_ref, part_ref, g3, x3, acc, flat = refs[9:]
    size_x, channels, plane = x_ref.shape
    size_z = refs[5].shape[-1]
    halo = z_halo(refs[7], refs[8], size_x + 2, plane // size_z + 2, size_z)
    weight_products(refs, halo, x_ref, g3, x3, acc)
    whole = to_flat(acc[...] * scale, channels, channels, flat)
    part_ref[...] = whole[:, : part_ref.shape[1]].astype(BF16)


def wgrad(sources, planes_x, shape, scale):
    channels = shape[0]
    return pl.pallas_call(
        functools.partial(wgrad_kernel, scale),
        in_specs=[VMEM] * 10,
        out_specs=VMEM,
        out_shape=jax.ShapeDtypeStruct((channels, 27 * channels), BF16),
        scratch_shapes=[
            g3_scratch(*shape),
            x3_scratch(*shape),
            acc_scratch(channels),
            flat_scratch(channels),
        ],
        compiler_params=params(32 * 2**20),
        cost_estimate=wgrad_cost(*shape),
        name="wgrad",
    )(*sources, planes_x)


def dgrad_kernel(*refs):
    w_ref, out_ref, g3, turned, weights, tile = refs[9:]
    _, size_x, size_y, size_z = out_ref.shape
    spread_weights(w_ref[...].astype(F32), turned, weights)
    halo = z_halo(refs[7], refs[8], size_x + 2, size_y + 2, size_z)
    input_products(refs, halo, g3, weights, tile, out_ref)


def dgrad(sources, kernel, shape):
    return pl.pallas_call(
        dgrad_kernel,
        in_specs=[VMEM] * 10,
        out_specs=VMEM,
        out_shape=jax.ShapeDtypeStruct(shape, BF16),
        scratch_shapes=dgrad_scratch(*shape),
        compiler_params=params(32 * 2**20),
        cost_estimate=dgrad_cost(*shape),
        name="dgrad",
    )(*sources, kernel)


def general_program(activations, preact, upstream, master, first_moment, second_moment, scale):
    shape = activations.shape
    channels, _, _, size_z = shape
    devices = math.prod(lax.axis_size(a) for a in AXES)
    share = master.shape[0]
    first, last = faces(preact, upstream)
    x_halos = (shifted(last, {"gx": 1}), shifted(first, {"gx": -1}))
    inner, planes_x = inner_planes(preact, upstream, activations)
    sent = jnp.broadcast_to(master.astype(BF16).reshape(1, 1, share), (devices, 1, share))
    kernel = lax.all_to_all(sent, AXES, 0, 0, tiled=True).reshape(channels, 27 * channels)
    planes = (x_halos[0], first, inner, last, x_halos[1])
    y_sent = y_faces(planes, size_z)
    y_halos = (shifted(y_sent[1], {"gy": 1}), shifted(y_sent[0], {"gy": -1}))
    zlo, zhi = z_faces(planes, y_halos)
    z_halos = (shifted(zhi, {"gz": 1}), shifted(zlo, {"gz": -1}))
    sources = (*planes, *y_halos, *z_halos)
    part = wgrad(sources, planes_x, shape, scale)
    part, kernel = lax.optimization_barrier((part, kernel))
    parts = lax.all_to_all(part.reshape(devices, 1, share), AXES, 0, 0, tiled=True)
    grad_input = dgrad(sources, kernel, shape)
    weight_grad = jnp.sum(parts.astype(F32), axis=0).reshape(-1)
    results = adam_step(master, first_moment, second_moment, weight_grad)
    return grad_input, weight_grad, *results


def shifted(value, moves):
    names = tuple(moves)
    sizes = [lax.axis_size(name) for name in names]
    pairs = []
    for source in range(math.prod(sizes)):
        rest, coords = source, []
        for size in reversed(sizes):
            coords.insert(0, rest % size)
            rest //= size
        coords = [
            (at + moves[name]) if moves[name] != "swap" else 1 - at
            for at, name in zip(coords, names)
        ]
        if all(0 <= at < size for at, size in zip(coords, sizes)):
            target = 0
            for at, size in zip(coords, sizes):
                target = target * size + at
            pairs.append((source, target))
    return lax.ppermute(value, names if len(names) > 1 else names[0], pairs)


def local(activations, preact, upstream, master, first_moment, second_moment):
    channels, size_x, size_y, size_z = activations.shape
    devices = math.prod(lax.axis_size(a) for a in AXES)
    share = master.shape[0]
    scale = 1.0 / math.sqrt(size_x * size_y * size_z * devices)
    in_pairs = (
        lax.axis_size("gy") == 2
        and channels % devices == 0
        and share % LANES == 0
        and channels // devices * lax.axis_size("gz") % 8 == 0
        and 2 * size_x * size_y <= LANES
        and (size_x + 2) * size_y <= LANES
    )
    program = pair_program if in_pairs else general_program
    return program(
        activations, preact, upstream, master, first_moment, second_moment, scale
    )


def solution(mesh):
    volume = P(None, "gx", "gy", "gz")
    flat = P(AXES)
    return jax.shard_map(
        local,
        mesh=mesh,
        in_specs=(volume, volume, volume, flat, flat, flat),
        out_specs=(volume, flat, flat, flat, flat),
        check_vma=False,
    )
```

```python
import functools
import math

import jax
import jax.numpy as jnp
from jax import lax
from jax.experimental import pallas as pl
from jax.experimental.pallas import tpu as pltpu
from jax.sharding import PartitionSpec as P

AXES = ("gx", "gy", "gz")
LANES = 128
VMEM = pl.BlockSpec(memory_space=pltpu.VMEM)
HBM = pl.BlockSpec(memory_space=pltpu.HBM)
F32 = jnp.float32
BF16 = jnp.bfloat16
FACES_VMEM = 56_200_000
INNER_VMEM = 53_000_000


def params(limit=24 * 2**20):
    return pltpu.CompilerParams(vmem_limit_bytes=limit)


def cost(flops, moved):
    return pl.CostEstimate(flops=flops, bytes_accessed=moved, transcendentals=0)


def to_planes(value, tile, write):
    channels, size_y, size_z = value.shape
    tile[...] = value.astype(F32).reshape(channels * size_y, size_z)
    for y in range(size_y):
        write(y, tile[pl.ds(y, channels, stride=size_y), :].astype(BF16))


def masked(p, u):
    return jnp.where(p > 0, u, jnp.zeros_like(u))


def face_kernel(p_ref, u_ref, low_ref, high_ref, p_buf, u_buf, tile, sems):
    size_x, size_z = p_ref.shape[1], p_ref.shape[3]
    copies = []
    for k, x in enumerate((0, size_x - 1)):
        pair = (
            pltpu.make_async_copy(p_ref.at[:, x], p_buf.at[k], sems.at[2 * k]),
            pltpu.make_async_copy(u_ref.at[:, x], u_buf.at[k], sems.at[2 * k + 1]),
        )
        for copy in pair:
            copy.start()
        copies.append(pair)
    for k, out_ref in enumerate((low_ref, high_ref)):
        for copy in copies[k]:
            copy.wait()

        def write(y, value):
            out_ref[:, y * size_z : (y + 1) * size_z] = value

        to_planes(masked(p_buf[k], u_buf[k]), tile.at[k], write)


def faces(preact, upstream):
    channels, size_x, size_y, size_z = preact.shape
    face = jax.ShapeDtypeStruct((channels, size_y * size_z), BF16)
    buffer = pltpu.VMEM((2, channels, size_y, size_z), BF16)
    return pl.pallas_call(
        face_kernel,
        in_specs=[HBM, HBM],
        out_specs=[VMEM] * 2,
        out_shape=[face, face],
        scratch_shapes=[
            buffer,
            buffer,
            pltpu.VMEM((2, channels * size_y, size_z), F32),
            pltpu.SemaphoreType.DMA((4,)),
        ],
        compiler_params=params(FACES_VMEM),
        cost_estimate=cost(0, 2**20),
        name="faces",
    )(preact, upstream)


def read_inner(p_ref, u_ref, a_ref, g_ref, x_ref, p_buf, u_buf, a_buf, tile, sems):
    channels, size_x, size_y, size_z = a_ref.shape
    inner = size_x - 2
    copies = []
    for x in range(inner):
        copies.append(
            (
                pltpu.make_async_copy(p_ref.at[:, x + 1], p_buf.at[x], sems.at[x]),
                pltpu.make_async_copy(u_ref.at[:, x + 1], u_buf.at[x], sems.at[inner + x]),
            )
        )
    for x in range(size_x):
        copies.append(
            (pltpu.make_async_copy(a_ref.at[:, x], a_buf.at[x], sems.at[2 * inner + x]),)
        )
    for group in copies:
        for copy in group:
            copy.start()
    for x in range(inner):
        for copy in copies[x]:
            copy.wait()

        def write(y, value):
            g_ref[x, :, y * size_z : (y + 1) * size_z] = value

        to_planes(masked(p_buf[x], u_buf[x]), tile.at[x % 2], write)
    for x in range(size_x):
        copies[inner + x][0].wait()

        def write(y, value):
            x_ref[x, :, y * size_z : (y + 1) * size_z] = value

        to_planes(a_buf[x], tile.at[x % 2], write)


def inner_kernel(*refs):
    read_inner(*refs)


def inner_outputs(channels, size_x, size_y, size_z):
    plane = size_y * size_z
    return [
        jax.ShapeDtypeStruct((size_x - 2, channels, plane), BF16),
        jax.ShapeDtypeStruct((size_x, channels, plane), BF16),
    ]


def inner_scratch(channels, size_x, size_y, size_z):
    return [
        pltpu.VMEM((size_x - 2, channels, size_y, size_z), BF16),
        pltpu.VMEM((size_x - 2, channels, size_y, size_z), BF16),
        pltpu.VMEM((size_x, channels, size_y, size_z), BF16),
        pltpu.VMEM((2, channels * size_y, size_z), F32),
        pltpu.SemaphoreType.DMA((3 * size_x - 4,)),
    ]


def inner_planes(preact, upstream, activations):
    shape = preact.shape
    return pl.pallas_call(
        inner_kernel,
        in_specs=[HBM] * 3,
        out_specs=[VMEM] * 2,
        out_shape=inner_outputs(*shape),
        scratch_shapes=inner_scratch(*shape),
        compiler_params=params(INNER_VMEM),
        cost_estimate=cost(0, 6 * 2**20),
        name="inner",
    )(preact, upstream, activations)


def body_of(refs, index):
    planes = refs[2].shape[0] + 4
    if 2 <= index < planes - 2:
        return refs[2].at[index - 2]
    return refs[{0: 0, 1: 1, planes - 2: 3, planes - 1: 4}[index]]


def y_halo(refs, index):
    me = lax.axis_index("gy")
    low = jnp.where(me > 0, refs[0][index].astype(F32), 0.0)
    high = jnp.where(me < lax.axis_size("gy") - 1, refs[1][index].astype(F32), 0.0)
    return low, high


def z_picker(rows_y, size_z):
    shape = (rows_y * size_z, 2 * LANES)
    voxel = lax.broadcasted_iota(jnp.int32, shape, 0)
    lane = lax.broadcasted_iota(jnp.int32, shape, 1)
    wanted = jnp.where(lane < LANES, lane * size_z, (lane - LANES) * size_z + size_z - 1)
    return (voxel == wanted).astype(F32).astype(BF16)


def z_tiles(planes, rows_y, size_z, numbers):
    channels = planes[0].shape[0]
    columns = jnp.dot(
        jnp.concatenate(planes, axis=0), z_picker(rows_y, size_z), preferred_element_type=F32
    )
    low = jnp.zeros((channels, LANES), F32)
    high = jnp.zeros((channels, LANES), F32)
    for index, number in enumerate(numbers):
        rows = columns[index * channels : (index + 1) * channels]
        low = low + pltpu.roll(rows[:, :LANES], number * rows_y, 1)
        high = high + pltpu.roll(rows[:, LANES:], number * rows_y, 1)
    return low, high


def put_columns(columns, row_of, rows_y, size_z):
    shape = (2 * LANES, rows_y * size_z)
    source = lax.broadcasted_iota(jnp.int32, shape, 0)
    voxel = lax.broadcasted_iota(jnp.int32, shape, 1)
    number = source % LANES
    place = row_of(number) * size_z + jnp.where(source < LANES, 0, size_z - 1)
    place = jnp.where(number < rows_y, place, -1)
    put = (voxel == place).astype(F32).astype(BF16)
    rows = [jnp.concatenate(pair, axis=1) for pair in columns]
    return jnp.dot(
        jnp.concatenate(rows, axis=0).astype(BF16), put, preferred_element_type=F32
    )


def z_halo(low_ref, high_ref, planes, rows_y, size_z):
    columns = []
    for index in range(planes):
        shift = -index * rows_y % LANES
        columns.append(
            [pltpu.roll(ref[...].astype(F32), shift, 1) for ref in (low_ref, high_ref)]
        )
    return put_columns(columns, lambda number: number, rows_y, size_z)


def pair_z_halo(low_ref, high_ref, planes, size_y, size_z):
    me = lax.axis_index("gy")
    sides = []
    for ref in (low_ref, high_ref):
        first, second = ref[0].astype(F32), ref[1].astype(F32)
        lane = lax.broadcasted_iota(jnp.int32, first.shape, 1)
        own = jnp.where(me == 0, first, second)
        before = jnp.where(me == 0, 0.0, first)
        after = jnp.where(me == 0, second, 0.0)
        columns = []
        for index in range(planes):
            start = index * size_y
            columns.append(
                jnp.where(
                    lane < size_y,
                    pltpu.roll(own, -start % LANES, 1),
                    jnp.where(
                        lane == size_y,
                        pltpu.roll(before, (1 - start) % LANES, 1),
                        pltpu.roll(after, (size_y + 1 - start) % LANES, 1),
                    ),
                )
            )
        sides.append(columns)

    def row_of(number):
        return jnp.where(number < size_y, number + 1, jnp.where(number == size_y, 0, size_y + 1))

    return put_columns(list(zip(*sides)), row_of, size_y + 2, size_z)


def shifted_plane(index, refs, halo, g3):
    channels, plane = refs[0].shape
    size_z = refs[5].shape[-1]
    rows_y = plane // size_z + 2
    base = 3 * channels * index
    lane = lax.broadcasted_iota(jnp.int32, (channels, size_z), 1)
    low, high = y_halo(refs[5:7], index)
    body = body_of(refs[:5], index)
    for row in range(rows_y):
        cols = slice(row * size_z, (row + 1) * size_z)
        if row == 0:
            wide = low
        elif row == rows_y - 1:
            wide = high
        else:
            wide = body[:, (row - 1) * size_z : row * size_z].astype(F32)
        edge = 0.0 if halo is None else halo[index * channels : (index + 1) * channels, cols]
        before = jnp.where(lane == 0, edge, pltpu.roll(wide, 1, 1))
        after = jnp.where(lane == size_z - 1, edge, pltpu.roll(wide, size_z - 1, 1))
        g3[base : base + channels, cols] = before.astype(BF16)
        g3[base + channels : base + 2 * channels, cols] = wide.astype(BF16)
        g3[base + 2 * channels : base + 3 * channels, cols] = after.astype(BF16)


def weight_products(refs, halo, x_ref, g3, x3, acc):
    size_x, channels, plane = x_ref.shape
    size_z = refs[5].shape[-1]
    group = 3 * channels
    zero = jnp.zeros((channels, 2 * size_z), BF16)
    done = 0
    for x in range(size_x):
        while done < x + 3:
            shifted_plane(done, refs, halo, g3)
            done += 1
        value = x_ref[x]
        for b in range(3):
            at = slice(b * channels, (b + 1) * channels)
            start = (2 - b) * size_z
            x3[x, at, start : start + plane] = value
            if start:
                x3[x, at, :start] = zero[:, :start]
            if start < 2 * size_z:
                x3[x, at, start + plane :] = zero[:, start:]
        product = lax.dot_general(
            g3[x * group : (x + 3) * group, :],
            x3[x],
            (((1,), (1,)), ((), ())),
            preferred_element_type=F32,
        )
        if x == 0:
            acc[...] = product
        else:
            acc[...] += product


def to_flat(value, count, channels, flat):
    height, width = value.shape
    wide = value
    if height % LANES:
        wide = jnp.concatenate([wide, jnp.zeros((-height % LANES, width), F32)], axis=0)
    if width % LANES:
        wide = jnp.concatenate([wide, jnp.zeros((wide.shape[0], -width % LANES), F32)], axis=1)
    turned = wide.T
    for b in range(3):
        rows = turned[b * channels : (b + 1) * channels]
        for block in range(9):
            start = block * count
            cell = rows[:, start // LANES * LANES : (start // LANES + 1) * LANES]
            tap = (2 - block // 3) * 9 + b * 3 + 2 - block % 3
            shift = -start % LANES
            flat[pl.ds(tap, channels, stride=27), :] = pltpu.roll(cell, shift, 1) if shift else cell
    return flat[...].T[:count]


def spread_weights(whole, turned, weights):
    channels, taps = whole.shape
    group = 3 * channels
    whole = jnp.concatenate([whole, jnp.zeros((LANES - channels, taps), F32)], axis=0)
    whole = jnp.concatenate([whole, jnp.zeros((LANES, -taps % LANES), F32)], axis=1)
    turned[...] = whole.T
    for b in range(3):
        blocks = []
        for a in range(3):
            for c in range(3):
                tap = (2 - a) * 9 + (2 - b) * 3 + 2 - c
                blocks.append(turned[pl.ds(tap, channels, stride=27), :][:, :channels])
        zero = jnp.zeros((channels, group), F32)
        weights[b, :channels] = jnp.concatenate(blocks + [zero], axis=1).astype(BF16)
        weights[b, channels:] = jnp.concatenate([zero] + blocks, axis=1).astype(BF16)


def input_products(refs, halo, g3, weights, tile, out_ref):
    channels, size_x, size_y, size_z = out_ref.shape
    group = 3 * channels
    plane = size_y * size_z
    done = 0
    for pair in range(size_x // 2):
        while done < 2 * pair + 4:
            shifted_plane(done, refs, halo, g3)
            done += 1
        at = slice(2 * pair * group, (2 * pair + 4) * group)
        total = None
        for b in range(3):
            product = jnp.dot(
                weights[b],
                g3[at, b * size_z : b * size_z + plane],
                preferred_element_type=F32,
            )
            total = product if total is None else total + product
        for half in range(2):
            for y in range(size_y):
                tile[half, pl.ds(y, channels, stride=size_y), :] = total[
                    half * channels : (half + 1) * channels, y * size_z : (y + 1) * size_z
                ]
            out_ref[:, 2 * pair + half] = (
                tile[half].reshape(channels, size_y, size_z).astype(BF16)
            )


def g3_scratch(channels, size_x, size_y, size_z):
    return pltpu.VMEM(((size_x + 2) * 3 * channels, (size_y + 2) * size_z), BF16)


def x3_scratch(channels, size_x, size_y, size_z):
    return pltpu.VMEM((size_x, 3 * channels, (size_y + 2) * size_z), BF16)


def acc_scratch(channels):
    return pltpu.VMEM((9 * channels, 3 * channels), F32)


def flat_scratch(channels):
    return pltpu.VMEM((-(-27 * channels // LANES) * LANES, LANES), F32)


def dgrad_scratch(channels, size_x, size_y, size_z):
    return [
        g3_scratch(channels, size_x, size_y, size_z),
        flat_scratch(channels),
        pltpu.VMEM((3, 2 * channels, 12 * channels), BF16),
        pltpu.VMEM((2, channels * size_y, size_z), F32),
    ]


def wgrad_cost(channels, size_x, size_y, size_z):
    return cost(54 * channels * channels * size_x * (size_y + 2) * size_z, 4 * 2**20)


def dgrad_cost(channels, size_x, size_y, size_z):
    return cost(72 * channels * channels * size_x * size_y * size_z, 4 * 2**20)


def row_for_other(body, size_z):
    plane = body.shape[-1]
    low, high = body[:, :size_z].astype(F32), body[:, plane - size_z :].astype(F32)
    return jnp.where(lax.axis_index("gy") == 0, high, low).astype(BF16)


def pair_inner_kernel(*refs):
    first_ref, last_ref, m_ref = refs[3:6]
    g_ref, x_ref, side_ref, sent_ref = refs[6:10]
    tile_ref, tile_sems = refs[15:]
    share = m_ref[...]
    height = tile_ref.shape[0] - share.shape[0]
    if height:
        share = jnp.concatenate([share, jnp.zeros((height, share.shape[1]), F32)], axis=0)
    tile_ref[...] = share.astype(BF16)
    copies = [
        pltpu.make_async_copy(tile_ref, sent_ref.at[device], tile_sems.at[device])
        for device in range(sent_ref.shape[0])
    ]
    for copy in copies:
        copy.start()
    read_inner(*refs[:3], g_ref, x_ref, *refs[10:15])
    size_z = side_ref.shape[-1]
    size_x, channels, plane = x_ref.shape
    size_y = plane // size_z
    bodies = [first_ref] + [g_ref.at[x] for x in range(size_x - 2)] + [last_ref]
    for x, body in enumerate(bodies):
        side_ref[x] = row_for_other(body, size_z)
    low, high = z_tiles([body[...] for body in bodies], size_y, size_z, range(1, size_x + 1))
    side_ref[size_x] = low.astype(BF16)
    side_ref[size_x + 1] = high.astype(BF16)
    low, high = z_tiles([x_ref[x] for x in range(size_x)], size_y, size_z, range(size_x))
    side_ref[size_x + 2] = (low + pltpu.roll(high, size_x * size_y, 1)).astype(BF16)
    for copy in copies:
        copy.wait()


def pair_inner(preact, upstream, activations, first, last, share, sent_shape):
    shape = preact.shape
    channels, size_x, _, size_z = shape
    return pl.pallas_call(
        pair_inner_kernel,
        in_specs=[HBM] * 3 + [VMEM] * 3,
        out_specs=[VMEM] * 3 + [HBM],
        out_shape=inner_outputs(*shape)
        + [
            jax.ShapeDtypeStruct((size_x + 3, channels, size_z), BF16),
            jax.ShapeDtypeStruct(sent_shape, BF16),
        ],
        scratch_shapes=inner_scratch(*shape)
        + [pltpu.VMEM(sent_shape[1:], BF16), pltpu.SemaphoreType.DMA((sent_shape[0],))],
        compiler_params=params(INNER_VMEM),
        cost_estimate=cost(0, 6 * 2**20),
        name="inner",
    )(preact, upstream, activations, first, last, share)


def side_kernel(xlo_ref, xhi_ref, own_ref, sent_ref):
    size_x = own_ref.shape[0] - 3
    size_z = own_ref.shape[-1]
    size_y = xlo_ref.shape[-1] // size_z
    sent_ref[0] = row_for_other(xlo_ref, size_z)
    for x in range(size_x):
        sent_ref[x + 1] = own_ref[x]
    sent_ref[size_x + 1] = row_for_other(xhi_ref, size_z)
    tiles = z_tiles([xlo_ref[...], xhi_ref[...]], size_y, size_z, (0, size_x + 1))
    for k in range(2):
        sent_ref[size_x + 2 + k] = (own_ref[size_x + k].astype(F32) + tiles[k]).astype(BF16)
    sent_ref[size_x + 4] = own_ref[size_x + 2]


def side(x_halos, own):
    return pl.pallas_call(
        side_kernel,
        in_specs=[VMEM] * 3,
        out_specs=VMEM,
        out_shape=jax.ShapeDtypeStruct((own.shape[0] + 2, *own.shape[1:]), BF16),
        compiler_params=params(),
        cost_estimate=cost(2**25, 2**19),
        name="side",
    )(*x_halos, own)


def both_columns(is_first, own, other, number, area):
    first = jnp.where(is_first, own, other).astype(F32)
    second = jnp.where(is_first, other, own).astype(F32)
    lane = lax.broadcasted_iota(jnp.int32, first.shape, 1)
    return jnp.where(
        lane < area,
        pltpu.roll(first, -number * area % LANES, 1),
        pltpu.roll(second, (1 - number) * area % LANES, 1),
    )


def join_kernel(area, own_ref, other_ref, low_ref, high_ref):
    at = own_ref.shape[0] - 3
    me = lax.axis_index("gy")
    for k, out_ref in enumerate((low_ref, high_ref)):
        out_ref[me] = own_ref[at + k]
        out_ref[1 - me] = other_ref[at + k]
    own, other = own_ref[at + 2].astype(F32), other_ref[at + 2].astype(F32)
    high_ref[2] = both_columns(me == 0, own, other, 1, area).astype(BF16)


def join(own, other, area):
    return pl.pallas_call(
        functools.partial(join_kernel, area),
        in_specs=[VMEM] * 2,
        out_specs=[VMEM] * 2,
        out_shape=[jax.ShapeDtypeStruct((n, *own.shape[1:]), BF16) for n in (2, 3)],
        compiler_params=params(),
        cost_estimate=cost(0, 2**17),
        name="join",
    )(own, other)


def pair_wgrad_kernel(span, *refs):
    x_ref, mine_ref, theirs_ref, g3, x3, acc = refs[7:]
    channels = x_ref.shape[1]
    weight_products(refs, None, x_ref, g3, x3, acc)
    is_first = lax.axis_index("gy") == 0
    width = 3 * channels
    halves = []
    for half in range(2):
        at = range(half * span, 9 * channels, 2 * span)
        halves.append(jnp.concatenate([acc[start : start + span, :] for start in at], axis=0))
    spare = jnp.zeros((halves[0].shape[0], mine_ref.shape[1] - width), F32)
    for ref, order in ((mine_ref, halves), (theirs_ref, halves[::-1])):
        picked = jnp.where(is_first, order[0], order[1])
        ref[...] = jnp.concatenate([picked, spare], axis=1)


def pair_wgrad(sources, planes_x, shape, span):
    channels = shape[0]
    width = -(-3 * channels // LANES) * LANES
    part = jax.ShapeDtypeStruct((9 * channels // 2, width), F32)
    return pl.pallas_call(
        functools.partial(pair_wgrad_kernel, span),
        in_specs=[VMEM] * 8,
        out_specs=[VMEM] * 2,
        out_shape=[part, part],
        scratch_shapes=[g3_scratch(*shape), x3_scratch(*shape), acc_scratch(channels)],
        compiler_params=params(32 * 2**20),
        cost_estimate=wgrad_cost(*shape),
        name="wgrad",
    )(*sources, planes_x)


def edge_kernel(span, sizes, own_ref, other_ref, ztiles_ref, below_ref, edge_ref):
    size_x, size_y = sizes
    channels = below_ref.shape[1]
    count = channels // 2
    area = size_x * size_y
    is_first = lax.axis_index("gy") == 0
    at = own_ref.shape[0] - 1
    own, other = own_ref[at].astype(F32), other_ref[at].astype(F32)
    columns = (both_columns(is_first, own, other, 0, area), below_ref[2].astype(F32))
    lane = lax.broadcasted_iota(jnp.int32, (channels, LANES), 1)
    row = lane % size_y
    few = lax.broadcasted_iota(jnp.int32, (count, LANES), 1)
    for number, (tile_ref, value) in enumerate(zip((below_ref, ztiles_ref), columns)):
        jump = area - size_y + 1
        before = jnp.where(lane >= area, pltpu.roll(value, jump, 1), 0.0)
        after = jnp.where(lane < area, pltpu.roll(value, LANES - jump, 1), 0.0)
        right = jnp.concatenate(
            [
                jnp.where(row > 0, pltpu.roll(value, 1, 1), before),
                value,
                jnp.where(row < size_y - 1, pltpu.roll(value, LANES - 1, 1), after),
            ],
            axis=0,
        )
        tiles = []
        for device in range(2):
            tile = tile_ref[device].astype(F32)
            halves = [
                jnp.concatenate(
                    [tile[s : s + span] for s in range(half * span, channels, 2 * span)], axis=0
                )
                for half in range(2)
            ]
            tiles.append(jnp.where(is_first, halves[0], halves[1]))
        left = []
        for a in range(3):
            first = pltpu.roll(tiles[0], -a * size_y % LANES, 1)
            second = pltpu.roll(tiles[1], (area - a * size_y) % LANES, 1)
            left.append(jnp.where(few < area, first, jnp.where(few < 2 * area, second, 0.0)))
        product = lax.dot_general(
            jnp.concatenate(left, axis=0).astype(BF16),
            right.astype(BF16),
            (((1,), (1,)), ((), ())),
            preferred_element_type=F32,
        )
        spare = jnp.zeros((3 * count, edge_ref.shape[2] - 3 * channels), F32)
        edge_ref[number] = jnp.concatenate([product, spare], axis=1)


def z_edges(own, other, ztiles, below, span, sizes, width):
    channels = own.shape[1]
    return pl.pallas_call(
        functools.partial(edge_kernel, span, sizes),
        in_specs=[VMEM] * 4,
        out_specs=VMEM,
        out_shape=jax.ShapeDtypeStruct((2, 3 * channels // 2, width), F32),
        compiler_params=params(),
        cost_estimate=cost(2**27, 2**20),
        name="edges",
    )(own, other, ztiles, below)


def finish_kernel(scale, rows, channels, mine_ref, other_ref, edge_ref, part_ref, flat, lines, chunks):
    count = channels // 2
    taps = 27 * channels
    total = mine_ref[...] + other_ref[...]
    blocks = []
    for a in range(3):
        for c in range(3):
            block = total[(3 * a + c) * count : (3 * a + c + 1) * count]
            if c != 1:
                block = block + edge_ref[c // 2, a * count : (a + 1) * count, :]
            blocks.append(block)
    whole = to_flat(jnp.concatenate(blocks, axis=0) * scale, count, channels, flat)
    pieces = whole.shape[1] // LANES
    for k in range(pieces):
        lines[k * count : (k + 1) * count, :] = whole[:, k * LANES : (k + 1) * LANES]
    number, tall, width = part_ref.shape
    parts = []
    for r in range(rows):
        found = [lines[pl.ds(k * count + r, number, stride=rows), :] for k in range(pieces)]
        parts.append(jnp.concatenate(found, axis=1)[:, :taps])
    line = jnp.concatenate(parts, axis=1)
    chunks[...] = jnp.zeros_like(chunks)
    for k in range(line.shape[1] // width):
        chunks[pl.ds(k, number, stride=tall), :] = line[:, k * width : (k + 1) * width]
    part_ref[...] = chunks[...].reshape(part_ref.shape).astype(BF16)


def finish(mine, other, edge, scale, rows, channels, part_shape):
    return pl.pallas_call(
        functools.partial(finish_kernel, scale, rows, channels),
        in_specs=[VMEM] * 3,
        out_specs=VMEM,
        out_shape=jax.ShapeDtypeStruct(part_shape, BF16),
        scratch_shapes=[
            flat_scratch(channels),
            pltpu.VMEM((-(-27 * channels // LANES) * channels // 2, LANES), F32),
            pltpu.VMEM((part_shape[0] * part_shape[1], part_shape[2]), F32),
        ],
        compiler_params=params(),
        cost_estimate=cost(2**24, 2**20),
        name="finish",
    )(mine, other, edge)


def adam_step(master, first, second, weight_grad):
    new_first = 0.9 * first + 0.1 * weight_grad
    new_second = 0.999 * second + 0.001 * weight_grad * weight_grad
    corr_first = 1.0 - (0.9**10) ** 10
    corr_second = 1.0 - (0.999**10) ** 10
    update = new_first / corr_first / (jnp.sqrt(new_second / corr_second) + 1e-08) + 0.01 * master
    return master - 0.05 * update, new_first, new_second


def adam_kernel(parts_ref, master_ref, first_ref, second_ref, *out_refs):
    weight_grad = parts_ref[0].astype(F32)
    for source in range(1, parts_ref.shape[0]):
        weight_grad = weight_grad + parts_ref[source].astype(F32)
    weight_grad = weight_grad[: master_ref.shape[0]]
    results = adam_step(master_ref[...], first_ref[...], second_ref[...], weight_grad)
    for out_ref, result in zip(out_refs, (weight_grad, *results)):
        out_ref[...] = result


def adam(parts, *states):
    share = states[0].shape[0]
    tiled = [state.reshape(share // LANES, LANES) for state in states]
    result = jax.ShapeDtypeStruct(tiled[0].shape, F32)
    outs = pl.pallas_call(
        adam_kernel,
        in_specs=[VMEM] * 4,
        out_specs=[VMEM] * 4,
        out_shape=[result] * 4,
        compiler_params=params(),
        cost_estimate=cost(2**18, 2**18),
        name="adam",
    )(parts, *tiled)
    return tuple(out.reshape(share) for out in outs)


def pair_dgrad_kernel(rows, *refs):
    w_ref, out_ref, g3, turned, weights, tile, chunks, lines = refs[9:]
    channels, size_x, size_y, size_z = out_ref.shape
    taps = 27 * channels
    count, height, width = w_ref.shape
    chunks[...] = w_ref[...].astype(F32).reshape(chunks.shape)
    line = jnp.concatenate(
        [chunks[pl.ds(k, count, stride=height), :] for k in range(rows * taps // width)], axis=1
    )
    pieces = lines.shape[0] // channels
    spare = jnp.zeros((count, pieces * LANES - taps), F32)
    for r in range(rows):
        found = jnp.concatenate([line[:, r * taps : (r + 1) * taps], spare], axis=1)
        for k in range(pieces):
            lines[pl.ds(k * channels + r, count, stride=rows), :] = found[
                :, k * LANES : (k + 1) * LANES
            ]
    whole = [lines[k * channels : (k + 1) * channels, :] for k in range(pieces)]
    spread_weights(jnp.concatenate(whole, axis=1)[:, :taps], turned, weights)
    halo = pair_z_halo(refs[7], refs[8], size_x + 2, size_y, size_z)
    input_products(refs, halo, g3, weights, tile, out_ref)


def pair_dgrad(sources, kernel, shape, rows):
    channels = shape[0]
    return pl.pallas_call(
        functools.partial(pair_dgrad_kernel, rows),
        in_specs=[VMEM] * 10,
        out_specs=VMEM,
        out_shape=jax.ShapeDtypeStruct(shape, BF16),
        scratch_shapes=dgrad_scratch(*shape)
        + [
            pltpu.VMEM((kernel.shape[0] * kernel.shape[1], kernel.shape[2]), F32),
            pltpu.VMEM((-(-27 * channels // LANES) * channels, LANES), F32),
        ],
        compiler_params=params(32 * 2**20),
        cost_estimate=dgrad_cost(*shape),
        name="dgrad",
    )(*sources, kernel)


def pair_program(activations, preact, upstream, master, first_moment, second_moment, scale):
    shape = activations.shape
    channels, size_x, size_y, _ = shape
    devices = math.prod(lax.axis_size(a) for a in AXES)
    rows = channels // devices
    span = lax.axis_size("gz") * rows
    used = master.shape[0] // LANES
    tall = -(-used // 16) * 16
    first, last = faces(preact, upstream)
    x_halos = (shifted(last, {"gx": 1}), shifted(first, {"gx": -1}))
    inner, planes_x, own, sent = pair_inner(
        preact,
        upstream,
        activations,
        first,
        last,
        master.reshape(used, LANES),
        (devices, tall, LANES),
    )
    kernel = lax.all_to_all(sent, AXES, 0, 0, tiled=True)
    planes = (x_halos[0], first, inner, last, x_halos[1])
    own = side(x_halos, own)
    other = shifted(own, {"gy": "swap"})
    zlo, zhi = join(own, other, size_x * size_y)
    below = shifted(zhi, {"gz": 1})
    sources = (*planes, other, other)
    mine, theirs = pair_wgrad(sources, planes_x, shape, span)
    theirs, below = lax.optimization_barrier((theirs, below))
    theirs = shifted(theirs, {"gy": "swap"})
    zlo, below = lax.optimization_barrier((zlo, below))
    above = shifted(zlo, {"gz": -1})
    edge = z_edges(own, other, zlo, below, span, (size_x, size_y), mine.shape[1])
    part = finish(mine, theirs, edge, scale, rows, channels, (devices // 2, tall, LANES))
    part, kernel = lax.optimization_barrier((part, kernel))
    parts = lax.all_to_all(part, ("gx", "gz"), 0, 0, tiled=True)
    grad_input = pair_dgrad((*sources, below, above), kernel, shape, rows)
    return grad_input, *adam(parts, master, first_moment, second_moment)


def yface_kernel(*refs):
    low_ref, high_ref = refs[5:]
    size_z = low_ref.shape[-1]
    for index in range(low_ref.shape[0]):
        body = body_of(refs[:5], index)
        plane = body.shape[-1]
        low_ref[index] = body[:, :size_z]
        high_ref[index] = body[:, plane - size_z :]


def y_faces(planes, size_z):
    inner, channels, _ = planes[2].shape
    face = jax.ShapeDtypeStruct((inner + 4, channels, size_z), BF16)
    return pl.pallas_call(
        yface_kernel,
        in_specs=[VMEM] * 5,
        out_specs=[VMEM] * 2,
        out_shape=[face] * 2,
        compiler_params=params(),
        cost_estimate=cost(0, 2**19),
        name="yfaces",
    )(*planes)


def zface_kernel(*refs):
    zlo_ref, zhi_ref = refs[7:]
    size_z = refs[5].shape[-1]
    whole = []
    for index in range(refs[5].shape[0]):
        low, high = y_halo(refs[5:7], index)
        body = body_of(refs[:5], index)[...]
        whole.append(jnp.concatenate([low.astype(BF16), body, high.astype(BF16)], axis=1))
    low, high = z_tiles(whole, whole[0].shape[1] // size_z, size_z, range(len(whole)))
    zlo_ref[...] = low.astype(BF16)
    zhi_ref[...] = high.astype(BF16)


def z_faces(planes, y_halos):
    face = jax.ShapeDtypeStruct((planes[0].shape[0], LANES), BF16)
    return pl.pallas_call(
        zface_kernel,
        in_specs=[VMEM] * 7,
        out_specs=[VMEM] * 2,
        out_shape=[face, face],
        compiler_params=params(),
        cost_estimate=cost(2**27, 2**21),
        name="zfaces",
    )(*planes, *y_halos)


def wgrad_kernel(scale, *refs):
    x_ref, part_ref, g3, x3, acc, flat = refs[9:]
    size_x, channels, plane = x_ref.shape
    size_z = refs[5].shape[-1]
    halo = z_halo(refs[7], refs[8], size_x + 2, plane // size_z + 2, size_z)
    weight_products(refs, halo, x_ref, g3, x3, acc)
    whole = to_flat(acc[...] * scale, channels, channels, flat)
    part_ref[...] = whole[:, : part_ref.shape[1]].astype(BF16)


def wgrad(sources, planes_x, shape, scale):
    channels = shape[0]
    return pl.pallas_call(
        functools.partial(wgrad_kernel, scale),
        in_specs=[VMEM] * 10,
        out_specs=VMEM,
        out_shape=jax.ShapeDtypeStruct((channels, 27 * channels), BF16),
        scratch_shapes=[
            g3_scratch(*shape),
            x3_scratch(*shape),
            acc_scratch(channels),
            flat_scratch(channels),
        ],
        compiler_params=params(32 * 2**20),
        cost_estimate=wgrad_cost(*shape),
        name="wgrad",
    )(*sources, planes_x)


def dgrad_kernel(*refs):
    w_ref, out_ref, g3, turned, weights, tile = refs[9:]
    _, size_x, size_y, size_z = out_ref.shape
    spread_weights(w_ref[...].astype(F32), turned, weights)
    halo = z_halo(refs[7], refs[8], size_x + 2, size_y + 2, size_z)
    input_products(refs, halo, g3, weights, tile, out_ref)


def dgrad(sources, kernel, shape):
    return pl.pallas_call(
        dgrad_kernel,
        in_specs=[VMEM] * 10,
        out_specs=VMEM,
        out_shape=jax.ShapeDtypeStruct(shape, BF16),
        scratch_shapes=dgrad_scratch(*shape),
        compiler_params=params(32 * 2**20),
        cost_estimate=dgrad_cost(*shape),
        name="dgrad",
    )(*sources, kernel)


def general_program(activations, preact, upstream, master, first_moment, second_moment, scale):
    shape = activations.shape
    channels, _, _, size_z = shape
    devices = math.prod(lax.axis_size(a) for a in AXES)
    share = master.shape[0]
    first, last = faces(preact, upstream)
    x_halos = (shifted(last, {"gx": 1}), shifted(first, {"gx": -1}))
    inner, planes_x = inner_planes(preact, upstream, activations)
    sent = jnp.broadcast_to(master.astype(BF16).reshape(1, 1, share), (devices, 1, share))
    kernel = lax.all_to_all(sent, AXES, 0, 0, tiled=True).reshape(channels, 27 * channels)
    planes = (x_halos[0], first, inner, last, x_halos[1])
    y_sent = y_faces(planes, size_z)
    y_halos = (shifted(y_sent[1], {"gy": 1}), shifted(y_sent[0], {"gy": -1}))
    zlo, zhi = z_faces(planes, y_halos)
    z_halos = (shifted(zhi, {"gz": 1}), shifted(zlo, {"gz": -1}))
    sources = (*planes, *y_halos, *z_halos)
    part = wgrad(sources, planes_x, shape, scale)
    part, kernel = lax.optimization_barrier((part, kernel))
    parts = lax.all_to_all(part.reshape(devices, 1, share), AXES, 0, 0, tiled=True)
    grad_input = dgrad(sources, kernel, shape)
    weight_grad = jnp.sum(parts.astype(F32), axis=0).reshape(-1)
    results = adam_step(master, first_moment, second_moment, weight_grad)
    return grad_input, weight_grad, *results


def shifted(value, moves):
    names = tuple(moves)
    sizes = [lax.axis_size(name) for name in names]
    pairs = []
    for source in range(math.prod(sizes)):
        rest, coords = source, []
        for size in reversed(sizes):
            coords.insert(0, rest % size)
            rest //= size
        coords = [
            (at + moves[name]) if moves[name] != "swap" else 1 - at
            for at, name in zip(coords, names)
        ]
        if all(0 <= at < size for at, size in zip(coords, sizes)):
            target = 0
            for at, size in zip(coords, sizes):
                target = target * size + at
            pairs.append((source, target))
    return lax.ppermute(value, names if len(names) > 1 else names[0], pairs)


def local(activations, preact, upstream, master, first_moment, second_moment):
    channels, size_x, size_y, size_z = activations.shape
    devices = math.prod(lax.axis_size(a) for a in AXES)
    share = master.shape[0]
    scale = 1.0 / math.sqrt(size_x * size_y * size_z * devices)
    in_pairs = (
        lax.axis_size("gy") == 2
        and channels % devices == 0
        and share % LANES == 0
        and channels // devices * lax.axis_size("gz") % 8 == 0
        and 2 * size_x * size_y <= LANES
        and (size_x + 2) * size_y <= LANES
    )
    program = pair_program if in_pairs else general_program
    return program(
        activations, preact, upstream, master, first_moment, second_moment, scale
    )


def solution(mesh):
    volume = P(None, "gx", "gy", "gz")
    flat = P(AXES)
    return jax.shard_map(
        local,
        mesh=mesh,
        in_specs=(volume, volume, volume, flat, flat, flat),
        out_specs=(volume, flat, flat, flat, flat),
        check_vma=False,
    )
```

```python
import functools
import math

import jax
import jax.numpy as jnp
from jax import lax
from jax.experimental import pallas as pl
from jax.experimental.pallas import tpu as pltpu
from jax.sharding import PartitionSpec as P

AXES = ("gx", "gy", "gz")
LANES = 128
VMEM = pl.BlockSpec(memory_space=pltpu.VMEM)
HBM = pl.BlockSpec(memory_space=pltpu.HBM)
F32 = jnp.float32
BF16 = jnp.bfloat16
FACES_VMEM = 56_200_000
INNER_VMEM = 53_000_000


def params(limit=24 * 2**20):
    return pltpu.CompilerParams(vmem_limit_bytes=limit)


def cost(flops, moved):
    return pl.CostEstimate(flops=flops, bytes_accessed=moved, transcendentals=0)


def to_planes(value, tile, write):
    channels, size_y, size_z = value.shape
    tile[...] = value.astype(F32).reshape(channels * size_y, size_z)
    for y in range(size_y):
        write(y, tile[pl.ds(y, channels, stride=size_y), :].astype(BF16))


def masked(p, u):
    return jnp.where(p > 0, u, jnp.zeros_like(u))


def face_kernel(p_ref, u_ref, m_ref, low_ref, high_ref, sent_ref, *scratch):
    p_buf, u_buf, tile, sems, share_ref, share_sems, m_buf = scratch
    size_x, size_z = p_ref.shape[1], p_ref.shape[3]
    copies = []
    for k, x in enumerate((0, size_x - 1)):
        pair = (
            pltpu.make_async_copy(p_ref.at[:, x], p_buf.at[k], sems.at[2 * k]),
            pltpu.make_async_copy(u_ref.at[:, x], u_buf.at[k], sems.at[2 * k + 1]),
        )
        for copy in pair:
            copy.start()
        copies.append(pair)
    read = pltpu.make_async_copy(m_ref, m_buf, sems.at[4])
    read.start()
    read.wait()
    share = m_buf[...]
    height = share_ref.shape[0] - share.shape[0]
    if height:
        share = jnp.concatenate([share, jnp.zeros((height, share.shape[1]), F32)], axis=0)
    share_ref[...] = share.astype(BF16)
    sends = [
        pltpu.make_async_copy(share_ref, sent_ref.at[device], share_sems.at[device])
        for device in range(sent_ref.shape[0])
    ]
    for copy in sends:
        copy.start()
    for k, out_ref in enumerate((low_ref, high_ref)):
        for copy in copies[k]:
            copy.wait()

        def write(y, value):
            out_ref[:, y * size_z : (y + 1) * size_z] = value

        to_planes(masked(p_buf[k], u_buf[k]), tile.at[k], write)
    for copy in sends:
        copy.wait()


def faces(preact, upstream, share, sent_shape):
    channels, size_x, size_y, size_z = preact.shape
    face = jax.ShapeDtypeStruct((channels, size_y * size_z), BF16)
    buffer = pltpu.VMEM((2, channels, size_y, size_z), BF16)
    return pl.pallas_call(
        face_kernel,
        in_specs=[HBM, HBM, HBM],
        out_specs=[VMEM, VMEM, HBM],
        out_shape=[face, face, jax.ShapeDtypeStruct(sent_shape, BF16)],
        scratch_shapes=[
            buffer,
            buffer,
            pltpu.VMEM((2, channels * size_y, size_z), F32),
            pltpu.SemaphoreType.DMA((5,)),
            pltpu.VMEM(sent_shape[1:], BF16),
            pltpu.SemaphoreType.DMA((sent_shape[0],)),
            pltpu.VMEM(share.shape, F32),
        ],
        compiler_params=params(FACES_VMEM),
        cost_estimate=cost(0, 2**20),
        name="faces",
    )(preact, upstream, share)


def read_inner(p_ref, u_ref, a_ref, g_ref, x_ref, p_buf, u_buf, a_buf, tile, sems):
    channels, size_x, size_y, size_z = a_ref.shape
    inner = size_x - 2
    copies = []
    for x in range(inner):
        copies.append(
            (
                pltpu.make_async_copy(p_ref.at[:, x + 1], p_buf.at[x], sems.at[x]),
                pltpu.make_async_copy(u_ref.at[:, x + 1], u_buf.at[x], sems.at[inner + x]),
            )
        )
    for x in range(size_x):
        copies.append(
            (pltpu.make_async_copy(a_ref.at[:, x], a_buf.at[x], sems.at[2 * inner + x]),)
        )
    for group in copies:
        for copy in group:
            copy.start()
    for x in range(inner):
        for copy in copies[x]:
            copy.wait()

        def write(y, value):
            g_ref[x, :, y * size_z : (y + 1) * size_z] = value

        to_planes(masked(p_buf[x], u_buf[x]), tile.at[x % 2], write)
    for x in range(size_x):
        copies[inner + x][0].wait()

        def write(y, value):
            x_ref[x, :, y * size_z : (y + 1) * size_z] = value

        to_planes(a_buf[x], tile.at[x % 2], write)


def inner_kernel(*refs):
    read_inner(*refs)


def inner_outputs(channels, size_x, size_y, size_z):
    plane = size_y * size_z
    return [
        jax.ShapeDtypeStruct((size_x - 2, channels, plane), BF16),
        jax.ShapeDtypeStruct((size_x, channels, plane), BF16),
    ]


def inner_scratch(channels, size_x, size_y, size_z):
    return [
        pltpu.VMEM((size_x - 2, channels, size_y, size_z), BF16),
        pltpu.VMEM((size_x - 2, channels, size_y, size_z), BF16),
        pltpu.VMEM((size_x, channels, size_y, size_z), BF16),
        pltpu.VMEM((2, channels * size_y, size_z), F32),
        pltpu.SemaphoreType.DMA((3 * size_x - 4,)),
    ]


def inner_planes(preact, upstream, activations):
    shape = preact.shape
    return pl.pallas_call(
        inner_kernel,
        in_specs=[HBM] * 3,
        out_specs=[VMEM] * 2,
        out_shape=inner_outputs(*shape),
        scratch_shapes=inner_scratch(*shape),
        compiler_params=params(INNER_VMEM),
        cost_estimate=cost(0, 6 * 2**20),
        name="inner",
    )(preact, upstream, activations)


def body_of(refs, index):
    planes = refs[2].shape[0] + 4
    if 2 <= index < planes - 2:
        return refs[2].at[index - 2]
    return refs[{0: 0, 1: 1, planes - 2: 3, planes - 1: 4}[index]]


def y_halo(refs, index):
    me = lax.axis_index("gy")
    low = jnp.where(me > 0, refs[0][index].astype(F32), 0.0)
    high = jnp.where(me < lax.axis_size("gy") - 1, refs[1][index].astype(F32), 0.0)
    return low, high


def z_picker(rows_y, size_z):
    shape = (rows_y * size_z, 2 * LANES)
    voxel = lax.broadcasted_iota(jnp.int32, shape, 0)
    lane = lax.broadcasted_iota(jnp.int32, shape, 1)
    wanted = jnp.where(lane < LANES, lane * size_z, (lane - LANES) * size_z + size_z - 1)
    return (voxel == wanted).astype(F32).astype(BF16)


def z_tiles(planes, rows_y, size_z, numbers):
    channels = planes[0].shape[0]
    columns = jnp.dot(
        jnp.concatenate(planes, axis=0), z_picker(rows_y, size_z), preferred_element_type=F32
    )
    low = jnp.zeros((channels, LANES), F32)
    high = jnp.zeros((channels, LANES), F32)
    for index, number in enumerate(numbers):
        rows = columns[index * channels : (index + 1) * channels]
        low = low + pltpu.roll(rows[:, :LANES], number * rows_y, 1)
        high = high + pltpu.roll(rows[:, LANES:], number * rows_y, 1)
    return low, high


def put_columns(columns, row_of, rows_y, size_z):
    shape = (2 * LANES, rows_y * size_z)
    source = lax.broadcasted_iota(jnp.int32, shape, 0)
    voxel = lax.broadcasted_iota(jnp.int32, shape, 1)
    number = source % LANES
    place = row_of(number) * size_z + jnp.where(source < LANES, 0, size_z - 1)
    place = jnp.where(number < rows_y, place, -1)
    put = (voxel == place).astype(F32).astype(BF16)
    rows = [jnp.concatenate(pair, axis=1) for pair in columns]
    return jnp.dot(
        jnp.concatenate(rows, axis=0).astype(BF16), put, preferred_element_type=F32
    )


def z_halo(low_ref, high_ref, planes, rows_y, size_z):
    columns = []
    for index in range(planes):
        shift = -index * rows_y % LANES
        columns.append(
            [pltpu.roll(ref[...].astype(F32), shift, 1) for ref in (low_ref, high_ref)]
        )
    return put_columns(columns, lambda number: number, rows_y, size_z)


def pair_z_halo(low_ref, high_ref, planes, size_y, size_z):
    me = lax.axis_index("gy")
    sides = []
    for ref in (low_ref, high_ref):
        first, second = ref[0].astype(F32), ref[1].astype(F32)
        lane = lax.broadcasted_iota(jnp.int32, first.shape, 1)
        own = jnp.where(me == 0, first, second)
        before = jnp.where(me == 0, 0.0, first)
        after = jnp.where(me == 0, second, 0.0)
        columns = []
        for index in range(planes):
            start = index * size_y
            columns.append(
                jnp.where(
                    lane < size_y,
                    pltpu.roll(own, -start % LANES, 1),
                    jnp.where(
                        lane == size_y,
                        pltpu.roll(before, (1 - start) % LANES, 1),
                        pltpu.roll(after, (size_y + 1 - start) % LANES, 1),
                    ),
                )
            )
        sides.append(columns)

    def row_of(number):
        return jnp.where(number < size_y, number + 1, jnp.where(number == size_y, 0, size_y + 1))

    return put_columns(list(zip(*sides)), row_of, size_y + 2, size_z)


def shifted_plane(index, refs, halo, g3):
    channels, plane = refs[0].shape
    size_z = refs[5].shape[-1]
    rows_y = plane // size_z + 2
    base = 3 * channels * index
    lane = lax.broadcasted_iota(jnp.int32, (channels, size_z), 1)
    low, high = y_halo(refs[5:7], index)
    body = body_of(refs[:5], index)
    for row in range(rows_y):
        cols = slice(row * size_z, (row + 1) * size_z)
        if row == 0:
            wide = low
        elif row == rows_y - 1:
            wide = high
        else:
            wide = body[:, (row - 1) * size_z : row * size_z].astype(F32)
        edge = 0.0 if halo is None else halo[index * channels : (index + 1) * channels, cols]
        before = jnp.where(lane == 0, edge, pltpu.roll(wide, 1, 1))
        after = jnp.where(lane == size_z - 1, edge, pltpu.roll(wide, size_z - 1, 1))
        g3[base : base + channels, cols] = before.astype(BF16)
        g3[base + channels : base + 2 * channels, cols] = wide.astype(BF16)
        g3[base + 2 * channels : base + 3 * channels, cols] = after.astype(BF16)


def weight_products(refs, halo, x_ref, g3, x3, acc):
    size_x, channels, plane = x_ref.shape
    size_z = refs[5].shape[-1]
    group = 3 * channels
    zero = jnp.zeros((channels, 2 * size_z), BF16)
    done = 0
    for x in range(size_x):
        while done < x + 3:
            shifted_plane(done, refs, halo, g3)
            done += 1
        value = x_ref[x]
        for b in range(3):
            at = slice(b * channels, (b + 1) * channels)
            start = (2 - b) * size_z
            x3[x, at, start : start + plane] = value
            if start:
                x3[x, at, :start] = zero[:, :start]
            if start < 2 * size_z:
                x3[x, at, start + plane :] = zero[:, start:]
        product = lax.dot_general(
            g3[x * group : (x + 3) * group, :],
            x3[x],
            (((1,), (1,)), ((), ())),
            preferred_element_type=F32,
        )
        if x == 0:
            acc[...] = product
        else:
            acc[...] += product


def to_flat(value, count, channels, flat):
    height, width = value.shape
    wide = value
    if height % LANES:
        wide = jnp.concatenate([wide, jnp.zeros((-height % LANES, width), F32)], axis=0)
    if width % LANES:
        wide = jnp.concatenate([wide, jnp.zeros((wide.shape[0], -width % LANES), F32)], axis=1)
    turned = wide.T
    for b in range(3):
        rows = turned[b * channels : (b + 1) * channels]
        for block in range(9):
            start = block * count
            cell = rows[:, start // LANES * LANES : (start // LANES + 1) * LANES]
            tap = (2 - block // 3) * 9 + b * 3 + 2 - block % 3
            shift = -start % LANES
            flat[pl.ds(tap, channels, stride=27), :] = pltpu.roll(cell, shift, 1) if shift else cell
    return flat[...].T[:count]


def spread_weights(whole, turned, weights):
    channels, taps = whole.shape
    group = 3 * channels
    whole = jnp.concatenate([whole, jnp.zeros((LANES - channels, taps), F32)], axis=0)
    whole = jnp.concatenate([whole, jnp.zeros((LANES, -taps % LANES), F32)], axis=1)
    turned[...] = whole.T
    for b in range(3):
        blocks = []
        for a in range(3):
            for c in range(3):
                tap = (2 - a) * 9 + (2 - b) * 3 + 2 - c
                blocks.append(turned[pl.ds(tap, channels, stride=27), :][:, :channels])
        zero = jnp.zeros((channels, group), F32)
        weights[b, :channels] = jnp.concatenate(blocks + [zero], axis=1).astype(BF16)
        weights[b, channels:] = jnp.concatenate([zero] + blocks, axis=1).astype(BF16)


def input_products(refs, halo, g3, weights, tile, out_ref):
    channels, size_x, size_y, size_z = out_ref.shape
    group = 3 * channels
    plane = size_y * size_z
    done = 0
    for pair in range(size_x // 2):
        while done < 2 * pair + 4:
            shifted_plane(done, refs, halo, g3)
            done += 1
        at = slice(2 * pair * group, (2 * pair + 4) * group)
        total = None
        for b in range(3):
            product = jnp.dot(
                weights[b],
                g3[at, b * size_z : b * size_z + plane],
                preferred_element_type=F32,
            )
            total = product if total is None else total + product
        for half in range(2):
            for y in range(size_y):
                tile[half, pl.ds(y, channels, stride=size_y), :] = total[
                    half * channels : (half + 1) * channels, y * size_z : (y + 1) * size_z
                ]
            out_ref[:, 2 * pair + half] = (
                tile[half].reshape(channels, size_y, size_z).astype(BF16)
            )


def g3_scratch(channels, size_x, size_y, size_z):
    return pltpu.VMEM(((size_x + 2) * 3 * channels, (size_y + 2) * size_z), BF16)


def x3_scratch(channels, size_x, size_y, size_z):
    return pltpu.VMEM((size_x, 3 * channels, (size_y + 2) * size_z), BF16)


def acc_scratch(channels):
    return pltpu.VMEM((9 * channels, 3 * channels), F32)


def flat_scratch(channels):
    return pltpu.VMEM((-(-27 * channels // LANES) * LANES, LANES), F32)


def dgrad_scratch(channels, size_x, size_y, size_z):
    return [
        g3_scratch(channels, size_x, size_y, size_z),
        flat_scratch(channels),
        pltpu.VMEM((3, 2 * channels, 12 * channels), BF16),
        pltpu.VMEM((2, channels * size_y, size_z), F32),
    ]


def wgrad_cost(channels, size_x, size_y, size_z):
    return cost(54 * channels * channels * size_x * (size_y + 2) * size_z, 4 * 2**20)


def dgrad_cost(channels, size_x, size_y, size_z):
    return cost(72 * channels * channels * size_x * size_y * size_z, 4 * 2**20)


def row_for_other(body, size_z):
    plane = body.shape[-1]
    low, high = body[:, :size_z].astype(F32), body[:, plane - size_z :].astype(F32)
    return jnp.where(lax.axis_index("gy") == 0, high, low).astype(BF16)


def pair_inner_kernel(*refs):
    first_ref, last_ref = refs[3:5]
    g_ref, x_ref, side_ref = refs[5:8]
    read_inner(*refs[:3], g_ref, x_ref, *refs[8:])
    size_z = side_ref.shape[-1]
    size_x, channels, plane = x_ref.shape
    size_y = plane // size_z
    bodies = [first_ref] + [g_ref.at[x] for x in range(size_x - 2)] + [last_ref]
    for x, body in enumerate(bodies):
        side_ref[x] = row_for_other(body, size_z)
    low, high = z_tiles([body[...] for body in bodies], size_y, size_z, range(1, size_x + 1))
    side_ref[size_x] = low.astype(BF16)
    side_ref[size_x + 1] = high.astype(BF16)
    low, high = z_tiles([x_ref[x] for x in range(size_x)], size_y, size_z, range(size_x))
    side_ref[size_x + 2] = (low + pltpu.roll(high, size_x * size_y, 1)).astype(BF16)


def pair_inner(preact, upstream, activations, first, last):
    shape = preact.shape
    channels, size_x, _, size_z = shape
    return pl.pallas_call(
        pair_inner_kernel,
        in_specs=[HBM] * 3 + [VMEM] * 2,
        out_specs=[VMEM] * 3,
        out_shape=inner_outputs(*shape)
        + [jax.ShapeDtypeStruct((size_x + 3, channels, size_z), BF16)],
        scratch_shapes=inner_scratch(*shape),
        compiler_params=params(INNER_VMEM),
        cost_estimate=cost(0, 6 * 2**20),
        name="inner",
    )(preact, upstream, activations, first, last)


def side_kernel(xlo_ref, xhi_ref, own_ref, sent_ref):
    size_x = own_ref.shape[0] - 3
    size_z = own_ref.shape[-1]
    size_y = xlo_ref.shape[-1] // size_z
    sent_ref[0] = row_for_other(xlo_ref, size_z)
    for x in range(size_x):
        sent_ref[x + 1] = own_ref[x]
    sent_ref[size_x + 1] = row_for_other(xhi_ref, size_z)
    tiles = z_tiles([xlo_ref[...], xhi_ref[...]], size_y, size_z, (0, size_x + 1))
    for k in range(2):
        sent_ref[size_x + 2 + k] = (own_ref[size_x + k].astype(F32) + tiles[k]).astype(BF16)
    sent_ref[size_x + 4] = own_ref[size_x + 2]


def side(x_halos, own):
    return pl.pallas_call(
        side_kernel,
        in_specs=[VMEM] * 3,
        out_specs=VMEM,
        out_shape=jax.ShapeDtypeStruct((own.shape[0] + 2, *own.shape[1:]), BF16),
        compiler_params=params(),
        cost_estimate=cost(2**25, 2**19),
        name="side",
    )(*x_halos, own)


def both_columns(is_first, own, other, number, area):
    first = jnp.where(is_first, own, other).astype(F32)
    second = jnp.where(is_first, other, own).astype(F32)
    lane = lax.broadcasted_iota(jnp.int32, first.shape, 1)
    return jnp.where(
        lane < area,
        pltpu.roll(first, -number * area % LANES, 1),
        pltpu.roll(second, (1 - number) * area % LANES, 1),
    )


def join_kernel(area, own_ref, other_ref, low_ref, high_ref):
    at = own_ref.shape[0] - 3
    me = lax.axis_index("gy")
    for k, out_ref in enumerate((low_ref, high_ref)):
        out_ref[me] = own_ref[at + k]
        out_ref[1 - me] = other_ref[at + k]
    own, other = own_ref[at + 2].astype(F32), other_ref[at + 2].astype(F32)
    high_ref[2] = both_columns(me == 0, own, other, 1, area).astype(BF16)


def join(own, other, area):
    return pl.pallas_call(
        functools.partial(join_kernel, area),
        in_specs=[VMEM] * 2,
        out_specs=[VMEM] * 2,
        out_shape=[jax.ShapeDtypeStruct((n, *own.shape[1:]), BF16) for n in (2, 3)],
        compiler_params=params(),
        cost_estimate=cost(0, 2**17),
        name="join",
    )(own, other)


def pair_wgrad_kernel(span, *refs):
    x_ref, mine_ref, theirs_ref, g3, x3, acc = refs[7:]
    channels = x_ref.shape[1]
    weight_products(refs, None, x_ref, g3, x3, acc)
    is_first = lax.axis_index("gy") == 0
    width = 3 * channels
    halves = []
    for half in range(2):
        at = range(half * span, 9 * channels, 2 * span)
        halves.append(jnp.concatenate([acc[start : start + span, :] for start in at], axis=0))
    spare = jnp.zeros((halves[0].shape[0], mine_ref.shape[1] - width), F32)
    for ref, order in ((mine_ref, halves), (theirs_ref, halves[::-1])):
        picked = jnp.where(is_first, order[0], order[1])
        ref[...] = jnp.concatenate([picked, spare], axis=1)


def pair_wgrad(sources, planes_x, shape, span):
    channels = shape[0]
    width = -(-3 * channels // LANES) * LANES
    part = jax.ShapeDtypeStruct((9 * channels // 2, width), F32)
    return pl.pallas_call(
        functools.partial(pair_wgrad_kernel, span),
        in_specs=[VMEM] * 8,
        out_specs=[VMEM] * 2,
        out_shape=[part, part],
        scratch_shapes=[g3_scratch(*shape), x3_scratch(*shape), acc_scratch(channels)],
        compiler_params=params(32 * 2**20),
        cost_estimate=wgrad_cost(*shape),
        name="wgrad",
    )(*sources, planes_x)


def edge_kernel(span, sizes, own_ref, other_ref, ztiles_ref, below_ref, edge_ref):
    size_x, size_y = sizes
    channels = below_ref.shape[1]
    count = channels // 2
    area = size_x * size_y
    is_first = lax.axis_index("gy") == 0
    at = own_ref.shape[0] - 1
    own, other = own_ref[at].astype(F32), other_ref[at].astype(F32)
    columns = (both_columns(is_first, own, other, 0, area), below_ref[2].astype(F32))
    lane = lax.broadcasted_iota(jnp.int32, (channels, LANES), 1)
    row = lane % size_y
    few = lax.broadcasted_iota(jnp.int32, (count, LANES), 1)
    for number, (tile_ref, value) in enumerate(zip((below_ref, ztiles_ref), columns)):
        jump = area - size_y + 1
        before = jnp.where(lane >= area, pltpu.roll(value, jump, 1), 0.0)
        after = jnp.where(lane < area, pltpu.roll(value, LANES - jump, 1), 0.0)
        right = jnp.concatenate(
            [
                jnp.where(row > 0, pltpu.roll(value, 1, 1), before),
                value,
                jnp.where(row < size_y - 1, pltpu.roll(value, LANES - 1, 1), after),
            ],
            axis=0,
        )
        tiles = []
        for device in range(2):
            tile = tile_ref[device].astype(F32)
            halves = [
                jnp.concatenate(
                    [tile[s : s + span] for s in range(half * span, channels, 2 * span)], axis=0
                )
                for half in range(2)
            ]
            tiles.append(jnp.where(is_first, halves[0], halves[1]))
        left = []
        for a in range(3):
            first = pltpu.roll(tiles[0], -a * size_y % LANES, 1)
            second = pltpu.roll(tiles[1], (area - a * size_y) % LANES, 1)
            left.append(jnp.where(few < area, first, jnp.where(few < 2 * area, second, 0.0)))
        product = lax.dot_general(
            jnp.concatenate(left, axis=0).astype(BF16),
            right.astype(BF16),
            (((1,), (1,)), ((), ())),
            preferred_element_type=F32,
        )
        spare = jnp.zeros((3 * count, edge_ref.shape[2] - 3 * channels), F32)
        edge_ref[number] = jnp.concatenate([product, spare], axis=1)


def z_edges(own, other, ztiles, below, span, sizes, width):
    channels = own.shape[1]
    return pl.pallas_call(
        functools.partial(edge_kernel, span, sizes),
        in_specs=[VMEM] * 4,
        out_specs=VMEM,
        out_shape=jax.ShapeDtypeStruct((2, 3 * channels // 2, width), F32),
        compiler_params=params(),
        cost_estimate=cost(2**27, 2**20),
        name="edges",
    )(own, other, ztiles, below)


def finish_kernel(scale, rows, channels, mine_ref, other_ref, edge_ref, part_ref, flat, lines, chunks):
    count = channels // 2
    taps = 27 * channels
    total = mine_ref[...] + other_ref[...]
    blocks = []
    for a in range(3):
        for c in range(3):
            block = total[(3 * a + c) * count : (3 * a + c + 1) * count]
            if c != 1:
                block = block + edge_ref[c // 2, a * count : (a + 1) * count, :]
            blocks.append(block)
    whole = to_flat(jnp.concatenate(blocks, axis=0) * scale, count, channels, flat)
    pieces = whole.shape[1] // LANES
    for k in range(pieces):
        lines[k * count : (k + 1) * count, :] = whole[:, k * LANES : (k + 1) * LANES]
    number, tall, width = part_ref.shape
    parts = []
    for r in range(rows):
        found = [lines[pl.ds(k * count + r, number, stride=rows), :] for k in range(pieces)]
        parts.append(jnp.concatenate(found, axis=1)[:, :taps])
    line = jnp.concatenate(parts, axis=1)
    chunks[...] = jnp.zeros_like(chunks)
    for k in range(line.shape[1] // width):
        chunks[pl.ds(k, number, stride=tall), :] = line[:, k * width : (k + 1) * width]
    part_ref[...] = chunks[...].reshape(part_ref.shape).astype(BF16)


def finish(mine, other, edge, scale, rows, channels, part_shape):
    return pl.pallas_call(
        functools.partial(finish_kernel, scale, rows, channels),
        in_specs=[VMEM] * 3,
        out_specs=VMEM,
        out_shape=jax.ShapeDtypeStruct(part_shape, BF16),
        scratch_shapes=[
            flat_scratch(channels),
            pltpu.VMEM((-(-27 * channels // LANES) * channels // 2, LANES), F32),
            pltpu.VMEM((part_shape[0] * part_shape[1], part_shape[2]), F32),
        ],
        compiler_params=params(),
        cost_estimate=cost(2**24, 2**20),
        name="finish",
    )(mine, other, edge)


def adam_step(master, first, second, weight_grad):
    new_first = 0.9 * first + 0.1 * weight_grad
    new_second = 0.999 * second + 0.001 * weight_grad * weight_grad
    corr_first = 1.0 - (0.9**10) ** 10
    corr_second = 1.0 - (0.999**10) ** 10
    update = new_first / corr_first / (jnp.sqrt(new_second / corr_second) + 1e-08) + 0.01 * master
    return master - 0.05 * update, new_first, new_second


def adam_kernel(parts_ref, master_ref, first_ref, second_ref, *out_refs):
    weight_grad = parts_ref[0].astype(F32)
    for source in range(1, parts_ref.shape[0]):
        weight_grad = weight_grad + parts_ref[source].astype(F32)
    weight_grad = weight_grad[: master_ref.shape[0]]
    results = adam_step(master_ref[...], first_ref[...], second_ref[...], weight_grad)
    for out_ref, result in zip(out_refs, (weight_grad, *results)):
        out_ref[...] = result


def adam(parts, *states):
    share = states[0].shape[0]
    tiled = [state.reshape(share // LANES, LANES) for state in states]
    result = jax.ShapeDtypeStruct(tiled[0].shape, F32)
    outs = pl.pallas_call(
        adam_kernel,
        in_specs=[VMEM] * 4,
        out_specs=[VMEM] * 4,
        out_shape=[result] * 4,
        compiler_params=params(),
        cost_estimate=cost(2**18, 2**18),
        name="adam",
    )(parts, *tiled)
    return tuple(out.reshape(share) for out in outs)


def pair_dgrad_kernel(rows, *refs):
    w_ref, out_ref, g3, turned, weights, tile, chunks, lines = refs[9:]
    channels, size_x, size_y, size_z = out_ref.shape
    taps = 27 * channels
    count, height, width = w_ref.shape
    chunks[...] = w_ref[...].astype(F32).reshape(chunks.shape)
    line = jnp.concatenate(
        [chunks[pl.ds(k, count, stride=height), :] for k in range(rows * taps // width)], axis=1
    )
    pieces = lines.shape[0] // channels
    spare = jnp.zeros((count, pieces * LANES - taps), F32)
    for r in range(rows):
        found = jnp.concatenate([line[:, r * taps : (r + 1) * taps], spare], axis=1)
        for k in range(pieces):
            lines[pl.ds(k * channels + r, count, stride=rows), :] = found[
                :, k * LANES : (k + 1) * LANES
            ]
    whole = [lines[k * channels : (k + 1) * channels, :] for k in range(pieces)]
    spread_weights(jnp.concatenate(whole, axis=1)[:, :taps], turned, weights)
    halo = pair_z_halo(refs[7], refs[8], size_x + 2, size_y, size_z)
    input_products(refs, halo, g3, weights, tile, out_ref)


def pair_dgrad(sources, kernel, shape, rows):
    channels = shape[0]
    return pl.pallas_call(
        functools.partial(pair_dgrad_kernel, rows),
        in_specs=[VMEM] * 10,
        out_specs=VMEM,
        out_shape=jax.ShapeDtypeStruct(shape, BF16),
        scratch_shapes=dgrad_scratch(*shape)
        + [
            pltpu.VMEM((kernel.shape[0] * kernel.shape[1], kernel.shape[2]), F32),
            pltpu.VMEM((-(-27 * channels // LANES) * channels, LANES), F32),
        ],
        compiler_params=params(32 * 2**20),
        cost_estimate=dgrad_cost(*shape),
        name="dgrad",
    )(*sources, kernel)


def pair_program(activations, preact, upstream, master, first_moment, second_moment, scale):
    shape = activations.shape
    channels, size_x, size_y, _ = shape
    devices = math.prod(lax.axis_size(a) for a in AXES)
    rows = channels // devices
    span = lax.axis_size("gz") * rows
    used = master.shape[0] // LANES
    tall = -(-used // 16) * 16
    first, last, sent = faces(
        preact, upstream, master.reshape(used, LANES), (devices, tall, LANES)
    )
    kernel = lax.all_to_all(sent, AXES, 0, 0, tiled=True)
    x_halos = (shifted(last, {"gx": 1}), shifted(first, {"gx": -1}))
    inner, planes_x, own = pair_inner(preact, upstream, activations, first, last)
    planes = (x_halos[0], first, inner, last, x_halos[1])
    own = side(x_halos, own)
    other = shifted(own, {"gy": "swap"})
    zlo, zhi = join(own, other, size_x * size_y)
    zhi, kernel = lax.optimization_barrier((zhi, kernel))
    below = shifted(zhi, {"gz": 1})
    sources = (*planes, other, other)
    mine, theirs = pair_wgrad(sources, planes_x, shape, span)
    theirs, below = lax.optimization_barrier((theirs, below))
    theirs = shifted(theirs, {"gy": "swap"})
    zlo, below = lax.optimization_barrier((zlo, below))
    above = shifted(zlo, {"gz": -1})
    edge = z_edges(own, other, zlo, below, span, (size_x, size_y), mine.shape[1])
    part = finish(mine, theirs, edge, scale, rows, channels, (devices // 2, tall, LANES))
    part, kernel = lax.optimization_barrier((part, kernel))
    parts = lax.all_to_all(part, ("gx", "gz"), 0, 0, tiled=True)
    grad_input = pair_dgrad((*sources, below, above), kernel, shape, rows)
    return grad_input, *adam(parts, master, first_moment, second_moment)


def yface_kernel(*refs):
    low_ref, high_ref = refs[5:]
    size_z = low_ref.shape[-1]
    for index in range(low_ref.shape[0]):
        body = body_of(refs[:5], index)
        plane = body.shape[-1]
        low_ref[index] = body[:, :size_z]
        high_ref[index] = body[:, plane - size_z :]


def y_faces(planes, size_z):
    inner, channels, _ = planes[2].shape
    face = jax.ShapeDtypeStruct((inner + 4, channels, size_z), BF16)
    return pl.pallas_call(
        yface_kernel,
        in_specs=[VMEM] * 5,
        out_specs=[VMEM] * 2,
        out_shape=[face] * 2,
        compiler_params=params(),
        cost_estimate=cost(0, 2**19),
        name="yfaces",
    )(*planes)


def zface_kernel(*refs):
    zlo_ref, zhi_ref = refs[7:]
    size_z = refs[5].shape[-1]
    whole = []
    for index in range(refs[5].shape[0]):
        low, high = y_halo(refs[5:7], index)
        body = body_of(refs[:5], index)[...]
        whole.append(jnp.concatenate([low.astype(BF16), body, high.astype(BF16)], axis=1))
    low, high = z_tiles(whole, whole[0].shape[1] // size_z, size_z, range(len(whole)))
    zlo_ref[...] = low.astype(BF16)
    zhi_ref[...] = high.astype(BF16)


def z_faces(planes, y_halos):
    face = jax.ShapeDtypeStruct((planes[0].shape[0], LANES), BF16)
    return pl.pallas_call(
        zface_kernel,
        in_specs=[VMEM] * 7,
        out_specs=[VMEM] * 2,
        out_shape=[face, face],
        compiler_params=params(),
        cost_estimate=cost(2**27, 2**21),
        name="zfaces",
    )(*planes, *y_halos)


def wgrad_kernel(scale, *refs):
    x_ref, part_ref, g3, x3, acc, flat = refs[9:]
    size_x, channels, plane = x_ref.shape
    size_z = refs[5].shape[-1]
    halo = z_halo(refs[7], refs[8], size_x + 2, plane // size_z + 2, size_z)
    weight_products(refs, halo, x_ref, g3, x3, acc)
    whole = to_flat(acc[...] * scale, channels, channels, flat)
    part_ref[...] = whole[:, : part_ref.shape[1]].astype(BF16)


def wgrad(sources, planes_x, shape, scale):
    channels = shape[0]
    return pl.pallas_call(
        functools.partial(wgrad_kernel, scale),
        in_specs=[VMEM] * 10,
        out_specs=VMEM,
        out_shape=jax.ShapeDtypeStruct((channels, 27 * channels), BF16),
        scratch_shapes=[
            g3_scratch(*shape),
            x3_scratch(*shape),
            acc_scratch(channels),
            flat_scratch(channels),
        ],
        compiler_params=params(32 * 2**20),
        cost_estimate=wgrad_cost(*shape),
        name="wgrad",
    )(*sources, planes_x)


def dgrad_kernel(*refs):
    w_ref, out_ref, g3, turned, weights, tile = refs[9:]
    _, size_x, size_y, size_z = out_ref.shape
    spread_weights(w_ref[...].astype(F32), turned, weights)
    halo = z_halo(refs[7], refs[8], size_x + 2, size_y + 2, size_z)
    input_products(refs, halo, g3, weights, tile, out_ref)


def dgrad(sources, kernel, shape):
    return pl.pallas_call(
        dgrad_kernel,
        in_specs=[VMEM] * 10,
        out_specs=VMEM,
        out_shape=jax.ShapeDtypeStruct(shape, BF16),
        scratch_shapes=dgrad_scratch(*shape),
        compiler_params=params(32 * 2**20),
        cost_estimate=dgrad_cost(*shape),
        name="dgrad",
    )(*sources, kernel)


def general_program(activations, preact, upstream, master, first_moment, second_moment, scale):
    shape = activations.shape
    channels, _, _, size_z = shape
    devices = math.prod(lax.axis_size(a) for a in AXES)
    share = master.shape[0]
    first, last, sent = faces(preact, upstream, master.reshape(1, share), (devices, 1, share))
    x_halos = (shifted(last, {"gx": 1}), shifted(first, {"gx": -1}))
    inner, planes_x = inner_planes(preact, upstream, activations)
    kernel = lax.all_to_all(sent, AXES, 0, 0, tiled=True).reshape(channels, 27 * channels)
    planes = (x_halos[0], first, inner, last, x_halos[1])
    y_sent = y_faces(planes, size_z)
    y_halos = (shifted(y_sent[1], {"gy": 1}), shifted(y_sent[0], {"gy": -1}))
    zlo, zhi = z_faces(planes, y_halos)
    z_halos = (shifted(zhi, {"gz": 1}), shifted(zlo, {"gz": -1}))
    sources = (*planes, *y_halos, *z_halos)
    part = wgrad(sources, planes_x, shape, scale)
    part, kernel = lax.optimization_barrier((part, kernel))
    parts = lax.all_to_all(part.reshape(devices, 1, share), AXES, 0, 0, tiled=True)
    grad_input = dgrad(sources, kernel, shape)
    weight_grad = jnp.sum(parts.astype(F32), axis=0).reshape(-1)
    results = adam_step(master, first_moment, second_moment, weight_grad)
    return grad_input, weight_grad, *results


def shifted(value, moves):
    names = tuple(moves)
    sizes = [lax.axis_size(name) for name in names]
    pairs = []
    for source in range(math.prod(sizes)):
        rest, coords = source, []
        for size in reversed(sizes):
            coords.insert(0, rest % size)
            rest //= size
        coords = [
            (at + moves[name]) if moves[name] != "swap" else 1 - at
            for at, name in zip(coords, names)
        ]
        if all(0 <= at < size for at, size in zip(coords, sizes)):
            target = 0
            for at, size in zip(coords, sizes):
                target = target * size + at
            pairs.append((source, target))
    return lax.ppermute(value, names if len(names) > 1 else names[0], pairs)


def local(activations, preact, upstream, master, first_moment, second_moment):
    channels, size_x, size_y, size_z = activations.shape
    devices = math.prod(lax.axis_size(a) for a in AXES)
    share = master.shape[0]
    scale = 1.0 / math.sqrt(size_x * size_y * size_z * devices)
    in_pairs = (
        lax.axis_size("gy") == 2
        and channels % devices == 0
        and share % LANES == 0
        and channels // devices * lax.axis_size("gz") % 8 == 0
        and 2 * size_x * size_y <= LANES
        and (size_x + 2) * size_y <= LANES
    )
    program = pair_program if in_pairs else general_program
    return program(
        activations, preact, upstream, master, first_moment, second_moment, scale
    )


def solution(mesh):
    volume = P(None, "gx", "gy", "gz")
    flat = P(AXES)
    return jax.shard_map(
        local,
        mesh=mesh,
        in_specs=(volume, volume, volume, flat, flat, flat),
        out_specs=(volume, flat, flat, flat, flat),
        check_vma=False,
    )
```

```python
import functools
import math

import jax
import jax.numpy as jnp
from jax import lax
from jax.experimental import pallas as pl
from jax.experimental.pallas import tpu as pltpu
from jax.sharding import PartitionSpec as P

AXES = ("gx", "gy", "gz")
LANES = 128
VMEM = pl.BlockSpec(memory_space=pltpu.VMEM)
HBM = pl.BlockSpec(memory_space=pltpu.HBM)
F32 = jnp.float32
BF16 = jnp.bfloat16
FACES_VMEM = 55_900_000
INNER_VMEM = 53_000_000


def params(limit=24 * 2**20):
    return pltpu.CompilerParams(vmem_limit_bytes=limit)


def cost(flops, moved):
    return pl.CostEstimate(flops=flops, bytes_accessed=moved, transcendentals=0)


def to_planes(value, tile, write):
    channels, size_y, size_z = value.shape
    tile[...] = value.astype(F32).reshape(channels * size_y, size_z)
    for y in range(size_y):
        write(y, tile[pl.ds(y, channels, stride=size_y), :].astype(BF16))


def masked(p, u):
    return jnp.where(p > 0, u, jnp.zeros_like(u))


def face_kernel(axis, p_ref, u_ref, *refs):
    p_buf, u_buf, tile, sems = refs[-4:]
    out_refs, swap_refs = refs[:2], refs[2:-4]
    size_x, size_z = p_ref.shape[1], p_ref.shape[3]
    copies = []
    for k, x in enumerate((0, size_x - 1)):
        pair = (
            pltpu.make_async_copy(p_ref.at[:, x], p_buf.at[k], sems.at[2 * k]),
            pltpu.make_async_copy(u_ref.at[:, x], u_buf.at[k], sems.at[2 * k + 1]),
        )
        for copy in pair:
            copy.start()
        copies.append(pair)
    for k, out_ref in enumerate(out_refs):
        for copy in copies[k]:
            copy.wait()

        def write(y, value):
            out_ref[:, y * size_z : (y + 1) * size_z] = value

        to_planes(masked(p_buf[k], u_buf[k]), tile.at[k], write)
    if axis is not None:
        odd = lax.rem(lax.axis_index(axis), 2) == 1

        @pl.when(odd)
        def _():
            for swap_ref, out_ref in zip(swap_refs, out_refs):
                swap_ref[...] = out_ref[...]

        @pl.when(jnp.logical_not(odd))
        def _():
            for swap_ref, out_ref in zip(swap_refs, out_refs[::-1]):
                swap_ref[...] = out_ref[...]


def faces(preact, upstream, axis=None):
    channels, size_x, size_y, size_z = preact.shape
    face = jax.ShapeDtypeStruct((channels, size_y * size_z), BF16)
    buffer = pltpu.VMEM((2, channels, size_y, size_z), BF16)
    count = 2 if axis is None else 4
    return pl.pallas_call(
        functools.partial(face_kernel, axis),
        in_specs=[HBM, HBM],
        out_specs=[VMEM] * count,
        out_shape=[face] * count,
        scratch_shapes=[
            buffer,
            buffer,
            pltpu.VMEM((2, channels * size_y, size_z), F32),
            pltpu.SemaphoreType.DMA((4,)),
        ],
        compiler_params=params(FACES_VMEM),
        cost_estimate=cost(0, 2**20),
        name="faces",
    )(preact, upstream)


def read_inner(p_ref, u_ref, a_ref, g_ref, x_ref, p_buf, u_buf, a_buf, tile, sems):
    channels, size_x, size_y, size_z = a_ref.shape
    inner = size_x - 2
    copies = []
    for x in range(inner):
        copies.append(
            (
                pltpu.make_async_copy(p_ref.at[:, x + 1], p_buf.at[x], sems.at[x]),
                pltpu.make_async_copy(u_ref.at[:, x + 1], u_buf.at[x], sems.at[inner + x]),
            )
        )
    for x in range(size_x):
        copies.append(
            (pltpu.make_async_copy(a_ref.at[:, x], a_buf.at[x], sems.at[2 * inner + x]),)
        )
    for group in copies:
        for copy in group:
            copy.start()
    for x in range(inner):
        for copy in copies[x]:
            copy.wait()

        def write(y, value):
            g_ref[x, :, y * size_z : (y + 1) * size_z] = value

        to_planes(masked(p_buf[x], u_buf[x]), tile.at[x % 2], write)
    for x in range(size_x):
        copies[inner + x][0].wait()

        def write(y, value):
            x_ref[x, :, y * size_z : (y + 1) * size_z] = value

        to_planes(a_buf[x], tile.at[x % 2], write)


def inner_kernel(*refs):
    read_inner(*refs)


def inner_outputs(channels, size_x, size_y, size_z):
    plane = size_y * size_z
    return [
        jax.ShapeDtypeStruct((size_x - 2, channels, plane), BF16),
        jax.ShapeDtypeStruct((size_x, channels, plane), BF16),
    ]


def inner_scratch(channels, size_x, size_y, size_z):
    return [
        pltpu.VMEM((size_x - 2, channels, size_y, size_z), BF16),
        pltpu.VMEM((size_x - 2, channels, size_y, size_z), BF16),
        pltpu.VMEM((size_x, channels, size_y, size_z), BF16),
        pltpu.VMEM((2, channels * size_y, size_z), F32),
        pltpu.SemaphoreType.DMA((3 * size_x - 4,)),
    ]


def inner_planes(preact, upstream, activations):
    shape = preact.shape
    return pl.pallas_call(
        inner_kernel,
        in_specs=[HBM] * 3,
        out_specs=[VMEM] * 2,
        out_shape=inner_outputs(*shape),
        scratch_shapes=inner_scratch(*shape),
        compiler_params=params(INNER_VMEM),
        cost_estimate=cost(0, 6 * 2**20),
        name="inner",
    )(preact, upstream, activations)


def body_of(refs, index):
    planes = refs[2].shape[0] + 4
    if 2 <= index < planes - 2:
        return refs[2].at[index - 2]
    return refs[{0: 0, 1: 1, planes - 2: 3, planes - 1: 4}[index]]


def y_halo(refs, index):
    me = lax.axis_index("gy")
    low = jnp.where(me > 0, refs[0][index].astype(F32), 0.0)
    high = jnp.where(me < lax.axis_size("gy") - 1, refs[1][index].astype(F32), 0.0)
    return low, high


def z_picker(rows_y, size_z):
    shape = (rows_y * size_z, 2 * LANES)
    voxel = lax.broadcasted_iota(jnp.int32, shape, 0)
    lane = lax.broadcasted_iota(jnp.int32, shape, 1)
    wanted = jnp.where(lane < LANES, lane * size_z, (lane - LANES) * size_z + size_z - 1)
    return (voxel == wanted).astype(F32).astype(BF16)


def z_tiles(planes, rows_y, size_z, numbers):
    channels = planes[0].shape[0]
    columns = jnp.dot(
        jnp.concatenate(planes, axis=0), z_picker(rows_y, size_z), preferred_element_type=F32
    )
    low = jnp.zeros((channels, LANES), F32)
    high = jnp.zeros((channels, LANES), F32)
    for index, number in enumerate(numbers):
        rows = columns[index * channels : (index + 1) * channels]
        low = low + pltpu.roll(rows[:, :LANES], number * rows_y, 1)
        high = high + pltpu.roll(rows[:, LANES:], number * rows_y, 1)
    return low, high


def put_columns(columns, row_of, rows_y, size_z):
    shape = (2 * LANES, rows_y * size_z)
    source = lax.broadcasted_iota(jnp.int32, shape, 0)
    voxel = lax.broadcasted_iota(jnp.int32, shape, 1)
    number = source % LANES
    place = row_of(number) * size_z + jnp.where(source < LANES, 0, size_z - 1)
    place = jnp.where(number < rows_y, place, -1)
    put = (voxel == place).astype(F32).astype(BF16)
    rows = [jnp.concatenate(pair, axis=1) for pair in columns]
    return jnp.dot(
        jnp.concatenate(rows, axis=0).astype(BF16), put, preferred_element_type=F32
    )


def z_halo(low_ref, high_ref, planes, rows_y, size_z):
    columns = []
    for index in range(planes):
        shift = -index * rows_y % LANES
        columns.append(
            [pltpu.roll(ref[...].astype(F32), shift, 1) for ref in (low_ref, high_ref)]
        )
    return put_columns(columns, lambda number: number, rows_y, size_z)


def pair_z_halo(low_ref, high_ref, planes, size_y, size_z):
    me = lax.axis_index("gy")
    sides = []
    for ref in (low_ref, high_ref):
        first, second = ref[0].astype(F32), ref[1].astype(F32)
        lane = lax.broadcasted_iota(jnp.int32, first.shape, 1)
        own = jnp.where(me == 0, first, second)
        before = jnp.where(me == 0, 0.0, first)
        after = jnp.where(me == 0, second, 0.0)
        columns = []
        for index in range(planes):
            start = index * size_y
            columns.append(
                jnp.where(
                    lane < size_y,
                    pltpu.roll(own, -start % LANES, 1),
                    jnp.where(
                        lane == size_y,
                        pltpu.roll(before, (1 - start) % LANES, 1),
                        pltpu.roll(after, (size_y + 1 - start) % LANES, 1),
                    ),
                )
            )
        sides.append(columns)

    def row_of(number):
        return jnp.where(number < size_y, number + 1, jnp.where(number == size_y, 0, size_y + 1))

    return put_columns(list(zip(*sides)), row_of, size_y + 2, size_z)


def shifted_plane(index, refs, halo, g3):
    channels, plane = refs[0].shape
    size_z = refs[5].shape[-1]
    rows_y = plane // size_z + 2
    base = 3 * channels * index
    lane = lax.broadcasted_iota(jnp.int32, (channels, size_z), 1)
    low, high = y_halo(refs[5:7], index)
    body = body_of(refs[:5], index)
    for row in range(rows_y):
        cols = slice(row * size_z, (row + 1) * size_z)
        if row == 0:
            wide = low
        elif row == rows_y - 1:
            wide = high
        else:
            wide = body[:, (row - 1) * size_z : row * size_z].astype(F32)
        edge = 0.0 if halo is None else halo[index * channels : (index + 1) * channels, cols]
        before = jnp.where(lane == 0, edge, pltpu.roll(wide, 1, 1))
        after = jnp.where(lane == size_z - 1, edge, pltpu.roll(wide, size_z - 1, 1))
        g3[base : base + channels, cols] = before.astype(BF16)
        g3[base + channels : base + 2 * channels, cols] = wide.astype(BF16)
        g3[base + 2 * channels : base + 3 * channels, cols] = after.astype(BF16)


def weight_products(refs, halo, x_ref, g3, x3, acc):
    size_x, channels, plane = x_ref.shape
    size_z = refs[5].shape[-1]
    group = 3 * channels
    zero = jnp.zeros((channels, 2 * size_z), BF16)
    done = 0
    for x in range(size_x):
        while done < x + 3:
            shifted_plane(done, refs, halo, g3)
            done += 1
        value = x_ref[x]
        for b in range(3):
            at = slice(b * channels, (b + 1) * channels)
            start = (2 - b) * size_z
            x3[x, at, start : start + plane] = value
            if start:
                x3[x, at, :start] = zero[:, :start]
            if start < 2 * size_z:
                x3[x, at, start + plane :] = zero[:, start:]
        product = lax.dot_general(
            g3[x * group : (x + 3) * group, :],
            x3[x],
            (((1,), (1,)), ((), ())),
            preferred_element_type=F32,
        )
        if x == 0:
            acc[...] = product
        else:
            acc[...] += product


def to_flat(value, count, channels, flat):
    height, width = value.shape
    wide = value
    if height % LANES:
        wide = jnp.concatenate([wide, jnp.zeros((-height % LANES, width), F32)], axis=0)
    if width % LANES:
        wide = jnp.concatenate([wide, jnp.zeros((wide.shape[0], -width % LANES), F32)], axis=1)
    turned = wide.T
    for b in range(3):
        rows = turned[b * channels : (b + 1) * channels]
        for block in range(9):
            start = block * count
            cell = rows[:, start // LANES * LANES : (start // LANES + 1) * LANES]
            tap = (2 - block // 3) * 9 + b * 3 + 2 - block % 3
            shift = -start % LANES
            flat[pl.ds(tap, channels, stride=27), :] = pltpu.roll(cell, shift, 1) if shift else cell
    return flat[...].T[:count]


def spread_weights(whole, turned, weights):
    channels, taps = whole.shape
    group = 3 * channels
    whole = jnp.concatenate([whole, jnp.zeros((LANES - channels, taps), F32)], axis=0)
    whole = jnp.concatenate([whole, jnp.zeros((LANES, -taps % LANES), F32)], axis=1)
    turned[...] = whole.T
    for b in range(3):
        blocks = []
        for a in range(3):
            for c in range(3):
                tap = (2 - a) * 9 + (2 - b) * 3 + 2 - c
                blocks.append(turned[pl.ds(tap, channels, stride=27), :][:, :channels])
        zero = jnp.zeros((channels, group), F32)
        weights[b, :channels] = jnp.concatenate(blocks + [zero], axis=1).astype(BF16)
        weights[b, channels:] = jnp.concatenate([zero] + blocks, axis=1).astype(BF16)


def input_products(refs, halo, g3, weights, tile, out_ref):
    channels, size_x, size_y, size_z = out_ref.shape
    group = 3 * channels
    plane = size_y * size_z
    done = 0
    for pair in range(size_x // 2):
        while done < 2 * pair + 4:
            shifted_plane(done, refs, halo, g3)
            done += 1
        at = slice(2 * pair * group, (2 * pair + 4) * group)
        total = None
        for b in range(3):
            product = jnp.dot(
                weights[b],
                g3[at, b * size_z : b * size_z + plane],
                preferred_element_type=F32,
            )
            total = product if total is None else total + product
        for half in range(2):
            for y in range(size_y):
                tile[half, pl.ds(y, channels, stride=size_y), :] = total[
                    half * channels : (half + 1) * channels, y * size_z : (y + 1) * size_z
                ]
            out_ref[:, 2 * pair + half] = (
                tile[half].reshape(channels, size_y, size_z).astype(BF16)
            )


def g3_scratch(channels, size_x, size_y, size_z):
    return pltpu.VMEM(((size_x + 2) * 3 * channels, (size_y + 2) * size_z), BF16)


def x3_scratch(channels, size_x, size_y, size_z):
    return pltpu.VMEM((size_x, 3 * channels, (size_y + 2) * size_z), BF16)


def acc_scratch(channels):
    return pltpu.VMEM((9 * channels, 3 * channels), F32)


def flat_scratch(channels):
    return pltpu.VMEM((-(-27 * channels // LANES) * LANES, LANES), F32)


def dgrad_scratch(channels, size_x, size_y, size_z):
    return [
        g3_scratch(channels, size_x, size_y, size_z),
        flat_scratch(channels),
        pltpu.VMEM((3, 2 * channels, 12 * channels), BF16),
        pltpu.VMEM((2, channels * size_y, size_z), F32),
    ]


def wgrad_cost(channels, size_x, size_y, size_z):
    return cost(54 * channels * channels * size_x * (size_y + 2) * size_z, 4 * 2**20)


def dgrad_cost(channels, size_x, size_y, size_z):
    return cost(72 * channels * channels * size_x * size_y * size_z, 4 * 2**20)


def row_for_other(body, size_z):
    plane = body.shape[-1]
    low, high = body[:, :size_z].astype(F32), body[:, plane - size_z :].astype(F32)
    return jnp.where(lax.axis_index("gy") == 0, high, low).astype(BF16)


def pair_inner_kernel(*refs):
    first_ref, last_ref, m_ref = refs[3:6]
    g_ref, x_ref, side_ref, sent_ref = refs[6:10]
    tile_ref, tile_sems = refs[15:]
    share = m_ref[...]
    height = tile_ref.shape[0] - share.shape[0]
    if height:
        share = jnp.concatenate([share, jnp.zeros((height, share.shape[1]), F32)], axis=0)
    tile_ref[...] = share.astype(BF16)
    copies = [
        pltpu.make_async_copy(tile_ref, sent_ref.at[device], tile_sems.at[device])
        for device in range(sent_ref.shape[0])
    ]
    for copy in copies:
        copy.start()
    read_inner(*refs[:3], g_ref, x_ref, *refs[10:15])
    size_z = side_ref.shape[-1]
    size_x, channels, plane = x_ref.shape
    size_y = plane // size_z
    bodies = [first_ref] + [g_ref.at[x] for x in range(size_x - 2)] + [last_ref]
    for x, body in enumerate(bodies):
        side_ref[x] = row_for_other(body, size_z)
    low, high = z_tiles([body[...] for body in bodies], size_y, size_z, range(1, size_x + 1))
    side_ref[size_x] = low.astype(BF16)
    side_ref[size_x + 1] = high.astype(BF16)
    low, high = z_tiles([x_ref[x] for x in range(size_x)], size_y, size_z, range(size_x))
    side_ref[size_x + 2] = (low + pltpu.roll(high, size_x * size_y, 1)).astype(BF16)
    for copy in copies:
        copy.wait()


def pair_inner(preact, upstream, activations, first, last, share, sent_shape):
    shape = preact.shape
    channels, size_x, _, size_z = shape
    return pl.pallas_call(
        pair_inner_kernel,
        in_specs=[HBM] * 3 + [VMEM] * 3,
        out_specs=[VMEM] * 3 + [HBM],
        out_shape=inner_outputs(*shape)
        + [
            jax.ShapeDtypeStruct((size_x + 3, channels, size_z), BF16),
            jax.ShapeDtypeStruct(sent_shape, BF16),
        ],
        scratch_shapes=inner_scratch(*shape)
        + [pltpu.VMEM(sent_shape[1:], BF16), pltpu.SemaphoreType.DMA((sent_shape[0],))],
        compiler_params=params(INNER_VMEM),
        cost_estimate=cost(0, 6 * 2**20),
        name="inner",
    )(preact, upstream, activations, first, last, share)


def side_kernel(odd_ref, even_ref, own_ref, sent_ref, xlo_ref, xhi_ref):
    size_x = own_ref.shape[0] - 3
    size_z = own_ref.shape[-1]
    size_y = xlo_ref.shape[-1] // size_z
    odd = lax.rem(lax.axis_index("gx"), 2) == 1
    first, second = even_ref[...].astype(F32), odd_ref[...].astype(F32)
    low = jnp.where(odd, first, second).astype(BF16)
    high = jnp.where(odd, second, first).astype(BF16)
    xlo_ref[...] = low
    xhi_ref[...] = high
    sent_ref[0] = row_for_other(low, size_z)
    for x in range(size_x):
        sent_ref[x + 1] = own_ref[x]
    sent_ref[size_x + 1] = row_for_other(high, size_z)
    tiles = z_tiles([low, high], size_y, size_z, (0, size_x + 1))
    for k in range(2):
        sent_ref[size_x + 2 + k] = (own_ref[size_x + k].astype(F32) + tiles[k]).astype(BF16)
    sent_ref[size_x + 4] = own_ref[size_x + 2]


def side(halves, own):
    plane = jax.ShapeDtypeStruct(halves[0].shape, BF16)
    return pl.pallas_call(
        side_kernel,
        in_specs=[VMEM] * 3,
        out_specs=[VMEM] * 3,
        out_shape=[
            jax.ShapeDtypeStruct((own.shape[0] + 2, *own.shape[1:]), BF16),
            plane,
            plane,
        ],
        compiler_params=params(),
        cost_estimate=cost(2**25, 2**19),
        name="side",
    )(*halves, own)


def both_columns(is_first, own, other, number, area):
    first = jnp.where(is_first, own, other).astype(F32)
    second = jnp.where(is_first, other, own).astype(F32)
    lane = lax.broadcasted_iota(jnp.int32, first.shape, 1)
    return jnp.where(
        lane < area,
        pltpu.roll(first, -number * area % LANES, 1),
        pltpu.roll(second, (1 - number) * area % LANES, 1),
    )


def join_kernel(area, own_ref, other_ref, low_ref, high_ref):
    at = own_ref.shape[0] - 3
    me = lax.axis_index("gy")
    for k, out_ref in enumerate((low_ref, high_ref)):
        out_ref[me] = own_ref[at + k]
        out_ref[1 - me] = other_ref[at + k]
    own, other = own_ref[at + 2].astype(F32), other_ref[at + 2].astype(F32)
    high_ref[2] = both_columns(me == 0, own, other, 1, area).astype(BF16)


def join(own, other, area):
    return pl.pallas_call(
        functools.partial(join_kernel, area),
        in_specs=[VMEM] * 2,
        out_specs=[VMEM] * 2,
        out_shape=[jax.ShapeDtypeStruct((n, *own.shape[1:]), BF16) for n in (2, 3)],
        compiler_params=params(),
        cost_estimate=cost(0, 2**17),
        name="join",
    )(own, other)


def pair_wgrad_kernel(span, *refs):
    x_ref, mine_ref, theirs_ref, g3, x3, acc = refs[7:]
    channels = x_ref.shape[1]
    weight_products(refs, None, x_ref, g3, x3, acc)
    is_first = lax.axis_index("gy") == 0
    width = 3 * channels
    halves = []
    for half in range(2):
        at = range(half * span, 9 * channels, 2 * span)
        halves.append(jnp.concatenate([acc[start : start + span, :] for start in at], axis=0))
    spare = jnp.zeros((halves[0].shape[0], mine_ref.shape[1] - width), F32)
    for ref, order in ((mine_ref, halves), (theirs_ref, halves[::-1])):
        picked = jnp.where(is_first, order[0], order[1])
        ref[...] = jnp.concatenate([picked, spare], axis=1)


def pair_wgrad(sources, planes_x, shape, span):
    channels = shape[0]
    width = -(-3 * channels // LANES) * LANES
    part = jax.ShapeDtypeStruct((9 * channels // 2, width), F32)
    return pl.pallas_call(
        functools.partial(pair_wgrad_kernel, span),
        in_specs=[VMEM] * 8,
        out_specs=[VMEM] * 2,
        out_shape=[part, part],
        scratch_shapes=[g3_scratch(*shape), x3_scratch(*shape), acc_scratch(channels)],
        compiler_params=params(32 * 2**20),
        cost_estimate=wgrad_cost(*shape),
        name="wgrad",
    )(*sources, planes_x)


def edge_kernel(span, sizes, own_ref, other_ref, ztiles_ref, below_ref, edge_ref):
    size_x, size_y = sizes
    channels = below_ref.shape[1]
    count = channels // 2
    area = size_x * size_y
    is_first = lax.axis_index("gy") == 0
    at = own_ref.shape[0] - 1
    own, other = own_ref[at].astype(F32), other_ref[at].astype(F32)
    columns = (both_columns(is_first, own, other, 0, area), below_ref[2].astype(F32))
    lane = lax.broadcasted_iota(jnp.int32, (channels, LANES), 1)
    row = lane % size_y
    few = lax.broadcasted_iota(jnp.int32, (count, LANES), 1)
    for number, (tile_ref, value) in enumerate(zip((below_ref, ztiles_ref), columns)):
        jump = area - size_y + 1
        before = jnp.where(lane >= area, pltpu.roll(value, jump, 1), 0.0)
        after = jnp.where(lane < area, pltpu.roll(value, LANES - jump, 1), 0.0)
        right = jnp.concatenate(
            [
                jnp.where(row > 0, pltpu.roll(value, 1, 1), before),
                value,
                jnp.where(row < size_y - 1, pltpu.roll(value, LANES - 1, 1), after),
            ],
            axis=0,
        )
        tiles = []
        for device in range(2):
            tile = tile_ref[device].astype(F32)
            halves = [
                jnp.concatenate(
                    [tile[s : s + span] for s in range(half * span, channels, 2 * span)], axis=0
                )
                for half in range(2)
            ]
            tiles.append(jnp.where(is_first, halves[0], halves[1]))
        left = []
        for a in range(3):
            first = pltpu.roll(tiles[0], -a * size_y % LANES, 1)
            second = pltpu.roll(tiles[1], (area - a * size_y) % LANES, 1)
            left.append(jnp.where(few < area, first, jnp.where(few < 2 * area, second, 0.0)))
        product = lax.dot_general(
            jnp.concatenate(left, axis=0).astype(BF16),
            right.astype(BF16),
            (((1,), (1,)), ((), ())),
            preferred_element_type=F32,
        )
        spare = jnp.zeros((3 * count, edge_ref.shape[2] - 3 * channels), F32)
        edge_ref[number] = jnp.concatenate([product, spare], axis=1)


def z_edges(own, other, ztiles, below, span, sizes, width):
    channels = own.shape[1]
    return pl.pallas_call(
        functools.partial(edge_kernel, span, sizes),
        in_specs=[VMEM] * 4,
        out_specs=VMEM,
        out_shape=jax.ShapeDtypeStruct((2, 3 * channels // 2, width), F32),
        compiler_params=params(),
        cost_estimate=cost(2**27, 2**20),
        name="edges",
    )(own, other, ztiles, below)


def finish_kernel(scale, rows, channels, mine_ref, other_ref, edge_ref, part_ref, flat, lines, chunks):
    count = channels // 2
    taps = 27 * channels
    total = mine_ref[...] + other_ref[...]
    blocks = []
    for a in range(3):
        for c in range(3):
            block = total[(3 * a + c) * count : (3 * a + c + 1) * count]
            if c != 1:
                block = block + edge_ref[c // 2, a * count : (a + 1) * count, :]
            blocks.append(block)
    whole = to_flat(jnp.concatenate(blocks, axis=0) * scale, count, channels, flat)
    pieces = whole.shape[1] // LANES
    for k in range(pieces):
        lines[k * count : (k + 1) * count, :] = whole[:, k * LANES : (k + 1) * LANES]
    number, tall, width = part_ref.shape
    parts = []
    for r in range(rows):
        found = [lines[pl.ds(k * count + r, number, stride=rows), :] for k in range(pieces)]
        parts.append(jnp.concatenate(found, axis=1)[:, :taps])
    line = jnp.concatenate(parts, axis=1)
    chunks[...] = jnp.zeros_like(chunks)
    for k in range(line.shape[1] // width):
        chunks[pl.ds(k, number, stride=tall), :] = line[:, k * width : (k + 1) * width]
    part_ref[...] = chunks[...].reshape(part_ref.shape).astype(BF16)


def finish(mine, other, edge, scale, rows, channels, part_shape):
    return pl.pallas_call(
        functools.partial(finish_kernel, scale, rows, channels),
        in_specs=[VMEM] * 3,
        out_specs=VMEM,
        out_shape=jax.ShapeDtypeStruct(part_shape, BF16),
        scratch_shapes=[
            flat_scratch(channels),
            pltpu.VMEM((-(-27 * channels // LANES) * channels // 2, LANES), F32),
            pltpu.VMEM((part_shape[0] * part_shape[1], part_shape[2]), F32),
        ],
        compiler_params=params(),
        cost_estimate=cost(2**24, 2**20),
        name="finish",
    )(mine, other, edge)


def adam_step(master, first, second, weight_grad):
    new_first = 0.9 * first + 0.1 * weight_grad
    new_second = 0.999 * second + 0.001 * weight_grad * weight_grad
    corr_first = 1.0 - (0.9**10) ** 10
    corr_second = 1.0 - (0.999**10) ** 10
    update = new_first / corr_first / (jnp.sqrt(new_second / corr_second) + 1e-08) + 0.01 * master
    return master - 0.05 * update, new_first, new_second


def adam_kernel(parts_ref, master_ref, first_ref, second_ref, *out_refs):
    weight_grad = parts_ref[0].astype(F32)
    for source in range(1, parts_ref.shape[0]):
        weight_grad = weight_grad + parts_ref[source].astype(F32)
    weight_grad = weight_grad[: master_ref.shape[0]]
    results = adam_step(master_ref[...], first_ref[...], second_ref[...], weight_grad)
    for out_ref, result in zip(out_refs, (weight_grad, *results)):
        out_ref[...] = result


def adam(parts, *states):
    share = states[0].shape[0]
    tiled = [state.reshape(share // LANES, LANES) for state in states]
    result = jax.ShapeDtypeStruct(tiled[0].shape, F32)
    outs = pl.pallas_call(
        adam_kernel,
        in_specs=[VMEM] * 4,
        out_specs=[VMEM] * 4,
        out_shape=[result] * 4,
        compiler_params=params(),
        cost_estimate=cost(2**18, 2**18),
        name="adam",
    )(parts, *tiled)
    return tuple(out.reshape(share) for out in outs)


def spread_kernel(rows, w_ref, weights_ref, turned, chunks, lines):
    count, height, width = w_ref.shape
    channels = rows * count
    taps = 27 * channels
    chunks[...] = w_ref[...].astype(F32).reshape(chunks.shape)
    line = jnp.concatenate(
        [chunks[pl.ds(k, count, stride=height), :] for k in range(rows * taps // width)], axis=1
    )
    pieces = lines.shape[0] // channels
    spare = jnp.zeros((count, pieces * LANES - taps), F32)
    for r in range(rows):
        found = jnp.concatenate([line[:, r * taps : (r + 1) * taps], spare], axis=1)
        for k in range(pieces):
            lines[pl.ds(k * channels + r, count, stride=rows), :] = found[
                :, k * LANES : (k + 1) * LANES
            ]
    whole = [lines[k * channels : (k + 1) * channels, :] for k in range(pieces)]
    spread_weights(jnp.concatenate(whole, axis=1)[:, :taps], turned, weights_ref)


def spread(kernel, channels, rows):
    return pl.pallas_call(
        functools.partial(spread_kernel, rows),
        in_specs=[VMEM],
        out_specs=VMEM,
        out_shape=jax.ShapeDtypeStruct((3, 2 * channels, 12 * channels), BF16),
        scratch_shapes=[
            flat_scratch(channels),
            pltpu.VMEM((kernel.shape[0] * kernel.shape[1], kernel.shape[2]), F32),
            pltpu.VMEM((-(-27 * channels // LANES) * channels, LANES), F32),
        ],
        compiler_params=params(),
        cost_estimate=cost(2**20, 2**21),
        name="spread",
    )(kernel)


def pair_dgrad_kernel(*refs):
    weights_ref, out_ref, g3, tile = refs[9:]
    _, size_x, size_y, size_z = out_ref.shape
    halo = pair_z_halo(refs[7], refs[8], size_x + 2, size_y, size_z)
    input_products(refs, halo, g3, weights_ref, tile, out_ref)


def pair_dgrad(sources, weights, shape):
    channels, _, size_y, size_z = shape
    return pl.pallas_call(
        pair_dgrad_kernel,
        in_specs=[VMEM] * 10,
        out_specs=VMEM,
        out_shape=jax.ShapeDtypeStruct(shape, BF16),
        scratch_shapes=[g3_scratch(*shape), pltpu.VMEM((2, channels * size_y, size_z), F32)],
        compiler_params=params(32 * 2**20),
        cost_estimate=dgrad_cost(*shape),
        name="dgrad",
    )(*sources, weights)


def pair_program(activations, preact, upstream, master, first_moment, second_moment, scale):
    shape = activations.shape
    channels, size_x, size_y, _ = shape
    devices = math.prod(lax.axis_size(a) for a in AXES)
    rows = channels // devices
    span = lax.axis_size("gz") * rows
    used = master.shape[0] // LANES
    tall = -(-used // 16) * 16
    first, last, *swaps = faces(preact, upstream, "gx")
    odd_halves = swapped(swaps[1], "gx", 1)
    even_halves = swapped(swaps[0], "gx", 0)
    inner, planes_x, own, sent = pair_inner(
        preact,
        upstream,
        activations,
        first,
        last,
        master.reshape(used, LANES),
        (devices, tall, LANES),
    )
    kernel = lax.all_to_all(sent, AXES, 0, 0, tiled=True)
    own, xlo, xhi = side((odd_halves, even_halves), own)
    planes = (xlo, first, inner, last, xhi)
    other = shifted(own, {"gy": "swap"})
    zlo, zhi = join(own, other, size_x * size_y)
    below = shifted(zhi, {"gz": 1})
    sources = (*planes, other, other)
    mine, theirs = pair_wgrad(sources, planes_x, shape, span)
    theirs, below = lax.optimization_barrier((theirs, below))
    theirs = shifted(theirs, {"gy": "swap"})
    edge = z_edges(own, other, zlo, below, span, (size_x, size_y), mine.shape[1])
    part = finish(mine, theirs, edge, scale, rows, channels, (devices // 2, tall, LANES))
    part, kernel, zlo = lax.optimization_barrier((part, kernel, zlo))
    parts = lax.all_to_all(part, ("gx", "gz"), 0, 0, tiled=True)
    above = shifted(zlo, {"gz": -1})
    weights = spread(kernel, channels, rows)
    grad_input = pair_dgrad((*sources, below, above), weights, shape)
    return grad_input, *adam(parts, master, first_moment, second_moment)


def yface_kernel(*refs):
    low_ref, high_ref = refs[5:]
    size_z = low_ref.shape[-1]
    for index in range(low_ref.shape[0]):
        body = body_of(refs[:5], index)
        plane = body.shape[-1]
        low_ref[index] = body[:, :size_z]
        high_ref[index] = body[:, plane - size_z :]


def y_faces(planes, size_z):
    inner, channels, _ = planes[2].shape
    face = jax.ShapeDtypeStruct((inner + 4, channels, size_z), BF16)
    return pl.pallas_call(
        yface_kernel,
        in_specs=[VMEM] * 5,
        out_specs=[VMEM] * 2,
        out_shape=[face] * 2,
        compiler_params=params(),
        cost_estimate=cost(0, 2**19),
        name="yfaces",
    )(*planes)


def zface_kernel(*refs):
    zlo_ref, zhi_ref = refs[7:]
    size_z = refs[5].shape[-1]
    whole = []
    for index in range(refs[5].shape[0]):
        low, high = y_halo(refs[5:7], index)
        body = body_of(refs[:5], index)[...]
        whole.append(jnp.concatenate([low.astype(BF16), body, high.astype(BF16)], axis=1))
    low, high = z_tiles(whole, whole[0].shape[1] // size_z, size_z, range(len(whole)))
    zlo_ref[...] = low.astype(BF16)
    zhi_ref[...] = high.astype(BF16)


def z_faces(planes, y_halos):
    face = jax.ShapeDtypeStruct((planes[0].shape[0], LANES), BF16)
    return pl.pallas_call(
        zface_kernel,
        in_specs=[VMEM] * 7,
        out_specs=[VMEM] * 2,
        out_shape=[face, face],
        compiler_params=params(),
        cost_estimate=cost(2**27, 2**21),
        name="zfaces",
    )(*planes, *y_halos)


def wgrad_kernel(scale, *refs):
    x_ref, part_ref, g3, x3, acc, flat = refs[9:]
    size_x, channels, plane = x_ref.shape
    size_z = refs[5].shape[-1]
    halo = z_halo(refs[7], refs[8], size_x + 2, plane // size_z + 2, size_z)
    weight_products(refs, halo, x_ref, g3, x3, acc)
    whole = to_flat(acc[...] * scale, channels, channels, flat)
    part_ref[...] = whole[:, : part_ref.shape[1]].astype(BF16)


def wgrad(sources, planes_x, shape, scale):
    channels = shape[0]
    return pl.pallas_call(
        functools.partial(wgrad_kernel, scale),
        in_specs=[VMEM] * 10,
        out_specs=VMEM,
        out_shape=jax.ShapeDtypeStruct((channels, 27 * channels), BF16),
        scratch_shapes=[
            g3_scratch(*shape),
            x3_scratch(*shape),
            acc_scratch(channels),
            flat_scratch(channels),
        ],
        compiler_params=params(32 * 2**20),
        cost_estimate=wgrad_cost(*shape),
        name="wgrad",
    )(*sources, planes_x)


def dgrad_kernel(*refs):
    w_ref, out_ref, g3, turned, weights, tile = refs[9:]
    _, size_x, size_y, size_z = out_ref.shape
    spread_weights(w_ref[...].astype(F32), turned, weights)
    halo = z_halo(refs[7], refs[8], size_x + 2, size_y + 2, size_z)
    input_products(refs, halo, g3, weights, tile, out_ref)


def dgrad(sources, kernel, shape):
    return pl.pallas_call(
        dgrad_kernel,
        in_specs=[VMEM] * 10,
        out_specs=VMEM,
        out_shape=jax.ShapeDtypeStruct(shape, BF16),
        scratch_shapes=dgrad_scratch(*shape),
        compiler_params=params(32 * 2**20),
        cost_estimate=dgrad_cost(*shape),
        name="dgrad",
    )(*sources, kernel)


def general_program(activations, preact, upstream, master, first_moment, second_moment, scale):
    shape = activations.shape
    channels, _, _, size_z = shape
    devices = math.prod(lax.axis_size(a) for a in AXES)
    share = master.shape[0]
    first, last = faces(preact, upstream)
    x_halos = (shifted(last, {"gx": 1}), shifted(first, {"gx": -1}))
    inner, planes_x = inner_planes(preact, upstream, activations)
    sent = jnp.broadcast_to(master.astype(BF16).reshape(1, 1, share), (devices, 1, share))
    kernel = lax.all_to_all(sent, AXES, 0, 0, tiled=True).reshape(channels, 27 * channels)
    planes = (x_halos[0], first, inner, last, x_halos[1])
    y_sent = y_faces(planes, size_z)
    y_halos = (shifted(y_sent[1], {"gy": 1}), shifted(y_sent[0], {"gy": -1}))
    zlo, zhi = z_faces(planes, y_halos)
    z_halos = (shifted(zhi, {"gz": 1}), shifted(zlo, {"gz": -1}))
    sources = (*planes, *y_halos, *z_halos)
    part = wgrad(sources, planes_x, shape, scale)
    part, kernel = lax.optimization_barrier((part, kernel))
    parts = lax.all_to_all(part.reshape(devices, 1, share), AXES, 0, 0, tiled=True)
    grad_input = dgrad(sources, kernel, shape)
    weight_grad = jnp.sum(parts.astype(F32), axis=0).reshape(-1)
    results = adam_step(master, first_moment, second_moment, weight_grad)
    return grad_input, weight_grad, *results


def shifted(value, moves):
    names = tuple(moves)
    sizes = [lax.axis_size(name) for name in names]
    pairs = []
    for source in range(math.prod(sizes)):
        rest, coords = source, []
        for size in reversed(sizes):
            coords.insert(0, rest % size)
            rest //= size
        coords = [
            (at + moves[name]) if moves[name] != "swap" else 1 - at
            for at, name in zip(coords, names)
        ]
        if all(0 <= at < size for at, size in zip(coords, sizes)):
            target = 0
            for at, size in zip(coords, sizes):
                target = target * size + at
            pairs.append((source, target))
    return lax.ppermute(value, names if len(names) > 1 else names[0], pairs)


def swapped(value, axis, start):
    pairs = []
    for low in range(start, lax.axis_size(axis) - 1, 2):
        pairs += [(low, low + 1), (low + 1, low)]
    return lax.ppermute(value, axis, pairs)


def local(activations, preact, upstream, master, first_moment, second_moment):
    channels, size_x, size_y, size_z = activations.shape
    devices = math.prod(lax.axis_size(a) for a in AXES)
    share = master.shape[0]
    scale = 1.0 / math.sqrt(size_x * size_y * size_z * devices)
    in_pairs = (
        lax.axis_size("gy") == 2
        and channels % devices == 0
        and share % LANES == 0
        and channels // devices * lax.axis_size("gz") % 8 == 0
        and 2 * size_x * size_y <= LANES
        and (size_x + 2) * size_y <= LANES
    )
    program = pair_program if in_pairs else general_program
    return program(
        activations, preact, upstream, master, first_moment, second_moment, scale
    )


def solution(mesh):
    volume = P(None, "gx", "gy", "gz")
    flat = P(AXES)
    return jax.shard_map(
        local,
        mesh=mesh,
        in_specs=(volume, volume, volume, flat, flat, flat),
        out_specs=(volume, flat, flat, flat, flat),
        check_vma=False,
    )
```

```python
import functools
import math

import jax
import jax.numpy as jnp
from jax import lax
from jax.experimental import pallas as pl
from jax.experimental.pallas import tpu as pltpu
from jax.sharding import PartitionSpec as P

AXES = ("gx", "gy", "gz")
LANES = 128
VMEM = pl.BlockSpec(memory_space=pltpu.VMEM)
HBM = pl.BlockSpec(memory_space=pltpu.HBM)
F32 = jnp.float32
BF16 = jnp.bfloat16
FACES_VMEM = 55_900_000
INNER_VMEM = 53_000_000


def params(limit=24 * 2**20):
    return pltpu.CompilerParams(vmem_limit_bytes=limit)


def cost(flops, moved):
    return pl.CostEstimate(flops=flops, bytes_accessed=moved, transcendentals=0)


def to_planes(value, tile, write, rows=1):
    channels, size_y, size_z = value.shape
    count = channels // rows
    tile[...] = value.astype(F32).reshape(channels * size_y, size_z)
    for y in range(size_y):
        for r in range(rows):
            picked = tile[pl.ds(r * size_y + y, count, stride=rows * size_y), :]
            write(slice(r * count, (r + 1) * count), y, picked.astype(BF16))


def masked(p, u):
    return jnp.where(p > 0, u, jnp.zeros_like(u))


def face_kernel(axis, rows, p_ref, u_ref, *refs):
    p_buf, u_buf, tile, sems = refs[-4:]
    out_refs, swap_refs = refs[:2], refs[2:-4]
    size_x, size_z = p_ref.shape[1], p_ref.shape[3]
    copies = []
    for k, x in enumerate((0, size_x - 1)):
        pair = (
            pltpu.make_async_copy(p_ref.at[:, x], p_buf.at[k], sems.at[2 * k]),
            pltpu.make_async_copy(u_ref.at[:, x], u_buf.at[k], sems.at[2 * k + 1]),
        )
        for copy in pair:
            copy.start()
        copies.append(pair)
    for k, out_ref in enumerate(out_refs):
        for copy in copies[k]:
            copy.wait()

        def write(at, y, value):
            out_ref[at, y * size_z : (y + 1) * size_z] = value

        to_planes(masked(p_buf[k], u_buf[k]), tile.at[k], write, rows)
    if axis is not None:
        odd = is_odd(axis)

        @pl.when(odd)
        def _():
            for swap_ref, out_ref in zip(swap_refs, out_refs):
                swap_ref[...] = out_ref[...]

        @pl.when(jnp.logical_not(odd))
        def _():
            for swap_ref, out_ref in zip(swap_refs, out_refs[::-1]):
                swap_ref[...] = out_ref[...]


def faces(preact, upstream, axis=None, rows=1):
    channels, size_x, size_y, size_z = preact.shape
    face = jax.ShapeDtypeStruct((channels, size_y * size_z), BF16)
    buffer = pltpu.VMEM((2, channels, size_y, size_z), BF16)
    count = 2 if axis is None else 4
    return pl.pallas_call(
        functools.partial(face_kernel, axis, rows),
        in_specs=[HBM, HBM],
        out_specs=[VMEM] * count,
        out_shape=[face] * count,
        scratch_shapes=[
            buffer,
            buffer,
            pltpu.VMEM((2, channels * size_y, size_z), F32),
            pltpu.SemaphoreType.DMA((4,)),
        ],
        compiler_params=params(FACES_VMEM),
        cost_estimate=cost(0, 2**20),
        name="faces",
    )(preact, upstream)


def read_inner(rows, p_ref, u_ref, a_ref, g_ref, x_ref, p_buf, u_buf, a_buf, tile, sems):
    channels, size_x, size_y, size_z = a_ref.shape
    inner = size_x - 2
    copies = []
    for x in range(inner):
        copies.append(
            (
                pltpu.make_async_copy(p_ref.at[:, x + 1], p_buf.at[x], sems.at[x]),
                pltpu.make_async_copy(u_ref.at[:, x + 1], u_buf.at[x], sems.at[inner + x]),
            )
        )
    for x in range(size_x):
        copies.append(
            (pltpu.make_async_copy(a_ref.at[:, x], a_buf.at[x], sems.at[2 * inner + x]),)
        )
    for group in copies:
        for copy in group:
            copy.start()
    for x in range(inner):
        for copy in copies[x]:
            copy.wait()

        def write(at, y, value):
            g_ref[x, at, y * size_z : (y + 1) * size_z] = value

        to_planes(masked(p_buf[x], u_buf[x]), tile.at[x % 2], write, rows)
    for x in range(size_x):
        copies[inner + x][0].wait()

        def write(at, y, value):
            x_ref[x, at, y * size_z : (y + 1) * size_z] = value

        to_planes(a_buf[x], tile.at[x % 2], write)


def inner_kernel(*refs):
    read_inner(1, *refs)


def inner_outputs(channels, size_x, size_y, size_z):
    plane = size_y * size_z
    return [
        jax.ShapeDtypeStruct((size_x - 2, channels, plane), BF16),
        jax.ShapeDtypeStruct((size_x, channels, plane), BF16),
    ]


def inner_scratch(channels, size_x, size_y, size_z):
    return [
        pltpu.VMEM((size_x - 2, channels, size_y, size_z), BF16),
        pltpu.VMEM((size_x - 2, channels, size_y, size_z), BF16),
        pltpu.VMEM((size_x, channels, size_y, size_z), BF16),
        pltpu.VMEM((2, channels * size_y, size_z), F32),
        pltpu.SemaphoreType.DMA((3 * size_x - 4,)),
    ]


def inner_planes(preact, upstream, activations):
    shape = preact.shape
    return pl.pallas_call(
        inner_kernel,
        in_specs=[HBM] * 3,
        out_specs=[VMEM] * 2,
        out_shape=inner_outputs(*shape),
        scratch_shapes=inner_scratch(*shape),
        compiler_params=params(INNER_VMEM),
        cost_estimate=cost(0, 6 * 2**20),
        name="inner",
    )(preact, upstream, activations)


def body_of(refs, index):
    planes = refs[2].shape[0] + 4
    if 2 <= index < planes - 2:
        return refs[2].at[index - 2]
    return refs[{0: 0, 1: 1, planes - 2: 3, planes - 1: 4}[index]]


def y_halo(refs, index):
    me = lax.axis_index("gy")
    low = jnp.where(me > 0, refs[0][index].astype(F32), 0.0)
    high = jnp.where(me < lax.axis_size("gy") - 1, refs[1][index].astype(F32), 0.0)
    return low, high


def z_picker(rows_y, size_z):
    shape = (rows_y * size_z, 2 * LANES)
    voxel = lax.broadcasted_iota(jnp.int32, shape, 0)
    lane = lax.broadcasted_iota(jnp.int32, shape, 1)
    wanted = jnp.where(lane < LANES, lane * size_z, (lane - LANES) * size_z + size_z - 1)
    return (voxel == wanted).astype(F32).astype(BF16)


def z_tiles(planes, rows_y, size_z, numbers):
    channels = planes[0].shape[0]
    columns = jnp.dot(
        jnp.concatenate(planes, axis=0), z_picker(rows_y, size_z), preferred_element_type=F32
    )
    low = jnp.zeros((channels, LANES), F32)
    high = jnp.zeros((channels, LANES), F32)
    for index, number in enumerate(numbers):
        rows = columns[index * channels : (index + 1) * channels]
        low = low + pltpu.roll(rows[:, :LANES], number * rows_y, 1)
        high = high + pltpu.roll(rows[:, LANES:], number * rows_y, 1)
    return low, high


def put_columns(columns, row_of, rows_y, size_z):
    shape = (2 * LANES, rows_y * size_z)
    source = lax.broadcasted_iota(jnp.int32, shape, 0)
    voxel = lax.broadcasted_iota(jnp.int32, shape, 1)
    number = source % LANES
    place = row_of(number) * size_z + jnp.where(source < LANES, 0, size_z - 1)
    place = jnp.where(number < rows_y, place, -1)
    put = (voxel == place).astype(F32).astype(BF16)
    rows = [jnp.concatenate(pair, axis=1) for pair in columns]
    return jnp.dot(
        jnp.concatenate(rows, axis=0).astype(BF16), put, preferred_element_type=F32
    )


def z_halo(low_ref, high_ref, planes, rows_y, size_z):
    columns = []
    for index in range(planes):
        shift = -index * rows_y % LANES
        columns.append(
            [pltpu.roll(ref[...].astype(F32), shift, 1) for ref in (low_ref, high_ref)]
        )
    return put_columns(columns, lambda number: number, rows_y, size_z)


def pair_z_halo(even_ref, odd_ref, planes, size_y, size_z):
    me, odd = lax.axis_index("gy"), is_odd("gz")
    sides = []
    for low, high in ((even_ref, odd_ref), (odd_ref, even_ref)):
        first, second = (either(odd, low[k], high[k]) for k in range(2))
        lane = lax.broadcasted_iota(jnp.int32, first.shape, 1)
        own = jnp.where(me == 0, first, second)
        before = jnp.where(me == 0, 0.0, first)
        after = jnp.where(me == 0, second, 0.0)
        columns = []
        for index in range(planes):
            start = index * size_y
            columns.append(
                jnp.where(
                    lane < size_y,
                    pltpu.roll(own, -start % LANES, 1),
                    jnp.where(
                        lane == size_y,
                        pltpu.roll(before, (1 - start) % LANES, 1),
                        pltpu.roll(after, (size_y + 1 - start) % LANES, 1),
                    ),
                )
            )
        sides.append(columns)

    def row_of(number):
        return jnp.where(number < size_y, number + 1, jnp.where(number == size_y, 0, size_y + 1))

    return put_columns(list(zip(*sides)), row_of, size_y + 2, size_z)


def shifted_plane(index, refs, halo, g3):
    channels, plane = refs[0].shape
    size_z = refs[5].shape[-1]
    rows_y = plane // size_z + 2
    base = 3 * channels * index
    lane = lax.broadcasted_iota(jnp.int32, (channels, size_z), 1)
    low, high = y_halo(refs[5:7], index)
    body = body_of(refs[:5], index)
    for row in range(rows_y):
        cols = slice(row * size_z, (row + 1) * size_z)
        if row == 0:
            wide = low
        elif row == rows_y - 1:
            wide = high
        else:
            wide = body[:, (row - 1) * size_z : row * size_z].astype(F32)
        edge = 0.0 if halo is None else halo[index * channels : (index + 1) * channels, cols]
        before = jnp.where(lane == 0, edge, pltpu.roll(wide, 1, 1))
        after = jnp.where(lane == size_z - 1, edge, pltpu.roll(wide, size_z - 1, 1))
        g3[base : base + channels, cols] = before.astype(BF16)
        g3[base + channels : base + 2 * channels, cols] = wide.astype(BF16)
        g3[base + 2 * channels : base + 3 * channels, cols] = after.astype(BF16)


def weight_products(refs, halo, x_ref, g3, x3, acc):
    size_x, channels, plane = x_ref.shape
    size_z = refs[5].shape[-1]
    group = 3 * channels
    zero = jnp.zeros((channels, 2 * size_z), BF16)
    done = 0
    for x in range(size_x):
        while done < x + 3:
            shifted_plane(done, refs, halo, g3)
            done += 1
        value = x_ref[x]
        for b in range(3):
            at = slice(b * channels, (b + 1) * channels)
            start = (2 - b) * size_z
            x3[x, at, start : start + plane] = value
            if start:
                x3[x, at, :start] = zero[:, :start]
            if start < 2 * size_z:
                x3[x, at, start + plane :] = zero[:, start:]
        product = lax.dot_general(
            g3[x * group : (x + 3) * group, :],
            x3[x],
            (((1,), (1,)), ((), ())),
            preferred_element_type=F32,
        )
        if x == 0:
            acc[...] = product
        else:
            acc[...] += product


def to_flat(value, count, channels, flat):
    height, width = value.shape
    wide = value
    if height % LANES:
        wide = jnp.concatenate([wide, jnp.zeros((-height % LANES, width), F32)], axis=0)
    if width % LANES:
        wide = jnp.concatenate([wide, jnp.zeros((wide.shape[0], -width % LANES), F32)], axis=1)
    turned = wide.T
    for b in range(3):
        rows = turned[b * channels : (b + 1) * channels]
        for block in range(9):
            start = block * count
            cell = rows[:, start // LANES * LANES : (start // LANES + 1) * LANES]
            tap = (2 - block // 3) * 9 + b * 3 + 2 - block % 3
            shift = -start % LANES
            flat[pl.ds(tap, channels, stride=27), :] = pltpu.roll(cell, shift, 1) if shift else cell
    return flat[...].T[:count]


def spread_weights(whole, turned, weights):
    channels, taps = whole.shape
    group = 3 * channels
    whole = jnp.concatenate([whole, jnp.zeros((LANES - channels, taps), F32)], axis=0)
    whole = jnp.concatenate([whole, jnp.zeros((LANES, -taps % LANES), F32)], axis=1)
    turned[...] = whole.T
    for b in range(3):
        blocks = []
        for a in range(3):
            for c in range(3):
                tap = (2 - a) * 9 + (2 - b) * 3 + 2 - c
                blocks.append(turned[pl.ds(tap, channels, stride=27), :][:, :channels])
        zero = jnp.zeros((channels, group), F32)
        weights[b, :channels] = jnp.concatenate(blocks + [zero], axis=1).astype(BF16)
        weights[b, channels:] = jnp.concatenate([zero] + blocks, axis=1).astype(BF16)


def input_products(refs, halo, g3, weights, tile, out_ref):
    channels, size_x, size_y, size_z = out_ref.shape
    group = 3 * channels
    plane = size_y * size_z
    done = 0
    for pair in range(size_x // 2):
        while done < 2 * pair + 4:
            shifted_plane(done, refs, halo, g3)
            done += 1
        at = slice(2 * pair * group, (2 * pair + 4) * group)
        total = None
        for b in range(3):
            product = jnp.dot(
                weights[b],
                g3[at, b * size_z : b * size_z + plane],
                preferred_element_type=F32,
            )
            total = product if total is None else total + product
        for half in range(2):
            for y in range(size_y):
                tile[half, pl.ds(y, channels, stride=size_y), :] = total[
                    half * channels : (half + 1) * channels, y * size_z : (y + 1) * size_z
                ]
            out_ref[:, 2 * pair + half] = (
                tile[half].reshape(channels, size_y, size_z).astype(BF16)
            )


def g3_scratch(channels, size_x, size_y, size_z):
    return pltpu.VMEM(((size_x + 2) * 3 * channels, (size_y + 2) * size_z), BF16)


def x3_scratch(channels, size_x, size_y, size_z):
    return pltpu.VMEM((size_x, 3 * channels, (size_y + 2) * size_z), BF16)


def acc_scratch(channels):
    return pltpu.VMEM((9 * channels, 3 * channels), F32)


def flat_scratch(channels):
    return pltpu.VMEM((-(-27 * channels // LANES) * LANES, LANES), F32)


def dgrad_scratch(channels, size_x, size_y, size_z):
    return [
        g3_scratch(channels, size_x, size_y, size_z),
        flat_scratch(channels),
        pltpu.VMEM((3, 2 * channels, 12 * channels), BF16),
        pltpu.VMEM((2, channels * size_y, size_z), F32),
    ]


def wgrad_cost(channels, size_x, size_y, size_z):
    return cost(54 * channels * channels * size_x * (size_y + 2) * size_z, 4 * 2**20)


def dgrad_cost(channels, size_x, size_y, size_z):
    return cost(72 * channels * channels * size_x * size_y * size_z, 4 * 2**20)


def row_for_other(body, size_z):
    plane = body.shape[-1]
    low, high = body[:, :size_z].astype(F32), body[:, plane - size_z :].astype(F32)
    return jnp.where(lax.axis_index("gy") == 0, high, low).astype(BF16)


def pair_inner_kernel(rows, *refs):
    first_ref, last_ref, m_ref = refs[3:6]
    g_ref, x_ref, side_ref, columns_ref, sent_ref = refs[6:11]
    tile_ref, tile_sems = refs[16:]
    share = m_ref[...]
    height = tile_ref.shape[0] - share.shape[0]
    if height:
        share = jnp.concatenate([share, jnp.zeros((height, share.shape[1]), F32)], axis=0)
    tile_ref[...] = share.astype(BF16)
    copies = [
        pltpu.make_async_copy(tile_ref, sent_ref.at[device], tile_sems.at[device])
        for device in range(sent_ref.shape[0])
    ]
    for copy in copies:
        copy.start()
    read_inner(rows, *refs[:3], g_ref, x_ref, *refs[11:16])
    size_z = side_ref.shape[-1]
    size_x, channels, plane = x_ref.shape
    size_y = plane // size_z
    bodies = [first_ref] + [g_ref.at[x] for x in range(size_x - 2)] + [last_ref]
    for x, body in enumerate(bodies):
        side_ref[x] = row_for_other(body, size_z)
    low, high = z_tiles([body[...] for body in bodies], size_y, size_z, range(1, size_x + 1))
    side_ref[size_x] = low.astype(BF16)
    side_ref[size_x + 1] = high.astype(BF16)
    low, high = z_tiles([x_ref[x] for x in range(size_x)], size_y, size_z, range(size_x))
    columns_ref[...] = (low + pltpu.roll(high, size_x * size_y, 1)).astype(BF16)
    for copy in copies:
        copy.wait()


def pair_inner(preact, upstream, activations, first, last, share, sent_shape, rows):
    shape = preact.shape
    channels, size_x, _, size_z = shape
    return pl.pallas_call(
        functools.partial(pair_inner_kernel, rows),
        in_specs=[HBM] * 3 + [VMEM] * 3,
        out_specs=[VMEM] * 4 + [HBM],
        out_shape=inner_outputs(*shape)
        + [
            jax.ShapeDtypeStruct((size_x + 2, channels, size_z), BF16),
            jax.ShapeDtypeStruct((channels, LANES), BF16),
            jax.ShapeDtypeStruct(sent_shape, BF16),
        ],
        scratch_shapes=inner_scratch(*shape)
        + [pltpu.VMEM(sent_shape[1:], BF16), pltpu.SemaphoreType.DMA((sent_shape[0],))],
        compiler_params=params(INNER_VMEM),
        cost_estimate=cost(0, 6 * 2**20),
        name="inner",
    )(preact, upstream, activations, first, last, share)


def is_odd(axis):
    return lax.rem(lax.axis_index(axis), 2) == 1


def either(condition, first, second):
    return jnp.where(condition, first.astype(F32), second.astype(F32))


def side_kernel(odd_ref, even_ref, own_ref, sent_ref, xlo_ref, xhi_ref):
    size_x = own_ref.shape[0] - 2
    size_z = own_ref.shape[-1]
    size_y = xlo_ref.shape[-1] // size_z
    odd = is_odd("gx")
    low = either(odd, even_ref[...], odd_ref[...]).astype(BF16)
    high = either(odd, odd_ref[...], even_ref[...]).astype(BF16)
    xlo_ref[...] = low
    xhi_ref[...] = high
    sent_ref[0] = row_for_other(low, size_z)
    for x in range(size_x):
        sent_ref[x + 1] = own_ref[x]
    sent_ref[size_x + 1] = row_for_other(high, size_z)
    tiles = z_tiles([low, high], size_y, size_z, (0, size_x + 1))
    for k in range(2):
        sent_ref[size_x + 2 + k] = (own_ref[size_x + k].astype(F32) + tiles[k]).astype(BF16)


def side(halves, own):
    plane = jax.ShapeDtypeStruct(halves[0].shape, BF16)
    return pl.pallas_call(
        side_kernel,
        in_specs=[VMEM] * 3,
        out_specs=[VMEM] * 3,
        out_shape=[
            jax.ShapeDtypeStruct((own.shape[0] + 2, *own.shape[1:]), BF16),
            plane,
            plane,
        ],
        compiler_params=params(),
        cost_estimate=cost(2**25, 2**19),
        name="side",
    )(*halves, own)


def own_columns(columns, number, area):
    me = lax.axis_index("gy")
    value = columns.astype(F32)
    lane = lax.broadcasted_iota(jnp.int32, value.shape, 1)
    first = pltpu.roll(value, -number * area % LANES, 1)
    second = pltpu.roll(value, (1 - number) * area % LANES, 1)
    first = jnp.where(lane < area, first, 0.0)
    second = jnp.where((lane >= area) & (lane < 2 * area), second, 0.0)
    return jnp.where(me == 0, first, second)


def join_kernel(area, own_ref, other_ref, columns_ref, even_ref, odd_ref):
    at = own_ref.shape[0] - 2
    me = lax.axis_index("gy")
    last = own_columns(columns_ref[...], 1, area).astype(BF16)

    def fill(up_ref, down_ref):
        for k, out_ref in enumerate((down_ref, up_ref)):
            out_ref[me] = own_ref[at + k]
            out_ref[1 - me] = other_ref[at + k]
        up_ref[2] = last
        down_ref[2] = last

    odd = is_odd("gz")

    @pl.when(odd)
    def _():
        fill(odd_ref, even_ref)

    @pl.when(jnp.logical_not(odd))
    def _():
        fill(even_ref, odd_ref)


def join(own, other, columns, area):
    return pl.pallas_call(
        functools.partial(join_kernel, area),
        in_specs=[VMEM] * 3,
        out_specs=[VMEM] * 2,
        out_shape=[jax.ShapeDtypeStruct((3, *own.shape[1:]), BF16)] * 2,
        compiler_params=params(),
        cost_estimate=cost(0, 2**17),
        name="join",
    )(own, other, columns)


def pair_wgrad_kernel(*refs):
    x_ref, acc_ref, g3, x3 = refs[7:]
    weight_products(refs, None, x_ref, g3, x3, acc_ref)


def pair_wgrad(sources, planes_x, shape):
    channels = shape[0]
    return pl.pallas_call(
        pair_wgrad_kernel,
        in_specs=[VMEM] * 8,
        out_specs=VMEM,
        out_shape=jax.ShapeDtypeStruct((9 * channels, 3 * channels), F32),
        scratch_shapes=[g3_scratch(*shape), x3_scratch(*shape)],
        compiler_params=params(32 * 2**20),
        cost_estimate=wgrad_cost(*shape),
        name="wgrad",
    )(*sources, planes_x)


def finish_kernel(scale, rows, sizes, *refs):
    acc_ref, columns_ref, even_ref, odd_ref, from_odd_ref, from_even_ref = refs[:6]
    part_ref, flat, chunks = refs[6:]
    size_x, size_y = sizes
    channels = columns_ref.shape[0]
    area = size_x * size_y
    odd = is_odd("gz")
    lane = lax.broadcasted_iota(jnp.int32, (channels, LANES), 1)
    row = lane % size_y
    jump = area - size_y + 1
    below = [either(odd, from_even_ref[k], from_odd_ref[k]) for k in range(3)]
    own = [either(odd, even_ref[k], odd_ref[k]) for k in range(2)]
    pairs = ((below[:2], own_columns(columns_ref[...], 0, area)), (own, below[2]))
    edges = []
    for tiles, value in pairs:
        before = jnp.where(lane >= area, pltpu.roll(value, jump, 1), 0.0)
        after = jnp.where(lane < area, pltpu.roll(value, LANES - jump, 1), 0.0)
        right = jnp.concatenate(
            [
                jnp.where(row > 0, pltpu.roll(value, 1, 1), before),
                value,
                jnp.where(row < size_y - 1, pltpu.roll(value, LANES - 1, 1), after),
            ],
            axis=0,
        )
        left = []
        for a in range(3):
            first = pltpu.roll(tiles[0], -a * size_y % LANES, 1)
            second = pltpu.roll(tiles[1], (area - a * size_y) % LANES, 1)
            left.append(jnp.where(lane < area, first, jnp.where(lane < 2 * area, second, 0.0)))
        edges.append(
            lax.dot_general(
                jnp.concatenate(left, axis=0).astype(BF16),
                right.astype(BF16),
                (((1,), (1,)), ((), ())),
                preferred_element_type=F32,
            )
        )
    blocks = []
    for a in range(3):
        for c in range(3):
            block = acc_ref[(3 * a + c) * channels : (3 * a + c + 1) * channels, :]
            if c != 1:
                block = block + edges[c // 2][a * channels : (a + 1) * channels]
            blocks.append(block)
    whole = to_flat(jnp.concatenate(blocks, axis=0) * scale, channels, channels, flat)
    count, height, width = part_ref.shape
    line = jnp.concatenate(
        [whole[r * count : (r + 1) * count, : 27 * channels] for r in range(rows)], axis=1
    )
    chunks[...] = jnp.zeros_like(chunks)
    for k in range(line.shape[1] // width):
        chunks[pl.ds(k, count, stride=height), :] = line[:, k * width : (k + 1) * width]
    part_ref[...] = chunks[...].reshape(part_ref.shape).astype(BF16)


def finish(acc, columns, sent, received, scale, rows, sizes, part_shape):
    channels = columns.shape[0]
    return pl.pallas_call(
        functools.partial(finish_kernel, scale, rows, sizes),
        in_specs=[VMEM] * 6,
        out_specs=VMEM,
        out_shape=jax.ShapeDtypeStruct(part_shape, BF16),
        scratch_shapes=[
            flat_scratch(channels),
            pltpu.VMEM((part_shape[0] * part_shape[1], part_shape[2]), F32),
        ],
        compiler_params=params(),
        cost_estimate=cost(2**27, 2**21),
        name="finish",
    )(acc, columns, *sent, *received[::-1])


def adam_step(master, first, second, weight_grad):
    new_first = 0.9 * first + 0.1 * weight_grad
    new_second = 0.999 * second + 0.001 * weight_grad * weight_grad
    corr_first = 1.0 - (0.9**10) ** 10
    corr_second = 1.0 - (0.999**10) ** 10
    update = new_first / corr_first / (jnp.sqrt(new_second / corr_second) + 1e-08) + 0.01 * master
    return master - 0.05 * update, new_first, new_second


def adam_kernel(parts_ref, master_ref, first_ref, second_ref, *out_refs):
    weight_grad = parts_ref[0].astype(F32)
    for source in range(1, parts_ref.shape[0]):
        weight_grad = weight_grad + parts_ref[source].astype(F32)
    weight_grad = weight_grad[: master_ref.shape[0]]
    results = adam_step(master_ref[...], first_ref[...], second_ref[...], weight_grad)
    for out_ref, result in zip(out_refs, (weight_grad, *results)):
        out_ref[...] = result


def adam(parts, *states):
    share = states[0].shape[0]
    tiled = [state.reshape(share // LANES, LANES) for state in states]
    result = jax.ShapeDtypeStruct(tiled[0].shape, F32)
    outs = pl.pallas_call(
        adam_kernel,
        in_specs=[VMEM] * 4,
        out_specs=[VMEM] * 4,
        out_shape=[result] * 4,
        compiler_params=params(),
        cost_estimate=cost(2**18, 2**18),
        name="adam",
    )(parts, *tiled)
    return tuple(out.reshape(share) for out in outs)


def spread_kernel(rows, w_ref, weights_ref, turned, chunks):
    count, height, width = w_ref.shape
    taps = 27 * rows * count
    chunks[...] = w_ref[...].astype(F32).reshape(chunks.shape)
    line = jnp.concatenate(
        [chunks[pl.ds(k, count, stride=height), :] for k in range(rows * taps // width)], axis=1
    )
    whole = jnp.concatenate([line[:, r * taps : (r + 1) * taps] for r in range(rows)], axis=0)
    spread_weights(whole, turned, weights_ref)


def spread(kernel, channels, rows):
    return pl.pallas_call(
        functools.partial(spread_kernel, rows),
        in_specs=[VMEM],
        out_specs=VMEM,
        out_shape=jax.ShapeDtypeStruct((3, 2 * channels, 12 * channels), BF16),
        scratch_shapes=[
            flat_scratch(channels),
            pltpu.VMEM((kernel.shape[0] * kernel.shape[1], kernel.shape[2]), F32),
        ],
        compiler_params=params(),
        cost_estimate=cost(2**20, 2**21),
        name="spread",
    )(kernel)


def pair_dgrad_kernel(*refs):
    weights_ref, out_ref, g3, tile = refs[9:]
    _, size_x, size_y, size_z = out_ref.shape
    halo = pair_z_halo(refs[7], refs[8], size_x + 2, size_y, size_z)
    input_products(refs, halo, g3, weights_ref, tile, out_ref)


def pair_dgrad(sources, weights, shape):
    channels, _, size_y, size_z = shape
    return pl.pallas_call(
        pair_dgrad_kernel,
        in_specs=[VMEM] * 10,
        out_specs=VMEM,
        out_shape=jax.ShapeDtypeStruct(shape, BF16),
        scratch_shapes=[g3_scratch(*shape), pltpu.VMEM((2, channels * size_y, size_z), F32)],
        compiler_params=params(32 * 2**20),
        cost_estimate=dgrad_cost(*shape),
        name="dgrad",
    )(*sources, weights)


def pair_program(activations, preact, upstream, master, first_moment, second_moment, scale):
    shape = activations.shape
    channels, size_x, size_y, _ = shape
    devices = math.prod(lax.axis_size(a) for a in AXES)
    rows = channels // devices
    used = master.shape[0] // LANES
    block = (devices, -(-used // 16) * 16, LANES)
    first, last, *swaps = faces(preact, upstream, "gx", rows)
    odd_halves = swapped(swaps[1], "gx", 1)
    even_halves = swapped(swaps[0], "gx", 0)
    inner, planes_x, own, columns, sent = pair_inner(
        preact, upstream, activations, first, last, master.reshape(used, LANES), block, rows
    )
    kernel = lax.all_to_all(sent, AXES, 0, 0, tiled=True)
    own, xlo, xhi = side((odd_halves, even_halves), own)
    planes = (xlo, first, inner, last, xhi)
    other = shifted(own, {"gy": "swap"})
    z_sent = join(own, other, columns, size_x * size_y)
    from_odd = swapped(z_sent[1], "gz", 1)
    from_even = swapped(z_sent[0], "gz", 0)
    sources = (*planes, other, other)
    acc = pair_wgrad(sources, planes_x, shape)
    z_received = (from_even, from_odd)
    part = finish(acc, columns, z_sent, z_received, scale, rows, (size_x, size_y), block)
    part, kernel = lax.optimization_barrier((part, kernel))
    parts = lax.all_to_all(part, AXES, 0, 0, tiled=True)
    weights = spread(kernel, channels, rows)
    grad_input = pair_dgrad((*sources, *z_received), weights, shape)
    return grad_input, *adam(parts, master, first_moment, second_moment)


def yface_kernel(*refs):
    low_ref, high_ref = refs[5:]
    size_z = low_ref.shape[-1]
    for index in range(low_ref.shape[0]):
        body = body_of(refs[:5], index)
        plane = body.shape[-1]
        low_ref[index] = body[:, :size_z]
        high_ref[index] = body[:, plane - size_z :]


def y_faces(planes, size_z):
    inner, channels, _ = planes[2].shape
    face = jax.ShapeDtypeStruct((inner + 4, channels, size_z), BF16)
    return pl.pallas_call(
        yface_kernel,
        in_specs=[VMEM] * 5,
        out_specs=[VMEM] * 2,
        out_shape=[face] * 2,
        compiler_params=params(),
        cost_estimate=cost(0, 2**19),
        name="yfaces",
    )(*planes)


def zface_kernel(*refs):
    zlo_ref, zhi_ref = refs[7:]
    size_z = refs[5].shape[-1]
    whole = []
    for index in range(refs[5].shape[0]):
        low, high = y_halo(refs[5:7], index)
        body = body_of(refs[:5], index)[...]
        whole.append(jnp.concatenate([low.astype(BF16), body, high.astype(BF16)], axis=1))
    low, high = z_tiles(whole, whole[0].shape[1] // size_z, size_z, range(len(whole)))
    zlo_ref[...] = low.astype(BF16)
    zhi_ref[...] = high.astype(BF16)


def z_faces(planes, y_halos):
    face = jax.ShapeDtypeStruct((planes[0].shape[0], LANES), BF16)
    return pl.pallas_call(
        zface_kernel,
        in_specs=[VMEM] * 7,
        out_specs=[VMEM] * 2,
        out_shape=[face, face],
        compiler_params=params(),
        cost_estimate=cost(2**27, 2**21),
        name="zfaces",
    )(*planes, *y_halos)


def wgrad_kernel(scale, *refs):
    x_ref, part_ref, g3, x3, acc, flat = refs[9:]
    size_x, channels, plane = x_ref.shape
    size_z = refs[5].shape[-1]
    halo = z_halo(refs[7], refs[8], size_x + 2, plane // size_z + 2, size_z)
    weight_products(refs, halo, x_ref, g3, x3, acc)
    whole = to_flat(acc[...] * scale, channels, channels, flat)
    part_ref[...] = whole[:, : part_ref.shape[1]].astype(BF16)


def wgrad(sources, planes_x, shape, scale):
    channels = shape[0]
    return pl.pallas_call(
        functools.partial(wgrad_kernel, scale),
        in_specs=[VMEM] * 10,
        out_specs=VMEM,
        out_shape=jax.ShapeDtypeStruct((channels, 27 * channels), BF16),
        scratch_shapes=[
            g3_scratch(*shape),
            x3_scratch(*shape),
            acc_scratch(channels),
            flat_scratch(channels),
        ],
        compiler_params=params(32 * 2**20),
        cost_estimate=wgrad_cost(*shape),
        name="wgrad",
    )(*sources, planes_x)


def dgrad_kernel(*refs):
    w_ref, out_ref, g3, turned, weights, tile = refs[9:]
    _, size_x, size_y, size_z = out_ref.shape
    spread_weights(w_ref[...].astype(F32), turned, weights)
    halo = z_halo(refs[7], refs[8], size_x + 2, size_y + 2, size_z)
    input_products(refs, halo, g3, weights, tile, out_ref)


def dgrad(sources, kernel, shape):
    return pl.pallas_call(
        dgrad_kernel,
        in_specs=[VMEM] * 10,
        out_specs=VMEM,
        out_shape=jax.ShapeDtypeStruct(shape, BF16),
        scratch_shapes=dgrad_scratch(*shape),
        compiler_params=params(32 * 2**20),
        cost_estimate=dgrad_cost(*shape),
        name="dgrad",
    )(*sources, kernel)


def general_program(activations, preact, upstream, master, first_moment, second_moment, scale):
    shape = activations.shape
    channels, _, _, size_z = shape
    devices = math.prod(lax.axis_size(a) for a in AXES)
    share = master.shape[0]
    first, last = faces(preact, upstream)
    x_halos = (shifted(last, {"gx": 1}), shifted(first, {"gx": -1}))
    inner, planes_x = inner_planes(preact, upstream, activations)
    sent = jnp.broadcast_to(master.astype(BF16).reshape(1, 1, share), (devices, 1, share))
    kernel = lax.all_to_all(sent, AXES, 0, 0, tiled=True).reshape(channels, 27 * channels)
    planes = (x_halos[0], first, inner, last, x_halos[1])
    y_sent = y_faces(planes, size_z)
    y_halos = (shifted(y_sent[1], {"gy": 1}), shifted(y_sent[0], {"gy": -1}))
    zlo, zhi = z_faces(planes, y_halos)
    z_halos = (shifted(zhi, {"gz": 1}), shifted(zlo, {"gz": -1}))
    sources = (*planes, *y_halos, *z_halos)
    part = wgrad(sources, planes_x, shape, scale)
    part, kernel = lax.optimization_barrier((part, kernel))
    parts = lax.all_to_all(part.reshape(devices, 1, share), AXES, 0, 0, tiled=True)
    grad_input = dgrad(sources, kernel, shape)
    weight_grad = jnp.sum(parts.astype(F32), axis=0).reshape(-1)
    results = adam_step(master, first_moment, second_moment, weight_grad)
    return grad_input, weight_grad, *results


def shifted(value, moves):
    names = tuple(moves)
    sizes = [lax.axis_size(name) for name in names]
    pairs = []
    for source in range(math.prod(sizes)):
        rest, coords = source, []
        for size in reversed(sizes):
            coords.insert(0, rest % size)
            rest //= size
        coords = [
            (at + moves[name]) if moves[name] != "swap" else 1 - at
            for at, name in zip(coords, names)
        ]
        if all(0 <= at < size for at, size in zip(coords, sizes)):
            target = 0
            for at, size in zip(coords, sizes):
                target = target * size + at
            pairs.append((source, target))
    return lax.ppermute(value, names if len(names) > 1 else names[0], pairs)


def swapped(value, axis, start):
    pairs = []
    for low in range(start, lax.axis_size(axis) - 1, 2):
        pairs += [(low, low + 1), (low + 1, low)]
    return lax.ppermute(value, axis, pairs)


def local(activations, preact, upstream, master, first_moment, second_moment):
    channels, size_x, size_y, size_z = activations.shape
    devices = math.prod(lax.axis_size(a) for a in AXES)
    share = master.shape[0]
    scale = 1.0 / math.sqrt(size_x * size_y * size_z * devices)
    in_pairs = (
        lax.axis_size("gy") == 2
        and channels % devices == 0
        and share % LANES == 0
        and channels // (channels // devices) % 16 == 0
        and 2 * size_x * size_y <= LANES
        and (size_x + 2) * size_y <= LANES
    )
    program = pair_program if in_pairs else general_program
    return program(
        activations, preact, upstream, master, first_moment, second_moment, scale
    )


def solution(mesh):
    volume = P(None, "gx", "gy", "gz")
    flat = P(AXES)
    return jax.shard_map(
        local,
        mesh=mesh,
        in_specs=(volume, volume, volume, flat, flat, flat),
        out_specs=(volume, flat, flat, flat, flat),
        check_vma=False,
    )
```

```python
import functools
import math

import jax
import jax.numpy as jnp
from jax import lax
from jax.experimental import pallas as pl
from jax.experimental.pallas import tpu as pltpu
from jax.sharding import PartitionSpec as P

AXES = ("gx", "gy", "gz")
LANES = 128
VMEM = pl.BlockSpec(memory_space=pltpu.VMEM)
HBM = pl.BlockSpec(memory_space=pltpu.HBM)
F32 = jnp.float32
BF16 = jnp.bfloat16
FACES_VMEM = 55_900_000
INNER_VMEM = 54_800_000


def params(limit=24 * 2**20):
    return pltpu.CompilerParams(vmem_limit_bytes=limit)


def cost(flops, moved):
    return pl.CostEstimate(flops=flops, bytes_accessed=moved, transcendentals=0)


def to_planes(value, tile, write, rows=1):
    channels, size_y, size_z = value.shape
    count = channels // rows
    tile[...] = value.astype(F32).reshape(channels * size_y, size_z)
    for y in range(size_y):
        for r in range(rows):
            picked = tile[pl.ds(r * size_y + y, count, stride=rows * size_y), :]
            write(slice(r * count, (r + 1) * count), y, picked.astype(BF16))


def masked(p, u):
    return jnp.where(p > 0, u, jnp.zeros_like(u))


def face_kernel(axis, rows, p_ref, u_ref, *refs):
    p_buf, u_buf, tile, sems = refs[-4:]
    out_refs, swap_refs = refs[:2], refs[2:-4]
    size_x, size_z = p_ref.shape[1], p_ref.shape[3]
    copies = []
    for k, x in enumerate((0, size_x - 1)):
        pair = (
            pltpu.make_async_copy(p_ref.at[:, x], p_buf.at[k], sems.at[2 * k]),
            pltpu.make_async_copy(u_ref.at[:, x], u_buf.at[k], sems.at[2 * k + 1]),
        )
        for copy in pair:
            copy.start()
        copies.append(pair)
    for k, out_ref in enumerate(out_refs):
        for copy in copies[k]:
            copy.wait()

        def write(at, y, value):
            out_ref[at, y * size_z : (y + 1) * size_z] = value

        to_planes(masked(p_buf[k], u_buf[k]), tile.at[k], write, rows)
    if axis is not None:
        odd = is_odd(axis)

        @pl.when(odd)
        def _():
            for swap_ref, out_ref in zip(swap_refs, out_refs):
                swap_ref[...] = out_ref[...]

        @pl.when(jnp.logical_not(odd))
        def _():
            for swap_ref, out_ref in zip(swap_refs, out_refs[::-1]):
                swap_ref[...] = out_ref[...]


def faces(preact, upstream, axis=None, rows=1):
    channels, size_x, size_y, size_z = preact.shape
    face = jax.ShapeDtypeStruct((channels, size_y * size_z), BF16)
    buffer = pltpu.VMEM((2, channels, size_y, size_z), BF16)
    count = 2 if axis is None else 4
    return pl.pallas_call(
        functools.partial(face_kernel, axis, rows),
        in_specs=[HBM, HBM],
        out_specs=[VMEM] * count,
        out_shape=[face] * count,
        scratch_shapes=[
            buffer,
            buffer,
            pltpu.VMEM((2, channels * size_y, size_z), F32),
            pltpu.SemaphoreType.DMA((4,)),
        ],
        compiler_params=params(FACES_VMEM),
        cost_estimate=cost(0, 2**20),
        name="faces",
    )(preact, upstream)


def read_inner(rows, p_ref, u_ref, g_ref, p_buf, u_buf, tile, sems):
    size_x, size_z = p_ref.shape[1], p_ref.shape[3]
    inner = size_x - 2
    copies = []
    for x in range(inner):
        pair = (
            pltpu.make_async_copy(p_ref.at[:, x + 1], p_buf.at[x], sems.at[x]),
            pltpu.make_async_copy(u_ref.at[:, x + 1], u_buf.at[x], sems.at[inner + x]),
        )
        for copy in pair:
            copy.start()
        copies.append(pair)
    for x in range(inner):
        for copy in copies[x]:
            copy.wait()

        def write(at, y, value):
            g_ref[x, at, y * size_z : (y + 1) * size_z] = value

        to_planes(masked(p_buf[x], u_buf[x]), tile.at[x % 2], write, rows)


def inner_kernel(*refs):
    read_inner(1, *refs)


def inner_output(channels, size_x, size_y, size_z):
    return jax.ShapeDtypeStruct((size_x - 2, channels, size_y * size_z), BF16)


def inner_scratch(channels, size_x, size_y, size_z):
    return [
        pltpu.VMEM((size_x - 2, channels, size_y, size_z), BF16),
        pltpu.VMEM((size_x - 2, channels, size_y, size_z), BF16),
        pltpu.VMEM((2, channels * size_y, size_z), F32),
        pltpu.SemaphoreType.DMA((2 * size_x - 4,)),
    ]


def inner_planes(preact, upstream):
    shape = preact.shape
    return pl.pallas_call(
        inner_kernel,
        in_specs=[HBM] * 2,
        out_specs=VMEM,
        out_shape=inner_output(*shape),
        scratch_shapes=inner_scratch(*shape),
        compiler_params=params(INNER_VMEM),
        cost_estimate=cost(0, 4 * 2**20),
        name="inner",
    )(preact, upstream)


def input_kernel(a_ref, x_ref, *refs):
    tile = refs[-1]
    channels, size_x, size_y, size_z = a_ref.shape
    for x in range(size_x):

        def write(at, y, value):
            x_ref[x, at, y * size_z : (y + 1) * size_z] = value

        to_planes(a_ref[:, x], tile.at[x % 2], write)
    if len(refs) > 1:
        low, high = z_tiles([x_ref[x] for x in range(size_x)], size_y, size_z, range(size_x))
        refs[0][...] = (low + pltpu.roll(high, size_x * size_y, 1)).astype(BF16)


def input_planes(activations, with_columns):
    channels, size_x, size_y, size_z = activations.shape
    outs = [jax.ShapeDtypeStruct((size_x, channels, size_y * size_z), BF16)]
    if with_columns:
        outs.append(jax.ShapeDtypeStruct((channels, LANES), BF16))
    return pl.pallas_call(
        input_kernel,
        in_specs=[VMEM],
        out_specs=[VMEM] * len(outs),
        out_shape=outs,
        scratch_shapes=[pltpu.VMEM((2, channels * size_y, size_z), F32)],
        compiler_params=params(),
        cost_estimate=cost(0, 2 * 2**20),
        name="inputs",
    )(activations)


def body_of(refs, index):
    planes = refs[2].shape[0] + 4
    if 2 <= index < planes - 2:
        return refs[2].at[index - 2]
    return refs[{0: 0, 1: 1, planes - 2: 3, planes - 1: 4}[index]]


def y_halo(refs, index):
    me = lax.axis_index("gy")
    low = jnp.where(me > 0, refs[0][index].astype(F32), 0.0)
    high = jnp.where(me < lax.axis_size("gy") - 1, refs[1][index].astype(F32), 0.0)
    return low, high


def z_picker(rows_y, size_z):
    shape = (rows_y * size_z, 2 * LANES)
    voxel = lax.broadcasted_iota(jnp.int32, shape, 0)
    lane = lax.broadcasted_iota(jnp.int32, shape, 1)
    wanted = jnp.where(lane < LANES, lane * size_z, (lane - LANES) * size_z + size_z - 1)
    return (voxel == wanted).astype(F32).astype(BF16)


def z_tiles(planes, rows_y, size_z, numbers):
    channels = planes[0].shape[0]
    columns = jnp.dot(
        jnp.concatenate(planes, axis=0), z_picker(rows_y, size_z), preferred_element_type=F32
    )
    low = jnp.zeros((channels, LANES), F32)
    high = jnp.zeros((channels, LANES), F32)
    for index, number in enumerate(numbers):
        rows = columns[index * channels : (index + 1) * channels]
        low = low + pltpu.roll(rows[:, :LANES], number * rows_y, 1)
        high = high + pltpu.roll(rows[:, LANES:], number * rows_y, 1)
    return low, high


def put_columns(columns, row_of, rows_y, size_z):
    shape = (2 * LANES, rows_y * size_z)
    source = lax.broadcasted_iota(jnp.int32, shape, 0)
    voxel = lax.broadcasted_iota(jnp.int32, shape, 1)
    number = source % LANES
    place = row_of(number) * size_z + jnp.where(source < LANES, 0, size_z - 1)
    place = jnp.where(number < rows_y, place, -1)
    put = (voxel == place).astype(F32).astype(BF16)
    rows = [jnp.concatenate(pair, axis=1) for pair in columns]
    return jnp.dot(
        jnp.concatenate(rows, axis=0).astype(BF16), put, preferred_element_type=F32
    ).astype(BF16)


def z_halo(low_ref, high_ref, planes, rows_y, size_z):
    columns = []
    for index in range(planes):
        shift = -index * rows_y % LANES
        columns.append(
            [pltpu.roll(ref[...].astype(F32), shift, 1) for ref in (low_ref, high_ref)]
        )
    return put_columns(columns, lambda number: number, rows_y, size_z)


def pair_z_halo(odd_ref, even_ref, planes, size_y, size_z):
    me, odd = lax.axis_index("gy"), is_odd("gz")
    sides = []
    for low, high in ((even_ref, odd_ref), (odd_ref, even_ref)):
        first, second = (either(odd, low[k], high[k]) for k in range(2))
        lane = lax.broadcasted_iota(jnp.int32, first.shape, 1)
        own = jnp.where(me == 0, first, second)
        before = jnp.where(me == 0, 0.0, first)
        after = jnp.where(me == 0, second, 0.0)
        columns = []
        for index in range(planes):
            start = index * size_y
            columns.append(
                jnp.where(
                    lane < size_y,
                    pltpu.roll(own, -start % LANES, 1),
                    jnp.where(
                        lane == size_y,
                        pltpu.roll(before, (1 - start) % LANES, 1),
                        pltpu.roll(after, (size_y + 1 - start) % LANES, 1),
                    ),
                )
            )
        sides.append(columns)

    def row_of(number):
        return jnp.where(number < size_y, number + 1, jnp.where(number == size_y, 0, size_y + 1))

    return put_columns(list(zip(*sides)), row_of, size_y + 2, size_z)


def shifted_plane(index, refs, halo, g3):
    channels, plane = refs[0].shape
    size_z = refs[5].shape[-1]
    rows_y = plane // size_z + 2
    base = 3 * channels * index
    lane = lax.broadcasted_iota(jnp.int32, (channels, size_z), 1)
    is_first, is_last = lane == 0, lane == size_z - 1
    low, high = y_halo(refs[5:7], index)
    body = body_of(refs[:5], index)
    for row in range(rows_y):
        cols = slice(row * size_z, (row + 1) * size_z)
        if row == 0:
            value = low.astype(BF16)
        elif row == rows_y - 1:
            value = high.astype(BF16)
        else:
            value = body[:, (row - 1) * size_z : row * size_z]
        if halo is None:
            edge = jnp.zeros_like(value)
        else:
            edge = halo[index * channels : (index + 1) * channels, cols]
        before = jnp.where(is_first, edge, pltpu.roll(value, 1, 1))
        after = jnp.where(is_last, edge, pltpu.roll(value, size_z - 1, 1))
        g3[base : base + channels, cols] = before
        g3[base + channels : base + 2 * channels, cols] = value
        g3[base + 2 * channels : base + 3 * channels, cols] = after


def weight_products(refs, halo, x_ref, g3, x3, acc):
    size_x, channels, plane = x_ref.shape
    size_z = refs[5].shape[-1]
    group = 3 * channels
    zero = jnp.zeros((channels, 2 * size_z), BF16)
    done = 0
    for x in range(size_x):
        while done < x + 3:
            shifted_plane(done, refs, halo, g3)
            done += 1
        value = x_ref[x]
        for b in range(3):
            at = slice(b * channels, (b + 1) * channels)
            start = (2 - b) * size_z
            x3[x, at, start : start + plane] = value
            if start:
                x3[x, at, :start] = zero[:, :start]
            if start < 2 * size_z:
                x3[x, at, start + plane :] = zero[:, start:]
        product = lax.dot_general(
            g3[x * group : (x + 3) * group, :],
            x3[x],
            (((1,), (1,)), ((), ())),
            preferred_element_type=F32,
        )
        if x == 0:
            acc[...] = product
        else:
            acc[...] += product


def to_flat(value, count, channels, flat):
    height, width = value.shape
    wide = value
    if height % LANES:
        wide = jnp.concatenate([wide, jnp.zeros((-height % LANES, width), F32)], axis=0)
    if width % LANES:
        wide = jnp.concatenate([wide, jnp.zeros((wide.shape[0], -width % LANES), F32)], axis=1)
    turned = wide.T
    for b in range(3):
        rows = turned[b * channels : (b + 1) * channels]
        for block in range(9):
            start = block * count
            cell = rows[:, start // LANES * LANES : (start // LANES + 1) * LANES]
            tap = (2 - block // 3) * 9 + b * 3 + 2 - block % 3
            shift = -start % LANES
            flat[pl.ds(tap, channels, stride=27), :] = pltpu.roll(cell, shift, 1) if shift else cell
    return flat[...].T[:count]


def spread_weights(whole, turned, weights):
    channels, taps = whole.shape
    group = 3 * channels
    whole = jnp.concatenate([whole, jnp.zeros((LANES - channels, taps), F32)], axis=0)
    whole = jnp.concatenate([whole, jnp.zeros((LANES, -taps % LANES), F32)], axis=1)
    turned[...] = whole.T
    for b in range(3):
        blocks = []
        for a in range(3):
            for c in range(3):
                tap = (2 - a) * 9 + (2 - b) * 3 + 2 - c
                blocks.append(turned[pl.ds(tap, channels, stride=27), :][:, :channels])
        zero = jnp.zeros((channels, group), F32)
        weights[b, :channels] = jnp.concatenate(blocks + [zero], axis=1).astype(BF16)
        weights[b, channels:] = jnp.concatenate([zero] + blocks, axis=1).astype(BF16)


def input_products(refs, halo, g3, weights, tile, out_ref):
    channels, size_x, size_y, size_z = out_ref.shape
    group = 3 * channels
    plane = size_y * size_z
    done = 0
    for pair in range(size_x // 2):
        while done < 2 * pair + 4:
            shifted_plane(done, refs, halo, g3)
            done += 1
        at = slice(2 * pair * group, (2 * pair + 4) * group)
        total = None
        for b in range(3):
            product = jnp.dot(
                weights[b],
                g3[at, b * size_z : b * size_z + plane],
                preferred_element_type=F32,
            )
            total = product if total is None else total + product
        for half in range(2):
            for y in range(size_y):
                tile[half, pl.ds(y, channels, stride=size_y), :] = total[
                    half * channels : (half + 1) * channels, y * size_z : (y + 1) * size_z
                ]
            out_ref[:, 2 * pair + half] = (
                tile[half].reshape(channels, size_y, size_z).astype(BF16)
            )


def g3_scratch(channels, size_x, size_y, size_z):
    return pltpu.VMEM(((size_x + 2) * 3 * channels, (size_y + 2) * size_z), BF16)


def x3_scratch(channels, size_x, size_y, size_z):
    return pltpu.VMEM((size_x, 3 * channels, (size_y + 2) * size_z), BF16)


def acc_scratch(channels):
    return pltpu.VMEM((9 * channels, 3 * channels), F32)


def flat_scratch(channels):
    return pltpu.VMEM((-(-27 * channels // LANES) * LANES, LANES), F32)


def dgrad_scratch(channels, size_x, size_y, size_z):
    return [
        g3_scratch(channels, size_x, size_y, size_z),
        flat_scratch(channels),
        pltpu.VMEM((3, 2 * channels, 12 * channels), BF16),
        pltpu.VMEM((2, channels * size_y, size_z), F32),
    ]


def wgrad_cost(channels, size_x, size_y, size_z):
    return cost(54 * channels * channels * size_x * (size_y + 2) * size_z, 4 * 2**20)


def dgrad_cost(channels, size_x, size_y, size_z):
    return cost(72 * channels * channels * size_x * size_y * size_z, 4 * 2**20)


def row_for_other(body, size_z):
    plane = body.shape[-1]
    low, high = body[:, :size_z].astype(F32), body[:, plane - size_z :].astype(F32)
    return jnp.where(lax.axis_index("gy") == 0, high, low).astype(BF16)


def pair_inner_kernel(rows, *refs):
    first_ref, last_ref, m_ref, g_ref, side_ref, sent_ref = refs[2:8]
    tile_ref, tile_sems = refs[12:]
    share = m_ref[...]
    height = tile_ref.shape[0] - share.shape[0]
    if height:
        share = jnp.concatenate([share, jnp.zeros((height, share.shape[1]), F32)], axis=0)
    tile_ref[...] = share.astype(BF16)
    copies = [
        pltpu.make_async_copy(tile_ref, sent_ref.at[device], tile_sems.at[device])
        for device in range(sent_ref.shape[0])
    ]
    for copy in copies:
        copy.start()
    read_inner(rows, *refs[:2], g_ref, *refs[8:12])
    size_z = side_ref.shape[-1]
    inner, _, plane = g_ref.shape
    size_x = inner + 2
    bodies = [first_ref] + [g_ref.at[x] for x in range(inner)] + [last_ref]
    for x, body in enumerate(bodies):
        side_ref[x] = row_for_other(body, size_z)
    low, high = z_tiles(
        [body[...] for body in bodies], plane // size_z, size_z, range(1, size_x + 1)
    )
    side_ref[size_x] = low.astype(BF16)
    side_ref[size_x + 1] = high.astype(BF16)
    for copy in copies:
        copy.wait()


def pair_inner(preact, upstream, first, last, share, sent_shape, rows):
    shape = preact.shape
    channels, size_x, _, size_z = shape
    return pl.pallas_call(
        functools.partial(pair_inner_kernel, rows),
        in_specs=[HBM] * 2 + [VMEM] * 3,
        out_specs=[VMEM] * 2 + [HBM],
        out_shape=[
            inner_output(*shape),
            jax.ShapeDtypeStruct((size_x + 2, channels, size_z), BF16),
            jax.ShapeDtypeStruct(sent_shape, BF16),
        ],
        scratch_shapes=inner_scratch(*shape)
        + [pltpu.VMEM(sent_shape[1:], BF16), pltpu.SemaphoreType.DMA((sent_shape[0],))],
        compiler_params=params(INNER_VMEM),
        cost_estimate=cost(0, 4 * 2**20),
        name="inner",
    )(preact, upstream, first, last, share)


def is_odd(axis):
    return lax.rem(lax.axis_index(axis), 2) == 1


def either(condition, first, second):
    return jnp.where(condition, first.astype(F32), second.astype(F32))


def side_kernel(odd_ref, even_ref, own_ref, sent_ref, xlo_ref, xhi_ref):
    size_x = own_ref.shape[0] - 2
    size_z = own_ref.shape[-1]
    size_y = xlo_ref.shape[-1] // size_z
    odd = is_odd("gx")
    low = either(odd, even_ref[...], odd_ref[...]).astype(BF16)
    high = either(odd, odd_ref[...], even_ref[...]).astype(BF16)
    xlo_ref[...] = low
    xhi_ref[...] = high
    sent_ref[0] = row_for_other(low, size_z)
    for x in range(size_x):
        sent_ref[x + 1] = own_ref[x]
    sent_ref[size_x + 1] = row_for_other(high, size_z)
    tiles = z_tiles([low, high], size_y, size_z, (0, size_x + 1))
    for k in range(2):
        sent_ref[size_x + 2 + k] = (own_ref[size_x + k].astype(F32) + tiles[k]).astype(BF16)


def side(halves, own):
    plane = jax.ShapeDtypeStruct(halves[0].shape, BF16)
    return pl.pallas_call(
        side_kernel,
        in_specs=[VMEM] * 3,
        out_specs=[VMEM] * 3,
        out_shape=[
            jax.ShapeDtypeStruct((own.shape[0] + 2, *own.shape[1:]), BF16),
            plane,
            plane,
        ],
        compiler_params=params(),
        cost_estimate=cost(2**25, 2**19),
        name="side",
    )(*halves, own)


def own_columns(columns, number, area):
    me = lax.axis_index("gy")
    value = columns.astype(F32)
    lane = lax.broadcasted_iota(jnp.int32, value.shape, 1)
    first = pltpu.roll(value, -number * area % LANES, 1)
    second = pltpu.roll(value, (1 - number) * area % LANES, 1)
    first = jnp.where(lane < area, first, 0.0)
    second = jnp.where((lane >= area) & (lane < 2 * area), second, 0.0)
    return jnp.where(me == 0, first, second)


def join_kernel(area, own_ref, other_ref, columns_ref, even_ref, odd_ref):
    at = own_ref.shape[0] - 2
    me = lax.axis_index("gy")
    last = own_columns(columns_ref[...], 1, area).astype(BF16)

    def fill(up_ref, down_ref):
        for k, out_ref in enumerate((down_ref, up_ref)):
            out_ref[me] = own_ref[at + k]
            out_ref[1 - me] = other_ref[at + k]
        up_ref[2] = last
        down_ref[2] = last

    odd = is_odd("gz")

    @pl.when(odd)
    def _():
        fill(odd_ref, even_ref)

    @pl.when(jnp.logical_not(odd))
    def _():
        fill(even_ref, odd_ref)


def join(own, other, columns, area):
    return pl.pallas_call(
        functools.partial(join_kernel, area),
        in_specs=[VMEM] * 3,
        out_specs=[VMEM] * 2,
        out_shape=[jax.ShapeDtypeStruct((3, *own.shape[1:]), BF16)] * 2,
        compiler_params=params(),
        cost_estimate=cost(0, 2**17),
        name="join",
    )(own, other, columns)


def pair_wgrad_kernel(*refs):
    x_ref, acc_ref, g3, x3 = refs[7:]
    weight_products(refs, None, x_ref, g3, x3, acc_ref)


def pair_wgrad(sources, planes_x, shape):
    channels = shape[0]
    return pl.pallas_call(
        pair_wgrad_kernel,
        in_specs=[VMEM] * 8,
        out_specs=VMEM,
        out_shape=jax.ShapeDtypeStruct((9 * channels, 3 * channels), F32),
        scratch_shapes=[g3_scratch(*shape), x3_scratch(*shape)],
        compiler_params=params(32 * 2**20),
        cost_estimate=wgrad_cost(*shape),
        name="wgrad",
    )(*sources, planes_x)


def finish_kernel(scale, rows, sizes, *refs):
    acc_ref, columns_ref, even_ref, odd_ref, from_odd_ref, from_even_ref = refs[:6]
    part_ref, flat, chunks = refs[6:]
    size_x, size_y = sizes
    channels = columns_ref.shape[0]
    area = size_x * size_y
    odd = is_odd("gz")
    lane = lax.broadcasted_iota(jnp.int32, (channels, LANES), 1)
    row = lane % size_y
    jump = area - size_y + 1
    below = [either(odd, from_even_ref[k], from_odd_ref[k]) for k in range(3)]
    own = [either(odd, even_ref[k], odd_ref[k]) for k in range(2)]
    pairs = ((below[:2], own_columns(columns_ref[...], 0, area)), (own, below[2]))
    edges = []
    for tiles, value in pairs:
        before = jnp.where(lane >= area, pltpu.roll(value, jump, 1), 0.0)
        after = jnp.where(lane < area, pltpu.roll(value, LANES - jump, 1), 0.0)
        right = jnp.concatenate(
            [
                jnp.where(row > 0, pltpu.roll(value, 1, 1), before),
                value,
                jnp.where(row < size_y - 1, pltpu.roll(value, LANES - 1, 1), after),
            ],
            axis=0,
        )
        left = []
        for a in range(3):
            first = pltpu.roll(tiles[0], -a * size_y % LANES, 1)
            second = pltpu.roll(tiles[1], (area - a * size_y) % LANES, 1)
            left.append(jnp.where(lane < area, first, jnp.where(lane < 2 * area, second, 0.0)))
        edges.append(
            lax.dot_general(
                jnp.concatenate(left, axis=0).astype(BF16),
                right.astype(BF16),
                (((1,), (1,)), ((), ())),
                preferred_element_type=F32,
            )
        )
    blocks = []
    for a in range(3):
        for c in range(3):
            block = acc_ref[(3 * a + c) * channels : (3 * a + c + 1) * channels, :]
            if c != 1:
                block = block + edges[c // 2][a * channels : (a + 1) * channels]
            blocks.append(block)
    whole = to_flat(jnp.concatenate(blocks, axis=0) * scale, channels, channels, flat)
    count, height, width = part_ref.shape
    line = jnp.concatenate(
        [whole[r * count : (r + 1) * count, : 27 * channels] for r in range(rows)], axis=1
    )
    chunks[...] = jnp.zeros_like(chunks)
    for k in range(line.shape[1] // width):
        chunks[pl.ds(k, count, stride=height), :] = line[:, k * width : (k + 1) * width]
    part_ref[...] = chunks[...].reshape(part_ref.shape).astype(BF16)


def finish(acc, columns, sent, received, scale, rows, sizes, part_shape):
    channels = columns.shape[0]
    return pl.pallas_call(
        functools.partial(finish_kernel, scale, rows, sizes),
        in_specs=[VMEM] * 6,
        out_specs=VMEM,
        out_shape=jax.ShapeDtypeStruct(part_shape, BF16),
        scratch_shapes=[
            flat_scratch(channels),
            pltpu.VMEM((part_shape[0] * part_shape[1], part_shape[2]), F32),
        ],
        compiler_params=params(),
        cost_estimate=cost(2**27, 2**21),
        name="finish",
    )(acc, columns, *sent, *received)


def adam_step(master, first, second, weight_grad):
    new_first = 0.9 * first + 0.1 * weight_grad
    new_second = 0.999 * second + 0.001 * weight_grad * weight_grad
    corr_first = 1.0 - (0.9**10) ** 10
    corr_second = 1.0 - (0.999**10) ** 10
    update = new_first / corr_first / (jnp.sqrt(new_second / corr_second) + 1e-08) + 0.01 * master
    return master - 0.05 * update, new_first, new_second


def adam_kernel(parts_ref, master_ref, first_ref, second_ref, *out_refs):
    weight_grad = parts_ref[0].astype(F32)
    for source in range(1, parts_ref.shape[0]):
        weight_grad = weight_grad + parts_ref[source].astype(F32)
    weight_grad = weight_grad[: master_ref.shape[0]]
    results = adam_step(master_ref[...], first_ref[...], second_ref[...], weight_grad)
    for out_ref, result in zip(out_refs, (weight_grad, *results)):
        out_ref[...] = result


def adam(parts, *states):
    share = states[0].shape[0]
    tiled = [state.reshape(share // LANES, LANES) for state in states]
    result = jax.ShapeDtypeStruct(tiled[0].shape, F32)
    outs = pl.pallas_call(
        adam_kernel,
        in_specs=[VMEM] * 4,
        out_specs=[VMEM] * 4,
        out_shape=[result] * 4,
        compiler_params=params(),
        cost_estimate=cost(2**18, 2**18),
        name="adam",
    )(parts, *tiled)
    return tuple(out.reshape(share) for out in outs)


def spread_kernel(rows, w_ref, weights_ref, turned, chunks):
    count, height, width = w_ref.shape
    taps = 27 * rows * count
    chunks[...] = w_ref[...].astype(F32).reshape(chunks.shape)
    line = jnp.concatenate(
        [chunks[pl.ds(k, count, stride=height), :] for k in range(rows * taps // width)], axis=1
    )
    whole = jnp.concatenate([line[:, r * taps : (r + 1) * taps] for r in range(rows)], axis=0)
    spread_weights(whole, turned, weights_ref)


def spread(kernel, channels, rows):
    return pl.pallas_call(
        functools.partial(spread_kernel, rows),
        in_specs=[VMEM],
        out_specs=VMEM,
        out_shape=jax.ShapeDtypeStruct((3, 2 * channels, 12 * channels), BF16),
        scratch_shapes=[
            flat_scratch(channels),
            pltpu.VMEM((kernel.shape[0] * kernel.shape[1], kernel.shape[2]), F32),
        ],
        compiler_params=params(),
        cost_estimate=cost(2**20, 2**21),
        name="spread",
    )(kernel)


def pair_dgrad_kernel(*refs):
    weights_ref, out_ref, g3, tile = refs[9:]
    _, size_x, size_y, size_z = out_ref.shape
    halo = pair_z_halo(refs[7], refs[8], size_x + 2, size_y, size_z)
    input_products(refs, halo, g3, weights_ref, tile, out_ref)


def pair_dgrad(sources, weights, shape):
    channels, _, size_y, size_z = shape
    return pl.pallas_call(
        pair_dgrad_kernel,
        in_specs=[VMEM] * 10,
        out_specs=VMEM,
        out_shape=jax.ShapeDtypeStruct(shape, BF16),
        scratch_shapes=[g3_scratch(*shape), pltpu.VMEM((2, channels * size_y, size_z), F32)],
        compiler_params=params(32 * 2**20),
        cost_estimate=dgrad_cost(*shape),
        name="dgrad",
    )(*sources, weights)


def pair_program(activations, preact, upstream, master, first_moment, second_moment, scale):
    shape = activations.shape
    channels, size_x, size_y, _ = shape
    devices = math.prod(lax.axis_size(a) for a in AXES)
    rows = channels // devices
    used = master.shape[0] // LANES
    block = (devices, -(-used // 16) * 16, LANES)
    first, last, *swaps = faces(preact, upstream, "gx", rows)
    odd_halves = swapped(swaps[1], "gx", 1)
    even_halves = swapped(swaps[0], "gx", 0)
    inner, own, sent = pair_inner(
        preact, upstream, first, last, master.reshape(used, LANES), block, rows
    )
    kernel = lax.all_to_all(sent, AXES, 0, 0, tiled=True)
    own, xlo, xhi = side((odd_halves, even_halves), own)
    planes = (xlo, first, inner, last, xhi)
    own, activations = lax.optimization_barrier((own, activations))
    other = shifted(own, {"gy": "swap"})
    planes_x, columns = input_planes(activations, True)
    z_sent = join(own, other, columns, size_x * size_y)
    from_odd = swapped(z_sent[1], "gz", 1)
    from_even = swapped(z_sent[0], "gz", 0)
    sources = (*planes, other, other)
    acc = pair_wgrad(sources, planes_x, shape)
    z_received = (from_odd, from_even)
    part = finish(acc, columns, z_sent, z_received, scale, rows, (size_x, size_y), block)
    part, kernel = lax.optimization_barrier((part, kernel))
    parts = lax.all_to_all(part, AXES, 0, 0, tiled=True)
    weights = spread(kernel, channels, rows)
    grad_input = pair_dgrad((*sources, *z_received), weights, shape)
    return grad_input, *adam(parts, master, first_moment, second_moment)


def yface_kernel(*refs):
    low_ref, high_ref = refs[5:]
    size_z = low_ref.shape[-1]
    for index in range(low_ref.shape[0]):
        body = body_of(refs[:5], index)
        plane = body.shape[-1]
        low_ref[index] = body[:, :size_z]
        high_ref[index] = body[:, plane - size_z :]


def y_faces(planes, size_z):
    inner, channels, _ = planes[2].shape
    face = jax.ShapeDtypeStruct((inner + 4, channels, size_z), BF16)
    return pl.pallas_call(
        yface_kernel,
        in_specs=[VMEM] * 5,
        out_specs=[VMEM] * 2,
        out_shape=[face] * 2,
        compiler_params=params(),
        cost_estimate=cost(0, 2**19),
        name="yfaces",
    )(*planes)


def zface_kernel(*refs):
    zlo_ref, zhi_ref = refs[7:]
    size_z = refs[5].shape[-1]
    whole = []
    for index in range(refs[5].shape[0]):
        low, high = y_halo(refs[5:7], index)
        body = body_of(refs[:5], index)[...]
        whole.append(jnp.concatenate([low.astype(BF16), body, high.astype(BF16)], axis=1))
    low, high = z_tiles(whole, whole[0].shape[1] // size_z, size_z, range(len(whole)))
    zlo_ref[...] = low.astype(BF16)
    zhi_ref[...] = high.astype(BF16)


def z_faces(planes, y_halos):
    face = jax.ShapeDtypeStruct((planes[0].shape[0], LANES), BF16)
    return pl.pallas_call(
        zface_kernel,
        in_specs=[VMEM] * 7,
        out_specs=[VMEM] * 2,
        out_shape=[face, face],
        compiler_params=params(),
        cost_estimate=cost(2**27, 2**21),
        name="zfaces",
    )(*planes, *y_halos)


def wgrad_kernel(scale, *refs):
    x_ref, part_ref, g3, x3, acc, flat = refs[9:]
    size_x, channels, plane = x_ref.shape
    size_z = refs[5].shape[-1]
    halo = z_halo(refs[7], refs[8], size_x + 2, plane // size_z + 2, size_z)
    weight_products(refs, halo, x_ref, g3, x3, acc)
    whole = to_flat(acc[...] * scale, channels, channels, flat)
    part_ref[...] = whole[:, : part_ref.shape[1]].astype(BF16)


def wgrad(sources, planes_x, shape, scale):
    channels = shape[0]
    return pl.pallas_call(
        functools.partial(wgrad_kernel, scale),
        in_specs=[VMEM] * 10,
        out_specs=VMEM,
        out_shape=jax.ShapeDtypeStruct((channels, 27 * channels), BF16),
        scratch_shapes=[
            g3_scratch(*shape),
            x3_scratch(*shape),
            acc_scratch(channels),
            flat_scratch(channels),
        ],
        compiler_params=params(32 * 2**20),
        cost_estimate=wgrad_cost(*shape),
        name="wgrad",
    )(*sources, planes_x)


def dgrad_kernel(*refs):
    w_ref, out_ref, g3, turned, weights, tile = refs[9:]
    _, size_x, size_y, size_z = out_ref.shape
    spread_weights(w_ref[...].astype(F32), turned, weights)
    halo = z_halo(refs[7], refs[8], size_x + 2, size_y + 2, size_z)
    input_products(refs, halo, g3, weights, tile, out_ref)


def dgrad(sources, kernel, shape):
    return pl.pallas_call(
        dgrad_kernel,
        in_specs=[VMEM] * 10,
        out_specs=VMEM,
        out_shape=jax.ShapeDtypeStruct(shape, BF16),
        scratch_shapes=dgrad_scratch(*shape),
        compiler_params=params(32 * 2**20),
        cost_estimate=dgrad_cost(*shape),
        name="dgrad",
    )(*sources, kernel)


def general_program(activations, preact, upstream, master, first_moment, second_moment, scale):
    shape = activations.shape
    channels, _, _, size_z = shape
    devices = math.prod(lax.axis_size(a) for a in AXES)
    share = master.shape[0]
    first, last = faces(preact, upstream)
    x_halos = (shifted(last, {"gx": 1}), shifted(first, {"gx": -1}))
    inner = inner_planes(preact, upstream)
    (planes_x,) = input_planes(activations, False)
    sent = jnp.broadcast_to(master.astype(BF16).reshape(1, 1, share), (devices, 1, share))
    kernel = lax.all_to_all(sent, AXES, 0, 0, tiled=True).reshape(channels, 27 * channels)
    planes = (x_halos[0], first, inner, last, x_halos[1])
    y_sent = y_faces(planes, size_z)
    y_halos = (shifted(y_sent[1], {"gy": 1}), shifted(y_sent[0], {"gy": -1}))
    zlo, zhi = z_faces(planes, y_halos)
    z_halos = (shifted(zhi, {"gz": 1}), shifted(zlo, {"gz": -1}))
    sources = (*planes, *y_halos, *z_halos)
    part = wgrad(sources, planes_x, shape, scale)
    part, kernel = lax.optimization_barrier((part, kernel))
    parts = lax.all_to_all(part.reshape(devices, 1, share), AXES, 0, 0, tiled=True)
    grad_input = dgrad(sources, kernel, shape)
    weight_grad = jnp.sum(parts.astype(F32), axis=0).reshape(-1)
    results = adam_step(master, first_moment, second_moment, weight_grad)
    return grad_input, weight_grad, *results


def shifted(value, moves):
    names = tuple(moves)
    sizes = [lax.axis_size(name) for name in names]
    pairs = []
    for source in range(math.prod(sizes)):
        rest, coords = source, []
        for size in reversed(sizes):
            coords.insert(0, rest % size)
            rest //= size
        coords = [
            (at + moves[name]) if moves[name] != "swap" else 1 - at
            for at, name in zip(coords, names)
        ]
        if all(0 <= at < size for at, size in zip(coords, sizes)):
            target = 0
            for at, size in zip(coords, sizes):
                target = target * size + at
            pairs.append((source, target))
    return lax.ppermute(value, names if len(names) > 1 else names[0], pairs)


def swapped(value, axis, start):
    pairs = []
    for low in range(start, lax.axis_size(axis) - 1, 2):
        pairs += [(low, low + 1), (low + 1, low)]
    return lax.ppermute(value, axis, pairs)


def local(activations, preact, upstream, master, first_moment, second_moment):
    channels, size_x, size_y, size_z = activations.shape
    devices = math.prod(lax.axis_size(a) for a in AXES)
    share = master.shape[0]
    scale = 1.0 / math.sqrt(size_x * size_y * size_z * devices)
    in_pairs = (
        lax.axis_size("gy") == 2
        and channels % devices == 0
        and share % LANES == 0
        and channels // (channels // devices) % 16 == 0
        and 2 * size_x * size_y <= LANES
        and (size_x + 2) * size_y <= LANES
    )
    program = pair_program if in_pairs else general_program
    return program(
        activations, preact, upstream, master, first_moment, second_moment, scale
    )


def solution(mesh):
    volume = P(None, "gx", "gy", "gz")
    flat = P(AXES)
    return jax.shard_map(
        local,
        mesh=mesh,
        in_specs=(volume, volume, volume, flat, flat, flat),
        out_specs=(volume, flat, flat, flat, flat),
        check_vma=False,
    )
```

```python
import functools
import math

import jax
import jax.numpy as jnp
from jax import lax
from jax.experimental import pallas as pl
from jax.experimental.pallas import tpu as pltpu
from jax.sharding import PartitionSpec as P

AXES = ("gx", "gy", "gz")
LANES = 128
VMEM = pl.BlockSpec(memory_space=pltpu.VMEM)
HBM = pl.BlockSpec(memory_space=pltpu.HBM)
F32 = jnp.float32
BF16 = jnp.bfloat16
FACES_VMEM = 55_900_000
INNER_VMEM = 54_800_000


def params(limit=24 * 2**20):
    return pltpu.CompilerParams(vmem_limit_bytes=limit)


def cost(flops, moved):
    return pl.CostEstimate(flops=flops, bytes_accessed=moved, transcendentals=0)


def to_planes(value, tile, write, rows=1):
    channels, size_y, size_z = value.shape
    count = channels // rows
    tile[...] = value.astype(F32).reshape(channels * size_y, size_z)
    for y in range(size_y):
        for r in range(rows):
            picked = tile[pl.ds(r * size_y + y, count, stride=rows * size_y), :]
            write(slice(r * count, (r + 1) * count), y, picked.astype(BF16))


def masked(p, u):
    return jnp.where(p > 0, u, jnp.zeros_like(u))


def choose(condition, out_ref, first_ref, second_ref):
    @pl.when(condition)
    def _():
        out_ref[...] = first_ref[...]

    @pl.when(jnp.logical_not(condition))
    def _():
        out_ref[...] = second_ref[...]


def face_kernel(axis, rows, p_ref, u_ref, *refs):
    p_buf, u_buf, tile, sems = refs[-4:]
    out_refs, swap_refs = refs[:2], refs[2:-4]
    size_x, size_z = p_ref.shape[1], p_ref.shape[3]
    copies = []
    for k, x in enumerate((0, size_x - 1)):
        pair = (
            pltpu.make_async_copy(p_ref.at[:, x], p_buf.at[k], sems.at[2 * k]),
            pltpu.make_async_copy(u_ref.at[:, x], u_buf.at[k], sems.at[2 * k + 1]),
        )
        for copy in pair:
            copy.start()
        copies.append(pair)
    for k, out_ref in enumerate(out_refs):
        for copy in copies[k]:
            copy.wait()

        def write(at, y, value):
            out_ref[at, y * size_z : (y + 1) * size_z] = value

        to_planes(masked(p_buf[k], u_buf[k]), tile.at[k], write, rows)
    if axis is not None:
        choose(is_odd(axis), swap_refs[0], out_refs[1], out_refs[0])


def faces(preact, upstream, axis=None, rows=1):
    channels, size_x, size_y, size_z = preact.shape
    face = jax.ShapeDtypeStruct((channels, size_y * size_z), BF16)
    buffer = pltpu.VMEM((2, channels, size_y, size_z), BF16)
    count = 2 if axis is None else 3
    return pl.pallas_call(
        functools.partial(face_kernel, axis, rows),
        in_specs=[HBM, HBM],
        out_specs=[VMEM] * count,
        out_shape=[face] * count,
        scratch_shapes=[
            buffer,
            buffer,
            pltpu.VMEM((2, channels * size_y, size_z), F32),
            pltpu.SemaphoreType.DMA((4,)),
        ],
        compiler_params=params(FACES_VMEM),
        cost_estimate=cost(0, 2**20),
        name="faces",
    )(preact, upstream)


def read_inner(rows, p_ref, u_ref, g_ref, p_buf, u_buf, tile, sems):
    size_x, size_z = p_ref.shape[1], p_ref.shape[3]
    inner = size_x - 2
    copies = []
    for x in range(inner):
        pair = (
            pltpu.make_async_copy(p_ref.at[:, x + 1], p_buf.at[x], sems.at[x]),
            pltpu.make_async_copy(u_ref.at[:, x + 1], u_buf.at[x], sems.at[inner + x]),
        )
        for copy in pair:
            copy.start()
        copies.append(pair)
    for x in range(inner):
        for copy in copies[x]:
            copy.wait()

        def write(at, y, value):
            g_ref[x, at, y * size_z : (y + 1) * size_z] = value

        to_planes(masked(p_buf[x], u_buf[x]), tile.at[x % 2], write, rows)


def inner_kernel(*refs):
    read_inner(1, *refs)


def inner_output(channels, size_x, size_y, size_z):
    return jax.ShapeDtypeStruct((size_x - 2, channels, size_y * size_z), BF16)


def inner_scratch(channels, size_x, size_y, size_z):
    return [
        pltpu.VMEM((size_x - 2, channels, size_y, size_z), BF16),
        pltpu.VMEM((size_x - 2, channels, size_y, size_z), BF16),
        pltpu.VMEM((2, channels * size_y, size_z), F32),
        pltpu.SemaphoreType.DMA((2 * size_x - 4,)),
    ]


def inner_planes(preact, upstream):
    shape = preact.shape
    return pl.pallas_call(
        inner_kernel,
        in_specs=[HBM] * 2,
        out_specs=VMEM,
        out_shape=inner_output(*shape),
        scratch_shapes=inner_scratch(*shape),
        compiler_params=params(INNER_VMEM),
        cost_estimate=cost(0, 4 * 2**20),
        name="inner",
    )(preact, upstream)


def input_kernel(a_ref, x_ref, *refs):
    tile = refs[-1]
    channels, size_x, size_y, size_z = a_ref.shape
    for x in range(size_x):

        def write(at, y, value):
            x_ref[x, at, y * size_z : (y + 1) * size_z] = value

        to_planes(a_ref[:, x], tile.at[x % 2], write)
    if len(refs) > 1:
        low, high = z_tiles([x_ref[x] for x in range(size_x)], size_y, size_z, range(size_x))
        refs[0][...] = (low + pltpu.roll(high, size_x * size_y, 1)).astype(BF16)


def input_planes(activations, with_columns):
    channels, size_x, size_y, size_z = activations.shape
    outs = [jax.ShapeDtypeStruct((size_x, channels, size_y * size_z), BF16)]
    if with_columns:
        outs.append(jax.ShapeDtypeStruct((channels, LANES), BF16))
    return pl.pallas_call(
        input_kernel,
        in_specs=[VMEM],
        out_specs=[VMEM] * len(outs),
        out_shape=outs,
        scratch_shapes=[pltpu.VMEM((2, channels * size_y, size_z), F32)],
        compiler_params=params(),
        cost_estimate=cost(0, 2 * 2**20),
        name="inputs",
    )(activations)


def body_of(refs, index):
    planes = refs[2].shape[0] + 4
    if 2 <= index < planes - 2:
        return refs[2].at[index - 2]
    return refs[{0: 0, 1: 1, planes - 2: 3, planes - 1: 4}[index]]


def y_halo(refs, index):
    me = lax.axis_index("gy")
    low = jnp.where(me > 0, refs[0][index].astype(F32), 0.0)
    high = jnp.where(me < lax.axis_size("gy") - 1, refs[1][index].astype(F32), 0.0)
    return low, high


def z_picker(rows_y, size_z):
    shape = (rows_y * size_z, 2 * LANES)
    voxel = lax.broadcasted_iota(jnp.int32, shape, 0)
    lane = lax.broadcasted_iota(jnp.int32, shape, 1)
    wanted = jnp.where(lane < LANES, lane * size_z, (lane - LANES) * size_z + size_z - 1)
    return (voxel == wanted).astype(F32).astype(BF16)


def z_tiles(planes, rows_y, size_z, numbers):
    channels = planes[0].shape[0]
    columns = jnp.dot(
        jnp.concatenate(planes, axis=0), z_picker(rows_y, size_z), preferred_element_type=F32
    )
    low = jnp.zeros((channels, LANES), F32)
    high = jnp.zeros((channels, LANES), F32)
    for index, number in enumerate(numbers):
        rows = columns[index * channels : (index + 1) * channels]
        low = low + pltpu.roll(rows[:, :LANES], number * rows_y, 1)
        high = high + pltpu.roll(rows[:, LANES:], number * rows_y, 1)
    return low, high


def put_columns(columns, row_of, rows_y, size_z):
    shape = (2 * LANES, rows_y * size_z)
    source = lax.broadcasted_iota(jnp.int32, shape, 0)
    voxel = lax.broadcasted_iota(jnp.int32, shape, 1)
    number = source % LANES
    place = row_of(number) * size_z + jnp.where(source < LANES, 0, size_z - 1)
    place = jnp.where(number < rows_y, place, -1)
    put = (voxel == place).astype(F32).astype(BF16)
    rows = [jnp.concatenate(pair, axis=1) for pair in columns]
    return jnp.dot(
        jnp.concatenate(rows, axis=0).astype(BF16), put, preferred_element_type=F32
    ).astype(BF16)


def z_halo(low_ref, high_ref, planes, rows_y, size_z):
    columns = []
    for index in range(planes):
        shift = -index * rows_y % LANES
        columns.append(
            [pltpu.roll(ref[...].astype(F32), shift, 1) for ref in (low_ref, high_ref)]
        )
    return put_columns(columns, lambda number: number, rows_y, size_z)


def pair_z_halo(odd_ref, even_ref, planes, size_y, size_z):
    me, odd = lax.axis_index("gy"), is_odd("gz")
    sides = []
    for low, high in ((even_ref, odd_ref), (odd_ref, even_ref)):
        first, second = (either(odd, low[k], high[k]) for k in range(2))
        lane = lax.broadcasted_iota(jnp.int32, first.shape, 1)
        own = jnp.where(me == 0, first, second)
        before = jnp.where(me == 0, 0.0, first)
        after = jnp.where(me == 0, second, 0.0)
        columns = []
        for index in range(planes):
            start = index * size_y
            columns.append(
                jnp.where(
                    lane < size_y,
                    pltpu.roll(own, -start % LANES, 1),
                    jnp.where(
                        lane == size_y,
                        pltpu.roll(before, (1 - start) % LANES, 1),
                        pltpu.roll(after, (size_y + 1 - start) % LANES, 1),
                    ),
                )
            )
        sides.append(columns)

    def row_of(number):
        return jnp.where(number < size_y, number + 1, jnp.where(number == size_y, 0, size_y + 1))

    return put_columns(list(zip(*sides)), row_of, size_y + 2, size_z)


def shifted_plane(index, refs, halo, g3):
    channels, plane = refs[0].shape
    size_z = refs[5].shape[-1]
    rows_y = plane // size_z + 2
    base = 3 * channels * index
    lane = lax.broadcasted_iota(jnp.int32, (channels, size_z), 1)
    is_first, is_last = lane == 0, lane == size_z - 1
    low, high = y_halo(refs[5:7], index)
    body = body_of(refs[:5], index)
    for row in range(rows_y):
        cols = slice(row * size_z, (row + 1) * size_z)
        if row == 0:
            value = low.astype(BF16)
        elif row == rows_y - 1:
            value = high.astype(BF16)
        else:
            value = body[:, (row - 1) * size_z : row * size_z]
        if halo is None:
            edge = jnp.zeros_like(value)
        else:
            edge = halo[index * channels : (index + 1) * channels, cols]
        before = jnp.where(is_first, edge, pltpu.roll(value, 1, 1))
        after = jnp.where(is_last, edge, pltpu.roll(value, size_z - 1, 1))
        g3[base : base + channels, cols] = before
        g3[base + channels : base + 2 * channels, cols] = value
        g3[base + 2 * channels : base + 3 * channels, cols] = after


def weight_products(refs, halo, x_ref, g3, x3, acc):
    size_x, channels, plane = x_ref.shape
    size_z = refs[5].shape[-1]
    group = 3 * channels
    zero = jnp.zeros((channels, 2 * size_z), BF16)
    done = 0
    for x in range(size_x):
        while done < x + 3:
            shifted_plane(done, refs, halo, g3)
            done += 1
        value = x_ref[x]
        for b in range(3):
            at = slice(b * channels, (b + 1) * channels)
            start = (2 - b) * size_z
            x3[x, at, start : start + plane] = value
            if start:
                x3[x, at, :start] = zero[:, :start]
            if start < 2 * size_z:
                x3[x, at, start + plane :] = zero[:, start:]
        product = lax.dot_general(
            g3[x * group : (x + 3) * group, :],
            x3[x],
            (((1,), (1,)), ((), ())),
            preferred_element_type=F32,
        )
        if x == 0:
            acc[...] = product
        else:
            acc[...] += product


def to_flat(value, count, channels, flat):
    height, width = value.shape
    wide = value
    if height % LANES:
        wide = jnp.concatenate([wide, jnp.zeros((-height % LANES, width), F32)], axis=0)
    if width % LANES:
        wide = jnp.concatenate([wide, jnp.zeros((wide.shape[0], -width % LANES), F32)], axis=1)
    turned = wide.T
    for b in range(3):
        rows = turned[b * channels : (b + 1) * channels]
        for block in range(9):
            start = block * count
            cell = rows[:, start // LANES * LANES : (start // LANES + 1) * LANES]
            tap = (2 - block // 3) * 9 + b * 3 + 2 - block % 3
            shift = -start % LANES
            flat[pl.ds(tap, channels, stride=27), :] = pltpu.roll(cell, shift, 1) if shift else cell
    return flat[...].T[:count]


def spread_weights(whole, turned, weights):
    channels, taps = whole.shape
    group = 3 * channels
    whole = jnp.concatenate([whole, jnp.zeros((LANES - channels, taps), F32)], axis=0)
    whole = jnp.concatenate([whole, jnp.zeros((LANES, -taps % LANES), F32)], axis=1)
    turned[...] = whole.T
    for b in range(3):
        blocks = []
        for a in range(3):
            for c in range(3):
                tap = (2 - a) * 9 + (2 - b) * 3 + 2 - c
                blocks.append(turned[pl.ds(tap, channels, stride=27), :][:, :channels])
        zero = jnp.zeros((channels, group), F32)
        weights[b, :channels] = jnp.concatenate(blocks + [zero], axis=1).astype(BF16)
        weights[b, channels:] = jnp.concatenate([zero] + blocks, axis=1).astype(BF16)


def input_products(refs, halo, g3, weights, tile, out_ref):
    channels, size_x, size_y, size_z = out_ref.shape
    group = 3 * channels
    plane = size_y * size_z
    done = 0
    for pair in range(size_x // 2):
        while done < 2 * pair + 4:
            shifted_plane(done, refs, halo, g3)
            done += 1
        at = slice(2 * pair * group, (2 * pair + 4) * group)
        total = None
        for b in range(3):
            product = jnp.dot(
                weights[b],
                g3[at, b * size_z : b * size_z + plane],
                preferred_element_type=F32,
            )
            total = product if total is None else total + product
        for half in range(2):
            for y in range(size_y):
                tile[half, pl.ds(y, channels, stride=size_y), :] = total[
                    half * channels : (half + 1) * channels, y * size_z : (y + 1) * size_z
                ]
            out_ref[:, 2 * pair + half] = (
                tile[half].reshape(channels, size_y, size_z).astype(BF16)
            )


def g3_scratch(channels, size_x, size_y, size_z):
    return pltpu.VMEM(((size_x + 2) * 3 * channels, (size_y + 2) * size_z), BF16)


def x3_scratch(channels, size_x, size_y, size_z):
    return pltpu.VMEM((size_x, 3 * channels, (size_y + 2) * size_z), BF16)


def acc_scratch(channels):
    return pltpu.VMEM((9 * channels, 3 * channels), F32)


def flat_scratch(channels):
    return pltpu.VMEM((-(-27 * channels // LANES) * LANES, LANES), F32)


def dgrad_scratch(channels, size_x, size_y, size_z):
    return [
        g3_scratch(channels, size_x, size_y, size_z),
        flat_scratch(channels),
        pltpu.VMEM((3, 2 * channels, 12 * channels), BF16),
        pltpu.VMEM((2, channels * size_y, size_z), F32),
    ]


def wgrad_cost(channels, size_x, size_y, size_z):
    return cost(54 * channels * channels * size_x * (size_y + 2) * size_z, 4 * 2**20)


def dgrad_cost(channels, size_x, size_y, size_z):
    return cost(72 * channels * channels * size_x * size_y * size_z, 4 * 2**20)


def row_for_other(body, size_z):
    plane = body.shape[-1]
    low, high = body[:, :size_z].astype(F32), body[:, plane - size_z :].astype(F32)
    return jnp.where(lax.axis_index("gy") == 0, high, low).astype(BF16)


def pair_inner_kernel(rows, *refs):
    first_ref, last_ref, m_ref, g_ref, side_ref, swap_ref, sent_ref = refs[2:9]
    tile_ref, tile_sems = refs[13:]
    choose(is_odd("gx"), swap_ref, first_ref, last_ref)
    share = m_ref[...]
    height = tile_ref.shape[0] - share.shape[0]
    if height:
        share = jnp.concatenate([share, jnp.zeros((height, share.shape[1]), F32)], axis=0)
    tile_ref[...] = share.astype(BF16)
    copies = [
        pltpu.make_async_copy(tile_ref, sent_ref.at[device], tile_sems.at[device])
        for device in range(sent_ref.shape[0])
    ]
    for copy in copies:
        copy.start()
    read_inner(rows, *refs[:2], g_ref, *refs[9:13])
    size_z = side_ref.shape[-1]
    inner, _, plane = g_ref.shape
    size_x = inner + 2
    bodies = [first_ref] + [g_ref.at[x] for x in range(inner)] + [last_ref]
    for x, body in enumerate(bodies):
        side_ref[x] = row_for_other(body, size_z)
    low, high = z_tiles(
        [body[...] for body in bodies], plane // size_z, size_z, range(1, size_x + 1)
    )
    side_ref[size_x] = low.astype(BF16)
    side_ref[size_x + 1] = high.astype(BF16)
    for copy in copies:
        copy.wait()


def pair_inner(preact, upstream, first, last, share, sent_shape, rows):
    shape = preact.shape
    channels, size_x, _, size_z = shape
    return pl.pallas_call(
        functools.partial(pair_inner_kernel, rows),
        in_specs=[HBM] * 2 + [VMEM] * 3,
        out_specs=[VMEM] * 3 + [HBM],
        out_shape=[
            inner_output(*shape),
            jax.ShapeDtypeStruct((size_x + 2, channels, size_z), BF16),
            jax.ShapeDtypeStruct(first.shape, BF16),
            jax.ShapeDtypeStruct(sent_shape, BF16),
        ],
        scratch_shapes=inner_scratch(*shape)
        + [pltpu.VMEM(sent_shape[1:], BF16), pltpu.SemaphoreType.DMA((sent_shape[0],))],
        compiler_params=params(INNER_VMEM),
        cost_estimate=cost(0, 4 * 2**20),
        name="inner",
    )(preact, upstream, first, last, share)


def is_odd(axis):
    return lax.rem(lax.axis_index(axis), 2) == 1


def either(condition, first, second):
    return jnp.where(condition, first.astype(F32), second.astype(F32))


def side_kernel(odd_ref, even_ref, own_ref, sent_ref, xlo_ref, xhi_ref):
    size_x = own_ref.shape[0] - 2
    size_z = own_ref.shape[-1]
    size_y = xlo_ref.shape[-1] // size_z
    odd = is_odd("gx")
    low = either(odd, even_ref[...], odd_ref[...]).astype(BF16)
    high = either(odd, odd_ref[...], even_ref[...]).astype(BF16)
    xlo_ref[...] = low
    xhi_ref[...] = high
    sent_ref[0] = row_for_other(low, size_z)
    for x in range(size_x):
        sent_ref[x + 1] = own_ref[x]
    sent_ref[size_x + 1] = row_for_other(high, size_z)
    lane = lax.broadcasted_iota(jnp.int32, (low.shape[0], LANES), 1)
    first, second = own_ref[size_x], own_ref[size_x + 1]
    for number, plane in ((0, low), (size_x + 1, high)):
        for y in range(size_y):
            at = number * size_y + y
            head = plane[:, y * size_z : y * size_z + LANES]
            tail = plane[:, (y + 1) * size_z - LANES : (y + 1) * size_z]
            first = jnp.where(lane == at, pltpu.roll(head, at, 1), first)
            second = jnp.where(lane == at, pltpu.roll(tail, at + 1, 1), second)
    sent_ref[size_x + 2] = first
    sent_ref[size_x + 3] = second


def side(halves, own):
    plane = jax.ShapeDtypeStruct(halves[0].shape, BF16)
    return pl.pallas_call(
        side_kernel,
        in_specs=[VMEM] * 3,
        out_specs=[VMEM] * 3,
        out_shape=[
            jax.ShapeDtypeStruct((own.shape[0] + 2, *own.shape[1:]), BF16),
            plane,
            plane,
        ],
        compiler_params=params(),
        cost_estimate=cost(2**25, 2**19),
        name="side",
    )(*halves, own)


def own_columns(columns, number, area):
    me = lax.axis_index("gy")
    value = columns.astype(F32)
    lane = lax.broadcasted_iota(jnp.int32, value.shape, 1)
    first = pltpu.roll(value, -number * area % LANES, 1)
    second = pltpu.roll(value, (1 - number) * area % LANES, 1)
    first = jnp.where(lane < area, first, 0.0)
    second = jnp.where((lane >= area) & (lane < 2 * area), second, 0.0)
    return jnp.where(me == 0, first, second)


def join_kernel(area, own_ref, other_ref, columns_ref, even_ref, odd_ref):
    at = own_ref.shape[0] - 2
    me = lax.axis_index("gy")
    last = own_columns(columns_ref[...], 1, area).astype(BF16)

    def fill(up_ref, down_ref):
        for k, out_ref in enumerate((down_ref, up_ref)):
            out_ref[me] = own_ref[at + k]
            out_ref[1 - me] = other_ref[at + k]
        up_ref[2] = last
        down_ref[2] = last

    odd = is_odd("gz")

    @pl.when(odd)
    def _():
        fill(odd_ref, even_ref)

    @pl.when(jnp.logical_not(odd))
    def _():
        fill(even_ref, odd_ref)


def join(own, other, columns, area):
    return pl.pallas_call(
        functools.partial(join_kernel, area),
        in_specs=[VMEM] * 3,
        out_specs=[VMEM] * 2,
        out_shape=[jax.ShapeDtypeStruct((3, *own.shape[1:]), BF16)] * 2,
        compiler_params=params(),
        cost_estimate=cost(0, 2**17),
        name="join",
    )(own, other, columns)


def pair_wgrad_kernel(*refs):
    x_ref, acc_ref, g3, x3 = refs[7:]
    weight_products(refs, None, x_ref, g3, x3, acc_ref)


def pair_wgrad(sources, planes_x, shape):
    channels = shape[0]
    return pl.pallas_call(
        pair_wgrad_kernel,
        in_specs=[VMEM] * 8,
        out_specs=VMEM,
        out_shape=jax.ShapeDtypeStruct((9 * channels, 3 * channels), F32),
        scratch_shapes=[g3_scratch(*shape), x3_scratch(*shape)],
        compiler_params=params(32 * 2**20),
        cost_estimate=wgrad_cost(*shape),
        name="wgrad",
    )(*sources, planes_x)


def finish_kernel(scale, rows, sizes, *refs):
    acc_ref, columns_ref, even_ref, odd_ref, from_odd_ref, from_even_ref = refs[:6]
    part_ref, chunks = refs[6:]
    size_x, size_y = sizes
    channels = columns_ref.shape[0]
    area = size_x * size_y
    odd = is_odd("gz")
    lane = lax.broadcasted_iota(jnp.int32, (channels, LANES), 1)
    row = lane % size_y
    jump = area - size_y + 1
    below = [either(odd, from_even_ref[k], from_odd_ref[k]) for k in range(3)]
    own = [either(odd, even_ref[k], odd_ref[k]) for k in range(2)]
    pairs = ((below[:2], own_columns(columns_ref[...], 0, area)), (own, below[2]))
    edges = []
    for tiles, value in pairs:
        before = jnp.where(lane >= area, pltpu.roll(value, jump, 1), 0.0)
        after = jnp.where(lane < area, pltpu.roll(value, LANES - jump, 1), 0.0)
        right = jnp.concatenate(
            [
                jnp.where(row > 0, pltpu.roll(value, 1, 1), before),
                value,
                jnp.where(row < size_y - 1, pltpu.roll(value, LANES - 1, 1), after),
            ],
            axis=0,
        )
        left = []
        for a in range(3):
            first = pltpu.roll(tiles[0], -a * size_y % LANES, 1)
            second = pltpu.roll(tiles[1], (area - a * size_y) % LANES, 1)
            left.append(jnp.where(lane < area, first, jnp.where(lane < 2 * area, second, 0.0)))
        edges.append(
            lax.dot_general(
                jnp.concatenate(left, axis=0).astype(BF16),
                right.astype(BF16),
                (((1,), (1,)), ((), ())),
                preferred_element_type=F32,
            )
        )
    count, height, width = part_ref.shape
    chunks[...] = jnp.zeros_like(chunks)
    pieces = rows * acc_ref.shape[1] // width
    for a in range(3):
        for c in range(3):
            at = 3 * a + c
            block = acc_ref[at * channels : (at + 1) * channels, :]
            if c != 1:
                block = block + edges[c // 2][a * channels : (a + 1) * channels]
            block = block * scale
            line = jnp.concatenate(
                [block[r * count : (r + 1) * count] for r in range(rows)], axis=1
            )
            for k in range(pieces):
                chunks[pl.ds(at * pieces + k, count, stride=height), :] = line[
                    :, k * width : (k + 1) * width
                ]
    part_ref[...] = chunks[...].reshape(part_ref.shape).astype(BF16)


def finish(acc, columns, sent, received, scale, rows, sizes, part_shape):
    channels = columns.shape[0]
    return pl.pallas_call(
        functools.partial(finish_kernel, scale, rows, sizes),
        in_specs=[VMEM] * 6,
        out_specs=VMEM,
        out_shape=jax.ShapeDtypeStruct(part_shape, BF16),
        scratch_shapes=[pltpu.VMEM((part_shape[0] * part_shape[1], part_shape[2]), F32)],
        compiler_params=params(),
        cost_estimate=cost(2**27, 2**21),
        name="finish",
    )(acc, columns, *sent, *received)


def adam_step(master, first, second, weight_grad):
    new_first = 0.9 * first + 0.1 * weight_grad
    new_second = 0.999 * second + 0.001 * weight_grad * weight_grad
    corr_first = 1.0 - (0.9**10) ** 10
    corr_second = 1.0 - (0.999**10) ** 10
    update = new_first / corr_first / (jnp.sqrt(new_second / corr_second) + 1e-08) + 0.01 * master
    return master - 0.05 * update, new_first, new_second


def in_flat_order(value, rows, places, spread_rows):
    taps = 27
    lane = lax.broadcasted_iota(jnp.int32, (9, LANES), 1)
    rows[: value.shape[0], :] = value
    thirds = [rows[pl.ds(k, 9, stride=3), :] for k in range(3)]
    half = LANES // 2
    by_y = (
        jnp.where(lane < half, thirds[0], thirds[1]),
        jnp.where(lane < half, pltpu.roll(thirds[0], half, 1), pltpu.roll(thirds[2], half, 1)),
        jnp.where(lane < half, thirds[1], thirds[2]),
    )
    places[...] = jnp.zeros_like(places)
    for b in range(3):
        spread_rows[b, :9, :] = by_y[b]
        for block in range(9):
            tap = (2 - block // 3) * 9 + b * 3 + 2 - block % 3
            places[tap : tap + 1, :] = spread_rows[b, block : block + 1, :]
    line = places[...].T
    number = lax.broadcasted_iota(jnp.int32, (LANES, LANES), 0) * taps
    column = lax.broadcasted_iota(jnp.int32, (LANES, LANES), 1)
    for bit in range(7):
        turn = 1 << bit
        line = jnp.where((number & turn) != 0, pltpu.roll(line, turn, 1), line)
    start = number & (LANES - 1)
    line = jnp.concatenate(
        [jnp.where(column >= start, line, 0.0), jnp.where(column < start, line, 0.0)], axis=0
    )
    target = lax.broadcasted_iota(jnp.int32, (32, 2 * LANES), 0)
    source = lax.broadcasted_iota(jnp.int32, (32, 2 * LANES), 1)
    goes = lax.shift_right_logical((source & (LANES - 1)) * taps, 7)
    goes = goes + jnp.where(source < LANES, 0, 1)
    pick = jnp.where(goes == target, 1.0, 0.0)
    return jnp.dot(
        pick, line, preferred_element_type=F32, precision=lax.Precision.HIGHEST
    )[:taps]


def adam_kernel(parts_ref, master_ref, first_ref, second_ref, *refs):
    out_refs, scratch = refs[:4], refs[4:]
    total = parts_ref[0].astype(F32)
    for source in range(1, parts_ref.shape[0]):
        total = total + parts_ref[source].astype(F32)
    weight_grad = in_flat_order(total, *scratch)
    results = adam_step(master_ref[...], first_ref[...], second_ref[...], weight_grad)
    for out_ref, result in zip(out_refs, (weight_grad, *results)):
        out_ref[...] = result


def adam(parts, *states):
    share = states[0].shape[0]
    tiled = [state.reshape(share // LANES, LANES) for state in states]
    result = jax.ShapeDtypeStruct(tiled[0].shape, F32)
    outs = pl.pallas_call(
        adam_kernel,
        in_specs=[VMEM] * 4,
        out_specs=[VMEM] * 4,
        out_shape=[result] * 4,
        scratch_shapes=[
            pltpu.VMEM(parts.shape[1:], F32),
            pltpu.VMEM((LANES, LANES), F32),
            pltpu.VMEM((3, 16, LANES), F32),
        ],
        compiler_params=params(),
        cost_estimate=cost(2**22, 2**19),
        name="adam",
    )(parts, *tiled)
    return tuple(out.reshape(share) for out in outs)


def spread_kernel(rows, w_ref, weights_ref, turned, chunks):
    count, height, width = w_ref.shape
    taps = 27 * rows * count
    chunks[...] = w_ref[...].astype(F32).reshape(chunks.shape)
    line = jnp.concatenate(
        [chunks[pl.ds(k, count, stride=height), :] for k in range(rows * taps // width)], axis=1
    )
    whole = jnp.concatenate([line[:, r * taps : (r + 1) * taps] for r in range(rows)], axis=0)
    spread_weights(whole, turned, weights_ref)


def spread(kernel, channels, rows):
    return pl.pallas_call(
        functools.partial(spread_kernel, rows),
        in_specs=[VMEM],
        out_specs=VMEM,
        out_shape=jax.ShapeDtypeStruct((3, 2 * channels, 12 * channels), BF16),
        scratch_shapes=[
            flat_scratch(channels),
            pltpu.VMEM((kernel.shape[0] * kernel.shape[1], kernel.shape[2]), F32),
        ],
        compiler_params=params(),
        cost_estimate=cost(2**20, 2**21),
        name="spread",
    )(kernel)


def pair_dgrad_kernel(*refs):
    weights_ref, out_ref, g3, tile = refs[9:]
    _, size_x, size_y, size_z = out_ref.shape
    halo = pair_z_halo(refs[7], refs[8], size_x + 2, size_y, size_z)
    input_products(refs, halo, g3, weights_ref, tile, out_ref)


def pair_dgrad(sources, weights, shape):
    channels, _, size_y, size_z = shape
    return pl.pallas_call(
        pair_dgrad_kernel,
        in_specs=[VMEM] * 10,
        out_specs=VMEM,
        out_shape=jax.ShapeDtypeStruct(shape, BF16),
        scratch_shapes=[g3_scratch(*shape), pltpu.VMEM((2, channels * size_y, size_z), F32)],
        compiler_params=params(32 * 2**20),
        cost_estimate=dgrad_cost(*shape),
        name="dgrad",
    )(*sources, weights)


def pair_program(activations, preact, upstream, master, first_moment, second_moment, scale):
    shape = activations.shape
    channels, size_x, size_y, _ = shape
    devices = math.prod(lax.axis_size(a) for a in AXES)
    rows = channels // devices
    used = master.shape[0] // LANES
    block = (devices, -(-used // 16) * 16, LANES)
    first, last, odd_sent = faces(preact, upstream, "gx", rows)
    odd_halves = swapped(odd_sent, "gx", 1)
    inner, own, even_sent, sent = pair_inner(
        preact, upstream, first, last, master.reshape(used, LANES), block, rows
    )
    even_halves = swapped(even_sent, "gx", 0)
    kernel = lax.all_to_all(sent, AXES, 0, 0, tiled=True)
    own, xlo, xhi = side((odd_halves, even_halves), own)
    planes = (xlo, first, inner, last, xhi)
    own, activations = lax.optimization_barrier((own, activations))
    other = shifted(own, {"gy": "swap"})
    planes_x, columns = input_planes(activations, True)
    z_sent = join(own, other, columns, size_x * size_y)
    from_odd = swapped(z_sent[1], "gz", 1)
    from_even = swapped(z_sent[0], "gz", 0)
    sources = (*planes, other, other)
    acc = pair_wgrad(sources, planes_x, shape)
    z_received = (from_odd, from_even)
    part = finish(acc, columns, z_sent, z_received, scale, rows, (size_x, size_y), block)
    part, kernel = lax.optimization_barrier((part, kernel))
    parts = lax.all_to_all(part, AXES, 0, 0, tiled=True)
    weights = spread(kernel, channels, rows)
    grad_input = pair_dgrad((*sources, *z_received), weights, shape)
    return grad_input, *adam(parts, master, first_moment, second_moment)


def yface_kernel(*refs):
    low_ref, high_ref = refs[5:]
    size_z = low_ref.shape[-1]
    for index in range(low_ref.shape[0]):
        body = body_of(refs[:5], index)
        plane = body.shape[-1]
        low_ref[index] = body[:, :size_z]
        high_ref[index] = body[:, plane - size_z :]


def y_faces(planes, size_z):
    inner, channels, _ = planes[2].shape
    face = jax.ShapeDtypeStruct((inner + 4, channels, size_z), BF16)
    return pl.pallas_call(
        yface_kernel,
        in_specs=[VMEM] * 5,
        out_specs=[VMEM] * 2,
        out_shape=[face] * 2,
        compiler_params=params(),
        cost_estimate=cost(0, 2**19),
        name="yfaces",
    )(*planes)


def zface_kernel(*refs):
    zlo_ref, zhi_ref = refs[7:]
    size_z = refs[5].shape[-1]
    whole = []
    for index in range(refs[5].shape[0]):
        low, high = y_halo(refs[5:7], index)
        body = body_of(refs[:5], index)[...]
        whole.append(jnp.concatenate([low.astype(BF16), body, high.astype(BF16)], axis=1))
    low, high = z_tiles(whole, whole[0].shape[1] // size_z, size_z, range(len(whole)))
    zlo_ref[...] = low.astype(BF16)
    zhi_ref[...] = high.astype(BF16)


def z_faces(planes, y_halos):
    face = jax.ShapeDtypeStruct((planes[0].shape[0], LANES), BF16)
    return pl.pallas_call(
        zface_kernel,
        in_specs=[VMEM] * 7,
        out_specs=[VMEM] * 2,
        out_shape=[face, face],
        compiler_params=params(),
        cost_estimate=cost(2**27, 2**21),
        name="zfaces",
    )(*planes, *y_halos)


def wgrad_kernel(scale, *refs):
    x_ref, part_ref, g3, x3, acc, flat = refs[9:]
    size_x, channels, plane = x_ref.shape
    size_z = refs[5].shape[-1]
    halo = z_halo(refs[7], refs[8], size_x + 2, plane // size_z + 2, size_z)
    weight_products(refs, halo, x_ref, g3, x3, acc)
    whole = to_flat(acc[...] * scale, channels, channels, flat)
    part_ref[...] = whole[:, : part_ref.shape[1]].astype(BF16)


def wgrad(sources, planes_x, shape, scale):
    channels = shape[0]
    return pl.pallas_call(
        functools.partial(wgrad_kernel, scale),
        in_specs=[VMEM] * 10,
        out_specs=VMEM,
        out_shape=jax.ShapeDtypeStruct((channels, 27 * channels), BF16),
        scratch_shapes=[
            g3_scratch(*shape),
            x3_scratch(*shape),
            acc_scratch(channels),
            flat_scratch(channels),
        ],
        compiler_params=params(32 * 2**20),
        cost_estimate=wgrad_cost(*shape),
        name="wgrad",
    )(*sources, planes_x)


def dgrad_kernel(*refs):
    w_ref, out_ref, g3, turned, weights, tile = refs[9:]
    _, size_x, size_y, size_z = out_ref.shape
    spread_weights(w_ref[...].astype(F32), turned, weights)
    halo = z_halo(refs[7], refs[8], size_x + 2, size_y + 2, size_z)
    input_products(refs, halo, g3, weights, tile, out_ref)


def dgrad(sources, kernel, shape):
    return pl.pallas_call(
        dgrad_kernel,
        in_specs=[VMEM] * 10,
        out_specs=VMEM,
        out_shape=jax.ShapeDtypeStruct(shape, BF16),
        scratch_shapes=dgrad_scratch(*shape),
        compiler_params=params(32 * 2**20),
        cost_estimate=dgrad_cost(*shape),
        name="dgrad",
    )(*sources, kernel)


def general_program(activations, preact, upstream, master, first_moment, second_moment, scale):
    shape = activations.shape
    channels, _, _, size_z = shape
    devices = math.prod(lax.axis_size(a) for a in AXES)
    share = master.shape[0]
    first, last = faces(preact, upstream)
    x_halos = (shifted(last, {"gx": 1}), shifted(first, {"gx": -1}))
    inner = inner_planes(preact, upstream)
    (planes_x,) = input_planes(activations, False)
    sent = jnp.broadcast_to(master.astype(BF16).reshape(1, 1, share), (devices, 1, share))
    kernel = lax.all_to_all(sent, AXES, 0, 0, tiled=True).reshape(channels, 27 * channels)
    planes = (x_halos[0], first, inner, last, x_halos[1])
    y_sent = y_faces(planes, size_z)
    y_halos = (shifted(y_sent[1], {"gy": 1}), shifted(y_sent[0], {"gy": -1}))
    zlo, zhi = z_faces(planes, y_halos)
    z_halos = (shifted(zhi, {"gz": 1}), shifted(zlo, {"gz": -1}))
    sources = (*planes, *y_halos, *z_halos)
    part = wgrad(sources, planes_x, shape, scale)
    part, kernel = lax.optimization_barrier((part, kernel))
    parts = lax.all_to_all(part.reshape(devices, 1, share), AXES, 0, 0, tiled=True)
    grad_input = dgrad(sources, kernel, shape)
    weight_grad = jnp.sum(parts.astype(F32), axis=0).reshape(-1)
    results = adam_step(master, first_moment, second_moment, weight_grad)
    return grad_input, weight_grad, *results


def shifted(value, moves):
    names = tuple(moves)
    sizes = [lax.axis_size(name) for name in names]
    pairs = []
    for source in range(math.prod(sizes)):
        rest, coords = source, []
        for size in reversed(sizes):
            coords.insert(0, rest % size)
            rest //= size
        coords = [
            (at + moves[name]) if moves[name] != "swap" else 1 - at
            for at, name in zip(coords, names)
        ]
        if all(0 <= at < size for at, size in zip(coords, sizes)):
            target = 0
            for at, size in zip(coords, sizes):
                target = target * size + at
            pairs.append((source, target))
    return lax.ppermute(value, names if len(names) > 1 else names[0], pairs)


def swapped(value, axis, start):
    pairs = []
    for low in range(start, lax.axis_size(axis) - 1, 2):
        pairs += [(low, low + 1), (low + 1, low)]
    return lax.ppermute(value, axis, pairs)


def local(activations, preact, upstream, master, first_moment, second_moment):
    channels, size_x, size_y, size_z = activations.shape
    devices = math.prod(lax.axis_size(a) for a in AXES)
    share = master.shape[0]
    scale = 1.0 / math.sqrt(size_x * size_y * size_z * devices)
    in_pairs = (
        lax.axis_size("gy") == 2
        and channels % devices == 0
        and share % LANES == 0
        and channels // devices * channels == LANES
        and 2 * size_x * size_y <= LANES
        and (size_x + 2) * size_y <= LANES
    )
    program = pair_program if in_pairs else general_program
    return program(
        activations, preact, upstream, master, first_moment, second_moment, scale
    )


def solution(mesh):
    volume = P(None, "gx", "gy", "gz")
    flat = P(AXES)
    return jax.shard_map(
        local,
        mesh=mesh,
        in_specs=(volume, volume, volume, flat, flat, flat),
        out_specs=(volume, flat, flat, flat, flat),
        check_vma=False,
    )
```

```python
import functools
import math

import jax
import jax.numpy as jnp
from jax import lax
from jax.experimental import pallas as pl
from jax.experimental.pallas import tpu as pltpu
from jax.sharding import PartitionSpec as P

AXES = ("gx", "gy", "gz")
LANES = 128
VMEM = pl.BlockSpec(memory_space=pltpu.VMEM)
HBM = pl.BlockSpec(memory_space=pltpu.HBM)
F32 = jnp.float32
BF16 = jnp.bfloat16
FACES_VMEM = 55_900_000
INNER_VMEM = 54_800_000


def params(limit=24 * 2**20):
    return pltpu.CompilerParams(vmem_limit_bytes=limit)


def cost(flops, moved):
    return pl.CostEstimate(flops=flops, bytes_accessed=moved, transcendentals=0)


def to_planes(value, tile, write, order=(1, 1)):
    channels, size_y, size_z = value.shape
    lines, rows = order
    count = channels // (lines * rows)
    tile[...] = value.astype(F32).reshape(channels * size_y, size_z)
    for y in range(size_y):
        for r in range(rows):
            found = []
            for e in range(lines):
                start = (e * rows + r) * size_y + y
                found.append(tile[pl.ds(start, count, stride=lines * rows * size_y), :])
            at = slice(r * lines * count, (r + 1) * lines * count)
            picked = found[0] if lines == 1 else jnp.concatenate(found, axis=0)
            write(at, y, picked.astype(BF16))


def masked(p, u):
    return jnp.where(p > 0, u, jnp.zeros_like(u))


def choose(condition, out_ref, first_ref, second_ref):
    @pl.when(condition)
    def _():
        out_ref[...] = first_ref[...]

    @pl.when(jnp.logical_not(condition))
    def _():
        out_ref[...] = second_ref[...]


def face_kernel(axis, order, p_ref, u_ref, *refs):
    p_buf, u_buf, tile, sems = refs[-4:]
    out_refs, swap_refs = refs[:2], refs[2:-4]
    size_x, size_z = p_ref.shape[1], p_ref.shape[3]
    copies = []
    for k, x in enumerate((0, size_x - 1)):
        pair = (
            pltpu.make_async_copy(p_ref.at[:, x], p_buf.at[k], sems.at[2 * k]),
            pltpu.make_async_copy(u_ref.at[:, x], u_buf.at[k], sems.at[2 * k + 1]),
        )
        for copy in pair:
            copy.start()
        copies.append(pair)
    for k, out_ref in enumerate(out_refs):
        for copy in copies[k]:
            copy.wait()

        def write(at, y, value):
            out_ref[at, y * size_z : (y + 1) * size_z] = value

        to_planes(masked(p_buf[k], u_buf[k]), tile.at[k], write, order)
    if axis is not None:
        choose(is_odd(axis), swap_refs[0], out_refs[1], out_refs[0])


def faces(preact, upstream, axis=None, order=(1, 1)):
    channels, size_x, size_y, size_z = preact.shape
    face = jax.ShapeDtypeStruct((channels, size_y * size_z), BF16)
    buffer = pltpu.VMEM((2, channels, size_y, size_z), BF16)
    count = 2 if axis is None else 3
    return pl.pallas_call(
        functools.partial(face_kernel, axis, order),
        in_specs=[HBM, HBM],
        out_specs=[VMEM] * count,
        out_shape=[face] * count,
        scratch_shapes=[
            buffer,
            buffer,
            pltpu.VMEM((2, channels * size_y, size_z), F32),
            pltpu.SemaphoreType.DMA((4,)),
        ],
        compiler_params=params(FACES_VMEM),
        cost_estimate=cost(0, 2**20),
        name="faces",
    )(preact, upstream)


def read_inner(order, p_ref, u_ref, g_ref, p_buf, u_buf, tile, sems):
    size_x, size_z = p_ref.shape[1], p_ref.shape[3]
    inner = size_x - 2
    copies = []
    for x in range(inner):
        pair = (
            pltpu.make_async_copy(p_ref.at[:, x + 1], p_buf.at[x], sems.at[x]),
            pltpu.make_async_copy(u_ref.at[:, x + 1], u_buf.at[x], sems.at[inner + x]),
        )
        for copy in pair:
            copy.start()
        copies.append(pair)
    for x in range(inner):
        for copy in copies[x]:
            copy.wait()

        def write(at, y, value):
            g_ref[x, at, y * size_z : (y + 1) * size_z] = value

        to_planes(masked(p_buf[x], u_buf[x]), tile.at[x % 2], write, order)


def inner_kernel(*refs):
    read_inner((1, 1), *refs)


def inner_output(channels, size_x, size_y, size_z):
    return jax.ShapeDtypeStruct((size_x - 2, channels, size_y * size_z), BF16)


def inner_scratch(channels, size_x, size_y, size_z):
    return [
        pltpu.VMEM((size_x - 2, channels, size_y, size_z), BF16),
        pltpu.VMEM((size_x - 2, channels, size_y, size_z), BF16),
        pltpu.VMEM((2, channels * size_y, size_z), F32),
        pltpu.SemaphoreType.DMA((2 * size_x - 4,)),
    ]


def inner_planes(preact, upstream):
    shape = preact.shape
    return pl.pallas_call(
        inner_kernel,
        in_specs=[HBM] * 2,
        out_specs=VMEM,
        out_shape=inner_output(*shape),
        scratch_shapes=inner_scratch(*shape),
        compiler_params=params(INNER_VMEM),
        cost_estimate=cost(0, 4 * 2**20),
        name="inner",
    )(preact, upstream)


def input_kernel(a_ref, x_ref, *refs):
    tile = refs[-1]
    channels, size_x, size_y, size_z = a_ref.shape
    for x in range(size_x):

        def write(at, y, value):
            x_ref[x, at, y * size_z : (y + 1) * size_z] = value

        to_planes(a_ref[:, x], tile.at[x % 2], write)
    if len(refs) > 1:
        low, high = z_tiles([x_ref[x] for x in range(size_x)], size_y, size_z, range(size_x))
        refs[0][...] = (low + pltpu.roll(high, size_x * size_y, 1)).astype(BF16)


def input_planes(activations, with_columns):
    channels, size_x, size_y, size_z = activations.shape
    outs = [jax.ShapeDtypeStruct((size_x, channels, size_y * size_z), BF16)]
    if with_columns:
        outs.append(jax.ShapeDtypeStruct((channels, LANES), BF16))
    return pl.pallas_call(
        input_kernel,
        in_specs=[VMEM],
        out_specs=[VMEM] * len(outs),
        out_shape=outs,
        scratch_shapes=[pltpu.VMEM((2, channels * size_y, size_z), F32)],
        compiler_params=params(),
        cost_estimate=cost(0, 2 * 2**20),
        name="inputs",
    )(activations)


def body_of(refs, index):
    planes = refs[2].shape[0] + 4
    if 2 <= index < planes - 2:
        return refs[2].at[index - 2]
    return refs[{0: 0, 1: 1, planes - 2: 3, planes - 1: 4}[index]]


def y_halo(refs, index):
    me = lax.axis_index("gy")
    low = jnp.where(me > 0, refs[0][index].astype(F32), 0.0)
    high = jnp.where(me < lax.axis_size("gy") - 1, refs[1][index].astype(F32), 0.0)
    return low, high


def z_picker(rows_y, size_z):
    shape = (rows_y * size_z, 2 * LANES)
    voxel = lax.broadcasted_iota(jnp.int32, shape, 0)
    lane = lax.broadcasted_iota(jnp.int32, shape, 1)
    wanted = jnp.where(lane < LANES, lane * size_z, (lane - LANES) * size_z + size_z - 1)
    return (voxel == wanted).astype(F32).astype(BF16)


def z_tiles(planes, rows_y, size_z, numbers):
    channels = planes[0].shape[0]
    columns = jnp.dot(
        jnp.concatenate(planes, axis=0), z_picker(rows_y, size_z), preferred_element_type=F32
    )
    low = jnp.zeros((channels, LANES), F32)
    high = jnp.zeros((channels, LANES), F32)
    for index, number in enumerate(numbers):
        rows = columns[index * channels : (index + 1) * channels]
        low = low + pltpu.roll(rows[:, :LANES], number * rows_y, 1)
        high = high + pltpu.roll(rows[:, LANES:], number * rows_y, 1)
    return low, high


def put_columns(columns, row_of, rows_y, size_z):
    shape = (2 * LANES, rows_y * size_z)
    source = lax.broadcasted_iota(jnp.int32, shape, 0)
    voxel = lax.broadcasted_iota(jnp.int32, shape, 1)
    number = source % LANES
    place = row_of(number) * size_z + jnp.where(source < LANES, 0, size_z - 1)
    place = jnp.where(number < rows_y, place, -1)
    put = (voxel == place).astype(F32).astype(BF16)
    rows = [jnp.concatenate(pair, axis=1) for pair in columns]
    return jnp.dot(
        jnp.concatenate(rows, axis=0).astype(BF16), put, preferred_element_type=F32
    ).astype(BF16)


def z_halo(low_ref, high_ref, planes, rows_y, size_z):
    columns = []
    for index in range(planes):
        shift = -index * rows_y % LANES
        columns.append(
            [pltpu.roll(ref[...].astype(F32), shift, 1) for ref in (low_ref, high_ref)]
        )
    return put_columns(columns, lambda number: number, rows_y, size_z)


def pair_z_halo(odd_ref, even_ref, planes, size_y, size_z):
    me, odd = lax.axis_index("gy"), is_odd("gz")
    sides = []
    for low, high in ((even_ref, odd_ref), (odd_ref, even_ref)):
        first, second = (either(odd, low[k], high[k]) for k in range(2))
        lane = lax.broadcasted_iota(jnp.int32, first.shape, 1)
        own = jnp.where(me == 0, first, second)
        before = jnp.where(me == 0, 0.0, first)
        after = jnp.where(me == 0, second, 0.0)
        columns = []
        for index in range(planes):
            start = index * size_y
            columns.append(
                jnp.where(
                    lane < size_y,
                    pltpu.roll(own, -start % LANES, 1),
                    jnp.where(
                        lane == size_y,
                        pltpu.roll(before, (1 - start) % LANES, 1),
                        pltpu.roll(after, (size_y + 1 - start) % LANES, 1),
                    ),
                )
            )
        sides.append(columns)

    def row_of(number):
        return jnp.where(number < size_y, number + 1, jnp.where(number == size_y, 0, size_y + 1))

    return put_columns(list(zip(*sides)), row_of, size_y + 2, size_z)


def shifted_plane(index, refs, halo, g3):
    channels, plane = refs[0].shape
    size_z = refs[5].shape[-1]
    rows_y = plane // size_z + 2
    base = 3 * channels * index
    lane = lax.broadcasted_iota(jnp.int32, (channels, size_z), 1)
    is_first, is_last = lane == 0, lane == size_z - 1
    low, high = y_halo(refs[5:7], index)
    body = body_of(refs[:5], index)
    for row in range(rows_y):
        cols = slice(row * size_z, (row + 1) * size_z)
        if row == 0:
            value = low.astype(BF16)
        elif row == rows_y - 1:
            value = high.astype(BF16)
        else:
            value = body[:, (row - 1) * size_z : row * size_z]
        if halo is None:
            edge = jnp.zeros_like(value)
        else:
            edge = halo[index * channels : (index + 1) * channels, cols]
        before = jnp.where(is_first, edge, pltpu.roll(value, 1, 1))
        after = jnp.where(is_last, edge, pltpu.roll(value, size_z - 1, 1))
        g3[base : base + channels, cols] = before
        g3[base + channels : base + 2 * channels, cols] = value
        g3[base + 2 * channels : base + 3 * channels, cols] = after


def weight_products(refs, halo, x_ref, g3, x3, acc):
    size_x, channels, plane = x_ref.shape
    size_z = refs[5].shape[-1]
    group = 3 * channels
    zero = jnp.zeros((channels, 2 * size_z), BF16)
    done = 0
    for x in range(size_x):
        while done < x + 3:
            shifted_plane(done, refs, halo, g3)
            done += 1
        value = x_ref[x]
        for b in range(3):
            at = slice(b * channels, (b + 1) * channels)
            start = (2 - b) * size_z
            x3[x, at, start : start + plane] = value
            if start:
                x3[x, at, :start] = zero[:, :start]
            if start < 2 * size_z:
                x3[x, at, start + plane :] = zero[:, start:]
        product = lax.dot_general(
            g3[x * group : (x + 3) * group, :],
            x3[x],
            (((1,), (1,)), ((), ())),
            preferred_element_type=F32,
        )
        if x == 0:
            acc[...] = product
        else:
            acc[...] += product


def to_flat(value, count, channels, flat):
    height, width = value.shape
    wide = value
    if height % LANES:
        wide = jnp.concatenate([wide, jnp.zeros((-height % LANES, width), F32)], axis=0)
    if width % LANES:
        wide = jnp.concatenate([wide, jnp.zeros((wide.shape[0], -width % LANES), F32)], axis=1)
    turned = wide.T
    for b in range(3):
        rows = turned[b * channels : (b + 1) * channels]
        for block in range(9):
            start = block * count
            cell = rows[:, start // LANES * LANES : (start // LANES + 1) * LANES]
            tap = (2 - block // 3) * 9 + b * 3 + 2 - block % 3
            shift = -start % LANES
            flat[pl.ds(tap, channels, stride=27), :] = pltpu.roll(cell, shift, 1) if shift else cell
    return flat[...].T[:count]


def spread_weights(whole, turned, weights):
    channels, taps = whole.shape
    group = 3 * channels
    whole = jnp.concatenate([whole, jnp.zeros((LANES - channels, taps), F32)], axis=0)
    whole = jnp.concatenate([whole, jnp.zeros((LANES, -taps % LANES), F32)], axis=1)
    turned[...] = whole.T
    for b in range(3):
        blocks = []
        for a in range(3):
            for c in range(3):
                tap = (2 - a) * 9 + (2 - b) * 3 + 2 - c
                blocks.append(turned[pl.ds(tap, channels, stride=27), :][:, :channels])
        zero = jnp.zeros((channels, group), F32)
        weights[b, :channels] = jnp.concatenate(blocks + [zero], axis=1).astype(BF16)
        weights[b, channels:] = jnp.concatenate([zero] + blocks, axis=1).astype(BF16)


def input_products(refs, halo, g3, weights, tile, out_ref):
    channels, size_x, size_y, size_z = out_ref.shape
    group = 3 * channels
    plane = size_y * size_z
    done = 0
    for pair in range(size_x // 2):
        while done < 2 * pair + 4:
            shifted_plane(done, refs, halo, g3)
            done += 1
        at = slice(2 * pair * group, (2 * pair + 4) * group)
        total = None
        for b in range(3):
            product = jnp.dot(
                weights[b],
                g3[at, b * size_z : b * size_z + plane],
                preferred_element_type=F32,
            )
            total = product if total is None else total + product
        for half in range(2):
            for y in range(size_y):
                tile[half, pl.ds(y, channels, stride=size_y), :] = total[
                    half * channels : (half + 1) * channels, y * size_z : (y + 1) * size_z
                ]
            out_ref[:, 2 * pair + half] = (
                tile[half].reshape(channels, size_y, size_z).astype(BF16)
            )


def g3_scratch(channels, size_x, size_y, size_z):
    return pltpu.VMEM(((size_x + 2) * 3 * channels, (size_y + 2) * size_z), BF16)


def x3_scratch(channels, size_x, size_y, size_z):
    return pltpu.VMEM((size_x, 3 * channels, (size_y + 2) * size_z), BF16)


def acc_scratch(channels):
    return pltpu.VMEM((9 * channels, 3 * channels), F32)


def flat_scratch(channels):
    return pltpu.VMEM((-(-27 * channels // LANES) * LANES, LANES), F32)


def dgrad_scratch(channels, size_x, size_y, size_z):
    return [
        g3_scratch(channels, size_x, size_y, size_z),
        flat_scratch(channels),
        pltpu.VMEM((3, 2 * channels, 12 * channels), BF16),
        pltpu.VMEM((2, channels * size_y, size_z), F32),
    ]


def wgrad_cost(channels, size_x, size_y, size_z):
    return cost(54 * channels * channels * size_x * (size_y + 2) * size_z, 4 * 2**20)


def dgrad_cost(channels, size_x, size_y, size_z):
    return cost(72 * channels * channels * size_x * size_y * size_z, 4 * 2**20)


def row_for_other(body, size_z):
    plane = body.shape[-1]
    low, high = body[:, :size_z].astype(F32), body[:, plane - size_z :].astype(F32)
    return jnp.where(lax.axis_index("gy") == 0, high, low).astype(BF16)


def pair_inner_kernel(order, *refs):
    first_ref, last_ref, m_ref, g_ref, side_ref, swap_ref, sent_ref = refs[2:9]
    tile, tile_ref, tile_sems = refs[9:]
    size_z = side_ref.shape[-1]
    choose(is_odd("gx"), swap_ref, first_ref, last_ref)
    share = m_ref[...]
    height = tile_ref.shape[0] - share.shape[0]
    if height:
        share = jnp.concatenate([share, jnp.zeros((height, share.shape[1]), F32)], axis=0)
    tile_ref[...] = share.astype(BF16)
    copies = [
        pltpu.make_async_copy(tile_ref, sent_ref.at[device], tile_sems.at[device])
        for device in range(sent_ref.shape[0])
    ]
    for copy in copies:
        copy.start()
    for x in range(g_ref.shape[0]):

        def write(at, y, value):
            g_ref[x, at, y * size_z : (y + 1) * size_z] = value

        to_planes(masked(refs[0][:, x + 1], refs[1][:, x + 1]), tile.at[x % 2], write, order)
    inner, _, plane = g_ref.shape
    size_x = inner + 2
    bodies = [first_ref] + [g_ref.at[x] for x in range(inner)] + [last_ref]
    for x, body in enumerate(bodies):
        side_ref[x] = row_for_other(body, size_z)
    low, high = z_tiles(
        [body[...] for body in bodies], plane // size_z, size_z, range(1, size_x + 1)
    )
    side_ref[size_x] = low.astype(BF16)
    side_ref[size_x + 1] = high.astype(BF16)
    for copy in copies:
        copy.wait()


def pair_inner(preact, upstream, first, last, share, sent_shape, order):
    shape = preact.shape
    channels, size_x, _, size_z = shape
    return pl.pallas_call(
        functools.partial(pair_inner_kernel, order),
        in_specs=[VMEM] * 5,
        out_specs=[VMEM] * 3 + [HBM],
        out_shape=[
            inner_output(*shape),
            jax.ShapeDtypeStruct((size_x + 2, channels, size_z), BF16),
            jax.ShapeDtypeStruct(first.shape, BF16),
            jax.ShapeDtypeStruct(sent_shape, BF16),
        ],
        scratch_shapes=[
            pltpu.VMEM((2, channels * shape[2], size_z), F32),
            pltpu.VMEM(sent_shape[1:], BF16),
            pltpu.SemaphoreType.DMA((sent_shape[0],)),
        ],
        compiler_params=params(),
        cost_estimate=cost(0, 4 * 2**20),
        name="inner",
    )(preact, upstream, first, last, share)


def is_odd(axis):
    return lax.rem(lax.axis_index(axis), 2) == 1


def either(condition, first, second):
    return jnp.where(condition, first.astype(F32), second.astype(F32))


def side_kernel(odd_ref, even_ref, own_ref, sent_ref, xlo_ref, xhi_ref):
    size_x = own_ref.shape[0] - 2
    size_z = own_ref.shape[-1]
    size_y = xlo_ref.shape[-1] // size_z
    odd = is_odd("gx")
    low = either(odd, even_ref[...], odd_ref[...]).astype(BF16)
    high = either(odd, odd_ref[...], even_ref[...]).astype(BF16)
    xlo_ref[...] = low
    xhi_ref[...] = high
    sent_ref[0] = row_for_other(low, size_z)
    for x in range(size_x):
        sent_ref[x + 1] = own_ref[x]
    sent_ref[size_x + 1] = row_for_other(high, size_z)
    lane = lax.broadcasted_iota(jnp.int32, (low.shape[0], LANES), 1)
    first, second = own_ref[size_x], own_ref[size_x + 1]
    for number, plane in ((0, low), (size_x + 1, high)):
        for y in range(size_y):
            at = number * size_y + y
            head = plane[:, y * size_z : y * size_z + LANES]
            tail = plane[:, (y + 1) * size_z - LANES : (y + 1) * size_z]
            first = jnp.where(lane == at, pltpu.roll(head, at, 1), first)
            second = jnp.where(lane == at, pltpu.roll(tail, at + 1, 1), second)
    sent_ref[size_x + 2] = first
    sent_ref[size_x + 3] = second


def side(halves, own):
    plane = jax.ShapeDtypeStruct(halves[0].shape, BF16)
    return pl.pallas_call(
        side_kernel,
        in_specs=[VMEM] * 3,
        out_specs=[VMEM] * 3,
        out_shape=[
            jax.ShapeDtypeStruct((own.shape[0] + 2, *own.shape[1:]), BF16),
            plane,
            plane,
        ],
        compiler_params=params(),
        cost_estimate=cost(2**25, 2**19),
        name="side",
    )(*halves, own)


def own_columns(columns, number, area):
    me = lax.axis_index("gy")
    value = columns.astype(F32)
    lane = lax.broadcasted_iota(jnp.int32, value.shape, 1)
    first = pltpu.roll(value, -number * area % LANES, 1)
    second = pltpu.roll(value, (1 - number) * area % LANES, 1)
    first = jnp.where(lane < area, first, 0.0)
    second = jnp.where((lane >= area) & (lane < 2 * area), second, 0.0)
    return jnp.where(me == 0, first, second)


def join_kernel(area, own_ref, other_ref, columns_ref, even_ref, odd_ref):
    at = own_ref.shape[0] - 2
    me = lax.axis_index("gy")
    last = own_columns(columns_ref[...], 1, area).astype(BF16)

    def fill(up_ref, down_ref):
        for k, out_ref in enumerate((down_ref, up_ref)):
            out_ref[me] = own_ref[at + k]
            out_ref[1 - me] = other_ref[at + k]
        up_ref[2] = last
        down_ref[2] = last

    odd = is_odd("gz")

    @pl.when(odd)
    def _():
        fill(odd_ref, even_ref)

    @pl.when(jnp.logical_not(odd))
    def _():
        fill(even_ref, odd_ref)


def join(own, other, columns, area):
    return pl.pallas_call(
        functools.partial(join_kernel, area),
        in_specs=[VMEM] * 3,
        out_specs=[VMEM] * 2,
        out_shape=[jax.ShapeDtypeStruct((3, *own.shape[1:]), BF16)] * 2,
        compiler_params=params(),
        cost_estimate=cost(0, 2**17),
        name="join",
    )(own, other, columns)


def pair_wgrad_kernel(*refs):
    x_ref, acc_ref, g3, x3 = refs[7:]
    weight_products(refs, None, x_ref, g3, x3, acc_ref)


def pair_wgrad(sources, planes_x, shape):
    channels = shape[0]
    return pl.pallas_call(
        pair_wgrad_kernel,
        in_specs=[VMEM] * 8,
        out_specs=VMEM,
        out_shape=jax.ShapeDtypeStruct((9 * channels, 3 * channels), F32),
        scratch_shapes=[g3_scratch(*shape), x3_scratch(*shape)],
        compiler_params=params(32 * 2**20),
        cost_estimate=wgrad_cost(*shape),
        name="wgrad",
    )(*sources, planes_x)


def finish_kernel(scale, rows, sizes, *refs):
    acc_ref, columns_ref, even_ref, odd_ref, from_odd_ref, from_even_ref = refs[:6]
    part_ref, chunks = refs[6:]
    size_x, size_y = sizes
    channels = columns_ref.shape[0]
    area = size_x * size_y
    odd = is_odd("gz")
    lane = lax.broadcasted_iota(jnp.int32, (channels, LANES), 1)
    row = lane % size_y
    jump = area - size_y + 1
    below = [either(odd, from_even_ref[k], from_odd_ref[k]) for k in range(3)]
    own = [either(odd, even_ref[k], odd_ref[k]) for k in range(2)]
    pairs = ((below[:2], own_columns(columns_ref[...], 0, area)), (own, below[2]))
    edges = []
    for tiles, value in pairs:
        before = jnp.where(lane >= area, pltpu.roll(value, jump, 1), 0.0)
        after = jnp.where(lane < area, pltpu.roll(value, LANES - jump, 1), 0.0)
        right = jnp.concatenate(
            [
                jnp.where(row > 0, pltpu.roll(value, 1, 1), before),
                value,
                jnp.where(row < size_y - 1, pltpu.roll(value, LANES - 1, 1), after),
            ],
            axis=0,
        )
        left = []
        for a in range(3):
            first = pltpu.roll(tiles[0], -a * size_y % LANES, 1)
            second = pltpu.roll(tiles[1], (area - a * size_y) % LANES, 1)
            left.append(jnp.where(lane < area, first, jnp.where(lane < 2 * area, second, 0.0)))
        edges.append(
            lax.dot_general(
                jnp.concatenate(left, axis=0).astype(BF16),
                right.astype(BF16),
                (((1,), (1,)), ((), ())),
                preferred_element_type=F32,
            )
        )
    count, height, width = part_ref.shape
    chunks[...] = jnp.zeros_like(chunks)
    pieces = rows * acc_ref.shape[1] // width
    for a in range(3):
        for c in range(3):
            at = 3 * a + c
            block = acc_ref[at * channels : (at + 1) * channels, :]
            if c != 1:
                block = block + edges[c // 2][a * channels : (a + 1) * channels]
            block = block * scale
            line = jnp.concatenate(
                [block[r * count : (r + 1) * count] for r in range(rows)], axis=1
            )
            for k in range(pieces):
                chunks[pl.ds(at * pieces + k, count, stride=height), :] = line[
                    :, k * width : (k + 1) * width
                ]
    part_ref[...] = chunks[...].reshape(part_ref.shape).astype(BF16)


def finish(acc, columns, sent, received, scale, rows, sizes, part_shape):
    channels = columns.shape[0]
    return pl.pallas_call(
        functools.partial(finish_kernel, scale, rows, sizes),
        in_specs=[VMEM] * 6,
        out_specs=VMEM,
        out_shape=jax.ShapeDtypeStruct(part_shape, BF16),
        scratch_shapes=[pltpu.VMEM((part_shape[0] * part_shape[1], part_shape[2]), F32)],
        compiler_params=params(),
        cost_estimate=cost(2**27, 2**21),
        name="finish",
    )(acc, columns, *sent, *received)


def adam_step(master, first, second, weight_grad):
    new_first = 0.9 * first + 0.1 * weight_grad
    new_second = 0.999 * second + 0.001 * weight_grad * weight_grad
    corr_first = 1.0 - (0.9**10) ** 10
    corr_second = 1.0 - (0.999**10) ** 10
    update = new_first / corr_first / (jnp.sqrt(new_second / corr_second) + 1e-08) + 0.01 * master
    return master - 0.05 * update, new_first, new_second


def in_flat_order(value, rows, places, spread_rows):
    taps = 27
    lane = lax.broadcasted_iota(jnp.int32, (9, LANES), 1)
    rows[: value.shape[0], :] = value
    thirds = [rows[pl.ds(k, 9, stride=3), :] for k in range(3)]
    half = LANES // 2
    by_y = (
        jnp.where(lane < half, thirds[0], thirds[1]),
        jnp.where(lane < half, pltpu.roll(thirds[0], half, 1), pltpu.roll(thirds[2], half, 1)),
        jnp.where(lane < half, thirds[1], thirds[2]),
    )
    places[...] = jnp.zeros_like(places)
    for b in range(3):
        spread_rows[b, :9, :] = by_y[b]
        for block in range(9):
            tap = (2 - block // 3) * 9 + b * 3 + 2 - block % 3
            places[tap : tap + 1, :] = spread_rows[b, block : block + 1, :]
    line = places[...].T
    number = lax.broadcasted_iota(jnp.int32, (LANES, LANES), 0) * taps
    column = lax.broadcasted_iota(jnp.int32, (LANES, LANES), 1)
    for bit in range(7):
        turn = 1 << bit
        line = jnp.where((number & turn) != 0, pltpu.roll(line, turn, 1), line)
    start = number & (LANES - 1)
    line = jnp.concatenate(
        [jnp.where(column >= start, line, 0.0), jnp.where(column < start, line, 0.0)], axis=0
    )
    target = lax.broadcasted_iota(jnp.int32, (32, 2 * LANES), 0)
    source = lax.broadcasted_iota(jnp.int32, (32, 2 * LANES), 1)
    goes = lax.shift_right_logical((source & (LANES - 1)) * taps, 7)
    goes = goes + jnp.where(source < LANES, 0, 1)
    pick = jnp.where(goes == target, 1.0, 0.0).astype(BF16)
    parts = []
    for _ in range(3):
        parts.append(line.astype(BF16))
        line = line - parts[-1].astype(F32)
    return jnp.dot(
        jnp.concatenate([pick] * 3, axis=1),
        jnp.concatenate(parts, axis=0),
        preferred_element_type=F32,
    )[:taps]


def adam_kernel(parts_ref, master_ref, first_ref, second_ref, *refs):
    out_refs, scratch = refs[:4], refs[4:]
    total = parts_ref[0].astype(F32)
    for source in range(1, parts_ref.shape[0]):
        total = total + parts_ref[source].astype(F32)
    weight_grad = in_flat_order(total, *scratch)
    results = adam_step(master_ref[...], first_ref[...], second_ref[...], weight_grad)
    for out_ref, result in zip(out_refs, (weight_grad, *results)):
        out_ref[...] = result


def adam(parts, *states):
    share = states[0].shape[0]
    tiled = [state.reshape(share // LANES, LANES) for state in states]
    result = jax.ShapeDtypeStruct(tiled[0].shape, F32)
    outs = pl.pallas_call(
        adam_kernel,
        in_specs=[VMEM] * 4,
        out_specs=[VMEM] * 4,
        out_shape=[result] * 4,
        scratch_shapes=[
            pltpu.VMEM(parts.shape[1:], F32),
            pltpu.VMEM((LANES, LANES), F32),
            pltpu.VMEM((3, 16, LANES), F32),
        ],
        compiler_params=params(),
        cost_estimate=cost(2**22, 2**19),
        name="adam",
    )(parts, *tiled)
    return tuple(out.reshape(share) for out in outs)


def spread_kernel(rows, w_ref, weights_ref, turned, chunks):
    count, height, width = w_ref.shape
    taps = 27 * rows * count
    chunks[...] = w_ref[...].astype(F32).reshape(chunks.shape)
    line = jnp.concatenate(
        [chunks[pl.ds(k, count, stride=height), :] for k in range(rows * taps // width)], axis=1
    )
    whole = jnp.concatenate([line[:, r * taps : (r + 1) * taps] for r in range(rows)], axis=0)
    spread_weights(whole, turned, weights_ref)


def spread(kernel, channels, rows):
    return pl.pallas_call(
        functools.partial(spread_kernel, rows),
        in_specs=[VMEM],
        out_specs=VMEM,
        out_shape=jax.ShapeDtypeStruct((3, 2 * channels, 12 * channels), BF16),
        scratch_shapes=[
            flat_scratch(channels),
            pltpu.VMEM((kernel.shape[0] * kernel.shape[1], kernel.shape[2]), F32),
        ],
        compiler_params=params(),
        cost_estimate=cost(2**20, 2**21),
        name="spread",
    )(kernel)


def pair_dgrad_kernel(*refs):
    weights_ref, out_ref, g3, tile = refs[9:]
    _, size_x, size_y, size_z = out_ref.shape
    halo = pair_z_halo(refs[7], refs[8], size_x + 2, size_y, size_z)
    input_products(refs, halo, g3, weights_ref, tile, out_ref)


def pair_dgrad(sources, weights, shape):
    channels, _, size_y, size_z = shape
    return pl.pallas_call(
        pair_dgrad_kernel,
        in_specs=[VMEM] * 10,
        out_specs=VMEM,
        out_shape=jax.ShapeDtypeStruct(shape, BF16),
        scratch_shapes=[g3_scratch(*shape), pltpu.VMEM((2, channels * size_y, size_z), F32)],
        compiler_params=params(32 * 2**20),
        cost_estimate=dgrad_cost(*shape),
        name="dgrad",
    )(*sources, weights)


def pair_program(activations, preact, upstream, master, first_moment, second_moment, scale):
    shape = activations.shape
    channels, size_x, size_y, _ = shape
    devices = math.prod(lax.axis_size(a) for a in AXES)
    rows = channels // devices
    used = master.shape[0] // LANES
    block = (devices, -(-used // 16) * 16, LANES)
    order = (lax.axis_size("gz"), rows)
    partners = ("gz", "gx", "gy")
    first, last, odd_sent = faces(preact, upstream, "gx", order)
    odd_halves = swapped(odd_sent, "gx", 1)
    inner, own, even_sent, sent = pair_inner(
        preact, upstream, first, last, master.reshape(used, LANES), block, order
    )
    even_halves = swapped(even_sent, "gx", 0)
    kernel = lax.all_to_all(sent, partners, 0, 0, tiled=True)
    own, xlo, xhi = side((odd_halves, even_halves), own)
    planes = (xlo, first, inner, last, xhi)
    own, activations = lax.optimization_barrier((own, activations))
    other = shifted(own, {"gy": "swap"})
    planes_x, columns = input_planes(activations, True)
    z_sent = join(own, other, columns, size_x * size_y)
    from_odd = swapped(z_sent[1], "gz", 1)
    from_even = swapped(z_sent[0], "gz", 0)
    sources = (*planes, other, other)
    acc = pair_wgrad(sources, planes_x, shape)
    z_received = (from_odd, from_even)
    part = finish(acc, columns, z_sent, z_received, scale, rows, (size_x, size_y), block)
    part, kernel = lax.optimization_barrier((part, kernel))
    parts = lax.all_to_all(part, partners, 0, 0, tiled=True)
    weights = spread(kernel, channels, rows)
    grad_input = pair_dgrad((*sources, *z_received), weights, shape)
    return grad_input, *adam(parts, master, first_moment, second_moment)


def yface_kernel(*refs):
    low_ref, high_ref = refs[5:]
    size_z = low_ref.shape[-1]
    for index in range(low_ref.shape[0]):
        body = body_of(refs[:5], index)
        plane = body.shape[-1]
        low_ref[index] = body[:, :size_z]
        high_ref[index] = body[:, plane - size_z :]


def y_faces(planes, size_z):
    inner, channels, _ = planes[2].shape
    face = jax.ShapeDtypeStruct((inner + 4, channels, size_z), BF16)
    return pl.pallas_call(
        yface_kernel,
        in_specs=[VMEM] * 5,
        out_specs=[VMEM] * 2,
        out_shape=[face] * 2,
        compiler_params=params(),
        cost_estimate=cost(0, 2**19),
        name="yfaces",
    )(*planes)


def zface_kernel(*refs):
    zlo_ref, zhi_ref = refs[7:]
    size_z = refs[5].shape[-1]
    whole = []
    for index in range(refs[5].shape[0]):
        low, high = y_halo(refs[5:7], index)
        body = body_of(refs[:5], index)[...]
        whole.append(jnp.concatenate([low.astype(BF16), body, high.astype(BF16)], axis=1))
    low, high = z_tiles(whole, whole[0].shape[1] // size_z, size_z, range(len(whole)))
    zlo_ref[...] = low.astype(BF16)
    zhi_ref[...] = high.astype(BF16)


def z_faces(planes, y_halos):
    face = jax.ShapeDtypeStruct((planes[0].shape[0], LANES), BF16)
    return pl.pallas_call(
        zface_kernel,
        in_specs=[VMEM] * 7,
        out_specs=[VMEM] * 2,
        out_shape=[face, face],
        compiler_params=params(),
        cost_estimate=cost(2**27, 2**21),
        name="zfaces",
    )(*planes, *y_halos)


def wgrad_kernel(scale, *refs):
    x_ref, part_ref, g3, x3, acc, flat = refs[9:]
    size_x, channels, plane = x_ref.shape
    size_z = refs[5].shape[-1]
    halo = z_halo(refs[7], refs[8], size_x + 2, plane // size_z + 2, size_z)
    weight_products(refs, halo, x_ref, g3, x3, acc)
    whole = to_flat(acc[...] * scale, channels, channels, flat)
    part_ref[...] = whole[:, : part_ref.shape[1]].astype(BF16)


def wgrad(sources, planes_x, shape, scale):
    channels = shape[0]
    return pl.pallas_call(
        functools.partial(wgrad_kernel, scale),
        in_specs=[VMEM] * 10,
        out_specs=VMEM,
        out_shape=jax.ShapeDtypeStruct((channels, 27 * channels), BF16),
        scratch_shapes=[
            g3_scratch(*shape),
            x3_scratch(*shape),
            acc_scratch(channels),
            flat_scratch(channels),
        ],
        compiler_params=params(32 * 2**20),
        cost_estimate=wgrad_cost(*shape),
        name="wgrad",
    )(*sources, planes_x)


def dgrad_kernel(*refs):
    w_ref, out_ref, g3, turned, weights, tile = refs[9:]
    _, size_x, size_y, size_z = out_ref.shape
    spread_weights(w_ref[...].astype(F32), turned, weights)
    halo = z_halo(refs[7], refs[8], size_x + 2, size_y + 2, size_z)
    input_products(refs, halo, g3, weights, tile, out_ref)


def dgrad(sources, kernel, shape):
    return pl.pallas_call(
        dgrad_kernel,
        in_specs=[VMEM] * 10,
        out_specs=VMEM,
        out_shape=jax.ShapeDtypeStruct(shape, BF16),
        scratch_shapes=dgrad_scratch(*shape),
        compiler_params=params(32 * 2**20),
        cost_estimate=dgrad_cost(*shape),
        name="dgrad",
    )(*sources, kernel)


def general_program(activations, preact, upstream, master, first_moment, second_moment, scale):
    shape = activations.shape
    channels, _, _, size_z = shape
    devices = math.prod(lax.axis_size(a) for a in AXES)
    share = master.shape[0]
    first, last = faces(preact, upstream)
    x_halos = (shifted(last, {"gx": 1}), shifted(first, {"gx": -1}))
    inner = inner_planes(preact, upstream)
    (planes_x,) = input_planes(activations, False)
    sent = jnp.broadcast_to(master.astype(BF16).reshape(1, 1, share), (devices, 1, share))
    kernel = lax.all_to_all(sent, AXES, 0, 0, tiled=True).reshape(channels, 27 * channels)
    planes = (x_halos[0], first, inner, last, x_halos[1])
    y_sent = y_faces(planes, size_z)
    y_halos = (shifted(y_sent[1], {"gy": 1}), shifted(y_sent[0], {"gy": -1}))
    zlo, zhi = z_faces(planes, y_halos)
    z_halos = (shifted(zhi, {"gz": 1}), shifted(zlo, {"gz": -1}))
    sources = (*planes, *y_halos, *z_halos)
    part = wgrad(sources, planes_x, shape, scale)
    part, kernel = lax.optimization_barrier((part, kernel))
    parts = lax.all_to_all(part.reshape(devices, 1, share), AXES, 0, 0, tiled=True)
    grad_input = dgrad(sources, kernel, shape)
    weight_grad = jnp.sum(parts.astype(F32), axis=0).reshape(-1)
    results = adam_step(master, first_moment, second_moment, weight_grad)
    return grad_input, weight_grad, *results


def shifted(value, moves):
    names = tuple(moves)
    sizes = [lax.axis_size(name) for name in names]
    pairs = []
    for source in range(math.prod(sizes)):
        rest, coords = source, []
        for size in reversed(sizes):
            coords.insert(0, rest % size)
            rest //= size
        coords = [
            (at + moves[name]) if moves[name] != "swap" else 1 - at
            for at, name in zip(coords, names)
        ]
        if all(0 <= at < size for at, size in zip(coords, sizes)):
            target = 0
            for at, size in zip(coords, sizes):
                target = target * size + at
            pairs.append((source, target))
    return lax.ppermute(value, names if len(names) > 1 else names[0], pairs)


def swapped(value, axis, start):
    pairs = []
    for low in range(start, lax.axis_size(axis) - 1, 2):
        pairs += [(low, low + 1), (low + 1, low)]
    return lax.ppermute(value, axis, pairs)


def local(activations, preact, upstream, master, first_moment, second_moment):
    channels, size_x, size_y, size_z = activations.shape
    devices = math.prod(lax.axis_size(a) for a in AXES)
    share = master.shape[0]
    scale = 1.0 / math.sqrt(size_x * size_y * size_z * devices)
    in_pairs = (
        lax.axis_size("gy") == 2
        and channels % devices == 0
        and share % LANES == 0
        and channels // devices * channels == LANES
        and 2 * size_x * size_y <= LANES
        and (size_x + 2) * size_y <= LANES
    )
    program = pair_program if in_pairs else general_program
    return program(
        activations, preact, upstream, master, first_moment, second_moment, scale
    )


def solution(mesh):
    volume = P(None, "gx", "gy", "gz")
    flat = P(AXES)
    return jax.shard_map(
        local,
        mesh=mesh,
        in_specs=(volume, volume, volume, flat, flat, flat),
        out_specs=(volume, flat, flat, flat, flat),
        check_vma=False,
    )
```

```python
import functools
import math

import jax
import jax.numpy as jnp
from jax import lax
from jax.experimental import pallas as pl
from jax.experimental.pallas import tpu as pltpu
from jax.sharding import PartitionSpec as P

AXES = ("gx", "gy", "gz")
LANES = 128
VMEM = pl.BlockSpec(memory_space=pltpu.VMEM)
HBM = pl.BlockSpec(memory_space=pltpu.HBM)
F32 = jnp.float32
BF16 = jnp.bfloat16
FACES_VMEM = 55_900_000
INNER_VMEM = 54_800_000


def params(limit=24 * 2**20):
    return pltpu.CompilerParams(vmem_limit_bytes=limit)


def cost(flops, moved):
    return pl.CostEstimate(flops=flops, bytes_accessed=moved, transcendentals=0)


def to_planes(value, tile, write, rows=1):
    channels, size_y, size_z = value.shape
    count = channels // rows
    tile[...] = value.astype(F32).reshape(channels * size_y, size_z)
    for y in range(size_y):
        for r in range(rows):
            picked = tile[pl.ds(r * size_y + y, count, stride=rows * size_y), :]
            write(slice(r * count, (r + 1) * count), y, picked.astype(BF16))


def masked(p, u):
    return jnp.where(p > 0, u, jnp.zeros_like(u))


def choose(condition, out_ref, first_ref, second_ref):
    @pl.when(condition)
    def _():
        out_ref[...] = first_ref[...]

    @pl.when(jnp.logical_not(condition))
    def _():
        out_ref[...] = second_ref[...]


def face_kernel(axis, rows, p_ref, u_ref, *refs):
    p_buf, u_buf, tile, sems = refs[-4:]
    out_refs, swap_refs = refs[:2], refs[2:-4]
    size_x, size_z = p_ref.shape[1], p_ref.shape[3]
    copies = []
    for k, x in enumerate((0, size_x - 1)):
        pair = (
            pltpu.make_async_copy(p_ref.at[:, x], p_buf.at[k], sems.at[2 * k]),
            pltpu.make_async_copy(u_ref.at[:, x], u_buf.at[k], sems.at[2 * k + 1]),
        )
        for copy in pair:
            copy.start()
        copies.append(pair)
    for k, out_ref in enumerate(out_refs):
        for copy in copies[k]:
            copy.wait()

        def write(at, y, value):
            out_ref[at, y * size_z : (y + 1) * size_z] = value

        to_planes(masked(p_buf[k], u_buf[k]), tile.at[k], write, rows)
    if axis is not None:
        choose(is_odd(axis), swap_refs[0], out_refs[1], out_refs[0])


def faces(preact, upstream, axis=None, rows=1):
    channels, size_x, size_y, size_z = preact.shape
    face = jax.ShapeDtypeStruct((channels, size_y * size_z), BF16)
    buffer = pltpu.VMEM((2, channels, size_y, size_z), BF16)
    count = 2 if axis is None else 3
    return pl.pallas_call(
        functools.partial(face_kernel, axis, rows),
        in_specs=[HBM, HBM],
        out_specs=[VMEM] * count,
        out_shape=[face] * count,
        scratch_shapes=[
            buffer,
            buffer,
            pltpu.VMEM((2, channels * size_y, size_z), F32),
            pltpu.SemaphoreType.DMA((4,)),
        ],
        compiler_params=params(FACES_VMEM),
        cost_estimate=cost(0, 2**20),
        name="faces",
    )(preact, upstream)


def read_inner(rows, p_ref, u_ref, g_ref, p_buf, u_buf, tile, sems):
    size_x, size_z = p_ref.shape[1], p_ref.shape[3]
    inner = size_x - 2
    copies = []
    for x in range(inner):
        pair = (
            pltpu.make_async_copy(p_ref.at[:, x + 1], p_buf.at[x], sems.at[x]),
            pltpu.make_async_copy(u_ref.at[:, x + 1], u_buf.at[x], sems.at[inner + x]),
        )
        for copy in pair:
            copy.start()
        copies.append(pair)
    for x in range(inner):
        for copy in copies[x]:
            copy.wait()

        def write(at, y, value):
            g_ref[x, at, y * size_z : (y + 1) * size_z] = value

        to_planes(masked(p_buf[x], u_buf[x]), tile.at[x % 2], write, rows)


def inner_kernel(*refs):
    read_inner(1, *refs)


def inner_output(channels, size_x, size_y, size_z):
    return jax.ShapeDtypeStruct((size_x - 2, channels, size_y * size_z), BF16)


def inner_scratch(channels, size_x, size_y, size_z):
    return [
        pltpu.VMEM((size_x - 2, channels, size_y, size_z), BF16),
        pltpu.VMEM((size_x - 2, channels, size_y, size_z), BF16),
        pltpu.VMEM((2, channels * size_y, size_z), F32),
        pltpu.SemaphoreType.DMA((2 * size_x - 4,)),
    ]


def inner_planes(preact, upstream):
    shape = preact.shape
    return pl.pallas_call(
        inner_kernel,
        in_specs=[HBM] * 2,
        out_specs=VMEM,
        out_shape=inner_output(*shape),
        scratch_shapes=inner_scratch(*shape),
        compiler_params=params(INNER_VMEM),
        cost_estimate=cost(0, 4 * 2**20),
        name="inner",
    )(preact, upstream)


def input_kernel(a_ref, x_ref, *refs):
    tile = refs[-1]
    channels, size_x, size_y, size_z = a_ref.shape
    for x in range(size_x):

        def write(at, y, value):
            x_ref[x, at, y * size_z : (y + 1) * size_z] = value

        to_planes(a_ref[:, x], tile.at[x % 2], write)
    if len(refs) > 1:
        low, high = z_tiles([x_ref[x] for x in range(size_x)], size_y, size_z, range(size_x))
        refs[0][...] = (low + pltpu.roll(high, size_x * size_y, 1)).astype(BF16)


def input_planes(activations, with_columns):
    channels, size_x, size_y, size_z = activations.shape
    outs = [jax.ShapeDtypeStruct((size_x, channels, size_y * size_z), BF16)]
    if with_columns:
        outs.append(jax.ShapeDtypeStruct((channels, LANES), BF16))
    return pl.pallas_call(
        input_kernel,
        in_specs=[VMEM],
        out_specs=[VMEM] * len(outs),
        out_shape=outs,
        scratch_shapes=[pltpu.VMEM((2, channels * size_y, size_z), F32)],
        compiler_params=params(),
        cost_estimate=cost(0, 2 * 2**20),
        name="inputs",
    )(activations)


def body_of(refs, index):
    planes = refs[2].shape[0] + 4
    if 2 <= index < planes - 2:
        return refs[2].at[index - 2]
    return refs[{0: 0, 1: 1, planes - 2: 3, planes - 1: 4}[index]]


def y_halo(refs, index):
    me = lax.axis_index("gy")
    low = jnp.where(me > 0, refs[0][index].astype(F32), 0.0)
    high = jnp.where(me < lax.axis_size("gy") - 1, refs[1][index].astype(F32), 0.0)
    return low, high


def z_picker(rows_y, size_z):
    shape = (rows_y * size_z, 2 * LANES)
    voxel = lax.broadcasted_iota(jnp.int32, shape, 0)
    lane = lax.broadcasted_iota(jnp.int32, shape, 1)
    wanted = jnp.where(lane < LANES, lane * size_z, (lane - LANES) * size_z + size_z - 1)
    return (voxel == wanted).astype(F32).astype(BF16)


def z_tiles(planes, rows_y, size_z, numbers):
    channels = planes[0].shape[0]
    columns = jnp.dot(
        jnp.concatenate(planes, axis=0), z_picker(rows_y, size_z), preferred_element_type=F32
    )
    low = jnp.zeros((channels, LANES), F32)
    high = jnp.zeros((channels, LANES), F32)
    for index, number in enumerate(numbers):
        rows = columns[index * channels : (index + 1) * channels]
        low = low + pltpu.roll(rows[:, :LANES], number * rows_y, 1)
        high = high + pltpu.roll(rows[:, LANES:], number * rows_y, 1)
    return low, high


def put_columns(columns, row_of, rows_y, size_z):
    shape = (2 * LANES, rows_y * size_z)
    source = lax.broadcasted_iota(jnp.int32, shape, 0)
    voxel = lax.broadcasted_iota(jnp.int32, shape, 1)
    number = source % LANES
    place = row_of(number) * size_z + jnp.where(source < LANES, 0, size_z - 1)
    place = jnp.where(number < rows_y, place, -1)
    put = (voxel == place).astype(F32).astype(BF16)
    rows = [jnp.concatenate(pair, axis=1) for pair in columns]
    return jnp.dot(
        jnp.concatenate(rows, axis=0).astype(BF16), put, preferred_element_type=F32
    ).astype(BF16)


def z_halo(low_ref, high_ref, planes, rows_y, size_z):
    columns = []
    for index in range(planes):
        shift = -index * rows_y % LANES
        columns.append(
            [pltpu.roll(ref[...].astype(F32), shift, 1) for ref in (low_ref, high_ref)]
        )
    return put_columns(columns, lambda number: number, rows_y, size_z)


def pair_z_halo(odd_ref, even_ref, planes, size_y, size_z):
    me, odd = lax.axis_index("gy"), is_odd("gz")
    sides = []
    for low, high in ((even_ref, odd_ref), (odd_ref, even_ref)):
        first, second = (either(odd, low[k], high[k]) for k in range(2))
        lane = lax.broadcasted_iota(jnp.int32, first.shape, 1)
        own = jnp.where(me == 0, first, second)
        before = jnp.where(me == 0, 0.0, first)
        after = jnp.where(me == 0, second, 0.0)
        columns = []
        for index in range(planes):
            start = index * size_y
            columns.append(
                jnp.where(
                    lane < size_y,
                    pltpu.roll(own, -start % LANES, 1),
                    jnp.where(
                        lane == size_y,
                        pltpu.roll(before, (1 - start) % LANES, 1),
                        pltpu.roll(after, (size_y + 1 - start) % LANES, 1),
                    ),
                )
            )
        sides.append(columns)

    def row_of(number):
        return jnp.where(number < size_y, number + 1, jnp.where(number == size_y, 0, size_y + 1))

    return put_columns(list(zip(*sides)), row_of, size_y + 2, size_z)


def shifted_plane(index, refs, halo, g3):
    channels, plane = refs[0].shape
    size_z = refs[5].shape[-1]
    rows_y = plane // size_z + 2
    base = 3 * channels * index
    lane = lax.broadcasted_iota(jnp.int32, (channels, size_z), 1)
    is_first, is_last = lane == 0, lane == size_z - 1
    low, high = y_halo(refs[5:7], index)
    body = body_of(refs[:5], index)
    for row in range(rows_y):
        cols = slice(row * size_z, (row + 1) * size_z)
        if row == 0:
            value = low.astype(BF16)
        elif row == rows_y - 1:
            value = high.astype(BF16)
        else:
            value = body[:, (row - 1) * size_z : row * size_z]
        if halo is None:
            edge = jnp.zeros_like(value)
        else:
            edge = halo[index * channels : (index + 1) * channels, cols]
        before = jnp.where(is_first, edge, pltpu.roll(value, 1, 1))
        after = jnp.where(is_last, edge, pltpu.roll(value, size_z - 1, 1))
        g3[base : base + channels, cols] = before
        g3[base + channels : base + 2 * channels, cols] = value
        g3[base + 2 * channels : base + 3 * channels, cols] = after


def weight_products(refs, halo, x_ref, g3, x3, acc):
    size_x, channels, plane = x_ref.shape
    size_z = refs[5].shape[-1]
    group = 3 * channels
    zero = jnp.zeros((channels, 2 * size_z), BF16)
    done = 0
    for x in range(size_x):
        while done < x + 3:
            shifted_plane(done, refs, halo, g3)
            done += 1
        value = x_ref[x]
        for b in range(3):
            at = slice(b * channels, (b + 1) * channels)
            start = (2 - b) * size_z
            x3[x, at, start : start + plane] = value
            if start:
                x3[x, at, :start] = zero[:, :start]
            if start < 2 * size_z:
                x3[x, at, start + plane :] = zero[:, start:]
        product = lax.dot_general(
            g3[x * group : (x + 3) * group, :],
            x3[x],
            (((1,), (1,)), ((), ())),
            preferred_element_type=F32,
        )
        if x == 0:
            acc[...] = product
        else:
            acc[...] += product


def to_flat(value, count, channels, flat):
    height, width = value.shape
    wide = value
    if height % LANES:
        wide = jnp.concatenate([wide, jnp.zeros((-height % LANES, width), F32)], axis=0)
    if width % LANES:
        wide = jnp.concatenate([wide, jnp.zeros((wide.shape[0], -width % LANES), F32)], axis=1)
    turned = wide.T
    for b in range(3):
        rows = turned[b * channels : (b + 1) * channels]
        for block in range(9):
            start = block * count
            cell = rows[:, start // LANES * LANES : (start // LANES + 1) * LANES]
            tap = (2 - block // 3) * 9 + b * 3 + 2 - block % 3
            shift = -start % LANES
            flat[pl.ds(tap, channels, stride=27), :] = pltpu.roll(cell, shift, 1) if shift else cell
    return flat[...].T[:count]


def spread_weights(whole, turned, weights):
    channels, taps = whole.shape
    group = 3 * channels
    whole = jnp.concatenate([whole, jnp.zeros((LANES - channels, taps), F32)], axis=0)
    whole = jnp.concatenate([whole, jnp.zeros((LANES, -taps % LANES), F32)], axis=1)
    turned[...] = whole.T
    for b in range(3):
        blocks = []
        for a in range(3):
            for c in range(3):
                tap = (2 - a) * 9 + (2 - b) * 3 + 2 - c
                blocks.append(turned[pl.ds(tap, channels, stride=27), :][:, :channels])
        zero = jnp.zeros((channels, group), F32)
        weights[b, :channels] = jnp.concatenate(blocks + [zero], axis=1).astype(BF16)
        weights[b, channels:] = jnp.concatenate([zero] + blocks, axis=1).astype(BF16)


def input_products(refs, halo, g3, weights, tile, out_ref):
    channels, size_x, size_y, size_z = out_ref.shape
    group = 3 * channels
    plane = size_y * size_z
    done = 0
    for pair in range(size_x // 2):
        while done < 2 * pair + 4:
            shifted_plane(done, refs, halo, g3)
            done += 1
        at = slice(2 * pair * group, (2 * pair + 4) * group)
        total = None
        for b in range(3):
            product = jnp.dot(
                weights[b],
                g3[at, b * size_z : b * size_z + plane],
                preferred_element_type=F32,
            )
            total = product if total is None else total + product
        for half in range(2):
            for y in range(size_y):
                tile[half, pl.ds(y, channels, stride=size_y), :] = total[
                    half * channels : (half + 1) * channels, y * size_z : (y + 1) * size_z
                ]
            out_ref[:, 2 * pair + half] = (
                tile[half].reshape(channels, size_y, size_z).astype(BF16)
            )


def g3_scratch(channels, size_x, size_y, size_z):
    return pltpu.VMEM(((size_x + 2) * 3 * channels, (size_y + 2) * size_z), BF16)


def x3_scratch(channels, size_x, size_y, size_z):
    return pltpu.VMEM((size_x, 3 * channels, (size_y + 2) * size_z), BF16)


def acc_scratch(channels):
    return pltpu.VMEM((9 * channels, 3 * channels), F32)


def flat_scratch(channels):
    return pltpu.VMEM((-(-27 * channels // LANES) * LANES, LANES), F32)


def dgrad_scratch(channels, size_x, size_y, size_z):
    return [
        g3_scratch(channels, size_x, size_y, size_z),
        flat_scratch(channels),
        pltpu.VMEM((3, 2 * channels, 12 * channels), BF16),
        pltpu.VMEM((2, channels * size_y, size_z), F32),
    ]


def wgrad_cost(channels, size_x, size_y, size_z):
    return cost(54 * channels * channels * size_x * (size_y + 2) * size_z, 4 * 2**20)


def dgrad_cost(channels, size_x, size_y, size_z):
    return cost(72 * channels * channels * size_x * size_y * size_z, 4 * 2**20)


def row_for_other(body, size_z):
    plane = body.shape[-1]
    low, high = body[:, :size_z].astype(F32), body[:, plane - size_z :].astype(F32)
    return jnp.where(lax.axis_index("gy") == 0, high, low).astype(BF16)


def pair_inner_kernel(rows, *refs):
    first_ref, last_ref, m_ref, g_ref, side_ref, swap_ref, sent_ref = refs[2:9]
    sent_buf, sent_sem = refs[13:]
    choose(is_odd("gx"), swap_ref, first_ref, last_ref)
    share = m_ref[...]
    height = sent_ref.shape[1] - share.shape[0]
    if height:
        share = jnp.concatenate([share, jnp.zeros((height, share.shape[1]), F32)], axis=0)
    share = share.astype(BF16)
    for device in range(sent_ref.shape[0]):
        sent_buf[device] = share
    send = pltpu.make_async_copy(sent_buf, sent_ref, sent_sem)
    send.start()
    read_inner(rows, *refs[:2], g_ref, *refs[9:13])
    size_z = side_ref.shape[-1]
    inner, _, plane = g_ref.shape
    size_x = inner + 2
    bodies = [first_ref] + [g_ref.at[x] for x in range(inner)] + [last_ref]
    for x, body in enumerate(bodies):
        side_ref[x] = row_for_other(body, size_z)
    low, high = z_tiles(
        [body[...] for body in bodies], plane // size_z, size_z, range(1, size_x + 1)
    )
    side_ref[size_x] = low.astype(BF16)
    side_ref[size_x + 1] = high.astype(BF16)
    send.wait()


def pair_inner(preact, upstream, first, last, share, sent_shape, rows):
    shape = preact.shape
    channels, size_x, _, size_z = shape
    return pl.pallas_call(
        functools.partial(pair_inner_kernel, rows),
        in_specs=[HBM] * 2 + [VMEM] * 3,
        out_specs=[VMEM] * 3 + [HBM],
        out_shape=[
            inner_output(*shape),
            jax.ShapeDtypeStruct((size_x + 2, channels, size_z), BF16),
            jax.ShapeDtypeStruct(first.shape, BF16),
            jax.ShapeDtypeStruct(sent_shape, BF16),
        ],
        scratch_shapes=inner_scratch(*shape)
        + [pltpu.VMEM(sent_shape, BF16), pltpu.SemaphoreType.DMA(())],
        compiler_params=params(INNER_VMEM),
        cost_estimate=cost(0, 4 * 2**20),
        name="inner",
    )(preact, upstream, first, last, share)


def is_odd(axis):
    return lax.rem(lax.axis_index(axis), 2) == 1


def either(condition, first, second):
    return jnp.where(condition, first.astype(F32), second.astype(F32))


def side_kernel(odd_ref, even_ref, own_ref, sent_ref, xlo_ref, xhi_ref):
    size_x = own_ref.shape[0] - 2
    size_z = own_ref.shape[-1]
    size_y = xlo_ref.shape[-1] // size_z
    odd = is_odd("gx")
    low = either(odd, even_ref[...], odd_ref[...]).astype(BF16)
    high = either(odd, odd_ref[...], even_ref[...]).astype(BF16)
    xlo_ref[...] = low
    xhi_ref[...] = high
    sent_ref[0] = row_for_other(low, size_z)
    for x in range(size_x):
        sent_ref[x + 1] = own_ref[x]
    sent_ref[size_x + 1] = row_for_other(high, size_z)
    lane = lax.broadcasted_iota(jnp.int32, (low.shape[0], LANES), 1)
    first, second = own_ref[size_x], own_ref[size_x + 1]
    for number, plane in ((0, low), (size_x + 1, high)):
        for y in range(size_y):
            at = number * size_y + y
            head = plane[:, y * size_z : y * size_z + LANES]
            tail = plane[:, (y + 1) * size_z - LANES : (y + 1) * size_z]
            first = jnp.where(lane == at, pltpu.roll(head, at, 1), first)
            second = jnp.where(lane == at, pltpu.roll(tail, at + 1, 1), second)
    sent_ref[size_x + 2] = first
    sent_ref[size_x + 3] = second


def side(halves, own):
    plane = jax.ShapeDtypeStruct(halves[0].shape, BF16)
    return pl.pallas_call(
        side_kernel,
        in_specs=[VMEM] * 3,
        out_specs=[VMEM] * 3,
        out_shape=[
            jax.ShapeDtypeStruct((own.shape[0] + 2, *own.shape[1:]), BF16),
            plane,
            plane,
        ],
        compiler_params=params(),
        cost_estimate=cost(2**25, 2**19),
        name="side",
    )(*halves, own)


def own_columns(columns, number, area):
    me = lax.axis_index("gy")
    value = columns.astype(F32)
    lane = lax.broadcasted_iota(jnp.int32, value.shape, 1)
    first = pltpu.roll(value, -number * area % LANES, 1)
    second = pltpu.roll(value, (1 - number) * area % LANES, 1)
    first = jnp.where(lane < area, first, 0.0)
    second = jnp.where((lane >= area) & (lane < 2 * area), second, 0.0)
    return jnp.where(me == 0, first, second)


def join_kernel(area, own_ref, other_ref, columns_ref, even_ref, odd_ref):
    at = own_ref.shape[0] - 2
    me = lax.axis_index("gy")
    last = own_columns(columns_ref[...], 1, area).astype(BF16)

    def fill(up_ref, down_ref):
        for k, out_ref in enumerate((down_ref, up_ref)):
            out_ref[me] = own_ref[at + k]
            out_ref[1 - me] = other_ref[at + k]
        up_ref[2] = last
        down_ref[2] = last

    odd = is_odd("gz")

    @pl.when(odd)
    def _():
        fill(odd_ref, even_ref)

    @pl.when(jnp.logical_not(odd))
    def _():
        fill(even_ref, odd_ref)


def join(own, other, columns, area):
    return pl.pallas_call(
        functools.partial(join_kernel, area),
        in_specs=[VMEM] * 3,
        out_specs=[VMEM] * 2,
        out_shape=[jax.ShapeDtypeStruct((3, *own.shape[1:]), BF16)] * 2,
        compiler_params=params(),
        cost_estimate=cost(0, 2**17),
        name="join",
    )(own, other, columns)


def pair_wgrad_kernel(*refs):
    x_ref, acc_ref, g3, x3 = refs[7:]
    weight_products(refs, None, x_ref, g3, x3, acc_ref)


def pair_wgrad(sources, planes_x, shape):
    channels = shape[0]
    return pl.pallas_call(
        pair_wgrad_kernel,
        in_specs=[VMEM] * 8,
        out_specs=VMEM,
        out_shape=jax.ShapeDtypeStruct((9 * channels, 3 * channels), F32),
        scratch_shapes=[g3_scratch(*shape), x3_scratch(*shape)],
        compiler_params=params(32 * 2**20),
        cost_estimate=wgrad_cost(*shape),
        name="wgrad",
    )(*sources, planes_x)


def finish_kernel(scale, rows, sizes, *refs):
    acc_ref, columns_ref, even_ref, odd_ref, from_odd_ref, from_even_ref = refs[:6]
    part_ref, chunks, part_buf, sems = refs[6:]
    size_x, size_y = sizes
    channels = columns_ref.shape[0]
    area = size_x * size_y
    odd = is_odd("gz")
    lane = lax.broadcasted_iota(jnp.int32, (channels, LANES), 1)
    row = lane % size_y
    jump = area - size_y + 1
    below = [either(odd, from_even_ref[k], from_odd_ref[k]) for k in range(3)]
    own = [either(odd, even_ref[k], odd_ref[k]) for k in range(2)]
    pairs = ((below[:2], own_columns(columns_ref[...], 0, area)), (own, below[2]))
    edges = []
    for tiles, value in pairs:
        before = jnp.where(lane >= area, pltpu.roll(value, jump, 1), 0.0)
        after = jnp.where(lane < area, pltpu.roll(value, LANES - jump, 1), 0.0)
        right = jnp.concatenate(
            [
                jnp.where(row > 0, pltpu.roll(value, 1, 1), before),
                value,
                jnp.where(row < size_y - 1, pltpu.roll(value, LANES - 1, 1), after),
            ],
            axis=0,
        )
        left = []
        for a in range(3):
            first = pltpu.roll(tiles[0], -a * size_y % LANES, 1)
            second = pltpu.roll(tiles[1], (area - a * size_y) % LANES, 1)
            left.append(jnp.where(lane < area, first, jnp.where(lane < 2 * area, second, 0.0)))
        edges.append(
            lax.dot_general(
                jnp.concatenate(left, axis=0).astype(BF16),
                right.astype(BF16),
                (((1,), (1,)), ((), ())),
                preferred_element_type=F32,
            )
        )
    count, height, width = part_ref.shape
    chunks[...] = jnp.zeros_like(chunks)
    pieces = rows * acc_ref.shape[1] // width
    for a in range(3):
        for c in range(3):
            at = 3 * a + c
            block = acc_ref[at * channels : (at + 1) * channels, :]
            if c != 1:
                block = block + edges[c // 2][a * channels : (a + 1) * channels]
            block = block * scale
            line = jnp.concatenate(
                [block[r * count : (r + 1) * count] for r in range(rows)], axis=1
            )
            for k in range(pieces):
                chunks[pl.ds(at * pieces + k, count, stride=height), :] = line[
                    :, k * width : (k + 1) * width
                ]
    pieces = sems.shape[0]
    step = count // pieces
    copies = []
    for k in range(pieces):
        piece = chunks[k * step * height : (k + 1) * step * height, :]
        at = pl.ds(k * step, step)
        part_buf[at] = piece.reshape(step, height, width).astype(BF16)
        copies.append(pltpu.make_async_copy(part_buf.at[at], part_ref.at[at], sems.at[k]))
        copies[-1].start()
    for copy in copies:
        copy.wait()


def finish(acc, columns, sent, received, scale, rows, sizes, part_shape):
    channels = columns.shape[0]
    return pl.pallas_call(
        functools.partial(finish_kernel, scale, rows, sizes),
        in_specs=[VMEM] * 6,
        out_specs=HBM,
        out_shape=jax.ShapeDtypeStruct(part_shape, BF16),
        scratch_shapes=[
            pltpu.VMEM((part_shape[0] * part_shape[1], part_shape[2]), F32),
            pltpu.VMEM(part_shape, BF16),
            pltpu.SemaphoreType.DMA((4,)),
        ],
        compiler_params=params(),
        cost_estimate=cost(2**27, 2**21),
        name="finish",
    )(acc, columns, *sent, *received)


def adam_step(master, first, second, weight_grad):
    new_first = 0.9 * first + 0.1 * weight_grad
    new_second = 0.999 * second + 0.001 * weight_grad * weight_grad
    corr_first = 1.0 - (0.9**10) ** 10
    corr_second = 1.0 - (0.999**10) ** 10
    update = new_first / corr_first / (jnp.sqrt(new_second / corr_second) + 1e-08) + 0.01 * master
    return master - 0.05 * update, new_first, new_second


def in_flat_order(value, rows, places, spread_rows):
    taps = 27
    lane = lax.broadcasted_iota(jnp.int32, (9, LANES), 1)
    rows[: value.shape[0], :] = value
    thirds = [rows[pl.ds(k, 9, stride=3), :] for k in range(3)]
    half = LANES // 2
    by_y = (
        jnp.where(lane < half, thirds[0], thirds[1]),
        jnp.where(lane < half, pltpu.roll(thirds[0], half, 1), pltpu.roll(thirds[2], half, 1)),
        jnp.where(lane < half, thirds[1], thirds[2]),
    )
    places[...] = jnp.zeros_like(places)
    for b in range(3):
        spread_rows[b, :9, :] = by_y[b]
        for block in range(9):
            tap = (2 - block // 3) * 9 + b * 3 + 2 - block % 3
            places[tap : tap + 1, :] = spread_rows[b, block : block + 1, :]
    line = places[...].T
    number = lax.broadcasted_iota(jnp.int32, (LANES, LANES), 0) * taps
    column = lax.broadcasted_iota(jnp.int32, (LANES, LANES), 1)
    turned = []
    for group in range(LANES // 8):
        piece = line[8 * group : 8 * (group + 1)]
        rest = 8 * group * taps % LANES
        for step in range(3):
            turn = rest // (3 - step)
            rest -= turn
            piece = pltpu.roll(piece, turn, 1, stride=taps // 3, stride_axis=0)
        turned.append(piece)
    line = jnp.concatenate(turned, axis=0)
    start = number & (LANES - 1)
    line = jnp.concatenate(
        [jnp.where(column >= start, line, 0.0), jnp.where(column < start, line, 0.0)], axis=0
    )
    target = lax.broadcasted_iota(jnp.int32, (32, 2 * LANES), 0)
    source = lax.broadcasted_iota(jnp.int32, (32, 2 * LANES), 1)
    goes = lax.shift_right_logical((source & (LANES - 1)) * taps, 7)
    goes = goes + jnp.where(source < LANES, 0, 1)
    pick = jnp.where(goes == target, 1.0, 0.0).astype(BF16)
    parts = []
    for _ in range(3):
        parts.append(line.astype(BF16))
        line = line - parts[-1].astype(F32)
    return jnp.dot(
        jnp.concatenate([pick] * 3, axis=1),
        jnp.concatenate(parts, axis=0),
        preferred_element_type=F32,
    )[:taps]


def adam_kernel(parts_ref, master_ref, first_ref, second_ref, *refs):
    out_refs, scratch = refs[:4], refs[4:]
    total = parts_ref[0].astype(F32)
    for source in range(1, parts_ref.shape[0]):
        total = total + parts_ref[source].astype(F32)
    weight_grad = in_flat_order(total, *scratch)
    results = adam_step(master_ref[...], first_ref[...], second_ref[...], weight_grad)
    for out_ref, result in zip(out_refs, (weight_grad, *results)):
        out_ref[...] = result


def adam(parts, *states):
    share = states[0].shape[0]
    tiled = [state.reshape(share // LANES, LANES) for state in states]
    result = jax.ShapeDtypeStruct(tiled[0].shape, F32)
    outs = pl.pallas_call(
        adam_kernel,
        in_specs=[VMEM] * 4,
        out_specs=[VMEM] * 4,
        out_shape=[result] * 4,
        scratch_shapes=[
            pltpu.VMEM(parts.shape[1:], F32),
            pltpu.VMEM((LANES, LANES), F32),
            pltpu.VMEM((3, 16, LANES), F32),
        ],
        compiler_params=params(),
        cost_estimate=cost(2**22, 2**19),
        name="adam",
    )(parts, *tiled)
    return tuple(out.reshape(share) for out in outs)


def spread_kernel(rows, w_ref, weights_ref, turned, chunks):
    count, height, width = w_ref.shape
    taps = 27 * rows * count
    chunks[...] = w_ref[...].astype(F32).reshape(chunks.shape)
    line = jnp.concatenate(
        [chunks[pl.ds(k, count, stride=height), :] for k in range(rows * taps // width)], axis=1
    )
    whole = jnp.concatenate([line[:, r * taps : (r + 1) * taps] for r in range(rows)], axis=0)
    spread_weights(whole, turned, weights_ref)


def spread(kernel, channels, rows):
    return pl.pallas_call(
        functools.partial(spread_kernel, rows),
        in_specs=[VMEM],
        out_specs=VMEM,
        out_shape=jax.ShapeDtypeStruct((3, 2 * channels, 12 * channels), BF16),
        scratch_shapes=[
            flat_scratch(channels),
            pltpu.VMEM((kernel.shape[0] * kernel.shape[1], kernel.shape[2]), F32),
        ],
        compiler_params=params(),
        cost_estimate=cost(2**20, 2**21),
        name="spread",
    )(kernel)


def pair_dgrad_kernel(*refs):
    weights_ref, out_ref, g3, tile = refs[9:]
    _, size_x, size_y, size_z = out_ref.shape
    halo = pair_z_halo(refs[7], refs[8], size_x + 2, size_y, size_z)
    input_products(refs, halo, g3, weights_ref, tile, out_ref)


def pair_dgrad(sources, weights, shape):
    channels, _, size_y, size_z = shape
    return pl.pallas_call(
        pair_dgrad_kernel,
        in_specs=[VMEM] * 10,
        out_specs=VMEM,
        out_shape=jax.ShapeDtypeStruct(shape, BF16),
        scratch_shapes=[g3_scratch(*shape), pltpu.VMEM((2, channels * size_y, size_z), F32)],
        compiler_params=params(32 * 2**20),
        cost_estimate=dgrad_cost(*shape),
        name="dgrad",
    )(*sources, weights)


def pair_program(activations, preact, upstream, master, first_moment, second_moment, scale):
    shape = activations.shape
    channels, size_x, size_y, _ = shape
    devices = math.prod(lax.axis_size(a) for a in AXES)
    rows = channels // devices
    used = master.shape[0] // LANES
    block = (devices, -(-used // 16) * 16, LANES)
    first, last, odd_sent = faces(preact, upstream, "gx", rows)
    odd_halves = swapped(odd_sent, "gx", 1)
    inner, own, even_sent, sent = pair_inner(
        preact, upstream, first, last, master.reshape(used, LANES), block, rows
    )
    even_halves = swapped(even_sent, "gx", 0)
    kernel = lax.all_to_all(sent, AXES, 0, 0, tiled=True)
    own, xlo, xhi = side((odd_halves, even_halves), own)
    planes = (xlo, first, inner, last, xhi)
    own, activations = lax.optimization_barrier((own, activations))
    other = shifted(own, {"gy": "swap"})
    planes_x, columns = input_planes(activations, True)
    z_sent = join(own, other, columns, size_x * size_y)
    from_odd = swapped(z_sent[1], "gz", 1)
    from_even = swapped(z_sent[0], "gz", 0)
    sources = (*planes, other, other)
    acc = pair_wgrad(sources, planes_x, shape)
    z_received = (from_odd, from_even)
    part = finish(acc, columns, z_sent, z_received, scale, rows, (size_x, size_y), block)
    part, kernel = lax.optimization_barrier((part, kernel))
    parts = lax.all_to_all(part, AXES, 0, 0, tiled=True)
    weights = spread(kernel, channels, rows)
    grad_input = pair_dgrad((*sources, *z_received), weights, shape)
    return grad_input, *adam(parts, master, first_moment, second_moment)


def yface_kernel(*refs):
    low_ref, high_ref = refs[5:]
    size_z = low_ref.shape[-1]
    for index in range(low_ref.shape[0]):
        body = body_of(refs[:5], index)
        plane = body.shape[-1]
        low_ref[index] = body[:, :size_z]
        high_ref[index] = body[:, plane - size_z :]


def y_faces(planes, size_z):
    inner, channels, _ = planes[2].shape
    face = jax.ShapeDtypeStruct((inner + 4, channels, size_z), BF16)
    return pl.pallas_call(
        yface_kernel,
        in_specs=[VMEM] * 5,
        out_specs=[VMEM] * 2,
        out_shape=[face] * 2,
        compiler_params=params(),
        cost_estimate=cost(0, 2**19),
        name="yfaces",
    )(*planes)


def zface_kernel(*refs):
    zlo_ref, zhi_ref = refs[7:]
    size_z = refs[5].shape[-1]
    whole = []
    for index in range(refs[5].shape[0]):
        low, high = y_halo(refs[5:7], index)
        body = body_of(refs[:5], index)[...]
        whole.append(jnp.concatenate([low.astype(BF16), body, high.astype(BF16)], axis=1))
    low, high = z_tiles(whole, whole[0].shape[1] // size_z, size_z, range(len(whole)))
    zlo_ref[...] = low.astype(BF16)
    zhi_ref[...] = high.astype(BF16)


def z_faces(planes, y_halos):
    face = jax.ShapeDtypeStruct((planes[0].shape[0], LANES), BF16)
    return pl.pallas_call(
        zface_kernel,
        in_specs=[VMEM] * 7,
        out_specs=[VMEM] * 2,
        out_shape=[face, face],
        compiler_params=params(),
        cost_estimate=cost(2**27, 2**21),
        name="zfaces",
    )(*planes, *y_halos)


def wgrad_kernel(scale, *refs):
    x_ref, part_ref, g3, x3, acc, flat = refs[9:]
    size_x, channels, plane = x_ref.shape
    size_z = refs[5].shape[-1]
    halo = z_halo(refs[7], refs[8], size_x + 2, plane // size_z + 2, size_z)
    weight_products(refs, halo, x_ref, g3, x3, acc)
    whole = to_flat(acc[...] * scale, channels, channels, flat)
    part_ref[...] = whole[:, : part_ref.shape[1]].astype(BF16)


def wgrad(sources, planes_x, shape, scale):
    channels = shape[0]
    return pl.pallas_call(
        functools.partial(wgrad_kernel, scale),
        in_specs=[VMEM] * 10,
        out_specs=VMEM,
        out_shape=jax.ShapeDtypeStruct((channels, 27 * channels), BF16),
        scratch_shapes=[
            g3_scratch(*shape),
            x3_scratch(*shape),
            acc_scratch(channels),
            flat_scratch(channels),
        ],
        compiler_params=params(32 * 2**20),
        cost_estimate=wgrad_cost(*shape),
        name="wgrad",
    )(*sources, planes_x)


def dgrad_kernel(*refs):
    w_ref, out_ref, g3, turned, weights, tile = refs[9:]
    _, size_x, size_y, size_z = out_ref.shape
    spread_weights(w_ref[...].astype(F32), turned, weights)
    halo = z_halo(refs[7], refs[8], size_x + 2, size_y + 2, size_z)
    input_products(refs, halo, g3, weights, tile, out_ref)


def dgrad(sources, kernel, shape):
    return pl.pallas_call(
        dgrad_kernel,
        in_specs=[VMEM] * 10,
        out_specs=VMEM,
        out_shape=jax.ShapeDtypeStruct(shape, BF16),
        scratch_shapes=dgrad_scratch(*shape),
        compiler_params=params(32 * 2**20),
        cost_estimate=dgrad_cost(*shape),
        name="dgrad",
    )(*sources, kernel)


def general_program(activations, preact, upstream, master, first_moment, second_moment, scale):
    shape = activations.shape
    channels, _, _, size_z = shape
    devices = math.prod(lax.axis_size(a) for a in AXES)
    share = master.shape[0]
    first, last = faces(preact, upstream)
    x_halos = (shifted(last, {"gx": 1}), shifted(first, {"gx": -1}))
    inner = inner_planes(preact, upstream)
    (planes_x,) = input_planes(activations, False)
    sent = jnp.broadcast_to(master.astype(BF16).reshape(1, 1, share), (devices, 1, share))
    kernel = lax.all_to_all(sent, AXES, 0, 0, tiled=True).reshape(channels, 27 * channels)
    planes = (x_halos[0], first, inner, last, x_halos[1])
    y_sent = y_faces(planes, size_z)
    y_halos = (shifted(y_sent[1], {"gy": 1}), shifted(y_sent[0], {"gy": -1}))
    zlo, zhi = z_faces(planes, y_halos)
    z_halos = (shifted(zhi, {"gz": 1}), shifted(zlo, {"gz": -1}))
    sources = (*planes, *y_halos, *z_halos)
    part = wgrad(sources, planes_x, shape, scale)
    part, kernel = lax.optimization_barrier((part, kernel))
    parts = lax.all_to_all(part.reshape(devices, 1, share), AXES, 0, 0, tiled=True)
    grad_input = dgrad(sources, kernel, shape)
    weight_grad = jnp.sum(parts.astype(F32), axis=0).reshape(-1)
    results = adam_step(master, first_moment, second_moment, weight_grad)
    return grad_input, weight_grad, *results


def shifted(value, moves):
    names = tuple(moves)
    sizes = [lax.axis_size(name) for name in names]
    pairs = []
    for source in range(math.prod(sizes)):
        rest, coords = source, []
        for size in reversed(sizes):
            coords.insert(0, rest % size)
            rest //= size
        coords = [
            (at + moves[name]) if moves[name] != "swap" else 1 - at
            for at, name in zip(coords, names)
        ]
        if all(0 <= at < size for at, size in zip(coords, sizes)):
            target = 0
            for at, size in zip(coords, sizes):
                target = target * size + at
            pairs.append((source, target))
    return lax.ppermute(value, names if len(names) > 1 else names[0], pairs)


def swapped(value, axis, start):
    pairs = []
    for low in range(start, lax.axis_size(axis) - 1, 2):
        pairs += [(low, low + 1), (low + 1, low)]
    return lax.ppermute(value, axis, pairs)


def local(activations, preact, upstream, master, first_moment, second_moment):
    channels, size_x, size_y, size_z = activations.shape
    devices = math.prod(lax.axis_size(a) for a in AXES)
    share = master.shape[0]
    scale = 1.0 / math.sqrt(size_x * size_y * size_z * devices)
    in_pairs = (
        lax.axis_size("gy") == 2
        and channels % devices == 0
        and share % LANES == 0
        and channels // devices * channels == LANES
        and 2 * size_x * size_y <= LANES
        and (size_x + 2) * size_y <= LANES
    )
    program = pair_program if in_pairs else general_program
    return program(
        activations, preact, upstream, master, first_moment, second_moment, scale
    )


def solution(mesh):
    volume = P(None, "gx", "gy", "gz")
    flat = P(AXES)
    return jax.shard_map(
        local,
        mesh=mesh,
        in_specs=(volume, volume, volume, flat, flat, flat),
        out_specs=(volume, flat, flat, flat, flat),
        check_vma=False,
    )
```

```python
import functools
import math

import jax
import jax.numpy as jnp
from jax import lax
from jax.experimental import pallas as pl
from jax.experimental.pallas import tpu as pltpu
from jax.sharding import PartitionSpec as P

AXES = ("gx", "gy", "gz")
LANES = 128
VMEM = pl.BlockSpec(memory_space=pltpu.VMEM)
HBM = pl.BlockSpec(memory_space=pltpu.HBM)
F32 = jnp.float32
BF16 = jnp.bfloat16
FACES_VMEM = 55_900_000
INNER_VMEM = 54_800_000


def params(limit=24 * 2**20):
    return pltpu.CompilerParams(vmem_limit_bytes=limit)


def cost(flops, moved):
    return pl.CostEstimate(flops=flops, bytes_accessed=moved, transcendentals=0)


def to_planes(value, tile, write, rows=1):
    channels, size_y, size_z = value.shape
    count = channels // rows
    tile[...] = value.astype(F32).reshape(channels * size_y, size_z)
    for y in range(size_y):
        for r in range(rows):
            picked = tile[pl.ds(r * size_y + y, count, stride=rows * size_y), :]
            write(slice(r * count, (r + 1) * count), y, picked.astype(BF16))


def masked(p, u):
    return jnp.where(p > 0, u, jnp.zeros_like(u))


def choose(condition, out_ref, first_ref, second_ref):
    @pl.when(condition)
    def _():
        out_ref[...] = first_ref[...]

    @pl.when(jnp.logical_not(condition))
    def _():
        out_ref[...] = second_ref[...]


def face_kernel(axis, rows, p_ref, u_ref, *refs):
    p_buf, u_buf, tile, sems = refs[-4:]
    out_refs, swap_refs = refs[:2], refs[2:-4]
    size_x, size_z = p_ref.shape[1], p_ref.shape[3]
    copies = []
    for k, x in enumerate((0, size_x - 1)):
        pair = (
            pltpu.make_async_copy(p_ref.at[:, x], p_buf.at[k], sems.at[2 * k]),
            pltpu.make_async_copy(u_ref.at[:, x], u_buf.at[k], sems.at[2 * k + 1]),
        )
        for copy in pair:
            copy.start()
        copies.append(pair)
    for k, out_ref in enumerate(out_refs):
        for copy in copies[k]:
            copy.wait()

        def write(at, y, value):
            out_ref[at, y * size_z : (y + 1) * size_z] = value

        to_planes(masked(p_buf[k], u_buf[k]), tile.at[k], write, rows)
    if axis is not None:
        choose(is_odd(axis), swap_refs[0], out_refs[1], out_refs[0])


def faces(preact, upstream, axis=None, rows=1):
    channels, size_x, size_y, size_z = preact.shape
    face = jax.ShapeDtypeStruct((channels, size_y * size_z), BF16)
    buffer = pltpu.VMEM((2, channels, size_y, size_z), BF16)
    count = 2 if axis is None else 3
    return pl.pallas_call(
        functools.partial(face_kernel, axis, rows),
        in_specs=[HBM, HBM],
        out_specs=[VMEM] * count,
        out_shape=[face] * count,
        scratch_shapes=[
            buffer,
            buffer,
            pltpu.VMEM((2, channels * size_y, size_z), F32),
            pltpu.SemaphoreType.DMA((4,)),
        ],
        compiler_params=params(FACES_VMEM),
        cost_estimate=cost(0, 2**20),
        name="faces",
    )(preact, upstream)


def read_inner(rows, p_ref, u_ref, g_ref, p_buf, u_buf, tile, sems):
    size_x, size_z = p_ref.shape[1], p_ref.shape[3]
    inner = size_x - 2
    copies = []
    for x in range(inner):
        pair = (
            pltpu.make_async_copy(p_ref.at[:, x + 1], p_buf.at[x], sems.at[x]),
            pltpu.make_async_copy(u_ref.at[:, x + 1], u_buf.at[x], sems.at[inner + x]),
        )
        for copy in pair:
            copy.start()
        copies.append(pair)
    for x in range(inner):
        for copy in copies[x]:
            copy.wait()

        def write(at, y, value):
            g_ref[x, at, y * size_z : (y + 1) * size_z] = value

        to_planes(masked(p_buf[x], u_buf[x]), tile.at[x % 2], write, rows)


def inner_kernel(*refs):
    read_inner(1, *refs)


def inner_output(channels, size_x, size_y, size_z):
    return jax.ShapeDtypeStruct((size_x - 2, channels, size_y * size_z), BF16)


def inner_scratch(channels, size_x, size_y, size_z):
    return [
        pltpu.VMEM((size_x - 2, channels, size_y, size_z), BF16),
        pltpu.VMEM((size_x - 2, channels, size_y, size_z), BF16),
        pltpu.VMEM((2, channels * size_y, size_z), F32),
        pltpu.SemaphoreType.DMA((2 * size_x - 4,)),
    ]


def inner_planes(preact, upstream):
    shape = preact.shape
    return pl.pallas_call(
        inner_kernel,
        in_specs=[HBM] * 2,
        out_specs=VMEM,
        out_shape=inner_output(*shape),
        scratch_shapes=inner_scratch(*shape),
        compiler_params=params(INNER_VMEM),
        cost_estimate=cost(0, 4 * 2**20),
        name="inner",
    )(preact, upstream)


def input_kernel(a_ref, x_ref, *refs):
    tile = refs[-1]
    channels, size_x, size_y, size_z = a_ref.shape
    for x in range(size_x):

        def write(at, y, value):
            x_ref[x, at, y * size_z : (y + 1) * size_z] = value

        to_planes(a_ref[:, x], tile.at[x % 2], write)
    if len(refs) > 1:
        low, high = z_tiles([x_ref[x] for x in range(size_x)], size_y, size_z, range(size_x))
        refs[0][...] = (low + pltpu.roll(high, size_x * size_y, 1)).astype(BF16)


def input_planes(activations, with_columns):
    channels, size_x, size_y, size_z = activations.shape
    outs = [jax.ShapeDtypeStruct((size_x, channels, size_y * size_z), BF16)]
    if with_columns:
        outs.append(jax.ShapeDtypeStruct((channels, LANES), BF16))
    return pl.pallas_call(
        input_kernel,
        in_specs=[VMEM],
        out_specs=[VMEM] * len(outs),
        out_shape=outs,
        scratch_shapes=[pltpu.VMEM((2, channels * size_y, size_z), F32)],
        compiler_params=params(),
        cost_estimate=cost(0, 2 * 2**20),
        name="inputs",
    )(activations)


def body_of(refs, index):
    planes = refs[2].shape[0] + 4
    if 2 <= index < planes - 2:
        return refs[2].at[index - 2]
    return refs[{0: 0, 1: 1, planes - 2: 3, planes - 1: 4}[index]]


def y_halo(refs, index):
    me = lax.axis_index("gy")
    low = jnp.where(me > 0, refs[0][index].astype(F32), 0.0)
    high = jnp.where(me < lax.axis_size("gy") - 1, refs[1][index].astype(F32), 0.0)
    return low, high


def z_picker(rows_y, size_z):
    shape = (rows_y * size_z, 2 * LANES)
    voxel = lax.broadcasted_iota(jnp.int32, shape, 0)
    lane = lax.broadcasted_iota(jnp.int32, shape, 1)
    wanted = jnp.where(lane < LANES, lane * size_z, (lane - LANES) * size_z + size_z - 1)
    return (voxel == wanted).astype(F32).astype(BF16)


def z_tiles(planes, rows_y, size_z, numbers):
    channels = planes[0].shape[0]
    columns = jnp.dot(
        jnp.concatenate(planes, axis=0), z_picker(rows_y, size_z), preferred_element_type=F32
    )
    low = jnp.zeros((channels, LANES), F32)
    high = jnp.zeros((channels, LANES), F32)
    for index, number in enumerate(numbers):
        rows = columns[index * channels : (index + 1) * channels]
        low = low + pltpu.roll(rows[:, :LANES], number * rows_y, 1)
        high = high + pltpu.roll(rows[:, LANES:], number * rows_y, 1)
    return low, high


def put_columns(columns, row_of, rows_y, size_z):
    shape = (2 * LANES, rows_y * size_z)
    source = lax.broadcasted_iota(jnp.int32, shape, 0)
    voxel = lax.broadcasted_iota(jnp.int32, shape, 1)
    number = source % LANES
    place = row_of(number) * size_z + jnp.where(source < LANES, 0, size_z - 1)
    place = jnp.where(number < rows_y, place, -1)
    put = (voxel == place).astype(F32).astype(BF16)
    rows = [jnp.concatenate(pair, axis=1) for pair in columns]
    return jnp.dot(
        jnp.concatenate(rows, axis=0).astype(BF16), put, preferred_element_type=F32
    ).astype(BF16)


def z_halo(low_ref, high_ref, planes, rows_y, size_z):
    columns = []
    for index in range(planes):
        shift = -index * rows_y % LANES
        columns.append(
            [pltpu.roll(ref[...].astype(F32), shift, 1) for ref in (low_ref, high_ref)]
        )
    return put_columns(columns, lambda number: number, rows_y, size_z)


def pair_z_halo(low_ref, high_ref, planes, size_y, size_z):
    me = lax.axis_index("gy")
    sides = []
    for ref in (low_ref, high_ref):
        first, second = ref[0].astype(F32), ref[1].astype(F32)
        lane = lax.broadcasted_iota(jnp.int32, first.shape, 1)
        own = jnp.where(me == 0, first, second)
        before = jnp.where(me == 0, 0.0, first)
        after = jnp.where(me == 0, second, 0.0)
        columns = []
        for index in range(planes):
            start = index * size_y
            columns.append(
                jnp.where(
                    lane < size_y,
                    pltpu.roll(own, -start % LANES, 1),
                    jnp.where(
                        lane == size_y,
                        pltpu.roll(before, (1 - start) % LANES, 1),
                        pltpu.roll(after, (size_y + 1 - start) % LANES, 1),
                    ),
                )
            )
        sides.append(columns)

    def row_of(number):
        return jnp.where(number < size_y, number + 1, jnp.where(number == size_y, 0, size_y + 1))

    return put_columns(list(zip(*sides)), row_of, size_y + 2, size_z)


def shifted_plane(index, refs, halo, g3):
    channels, plane = refs[0].shape
    size_z = refs[5].shape[-1]
    rows_y = plane // size_z + 2
    base = 3 * channels * index
    lane = lax.broadcasted_iota(jnp.int32, (channels, size_z), 1)
    is_first, is_last = lane == 0, lane == size_z - 1
    low, high = y_halo(refs[5:7], index)
    body = body_of(refs[:5], index)
    for row in range(rows_y):
        cols = slice(row * size_z, (row + 1) * size_z)
        if row == 0:
            value = low.astype(BF16)
        elif row == rows_y - 1:
            value = high.astype(BF16)
        else:
            value = body[:, (row - 1) * size_z : row * size_z]
        if halo is None:
            edge = jnp.zeros_like(value)
        else:
            edge = halo[index * channels : (index + 1) * channels, cols]
        before = jnp.where(is_first, edge, pltpu.roll(value, 1, 1))
        after = jnp.where(is_last, edge, pltpu.roll(value, size_z - 1, 1))
        g3[base : base + channels, cols] = before
        g3[base + channels : base + 2 * channels, cols] = value
        g3[base + 2 * channels : base + 3 * channels, cols] = after


def weight_products(refs, halo, x_ref, g3, x3, acc):
    size_x, channels, plane = x_ref.shape
    size_z = refs[5].shape[-1]
    group = 3 * channels
    zero = jnp.zeros((channels, 2 * size_z), BF16)
    done = 0
    for x in range(0, size_x, 2):
        while done < x + 4:
            shifted_plane(done, refs, halo, g3)
            done += 1
        for plane_x in (x, x + 1):
            value = x_ref[plane_x]
            for b in range(3):
                at = slice(b * channels, (b + 1) * channels)
                start = (2 - b) * size_z
                x3[plane_x, at, start : start + plane] = value
                if start:
                    x3[plane_x, at, :start] = zero[:, :start]
                if start < 2 * size_z:
                    x3[plane_x, at, start + plane :] = zero[:, start:]
        product = lax.dot_general(
            jnp.concatenate(
                [g3[x * group : (x + 3) * group, :], g3[(x + 1) * group : (x + 4) * group, :]],
                axis=1,
            ),
            jnp.concatenate([x3[x], x3[x + 1]], axis=1),
            (((1,), (1,)), ((), ())),
            preferred_element_type=F32,
        )
        if x == 0:
            acc[...] = product
        else:
            acc[...] += product


def to_flat(value, count, channels, flat):
    height, width = value.shape
    wide = value
    if height % LANES:
        wide = jnp.concatenate([wide, jnp.zeros((-height % LANES, width), F32)], axis=0)
    if width % LANES:
        wide = jnp.concatenate([wide, jnp.zeros((wide.shape[0], -width % LANES), F32)], axis=1)
    turned = wide.T
    for b in range(3):
        rows = turned[b * channels : (b + 1) * channels]
        for block in range(9):
            start = block * count
            cell = rows[:, start // LANES * LANES : (start // LANES + 1) * LANES]
            tap = (2 - block // 3) * 9 + b * 3 + 2 - block % 3
            shift = -start % LANES
            flat[pl.ds(tap, channels, stride=27), :] = pltpu.roll(cell, shift, 1) if shift else cell
    return flat[...].T[:count]


def spread_weights(whole, turned, weights):
    channels, taps = whole.shape
    group = 3 * channels
    whole = jnp.concatenate([whole, jnp.zeros((LANES - channels, taps), F32)], axis=0)
    whole = jnp.concatenate([whole, jnp.zeros((LANES, -taps % LANES), F32)], axis=1)
    turned[...] = whole.T
    for b in range(3):
        blocks = []
        for a in range(3):
            for c in range(3):
                tap = (2 - a) * 9 + (2 - b) * 3 + 2 - c
                blocks.append(turned[pl.ds(tap, channels, stride=27), :][:, :channels])
        zero = jnp.zeros((channels, group), F32)
        weights[b, :channels] = jnp.concatenate(blocks + [zero], axis=1).astype(BF16)
        weights[b, channels:] = jnp.concatenate([zero] + blocks, axis=1).astype(BF16)


def input_products(refs, halo, g3, weights, tile, out_ref):
    channels, size_x, size_y, size_z = out_ref.shape
    group = 3 * channels
    plane = size_y * size_z
    done = 0
    for pair in range(size_x // 2):
        while done < 2 * pair + 4:
            shifted_plane(done, refs, halo, g3)
            done += 1
        at = slice(2 * pair * group, (2 * pair + 4) * group)
        total = None
        for b in range(3):
            product = jnp.dot(
                weights[b],
                g3[at, b * size_z : b * size_z + plane],
                preferred_element_type=F32,
            )
            total = product if total is None else total + product
        for half in range(2):
            for y in range(size_y):
                tile[half, pl.ds(y, channels, stride=size_y), :] = total[
                    half * channels : (half + 1) * channels, y * size_z : (y + 1) * size_z
                ]
            out_ref[:, 2 * pair + half] = (
                tile[half].reshape(channels, size_y, size_z).astype(BF16)
            )


def g3_scratch(channels, size_x, size_y, size_z):
    return pltpu.VMEM(((size_x + 2) * 3 * channels, (size_y + 2) * size_z), BF16)


def x3_scratch(channels, size_x, size_y, size_z):
    return pltpu.VMEM((size_x, 3 * channels, (size_y + 2) * size_z), BF16)


def acc_scratch(channels):
    return pltpu.VMEM((9 * channels, 3 * channels), F32)


def flat_scratch(channels):
    return pltpu.VMEM((-(-27 * channels // LANES) * LANES, LANES), F32)


def dgrad_scratch(channels, size_x, size_y, size_z):
    return [
        g3_scratch(channels, size_x, size_y, size_z),
        flat_scratch(channels),
        pltpu.VMEM((3, 2 * channels, 12 * channels), BF16),
        pltpu.VMEM((2, channels * size_y, size_z), F32),
    ]


def wgrad_cost(channels, size_x, size_y, size_z):
    return cost(54 * channels * channels * size_x * (size_y + 2) * size_z, 4 * 2**20)


def dgrad_cost(channels, size_x, size_y, size_z):
    return cost(72 * channels * channels * size_x * size_y * size_z, 4 * 2**20)


def turned_columns(planes, low, high, size_y, size_z):
    lane = lax.broadcasted_iota(jnp.int32, low.shape, 1)
    for number, plane in planes:
        for y in range(size_y):
            at = number * size_y + y
            head = plane[:, y * size_z : y * size_z + LANES]
            tail = plane[:, (y + 1) * size_z - LANES : (y + 1) * size_z]
            low = jnp.where(lane == at, pltpu.roll(head, at, 1), low)
            high = jnp.where(lane == at, pltpu.roll(tail, at + 1, 1), high)
    return low, high


def row_for_other(body, size_z):
    plane = body.shape[-1]
    low, high = body[:, :size_z].astype(F32), body[:, plane - size_z :].astype(F32)
    return jnp.where(lax.axis_index("gy") == 0, high, low).astype(BF16)


def pair_inner_kernel(rows, *refs):
    first_ref, last_ref, m_ref, g_ref, side_ref, swap_ref, sent_ref = refs[2:9]
    sent_buf, sent_sem = refs[13:]
    choose(is_odd("gx"), swap_ref, first_ref, last_ref)
    share = m_ref[...]
    height = sent_ref.shape[1] - share.shape[0]
    if height:
        share = jnp.concatenate([share, jnp.zeros((height, share.shape[1]), F32)], axis=0)
    share = share.astype(BF16)
    for device in range(sent_ref.shape[0]):
        sent_buf[device] = share
    send = pltpu.make_async_copy(sent_buf, sent_ref, sent_sem)
    send.start()
    read_inner(rows, *refs[:2], g_ref, *refs[9:13])
    size_z = side_ref.shape[-1]
    inner, _, plane = g_ref.shape
    size_x = inner + 2
    bodies = [first_ref] + [g_ref.at[x] for x in range(inner)] + [last_ref]
    for x, body in enumerate(bodies):
        side_ref[x] = row_for_other(body, size_z)
    low = jnp.zeros((first_ref.shape[0], LANES), BF16)
    low, high = turned_columns(
        [(x + 1, body) for x, body in enumerate(bodies)], low, low, plane // size_z, size_z
    )
    side_ref[size_x] = low
    side_ref[size_x + 1] = high
    send.wait()


def pair_inner(preact, upstream, first, last, share, sent_shape, rows):
    shape = preact.shape
    channels, size_x, _, size_z = shape
    return pl.pallas_call(
        functools.partial(pair_inner_kernel, rows),
        in_specs=[HBM] * 2 + [VMEM] * 3,
        out_specs=[VMEM] * 3 + [HBM],
        out_shape=[
            inner_output(*shape),
            jax.ShapeDtypeStruct((size_x + 2, channels, size_z), BF16),
            jax.ShapeDtypeStruct(first.shape, BF16),
            jax.ShapeDtypeStruct(sent_shape, BF16),
        ],
        scratch_shapes=inner_scratch(*shape)
        + [pltpu.VMEM(sent_shape, BF16), pltpu.SemaphoreType.DMA(())],
        compiler_params=params(INNER_VMEM),
        cost_estimate=cost(0, 4 * 2**20),
        name="inner",
    )(preact, upstream, first, last, share)


def is_odd(axis):
    return lax.rem(lax.axis_index(axis), 2) == 1


def either(condition, first, second):
    return jnp.where(condition, first.astype(F32), second.astype(F32))


def side_kernel(odd_ref, even_ref, own_ref, sent_ref, xlo_ref, xhi_ref):
    size_x = own_ref.shape[0] - 2
    size_z = own_ref.shape[-1]
    size_y = xlo_ref.shape[-1] // size_z
    odd = is_odd("gx")
    low = either(odd, even_ref[...], odd_ref[...]).astype(BF16)
    high = either(odd, odd_ref[...], even_ref[...]).astype(BF16)
    xlo_ref[...] = low
    xhi_ref[...] = high
    sent_ref[0] = row_for_other(low, size_z)
    for x in range(size_x):
        sent_ref[x + 1] = own_ref[x]
    sent_ref[size_x + 1] = row_for_other(high, size_z)
    first, second = turned_columns(
        ((0, low), (size_x + 1, high)), own_ref[size_x], own_ref[size_x + 1], size_y, size_z
    )
    sent_ref[size_x + 2] = first
    sent_ref[size_x + 3] = second


def side(halves, own):
    plane = jax.ShapeDtypeStruct(halves[0].shape, BF16)
    return pl.pallas_call(
        side_kernel,
        in_specs=[VMEM] * 3,
        out_specs=[VMEM] * 3,
        out_shape=[
            jax.ShapeDtypeStruct((own.shape[0] + 2, *own.shape[1:]), BF16),
            plane,
            plane,
        ],
        compiler_params=params(),
        cost_estimate=cost(2**25, 2**19),
        name="side",
    )(*halves, own)


def own_columns(columns, number, area):
    me = lax.axis_index("gy")
    value = columns.astype(F32)
    lane = lax.broadcasted_iota(jnp.int32, value.shape, 1)
    first = pltpu.roll(value, -number * area % LANES, 1)
    second = pltpu.roll(value, (1 - number) * area % LANES, 1)
    first = jnp.where(lane < area, first, 0.0)
    second = jnp.where((lane >= area) & (lane < 2 * area), second, 0.0)
    return jnp.where(me == 0, first, second)


def join_kernel(area, own_ref, other_ref, columns_ref, down_ref, up_ref):
    at = own_ref.shape[0] - 2
    me = lax.axis_index("gy")
    for k, out_ref in enumerate((down_ref, up_ref)):
        out_ref[me] = own_ref[at + k]
        out_ref[1 - me] = other_ref[at + k]
    up_ref[2] = own_columns(columns_ref[...], 1, area).astype(BF16)


def join(own, other, columns, area):
    return pl.pallas_call(
        functools.partial(join_kernel, area),
        in_specs=[VMEM] * 3,
        out_specs=[VMEM] * 2,
        out_shape=[jax.ShapeDtypeStruct((n, *own.shape[1:]), BF16) for n in (2, 3)],
        compiler_params=params(),
        cost_estimate=cost(0, 2**17),
        name="join",
    )(own, other, columns)


def pair_wgrad_kernel(*refs):
    x_ref, acc_ref, g3, x3 = refs[7:]
    weight_products(refs, None, x_ref, g3, x3, acc_ref)


def pair_wgrad(sources, planes_x, shape):
    channels = shape[0]
    return pl.pallas_call(
        pair_wgrad_kernel,
        in_specs=[VMEM] * 8,
        out_specs=VMEM,
        out_shape=jax.ShapeDtypeStruct((9 * channels, 3 * channels), F32),
        scratch_shapes=[g3_scratch(*shape), x3_scratch(*shape)],
        compiler_params=params(32 * 2**20),
        cost_estimate=wgrad_cost(*shape),
        name="wgrad",
    )(*sources, planes_x)


def finish_kernel(scale, rows, sizes, *refs):
    acc_ref, columns_ref, down_ref, from_below_ref = refs[:4]
    part_ref, chunks, part_buf, sems = refs[4:]
    size_x, size_y = sizes
    channels = columns_ref.shape[0]
    area = size_x * size_y
    lane = lax.broadcasted_iota(jnp.int32, (channels, LANES), 1)
    row = lane % size_y
    jump = area - size_y + 1
    below = [from_below_ref[k].astype(F32) for k in range(3)]
    own = [down_ref[k].astype(F32) for k in range(2)]
    pairs = ((below[:2], own_columns(columns_ref[...], 0, area)), (own, below[2]))
    edges = []
    for tiles, value in pairs:
        before = jnp.where(lane >= area, pltpu.roll(value, jump, 1), 0.0)
        after = jnp.where(lane < area, pltpu.roll(value, LANES - jump, 1), 0.0)
        right = jnp.concatenate(
            [
                jnp.where(row > 0, pltpu.roll(value, 1, 1), before),
                value,
                jnp.where(row < size_y - 1, pltpu.roll(value, LANES - 1, 1), after),
            ],
            axis=0,
        )
        left = []
        for a in range(3):
            first = pltpu.roll(tiles[0], -a * size_y % LANES, 1)
            second = pltpu.roll(tiles[1], (area - a * size_y) % LANES, 1)
            left.append(jnp.where(lane < area, first, jnp.where(lane < 2 * area, second, 0.0)))
        edges.append(
            lax.dot_general(
                jnp.concatenate(left, axis=0).astype(BF16),
                right.astype(BF16),
                (((1,), (1,)), ((), ())),
                preferred_element_type=F32,
            )
        )
    count, height, width = part_ref.shape
    chunks[...] = jnp.zeros_like(chunks)
    pieces = rows * acc_ref.shape[1] // width
    for a in range(3):
        for c in range(3):
            at = 3 * a + c
            block = acc_ref[at * channels : (at + 1) * channels, :]
            if c != 1:
                block = block + edges[c // 2][a * channels : (a + 1) * channels]
            block = block * scale
            line = jnp.concatenate(
                [block[r * count : (r + 1) * count] for r in range(rows)], axis=1
            )
            for k in range(pieces):
                chunks[pl.ds(at * pieces + k, count, stride=height), :] = line[
                    :, k * width : (k + 1) * width
                ]
    pieces = sems.shape[0]
    step = count // pieces
    copies = []
    for k in range(pieces):
        piece = chunks[k * step * height : (k + 1) * step * height, :]
        at = pl.ds(k * step, step)
        part_buf[at] = piece.reshape(step, height, width).astype(BF16)
        copies.append(pltpu.make_async_copy(part_buf.at[at], part_ref.at[at], sems.at[k]))
        copies[-1].start()
    for copy in copies:
        copy.wait()


def finish(acc, columns, down, below, scale, rows, sizes, part_shape):
    channels = columns.shape[0]
    return pl.pallas_call(
        functools.partial(finish_kernel, scale, rows, sizes),
        in_specs=[VMEM] * 4,
        out_specs=HBM,
        out_shape=jax.ShapeDtypeStruct(part_shape, BF16),
        scratch_shapes=[
            pltpu.VMEM((part_shape[0] * part_shape[1], part_shape[2]), F32),
            pltpu.VMEM(part_shape, BF16),
            pltpu.SemaphoreType.DMA((4,)),
        ],
        compiler_params=params(),
        cost_estimate=cost(2**27, 2**21),
        name="finish",
    )(acc, columns, down, below)


def adam_step(master, first, second, weight_grad):
    new_first = 0.9 * first + 0.1 * weight_grad
    new_second = 0.999 * second + 0.001 * weight_grad * weight_grad
    corr_first = 1.0 - (0.9**10) ** 10
    corr_second = 1.0 - (0.999**10) ** 10
    update = new_first / corr_first / (jnp.sqrt(new_second / corr_second) + 1e-08) + 0.01 * master
    return master - 0.05 * update, new_first, new_second


def in_flat_order(value, rows, places, spread_rows):
    taps = 27
    lane = lax.broadcasted_iota(jnp.int32, (9, LANES), 1)
    rows[: value.shape[0], :] = value
    thirds = [rows[pl.ds(k, 9, stride=3), :] for k in range(3)]
    half = LANES // 2
    by_y = (
        jnp.where(lane < half, thirds[0], thirds[1]),
        jnp.where(lane < half, pltpu.roll(thirds[0], half, 1), pltpu.roll(thirds[2], half, 1)),
        jnp.where(lane < half, thirds[1], thirds[2]),
    )
    places[...] = jnp.zeros_like(places)
    for b in range(3):
        spread_rows[b, :9, :] = by_y[b]
        for block in range(9):
            tap = (2 - block // 3) * 9 + b * 3 + 2 - block % 3
            places[tap : tap + 1, :] = spread_rows[b, block : block + 1, :]
    line = places[...].T
    number = lax.broadcasted_iota(jnp.int32, (LANES, LANES), 0) * taps
    column = lax.broadcasted_iota(jnp.int32, (LANES, LANES), 1)
    turned = []
    for group in range(LANES // 8):
        piece = line[8 * group : 8 * (group + 1)]
        rest = 8 * group * taps % LANES
        for step in range(3):
            turn = rest // (3 - step)
            rest -= turn
            piece = pltpu.roll(piece, turn, 1, stride=taps // 3, stride_axis=0)
        turned.append(piece)
    line = jnp.concatenate(turned, axis=0)
    start = number & (LANES - 1)
    line = jnp.concatenate(
        [jnp.where(column >= start, line, 0.0), jnp.where(column < start, line, 0.0)], axis=0
    )
    target = lax.broadcasted_iota(jnp.int32, (32, 2 * LANES), 0)
    source = lax.broadcasted_iota(jnp.int32, (32, 2 * LANES), 1)
    goes = lax.shift_right_logical((source & (LANES - 1)) * taps, 7)
    goes = goes + jnp.where(source < LANES, 0, 1)
    pick = jnp.where(goes == target, 1.0, 0.0).astype(BF16)
    parts = []
    for _ in range(3):
        parts.append(line.astype(BF16))
        line = line - parts[-1].astype(F32)
    return jnp.dot(
        jnp.concatenate([pick] * 3, axis=1),
        jnp.concatenate(parts, axis=0),
        preferred_element_type=F32,
    )[:taps]


def adam_kernel(parts_ref, master_ref, first_ref, second_ref, *refs):
    out_refs, scratch = refs[:4], refs[4:]
    total = parts_ref[0].astype(F32)
    for source in range(1, parts_ref.shape[0]):
        total = total + parts_ref[source].astype(F32)
    weight_grad = in_flat_order(total, *scratch)
    results = adam_step(master_ref[...], first_ref[...], second_ref[...], weight_grad)
    for out_ref, result in zip(out_refs, (weight_grad, *results)):
        out_ref[...] = result


def adam(parts, *states):
    share = states[0].shape[0]
    tiled = [state.reshape(share // LANES, LANES) for state in states]
    result = jax.ShapeDtypeStruct(tiled[0].shape, F32)
    outs = pl.pallas_call(
        adam_kernel,
        in_specs=[VMEM] * 4,
        out_specs=[VMEM] * 4,
        out_shape=[result] * 4,
        scratch_shapes=[
            pltpu.VMEM(parts.shape[1:], F32),
            pltpu.VMEM((LANES, LANES), F32),
            pltpu.VMEM((3, 16, LANES), F32),
        ],
        compiler_params=params(),
        cost_estimate=cost(2**22, 2**19),
        name="adam",
    )(parts, *tiled)
    return tuple(out.reshape(share) for out in outs)


def lines_kernel(rows, w_ref, whole_ref, chunks):
    count, height, width = w_ref.shape
    taps = whole_ref.shape[1]
    chunks[...] = w_ref[...].astype(F32).reshape(chunks.shape)
    line = jnp.concatenate(
        [chunks[pl.ds(k, count, stride=height), :] for k in range(rows * taps // width)], axis=1
    )
    for r in range(rows):
        whole_ref[r * count : (r + 1) * count, :] = line[:, r * taps : (r + 1) * taps]


def lines(kernel, channels, rows):
    return pl.pallas_call(
        functools.partial(lines_kernel, rows),
        in_specs=[VMEM],
        out_specs=VMEM,
        out_shape=jax.ShapeDtypeStruct((channels, 27 * channels), F32),
        scratch_shapes=[pltpu.VMEM((kernel.shape[0] * kernel.shape[1], kernel.shape[2]), F32)],
        compiler_params=params(),
        cost_estimate=cost(0, 2**20),
        name="lines",
    )(kernel)


def spread_kernel(whole_ref, weights_ref, turned):
    spread_weights(whole_ref[...], turned, weights_ref)


def spread(whole):
    channels = whole.shape[0]
    return pl.pallas_call(
        spread_kernel,
        in_specs=[VMEM],
        out_specs=VMEM,
        out_shape=jax.ShapeDtypeStruct((3, 2 * channels, 12 * channels), BF16),
        scratch_shapes=[flat_scratch(channels)],
        compiler_params=params(),
        cost_estimate=cost(2**20, 2**21),
        name="spread",
    )(whole)


def pair_dgrad_kernel(*refs):
    weights_ref, out_ref, g3, tile = refs[9:]
    _, size_x, size_y, size_z = out_ref.shape
    halo = pair_z_halo(refs[7], refs[8], size_x + 2, size_y, size_z)
    input_products(refs, halo, g3, weights_ref, tile, out_ref)


def pair_dgrad(sources, weights, shape):
    channels, _, size_y, size_z = shape
    return pl.pallas_call(
        pair_dgrad_kernel,
        in_specs=[VMEM] * 10,
        out_specs=VMEM,
        out_shape=jax.ShapeDtypeStruct(shape, BF16),
        scratch_shapes=[g3_scratch(*shape), pltpu.VMEM((2, channels * size_y, size_z), F32)],
        compiler_params=params(32 * 2**20),
        cost_estimate=cost(0, 2**10),
        name="dgrad",
    )(*sources, weights)


def pair_program(activations, preact, upstream, master, first_moment, second_moment, scale):
    shape = activations.shape
    channels, size_x, size_y, _ = shape
    devices = math.prod(lax.axis_size(a) for a in AXES)
    rows = channels // devices
    used = master.shape[0] // LANES
    block = (devices, -(-used // 16) * 16, LANES)
    first, last, odd_sent = faces(preact, upstream, "gx", rows)
    odd_halves = swapped(odd_sent, "gx", 1)
    inner, own, even_sent, sent = pair_inner(
        preact, upstream, first, last, master.reshape(used, LANES), block, rows
    )
    even_halves = swapped(even_sent, "gx", 0)
    kernel = lax.all_to_all(sent, AXES, 0, 0, tiled=True)
    own, xlo, xhi = side((odd_halves, even_halves), own)
    planes = (xlo, first, inner, last, xhi)
    own, activations = lax.optimization_barrier((own, activations))
    other = shifted(own, {"gy": "swap"})
    planes_x, columns = input_planes(activations, True)
    down, up = join(own, other, columns, size_x * size_y)
    below = shifted(up, {"gz": 1})
    sources = (*planes, other, other)
    acc = pair_wgrad(sources, planes_x, shape)
    part = finish(acc, columns, down, below, scale, rows, (size_x, size_y), block)
    part, kernel = lax.optimization_barrier((part, kernel))
    parts = lax.all_to_all(part, AXES, 0, 0, tiled=True)
    whole = lines(kernel, channels, rows)
    whole, down = lax.optimization_barrier((whole, down))
    above = shifted(down, {"gz": -1})
    grad_input = pair_dgrad((*sources, below, above), spread(whole), shape)
    return grad_input, *adam(parts, master, first_moment, second_moment)


def yface_kernel(*refs):
    low_ref, high_ref = refs[5:]
    size_z = low_ref.shape[-1]
    for index in range(low_ref.shape[0]):
        body = body_of(refs[:5], index)
        plane = body.shape[-1]
        low_ref[index] = body[:, :size_z]
        high_ref[index] = body[:, plane - size_z :]


def y_faces(planes, size_z):
    inner, channels, _ = planes[2].shape
    face = jax.ShapeDtypeStruct((inner + 4, channels, size_z), BF16)
    return pl.pallas_call(
        yface_kernel,
        in_specs=[VMEM] * 5,
        out_specs=[VMEM] * 2,
        out_shape=[face] * 2,
        compiler_params=params(),
        cost_estimate=cost(0, 2**19),
        name="yfaces",
    )(*planes)


def zface_kernel(*refs):
    zlo_ref, zhi_ref = refs[7:]
    size_z = refs[5].shape[-1]
    whole = []
    for index in range(refs[5].shape[0]):
        low, high = y_halo(refs[5:7], index)
        body = body_of(refs[:5], index)[...]
        whole.append(jnp.concatenate([low.astype(BF16), body, high.astype(BF16)], axis=1))
    low, high = z_tiles(whole, whole[0].shape[1] // size_z, size_z, range(len(whole)))
    zlo_ref[...] = low.astype(BF16)
    zhi_ref[...] = high.astype(BF16)


def z_faces(planes, y_halos):
    face = jax.ShapeDtypeStruct((planes[0].shape[0], LANES), BF16)
    return pl.pallas_call(
        zface_kernel,
        in_specs=[VMEM] * 7,
        out_specs=[VMEM] * 2,
        out_shape=[face, face],
        compiler_params=params(),
        cost_estimate=cost(2**27, 2**21),
        name="zfaces",
    )(*planes, *y_halos)


def wgrad_kernel(scale, *refs):
    x_ref, part_ref, g3, x3, acc, flat = refs[9:]
    size_x, channels, plane = x_ref.shape
    size_z = refs[5].shape[-1]
    halo = z_halo(refs[7], refs[8], size_x + 2, plane // size_z + 2, size_z)
    weight_products(refs, halo, x_ref, g3, x3, acc)
    whole = to_flat(acc[...] * scale, channels, channels, flat)
    part_ref[...] = whole[:, : part_ref.shape[1]].astype(BF16)


def wgrad(sources, planes_x, shape, scale):
    channels = shape[0]
    return pl.pallas_call(
        functools.partial(wgrad_kernel, scale),
        in_specs=[VMEM] * 10,
        out_specs=VMEM,
        out_shape=jax.ShapeDtypeStruct((channels, 27 * channels), BF16),
        scratch_shapes=[
            g3_scratch(*shape),
            x3_scratch(*shape),
            acc_scratch(channels),
            flat_scratch(channels),
        ],
        compiler_params=params(32 * 2**20),
        cost_estimate=wgrad_cost(*shape),
        name="wgrad",
    )(*sources, planes_x)


def dgrad_kernel(*refs):
    w_ref, out_ref, g3, turned, weights, tile = refs[9:]
    _, size_x, size_y, size_z = out_ref.shape
    spread_weights(w_ref[...].astype(F32), turned, weights)
    halo = z_halo(refs[7], refs[8], size_x + 2, size_y + 2, size_z)
    input_products(refs, halo, g3, weights, tile, out_ref)


def dgrad(sources, kernel, shape):
    return pl.pallas_call(
        dgrad_kernel,
        in_specs=[VMEM] * 10,
        out_specs=VMEM,
        out_shape=jax.ShapeDtypeStruct(shape, BF16),
        scratch_shapes=dgrad_scratch(*shape),
        compiler_params=params(32 * 2**20),
        cost_estimate=dgrad_cost(*shape),
        name="dgrad",
    )(*sources, kernel)


def general_program(activations, preact, upstream, master, first_moment, second_moment, scale):
    shape = activations.shape
    channels, _, _, size_z = shape
    devices = math.prod(lax.axis_size(a) for a in AXES)
    share = master.shape[0]
    first, last = faces(preact, upstream)
    x_halos = (shifted(last, {"gx": 1}), shifted(first, {"gx": -1}))
    inner = inner_planes(preact, upstream)
    (planes_x,) = input_planes(activations, False)
    sent = jnp.broadcast_to(master.astype(BF16).reshape(1, 1, share), (devices, 1, share))
    kernel = lax.all_to_all(sent, AXES, 0, 0, tiled=True).reshape(channels, 27 * channels)
    planes = (x_halos[0], first, inner, last, x_halos[1])
    y_sent = y_faces(planes, size_z)
    y_halos = (shifted(y_sent[1], {"gy": 1}), shifted(y_sent[0], {"gy": -1}))
    zlo, zhi = z_faces(planes, y_halos)
    z_halos = (shifted(zhi, {"gz": 1}), shifted(zlo, {"gz": -1}))
    sources = (*planes, *y_halos, *z_halos)
    part = wgrad(sources, planes_x, shape, scale)
    part, kernel = lax.optimization_barrier((part, kernel))
    parts = lax.all_to_all(part.reshape(devices, 1, share), AXES, 0, 0, tiled=True)
    grad_input = dgrad(sources, kernel, shape)
    weight_grad = jnp.sum(parts.astype(F32), axis=0).reshape(-1)
    results = adam_step(master, first_moment, second_moment, weight_grad)
    return grad_input, weight_grad, *results


def shifted(value, moves):
    names = tuple(moves)
    sizes = [lax.axis_size(name) for name in names]
    pairs = []
    for source in range(math.prod(sizes)):
        rest, coords = source, []
        for size in reversed(sizes):
            coords.insert(0, rest % size)
            rest //= size
        coords = [
            (at + moves[name]) if moves[name] != "swap" else 1 - at
            for at, name in zip(coords, names)
        ]
        if all(0 <= at < size for at, size in zip(coords, sizes)):
            target = 0
            for at, size in zip(coords, sizes):
                target = target * size + at
            pairs.append((source, target))
    return lax.ppermute(value, names if len(names) > 1 else names[0], pairs)


def swapped(value, axis, start):
    pairs = []
    for low in range(start, lax.axis_size(axis) - 1, 2):
        pairs += [(low, low + 1), (low + 1, low)]
    return lax.ppermute(value, axis, pairs)


def local(activations, preact, upstream, master, first_moment, second_moment):
    channels, size_x, size_y, size_z = activations.shape
    devices = math.prod(lax.axis_size(a) for a in AXES)
    share = master.shape[0]
    scale = 1.0 / math.sqrt(size_x * size_y * size_z * devices)
    in_pairs = (
        lax.axis_size("gy") == 2
        and channels % devices == 0
        and share % LANES == 0
        and channels // devices * channels == LANES
        and 2 * size_x * size_y <= LANES
        and (size_x + 2) * size_y <= LANES
    )
    program = pair_program if in_pairs else general_program
    return program(
        activations, preact, upstream, master, first_moment, second_moment, scale
    )


def solution(mesh):
    volume = P(None, "gx", "gy", "gz")
    flat = P(AXES)
    return jax.shard_map(
        local,
        mesh=mesh,
        in_specs=(volume, volume, volume, flat, flat, flat),
        out_specs=(volume, flat, flat, flat, flat),
        check_vma=False,
    )
```

```python
import functools
import math

import jax
import jax.numpy as jnp
from jax import lax
from jax.experimental import pallas as pl
from jax.experimental.pallas import tpu as pltpu
from jax.sharding import PartitionSpec as P

AXES = ("gx", "gy", "gz")
LANES = 128
VMEM = pl.BlockSpec(memory_space=pltpu.VMEM)
HBM = pl.BlockSpec(memory_space=pltpu.HBM)
F32 = jnp.float32
BF16 = jnp.bfloat16
FACES_VMEM = 55_900_000
INNER_VMEM = 54_800_000


def params(limit=24 * 2**20):
    return pltpu.CompilerParams(vmem_limit_bytes=limit)


def cost(flops, moved):
    return pl.CostEstimate(flops=flops, bytes_accessed=moved, transcendentals=0)


def to_planes(value, tile, write, rows=1):
    channels, size_y, size_z = value.shape
    count = channels // rows
    tile[...] = value.astype(F32).reshape(channels * size_y, size_z)
    for y in range(size_y):
        for r in range(rows):
            picked = tile[pl.ds(r * size_y + y, count, stride=rows * size_y), :]
            write(slice(r * count, (r + 1) * count), y, picked.astype(BF16))


QUAD = 4


def to_quads(rows, write):
    for k in range(rows.shape[-2] // QUAD):
        write(slice(k * LANES, (k + 1) * LANES), rows[..., k * QUAD : (k + 1) * QUAD, :])


def masked(p, u):
    return jnp.where(p > 0, u, jnp.zeros_like(u))


def choose(condition, out_ref, first_ref, second_ref):
    @pl.when(condition)
    def _():
        out_ref[...] = first_ref[...]

    @pl.when(jnp.logical_not(condition))
    def _():
        out_ref[...] = second_ref[...]


def face_kernel(axis, rows, p_ref, u_ref, *refs):
    p_buf, u_buf, tile, sems = refs[-4:]
    out_refs, swap_refs = refs[:2], refs[2:-4]
    size_x, size_z = p_ref.shape[1], p_ref.shape[3]
    copies = []
    for k, x in enumerate((0, size_x - 1)):
        pair = (
            pltpu.make_async_copy(p_ref.at[:, x], p_buf.at[k], sems.at[2 * k]),
            pltpu.make_async_copy(u_ref.at[:, x], u_buf.at[k], sems.at[2 * k + 1]),
        )
        for copy in pair:
            copy.start()
        copies.append(pair)
    for k, out_ref in enumerate(out_refs):
        for copy in copies[k]:
            copy.wait()

        def write(at, y, value):
            out_ref[at, y * size_z : (y + 1) * size_z] = value

        to_planes(masked(p_buf[k], u_buf[k]), tile.at[k], write, rows)
    if axis is not None:
        choose(is_odd(axis), swap_refs[0], out_refs[1], out_refs[0])


def faces(preact, upstream, axis=None, rows=1):
    channels, size_x, size_y, size_z = preact.shape
    face = jax.ShapeDtypeStruct((channels, size_y * size_z), BF16)
    buffer = pltpu.VMEM((2, channels, size_y, size_z), BF16)
    count = 2 if axis is None else 3
    return pl.pallas_call(
        functools.partial(face_kernel, axis, rows),
        in_specs=[HBM, HBM],
        out_specs=[VMEM] * count,
        out_shape=[face] * count,
        scratch_shapes=[
            buffer,
            buffer,
            pltpu.VMEM((2, channels * size_y, size_z), F32),
            pltpu.SemaphoreType.DMA((4,)),
        ],
        compiler_params=params(FACES_VMEM),
        cost_estimate=cost(0, 2**20),
        name="faces",
    )(preact, upstream)


def read_inner(rows, p_ref, u_ref, g_ref, p_buf, u_buf, tile, sems):
    size_x, size_z = p_ref.shape[1], p_ref.shape[3]
    inner = size_x - 2
    copies = []
    for x in range(inner):
        pair = (
            pltpu.make_async_copy(p_ref.at[:, x + 1], p_buf.at[x], sems.at[x]),
            pltpu.make_async_copy(u_ref.at[:, x + 1], u_buf.at[x], sems.at[inner + x]),
        )
        for copy in pair:
            copy.start()
        copies.append(pair)
    for x in range(inner):
        for copy in copies[x]:
            copy.wait()

        def write(at, y, value):
            g_ref[x, at, y * size_z : (y + 1) * size_z] = value

        to_planes(masked(p_buf[x], u_buf[x]), tile.at[x % 2], write, rows)


def inner_kernel(*refs):
    read_inner(1, *refs)


def inner_output(channels, size_x, size_y, size_z):
    return jax.ShapeDtypeStruct((size_x - 2, channels, size_y * size_z), BF16)


def inner_scratch(channels, size_x, size_y, size_z):
    return [
        pltpu.VMEM((size_x - 2, channels, size_y, size_z), BF16),
        pltpu.VMEM((size_x - 2, channels, size_y, size_z), BF16),
        pltpu.VMEM((2, channels * size_y, size_z), F32),
        pltpu.SemaphoreType.DMA((2 * size_x - 4,)),
    ]


def inner_planes(preact, upstream):
    shape = preact.shape
    return pl.pallas_call(
        inner_kernel,
        in_specs=[HBM] * 2,
        out_specs=VMEM,
        out_shape=inner_output(*shape),
        scratch_shapes=inner_scratch(*shape),
        compiler_params=params(INNER_VMEM),
        cost_estimate=cost(0, 4 * 2**20),
        name="inner",
    )(preact, upstream)


def input_kernel(a_ref, x_ref, *refs):
    tile = refs[-1]
    channels, size_x, size_y, size_z = a_ref.shape
    for x in range(size_x):

        def write(at, y, value):
            x_ref[x, at, y * size_z : (y + 1) * size_z] = value

        to_planes(a_ref[:, x], tile.at[x % 2], write)
    if len(refs) > 1:
        low, high = z_tiles([x_ref[x] for x in range(size_x)], size_y, size_z, range(size_x))
        refs[0][...] = (low + pltpu.roll(high, size_x * size_y, 1)).astype(BF16)


def input_planes(activations, with_columns):
    channels, size_x, size_y, size_z = activations.shape
    outs = [jax.ShapeDtypeStruct((size_x, channels, size_y * size_z), BF16)]
    if with_columns:
        outs.append(jax.ShapeDtypeStruct((channels, LANES), BF16))
    return pl.pallas_call(
        input_kernel,
        in_specs=[VMEM],
        out_specs=[VMEM] * len(outs),
        out_shape=outs,
        scratch_shapes=[pltpu.VMEM((2, channels * size_y, size_z), F32)],
        compiler_params=params(),
        cost_estimate=cost(0, 2 * 2**20),
        name="inputs",
    )(activations)


def body_of(refs, index):
    planes = refs[2].shape[0] + 4
    if 2 <= index < planes - 2:
        return refs[2].at[index - 2]
    return refs[{0: 0, 1: 1, planes - 2: 3, planes - 1: 4}[index]]


def y_halo(refs, index):
    me = lax.axis_index("gy")
    low = jnp.where(me > 0, refs[0][index].astype(F32), 0.0)
    high = jnp.where(me < lax.axis_size("gy") - 1, refs[1][index].astype(F32), 0.0)
    return low, high


def z_picker(rows_y, size_z):
    shape = (rows_y * size_z, 2 * LANES)
    voxel = lax.broadcasted_iota(jnp.int32, shape, 0)
    lane = lax.broadcasted_iota(jnp.int32, shape, 1)
    wanted = jnp.where(lane < LANES, lane * size_z, (lane - LANES) * size_z + size_z - 1)
    return (voxel == wanted).astype(F32).astype(BF16)


def z_tiles(planes, rows_y, size_z, numbers):
    channels = planes[0].shape[0]
    columns = jnp.dot(
        jnp.concatenate(planes, axis=0), z_picker(rows_y, size_z), preferred_element_type=F32
    )
    low = jnp.zeros((channels, LANES), F32)
    high = jnp.zeros((channels, LANES), F32)
    for index, number in enumerate(numbers):
        rows = columns[index * channels : (index + 1) * channels]
        low = low + pltpu.roll(rows[:, :LANES], number * rows_y, 1)
        high = high + pltpu.roll(rows[:, LANES:], number * rows_y, 1)
    return low, high


def put_columns(columns, row_of, rows_y, size_z):
    shape = (2 * LANES, rows_y * size_z)
    source = lax.broadcasted_iota(jnp.int32, shape, 0)
    voxel = lax.broadcasted_iota(jnp.int32, shape, 1)
    number = source % LANES
    place = row_of(number) * size_z + jnp.where(source < LANES, 0, size_z - 1)
    place = jnp.where(number < rows_y, place, -1)
    put = (voxel == place).astype(F32).astype(BF16)
    rows = [jnp.concatenate(pair, axis=1) for pair in columns]
    return jnp.dot(
        jnp.concatenate(rows, axis=0).astype(BF16), put, preferred_element_type=F32
    ).astype(BF16)


def z_halo(low_ref, high_ref, planes, rows_y, size_z):
    columns = []
    for index in range(planes):
        shift = -index * rows_y % LANES
        columns.append(
            [pltpu.roll(ref[...].astype(F32), shift, 1) for ref in (low_ref, high_ref)]
        )
    return put_columns(columns, lambda number: number, rows_y, size_z)


def pair_z_halo(odd_ref, even_ref, planes, size_y, size_z):
    me, odd = lax.axis_index("gy"), is_odd("gz")
    sides = []
    for low, high in ((even_ref, odd_ref), (odd_ref, even_ref)):
        first, second = (either(odd, low[k], high[k]) for k in range(2))
        lane = lax.broadcasted_iota(jnp.int32, first.shape, 1)
        own = jnp.where(me == 0, first, second)
        before = jnp.where(me == 0, 0.0, first)
        after = jnp.where(me == 0, second, 0.0)
        columns = []
        for index in range(planes):
            start = index * size_y
            columns.append(
                jnp.where(
                    lane < size_y,
                    pltpu.roll(own, -start % LANES, 1),
                    jnp.where(
                        lane == size_y,
                        pltpu.roll(before, (1 - start) % LANES, 1),
                        pltpu.roll(after, (size_y + 1 - start) % LANES, 1),
                    ),
                )
            )
        sides.append(columns)

    def row_of(number):
        return jnp.where(number < size_y, number + 1, jnp.where(number == size_y, 0, size_y + 1))

    return put_columns(list(zip(*sides)), row_of, size_y + 2, size_z)


def shifted_plane(index, refs, halo, g3):
    channels, plane = refs[0].shape
    size_z = refs[5].shape[-1]
    rows_y = plane // size_z + 2
    base = 3 * channels * index
    lane = lax.broadcasted_iota(jnp.int32, (channels, size_z), 1)
    is_first, is_last = lane == 0, lane == size_z - 1
    low, high = y_halo(refs[5:7], index)
    body = body_of(refs[:5], index)
    for row in range(rows_y):
        cols = slice(row * size_z, (row + 1) * size_z)
        if row == 0:
            value = low.astype(BF16)
        elif row == rows_y - 1:
            value = high.astype(BF16)
        else:
            value = body[:, (row - 1) * size_z : row * size_z]
        if halo is None:
            edge = jnp.zeros_like(value)
        else:
            edge = halo[index * channels : (index + 1) * channels, cols]
        before = jnp.where(is_first, edge, pltpu.roll(value, 1, 1))
        after = jnp.where(is_last, edge, pltpu.roll(value, size_z - 1, 1))
        g3[base : base + channels, cols] = before
        g3[base + channels : base + 2 * channels, cols] = value
        g3[base + 2 * channels : base + 3 * channels, cols] = after


def weight_products(refs, halo, x_ref, g3, x3, acc):
    size_x, channels, plane = x_ref.shape
    size_z = refs[5].shape[-1]
    group = 3 * channels
    zero = jnp.zeros((channels, 2 * size_z), BF16)
    done = 0
    for x in range(0, size_x, 2):
        while done < x + 4:
            shifted_plane(done, refs, halo, g3)
            done += 1
        for plane_x in (x, x + 1):
            value = x_ref[plane_x]
            for b in range(3):
                at = slice(b * channels, (b + 1) * channels)
                start = (2 - b) * size_z
                x3[plane_x, at, start : start + plane] = value
                if start:
                    x3[plane_x, at, :start] = zero[:, :start]
                if start < 2 * size_z:
                    x3[plane_x, at, start + plane :] = zero[:, start:]
        product = lax.dot_general(
            jnp.concatenate(
                [g3[x * group : (x + 3) * group, :], g3[(x + 1) * group : (x + 4) * group, :]],
                axis=1,
            ),
            jnp.concatenate([x3[x], x3[x + 1]], axis=1),
            (((1,), (1,)), ((), ())),
            preferred_element_type=F32,
        )
        if x == 0:
            acc[...] = product
        else:
            acc[...] += product


def to_flat(value, count, channels, flat):
    height, width = value.shape
    wide = value
    if height % LANES:
        wide = jnp.concatenate([wide, jnp.zeros((-height % LANES, width), F32)], axis=0)
    if width % LANES:
        wide = jnp.concatenate([wide, jnp.zeros((wide.shape[0], -width % LANES), F32)], axis=1)
    turned = wide.T
    for b in range(3):
        rows = turned[b * channels : (b + 1) * channels]
        for block in range(9):
            start = block * count
            cell = rows[:, start // LANES * LANES : (start // LANES + 1) * LANES]
            tap = (2 - block // 3) * 9 + b * 3 + 2 - block % 3
            shift = -start % LANES
            flat[pl.ds(tap, channels, stride=27), :] = pltpu.roll(cell, shift, 1) if shift else cell
    return flat[...].T[:count]


def spread_weights(whole, turned, weights):
    channels, taps = whole.shape
    group = 3 * channels
    whole = jnp.concatenate([whole, jnp.zeros((LANES - channels, taps), F32)], axis=0)
    whole = jnp.concatenate([whole, jnp.zeros((LANES, -taps % LANES), F32)], axis=1)
    turned[...] = whole.T
    for b in range(3):
        blocks = []
        for a in range(3):
            for c in range(3):
                tap = (2 - a) * 9 + (2 - b) * 3 + 2 - c
                blocks.append(turned[pl.ds(tap, channels, stride=27), :][:, :channels])
        zero = jnp.zeros((channels, group), F32)
        weights[b, :channels] = jnp.concatenate(blocks + [zero], axis=1).astype(BF16)
        weights[b, channels:] = jnp.concatenate([zero] + blocks, axis=1).astype(BF16)


def input_products(refs, halo, g3, weights, tile, out_ref):
    channels, size_x, size_y, size_z = out_ref.shape
    group = 3 * channels
    plane = size_y * size_z
    done = 0
    for pair in range(size_x // 2):
        while done < 2 * pair + 4:
            shifted_plane(done, refs, halo, g3)
            done += 1
        at = slice(2 * pair * group, (2 * pair + 4) * group)
        total = None
        for b in range(3):
            product = jnp.dot(
                weights[b],
                g3[at, b * size_z : b * size_z + plane],
                preferred_element_type=F32,
            )
            total = product if total is None else total + product
        for half in range(2):
            for y in range(size_y):
                tile[half, pl.ds(y, channels, stride=size_y), :] = total[
                    half * channels : (half + 1) * channels, y * size_z : (y + 1) * size_z
                ]
            out_ref[:, 2 * pair + half] = (
                tile[half].reshape(channels, size_y, size_z).astype(BF16)
            )


def g3_scratch(channels, size_x, size_y, size_z):
    return pltpu.VMEM(((size_x + 2) * 3 * channels, (size_y + 2) * size_z), BF16)


def x3_scratch(channels, size_x, size_y, size_z):
    return pltpu.VMEM((size_x, 3 * channels, (size_y + 2) * size_z), BF16)


def acc_scratch(channels):
    return pltpu.VMEM((9 * channels, 3 * channels), F32)


def flat_scratch(channels):
    return pltpu.VMEM((-(-27 * channels // LANES) * LANES, LANES), F32)


def dgrad_scratch(channels, size_x, size_y, size_z):
    return [
        g3_scratch(channels, size_x, size_y, size_z),
        flat_scratch(channels),
        pltpu.VMEM((3, 2 * channels, 12 * channels), BF16),
        pltpu.VMEM((2, channels * size_y, size_z), F32),
    ]


def wgrad_cost(channels, size_x, size_y, size_z):
    return cost(54 * channels * channels * size_x * (size_y + 2) * size_z, 4 * 2**20)


def dgrad_cost(channels, size_x, size_y, size_z):
    return cost(72 * channels * channels * size_x * size_y * size_z, 4 * 2**20)


def row_for_other(body, size_z):
    plane = body.shape[-1]
    low, high = body[:, :size_z].astype(F32), body[:, plane - size_z :].astype(F32)
    return jnp.where(lax.axis_index("gy") == 0, high, low).astype(BF16)


def pair_inner_kernel(rows, *refs):
    first_ref, last_ref, m_ref, g_ref, side_ref, swap_ref, sent_ref = refs[2:9]
    sent_buf, sent_sem = refs[13:]
    choose(is_odd("gx"), swap_ref, first_ref, last_ref)
    share = m_ref[...]
    share = jnp.concatenate(
        [share, jnp.zeros((-share.shape[0] % QUAD, share.shape[1]), F32)], axis=0
    )

    def write(at, quad):
        quad = quad.astype(BF16)
        sent_buf[:, :, at] = jnp.broadcast_to(quad[None], (sent_buf.shape[0], *quad.shape))

    to_quads(share, write)
    send = pltpu.make_async_copy(sent_buf, sent_ref, sent_sem)
    send.start()
    read_inner(rows, *refs[:2], g_ref, *refs[9:13])
    size_z = side_ref.shape[-1]
    inner, _, plane = g_ref.shape
    size_x = inner + 2
    bodies = [first_ref] + [g_ref.at[x] for x in range(inner)] + [last_ref]
    for x, body in enumerate(bodies):
        side_ref[x] = row_for_other(body, size_z)
    low, high = z_tiles(
        [body[...] for body in bodies], plane // size_z, size_z, range(1, size_x + 1)
    )
    side_ref[size_x] = low.astype(BF16)
    side_ref[size_x + 1] = high.astype(BF16)
    send.wait()


def pair_inner(preact, upstream, first, last, share, sent_shape, rows):
    shape = preact.shape
    channels, size_x, _, size_z = shape
    return pl.pallas_call(
        functools.partial(pair_inner_kernel, rows),
        in_specs=[HBM] * 2 + [VMEM] * 3,
        out_specs=[VMEM] * 3 + [HBM],
        out_shape=[
            inner_output(*shape),
            jax.ShapeDtypeStruct((size_x + 2, channels, size_z), BF16),
            jax.ShapeDtypeStruct(first.shape, BF16),
            jax.ShapeDtypeStruct(sent_shape, BF16),
        ],
        scratch_shapes=inner_scratch(*shape)
        + [pltpu.VMEM(sent_shape, BF16), pltpu.SemaphoreType.DMA(())],
        compiler_params=params(INNER_VMEM),
        cost_estimate=cost(0, 4 * 2**20),
        name="inner",
    )(preact, upstream, first, last, share)


def is_odd(axis):
    return lax.rem(lax.axis_index(axis), 2) == 1


def either(condition, first, second):
    return jnp.where(condition, first.astype(F32), second.astype(F32))


def side_kernel(odd_ref, even_ref, own_ref, sent_ref, xlo_ref, xhi_ref):
    size_x = own_ref.shape[0] - 2
    size_z = own_ref.shape[-1]
    size_y = xlo_ref.shape[-1] // size_z
    odd = is_odd("gx")
    low = either(odd, even_ref[...], odd_ref[...]).astype(BF16)
    high = either(odd, odd_ref[...], even_ref[...]).astype(BF16)
    xlo_ref[...] = low
    xhi_ref[...] = high
    sent_ref[0] = row_for_other(low, size_z)
    for x in range(size_x):
        sent_ref[x + 1] = own_ref[x]
    sent_ref[size_x + 1] = row_for_other(high, size_z)
    lane = lax.broadcasted_iota(jnp.int32, (low.shape[0], LANES), 1)
    first, second = own_ref[size_x], own_ref[size_x + 1]
    for number, plane in ((0, low), (size_x + 1, high)):
        for y in range(size_y):
            at = number * size_y + y
            head = plane[:, y * size_z : y * size_z + LANES]
            tail = plane[:, (y + 1) * size_z - LANES : (y + 1) * size_z]
            first = jnp.where(lane == at, pltpu.roll(head, at, 1), first)
            second = jnp.where(lane == at, pltpu.roll(tail, at + 1, 1), second)
    sent_ref[size_x + 2] = first
    sent_ref[size_x + 3] = second


def side(halves, own):
    plane = jax.ShapeDtypeStruct(halves[0].shape, BF16)
    return pl.pallas_call(
        side_kernel,
        in_specs=[VMEM] * 3,
        out_specs=[VMEM] * 3,
        out_shape=[
            jax.ShapeDtypeStruct((own.shape[0] + 2, *own.shape[1:]), BF16),
            plane,
            plane,
        ],
        compiler_params=params(),
        cost_estimate=cost(2**25, 2**19),
        name="side",
    )(*halves, own)


def own_columns(columns, number, area):
    me = lax.axis_index("gy")
    value = columns.astype(F32)
    lane = lax.broadcasted_iota(jnp.int32, value.shape, 1)
    first = pltpu.roll(value, -number * area % LANES, 1)
    second = pltpu.roll(value, (1 - number) * area % LANES, 1)
    first = jnp.where(lane < area, first, 0.0)
    second = jnp.where((lane >= area) & (lane < 2 * area), second, 0.0)
    return jnp.where(me == 0, first, second)


def join_kernel(area, own_ref, other_ref, columns_ref, even_ref, odd_ref):
    at = own_ref.shape[0] - 2
    me = lax.axis_index("gy")
    last = own_columns(columns_ref[...], 1, area).astype(BF16)

    def fill(up_ref, down_ref):
        for k, out_ref in enumerate((down_ref, up_ref)):
            out_ref[me] = own_ref[at + k]
            out_ref[1 - me] = other_ref[at + k]
        up_ref[2] = last
        down_ref[2] = last

    odd = is_odd("gz")

    @pl.when(odd)
    def _():
        fill(odd_ref, even_ref)

    @pl.when(jnp.logical_not(odd))
    def _():
        fill(even_ref, odd_ref)


def join(own, other, columns, area):
    return pl.pallas_call(
        functools.partial(join_kernel, area),
        in_specs=[VMEM] * 3,
        out_specs=[VMEM] * 2,
        out_shape=[jax.ShapeDtypeStruct((3, *own.shape[1:]), BF16)] * 2,
        compiler_params=params(),
        cost_estimate=cost(0, 2**17),
        name="join",
    )(own, other, columns)


def pair_wgrad_kernel(*refs):
    x_ref, acc_ref, g3, x3 = refs[7:]
    weight_products(refs, None, x_ref, g3, x3, acc_ref)


def pair_wgrad(sources, planes_x, shape):
    channels = shape[0]
    return pl.pallas_call(
        pair_wgrad_kernel,
        in_specs=[VMEM] * 8,
        out_specs=VMEM,
        out_shape=jax.ShapeDtypeStruct((9 * channels, 3 * channels), F32),
        scratch_shapes=[g3_scratch(*shape), x3_scratch(*shape)],
        compiler_params=params(32 * 2**20),
        cost_estimate=wgrad_cost(*shape),
        name="wgrad",
    )(*sources, planes_x)


def finish_kernel(scale, rows, sizes, *refs):
    acc_ref, columns_ref, even_ref, odd_ref, from_odd_ref, from_even_ref = refs[:6]
    part_ref, chunks = refs[6:]
    size_x, size_y = sizes
    channels = columns_ref.shape[0]
    area = size_x * size_y
    odd = is_odd("gz")
    lane = lax.broadcasted_iota(jnp.int32, (channels, LANES), 1)
    row = lane % size_y
    jump = area - size_y + 1
    below = [either(odd, from_even_ref[k], from_odd_ref[k]) for k in range(3)]
    own = [either(odd, even_ref[k], odd_ref[k]) for k in range(2)]
    pairs = ((below[:2], own_columns(columns_ref[...], 0, area)), (own, below[2]))
    edges = []
    for tiles, value in pairs:
        before = jnp.where(lane >= area, pltpu.roll(value, jump, 1), 0.0)
        after = jnp.where(lane < area, pltpu.roll(value, LANES - jump, 1), 0.0)
        right = jnp.concatenate(
            [
                jnp.where(row > 0, pltpu.roll(value, 1, 1), before),
                value,
                jnp.where(row < size_y - 1, pltpu.roll(value, LANES - 1, 1), after),
            ],
            axis=0,
        )
        left = []
        for a in range(3):
            first = pltpu.roll(tiles[0], -a * size_y % LANES, 1)
            second = pltpu.roll(tiles[1], (area - a * size_y) % LANES, 1)
            left.append(jnp.where(lane < area, first, jnp.where(lane < 2 * area, second, 0.0)))
        edges.append(
            lax.dot_general(
                jnp.concatenate(left, axis=0).astype(BF16),
                right.astype(BF16),
                (((1,), (1,)), ((), ())),
                preferred_element_type=F32,
            )
        )
    count = part_ref.shape[0]
    height, width = chunks.shape[0] // count, LANES
    chunks[...] = jnp.zeros_like(chunks)
    pieces = rows * acc_ref.shape[1] // width
    for a in range(3):
        for c in range(3):
            at = 3 * a + c
            block = acc_ref[at * channels : (at + 1) * channels, :]
            if c != 1:
                block = block + edges[c // 2][a * channels : (a + 1) * channels]
            block = block * scale
            line = jnp.concatenate(
                [block[r * count : (r + 1) * count] for r in range(rows)], axis=1
            )
            for k in range(pieces):
                chunks[pl.ds(at * pieces + k, count, stride=height), :] = line[
                    :, k * width : (k + 1) * width
                ]

    def write(at, quads):
        part_ref[:, :, at] = quads.astype(BF16)

    whole = chunks[...].reshape(count, height, width)
    to_quads(whole[:, : part_ref.shape[2] // LANES * QUAD], write)


def finish(acc, columns, sent, received, scale, rows, sizes, part_shape):
    channels = columns.shape[0]
    return pl.pallas_call(
        functools.partial(finish_kernel, scale, rows, sizes),
        in_specs=[VMEM] * 6,
        out_specs=VMEM,
        out_shape=jax.ShapeDtypeStruct(part_shape, BF16),
        scratch_shapes=[
            pltpu.VMEM((part_shape[0] * -(-part_shape[2] // LANES * QUAD // 8) * 8, LANES), F32),
        ],
        compiler_params=params(),
        cost_estimate=cost(2**27, 2**21),
        name="finish",
    )(acc, columns, *sent, *received)


def adam_step(master, first, second, weight_grad):
    new_first = 0.9 * first + 0.1 * weight_grad
    new_second = 0.999 * second + 0.001 * weight_grad * weight_grad
    corr_first = 1.0 - (0.9**10) ** 10
    corr_second = 1.0 - (0.999**10) ** 10
    update = new_first / corr_first / (jnp.sqrt(new_second / corr_second) + 1e-08) + 0.01 * master
    return master - 0.05 * update, new_first, new_second


def in_flat_order(value, rows, places, spread_rows):
    taps = 27
    lane = lax.broadcasted_iota(jnp.int32, (9, LANES), 1)
    for k in range(value.shape[1] // LANES):
        rows[k * QUAD : (k + 1) * QUAD, :] = value[:, k * LANES : (k + 1) * LANES]
    thirds = [rows[pl.ds(k, 9, stride=3), :] for k in range(3)]
    half = LANES // 2
    by_y = (
        jnp.where(lane < half, thirds[0], thirds[1]),
        jnp.where(lane < half, pltpu.roll(thirds[0], half, 1), pltpu.roll(thirds[2], half, 1)),
        jnp.where(lane < half, thirds[1], thirds[2]),
    )
    places[...] = jnp.zeros_like(places)
    for b in range(3):
        spread_rows[b, :9, :] = by_y[b]
        for block in range(9):
            tap = (2 - block // 3) * 9 + b * 3 + 2 - block % 3
            places[tap : tap + 1, :] = spread_rows[b, block : block + 1, :]
    line = places[...].T
    number = lax.broadcasted_iota(jnp.int32, (LANES, LANES), 0) * taps
    column = lax.broadcasted_iota(jnp.int32, (LANES, LANES), 1)
    turned = []
    for group in range(LANES // 8):
        piece = line[8 * group : 8 * (group + 1)]
        rest = 8 * group * taps % LANES
        for step in range(3):
            turn = rest // (3 - step)
            rest -= turn
            piece = pltpu.roll(piece, turn, 1, stride=taps // 3, stride_axis=0)
        turned.append(piece)
    line = jnp.concatenate(turned, axis=0)
    start = number & (LANES - 1)
    line = jnp.concatenate(
        [jnp.where(column >= start, line, 0.0), jnp.where(column < start, line, 0.0)], axis=0
    )
    target = lax.broadcasted_iota(jnp.int32, (32, 2 * LANES), 0)
    source = lax.broadcasted_iota(jnp.int32, (32, 2 * LANES), 1)
    goes = lax.shift_right_logical((source & (LANES - 1)) * taps, 7)
    goes = goes + jnp.where(source < LANES, 0, 1)
    pick = jnp.where(goes == target, 1.0, 0.0).astype(BF16)
    parts = []
    for _ in range(3):
        parts.append(line.astype(BF16))
        line = line - parts[-1].astype(F32)
    return jnp.dot(
        jnp.concatenate([pick] * 3, axis=1),
        jnp.concatenate(parts, axis=0),
        preferred_element_type=F32,
    )[:taps]


def adam_kernel(parts_ref, master_ref, first_ref, second_ref, *refs):
    out_refs, scratch = refs[:4], refs[4:]
    total = parts_ref[0].astype(F32)
    for source in range(1, parts_ref.shape[0]):
        total = total + parts_ref[source].astype(F32)
    weight_grad = in_flat_order(total, *scratch)
    results = adam_step(master_ref[...], first_ref[...], second_ref[...], weight_grad)
    for out_ref, result in zip(out_refs, (weight_grad, *results)):
        out_ref[...] = result


def adam(parts, *states):
    share = states[0].shape[0]
    tiled = [state.reshape(share // LANES, LANES) for state in states]
    result = jax.ShapeDtypeStruct(tiled[0].shape, F32)
    outs = pl.pallas_call(
        adam_kernel,
        in_specs=[VMEM] * 4,
        out_specs=[VMEM] * 4,
        out_shape=[result] * 4,
        scratch_shapes=[
            pltpu.VMEM((32, LANES), F32),
            pltpu.VMEM((LANES, LANES), F32),
            pltpu.VMEM((3, 16, LANES), F32),
        ],
        compiler_params=params(),
        cost_estimate=cost(2**22, 2**19),
        name="adam",
    )(parts, *tiled)
    return tuple(out.reshape(share) for out in outs)


def spread_kernel(rows, w_ref, weights_ref, turned, chunks):
    count = w_ref.shape[0]
    height = chunks.shape[0] // count
    taps = 27 * rows * count
    quads = [
        w_ref[:, :, k * LANES : (k + 1) * LANES].astype(F32)
        for k in range(w_ref.shape[2] // LANES)
    ]
    spare = jnp.zeros((count, height - QUAD * len(quads), LANES), F32)
    chunks[...] = jnp.concatenate(quads + [spare], axis=1).reshape(chunks.shape)
    line = jnp.concatenate(
        [chunks[pl.ds(k, count, stride=height), :] for k in range(rows * taps // LANES)], axis=1
    )
    whole = jnp.concatenate([line[:, r * taps : (r + 1) * taps] for r in range(rows)], axis=0)
    spread_weights(whole, turned, weights_ref)


def spread(kernel, channels, rows):
    return pl.pallas_call(
        functools.partial(spread_kernel, rows),
        in_specs=[VMEM],
        out_specs=VMEM,
        out_shape=jax.ShapeDtypeStruct((3, 2 * channels, 12 * channels), BF16),
        scratch_shapes=[
            flat_scratch(channels),
            pltpu.VMEM((kernel.shape[0] * 32, LANES), F32),
        ],
        compiler_params=params(),
        cost_estimate=cost(2**20, 2**21),
        name="spread",
    )(kernel)


def pair_dgrad_kernel(*refs):
    weights_ref, out_ref, g3, tile = refs[9:]
    _, size_x, size_y, size_z = out_ref.shape
    halo = pair_z_halo(refs[7], refs[8], size_x + 2, size_y, size_z)
    input_products(refs, halo, g3, weights_ref, tile, out_ref)


def pair_dgrad(sources, weights, shape):
    channels, _, size_y, size_z = shape
    return pl.pallas_call(
        pair_dgrad_kernel,
        in_specs=[VMEM] * 10,
        out_specs=VMEM,
        out_shape=jax.ShapeDtypeStruct(shape, BF16),
        scratch_shapes=[g3_scratch(*shape), pltpu.VMEM((2, channels * size_y, size_z), F32)],
        compiler_params=params(32 * 2**20),
        cost_estimate=dgrad_cost(*shape),
        name="dgrad",
    )(*sources, weights)


def pair_program(activations, preact, upstream, master, first_moment, second_moment, scale):
    shape = activations.shape
    channels, size_x, size_y, _ = shape
    devices = math.prod(lax.axis_size(a) for a in AXES)
    rows = channels // devices
    used = master.shape[0] // LANES
    block = (devices, QUAD, -(-used // QUAD) * LANES)
    first, last, odd_sent = faces(preact, upstream, "gx", rows)
    odd_halves = swapped(odd_sent, "gx", 1)
    inner, own, even_sent, sent = pair_inner(
        preact, upstream, first, last, master.reshape(used, LANES), block, rows
    )
    even_halves = swapped(even_sent, "gx", 0)
    kernel = lax.all_to_all(sent, AXES, 0, 0, tiled=True)
    own, xlo, xhi = side((odd_halves, even_halves), own)
    planes = (xlo, first, inner, last, xhi)
    own, activations = lax.optimization_barrier((own, activations))
    other = shifted(own, {"gy": "swap"})
    planes_x, columns = input_planes(activations, True)
    z_sent = join(own, other, columns, size_x * size_y)
    from_odd = swapped(z_sent[1], "gz", 1)
    from_even = swapped(z_sent[0], "gz", 0)
    sources = (*planes, other, other)
    acc = pair_wgrad(sources, planes_x, shape)
    z_received = (from_odd, from_even)
    part = finish(acc, columns, z_sent, z_received, scale, rows, (size_x, size_y), block)
    part, kernel = lax.optimization_barrier((part, kernel))
    parts = lax.all_to_all(part, AXES, 0, 0, tiled=True)
    weights = spread(kernel, channels, rows)
    grad_input = pair_dgrad((*sources, *z_received), weights, shape)
    return grad_input, *adam(parts, master, first_moment, second_moment)


def yface_kernel(*refs):
    low_ref, high_ref = refs[5:]
    size_z = low_ref.shape[-1]
    for index in range(low_ref.shape[0]):
        body = body_of(refs[:5], index)
        plane = body.shape[-1]
        low_ref[index] = body[:, :size_z]
        high_ref[index] = body[:, plane - size_z :]


def y_faces(planes, size_z):
    inner, channels, _ = planes[2].shape
    face = jax.ShapeDtypeStruct((inner + 4, channels, size_z), BF16)
    return pl.pallas_call(
        yface_kernel,
        in_specs=[VMEM] * 5,
        out_specs=[VMEM] * 2,
        out_shape=[face] * 2,
        compiler_params=params(),
        cost_estimate=cost(0, 2**19),
        name="yfaces",
    )(*planes)


def zface_kernel(*refs):
    zlo_ref, zhi_ref = refs[7:]
    size_z = refs[5].shape[-1]
    whole = []
    for index in range(refs[5].shape[0]):
        low, high = y_halo(refs[5:7], index)
        body = body_of(refs[:5], index)[...]
        whole.append(jnp.concatenate([low.astype(BF16), body, high.astype(BF16)], axis=1))
    low, high = z_tiles(whole, whole[0].shape[1] // size_z, size_z, range(len(whole)))
    zlo_ref[...] = low.astype(BF16)
    zhi_ref[...] = high.astype(BF16)


def z_faces(planes, y_halos):
    face = jax.ShapeDtypeStruct((planes[0].shape[0], LANES), BF16)
    return pl.pallas_call(
        zface_kernel,
        in_specs=[VMEM] * 7,
        out_specs=[VMEM] * 2,
        out_shape=[face, face],
        compiler_params=params(),
        cost_estimate=cost(2**27, 2**21),
        name="zfaces",
    )(*planes, *y_halos)


def wgrad_kernel(scale, *refs):
    x_ref, part_ref, g3, x3, acc, flat = refs[9:]
    size_x, channels, plane = x_ref.shape
    size_z = refs[5].shape[-1]
    halo = z_halo(refs[7], refs[8], size_x + 2, plane // size_z + 2, size_z)
    weight_products(refs, halo, x_ref, g3, x3, acc)
    whole = to_flat(acc[...] * scale, channels, channels, flat)
    part_ref[...] = whole[:, : part_ref.shape[1]].astype(BF16)


def wgrad(sources, planes_x, shape, scale):
    channels = shape[0]
    return pl.pallas_call(
        functools.partial(wgrad_kernel, scale),
        in_specs=[VMEM] * 10,
        out_specs=VMEM,
        out_shape=jax.ShapeDtypeStruct((channels, 27 * channels), BF16),
        scratch_shapes=[
            g3_scratch(*shape),
            x3_scratch(*shape),
            acc_scratch(channels),
            flat_scratch(channels),
        ],
        compiler_params=params(32 * 2**20),
        cost_estimate=wgrad_cost(*shape),
        name="wgrad",
    )(*sources, planes_x)


def dgrad_kernel(*refs):
    w_ref, out_ref, g3, turned, weights, tile = refs[9:]
    _, size_x, size_y, size_z = out_ref.shape
    spread_weights(w_ref[...].astype(F32), turned, weights)
    halo = z_halo(refs[7], refs[8], size_x + 2, size_y + 2, size_z)
    input_products(refs, halo, g3, weights, tile, out_ref)


def dgrad(sources, kernel, shape):
    return pl.pallas_call(
        dgrad_kernel,
        in_specs=[VMEM] * 10,
        out_specs=VMEM,
        out_shape=jax.ShapeDtypeStruct(shape, BF16),
        scratch_shapes=dgrad_scratch(*shape),
        compiler_params=params(32 * 2**20),
        cost_estimate=dgrad_cost(*shape),
        name="dgrad",
    )(*sources, kernel)


def general_program(activations, preact, upstream, master, first_moment, second_moment, scale):
    shape = activations.shape
    channels, _, _, size_z = shape
    devices = math.prod(lax.axis_size(a) for a in AXES)
    share = master.shape[0]
    first, last = faces(preact, upstream)
    x_halos = (shifted(last, {"gx": 1}), shifted(first, {"gx": -1}))
    inner = inner_planes(preact, upstream)
    (planes_x,) = input_planes(activations, False)
    sent = jnp.broadcast_to(master.astype(BF16).reshape(1, 1, share), (devices, 1, share))
    kernel = lax.all_to_all(sent, AXES, 0, 0, tiled=True).reshape(channels, 27 * channels)
    planes = (x_halos[0], first, inner, last, x_halos[1])
    y_sent = y_faces(planes, size_z)
    y_halos = (shifted(y_sent[1], {"gy": 1}), shifted(y_sent[0], {"gy": -1}))
    zlo, zhi = z_faces(planes, y_halos)
    z_halos = (shifted(zhi, {"gz": 1}), shifted(zlo, {"gz": -1}))
    sources = (*planes, *y_halos, *z_halos)
    part = wgrad(sources, planes_x, shape, scale)
    part, kernel = lax.optimization_barrier((part, kernel))
    parts = lax.all_to_all(part.reshape(devices, 1, share), AXES, 0, 0, tiled=True)
    grad_input = dgrad(sources, kernel, shape)
    weight_grad = jnp.sum(parts.astype(F32), axis=0).reshape(-1)
    results = adam_step(master, first_moment, second_moment, weight_grad)
    return grad_input, weight_grad, *results


def shifted(value, moves):
    names = tuple(moves)
    sizes = [lax.axis_size(name) for name in names]
    pairs = []
    for source in range(math.prod(sizes)):
        rest, coords = source, []
        for size in reversed(sizes):
            coords.insert(0, rest % size)
            rest //= size
        coords = [
            (at + moves[name]) if moves[name] != "swap" else 1 - at
            for at, name in zip(coords, names)
        ]
        if all(0 <= at < size for at, size in zip(coords, sizes)):
            target = 0
            for at, size in zip(coords, sizes):
                target = target * size + at
            pairs.append((source, target))
    return lax.ppermute(value, names if len(names) > 1 else names[0], pairs)


def swapped(value, axis, start):
    pairs = []
    for low in range(start, lax.axis_size(axis) - 1, 2):
        pairs += [(low, low + 1), (low + 1, low)]
    return lax.ppermute(value, axis, pairs)


def local(activations, preact, upstream, master, first_moment, second_moment):
    channels, size_x, size_y, size_z = activations.shape
    devices = math.prod(lax.axis_size(a) for a in AXES)
    share = master.shape[0]
    scale = 1.0 / math.sqrt(size_x * size_y * size_z * devices)
    in_pairs = (
        lax.axis_size("gy") == 2
        and channels % devices == 0
        and share % LANES == 0
        and channels // devices * channels == LANES
        and 2 * size_x * size_y <= LANES
        and (size_x + 2) * size_y <= LANES
    )
    program = pair_program if in_pairs else general_program
    return program(
        activations, preact, upstream, master, first_moment, second_moment, scale
    )


def solution(mesh):
    volume = P(None, "gx", "gy", "gz")
    flat = P(AXES)
    return jax.shard_map(
        local,
        mesh=mesh,
        in_specs=(volume, volume, volume, flat, flat, flat),
        out_specs=(volume, flat, flat, flat, flat),
        check_vma=False,
    )
```

```python
import functools
import math

import jax
import jax.numpy as jnp
from jax import lax
from jax.experimental import pallas as pl
from jax.experimental.pallas import tpu as pltpu
from jax.sharding import PartitionSpec as P

AXES = ("gx", "gy", "gz")
LANES = 128
VMEM = pl.BlockSpec(memory_space=pltpu.VMEM)
HBM = pl.BlockSpec(memory_space=pltpu.HBM)
F32 = jnp.float32
BF16 = jnp.bfloat16
FACES_VMEM = 55_900_000
INNER_VMEM = 54_800_000
ENDS_VMEM = 54_800_000
MIDDLES_VMEM = 53_600_000


def params(limit=24 * 2**20):
    return pltpu.CompilerParams(vmem_limit_bytes=limit)


def cost(flops, moved):
    return pl.CostEstimate(flops=flops, bytes_accessed=moved, transcendentals=0)


def to_planes(value, tile, write, rows=1):
    channels, size_y, size_z = value.shape
    count = channels // rows
    tile[...] = value.astype(F32).reshape(channels * size_y, size_z)
    for y in range(size_y):
        for r in range(rows):
            picked = tile[pl.ds(r * size_y + y, count, stride=rows * size_y), :]
            write(slice(r * count, (r + 1) * count), y, picked.astype(BF16))


QUAD = 4


def to_quads(rows, write):
    for k in range(rows.shape[-2] // QUAD):
        write(slice(k * LANES, (k + 1) * LANES), rows[..., k * QUAD : (k + 1) * QUAD, :])


def masked(p, u):
    return jnp.where(p > 0, u, jnp.zeros_like(u))


def choose(condition, out_ref, first_ref, second_ref):
    @pl.when(condition)
    def _():
        out_ref[...] = first_ref[...]

    @pl.when(jnp.logical_not(condition))
    def _():
        out_ref[...] = second_ref[...]


def face_kernel(axis, rows, p_ref, u_ref, *refs):
    p_buf, u_buf, tile, sems = refs[-4:]
    out_refs, swap_refs = refs[:2], refs[2:-4]
    size_x, size_z = p_ref.shape[1], p_ref.shape[3]
    copies = []
    for k, x in enumerate((0, size_x - 1)):
        pair = (
            pltpu.make_async_copy(p_ref.at[:, x], p_buf.at[k], sems.at[2 * k]),
            pltpu.make_async_copy(u_ref.at[:, x], u_buf.at[k], sems.at[2 * k + 1]),
        )
        for copy in pair:
            copy.start()
        copies.append(pair)
    for k, out_ref in enumerate(out_refs):
        for copy in copies[k]:
            copy.wait()

        def write(at, y, value):
            out_ref[at, y * size_z : (y + 1) * size_z] = value

        to_planes(masked(p_buf[k], u_buf[k]), tile.at[k], write, rows)
    if axis is not None:
        choose(is_odd(axis), swap_refs[0], out_refs[1], out_refs[0])


def faces(preact, upstream, axis=None, rows=1):
    channels, size_x, size_y, size_z = preact.shape
    face = jax.ShapeDtypeStruct((channels, size_y * size_z), BF16)
    buffer = pltpu.VMEM((2, channels, size_y, size_z), BF16)
    count = 2 if axis is None else 3
    return pl.pallas_call(
        functools.partial(face_kernel, axis, rows),
        in_specs=[HBM, HBM],
        out_specs=[VMEM] * count,
        out_shape=[face] * count,
        scratch_shapes=[
            buffer,
            buffer,
            pltpu.VMEM((2, channels * size_y, size_z), F32),
            pltpu.SemaphoreType.DMA((4,)),
        ],
        compiler_params=params(FACES_VMEM),
        cost_estimate=cost(0, 2**20),
        name="faces",
    )(preact, upstream)


def read_inner(rows, p_ref, u_ref, g_ref, p_buf, u_buf, tile, sems):
    size_x, size_z = p_ref.shape[1], p_ref.shape[3]
    inner = size_x - 2
    copies = []
    for x in range(inner):
        pair = (
            pltpu.make_async_copy(p_ref.at[:, x + 1], p_buf.at[x], sems.at[x]),
            pltpu.make_async_copy(u_ref.at[:, x + 1], u_buf.at[x], sems.at[inner + x]),
        )
        for copy in pair:
            copy.start()
        copies.append(pair)
    for x in range(inner):
        for copy in copies[x]:
            copy.wait()

        def write(at, y, value):
            g_ref[x, at, y * size_z : (y + 1) * size_z] = value

        to_planes(masked(p_buf[x], u_buf[x]), tile.at[x % 2], write, rows)


def inner_kernel(*refs):
    read_inner(1, *refs)


def inner_output(channels, size_x, size_y, size_z):
    return jax.ShapeDtypeStruct((size_x - 2, channels, size_y * size_z), BF16)


def inner_scratch(channels, size_x, size_y, size_z):
    return [
        pltpu.VMEM((size_x - 2, channels, size_y, size_z), BF16),
        pltpu.VMEM((size_x - 2, channels, size_y, size_z), BF16),
        pltpu.VMEM((2, channels * size_y, size_z), F32),
        pltpu.SemaphoreType.DMA((2 * size_x - 4,)),
    ]


def inner_planes(preact, upstream):
    shape = preact.shape
    return pl.pallas_call(
        inner_kernel,
        in_specs=[HBM] * 2,
        out_specs=VMEM,
        out_shape=inner_output(*shape),
        scratch_shapes=inner_scratch(*shape),
        compiler_params=params(INNER_VMEM),
        cost_estimate=cost(0, 4 * 2**20),
        name="inner",
    )(preact, upstream)


def input_kernel(a_ref, x_ref, *refs):
    tile = refs[-1]
    channels, size_x, size_y, size_z = a_ref.shape
    for x in range(size_x):

        def write(at, y, value):
            x_ref[x, at, y * size_z : (y + 1) * size_z] = value

        to_planes(a_ref[:, x], tile.at[x % 2], write)
    if len(refs) > 1:
        low, high = z_tiles([x_ref[x] for x in range(size_x)], size_y, size_z, range(size_x))
        refs[0][...] = (low + pltpu.roll(high, size_x * size_y, 1)).astype(BF16)


def input_planes(activations, with_columns):
    channels, size_x, size_y, size_z = activations.shape
    outs = [jax.ShapeDtypeStruct((size_x, channels, size_y * size_z), BF16)]
    if with_columns:
        outs.append(jax.ShapeDtypeStruct((channels, LANES), BF16))
    return pl.pallas_call(
        input_kernel,
        in_specs=[VMEM],
        out_specs=[VMEM] * len(outs),
        out_shape=outs,
        scratch_shapes=[pltpu.VMEM((2, channels * size_y, size_z), F32)],
        compiler_params=params(),
        cost_estimate=cost(0, 2 * 2**20),
        name="inputs",
    )(activations)


def body_of(refs, index):
    planes = refs[2].shape[0] + 4
    if 2 <= index < planes - 2:
        return refs[2].at[index - 2]
    return refs[{0: 0, 1: 1, planes - 2: 3, planes - 1: 4}[index]]


def y_halo(refs, index):
    me = lax.axis_index("gy")
    low = jnp.where(me > 0, refs[0][index].astype(F32), 0.0)
    high = jnp.where(me < lax.axis_size("gy") - 1, refs[1][index].astype(F32), 0.0)
    return low, high


def z_picker(rows_y, size_z):
    shape = (rows_y * size_z, 2 * LANES)
    voxel = lax.broadcasted_iota(jnp.int32, shape, 0)
    lane = lax.broadcasted_iota(jnp.int32, shape, 1)
    wanted = jnp.where(lane < LANES, lane * size_z, (lane - LANES) * size_z + size_z - 1)
    return (voxel == wanted).astype(F32).astype(BF16)


def z_tiles(planes, rows_y, size_z, numbers):
    channels = planes[0].shape[0]
    columns = jnp.dot(
        jnp.concatenate(planes, axis=0), z_picker(rows_y, size_z), preferred_element_type=F32
    )
    low = jnp.zeros((channels, LANES), F32)
    high = jnp.zeros((channels, LANES), F32)
    for index, number in enumerate(numbers):
        rows = columns[index * channels : (index + 1) * channels]
        low = low + pltpu.roll(rows[:, :LANES], number * rows_y, 1)
        high = high + pltpu.roll(rows[:, LANES:], number * rows_y, 1)
    return low, high


def put_columns(columns, row_of, rows_y, size_z):
    shape = (2 * LANES, rows_y * size_z)
    source = lax.broadcasted_iota(jnp.int32, shape, 0)
    voxel = lax.broadcasted_iota(jnp.int32, shape, 1)
    number = source % LANES
    place = row_of(number) * size_z + jnp.where(source < LANES, 0, size_z - 1)
    place = jnp.where(number < rows_y, place, -1)
    put = (voxel == place).astype(F32).astype(BF16)
    rows = [jnp.concatenate(pair, axis=1) for pair in columns]
    return jnp.dot(
        jnp.concatenate(rows, axis=0).astype(BF16), put, preferred_element_type=F32
    ).astype(BF16)


def z_halo(low_ref, high_ref, planes, rows_y, size_z):
    columns = []
    for index in range(planes):
        shift = -index * rows_y % LANES
        columns.append(
            [pltpu.roll(ref[...].astype(F32), shift, 1) for ref in (low_ref, high_ref)]
        )
    return put_columns(columns, lambda number: number, rows_y, size_z)


def pair_z_halo(odd_ref, even_ref, planes, size_y, size_z):
    me, odd = lax.axis_index("gy"), is_odd("gz")
    sides = []
    for low, high in ((even_ref, odd_ref), (odd_ref, even_ref)):
        first, second = (either(odd, low[k], high[k]) for k in range(2))
        lane = lax.broadcasted_iota(jnp.int32, first.shape, 1)
        own = jnp.where(me == 0, first, second)
        before = jnp.where(me == 0, 0.0, first)
        after = jnp.where(me == 0, second, 0.0)
        columns = []
        for index in range(planes):
            start = index * size_y
            columns.append(
                jnp.where(
                    lane < size_y,
                    pltpu.roll(own, -start % LANES, 1),
                    jnp.where(
                        lane == size_y,
                        pltpu.roll(before, (1 - start) % LANES, 1),
                        pltpu.roll(after, (size_y + 1 - start) % LANES, 1),
                    ),
                )
            )
        sides.append(columns)

    def row_of(number):
        return jnp.where(number < size_y, number + 1, jnp.where(number == size_y, 0, size_y + 1))

    return put_columns(list(zip(*sides)), row_of, size_y + 2, size_z)


def shifted_plane(index, refs, halo, g3):
    channels, plane = refs[0].shape
    size_z = refs[5].shape[-1]
    rows_y = plane // size_z + 2
    base = 3 * channels * index
    lane = lax.broadcasted_iota(jnp.int32, (channels, size_z), 1)
    is_first, is_last = lane == 0, lane == size_z - 1
    low, high = y_halo(refs[5:7], index)
    body = body_of(refs[:5], index)
    for row in range(rows_y):
        cols = slice(row * size_z, (row + 1) * size_z)
        if row == 0:
            value = low.astype(BF16)
        elif row == rows_y - 1:
            value = high.astype(BF16)
        else:
            value = body[:, (row - 1) * size_z : row * size_z]
        if halo is None:
            edge = jnp.zeros_like(value)
        else:
            edge = halo[index * channels : (index + 1) * channels, cols]
        before = jnp.where(is_first, edge, pltpu.roll(value, 1, 1))
        after = jnp.where(is_last, edge, pltpu.roll(value, size_z - 1, 1))
        g3[base : base + channels, cols] = before
        g3[base + channels : base + 2 * channels, cols] = value
        g3[base + 2 * channels : base + 3 * channels, cols] = after


def weight_products(refs, halo, x_ref, g3, x3, acc):
    size_x, channels, plane = x_ref.shape
    size_z = refs[5].shape[-1]
    group = 3 * channels
    zero = jnp.zeros((channels, 2 * size_z), BF16)
    done = 0
    for x in range(0, size_x, 2):
        while done < x + 4:
            shifted_plane(done, refs, halo, g3)
            done += 1
        for plane_x in (x, x + 1):
            value = x_ref[plane_x]
            for b in range(3):
                at = slice(b * channels, (b + 1) * channels)
                start = (2 - b) * size_z
                x3[plane_x, at, start : start + plane] = value
                if start:
                    x3[plane_x, at, :start] = zero[:, :start]
                if start < 2 * size_z:
                    x3[plane_x, at, start + plane :] = zero[:, start:]
        product = lax.dot_general(
            jnp.concatenate(
                [g3[x * group : (x + 3) * group, :], g3[(x + 1) * group : (x + 4) * group, :]],
                axis=1,
            ),
            jnp.concatenate([x3[x], x3[x + 1]], axis=1),
            (((1,), (1,)), ((), ())),
            preferred_element_type=F32,
        )
        if x == 0:
            acc[...] = product
        else:
            acc[...] += product


def to_flat(value, count, channels, flat):
    height, width = value.shape
    wide = value
    if height % LANES:
        wide = jnp.concatenate([wide, jnp.zeros((-height % LANES, width), F32)], axis=0)
    if width % LANES:
        wide = jnp.concatenate([wide, jnp.zeros((wide.shape[0], -width % LANES), F32)], axis=1)
    turned = wide.T
    for b in range(3):
        rows = turned[b * channels : (b + 1) * channels]
        for block in range(9):
            start = block * count
            cell = rows[:, start // LANES * LANES : (start // LANES + 1) * LANES]
            tap = (2 - block // 3) * 9 + b * 3 + 2 - block % 3
            shift = -start % LANES
            flat[pl.ds(tap, channels, stride=27), :] = pltpu.roll(cell, shift, 1) if shift else cell
    return flat[...].T[:count]


def spread_weights(whole, turned, weights):
    channels, taps = whole.shape
    group = 3 * channels
    whole = jnp.concatenate([whole, jnp.zeros((LANES - channels, taps), F32)], axis=0)
    whole = jnp.concatenate([whole, jnp.zeros((LANES, -taps % LANES), F32)], axis=1)
    turned[...] = whole.T
    for b in range(3):
        blocks = []
        for a in range(3):
            for c in range(3):
                tap = (2 - a) * 9 + (2 - b) * 3 + 2 - c
                blocks.append(turned[pl.ds(tap, channels, stride=27), :][:, :channels])
        zero = jnp.zeros((channels, group), F32)
        weights[b, :channels] = jnp.concatenate(blocks + [zero], axis=1).astype(BF16)
        weights[b, channels:] = jnp.concatenate([zero] + blocks, axis=1).astype(BF16)


def input_products(refs, halo, g3, weights, tile, out_ref):
    channels, size_x, size_y, size_z = out_ref.shape
    group = 3 * channels
    plane = size_y * size_z
    done = 0
    for pair in range(size_x // 2):
        while done < 2 * pair + 4:
            shifted_plane(done, refs, halo, g3)
            done += 1
        at = slice(2 * pair * group, (2 * pair + 4) * group)
        total = None
        for b in range(3):
            product = jnp.dot(
                weights[b],
                g3[at, b * size_z : b * size_z + plane],
                preferred_element_type=F32,
            )
            total = product if total is None else total + product
        for half in range(2):
            for y in range(size_y):
                tile[half, pl.ds(y, channels, stride=size_y), :] = total[
                    half * channels : (half + 1) * channels, y * size_z : (y + 1) * size_z
                ]
            out_ref[:, 2 * pair + half] = (
                tile[half].reshape(channels, size_y, size_z).astype(BF16)
            )


def g3_scratch(channels, size_x, size_y, size_z):
    return pltpu.VMEM(((size_x + 2) * 3 * channels, (size_y + 2) * size_z), BF16)


def x3_scratch(channels, size_x, size_y, size_z):
    return pltpu.VMEM((size_x, 3 * channels, (size_y + 2) * size_z), BF16)


def acc_scratch(channels):
    return pltpu.VMEM((9 * channels, 3 * channels), F32)


def flat_scratch(channels):
    return pltpu.VMEM((-(-27 * channels // LANES) * LANES, LANES), F32)


def dgrad_scratch(channels, size_x, size_y, size_z):
    return [
        g3_scratch(channels, size_x, size_y, size_z),
        flat_scratch(channels),
        pltpu.VMEM((3, 2 * channels, 12 * channels), BF16),
        pltpu.VMEM((2, channels * size_y, size_z), F32),
    ]


def wgrad_cost(channels, size_x, size_y, size_z):
    return cost(54 * channels * channels * size_x * (size_y + 2) * size_z, 4 * 2**20)


def dgrad_cost(channels, size_x, size_y, size_z):
    return cost(72 * channels * channels * size_x * size_y * size_z, 4 * 2**20)


def row_for_other(body, size_z):
    plane = body.shape[-1]
    low, high = body[:, :size_z].astype(F32), body[:, plane - size_z :].astype(F32)
    return jnp.where(lax.axis_index("gy") == 0, high, low).astype(BF16)


def in_odd_swaps(axis):
    me, count = lax.axis_index(axis), lax.axis_size(axis)
    return (me > 0) & (me < count - 1 + count % 2)


def own_planes(order, p_ref, u_ref, first_ref, last_ref, g_ref, side_ref, *scratch):
    read_inner(order, p_ref, u_ref, g_ref, *scratch)
    size_z = side_ref.shape[-1]
    inner, _, plane = g_ref.shape
    size_x = inner + 2
    bodies = [first_ref] + [g_ref.at[x] for x in range(inner)] + [last_ref]
    for x, body in enumerate(bodies):
        side_ref[x] = row_for_other(body, size_z)
    low, high = z_tiles(
        [body[...] for body in bodies], plane // size_z, size_z, range(1, size_x + 1)
    )
    side_ref[size_x] = low.astype(BF16)
    side_ref[size_x + 1] = high.astype(BF16)


def ends_kernel(order, *refs):
    choose(is_odd("gx"), refs[6], refs[2], refs[3])

    @pl.when(jnp.logical_not(in_odd_swaps("gx")))
    def _():
        own_planes(order, *refs[:6], *refs[7:])


def middles_kernel(order, *refs):
    m_ref, g_before_ref, side_before_ref, g_ref, side_ref, sent_ref = refs[4:10]
    sent_buf, sent_sem = refs[14:]
    share = m_ref[...]
    share = jnp.concatenate(
        [share, jnp.zeros((-share.shape[0] % QUAD, share.shape[1]), F32)], axis=0
    )

    def write(at, quad):
        quad = quad.astype(BF16)
        sent_buf[:, :, at] = jnp.broadcast_to(quad[None], (sent_buf.shape[0], *quad.shape))

    to_quads(share, write)
    send = pltpu.make_async_copy(sent_buf, sent_ref, sent_sem)
    send.start()
    middle = in_odd_swaps("gx")

    @pl.when(middle)
    def _():
        own_planes(order, *refs[:4], g_ref, side_ref, *refs[10:14])

    @pl.when(jnp.logical_not(middle))
    def _():
        g_ref[...] = g_before_ref[...]
        side_ref[...] = side_before_ref[...]

    send.wait()


def pair_inner(preact, upstream, first, last, share, sent_shape, order):
    shape = preact.shape
    channels, size_x, _, size_z = shape
    made = [
        inner_output(*shape),
        jax.ShapeDtypeStruct((size_x + 2, channels, size_z), BF16),
    ]
    *before, swap = pl.pallas_call(
        functools.partial(ends_kernel, order),
        in_specs=[HBM] * 2 + [VMEM] * 2,
        out_specs=[VMEM] * 3,
        out_shape=made + [jax.ShapeDtypeStruct(first.shape, BF16)],
        scratch_shapes=inner_scratch(*shape),
        compiler_params=params(ENDS_VMEM),
        cost_estimate=cost(0, 2**20),
        name="ends",
    )(preact, upstream, first, last)
    g, side_rows, sent = pl.pallas_call(
        functools.partial(middles_kernel, order),
        in_specs=[HBM] * 2 + [VMEM] * 5,
        out_specs=[VMEM] * 2 + [HBM],
        out_shape=made + [jax.ShapeDtypeStruct(sent_shape, BF16)],
        scratch_shapes=inner_scratch(*shape)
        + [pltpu.VMEM(sent_shape, BF16), pltpu.SemaphoreType.DMA(())],
        compiler_params=params(MIDDLES_VMEM),
        cost_estimate=cost(0, 4 * 2**20),
        name="middles",
    )(preact, upstream, first, last, share, *before)
    return g, side_rows, swap, sent


def is_odd(axis):
    return lax.rem(lax.axis_index(axis), 2) == 1


def either(condition, first, second):
    return jnp.where(condition, first.astype(F32), second.astype(F32))


def side_kernel(odd_ref, even_ref, own_ref, sent_ref, xlo_ref, xhi_ref):
    size_x = own_ref.shape[0] - 2
    size_z = own_ref.shape[-1]
    size_y = xlo_ref.shape[-1] // size_z
    odd = is_odd("gx")
    low = either(odd, even_ref[...], odd_ref[...]).astype(BF16)
    high = either(odd, odd_ref[...], even_ref[...]).astype(BF16)
    xlo_ref[...] = low
    xhi_ref[...] = high
    sent_ref[0] = row_for_other(low, size_z)
    for x in range(size_x):
        sent_ref[x + 1] = own_ref[x]
    sent_ref[size_x + 1] = row_for_other(high, size_z)
    lane = lax.broadcasted_iota(jnp.int32, (low.shape[0], LANES), 1)
    first, second = own_ref[size_x], own_ref[size_x + 1]
    for number, plane in ((0, low), (size_x + 1, high)):
        for y in range(size_y):
            at = number * size_y + y
            head = plane[:, y * size_z : y * size_z + LANES]
            tail = plane[:, (y + 1) * size_z - LANES : (y + 1) * size_z]
            first = jnp.where(lane == at, pltpu.roll(head, at, 1), first)
            second = jnp.where(lane == at, pltpu.roll(tail, at + 1, 1), second)
    sent_ref[size_x + 2] = first
    sent_ref[size_x + 3] = second


def side(halves, own):
    plane = jax.ShapeDtypeStruct(halves[0].shape, BF16)
    return pl.pallas_call(
        side_kernel,
        in_specs=[VMEM] * 3,
        out_specs=[VMEM] * 3,
        out_shape=[
            jax.ShapeDtypeStruct((own.shape[0] + 2, *own.shape[1:]), BF16),
            plane,
            plane,
        ],
        compiler_params=params(),
        cost_estimate=cost(2**25, 2**19),
        name="side",
    )(*halves, own)


def own_columns(columns, number, area):
    me = lax.axis_index("gy")
    value = columns.astype(F32)
    lane = lax.broadcasted_iota(jnp.int32, value.shape, 1)
    first = pltpu.roll(value, -number * area % LANES, 1)
    second = pltpu.roll(value, (1 - number) * area % LANES, 1)
    first = jnp.where(lane < area, first, 0.0)
    second = jnp.where((lane >= area) & (lane < 2 * area), second, 0.0)
    return jnp.where(me == 0, first, second)


def join_kernel(area, own_ref, other_ref, columns_ref, even_ref, odd_ref):
    at = own_ref.shape[0] - 2
    me = lax.axis_index("gy")
    last = own_columns(columns_ref[...], 1, area).astype(BF16)

    def fill(up_ref, down_ref):
        for k, out_ref in enumerate((down_ref, up_ref)):
            out_ref[me] = own_ref[at + k]
            out_ref[1 - me] = other_ref[at + k]
        up_ref[2] = last
        down_ref[2] = last

    odd = is_odd("gz")

    @pl.when(odd)
    def _():
        fill(odd_ref, even_ref)

    @pl.when(jnp.logical_not(odd))
    def _():
        fill(even_ref, odd_ref)


def join(own, other, columns, area):
    return pl.pallas_call(
        functools.partial(join_kernel, area),
        in_specs=[VMEM] * 3,
        out_specs=[VMEM] * 2,
        out_shape=[jax.ShapeDtypeStruct((3, *own.shape[1:]), BF16)] * 2,
        compiler_params=params(),
        cost_estimate=cost(0, 2**17),
        name="join",
    )(own, other, columns)


def pair_wgrad_kernel(*refs):
    x_ref, acc_ref, g3, x3 = refs[7:]
    weight_products(refs, None, x_ref, g3, x3, acc_ref)


def pair_wgrad(sources, planes_x, shape):
    channels = shape[0]
    return pl.pallas_call(
        pair_wgrad_kernel,
        in_specs=[VMEM] * 8,
        out_specs=VMEM,
        out_shape=jax.ShapeDtypeStruct((9 * channels, 3 * channels), F32),
        scratch_shapes=[g3_scratch(*shape), x3_scratch(*shape)],
        compiler_params=params(32 * 2**20),
        cost_estimate=wgrad_cost(*shape),
        name="wgrad",
    )(*sources, planes_x)


def finish_kernel(scale, rows, sizes, *refs):
    acc_ref, columns_ref, even_ref, odd_ref, from_odd_ref, from_even_ref = refs[:6]
    part_ref, chunks = refs[6:]
    size_x, size_y = sizes
    channels = columns_ref.shape[0]
    area = size_x * size_y
    odd = is_odd("gz")
    lane = lax.broadcasted_iota(jnp.int32, (channels, LANES), 1)
    row = lane % size_y
    jump = area - size_y + 1
    below = [either(odd, from_even_ref[k], from_odd_ref[k]) for k in range(3)]
    own = [either(odd, even_ref[k], odd_ref[k]) for k in range(2)]
    pairs = ((below[:2], own_columns(columns_ref[...], 0, area)), (own, below[2]))
    edges = []
    for tiles, value in pairs:
        before = jnp.where(lane >= area, pltpu.roll(value, jump, 1), 0.0)
        after = jnp.where(lane < area, pltpu.roll(value, LANES - jump, 1), 0.0)
        right = jnp.concatenate(
            [
                jnp.where(row > 0, pltpu.roll(value, 1, 1), before),
                value,
                jnp.where(row < size_y - 1, pltpu.roll(value, LANES - 1, 1), after),
            ],
            axis=0,
        )
        left = []
        for a in range(3):
            first = pltpu.roll(tiles[0], -a * size_y % LANES, 1)
            second = pltpu.roll(tiles[1], (area - a * size_y) % LANES, 1)
            left.append(jnp.where(lane < area, first, jnp.where(lane < 2 * area, second, 0.0)))
        edges.append(
            lax.dot_general(
                jnp.concatenate(left, axis=0).astype(BF16),
                right.astype(BF16),
                (((1,), (1,)), ((), ())),
                preferred_element_type=F32,
            )
        )
    count = part_ref.shape[0]
    height, width = chunks.shape[0] // count, LANES
    chunks[...] = jnp.zeros_like(chunks)
    pieces = rows * acc_ref.shape[1] // width
    for a in range(3):
        for c in range(3):
            at = 3 * a + c
            block = acc_ref[at * channels : (at + 1) * channels, :]
            if c != 1:
                block = block + edges[c // 2][a * channels : (a + 1) * channels]
            block = block * scale
            line = jnp.concatenate(
                [block[r * count : (r + 1) * count] for r in range(rows)], axis=1
            )
            for k in range(pieces):
                chunks[pl.ds(at * pieces + k, count, stride=height), :] = line[
                    :, k * width : (k + 1) * width
                ]

    def write(at, quads):
        part_ref[:, :, at] = quads.astype(BF16)

    whole = chunks[...].reshape(count, height, width)
    to_quads(whole[:, : part_ref.shape[2] // LANES * QUAD], write)


def finish(acc, columns, sent, received, scale, rows, sizes, part_shape):
    channels = columns.shape[0]
    return pl.pallas_call(
        functools.partial(finish_kernel, scale, rows, sizes),
        in_specs=[VMEM] * 6,
        out_specs=VMEM,
        out_shape=jax.ShapeDtypeStruct(part_shape, BF16),
        scratch_shapes=[
            pltpu.VMEM((part_shape[0] * -(-part_shape[2] // LANES * QUAD // 8) * 8, LANES), F32),
        ],
        compiler_params=params(),
        cost_estimate=cost(2**27, 2**21),
        name="finish",
    )(acc, columns, *sent, *received)


def adam_step(master, first, second, weight_grad):
    new_first = 0.9 * first + 0.1 * weight_grad
    new_second = 0.999 * second + 0.001 * weight_grad * weight_grad
    corr_first = 1.0 - (0.9**10) ** 10
    corr_second = 1.0 - (0.999**10) ** 10
    update = new_first / corr_first / (jnp.sqrt(new_second / corr_second) + 1e-08) + 0.01 * master
    return master - 0.05 * update, new_first, new_second


def in_flat_order(value, rows, places, spread_rows):
    taps = 27
    lane = lax.broadcasted_iota(jnp.int32, (9, LANES), 1)
    for k in range(value.shape[1] // LANES):
        rows[k * QUAD : (k + 1) * QUAD, :] = value[:, k * LANES : (k + 1) * LANES]
    thirds = [rows[pl.ds(k, 9, stride=3), :] for k in range(3)]
    half = LANES // 2
    by_y = (
        jnp.where(lane < half, thirds[0], thirds[1]),
        jnp.where(lane < half, pltpu.roll(thirds[0], half, 1), pltpu.roll(thirds[2], half, 1)),
        jnp.where(lane < half, thirds[1], thirds[2]),
    )
    places[...] = jnp.zeros_like(places)
    for b in range(3):
        spread_rows[b, :9, :] = by_y[b]
        for block in range(9):
            tap = (2 - block // 3) * 9 + b * 3 + 2 - block % 3
            places[tap : tap + 1, :] = spread_rows[b, block : block + 1, :]
    line = places[...].T
    number = lax.broadcasted_iota(jnp.int32, (LANES, LANES), 0) * taps
    column = lax.broadcasted_iota(jnp.int32, (LANES, LANES), 1)
    turned = []
    for group in range(LANES // 8):
        piece = line[8 * group : 8 * (group + 1)]
        rest = 8 * group * taps % LANES
        for step in range(3):
            turn = rest // (3 - step)
            rest -= turn
            piece = pltpu.roll(piece, turn, 1, stride=taps // 3, stride_axis=0)
        turned.append(piece)
    line = jnp.concatenate(turned, axis=0)
    start = number & (LANES - 1)
    line = jnp.concatenate(
        [jnp.where(column >= start, line, 0.0), jnp.where(column < start, line, 0.0)], axis=0
    )
    target = lax.broadcasted_iota(jnp.int32, (32, 2 * LANES), 0)
    source = lax.broadcasted_iota(jnp.int32, (32, 2 * LANES), 1)
    goes = lax.shift_right_logical((source & (LANES - 1)) * taps, 7)
    goes = goes + jnp.where(source < LANES, 0, 1)
    pick = jnp.where(goes == target, 1.0, 0.0).astype(BF16)
    parts = []
    for _ in range(3):
        parts.append(line.astype(BF16))
        line = line - parts[-1].astype(F32)
    return jnp.dot(
        jnp.concatenate([pick] * 3, axis=1),
        jnp.concatenate(parts, axis=0),
        preferred_element_type=F32,
    )[:taps]


def adam_kernel(parts_ref, master_ref, first_ref, second_ref, *refs):
    out_refs, scratch = refs[:4], refs[4:]
    total = parts_ref[0].astype(F32)
    for source in range(1, parts_ref.shape[0]):
        total = total + parts_ref[source].astype(F32)
    weight_grad = in_flat_order(total, *scratch)
    results = adam_step(master_ref[...], first_ref[...], second_ref[...], weight_grad)
    for out_ref, result in zip(out_refs, (weight_grad, *results)):
        out_ref[...] = result


def adam(parts, *states):
    share = states[0].shape[0]
    tiled = [state.reshape(share // LANES, LANES) for state in states]
    result = jax.ShapeDtypeStruct(tiled[0].shape, F32)
    outs = pl.pallas_call(
        adam_kernel,
        in_specs=[VMEM] * 4,
        out_specs=[VMEM] * 4,
        out_shape=[result] * 4,
        scratch_shapes=[
            pltpu.VMEM((32, LANES), F32),
            pltpu.VMEM((LANES, LANES), F32),
            pltpu.VMEM((3, 16, LANES), F32),
        ],
        compiler_params=params(),
        cost_estimate=cost(2**22, 2**19),
        name="adam",
    )(parts, *tiled)
    return tuple(out.reshape(share) for out in outs)


def spread_kernel(rows, w_ref, weights_ref, turned, chunks):
    count = w_ref.shape[0]
    height = chunks.shape[0] // count
    taps = 27 * rows * count
    quads = [
        w_ref[:, :, k * LANES : (k + 1) * LANES].astype(F32)
        for k in range(w_ref.shape[2] // LANES)
    ]
    spare = jnp.zeros((count, height - QUAD * len(quads), LANES), F32)
    chunks[...] = jnp.concatenate(quads + [spare], axis=1).reshape(chunks.shape)
    line = jnp.concatenate(
        [chunks[pl.ds(k, count, stride=height), :] for k in range(rows * taps // LANES)], axis=1
    )
    whole = jnp.concatenate([line[:, r * taps : (r + 1) * taps] for r in range(rows)], axis=0)
    spread_weights(whole, turned, weights_ref)


def spread(kernel, channels, rows):
    return pl.pallas_call(
        functools.partial(spread_kernel, rows),
        in_specs=[VMEM],
        out_specs=VMEM,
        out_shape=jax.ShapeDtypeStruct((3, 2 * channels, 12 * channels), BF16),
        scratch_shapes=[
            flat_scratch(channels),
            pltpu.VMEM((kernel.shape[0] * 32, LANES), F32),
        ],
        compiler_params=params(),
        cost_estimate=cost(2**20, 2**21),
        name="spread",
    )(kernel)


def pair_dgrad_kernel(*refs):
    weights_ref, out_ref, g3, tile = refs[9:]
    _, size_x, size_y, size_z = out_ref.shape
    halo = pair_z_halo(refs[7], refs[8], size_x + 2, size_y, size_z)
    input_products(refs, halo, g3, weights_ref, tile, out_ref)


def pair_dgrad(sources, weights, shape):
    channels, _, size_y, size_z = shape
    return pl.pallas_call(
        pair_dgrad_kernel,
        in_specs=[VMEM] * 10,
        out_specs=VMEM,
        out_shape=jax.ShapeDtypeStruct(shape, BF16),
        scratch_shapes=[g3_scratch(*shape), pltpu.VMEM((2, channels * size_y, size_z), F32)],
        compiler_params=params(32 * 2**20),
        cost_estimate=dgrad_cost(*shape),
        name="dgrad",
    )(*sources, weights)


def pair_program(activations, preact, upstream, master, first_moment, second_moment, scale):
    shape = activations.shape
    channels, size_x, size_y, _ = shape
    devices = math.prod(lax.axis_size(a) for a in AXES)
    rows = channels // devices
    used = master.shape[0] // LANES
    block = (devices, QUAD, -(-used // QUAD) * LANES)
    first, last, odd_sent = faces(preact, upstream, "gx", rows)
    odd_halves = swapped(odd_sent, "gx", 1)
    inner, own, even_sent, sent = pair_inner(
        preact, upstream, first, last, master.reshape(used, LANES), block, rows
    )
    even_halves = swapped(even_sent, "gx", 0)
    kernel = lax.all_to_all(sent, AXES, 0, 0, tiled=True)
    own, xlo, xhi = side((odd_halves, even_halves), own)
    planes = (xlo, first, inner, last, xhi)
    own, activations = lax.optimization_barrier((own, activations))
    other = shifted(own, {"gy": "swap"})
    planes_x, columns = input_planes(activations, True)
    z_sent = join(own, other, columns, size_x * size_y)
    from_odd = swapped(z_sent[1], "gz", 1)
    from_even = swapped(z_sent[0], "gz", 0)
    sources = (*planes, other, other)
    acc = pair_wgrad(sources, planes_x, shape)
    z_received = (from_odd, from_even)
    part = finish(acc, columns, z_sent, z_received, scale, rows, (size_x, size_y), block)
    part, kernel = lax.optimization_barrier((part, kernel))
    parts = lax.all_to_all(part, AXES, 0, 0, tiled=True)
    weights = spread(kernel, channels, rows)
    grad_input = pair_dgrad((*sources, *z_received), weights, shape)
    return grad_input, *adam(parts, master, first_moment, second_moment)


def yface_kernel(*refs):
    low_ref, high_ref = refs[5:]
    size_z = low_ref.shape[-1]
    for index in range(low_ref.shape[0]):
        body = body_of(refs[:5], index)
        plane = body.shape[-1]
        low_ref[index] = body[:, :size_z]
        high_ref[index] = body[:, plane - size_z :]


def y_faces(planes, size_z):
    inner, channels, _ = planes[2].shape
    face = jax.ShapeDtypeStruct((inner + 4, channels, size_z), BF16)
    return pl.pallas_call(
        yface_kernel,
        in_specs=[VMEM] * 5,
        out_specs=[VMEM] * 2,
        out_shape=[face] * 2,
        compiler_params=params(),
        cost_estimate=cost(0, 2**19),
        name="yfaces",
    )(*planes)


def zface_kernel(*refs):
    zlo_ref, zhi_ref = refs[7:]
    size_z = refs[5].shape[-1]
    whole = []
    for index in range(refs[5].shape[0]):
        low, high = y_halo(refs[5:7], index)
        body = body_of(refs[:5], index)[...]
        whole.append(jnp.concatenate([low.astype(BF16), body, high.astype(BF16)], axis=1))
    low, high = z_tiles(whole, whole[0].shape[1] // size_z, size_z, range(len(whole)))
    zlo_ref[...] = low.astype(BF16)
    zhi_ref[...] = high.astype(BF16)


def z_faces(planes, y_halos):
    face = jax.ShapeDtypeStruct((planes[0].shape[0], LANES), BF16)
    return pl.pallas_call(
        zface_kernel,
        in_specs=[VMEM] * 7,
        out_specs=[VMEM] * 2,
        out_shape=[face, face],
        compiler_params=params(),
        cost_estimate=cost(2**27, 2**21),
        name="zfaces",
    )(*planes, *y_halos)


def wgrad_kernel(scale, *refs):
    x_ref, part_ref, g3, x3, acc, flat = refs[9:]
    size_x, channels, plane = x_ref.shape
    size_z = refs[5].shape[-1]
    halo = z_halo(refs[7], refs[8], size_x + 2, plane // size_z + 2, size_z)
    weight_products(refs, halo, x_ref, g3, x3, acc)
    whole = to_flat(acc[...] * scale, channels, channels, flat)
    part_ref[...] = whole[:, : part_ref.shape[1]].astype(BF16)


def wgrad(sources, planes_x, shape, scale):
    channels = shape[0]
    return pl.pallas_call(
        functools.partial(wgrad_kernel, scale),
        in_specs=[VMEM] * 10,
        out_specs=VMEM,
        out_shape=jax.ShapeDtypeStruct((channels, 27 * channels), BF16),
        scratch_shapes=[
            g3_scratch(*shape),
            x3_scratch(*shape),
            acc_scratch(channels),
            flat_scratch(channels),
        ],
        compiler_params=params(32 * 2**20),
        cost_estimate=wgrad_cost(*shape),
        name="wgrad",
    )(*sources, planes_x)


def dgrad_kernel(*refs):
    w_ref, out_ref, g3, turned, weights, tile = refs[9:]
    _, size_x, size_y, size_z = out_ref.shape
    spread_weights(w_ref[...].astype(F32), turned, weights)
    halo = z_halo(refs[7], refs[8], size_x + 2, size_y + 2, size_z)
    input_products(refs, halo, g3, weights, tile, out_ref)


def dgrad(sources, kernel, shape):
    return pl.pallas_call(
        dgrad_kernel,
        in_specs=[VMEM] * 10,
        out_specs=VMEM,
        out_shape=jax.ShapeDtypeStruct(shape, BF16),
        scratch_shapes=dgrad_scratch(*shape),
        compiler_params=params(32 * 2**20),
        cost_estimate=dgrad_cost(*shape),
        name="dgrad",
    )(*sources, kernel)


def general_program(activations, preact, upstream, master, first_moment, second_moment, scale):
    shape = activations.shape
    channels, _, _, size_z = shape
    devices = math.prod(lax.axis_size(a) for a in AXES)
    share = master.shape[0]
    first, last = faces(preact, upstream)
    x_halos = (shifted(last, {"gx": 1}), shifted(first, {"gx": -1}))
    inner = inner_planes(preact, upstream)
    (planes_x,) = input_planes(activations, False)
    sent = jnp.broadcast_to(master.astype(BF16).reshape(1, 1, share), (devices, 1, share))
    kernel = lax.all_to_all(sent, AXES, 0, 0, tiled=True).reshape(channels, 27 * channels)
    planes = (x_halos[0], first, inner, last, x_halos[1])
    y_sent = y_faces(planes, size_z)
    y_halos = (shifted(y_sent[1], {"gy": 1}), shifted(y_sent[0], {"gy": -1}))
    zlo, zhi = z_faces(planes, y_halos)
    z_halos = (shifted(zhi, {"gz": 1}), shifted(zlo, {"gz": -1}))
    sources = (*planes, *y_halos, *z_halos)
    part = wgrad(sources, planes_x, shape, scale)
    part, kernel = lax.optimization_barrier((part, kernel))
    parts = lax.all_to_all(part.reshape(devices, 1, share), AXES, 0, 0, tiled=True)
    grad_input = dgrad(sources, kernel, shape)
    weight_grad = jnp.sum(parts.astype(F32), axis=0).reshape(-1)
    results = adam_step(master, first_moment, second_moment, weight_grad)
    return grad_input, weight_grad, *results


def shifted(value, moves):
    names = tuple(moves)
    sizes = [lax.axis_size(name) for name in names]
    pairs = []
    for source in range(math.prod(sizes)):
        rest, coords = source, []
        for size in reversed(sizes):
            coords.insert(0, rest % size)
            rest //= size
        coords = [
            (at + moves[name]) if moves[name] != "swap" else 1 - at
            for at, name in zip(coords, names)
        ]
        if all(0 <= at < size for at, size in zip(coords, sizes)):
            target = 0
            for at, size in zip(coords, sizes):
                target = target * size + at
            pairs.append((source, target))
    return lax.ppermute(value, names if len(names) > 1 else names[0], pairs)


def swapped(value, axis, start):
    pairs = []
    for low in range(start, lax.axis_size(axis) - 1, 2):
        pairs += [(low, low + 1), (low + 1, low)]
    return lax.ppermute(value, axis, pairs)


def local(activations, preact, upstream, master, first_moment, second_moment):
    channels, size_x, size_y, size_z = activations.shape
    devices = math.prod(lax.axis_size(a) for a in AXES)
    share = master.shape[0]
    scale = 1.0 / math.sqrt(size_x * size_y * size_z * devices)
    in_pairs = (
        lax.axis_size("gy") == 2
        and channels % devices == 0
        and share % LANES == 0
        and channels // devices * channels == LANES
        and 2 * size_x * size_y <= LANES
        and (size_x + 2) * size_y <= LANES
    )
    program = pair_program if in_pairs else general_program
    return program(
        activations, preact, upstream, master, first_moment, second_moment, scale
    )


def solution(mesh):
    volume = P(None, "gx", "gy", "gz")
    flat = P(AXES)
    return jax.shard_map(
        local,
        mesh=mesh,
        in_specs=(volume, volume, volume, flat, flat, flat),
        out_specs=(volume, flat, flat, flat, flat),
        check_vma=False,
    )
```

```python
import functools
import math

import jax
import jax.numpy as jnp
from jax import lax
from jax.experimental import pallas as pl
from jax.experimental.pallas import tpu as pltpu
from jax.sharding import PartitionSpec as P

AXES = ("gx", "gy", "gz")
LANES = 128
VMEM = pl.BlockSpec(memory_space=pltpu.VMEM)
HBM = pl.BlockSpec(memory_space=pltpu.HBM)
F32 = jnp.float32
BF16 = jnp.bfloat16
FACES_VMEM = 55_900_000
INNER_VMEM = 54_800_000
ENDS_VMEM = 54_800_000
MIDDLES_VMEM = 54_600_000


def params(limit=24 * 2**20):
    return pltpu.CompilerParams(vmem_limit_bytes=limit)


def cost(flops, moved):
    return pl.CostEstimate(flops=flops, bytes_accessed=moved, transcendentals=0)


def to_planes(value, tile, write, rows=1):
    channels, size_y, size_z = value.shape
    count = channels // rows
    tile[...] = value.astype(F32).reshape(channels * size_y, size_z)
    for y in range(size_y):
        for r in range(rows):
            picked = tile[pl.ds(r * size_y + y, count, stride=rows * size_y), :]
            write(slice(r * count, (r + 1) * count), y, picked.astype(BF16))


QUAD = 4


def to_quads(rows, write):
    for k in range(rows.shape[-2] // QUAD):
        write(slice(k * LANES, (k + 1) * LANES), rows[..., k * QUAD : (k + 1) * QUAD, :])


def masked(p, u):
    return jnp.where(p > 0, u, jnp.zeros_like(u))


def choose(condition, out_ref, first_ref, second_ref):
    @pl.when(condition)
    def _():
        out_ref[...] = first_ref[...]

    @pl.when(jnp.logical_not(condition))
    def _():
        out_ref[...] = second_ref[...]


def face_kernel(axis, rows, p_ref, u_ref, *refs):
    p_buf, u_buf, tile, sems = refs[-4:]
    out_refs, swap_refs = refs[:2], refs[2:-4]
    size_x, size_z = p_ref.shape[1], p_ref.shape[3]
    copies = []
    for k, x in enumerate((0, size_x - 1)):
        pair = (
            pltpu.make_async_copy(p_ref.at[:, x], p_buf.at[k], sems.at[2 * k]),
            pltpu.make_async_copy(u_ref.at[:, x], u_buf.at[k], sems.at[2 * k + 1]),
        )
        for copy in pair:
            copy.start()
        copies.append(pair)
    for k, out_ref in enumerate(out_refs):
        for copy in copies[k]:
            copy.wait()

        def write(at, y, value):
            out_ref[at, y * size_z : (y + 1) * size_z] = value

        to_planes(masked(p_buf[k], u_buf[k]), tile.at[k], write, rows)
    if axis is not None:
        choose(is_odd(axis), swap_refs[0], out_refs[1], out_refs[0])


def faces(preact, upstream, axis=None, rows=1):
    channels, size_x, size_y, size_z = preact.shape
    face = jax.ShapeDtypeStruct((channels, size_y * size_z), BF16)
    buffer = pltpu.VMEM((2, channels, size_y, size_z), BF16)
    count = 2 if axis is None else 3
    return pl.pallas_call(
        functools.partial(face_kernel, axis, rows),
        in_specs=[HBM, HBM],
        out_specs=[VMEM] * count,
        out_shape=[face] * count,
        scratch_shapes=[
            buffer,
            buffer,
            pltpu.VMEM((2, channels * size_y, size_z), F32),
            pltpu.SemaphoreType.DMA((4,)),
        ],
        compiler_params=params(FACES_VMEM),
        cost_estimate=cost(0, 2**20),
        name="faces",
    )(preact, upstream)


def fetch(planes, p_ref, u_ref, p_buf, u_buf, sems):
    copies = []
    for x in planes:
        pair = (
            pltpu.make_async_copy(p_ref.at[:, x + 1], p_buf.at[x], sems.at[2 * x]),
            pltpu.make_async_copy(u_ref.at[:, x + 1], u_buf.at[x], sems.at[2 * x + 1]),
        )
        for copy in pair:
            copy.start()
        copies.append(pair)
    return copies


def settle(order, planes, copies, g_ref, p_buf, u_buf, tile):
    size_z = p_buf.shape[-1]
    for x, pair in zip(planes, copies):
        for copy in pair:
            copy.wait()

        def write(at, y, value):
            g_ref[x, at, y * size_z : (y + 1) * size_z] = value

        to_planes(masked(p_buf[x], u_buf[x]), tile.at[x % 2], write, order)


def read_inner(order, planes, p_ref, u_ref, g_ref, p_buf, u_buf, tile, sems):
    copies = fetch(planes, p_ref, u_ref, p_buf, u_buf, sems)
    settle(order, planes, copies, g_ref, p_buf, u_buf, tile)


def inner_kernel(*refs):
    read_inner(1, range(refs[2].shape[0]), *refs)


def inner_output(channels, size_x, size_y, size_z):
    return jax.ShapeDtypeStruct((size_x - 2, channels, size_y * size_z), BF16)


def inner_scratch(channels, size_x, size_y, size_z):
    return [
        pltpu.VMEM((size_x - 2, channels, size_y, size_z), BF16),
        pltpu.VMEM((size_x - 2, channels, size_y, size_z), BF16),
        pltpu.VMEM((2, channels * size_y, size_z), F32),
        pltpu.SemaphoreType.DMA((2 * size_x - 4,)),
    ]


def inner_planes(preact, upstream):
    shape = preact.shape
    return pl.pallas_call(
        inner_kernel,
        in_specs=[HBM] * 2,
        out_specs=VMEM,
        out_shape=inner_output(*shape),
        scratch_shapes=inner_scratch(*shape),
        compiler_params=params(INNER_VMEM),
        cost_estimate=cost(0, 4 * 2**20),
        name="inner",
    )(preact, upstream)


def input_kernel(a_ref, x_ref, *refs):
    tile = refs[-1]
    channels, size_x, size_y, size_z = a_ref.shape
    for x in range(size_x):

        def write(at, y, value):
            x_ref[x, at, y * size_z : (y + 1) * size_z] = value

        to_planes(a_ref[:, x], tile.at[x % 2], write)
    if len(refs) > 1:
        low, high = z_tiles([x_ref[x] for x in range(size_x)], size_y, size_z, range(size_x))
        refs[0][...] = (low + pltpu.roll(high, size_x * size_y, 1)).astype(BF16)


def input_planes(activations, with_columns):
    channels, size_x, size_y, size_z = activations.shape
    outs = [jax.ShapeDtypeStruct((size_x, channels, size_y * size_z), BF16)]
    if with_columns:
        outs.append(jax.ShapeDtypeStruct((channels, LANES), BF16))
    return pl.pallas_call(
        input_kernel,
        in_specs=[VMEM],
        out_specs=[VMEM] * len(outs),
        out_shape=outs,
        scratch_shapes=[pltpu.VMEM((2, channels * size_y, size_z), F32)],
        compiler_params=params(),
        cost_estimate=cost(0, 2 * 2**20),
        name="inputs",
    )(activations)


def body_of(refs, index):
    planes = refs[2].shape[0] + 4
    if 2 <= index < planes - 2:
        return refs[2].at[index - 2]
    return refs[{0: 0, 1: 1, planes - 2: 3, planes - 1: 4}[index]]


def y_halo(refs, index):
    me = lax.axis_index("gy")
    low = jnp.where(me > 0, refs[0][index].astype(F32), 0.0)
    high = jnp.where(me < lax.axis_size("gy") - 1, refs[1][index].astype(F32), 0.0)
    return low, high


def z_picker(rows_y, size_z):
    shape = (rows_y * size_z, 2 * LANES)
    voxel = lax.broadcasted_iota(jnp.int32, shape, 0)
    lane = lax.broadcasted_iota(jnp.int32, shape, 1)
    wanted = jnp.where(lane < LANES, lane * size_z, (lane - LANES) * size_z + size_z - 1)
    return (voxel == wanted).astype(F32).astype(BF16)


def z_tiles(planes, rows_y, size_z, numbers):
    channels = planes[0].shape[0]
    columns = jnp.dot(
        jnp.concatenate(planes, axis=0), z_picker(rows_y, size_z), preferred_element_type=F32
    )
    low = jnp.zeros((channels, LANES), F32)
    high = jnp.zeros((channels, LANES), F32)
    for index, number in enumerate(numbers):
        rows = columns[index * channels : (index + 1) * channels]
        low = low + pltpu.roll(rows[:, :LANES], number * rows_y, 1)
        high = high + pltpu.roll(rows[:, LANES:], number * rows_y, 1)
    return low, high


def put_columns(columns, row_of, rows_y, size_z):
    shape = (2 * LANES, rows_y * size_z)
    source = lax.broadcasted_iota(jnp.int32, shape, 0)
    voxel = lax.broadcasted_iota(jnp.int32, shape, 1)
    number = source % LANES
    place = row_of(number) * size_z + jnp.where(source < LANES, 0, size_z - 1)
    place = jnp.where(number < rows_y, place, -1)
    put = (voxel == place).astype(F32).astype(BF16)
    rows = [jnp.concatenate(pair, axis=1) for pair in columns]
    return jnp.dot(
        jnp.concatenate(rows, axis=0).astype(BF16), put, preferred_element_type=F32
    ).astype(BF16)


def z_halo(low_ref, high_ref, planes, rows_y, size_z):
    columns = []
    for index in range(planes):
        shift = -index * rows_y % LANES
        columns.append(
            [pltpu.roll(ref[...].astype(F32), shift, 1) for ref in (low_ref, high_ref)]
        )
    return put_columns(columns, lambda number: number, rows_y, size_z)


def pair_z_halo(odd_ref, even_ref, planes, size_y, size_z):
    me, odd = lax.axis_index("gy"), is_odd("gz")
    sides = []
    for low, high in ((even_ref, odd_ref), (odd_ref, even_ref)):
        first, second = (either(odd, low[k], high[k]) for k in range(2))
        lane = lax.broadcasted_iota(jnp.int32, first.shape, 1)
        own = jnp.where(me == 0, first, second)
        before = jnp.where(me == 0, 0.0, first)
        after = jnp.where(me == 0, second, 0.0)
        columns = []
        for index in range(planes):
            start = index * size_y
            columns.append(
                jnp.where(
                    lane < size_y,
                    pltpu.roll(own, -start % LANES, 1),
                    jnp.where(
                        lane == size_y,
                        pltpu.roll(before, (1 - start) % LANES, 1),
                        pltpu.roll(after, (size_y + 1 - start) % LANES, 1),
                    ),
                )
            )
        sides.append(columns)

    def row_of(number):
        return jnp.where(number < size_y, number + 1, jnp.where(number == size_y, 0, size_y + 1))

    return put_columns(list(zip(*sides)), row_of, size_y + 2, size_z)


def shifted_plane(index, refs, halo, g3):
    channels, plane = refs[0].shape
    size_z = refs[5].shape[-1]
    rows_y = plane // size_z + 2
    base = 3 * channels * index
    lane = lax.broadcasted_iota(jnp.int32, (channels, size_z), 1)
    is_first, is_last = lane == 0, lane == size_z - 1
    low, high = y_halo(refs[5:7], index)
    body = body_of(refs[:5], index)
    for row in range(rows_y):
        cols = slice(row * size_z, (row + 1) * size_z)
        if row == 0:
            value = low.astype(BF16)
        elif row == rows_y - 1:
            value = high.astype(BF16)
        else:
            value = body[:, (row - 1) * size_z : row * size_z]
        if halo is None:
            edge = jnp.zeros_like(value)
        else:
            edge = halo[index * channels : (index + 1) * channels, cols]
        before = jnp.where(is_first, edge, pltpu.roll(value, 1, 1))
        after = jnp.where(is_last, edge, pltpu.roll(value, size_z - 1, 1))
        g3[base : base + channels, cols] = before
        g3[base + channels : base + 2 * channels, cols] = value
        g3[base + 2 * channels : base + 3 * channels, cols] = after


def weight_products(refs, halo, x_ref, g3, x3, acc):
    size_x, channels, plane = x_ref.shape
    size_z = refs[5].shape[-1]
    group = 3 * channels
    zero = jnp.zeros((channels, 2 * size_z), BF16)
    done = 0
    for x in range(0, size_x, 2):
        while done < x + 4:
            shifted_plane(done, refs, halo, g3)
            done += 1
        for plane_x in (x, x + 1):
            value = x_ref[plane_x]
            for b in range(3):
                at = slice(b * channels, (b + 1) * channels)
                start = (2 - b) * size_z
                x3[plane_x, at, start : start + plane] = value
                if start:
                    x3[plane_x, at, :start] = zero[:, :start]
                if start < 2 * size_z:
                    x3[plane_x, at, start + plane :] = zero[:, start:]
        product = lax.dot_general(
            jnp.concatenate(
                [g3[x * group : (x + 3) * group, :], g3[(x + 1) * group : (x + 4) * group, :]],
                axis=1,
            ),
            jnp.concatenate([x3[x], x3[x + 1]], axis=1),
            (((1,), (1,)), ((), ())),
            preferred_element_type=F32,
        )
        if x == 0:
            acc[...] = product
        else:
            acc[...] += product


def to_flat(value, count, channels, flat):
    height, width = value.shape
    wide = value
    if height % LANES:
        wide = jnp.concatenate([wide, jnp.zeros((-height % LANES, width), F32)], axis=0)
    if width % LANES:
        wide = jnp.concatenate([wide, jnp.zeros((wide.shape[0], -width % LANES), F32)], axis=1)
    turned = wide.T
    for b in range(3):
        rows = turned[b * channels : (b + 1) * channels]
        for block in range(9):
            start = block * count
            cell = rows[:, start // LANES * LANES : (start // LANES + 1) * LANES]
            tap = (2 - block // 3) * 9 + b * 3 + 2 - block % 3
            shift = -start % LANES
            flat[pl.ds(tap, channels, stride=27), :] = pltpu.roll(cell, shift, 1) if shift else cell
    return flat[...].T[:count]


def spread_weights(whole, turned, weights):
    channels, taps = whole.shape
    group = 3 * channels
    whole = jnp.concatenate([whole, jnp.zeros((LANES - channels, taps), F32)], axis=0)
    whole = jnp.concatenate([whole, jnp.zeros((LANES, -taps % LANES), F32)], axis=1)
    turned[...] = whole.T
    for b in range(3):
        blocks = []
        for a in range(3):
            for c in range(3):
                tap = (2 - a) * 9 + (2 - b) * 3 + 2 - c
                blocks.append(turned[pl.ds(tap, channels, stride=27), :][:, :channels])
        zero = jnp.zeros((channels, group), F32)
        weights[b, :channels] = jnp.concatenate(blocks + [zero], axis=1).astype(BF16)
        weights[b, channels:] = jnp.concatenate([zero] + blocks, axis=1).astype(BF16)


def input_products(refs, halo, g3, weights, tile, out_ref):
    channels, size_x, size_y, size_z = out_ref.shape
    group = 3 * channels
    plane = size_y * size_z
    done = 0
    for pair in range(size_x // 2):
        while done < 2 * pair + 4:
            shifted_plane(done, refs, halo, g3)
            done += 1
        at = slice(2 * pair * group, (2 * pair + 4) * group)
        total = None
        for b in range(3):
            product = jnp.dot(
                weights[b],
                g3[at, b * size_z : b * size_z + plane],
                preferred_element_type=F32,
            )
            total = product if total is None else total + product
        for half in range(2):
            for y in range(size_y):
                tile[half, pl.ds(y, channels, stride=size_y), :] = total[
                    half * channels : (half + 1) * channels, y * size_z : (y + 1) * size_z
                ]
            out_ref[:, 2 * pair + half] = (
                tile[half].reshape(channels, size_y, size_z).astype(BF16)
            )


def g3_scratch(channels, size_x, size_y, size_z):
    return pltpu.VMEM(((size_x + 2) * 3 * channels, (size_y + 2) * size_z), BF16)


def x3_scratch(channels, size_x, size_y, size_z):
    return pltpu.VMEM((size_x, 3 * channels, (size_y + 2) * size_z), BF16)


def acc_scratch(channels):
    return pltpu.VMEM((9 * channels, 3 * channels), F32)


def flat_scratch(channels):
    return pltpu.VMEM((-(-27 * channels // LANES) * LANES, LANES), F32)


def dgrad_scratch(channels, size_x, size_y, size_z):
    return [
        g3_scratch(channels, size_x, size_y, size_z),
        flat_scratch(channels),
        pltpu.VMEM((3, 2 * channels, 12 * channels), BF16),
        pltpu.VMEM((2, channels * size_y, size_z), F32),
    ]


def wgrad_cost(channels, size_x, size_y, size_z):
    return cost(54 * channels * channels * size_x * (size_y + 2) * size_z, 4 * 2**20)


def dgrad_cost(channels, size_x, size_y, size_z):
    return cost(72 * channels * channels * size_x * size_y * size_z, 4 * 2**20)


def row_for_other(body, size_z):
    plane = body.shape[-1]
    low, high = body[:, :size_z].astype(F32), body[:, plane - size_z :].astype(F32)
    return jnp.where(lax.axis_index("gy") == 0, high, low).astype(BF16)


def in_odd_swaps(axis):
    me, count = lax.axis_index(axis), lax.axis_size(axis)
    return (me > 0) & (me < count - 1 + count % 2)


def ends_kernel(order, *refs):
    choose(is_odd("gx"), refs[5], refs[2], refs[3])

    @pl.when(jnp.logical_not(in_odd_swaps("gx")))
    def _():
        read_inner(order, range(refs[4].shape[0]), *refs[:2], refs[4], *refs[6:])


def middles_kernel(order, *refs):
    p_ref, u_ref, first_ref, last_ref, m_ref, before_ref, g_ref, side_ref, sent_ref = refs[:9]
    p_buf, u_buf, tile, sems, sent_buf, sent_sem = refs[9:]
    half = before_ref.shape[0]
    inner, _, plane = g_ref.shape
    later = range(half, inner)
    copies = fetch(later, p_ref, u_ref, p_buf, u_buf, sems)
    share = m_ref[...]
    share = jnp.concatenate(
        [share, jnp.zeros((-share.shape[0] % QUAD, share.shape[1]), F32)], axis=0
    )

    def write(at, quad):
        quad = quad.astype(BF16)
        sent_buf[:, :, at] = jnp.broadcast_to(quad[None], (sent_buf.shape[0], *quad.shape))

    to_quads(share, write)
    send = pltpu.make_async_copy(sent_buf, sent_ref, sent_sem)
    send.start()
    middle = in_odd_swaps("gx")

    @pl.when(middle)
    def _():
        read_inner(order, range(half), p_ref, u_ref, g_ref, p_buf, u_buf, tile, sems)

    @pl.when(jnp.logical_not(middle))
    def _():
        g_ref[:half] = before_ref[...]

    settle(order, later, copies, g_ref, p_buf, u_buf, tile)
    size_z = side_ref.shape[-1]
    size_x = inner + 2
    bodies = [first_ref] + [g_ref.at[x] for x in range(inner)] + [last_ref]
    for x, body in enumerate(bodies):
        side_ref[x] = row_for_other(body, size_z)
    low, high = z_tiles(
        [body[...] for body in bodies], plane // size_z, size_z, range(1, size_x + 1)
    )
    side_ref[size_x] = low.astype(BF16)
    side_ref[size_x + 1] = high.astype(BF16)
    send.wait()


def pair_inner(preact, upstream, first, last, share, sent_shape, order):
    shape = preact.shape
    channels, size_x, _, size_z = shape
    made = [
        inner_output(*shape),
        jax.ShapeDtypeStruct((size_x + 2, channels, size_z), BF16),
    ]
    half = jax.ShapeDtypeStruct((made[0].shape[0] // 2, *made[0].shape[1:]), BF16)
    before, swap = pl.pallas_call(
        functools.partial(ends_kernel, order),
        in_specs=[HBM] * 2 + [VMEM] * 2,
        out_specs=[VMEM] * 2,
        out_shape=[half, jax.ShapeDtypeStruct(first.shape, BF16)],
        scratch_shapes=inner_scratch(*shape),
        compiler_params=params(ENDS_VMEM),
        cost_estimate=cost(0, 2**20),
        name="ends",
    )(preact, upstream, first, last)
    g, side_rows, sent = pl.pallas_call(
        functools.partial(middles_kernel, order),
        in_specs=[HBM] * 2 + [VMEM] * 4,
        out_specs=[VMEM] * 2 + [HBM],
        out_shape=made + [jax.ShapeDtypeStruct(sent_shape, BF16)],
        scratch_shapes=inner_scratch(*shape)
        + [pltpu.VMEM(sent_shape, BF16), pltpu.SemaphoreType.DMA(())],
        compiler_params=params(MIDDLES_VMEM),
        cost_estimate=cost(0, 4 * 2**20),
        name="middles",
    )(preact, upstream, first, last, share, before)
    return g, side_rows, swap, sent


def is_odd(axis):
    return lax.rem(lax.axis_index(axis), 2) == 1


def either(condition, first, second):
    return jnp.where(condition, first.astype(F32), second.astype(F32))


def side_kernel(odd_ref, even_ref, own_ref, sent_ref, xlo_ref, xhi_ref):
    size_x = own_ref.shape[0] - 2
    size_z = own_ref.shape[-1]
    size_y = xlo_ref.shape[-1] // size_z
    odd = is_odd("gx")
    low = either(odd, even_ref[...], odd_ref[...]).astype(BF16)
    high = either(odd, odd_ref[...], even_ref[...]).astype(BF16)
    xlo_ref[...] = low
    xhi_ref[...] = high
    sent_ref[0] = row_for_other(low, size_z)
    for x in range(size_x):
        sent_ref[x + 1] = own_ref[x]
    sent_ref[size_x + 1] = row_for_other(high, size_z)
    lane = lax.broadcasted_iota(jnp.int32, (low.shape[0], LANES), 1)
    first, second = own_ref[size_x], own_ref[size_x + 1]
    for number, plane in ((0, low), (size_x + 1, high)):
        for y in range(size_y):
            at = number * size_y + y
            head = plane[:, y * size_z : y * size_z + LANES]
            tail = plane[:, (y + 1) * size_z - LANES : (y + 1) * size_z]
            first = jnp.where(lane == at, pltpu.roll(head, at, 1), first)
            second = jnp.where(lane == at, pltpu.roll(tail, at + 1, 1), second)
    sent_ref[size_x + 2] = first
    sent_ref[size_x + 3] = second


def side(halves, own):
    plane = jax.ShapeDtypeStruct(halves[0].shape, BF16)
    return pl.pallas_call(
        side_kernel,
        in_specs=[VMEM] * 3,
        out_specs=[VMEM] * 3,
        out_shape=[
            jax.ShapeDtypeStruct((own.shape[0] + 2, *own.shape[1:]), BF16),
            plane,
            plane,
        ],
        compiler_params=params(),
        cost_estimate=cost(2**25, 2**19),
        name="side",
    )(*halves, own)


def own_columns(columns, number, area):
    me = lax.axis_index("gy")
    value = columns.astype(F32)
    lane = lax.broadcasted_iota(jnp.int32, value.shape, 1)
    first = pltpu.roll(value, -number * area % LANES, 1)
    second = pltpu.roll(value, (1 - number) * area % LANES, 1)
    first = jnp.where(lane < area, first, 0.0)
    second = jnp.where((lane >= area) & (lane < 2 * area), second, 0.0)
    return jnp.where(me == 0, first, second)


def join_kernel(area, own_ref, other_ref, columns_ref, even_ref, odd_ref):
    at = own_ref.shape[0] - 2
    me = lax.axis_index("gy")
    last = own_columns(columns_ref[...], 1, area).astype(BF16)

    def fill(up_ref, down_ref):
        for k, out_ref in enumerate((down_ref, up_ref)):
            out_ref[me] = own_ref[at + k]
            out_ref[1 - me] = other_ref[at + k]
        up_ref[2] = last
        down_ref[2] = last

    odd = is_odd("gz")

    @pl.when(odd)
    def _():
        fill(odd_ref, even_ref)

    @pl.when(jnp.logical_not(odd))
    def _():
        fill(even_ref, odd_ref)


def join(own, other, columns, area):
    return pl.pallas_call(
        functools.partial(join_kernel, area),
        in_specs=[VMEM] * 3,
        out_specs=[VMEM] * 2,
        out_shape=[jax.ShapeDtypeStruct((3, *own.shape[1:]), BF16)] * 2,
        compiler_params=params(),
        cost_estimate=cost(0, 2**17),
        name="join",
    )(own, other, columns)


def pair_wgrad_kernel(*refs):
    x_ref, acc_ref, g3, x3 = refs[7:]
    weight_products(refs, None, x_ref, g3, x3, acc_ref)


def pair_wgrad(sources, planes_x, shape):
    channels = shape[0]
    return pl.pallas_call(
        pair_wgrad_kernel,
        in_specs=[VMEM] * 8,
        out_specs=VMEM,
        out_shape=jax.ShapeDtypeStruct((9 * channels, 3 * channels), F32),
        scratch_shapes=[g3_scratch(*shape), x3_scratch(*shape)],
        compiler_params=params(32 * 2**20),
        cost_estimate=wgrad_cost(*shape),
        name="wgrad",
    )(*sources, planes_x)


def finish_kernel(scale, rows, sizes, *refs):
    acc_ref, columns_ref, even_ref, odd_ref, from_odd_ref, from_even_ref = refs[:6]
    part_ref, chunks = refs[6:]
    size_x, size_y = sizes
    channels = columns_ref.shape[0]
    area = size_x * size_y
    odd = is_odd("gz")
    lane = lax.broadcasted_iota(jnp.int32, (channels, LANES), 1)
    row = lane % size_y
    jump = area - size_y + 1
    below = [either(odd, from_even_ref[k], from_odd_ref[k]) for k in range(3)]
    own = [either(odd, even_ref[k], odd_ref[k]) for k in range(2)]
    pairs = ((below[:2], own_columns(columns_ref[...], 0, area)), (own, below[2]))
    edges = []
    for tiles, value in pairs:
        before = jnp.where(lane >= area, pltpu.roll(value, jump, 1), 0.0)
        after = jnp.where(lane < area, pltpu.roll(value, LANES - jump, 1), 0.0)
        right = jnp.concatenate(
            [
                jnp.where(row > 0, pltpu.roll(value, 1, 1), before),
                value,
                jnp.where(row < size_y - 1, pltpu.roll(value, LANES - 1, 1), after),
            ],
            axis=0,
        )
        left = []
        for a in range(3):
            first = pltpu.roll(tiles[0], -a * size_y % LANES, 1)
            second = pltpu.roll(tiles[1], (area - a * size_y) % LANES, 1)
            left.append(jnp.where(lane < area, first, jnp.where(lane < 2 * area, second, 0.0)))
        edges.append(
            lax.dot_general(
                jnp.concatenate(left, axis=0).astype(BF16),
                right.astype(BF16),
                (((1,), (1,)), ((), ())),
                preferred_element_type=F32,
            )
        )
    count = part_ref.shape[0]
    height, width = chunks.shape[0] // count, LANES
    chunks[...] = jnp.zeros_like(chunks)
    pieces = rows * acc_ref.shape[1] // width
    for a in range(3):
        for c in range(3):
            at = 3 * a + c
            block = acc_ref[at * channels : (at + 1) * channels, :]
            if c != 1:
                block = block + edges[c // 2][a * channels : (a + 1) * channels]
            block = block * scale
            line = jnp.concatenate(
                [block[r * count : (r + 1) * count] for r in range(rows)], axis=1
            )
            for k in range(pieces):
                chunks[pl.ds(at * pieces + k, count, stride=height), :] = line[
                    :, k * width : (k + 1) * width
                ]

    def write(at, quads):
        part_ref[:, :, at] = quads.astype(BF16)

    whole = chunks[...].reshape(count, height, width)
    to_quads(whole[:, : part_ref.shape[2] // LANES * QUAD], write)


def finish(acc, columns, sent, received, scale, rows, sizes, part_shape):
    channels = columns.shape[0]
    return pl.pallas_call(
        functools.partial(finish_kernel, scale, rows, sizes),
        in_specs=[VMEM] * 6,
        out_specs=VMEM,
        out_shape=jax.ShapeDtypeStruct(part_shape, BF16),
        scratch_shapes=[
            pltpu.VMEM((part_shape[0] * -(-part_shape[2] // LANES * QUAD // 8) * 8, LANES), F32),
        ],
        compiler_params=params(),
        cost_estimate=cost(2**27, 2**21),
        name="finish",
    )(acc, columns, *sent, *received)


def adam_step(master, first, second, weight_grad):
    new_first = 0.9 * first + 0.1 * weight_grad
    new_second = 0.999 * second + 0.001 * weight_grad * weight_grad
    corr_first = 1.0 - (0.9**10) ** 10
    corr_second = 1.0 - (0.999**10) ** 10
    update = new_first / corr_first / (jnp.sqrt(new_second / corr_second) + 1e-08) + 0.01 * master
    return master - 0.05 * update, new_first, new_second


def in_flat_order(value, rows, places, spread_rows):
    taps = 27
    lane = lax.broadcasted_iota(jnp.int32, (9, LANES), 1)
    for k in range(value.shape[1] // LANES):
        rows[k * QUAD : (k + 1) * QUAD, :] = value[:, k * LANES : (k + 1) * LANES]
    thirds = [rows[pl.ds(k, 9, stride=3), :] for k in range(3)]
    half = LANES // 2
    by_y = (
        jnp.where(lane < half, thirds[0], thirds[1]),
        jnp.where(lane < half, pltpu.roll(thirds[0], half, 1), pltpu.roll(thirds[2], half, 1)),
        jnp.where(lane < half, thirds[1], thirds[2]),
    )
    places[...] = jnp.zeros_like(places)
    for b in range(3):
        spread_rows[b, :9, :] = by_y[b]
        for block in range(9):
            tap = (2 - block // 3) * 9 + b * 3 + 2 - block % 3
            places[tap : tap + 1, :] = spread_rows[b, block : block + 1, :]
    line = places[...].T
    number = lax.broadcasted_iota(jnp.int32, (LANES, LANES), 0) * taps
    column = lax.broadcasted_iota(jnp.int32, (LANES, LANES), 1)
    turned = []
    for group in range(LANES // 8):
        piece = line[8 * group : 8 * (group + 1)]
        rest = 8 * group * taps % LANES
        for step in range(3):
            turn = rest // (3 - step)
            rest -= turn
            piece = pltpu.roll(piece, turn, 1, stride=taps // 3, stride_axis=0)
        turned.append(piece)
    line = jnp.concatenate(turned, axis=0)
    start = number & (LANES - 1)
    line = jnp.concatenate(
        [jnp.where(column >= start, line, 0.0), jnp.where(column < start, line, 0.0)], axis=0
    )
    target = lax.broadcasted_iota(jnp.int32, (32, 2 * LANES), 0)
    source = lax.broadcasted_iota(jnp.int32, (32, 2 * LANES), 1)
    goes = lax.shift_right_logical((source & (LANES - 1)) * taps, 7)
    goes = goes + jnp.where(source < LANES, 0, 1)
    pick = jnp.where(goes == target, 1.0, 0.0).astype(BF16)
    parts = []
    for _ in range(3):
        parts.append(line.astype(BF16))
        line = line - parts[-1].astype(F32)
    return jnp.dot(
        jnp.concatenate([pick] * 3, axis=1),
        jnp.concatenate(parts, axis=0),
        preferred_element_type=F32,
    )[:taps]


def adam_kernel(parts_ref, master_ref, first_ref, second_ref, *refs):
    out_refs, scratch = refs[:4], refs[4:]
    total = parts_ref[0].astype(F32)
    for source in range(1, parts_ref.shape[0]):
        total = total + parts_ref[source].astype(F32)
    weight_grad = in_flat_order(total, *scratch)
    results = adam_step(master_ref[...], first_ref[...], second_ref[...], weight_grad)
    for out_ref, result in zip(out_refs, (weight_grad, *results)):
        out_ref[...] = result


def adam(parts, *states):
    share = states[0].shape[0]
    tiled = [state.reshape(share // LANES, LANES) for state in states]
    result = jax.ShapeDtypeStruct(tiled[0].shape, F32)
    outs = pl.pallas_call(
        adam_kernel,
        in_specs=[VMEM] * 4,
        out_specs=[VMEM] * 4,
        out_shape=[result] * 4,
        scratch_shapes=[
            pltpu.VMEM((32, LANES), F32),
            pltpu.VMEM((LANES, LANES), F32),
            pltpu.VMEM((3, 16, LANES), F32),
        ],
        compiler_params=params(),
        cost_estimate=cost(2**22, 2**19),
        name="adam",
    )(parts, *tiled)
    return tuple(out.reshape(share) for out in outs)


def spread_kernel(rows, w_ref, weights_ref, turned, chunks):
    count = w_ref.shape[0]
    height = chunks.shape[0] // count
    taps = 27 * rows * count
    quads = [
        w_ref[:, :, k * LANES : (k + 1) * LANES].astype(F32)
        for k in range(w_ref.shape[2] // LANES)
    ]
    spare = jnp.zeros((count, height - QUAD * len(quads), LANES), F32)
    chunks[...] = jnp.concatenate(quads + [spare], axis=1).reshape(chunks.shape)
    line = jnp.concatenate(
        [chunks[pl.ds(k, count, stride=height), :] for k in range(rows * taps // LANES)], axis=1
    )
    whole = jnp.concatenate([line[:, r * taps : (r + 1) * taps] for r in range(rows)], axis=0)
    spread_weights(whole, turned, weights_ref)


def spread(kernel, channels, rows):
    return pl.pallas_call(
        functools.partial(spread_kernel, rows),
        in_specs=[VMEM],
        out_specs=VMEM,
        out_shape=jax.ShapeDtypeStruct((3, 2 * channels, 12 * channels), BF16),
        scratch_shapes=[
            flat_scratch(channels),
            pltpu.VMEM((kernel.shape[0] * 32, LANES), F32),
        ],
        compiler_params=params(),
        cost_estimate=cost(2**20, 2**21),
        name="spread",
    )(kernel)


def pair_dgrad_kernel(*refs):
    weights_ref, out_ref, g3, tile = refs[9:]
    _, size_x, size_y, size_z = out_ref.shape
    halo = pair_z_halo(refs[7], refs[8], size_x + 2, size_y, size_z)
    input_products(refs, halo, g3, weights_ref, tile, out_ref)


def pair_dgrad(sources, weights, shape):
    channels, _, size_y, size_z = shape
    return pl.pallas_call(
        pair_dgrad_kernel,
        in_specs=[VMEM] * 10,
        out_specs=VMEM,
        out_shape=jax.ShapeDtypeStruct(shape, BF16),
        scratch_shapes=[g3_scratch(*shape), pltpu.VMEM((2, channels * size_y, size_z), F32)],
        compiler_params=params(32 * 2**20),
        cost_estimate=dgrad_cost(*shape),
        name="dgrad",
    )(*sources, weights)


def pair_program(activations, preact, upstream, master, first_moment, second_moment, scale):
    shape = activations.shape
    channels, size_x, size_y, _ = shape
    devices = math.prod(lax.axis_size(a) for a in AXES)
    rows = channels // devices
    used = master.shape[0] // LANES
    block = (devices, QUAD, -(-used // QUAD) * LANES)
    first, last, odd_sent = faces(preact, upstream, "gx", rows)
    odd_halves = swapped(odd_sent, "gx", 1)
    inner, own, even_sent, sent = pair_inner(
        preact, upstream, first, last, master.reshape(used, LANES), block, rows
    )
    even_halves = swapped(even_sent, "gx", 0)
    kernel = lax.all_to_all(sent, AXES, 0, 0, tiled=True)
    own, xlo, xhi = side((odd_halves, even_halves), own)
    planes = (xlo, first, inner, last, xhi)
    own, activations = lax.optimization_barrier((own, activations))
    other = shifted(own, {"gy": "swap"})
    planes_x, columns = input_planes(activations, True)
    z_sent = join(own, other, columns, size_x * size_y)
    from_odd = swapped(z_sent[1], "gz", 1)
    from_even = swapped(z_sent[0], "gz", 0)
    sources = (*planes, other, other)
    acc = pair_wgrad(sources, planes_x, shape)
    z_received = (from_odd, from_even)
    part = finish(acc, columns, z_sent, z_received, scale, rows, (size_x, size_y), block)
    part, kernel = lax.optimization_barrier((part, kernel))
    parts = lax.all_to_all(part, AXES, 0, 0, tiled=True)
    weights = spread(kernel, channels, rows)
    grad_input = pair_dgrad((*sources, *z_received), weights, shape)
    return grad_input, *adam(parts, master, first_moment, second_moment)


def yface_kernel(*refs):
    low_ref, high_ref = refs[5:]
    size_z = low_ref.shape[-1]
    for index in range(low_ref.shape[0]):
        body = body_of(refs[:5], index)
        plane = body.shape[-1]
        low_ref[index] = body[:, :size_z]
        high_ref[index] = body[:, plane - size_z :]


def y_faces(planes, size_z):
    inner, channels, _ = planes[2].shape
    face = jax.ShapeDtypeStruct((inner + 4, channels, size_z), BF16)
    return pl.pallas_call(
        yface_kernel,
        in_specs=[VMEM] * 5,
        out_specs=[VMEM] * 2,
        out_shape=[face] * 2,
        compiler_params=params(),
        cost_estimate=cost(0, 2**19),
        name="yfaces",
    )(*planes)


def zface_kernel(*refs):
    zlo_ref, zhi_ref = refs[7:]
    size_z = refs[5].shape[-1]
    whole = []
    for index in range(refs[5].shape[0]):
        low, high = y_halo(refs[5:7], index)
        body = body_of(refs[:5], index)[...]
        whole.append(jnp.concatenate([low.astype(BF16), body, high.astype(BF16)], axis=1))
    low, high = z_tiles(whole, whole[0].shape[1] // size_z, size_z, range(len(whole)))
    zlo_ref[...] = low.astype(BF16)
    zhi_ref[...] = high.astype(BF16)


def z_faces(planes, y_halos):
    face = jax.ShapeDtypeStruct((planes[0].shape[0], LANES), BF16)
    return pl.pallas_call(
        zface_kernel,
        in_specs=[VMEM] * 7,
        out_specs=[VMEM] * 2,
        out_shape=[face, face],
        compiler_params=params(),
        cost_estimate=cost(2**27, 2**21),
        name="zfaces",
    )(*planes, *y_halos)


def wgrad_kernel(scale, *refs):
    x_ref, part_ref, g3, x3, acc, flat = refs[9:]
    size_x, channels, plane = x_ref.shape
    size_z = refs[5].shape[-1]
    halo = z_halo(refs[7], refs[8], size_x + 2, plane // size_z + 2, size_z)
    weight_products(refs, halo, x_ref, g3, x3, acc)
    whole = to_flat(acc[...] * scale, channels, channels, flat)
    part_ref[...] = whole[:, : part_ref.shape[1]].astype(BF16)


def wgrad(sources, planes_x, shape, scale):
    channels = shape[0]
    return pl.pallas_call(
        functools.partial(wgrad_kernel, scale),
        in_specs=[VMEM] * 10,
        out_specs=VMEM,
        out_shape=jax.ShapeDtypeStruct((channels, 27 * channels), BF16),
        scratch_shapes=[
            g3_scratch(*shape),
            x3_scratch(*shape),
            acc_scratch(channels),
            flat_scratch(channels),
        ],
        compiler_params=params(32 * 2**20),
        cost_estimate=wgrad_cost(*shape),
        name="wgrad",
    )(*sources, planes_x)


def dgrad_kernel(*refs):
    w_ref, out_ref, g3, turned, weights, tile = refs[9:]
    _, size_x, size_y, size_z = out_ref.shape
    spread_weights(w_ref[...].astype(F32), turned, weights)
    halo = z_halo(refs[7], refs[8], size_x + 2, size_y + 2, size_z)
    input_products(refs, halo, g3, weights, tile, out_ref)


def dgrad(sources, kernel, shape):
    return pl.pallas_call(
        dgrad_kernel,
        in_specs=[VMEM] * 10,
        out_specs=VMEM,
        out_shape=jax.ShapeDtypeStruct(shape, BF16),
        scratch_shapes=dgrad_scratch(*shape),
        compiler_params=params(32 * 2**20),
        cost_estimate=dgrad_cost(*shape),
        name="dgrad",
    )(*sources, kernel)


def general_program(activations, preact, upstream, master, first_moment, second_moment, scale):
    shape = activations.shape
    channels, _, _, size_z = shape
    devices = math.prod(lax.axis_size(a) for a in AXES)
    share = master.shape[0]
    first, last = faces(preact, upstream)
    x_halos = (shifted(last, {"gx": 1}), shifted(first, {"gx": -1}))
    inner = inner_planes(preact, upstream)
    (planes_x,) = input_planes(activations, False)
    sent = jnp.broadcast_to(master.astype(BF16).reshape(1, 1, share), (devices, 1, share))
    kernel = lax.all_to_all(sent, AXES, 0, 0, tiled=True).reshape(channels, 27 * channels)
    planes = (x_halos[0], first, inner, last, x_halos[1])
    y_sent = y_faces(planes, size_z)
    y_halos = (shifted(y_sent[1], {"gy": 1}), shifted(y_sent[0], {"gy": -1}))
    zlo, zhi = z_faces(planes, y_halos)
    z_halos = (shifted(zhi, {"gz": 1}), shifted(zlo, {"gz": -1}))
    sources = (*planes, *y_halos, *z_halos)
    part = wgrad(sources, planes_x, shape, scale)
    part, kernel = lax.optimization_barrier((part, kernel))
    parts = lax.all_to_all(part.reshape(devices, 1, share), AXES, 0, 0, tiled=True)
    grad_input = dgrad(sources, kernel, shape)
    weight_grad = jnp.sum(parts.astype(F32), axis=0).reshape(-1)
    results = adam_step(master, first_moment, second_moment, weight_grad)
    return grad_input, weight_grad, *results


def shifted(value, moves):
    names = tuple(moves)
    sizes = [lax.axis_size(name) for name in names]
    pairs = []
    for source in range(math.prod(sizes)):
        rest, coords = source, []
        for size in reversed(sizes):
            coords.insert(0, rest % size)
            rest //= size
        coords = [
            (at + moves[name]) if moves[name] != "swap" else 1 - at
            for at, name in zip(coords, names)
        ]
        if all(0 <= at < size for at, size in zip(coords, sizes)):
            target = 0
            for at, size in zip(coords, sizes):
                target = target * size + at
            pairs.append((source, target))
    return lax.ppermute(value, names if len(names) > 1 else names[0], pairs)


def swapped(value, axis, start):
    pairs = []
    for low in range(start, lax.axis_size(axis) - 1, 2):
        pairs += [(low, low + 1), (low + 1, low)]
    return lax.ppermute(value, axis, pairs)


def local(activations, preact, upstream, master, first_moment, second_moment):
    channels, size_x, size_y, size_z = activations.shape
    devices = math.prod(lax.axis_size(a) for a in AXES)
    share = master.shape[0]
    scale = 1.0 / math.sqrt(size_x * size_y * size_z * devices)
    in_pairs = (
        lax.axis_size("gy") == 2
        and channels % devices == 0
        and share % LANES == 0
        and channels // devices * channels == LANES
        and 2 * size_x * size_y <= LANES
        and (size_x + 2) * size_y <= LANES
    )
    program = pair_program if in_pairs else general_program
    return program(
        activations, preact, upstream, master, first_moment, second_moment, scale
    )


def solution(mesh):
    volume = P(None, "gx", "gy", "gz")
    flat = P(AXES)
    return jax.shard_map(
        local,
        mesh=mesh,
        in_specs=(volume, volume, volume, flat, flat, flat),
        out_specs=(volume, flat, flat, flat, flat),
        check_vma=False,
    )
```

```python
import functools
import math

import jax
import jax.numpy as jnp
from jax import lax
from jax.experimental import pallas as pl
from jax.experimental.pallas import tpu as pltpu
from jax.sharding import PartitionSpec as P

AXES = ("gx", "gy", "gz")
LANES = 128
VMEM = pl.BlockSpec(memory_space=pltpu.VMEM)
HBM = pl.BlockSpec(memory_space=pltpu.HBM)
F32 = jnp.float32
BF16 = jnp.bfloat16
FACES_VMEM = 55_900_000
INNER_VMEM = 54_800_000
ENDS_VMEM = 54_800_000
MIDDLES_VMEM = 53_600_000


def params(limit=24 * 2**20):
    return pltpu.CompilerParams(vmem_limit_bytes=limit)


def cost(flops, moved):
    return pl.CostEstimate(flops=flops, bytes_accessed=moved, transcendentals=0)


def to_planes(value, tile, write, rows=1):
    channels, size_y, size_z = value.shape
    count = channels // rows
    tile[...] = value.astype(F32).reshape(channels * size_y, size_z)
    for y in range(size_y):
        for r in range(rows):
            picked = tile[pl.ds(r * size_y + y, count, stride=rows * size_y), :]
            write(slice(r * count, (r + 1) * count), y, picked.astype(BF16))


QUAD = 4


def to_quads(rows, write):
    for k in range(rows.shape[-2] // QUAD):
        write(slice(k * LANES, (k + 1) * LANES), rows[..., k * QUAD : (k + 1) * QUAD, :])


def masked(p, u):
    return jnp.where(p > 0, u, jnp.zeros_like(u))


def choose(condition, out_ref, first_ref, second_ref):
    @pl.when(condition)
    def _():
        out_ref[...] = first_ref[...]

    @pl.when(jnp.logical_not(condition))
    def _():
        out_ref[...] = second_ref[...]


def face_kernel(axis, rows, p_ref, u_ref, *refs):
    p_buf, u_buf, tile, sems = refs[-4:]
    out_refs, swap_refs = refs[:2], refs[2:-4]
    size_x, size_z = p_ref.shape[1], p_ref.shape[3]
    copies = []
    for k, x in enumerate((0, size_x - 1)):
        pair = (
            pltpu.make_async_copy(p_ref.at[:, x], p_buf.at[k], sems.at[2 * k]),
            pltpu.make_async_copy(u_ref.at[:, x], u_buf.at[k], sems.at[2 * k + 1]),
        )
        for copy in pair:
            copy.start()
        copies.append(pair)
    for k, out_ref in enumerate(out_refs):
        for copy in copies[k]:
            copy.wait()

        def write(at, y, value):
            out_ref[at, y * size_z : (y + 1) * size_z] = value

        to_planes(masked(p_buf[k], u_buf[k]), tile.at[k], write, rows)
    if axis is not None:
        choose(is_odd(axis), swap_refs[0], out_refs[1], out_refs[0])


def faces(preact, upstream, axis=None, rows=1):
    channels, size_x, size_y, size_z = preact.shape
    face = jax.ShapeDtypeStruct((channels, size_y * size_z), BF16)
    buffer = pltpu.VMEM((2, channels, size_y, size_z), BF16)
    count = 2 if axis is None else 3
    return pl.pallas_call(
        functools.partial(face_kernel, axis, rows),
        in_specs=[HBM, HBM],
        out_specs=[VMEM] * count,
        out_shape=[face] * count,
        scratch_shapes=[
            buffer,
            buffer,
            pltpu.VMEM((2, channels * size_y, size_z), F32),
            pltpu.SemaphoreType.DMA((4,)),
        ],
        compiler_params=params(FACES_VMEM),
        cost_estimate=cost(0, 2**20),
        name="faces",
    )(preact, upstream)


def fetch(planes, p_ref, u_ref, p_buf, u_buf, sems):
    copies = []
    for x in planes:
        pair = (
            pltpu.make_async_copy(p_ref.at[:, x + 1], p_buf.at[x], sems.at[2 * x]),
            pltpu.make_async_copy(u_ref.at[:, x + 1], u_buf.at[x], sems.at[2 * x + 1]),
        )
        for copy in pair:
            copy.start()
        copies.append(pair)
    return copies


def settle(order, planes, copies, g_ref, p_buf, u_buf, tile):
    size_z = p_buf.shape[-1]
    for x, pair in zip(planes, copies):
        for copy in pair:
            copy.wait()

        def write(at, y, value):
            g_ref[x, at, y * size_z : (y + 1) * size_z] = value

        to_planes(masked(p_buf[x], u_buf[x]), tile.at[x % 2], write, order)


def read_inner(order, planes, p_ref, u_ref, g_ref, p_buf, u_buf, tile, sems):
    copies = fetch(planes, p_ref, u_ref, p_buf, u_buf, sems)
    settle(order, planes, copies, g_ref, p_buf, u_buf, tile)


def inner_kernel(*refs):
    read_inner(1, range(refs[2].shape[0]), *refs)


def inner_output(channels, size_x, size_y, size_z):
    return jax.ShapeDtypeStruct((size_x - 2, channels, size_y * size_z), BF16)


def inner_scratch(channels, size_x, size_y, size_z):
    return [
        pltpu.VMEM((size_x - 2, channels, size_y, size_z), BF16),
        pltpu.VMEM((size_x - 2, channels, size_y, size_z), BF16),
        pltpu.VMEM((2, channels * size_y, size_z), F32),
        pltpu.SemaphoreType.DMA((2 * size_x - 4,)),
    ]


def inner_planes(preact, upstream):
    shape = preact.shape
    return pl.pallas_call(
        inner_kernel,
        in_specs=[HBM] * 2,
        out_specs=VMEM,
        out_shape=inner_output(*shape),
        scratch_shapes=inner_scratch(*shape),
        compiler_params=params(INNER_VMEM),
        cost_estimate=cost(0, 4 * 2**20),
        name="inner",
    )(preact, upstream)


def input_kernel(a_ref, x_ref, *refs):
    tile = refs[-1]
    channels, size_x, size_y, size_z = a_ref.shape
    for x in range(size_x):

        def write(at, y, value):
            x_ref[x, at, y * size_z : (y + 1) * size_z] = value

        to_planes(a_ref[:, x], tile.at[x % 2], write)
    if len(refs) > 1:
        low, high = z_tiles([x_ref[x] for x in range(size_x)], size_y, size_z, range(size_x))
        refs[0][...] = (low + pltpu.roll(high, size_x * size_y, 1)).astype(BF16)


def input_planes(activations, with_columns):
    channels, size_x, size_y, size_z = activations.shape
    outs = [jax.ShapeDtypeStruct((size_x, channels, size_y * size_z), BF16)]
    if with_columns:
        outs.append(jax.ShapeDtypeStruct((channels, LANES), BF16))
    return pl.pallas_call(
        input_kernel,
        in_specs=[VMEM],
        out_specs=[VMEM] * len(outs),
        out_shape=outs,
        scratch_shapes=[pltpu.VMEM((2, channels * size_y, size_z), F32)],
        compiler_params=params(),
        cost_estimate=cost(0, 2 * 2**20),
        name="inputs",
    )(activations)


def body_of(refs, index):
    planes = refs[2].shape[0] + 4
    if 2 <= index < planes - 2:
        return refs[2].at[index - 2]
    return refs[{0: 0, 1: 1, planes - 2: 3, planes - 1: 4}[index]]


def y_halo(refs, index):
    me = lax.axis_index("gy")
    low = jnp.where(me > 0, refs[0][index].astype(F32), 0.0)
    high = jnp.where(me < lax.axis_size("gy") - 1, refs[1][index].astype(F32), 0.0)
    return low, high


def z_picker(rows_y, size_z):
    shape = (rows_y * size_z, 2 * LANES)
    voxel = lax.broadcasted_iota(jnp.int32, shape, 0)
    lane = lax.broadcasted_iota(jnp.int32, shape, 1)
    wanted = jnp.where(lane < LANES, lane * size_z, (lane - LANES) * size_z + size_z - 1)
    return (voxel == wanted).astype(F32).astype(BF16)


def z_tiles(planes, rows_y, size_z, numbers):
    channels = planes[0].shape[0]
    columns = jnp.dot(
        jnp.concatenate(planes, axis=0), z_picker(rows_y, size_z), preferred_element_type=F32
    )
    low = jnp.zeros((channels, LANES), F32)
    high = jnp.zeros((channels, LANES), F32)
    for index, number in enumerate(numbers):
        rows = columns[index * channels : (index + 1) * channels]
        low = low + pltpu.roll(rows[:, :LANES], number * rows_y, 1)
        high = high + pltpu.roll(rows[:, LANES:], number * rows_y, 1)
    return low, high


def put_columns(columns, row_of, rows_y, size_z):
    shape = (2 * LANES, rows_y * size_z)
    source = lax.broadcasted_iota(jnp.int32, shape, 0)
    voxel = lax.broadcasted_iota(jnp.int32, shape, 1)
    number = source % LANES
    place = row_of(number) * size_z + jnp.where(source < LANES, 0, size_z - 1)
    place = jnp.where(number < rows_y, place, -1)
    put = (voxel == place).astype(F32).astype(BF16)
    rows = [jnp.concatenate(pair, axis=1) for pair in columns]
    return jnp.dot(
        jnp.concatenate(rows, axis=0).astype(BF16), put, preferred_element_type=F32
    ).astype(BF16)


def z_halo(low_ref, high_ref, planes, rows_y, size_z):
    columns = []
    for index in range(planes):
        shift = -index * rows_y % LANES
        columns.append(
            [pltpu.roll(ref[...].astype(F32), shift, 1) for ref in (low_ref, high_ref)]
        )
    return put_columns(columns, lambda number: number, rows_y, size_z)


def pair_z_halo(odd_ref, even_ref, planes, size_y, size_z):
    me, odd = lax.axis_index("gy"), is_odd("gz")
    sides = []
    for low, high in ((even_ref, odd_ref), (odd_ref, even_ref)):
        first, second = (either(odd, low[k], high[k]) for k in range(2))
        lane = lax.broadcasted_iota(jnp.int32, first.shape, 1)
        own = jnp.where(me == 0, first, second)
        before = jnp.where(me == 0, 0.0, first)
        after = jnp.where(me == 0, second, 0.0)
        columns = []
        for index in range(planes):
            start = index * size_y
            columns.append(
                jnp.where(
                    lane < size_y,
                    pltpu.roll(own, -start % LANES, 1),
                    jnp.where(
                        lane == size_y,
                        pltpu.roll(before, (1 - start) % LANES, 1),
                        pltpu.roll(after, (size_y + 1 - start) % LANES, 1),
                    ),
                )
            )
        sides.append(columns)

    def row_of(number):
        return jnp.where(number < size_y, number + 1, jnp.where(number == size_y, 0, size_y + 1))

    return put_columns(list(zip(*sides)), row_of, size_y + 2, size_z)


def shifted_plane(index, refs, halo, g3):
    channels, plane = refs[0].shape
    size_z = refs[5].shape[-1]
    rows_y = plane // size_z + 2
    base = 3 * channels * index
    lane = lax.broadcasted_iota(jnp.int32, (channels, size_z), 1)
    is_first, is_last = lane == 0, lane == size_z - 1
    low, high = y_halo(refs[5:7], index)
    body = body_of(refs[:5], index)
    for row in range(rows_y):
        cols = slice(row * size_z, (row + 1) * size_z)
        if row == 0:
            value = low.astype(BF16)
        elif row == rows_y - 1:
            value = high.astype(BF16)
        else:
            value = body[:, (row - 1) * size_z : row * size_z]
        if halo is None:
            edge = jnp.zeros_like(value)
        else:
            edge = halo[index * channels : (index + 1) * channels, cols]
        before = jnp.where(is_first, edge, pltpu.roll(value, 1, 1))
        after = jnp.where(is_last, edge, pltpu.roll(value, size_z - 1, 1))
        g3[base : base + channels, cols] = before
        g3[base + channels : base + 2 * channels, cols] = value
        g3[base + 2 * channels : base + 3 * channels, cols] = after


def weight_products(refs, halo, x_ref, g3, x3, acc):
    size_x, channels, plane = x_ref.shape
    size_z = refs[5].shape[-1]
    group = 3 * channels
    zero = jnp.zeros((channels, 2 * size_z), BF16)
    done = 0
    for x in range(0, size_x, 2):
        while done < x + 4:
            shifted_plane(done, refs, halo, g3)
            done += 1
        for plane_x in (x, x + 1):
            value = x_ref[plane_x]
            for b in range(3):
                at = slice(b * channels, (b + 1) * channels)
                start = (2 - b) * size_z
                x3[plane_x, at, start : start + plane] = value
                if start:
                    x3[plane_x, at, :start] = zero[:, :start]
                if start < 2 * size_z:
                    x3[plane_x, at, start + plane :] = zero[:, start:]
        product = lax.dot_general(
            jnp.concatenate(
                [g3[x * group : (x + 3) * group, :], g3[(x + 1) * group : (x + 4) * group, :]],
                axis=1,
            ),
            jnp.concatenate([x3[x], x3[x + 1]], axis=1),
            (((1,), (1,)), ((), ())),
            preferred_element_type=F32,
        )
        if x == 0:
            acc[...] = product
        else:
            acc[...] += product


def to_flat(value, count, channels, flat):
    height, width = value.shape
    wide = value
    if height % LANES:
        wide = jnp.concatenate([wide, jnp.zeros((-height % LANES, width), F32)], axis=0)
    if width % LANES:
        wide = jnp.concatenate([wide, jnp.zeros((wide.shape[0], -width % LANES), F32)], axis=1)
    turned = wide.T
    for b in range(3):
        rows = turned[b * channels : (b + 1) * channels]
        for block in range(9):
            start = block * count
            cell = rows[:, start // LANES * LANES : (start // LANES + 1) * LANES]
            tap = (2 - block // 3) * 9 + b * 3 + 2 - block % 3
            shift = -start % LANES
            flat[pl.ds(tap, channels, stride=27), :] = pltpu.roll(cell, shift, 1) if shift else cell
    return flat[...].T[:count]


def spread_weights(whole, turned, weights):
    channels, taps = whole.shape
    group = 3 * channels
    whole = jnp.concatenate([whole, jnp.zeros((LANES - channels, taps), F32)], axis=0)
    whole = jnp.concatenate([whole, jnp.zeros((LANES, -taps % LANES), F32)], axis=1)
    turned[...] = whole.T
    for b in range(3):
        blocks = []
        for a in range(3):
            for c in range(3):
                tap = (2 - a) * 9 + (2 - b) * 3 + 2 - c
                blocks.append(turned[pl.ds(tap, channels, stride=27), :][:, :channels])
        zero = jnp.zeros((channels, group), F32)
        weights[b, :channels] = jnp.concatenate(blocks + [zero], axis=1).astype(BF16)
        weights[b, channels:] = jnp.concatenate([zero] + blocks, axis=1).astype(BF16)


def input_products(refs, halo, g3, weights, tile, out_ref):
    channels, size_x, size_y, size_z = out_ref.shape
    group = 3 * channels
    plane = size_y * size_z
    done = 0
    for pair in range(size_x // 2):
        while done < 2 * pair + 4:
            shifted_plane(done, refs, halo, g3)
            done += 1
        at = slice(2 * pair * group, (2 * pair + 4) * group)
        total = None
        for b in range(3):
            product = jnp.dot(
                weights[b],
                g3[at, b * size_z : b * size_z + plane],
                preferred_element_type=F32,
            )
            total = product if total is None else total + product
        for half in range(2):
            for y in range(size_y):
                tile[half, pl.ds(y, channels, stride=size_y), :] = total[
                    half * channels : (half + 1) * channels, y * size_z : (y + 1) * size_z
                ]
            out_ref[:, 2 * pair + half] = (
                tile[half].reshape(channels, size_y, size_z).astype(BF16)
            )


def g3_scratch(channels, size_x, size_y, size_z):
    return pltpu.VMEM(((size_x + 2) * 3 * channels, (size_y + 2) * size_z), BF16)


def x3_scratch(channels, size_x, size_y, size_z):
    return pltpu.VMEM((size_x, 3 * channels, (size_y + 2) * size_z), BF16)


def acc_scratch(channels):
    return pltpu.VMEM((9 * channels, 3 * channels), F32)


def flat_scratch(channels):
    return pltpu.VMEM((-(-27 * channels // LANES) * LANES, LANES), F32)


def dgrad_scratch(channels, size_x, size_y, size_z):
    return [
        g3_scratch(channels, size_x, size_y, size_z),
        flat_scratch(channels),
        pltpu.VMEM((3, 2 * channels, 12 * channels), BF16),
        pltpu.VMEM((2, channels * size_y, size_z), F32),
    ]


def wgrad_cost(channels, size_x, size_y, size_z):
    return cost(54 * channels * channels * size_x * (size_y + 2) * size_z, 4 * 2**20)


def dgrad_cost(channels, size_x, size_y, size_z):
    return cost(72 * channels * channels * size_x * size_y * size_z, 4 * 2**20)


def row_for_other(body, size_z):
    plane = body.shape[-1]
    low, high = body[:, :size_z].astype(F32), body[:, plane - size_z :].astype(F32)
    return jnp.where(lax.axis_index("gy") == 0, high, low).astype(BF16)


def in_odd_swaps(axis):
    me, count = lax.axis_index(axis), lax.axis_size(axis)
    return (me > 0) & (me < count - 1 + count % 2)


def ends_kernel(order, *refs):
    choose(is_odd("gx"), refs[5], refs[2], refs[3])

    @pl.when(jnp.logical_not(in_odd_swaps("gx")))
    def _():
        read_inner(order, range(refs[4].shape[0]), *refs[:2], refs[4], *refs[6:])


def middles_kernel(order, *refs):
    p_ref, u_ref, first_ref, last_ref, m_ref, before_ref, g_ref, side_ref, sent_ref = refs[:9]
    p_buf, u_buf, tile, sems, sent_buf, sent_sem = refs[9:]
    half = before_ref.shape[0]
    inner, _, plane = g_ref.shape
    later = range(half, inner)
    copies = fetch(later, p_ref, u_ref, p_buf, u_buf, sems)
    share = m_ref[...]
    share = jnp.concatenate(
        [share, jnp.zeros((-share.shape[0] % QUAD, share.shape[1]), F32)], axis=0
    )

    def write(at, quad):
        quad = quad.astype(BF16)
        sent_buf[:, :, at] = jnp.broadcast_to(quad[None], (sent_buf.shape[0], *quad.shape))

    to_quads(share, write)
    send = pltpu.make_async_copy(sent_buf, sent_ref, sent_sem)
    send.start()
    middle = in_odd_swaps("gx")

    @pl.when(middle)
    def _():
        read_inner(order, range(half), p_ref, u_ref, g_ref, p_buf, u_buf, tile, sems)

    @pl.when(jnp.logical_not(middle))
    def _():
        g_ref[:half] = before_ref[...]

    settle(order, later, copies, g_ref, p_buf, u_buf, tile)
    size_z = side_ref.shape[-1]
    size_x = inner + 2
    bodies = [first_ref] + [g_ref.at[x] for x in range(inner)] + [last_ref]
    for x, body in enumerate(bodies):
        side_ref[x] = row_for_other(body, size_z)
    low, high = z_tiles(
        [body[...] for body in bodies], plane // size_z, size_z, range(1, size_x + 1)
    )
    side_ref[size_x] = low.astype(BF16)
    side_ref[size_x + 1] = high.astype(BF16)
    send.wait()


def pair_inner(preact, upstream, first, last, share, sent_shape, order):
    shape = preact.shape
    channels, size_x, _, size_z = shape
    made = [
        inner_output(*shape),
        jax.ShapeDtypeStruct((size_x + 2, channels, size_z), BF16),
    ]
    half = jax.ShapeDtypeStruct((made[0].shape[0] // 2, *made[0].shape[1:]), BF16)
    before, swap = pl.pallas_call(
        functools.partial(ends_kernel, order),
        in_specs=[HBM] * 2 + [VMEM] * 2,
        out_specs=[VMEM] * 2,
        out_shape=[half, jax.ShapeDtypeStruct(first.shape, BF16)],
        scratch_shapes=inner_scratch(*shape),
        compiler_params=params(ENDS_VMEM),
        cost_estimate=cost(0, 2**20),
        name="ends",
    )(preact, upstream, first, last)
    g, side_rows, sent = pl.pallas_call(
        functools.partial(middles_kernel, order),
        in_specs=[HBM] * 2 + [VMEM] * 4,
        out_specs=[VMEM] * 2 + [HBM],
        out_shape=made + [jax.ShapeDtypeStruct(sent_shape, BF16)],
        scratch_shapes=inner_scratch(*shape)
        + [pltpu.VMEM(sent_shape, BF16), pltpu.SemaphoreType.DMA(())],
        compiler_params=params(MIDDLES_VMEM),
        cost_estimate=cost(0, 4 * 2**20),
        name="middles",
    )(preact, upstream, first, last, share, before)
    return g, side_rows, swap, sent


def is_odd(axis):
    return lax.rem(lax.axis_index(axis), 2) == 1


def either(condition, first, second):
    return jnp.where(condition, first.astype(F32), second.astype(F32))


def side_kernel(odd_ref, even_ref, own_ref, sent_ref, xlo_ref, xhi_ref):
    size_x = own_ref.shape[0] - 2
    size_z = own_ref.shape[-1]
    size_y = xlo_ref.shape[-1] // size_z
    odd = is_odd("gx")
    low = either(odd, even_ref[...], odd_ref[...]).astype(BF16)
    high = either(odd, odd_ref[...], even_ref[...]).astype(BF16)
    xlo_ref[...] = low
    xhi_ref[...] = high
    sent_ref[0] = row_for_other(low, size_z)
    for x in range(size_x):
        sent_ref[x + 1] = own_ref[x]
    sent_ref[size_x + 1] = row_for_other(high, size_z)
    lane = lax.broadcasted_iota(jnp.int32, (low.shape[0], LANES), 1)
    first, second = own_ref[size_x], own_ref[size_x + 1]
    for number, plane in ((0, low), (size_x + 1, high)):
        for y in range(size_y):
            at = number * size_y + y
            head = plane[:, y * size_z : y * size_z + LANES]
            tail = plane[:, (y + 1) * size_z - LANES : (y + 1) * size_z]
            first = jnp.where(lane == at, pltpu.roll(head, at, 1), first)
            second = jnp.where(lane == at, pltpu.roll(tail, at + 1, 1), second)
    sent_ref[size_x + 2] = first
    sent_ref[size_x + 3] = second


def side(halves, own):
    plane = jax.ShapeDtypeStruct(halves[0].shape, BF16)
    return pl.pallas_call(
        side_kernel,
        in_specs=[VMEM] * 3,
        out_specs=[VMEM] * 3,
        out_shape=[
            jax.ShapeDtypeStruct((own.shape[0] + 2, *own.shape[1:]), BF16),
            plane,
            plane,
        ],
        compiler_params=params(),
        cost_estimate=cost(2**25, 2**19),
        name="side",
    )(*halves, own)


def own_columns(columns, number, area):
    me = lax.axis_index("gy")
    value = columns.astype(F32)
    lane = lax.broadcasted_iota(jnp.int32, value.shape, 1)
    first = pltpu.roll(value, -number * area % LANES, 1)
    second = pltpu.roll(value, (1 - number) * area % LANES, 1)
    first = jnp.where(lane < area, first, 0.0)
    second = jnp.where((lane >= area) & (lane < 2 * area), second, 0.0)
    return jnp.where(me == 0, first, second)


def join_kernel(area, own_ref, other_ref, columns_ref, even_ref, odd_ref):
    at = own_ref.shape[0] - 2
    me = lax.axis_index("gy")
    last = own_columns(columns_ref[...], 1, area).astype(BF16)

    def fill(up_ref, down_ref):
        for k, out_ref in enumerate((down_ref, up_ref)):
            out_ref[me] = own_ref[at + k]
            out_ref[1 - me] = other_ref[at + k]
        up_ref[2] = last
        down_ref[2] = last

    odd = is_odd("gz")

    @pl.when(odd)
    def _():
        fill(odd_ref, even_ref)

    @pl.when(jnp.logical_not(odd))
    def _():
        fill(even_ref, odd_ref)


def join(own, other, columns, area):
    return pl.pallas_call(
        functools.partial(join_kernel, area),
        in_specs=[VMEM] * 3,
        out_specs=[VMEM] * 2,
        out_shape=[jax.ShapeDtypeStruct((3, *own.shape[1:]), BF16)] * 2,
        compiler_params=params(),
        cost_estimate=cost(0, 2**17),
        name="join",
    )(own, other, columns)


def pair_wgrad_kernel(*refs):
    x_ref, acc_ref, g3, x3 = refs[7:]
    weight_products(refs, None, x_ref, g3, x3, acc_ref)


def pair_wgrad(sources, planes_x, shape):
    channels = shape[0]
    return pl.pallas_call(
        pair_wgrad_kernel,
        in_specs=[VMEM] * 8,
        out_specs=VMEM,
        out_shape=jax.ShapeDtypeStruct((9 * channels, 3 * channels), F32),
        scratch_shapes=[g3_scratch(*shape), x3_scratch(*shape)],
        compiler_params=params(32 * 2**20),
        cost_estimate=wgrad_cost(*shape),
        name="wgrad",
    )(*sources, planes_x)


def finish_kernel(scale, rows, sizes, *refs):
    acc_ref, columns_ref, even_ref, odd_ref, from_odd_ref, from_even_ref = refs[:6]
    part_ref, chunks = refs[6:]
    size_x, size_y = sizes
    channels = columns_ref.shape[0]
    area = size_x * size_y
    odd = is_odd("gz")
    lane = lax.broadcasted_iota(jnp.int32, (channels, LANES), 1)
    row = lane % size_y
    jump = area - size_y + 1
    below = [either(odd, from_even_ref[k], from_odd_ref[k]) for k in range(3)]
    own = [either(odd, even_ref[k], odd_ref[k]) for k in range(2)]
    pairs = ((below[:2], own_columns(columns_ref[...], 0, area)), (own, below[2]))
    edges = []
    for tiles, value in pairs:
        before = jnp.where(lane >= area, pltpu.roll(value, jump, 1), 0.0)
        after = jnp.where(lane < area, pltpu.roll(value, LANES - jump, 1), 0.0)
        right = jnp.concatenate(
            [
                jnp.where(row > 0, pltpu.roll(value, 1, 1), before),
                value,
                jnp.where(row < size_y - 1, pltpu.roll(value, LANES - 1, 1), after),
            ],
            axis=0,
        )
        left = []
        for a in range(3):
            first = pltpu.roll(tiles[0], -a * size_y % LANES, 1)
            second = pltpu.roll(tiles[1], (area - a * size_y) % LANES, 1)
            left.append(jnp.where(lane < area, first, jnp.where(lane < 2 * area, second, 0.0)))
        edges.append(
            lax.dot_general(
                jnp.concatenate(left, axis=0).astype(BF16),
                right.astype(BF16),
                (((1,), (1,)), ((), ())),
                preferred_element_type=F32,
            )
        )
    count = part_ref.shape[0]
    height, width = chunks.shape[0] // count, LANES
    chunks[...] = jnp.zeros_like(chunks)
    pieces = rows * acc_ref.shape[1] // width
    for a in range(3):
        for c in range(3):
            at = 3 * a + c
            block = acc_ref[at * channels : (at + 1) * channels, :]
            if c != 1:
                block = block + edges[c // 2][a * channels : (a + 1) * channels]
            block = block * scale
            line = jnp.concatenate(
                [block[r * count : (r + 1) * count] for r in range(rows)], axis=1
            )
            for k in range(pieces):
                chunks[pl.ds(at * pieces + k, count, stride=height), :] = line[
                    :, k * width : (k + 1) * width
                ]

    def write(at, quads):
        part_ref[:, :, at] = quads.astype(BF16)

    whole = chunks[...].reshape(count, height, width)
    to_quads(whole[:, : part_ref.shape[2] // LANES * QUAD], write)


def finish(acc, columns, sent, received, scale, rows, sizes, part_shape):
    channels = columns.shape[0]
    return pl.pallas_call(
        functools.partial(finish_kernel, scale, rows, sizes),
        in_specs=[VMEM] * 6,
        out_specs=VMEM,
        out_shape=jax.ShapeDtypeStruct(part_shape, BF16),
        scratch_shapes=[
            pltpu.VMEM((part_shape[0] * -(-part_shape[2] // LANES * QUAD // 8) * 8, LANES), F32),
        ],
        compiler_params=params(),
        cost_estimate=cost(2**27, 2**21),
        name="finish",
    )(acc, columns, *sent, *received)


def adam_step(master, first, second, weight_grad):
    new_first = 0.9 * first + 0.1 * weight_grad
    new_second = 0.999 * second + 0.001 * weight_grad * weight_grad
    corr_first = 1.0 - (0.9**10) ** 10
    corr_second = 1.0 - (0.999**10) ** 10
    update = new_first / corr_first / (jnp.sqrt(new_second / corr_second) + 1e-08) + 0.01 * master
    return master - 0.05 * update, new_first, new_second


def in_flat_order(value, rows, places, spread_rows):
    taps = 27
    lane = lax.broadcasted_iota(jnp.int32, (9, LANES), 1)
    for k in range(value.shape[1] // LANES):
        rows[k * QUAD : (k + 1) * QUAD, :] = value[:, k * LANES : (k + 1) * LANES]
    thirds = [rows[pl.ds(k, 9, stride=3), :] for k in range(3)]
    half = LANES // 2
    by_y = (
        jnp.where(lane < half, thirds[0], thirds[1]),
        jnp.where(lane < half, pltpu.roll(thirds[0], half, 1), pltpu.roll(thirds[2], half, 1)),
        jnp.where(lane < half, thirds[1], thirds[2]),
    )
    places[...] = jnp.zeros_like(places)
    for b in range(3):
        spread_rows[b, :9, :] = by_y[b]
        for block in range(9):
            tap = (2 - block // 3) * 9 + b * 3 + 2 - block % 3
            places[tap : tap + 1, :] = spread_rows[b, block : block + 1, :]
    line = places[...].T
    number = lax.broadcasted_iota(jnp.int32, (LANES, LANES), 0) * taps
    column = lax.broadcasted_iota(jnp.int32, (LANES, LANES), 1)
    turned = []
    for group in range(LANES // 8):
        piece = line[8 * group : 8 * (group + 1)]
        rest = 8 * group * taps % LANES
        for step in range(3):
            turn = rest // (3 - step)
            rest -= turn
            piece = pltpu.roll(piece, turn, 1, stride=taps // 3, stride_axis=0)
        turned.append(piece)
    line = jnp.concatenate(turned, axis=0)
    start = number & (LANES - 1)
    line = jnp.concatenate(
        [jnp.where(column >= start, line, 0.0), jnp.where(column < start, line, 0.0)], axis=0
    )
    target = lax.broadcasted_iota(jnp.int32, (32, 2 * LANES), 0)
    source = lax.broadcasted_iota(jnp.int32, (32, 2 * LANES), 1)
    goes = lax.shift_right_logical((source & (LANES - 1)) * taps, 7)
    goes = goes + jnp.where(source < LANES, 0, 1)
    pick = jnp.where(goes == target, 1.0, 0.0).astype(BF16)
    parts = []
    for _ in range(3):
        parts.append(line.astype(BF16))
        line = line - parts[-1].astype(F32)
    return jnp.dot(
        jnp.concatenate([pick] * 3, axis=1),
        jnp.concatenate(parts, axis=0),
        preferred_element_type=F32,
    )[:taps]


def adam_kernel(parts_ref, master_ref, first_ref, second_ref, *refs):
    out_refs, scratch = refs[:4], refs[4:]
    total = parts_ref[0].astype(F32)
    for source in range(1, parts_ref.shape[0]):
        total = total + parts_ref[source].astype(F32)
    weight_grad = in_flat_order(total, *scratch)
    results = adam_step(master_ref[...], first_ref[...], second_ref[...], weight_grad)
    for out_ref, result in zip(out_refs, (weight_grad, *results)):
        out_ref[...] = result


def adam(parts, *states):
    share = states[0].shape[0]
    tiled = [state.reshape(share // LANES, LANES) for state in states]
    result = jax.ShapeDtypeStruct(tiled[0].shape, F32)
    outs = pl.pallas_call(
        adam_kernel,
        in_specs=[VMEM] * 4,
        out_specs=[VMEM] * 4,
        out_shape=[result] * 4,
        scratch_shapes=[
            pltpu.VMEM((32, LANES), F32),
            pltpu.VMEM((LANES, LANES), F32),
            pltpu.VMEM((3, 16, LANES), F32),
        ],
        compiler_params=params(),
        cost_estimate=cost(2**22, 2**19),
        name="adam",
    )(parts, *tiled)
    return tuple(out.reshape(share) for out in outs)


def spread_kernel(rows, w_ref, weights_ref, turned, chunks):
    count = w_ref.shape[0]
    height = chunks.shape[0] // count
    taps = 27 * rows * count
    quads = [
        w_ref[:, :, k * LANES : (k + 1) * LANES].astype(F32)
        for k in range(w_ref.shape[2] // LANES)
    ]
    spare = jnp.zeros((count, height - QUAD * len(quads), LANES), F32)
    chunks[...] = jnp.concatenate(quads + [spare], axis=1).reshape(chunks.shape)
    line = jnp.concatenate(
        [chunks[pl.ds(k, count, stride=height), :] for k in range(rows * taps // LANES)], axis=1
    )
    whole = jnp.concatenate([line[:, r * taps : (r + 1) * taps] for r in range(rows)], axis=0)
    spread_weights(whole, turned, weights_ref)


def spread(kernel, channels, rows):
    return pl.pallas_call(
        functools.partial(spread_kernel, rows),
        in_specs=[VMEM],
        out_specs=VMEM,
        out_shape=jax.ShapeDtypeStruct((3, 2 * channels, 12 * channels), BF16),
        scratch_shapes=[
            flat_scratch(channels),
            pltpu.VMEM((kernel.shape[0] * 32, LANES), F32),
        ],
        compiler_params=params(),
        cost_estimate=cost(2**20, 2**21),
        name="spread",
    )(kernel)


def pair_dgrad_kernel(*refs):
    weights_ref, out_ref, g3, tile = refs[9:]
    _, size_x, size_y, size_z = out_ref.shape
    halo = pair_z_halo(refs[7], refs[8], size_x + 2, size_y, size_z)
    input_products(refs, halo, g3, weights_ref, tile, out_ref)


def pair_dgrad(sources, weights, shape):
    channels, _, size_y, size_z = shape
    return pl.pallas_call(
        pair_dgrad_kernel,
        in_specs=[VMEM] * 10,
        out_specs=VMEM,
        out_shape=jax.ShapeDtypeStruct(shape, BF16),
        scratch_shapes=[g3_scratch(*shape), pltpu.VMEM((2, channels * size_y, size_z), F32)],
        compiler_params=params(32 * 2**20),
        cost_estimate=dgrad_cost(*shape),
        name="dgrad",
    )(*sources, weights)


def pair_program(activations, preact, upstream, master, first_moment, second_moment, scale):
    shape = activations.shape
    channels, size_x, size_y, _ = shape
    devices = math.prod(lax.axis_size(a) for a in AXES)
    rows = channels // devices
    used = master.shape[0] // LANES
    block = (devices, QUAD, -(-used // QUAD) * LANES)
    first, last, odd_sent = faces(preact, upstream, "gx", rows)
    odd_halves = swapped(odd_sent, "gx", 1)
    inner, own, even_sent, sent = pair_inner(
        preact, upstream, first, last, master.reshape(used, LANES), block, rows
    )
    even_halves = swapped(even_sent, "gx", 0)
    kernel = lax.all_to_all(sent, AXES, 0, 0, tiled=True)
    own, xlo, xhi = side((odd_halves, even_halves), own)
    planes = (xlo, first, inner, last, xhi)
    own, activations = lax.optimization_barrier((own, activations))
    other = shifted(own, {"gy": "swap"})
    planes_x, columns = input_planes(activations, True)
    z_sent = join(own, other, columns, size_x * size_y)
    from_odd = swapped(z_sent[1], "gz", 1)
    from_even = swapped(z_sent[0], "gz", 0)
    sources = (*planes, other, other)
    acc = pair_wgrad(sources, planes_x, shape)
    z_received = (from_odd, from_even)
    part = finish(acc, columns, z_sent, z_received, scale, rows, (size_x, size_y), block)
    part, kernel = lax.optimization_barrier((part, kernel))
    parts = lax.all_to_all(part, AXES, 0, 0, tiled=True)
    weights = spread(kernel, channels, rows)
    grad_input = pair_dgrad((*sources, *z_received), weights, shape)
    return grad_input, *adam(parts, master, first_moment, second_moment)


def yface_kernel(*refs):
    low_ref, high_ref = refs[5:]
    size_z = low_ref.shape[-1]
    for index in range(low_ref.shape[0]):
        body = body_of(refs[:5], index)
        plane = body.shape[-1]
        low_ref[index] = body[:, :size_z]
        high_ref[index] = body[:, plane - size_z :]


def y_faces(planes, size_z):
    inner, channels, _ = planes[2].shape
    face = jax.ShapeDtypeStruct((inner + 4, channels, size_z), BF16)
    return pl.pallas_call(
        yface_kernel,
        in_specs=[VMEM] * 5,
        out_specs=[VMEM] * 2,
        out_shape=[face] * 2,
        compiler_params=params(),
        cost_estimate=cost(0, 2**19),
        name="yfaces",
    )(*planes)


def zface_kernel(*refs):
    zlo_ref, zhi_ref = refs[7:]
    size_z = refs[5].shape[-1]
    whole = []
    for index in range(refs[5].shape[0]):
        low, high = y_halo(refs[5:7], index)
        body = body_of(refs[:5], index)[...]
        whole.append(jnp.concatenate([low.astype(BF16), body, high.astype(BF16)], axis=1))
    low, high = z_tiles(whole, whole[0].shape[1] // size_z, size_z, range(len(whole)))
    zlo_ref[...] = low.astype(BF16)
    zhi_ref[...] = high.astype(BF16)


def z_faces(planes, y_halos):
    face = jax.ShapeDtypeStruct((planes[0].shape[0], LANES), BF16)
    return pl.pallas_call(
        zface_kernel,
        in_specs=[VMEM] * 7,
        out_specs=[VMEM] * 2,
        out_shape=[face, face],
        compiler_params=params(),
        cost_estimate=cost(2**27, 2**21),
        name="zfaces",
    )(*planes, *y_halos)


def wgrad_kernel(scale, *refs):
    x_ref, part_ref, g3, x3, acc, flat = refs[9:]
    size_x, channels, plane = x_ref.shape
    size_z = refs[5].shape[-1]
    halo = z_halo(refs[7], refs[8], size_x + 2, plane // size_z + 2, size_z)
    weight_products(refs, halo, x_ref, g3, x3, acc)
    whole = to_flat(acc[...] * scale, channels, channels, flat)
    part_ref[...] = whole[:, : part_ref.shape[1]].astype(BF16)


def wgrad(sources, planes_x, shape, scale):
    channels = shape[0]
    return pl.pallas_call(
        functools.partial(wgrad_kernel, scale),
        in_specs=[VMEM] * 10,
        out_specs=VMEM,
        out_shape=jax.ShapeDtypeStruct((channels, 27 * channels), BF16),
        scratch_shapes=[
            g3_scratch(*shape),
            x3_scratch(*shape),
            acc_scratch(channels),
            flat_scratch(channels),
        ],
        compiler_params=params(32 * 2**20),
        cost_estimate=wgrad_cost(*shape),
        name="wgrad",
    )(*sources, planes_x)


def dgrad_kernel(*refs):
    w_ref, out_ref, g3, turned, weights, tile = refs[9:]
    _, size_x, size_y, size_z = out_ref.shape
    spread_weights(w_ref[...].astype(F32), turned, weights)
    halo = z_halo(refs[7], refs[8], size_x + 2, size_y + 2, size_z)
    input_products(refs, halo, g3, weights, tile, out_ref)


def dgrad(sources, kernel, shape):
    return pl.pallas_call(
        dgrad_kernel,
        in_specs=[VMEM] * 10,
        out_specs=VMEM,
        out_shape=jax.ShapeDtypeStruct(shape, BF16),
        scratch_shapes=dgrad_scratch(*shape),
        compiler_params=params(32 * 2**20),
        cost_estimate=dgrad_cost(*shape),
        name="dgrad",
    )(*sources, kernel)


def general_program(activations, preact, upstream, master, first_moment, second_moment, scale):
    shape = activations.shape
    channels, _, _, size_z = shape
    devices = math.prod(lax.axis_size(a) for a in AXES)
    share = master.shape[0]
    first, last = faces(preact, upstream)
    x_halos = (shifted(last, {"gx": 1}), shifted(first, {"gx": -1}))
    inner = inner_planes(preact, upstream)
    (planes_x,) = input_planes(activations, False)
    sent = jnp.broadcast_to(master.astype(BF16).reshape(1, 1, share), (devices, 1, share))
    kernel = lax.all_to_all(sent, AXES, 0, 0, tiled=True).reshape(channels, 27 * channels)
    planes = (x_halos[0], first, inner, last, x_halos[1])
    y_sent = y_faces(planes, size_z)
    y_halos = (shifted(y_sent[1], {"gy": 1}), shifted(y_sent[0], {"gy": -1}))
    zlo, zhi = z_faces(planes, y_halos)
    z_halos = (shifted(zhi, {"gz": 1}), shifted(zlo, {"gz": -1}))
    sources = (*planes, *y_halos, *z_halos)
    part = wgrad(sources, planes_x, shape, scale)
    part, kernel = lax.optimization_barrier((part, kernel))
    parts = lax.all_to_all(part.reshape(devices, 1, share), AXES, 0, 0, tiled=True)
    grad_input = dgrad(sources, kernel, shape)
    weight_grad = jnp.sum(parts.astype(F32), axis=0).reshape(-1)
    results = adam_step(master, first_moment, second_moment, weight_grad)
    return grad_input, weight_grad, *results


def shifted(value, moves):
    names = tuple(moves)
    sizes = [lax.axis_size(name) for name in names]
    pairs = []
    for source in range(math.prod(sizes)):
        rest, coords = source, []
        for size in reversed(sizes):
            coords.insert(0, rest % size)
            rest //= size
        coords = [
            (at + moves[name]) if moves[name] != "swap" else 1 - at
            for at, name in zip(coords, names)
        ]
        if all(0 <= at < size for at, size in zip(coords, sizes)):
            target = 0
            for at, size in zip(coords, sizes):
                target = target * size + at
            pairs.append((source, target))
    return lax.ppermute(value, names if len(names) > 1 else names[0], pairs)


def swapped(value, axis, start):
    pairs = []
    for low in range(start, lax.axis_size(axis) - 1, 2):
        pairs += [(low, low + 1), (low + 1, low)]
    return lax.ppermute(value, axis, pairs)


def local(activations, preact, upstream, master, first_moment, second_moment):
    channels, size_x, size_y, size_z = activations.shape
    devices = math.prod(lax.axis_size(a) for a in AXES)
    share = master.shape[0]
    scale = 1.0 / math.sqrt(size_x * size_y * size_z * devices)
    in_pairs = (
        lax.axis_size("gy") == 2
        and channels % devices == 0
        and share % LANES == 0
        and channels // devices * channels == LANES
        and 2 * size_x * size_y <= LANES
        and (size_x + 2) * size_y <= LANES
    )
    program = pair_program if in_pairs else general_program
    return program(
        activations, preact, upstream, master, first_moment, second_moment, scale
    )


def solution(mesh):
    volume = P(None, "gx", "gy", "gz")
    flat = P(AXES)
    return jax.shard_map(
        local,
        mesh=mesh,
        in_specs=(volume, volume, volume, flat, flat, flat),
        out_specs=(volume, flat, flat, flat, flat),
        check_vma=False,
    )
```

```python
import functools
import math

import jax
import jax.numpy as jnp
from jax import lax
from jax.experimental import pallas as pl
from jax.experimental.pallas import tpu as pltpu
from jax.sharding import PartitionSpec as P

AXES = ("gx", "gy", "gz")
LANES = 128
VMEM = pl.BlockSpec(memory_space=pltpu.VMEM)
HBM = pl.BlockSpec(memory_space=pltpu.HBM)
F32 = jnp.float32
BF16 = jnp.bfloat16
FACES_VMEM = 55_900_000
INNER_VMEM = 54_800_000
ENDS_VMEM = 54_800_000
MIDDLES_VMEM = 54_600_000


def params(limit=24 * 2**20):
    return pltpu.CompilerParams(vmem_limit_bytes=limit)


def cost(flops, moved):
    return pl.CostEstimate(flops=flops, bytes_accessed=moved, transcendentals=0)


def to_planes(value, tile, write, rows=1):
    channels, size_y, size_z = value.shape
    count = channels // rows
    tile[...] = value.astype(F32).reshape(channels * size_y, size_z)
    for y in range(size_y):
        for r in range(rows):
            picked = tile[pl.ds(r * size_y + y, count, stride=rows * size_y), :]
            write(slice(r * count, (r + 1) * count), y, picked.astype(BF16))


QUAD = 4


def to_quads(rows, write):
    for k in range(rows.shape[-2] // QUAD):
        write(slice(k * LANES, (k + 1) * LANES), rows[..., k * QUAD : (k + 1) * QUAD, :])


def masked(p, u):
    return jnp.where(p.astype(F32) > 0, u.astype(F32), 0.0)


def choose(condition, out_ref, first_ref, second_ref):
    @pl.when(condition)
    def _():
        out_ref[...] = first_ref[...]

    @pl.when(jnp.logical_not(condition))
    def _():
        out_ref[...] = second_ref[...]


def face_kernel(axis, rows, p_ref, u_ref, *refs):
    p_buf, u_buf, tile, sems = refs[-4:]
    out_refs, swap_refs = refs[:2], refs[2:-4]
    size_x, size_z = p_ref.shape[1], p_ref.shape[3]
    copies = []
    for k, x in enumerate((0, size_x - 1)):
        pair = (
            pltpu.make_async_copy(p_ref.at[:, x], p_buf.at[k], sems.at[2 * k]),
            pltpu.make_async_copy(u_ref.at[:, x], u_buf.at[k], sems.at[2 * k + 1]),
        )
        for copy in pair:
            copy.start()
        copies.append(pair)
    for k, out_ref in enumerate(out_refs):
        for copy in copies[k]:
            copy.wait()

        def write(at, y, value):
            out_ref[at, y * size_z : (y + 1) * size_z] = value

        to_planes(masked(p_buf[k], u_buf[k]), tile.at[k], write, rows)
    if axis is not None:
        choose(is_odd(axis), swap_refs[0], out_refs[1], out_refs[0])


def faces(preact, upstream, axis=None, rows=1):
    channels, size_x, size_y, size_z = preact.shape
    face = jax.ShapeDtypeStruct((channels, size_y * size_z), BF16)
    buffer = pltpu.VMEM((2, channels, size_y, size_z), BF16)
    count = 2 if axis is None else 3
    return pl.pallas_call(
        functools.partial(face_kernel, axis, rows),
        in_specs=[HBM, HBM],
        out_specs=[VMEM] * count,
        out_shape=[face] * count,
        scratch_shapes=[
            buffer,
            buffer,
            pltpu.VMEM((2, channels * size_y, size_z), F32),
            pltpu.SemaphoreType.DMA((4,)),
        ],
        compiler_params=params(FACES_VMEM),
        cost_estimate=cost(0, 2**20),
        name="faces",
    )(preact, upstream)


def fetch(planes, p_ref, u_ref, p_buf, u_buf, sems):
    copies = []
    for x in planes:
        pair = (
            pltpu.make_async_copy(p_ref.at[:, x + 1], p_buf.at[x], sems.at[2 * x]),
            pltpu.make_async_copy(u_ref.at[:, x + 1], u_buf.at[x], sems.at[2 * x + 1]),
        )
        for copy in pair:
            copy.start()
        copies.append(pair)
    return copies


def settle(order, planes, copies, g_ref, p_buf, u_buf, tile):
    size_z = p_buf.shape[-1]
    for x, pair in zip(planes, copies):
        for copy in pair:
            copy.wait()

        def write(at, y, value):
            g_ref[x, at, y * size_z : (y + 1) * size_z] = value

        to_planes(masked(p_buf[x], u_buf[x]), tile.at[x % 2], write, order)


def read_inner(order, planes, p_ref, u_ref, g_ref, p_buf, u_buf, tile, sems):
    copies = fetch(planes, p_ref, u_ref, p_buf, u_buf, sems)
    settle(order, planes, copies, g_ref, p_buf, u_buf, tile)


def inner_kernel(*refs):
    read_inner(1, range(refs[2].shape[0]), *refs)


def inner_output(channels, size_x, size_y, size_z):
    return jax.ShapeDtypeStruct((size_x - 2, channels, size_y * size_z), BF16)


def inner_scratch(channels, size_x, size_y, size_z):
    return [
        pltpu.VMEM((size_x - 2, channels, size_y, size_z), BF16),
        pltpu.VMEM((size_x - 2, channels, size_y, size_z), BF16),
        pltpu.VMEM((2, channels * size_y, size_z), F32),
        pltpu.SemaphoreType.DMA((2 * size_x - 4,)),
    ]


def inner_planes(preact, upstream):
    shape = preact.shape
    return pl.pallas_call(
        inner_kernel,
        in_specs=[HBM] * 2,
        out_specs=VMEM,
        out_shape=inner_output(*shape),
        scratch_shapes=inner_scratch(*shape),
        compiler_params=params(INNER_VMEM),
        cost_estimate=cost(0, 4 * 2**20),
        name="inner",
    )(preact, upstream)


def input_kernel(a_ref, x_ref, *refs):
    tile = refs[-1]
    channels, size_x, size_y, size_z = a_ref.shape
    for x in range(size_x):

        def write(at, y, value):
            x_ref[x, at, y * size_z : (y + 1) * size_z] = value

        to_planes(a_ref[:, x], tile.at[x % 2], write)
    if len(refs) > 1:
        low, high = z_tiles([x_ref[x] for x in range(size_x)], size_y, size_z, range(size_x))
        refs[0][...] = (low + pltpu.roll(high, size_x * size_y, 1)).astype(BF16)


def input_planes(activations, with_columns):
    channels, size_x, size_y, size_z = activations.shape
    outs = [jax.ShapeDtypeStruct((size_x, channels, size_y * size_z), BF16)]
    if with_columns:
        outs.append(jax.ShapeDtypeStruct((channels, LANES), BF16))
    return pl.pallas_call(
        input_kernel,
        in_specs=[VMEM],
        out_specs=[VMEM] * len(outs),
        out_shape=outs,
        scratch_shapes=[pltpu.VMEM((2, channels * size_y, size_z), F32)],
        compiler_params=params(),
        cost_estimate=cost(0, 2 * 2**20),
        name="inputs",
    )(activations)


def body_of(refs, index):
    planes = refs[2].shape[0] + 4
    if 2 <= index < planes - 2:
        return refs[2].at[index - 2]
    return refs[{0: 0, 1: 1, planes - 2: 3, planes - 1: 4}[index]]


def y_halo(refs, index):
    me = lax.axis_index("gy")
    low = jnp.where(me > 0, refs[0][index].astype(F32), 0.0)
    high = jnp.where(me < lax.axis_size("gy") - 1, refs[1][index].astype(F32), 0.0)
    return low, high


def z_picker(rows_y, size_z):
    shape = (rows_y * size_z, 2 * LANES)
    voxel = lax.broadcasted_iota(jnp.int32, shape, 0)
    lane = lax.broadcasted_iota(jnp.int32, shape, 1)
    wanted = jnp.where(lane < LANES, lane * size_z, (lane - LANES) * size_z + size_z - 1)
    return (voxel == wanted).astype(F32).astype(BF16)


def z_tiles(planes, rows_y, size_z, numbers):
    channels = planes[0].shape[0]
    columns = jnp.dot(
        jnp.concatenate(planes, axis=0), z_picker(rows_y, size_z), preferred_element_type=F32
    )
    low = jnp.zeros((channels, LANES), F32)
    high = jnp.zeros((channels, LANES), F32)
    for index, number in enumerate(numbers):
        rows = columns[index * channels : (index + 1) * channels]
        low = low + pltpu.roll(rows[:, :LANES], number * rows_y, 1)
        high = high + pltpu.roll(rows[:, LANES:], number * rows_y, 1)
    return low, high


def put_columns(columns, row_of, rows_y, size_z):
    shape = (2 * LANES, rows_y * size_z)
    source = lax.broadcasted_iota(jnp.int32, shape, 0)
    voxel = lax.broadcasted_iota(jnp.int32, shape, 1)
    number = source % LANES
    place = row_of(number) * size_z + jnp.where(source < LANES, 0, size_z - 1)
    place = jnp.where(number < rows_y, place, -1)
    put = (voxel == place).astype(F32).astype(BF16)
    rows = [jnp.concatenate(pair, axis=1) for pair in columns]
    return jnp.dot(
        jnp.concatenate(rows, axis=0).astype(BF16), put, preferred_element_type=F32
    ).astype(BF16)


def z_halo(low_ref, high_ref, planes, rows_y, size_z):
    columns = []
    for index in range(planes):
        shift = -index * rows_y % LANES
        columns.append(
            [pltpu.roll(ref[...].astype(F32), shift, 1) for ref in (low_ref, high_ref)]
        )
    return put_columns(columns, lambda number: number, rows_y, size_z)


def pair_z_halo(odd_ref, even_ref, planes, size_y, size_z):
    me, odd = lax.axis_index("gy"), is_odd("gz")
    sides = []
    for low, high in ((even_ref, odd_ref), (odd_ref, even_ref)):
        first, second = (either(odd, low[k], high[k]) for k in range(2))
        lane = lax.broadcasted_iota(jnp.int32, first.shape, 1)
        own = jnp.where(me == 0, first, second)
        before = jnp.where(me == 0, 0.0, first)
        after = jnp.where(me == 0, second, 0.0)
        columns = []
        for index in range(planes):
            start = index * size_y
            columns.append(
                jnp.where(
                    lane < size_y,
                    pltpu.roll(own, -start % LANES, 1),
                    jnp.where(
                        lane == size_y,
                        pltpu.roll(before, (1 - start) % LANES, 1),
                        pltpu.roll(after, (size_y + 1 - start) % LANES, 1),
                    ),
                )
            )
        sides.append(columns)

    def row_of(number):
        return jnp.where(number < size_y, number + 1, jnp.where(number == size_y, 0, size_y + 1))

    return put_columns(list(zip(*sides)), row_of, size_y + 2, size_z)


def shifted_plane(index, refs, halo, g3):
    channels, plane = refs[0].shape
    size_z = refs[5].shape[-1]
    rows_y = plane // size_z + 2
    base = 3 * channels * index
    lane = lax.broadcasted_iota(jnp.int32, (channels, size_z), 1)
    is_first, is_last = lane == 0, lane == size_z - 1
    low, high = y_halo(refs[5:7], index)
    body = body_of(refs[:5], index)
    for row in range(rows_y):
        cols = slice(row * size_z, (row + 1) * size_z)
        if row == 0:
            value = low.astype(BF16)
        elif row == rows_y - 1:
            value = high.astype(BF16)
        else:
            value = body[:, (row - 1) * size_z : row * size_z]
        if halo is None:
            edge = jnp.zeros_like(value)
        else:
            edge = halo[index * channels : (index + 1) * channels, cols]
        before = jnp.where(is_first, edge, pltpu.roll(value, 1, 1))
        after = jnp.where(is_last, edge, pltpu.roll(value, size_z - 1, 1))
        g3[base : base + channels, cols] = before
        g3[base + channels : base + 2 * channels, cols] = value
        g3[base + 2 * channels : base + 3 * channels, cols] = after


def weight_products(refs, halo, x_ref, g3, x3, acc):
    size_x, channels, plane = x_ref.shape
    size_z = refs[5].shape[-1]
    group = 3 * channels
    zero = jnp.zeros((channels, 2 * size_z), BF16)
    done = 0
    for x in range(0, size_x, 2):
        while done < x + 4:
            shifted_plane(done, refs, halo, g3)
            done += 1
        for plane_x in (x, x + 1):
            value = x_ref[plane_x]
            for b in range(3):
                at = slice(b * channels, (b + 1) * channels)
                start = (2 - b) * size_z
                x3[plane_x, at, start : start + plane] = value
                if start:
                    x3[plane_x, at, :start] = zero[:, :start]
                if start < 2 * size_z:
                    x3[plane_x, at, start + plane :] = zero[:, start:]
        product = lax.dot_general(
            jnp.concatenate(
                [g3[x * group : (x + 3) * group, :], g3[(x + 1) * group : (x + 4) * group, :]],
                axis=1,
            ),
            jnp.concatenate([x3[x], x3[x + 1]], axis=1),
            (((1,), (1,)), ((), ())),
            preferred_element_type=F32,
        )
        if x == 0:
            acc[...] = product
        else:
            acc[...] += product


def to_flat(value, count, channels, flat):
    height, width = value.shape
    wide = value
    if height % LANES:
        wide = jnp.concatenate([wide, jnp.zeros((-height % LANES, width), F32)], axis=0)
    if width % LANES:
        wide = jnp.concatenate([wide, jnp.zeros((wide.shape[0], -width % LANES), F32)], axis=1)
    turned = wide.T
    for b in range(3):
        rows = turned[b * channels : (b + 1) * channels]
        for block in range(9):
            start = block * count
            cell = rows[:, start // LANES * LANES : (start // LANES + 1) * LANES]
            tap = (2 - block // 3) * 9 + b * 3 + 2 - block % 3
            shift = -start % LANES
            flat[pl.ds(tap, channels, stride=27), :] = pltpu.roll(cell, shift, 1) if shift else cell
    return flat[...].T[:count]


def spread_weights(whole, turned, weights):
    channels, taps = whole.shape
    group = 3 * channels
    whole = jnp.concatenate([whole, jnp.zeros((LANES - channels, taps), F32)], axis=0)
    whole = jnp.concatenate([whole, jnp.zeros((LANES, -taps % LANES), F32)], axis=1)
    turned[...] = whole.T
    for b in range(3):
        blocks = []
        for a in range(3):
            for c in range(3):
                tap = (2 - a) * 9 + (2 - b) * 3 + 2 - c
                blocks.append(turned[pl.ds(tap, channels, stride=27), :][:, :channels])
        zero = jnp.zeros((channels, group), F32)
        weights[b, :channels] = jnp.concatenate(blocks + [zero], axis=1).astype(BF16)
        weights[b, channels:] = jnp.concatenate([zero] + blocks, axis=1).astype(BF16)


def input_products(refs, halo, g3, weights, tile, out_ref):
    channels, size_x, size_y, size_z = out_ref.shape
    group = 3 * channels
    plane = size_y * size_z
    done = 0
    for pair in range(size_x // 2):
        while done < 2 * pair + 4:
            shifted_plane(done, refs, halo, g3)
            done += 1
        at = slice(2 * pair * group, (2 * pair + 4) * group)
        total = None
        for b in range(3):
            product = jnp.dot(
                weights[b],
                g3[at, b * size_z : b * size_z + plane],
                preferred_element_type=F32,
            )
            total = product if total is None else total + product
        for half in range(2):
            for y in range(size_y):
                tile[half, pl.ds(y, channels, stride=size_y), :] = total[
                    half * channels : (half + 1) * channels, y * size_z : (y + 1) * size_z
                ]
            out_ref[:, 2 * pair + half] = (
                tile[half].reshape(channels, size_y, size_z).astype(BF16)
            )


def g3_scratch(channels, size_x, size_y, size_z):
    return pltpu.VMEM(((size_x + 2) * 3 * channels, (size_y + 2) * size_z), BF16)


def x3_scratch(channels, size_x, size_y, size_z):
    return pltpu.VMEM((size_x, 3 * channels, (size_y + 2) * size_z), BF16)


def acc_scratch(channels):
    return pltpu.VMEM((9 * channels, 3 * channels), F32)


def flat_scratch(channels):
    return pltpu.VMEM((-(-27 * channels // LANES) * LANES, LANES), F32)


def dgrad_scratch(channels, size_x, size_y, size_z):
    return [
        g3_scratch(channels, size_x, size_y, size_z),
        flat_scratch(channels),
        pltpu.VMEM((3, 2 * channels, 12 * channels), BF16),
        pltpu.VMEM((2, channels * size_y, size_z), F32),
    ]


def wgrad_cost(channels, size_x, size_y, size_z):
    return cost(54 * channels * channels * size_x * (size_y + 2) * size_z, 4 * 2**20)


def dgrad_cost(channels, size_x, size_y, size_z):
    return cost(72 * channels * channels * size_x * size_y * size_z, 4 * 2**20)


def row_for_other(body, size_z):
    plane = body.shape[-1]
    low, high = body[:, :size_z].astype(F32), body[:, plane - size_z :].astype(F32)
    return jnp.where(lax.axis_index("gy") == 0, high, low).astype(BF16)


def in_odd_swaps(axis):
    me, count = lax.axis_index(axis), lax.axis_size(axis)
    return (me > 0) & (me < count - 1 + count % 2)


def ends_kernel(order, *refs):
    choose(is_odd("gx"), refs[5], refs[2], refs[3])

    @pl.when(jnp.logical_not(in_odd_swaps("gx")))
    def _():
        read_inner(order, range(refs[4].shape[0]), *refs[:2], refs[4], *refs[6:])


def middles_kernel(order, *refs):
    p_ref, u_ref, first_ref, last_ref, m_ref, before_ref, g_ref, side_ref, sent_ref = refs[:9]
    p_buf, u_buf, tile, sems, sent_buf, sent_sem = refs[9:]
    half = before_ref.shape[0]
    inner, _, plane = g_ref.shape
    later = range(half, inner)
    copies = fetch(later, p_ref, u_ref, p_buf, u_buf, sems)
    share = m_ref[...]
    share = jnp.concatenate(
        [share, jnp.zeros((-share.shape[0] % QUAD, share.shape[1]), F32)], axis=0
    )

    def write(at, quad):
        quad = quad.astype(BF16)
        sent_buf[:, :, at] = jnp.broadcast_to(quad[None], (sent_buf.shape[0], *quad.shape))

    to_quads(share, write)
    send = pltpu.make_async_copy(sent_buf, sent_ref, sent_sem)
    send.start()
    middle = in_odd_swaps("gx")

    @pl.when(middle)
    def _():
        read_inner(order, range(half), p_ref, u_ref, g_ref, p_buf, u_buf, tile, sems)

    @pl.when(jnp.logical_not(middle))
    def _():
        g_ref[:half] = before_ref[...]

    settle(order, later, copies, g_ref, p_buf, u_buf, tile)
    size_z = side_ref.shape[-1]
    size_x = inner + 2
    bodies = [first_ref] + [g_ref.at[x] for x in range(inner)] + [last_ref]
    for x, body in enumerate(bodies):
        side_ref[x] = row_for_other(body, size_z)
    low, high = z_tiles(
        [body[...] for body in bodies], plane // size_z, size_z, range(1, size_x + 1)
    )
    side_ref[size_x] = low.astype(BF16)
    side_ref[size_x + 1] = high.astype(BF16)
    send.wait()


def pair_inner(preact, upstream, first, last, share, sent_shape, order):
    shape = preact.shape
    channels, size_x, _, size_z = shape
    made = [
        inner_output(*shape),
        jax.ShapeDtypeStruct((size_x + 2, channels, size_z), BF16),
    ]
    half = jax.ShapeDtypeStruct((made[0].shape[0] // 2, *made[0].shape[1:]), BF16)
    before, swap = pl.pallas_call(
        functools.partial(ends_kernel, order),
        in_specs=[HBM] * 2 + [VMEM] * 2,
        out_specs=[VMEM] * 2,
        out_shape=[half, jax.ShapeDtypeStruct(first.shape, BF16)],
        scratch_shapes=inner_scratch(*shape),
        compiler_params=params(ENDS_VMEM),
        cost_estimate=cost(0, 2**20),
        name="ends",
    )(preact, upstream, first, last)
    g, side_rows, sent = pl.pallas_call(
        functools.partial(middles_kernel, order),
        in_specs=[HBM] * 2 + [VMEM] * 4,
        out_specs=[VMEM] * 2 + [HBM],
        out_shape=made + [jax.ShapeDtypeStruct(sent_shape, BF16)],
        scratch_shapes=inner_scratch(*shape)
        + [pltpu.VMEM(sent_shape, BF16), pltpu.SemaphoreType.DMA(())],
        compiler_params=params(MIDDLES_VMEM),
        cost_estimate=cost(0, 4 * 2**20),
        name="middles",
    )(preact, upstream, first, last, share, before)
    return g, side_rows, swap, sent


def is_odd(axis):
    return lax.rem(lax.axis_index(axis), 2) == 1


def either(condition, first, second):
    return jnp.where(condition, first.astype(F32), second.astype(F32))


def side_kernel(odd_ref, even_ref, own_ref, sent_ref, xlo_ref, xhi_ref):
    size_x = own_ref.shape[0] - 2
    size_z = own_ref.shape[-1]
    size_y = xlo_ref.shape[-1] // size_z
    odd = is_odd("gx")
    low = either(odd, even_ref[...], odd_ref[...]).astype(BF16)
    high = either(odd, odd_ref[...], even_ref[...]).astype(BF16)
    xlo_ref[...] = low
    xhi_ref[...] = high
    sent_ref[0] = row_for_other(low, size_z)
    for x in range(size_x):
        sent_ref[x + 1] = own_ref[x]
    sent_ref[size_x + 1] = row_for_other(high, size_z)
    lane = lax.broadcasted_iota(jnp.int32, (low.shape[0], LANES), 1)
    first, second = own_ref[size_x], own_ref[size_x + 1]
    for number, plane in ((0, low), (size_x + 1, high)):
        for y in range(size_y):
            at = number * size_y + y
            head = plane[:, y * size_z : y * size_z + LANES]
            tail = plane[:, (y + 1) * size_z - LANES : (y + 1) * size_z]
            first = jnp.where(lane == at, pltpu.roll(head, at, 1), first)
            second = jnp.where(lane == at, pltpu.roll(tail, at + 1, 1), second)
    sent_ref[size_x + 2] = first
    sent_ref[size_x + 3] = second


def side(halves, own):
    plane = jax.ShapeDtypeStruct(halves[0].shape, BF16)
    return pl.pallas_call(
        side_kernel,
        in_specs=[VMEM] * 3,
        out_specs=[VMEM] * 3,
        out_shape=[
            jax.ShapeDtypeStruct((own.shape[0] + 2, *own.shape[1:]), BF16),
            plane,
            plane,
        ],
        compiler_params=params(),
        cost_estimate=cost(2**25, 2**19),
        name="side",
    )(*halves, own)


def own_columns(columns, number, area):
    me = lax.axis_index("gy")
    value = columns.astype(F32)
    lane = lax.broadcasted_iota(jnp.int32, value.shape, 1)
    first = pltpu.roll(value, -number * area % LANES, 1)
    second = pltpu.roll(value, (1 - number) * area % LANES, 1)
    first = jnp.where(lane < area, first, 0.0)
    second = jnp.where((lane >= area) & (lane < 2 * area), second, 0.0)
    return jnp.where(me == 0, first, second)


def join_kernel(area, own_ref, other_ref, columns_ref, even_ref, odd_ref):
    at = own_ref.shape[0] - 2
    me = lax.axis_index("gy")
    last = own_columns(columns_ref[...], 1, area).astype(BF16)

    def fill(up_ref, down_ref):
        for k, out_ref in enumerate((down_ref, up_ref)):
            out_ref[me] = own_ref[at + k]
            out_ref[1 - me] = other_ref[at + k]
        up_ref[2] = last
        down_ref[2] = last

    odd = is_odd("gz")

    @pl.when(odd)
    def _():
        fill(odd_ref, even_ref)

    @pl.when(jnp.logical_not(odd))
    def _():
        fill(even_ref, odd_ref)


def join(own, other, columns, area):
    return pl.pallas_call(
        functools.partial(join_kernel, area),
        in_specs=[VMEM] * 3,
        out_specs=[VMEM] * 2,
        out_shape=[jax.ShapeDtypeStruct((3, *own.shape[1:]), BF16)] * 2,
        compiler_params=params(),
        cost_estimate=cost(0, 2**17),
        name="join",
    )(own, other, columns)


def pair_wgrad_kernel(*refs):
    x_ref, acc_ref, g3, x3 = refs[7:]
    weight_products(refs, None, x_ref, g3, x3, acc_ref)


def pair_wgrad(sources, planes_x, shape):
    channels = shape[0]
    return pl.pallas_call(
        pair_wgrad_kernel,
        in_specs=[VMEM] * 8,
        out_specs=VMEM,
        out_shape=jax.ShapeDtypeStruct((9 * channels, 3 * channels), F32),
        scratch_shapes=[g3_scratch(*shape), x3_scratch(*shape)],
        compiler_params=params(32 * 2**20),
        cost_estimate=wgrad_cost(*shape),
        name="wgrad",
    )(*sources, planes_x)


def finish_kernel(scale, rows, sizes, *refs):
    acc_ref, columns_ref, even_ref, odd_ref, from_odd_ref, from_even_ref = refs[:6]
    part_ref, chunks = refs[6:]
    size_x, size_y = sizes
    channels = columns_ref.shape[0]
    area = size_x * size_y
    odd = is_odd("gz")
    lane = lax.broadcasted_iota(jnp.int32, (channels, LANES), 1)
    row = lane % size_y
    jump = area - size_y + 1
    below = [either(odd, from_even_ref[k], from_odd_ref[k]) for k in range(3)]
    own = [either(odd, even_ref[k], odd_ref[k]) for k in range(2)]
    pairs = ((below[:2], own_columns(columns_ref[...], 0, area)), (own, below[2]))
    edges = []
    for tiles, value in pairs:
        before = jnp.where(lane >= area, pltpu.roll(value, jump, 1), 0.0)
        after = jnp.where(lane < area, pltpu.roll(value, LANES - jump, 1), 0.0)
        right = jnp.concatenate(
            [
                jnp.where(row > 0, pltpu.roll(value, 1, 1), before),
                value,
                jnp.where(row < size_y - 1, pltpu.roll(value, LANES - 1, 1), after),
            ],
            axis=0,
        )
        left = []
        for a in range(3):
            first = pltpu.roll(tiles[0], -a * size_y % LANES, 1)
            second = pltpu.roll(tiles[1], (area - a * size_y) % LANES, 1)
            left.append(jnp.where(lane < area, first, jnp.where(lane < 2 * area, second, 0.0)))
        edges.append(
            lax.dot_general(
                jnp.concatenate(left, axis=0).astype(BF16),
                right.astype(BF16),
                (((1,), (1,)), ((), ())),
                preferred_element_type=F32,
            )
        )
    count = part_ref.shape[0]
    height, width = chunks.shape[0] // count, LANES
    chunks[...] = jnp.zeros_like(chunks)
    pieces = rows * acc_ref.shape[1] // width
    for a in range(3):
        for c in range(3):
            at = 3 * a + c
            block = acc_ref[at * channels : (at + 1) * channels, :]
            if c != 1:
                block = block + edges[c // 2][a * channels : (a + 1) * channels]
            block = block * scale
            line = jnp.concatenate(
                [block[r * count : (r + 1) * count] for r in range(rows)], axis=1
            )
            for k in range(pieces):
                chunks[pl.ds(at * pieces + k, count, stride=height), :] = line[
                    :, k * width : (k + 1) * width
                ]

    def write(at, quads):
        part_ref[:, :, at] = quads.astype(BF16)

    whole = chunks[...].reshape(count, height, width)
    to_quads(whole[:, : part_ref.shape[2] // LANES * QUAD], write)


def finish(acc, columns, sent, received, scale, rows, sizes, part_shape):
    channels = columns.shape[0]
    return pl.pallas_call(
        functools.partial(finish_kernel, scale, rows, sizes),
        in_specs=[VMEM] * 6,
        out_specs=VMEM,
        out_shape=jax.ShapeDtypeStruct(part_shape, BF16),
        scratch_shapes=[
            pltpu.VMEM((part_shape[0] * -(-part_shape[2] // LANES * QUAD // 8) * 8, LANES), F32),
        ],
        compiler_params=params(),
        cost_estimate=cost(2**27, 2**21),
        name="finish",
    )(acc, columns, *sent, *received)


def adam_step(master, first, second, weight_grad):
    new_first = 0.9 * first + 0.1 * weight_grad
    new_second = 0.999 * second + 0.001 * weight_grad * weight_grad
    corr_first = 1.0 - (0.9**10) ** 10
    corr_second = 1.0 - (0.999**10) ** 10
    update = new_first / corr_first / (jnp.sqrt(new_second / corr_second) + 1e-08) + 0.01 * master
    return master - 0.05 * update, new_first, new_second


def in_flat_order(value, rows, places, spread_rows):
    taps = 27
    lane = lax.broadcasted_iota(jnp.int32, (9, LANES), 1)
    for k in range(value.shape[1] // LANES):
        rows[k * QUAD : (k + 1) * QUAD, :] = value[:, k * LANES : (k + 1) * LANES]
    thirds = [rows[pl.ds(k, 9, stride=3), :] for k in range(3)]
    half = LANES // 2
    by_y = (
        jnp.where(lane < half, thirds[0], thirds[1]),
        jnp.where(lane < half, pltpu.roll(thirds[0], half, 1), pltpu.roll(thirds[2], half, 1)),
        jnp.where(lane < half, thirds[1], thirds[2]),
    )
    places[...] = jnp.zeros_like(places)
    for b in range(3):
        spread_rows[b, :9, :] = by_y[b]
        for block in range(9):
            tap = (2 - block // 3) * 9 + b * 3 + 2 - block % 3
            places[tap : tap + 1, :] = spread_rows[b, block : block + 1, :]
    line = places[...].T
    number = lax.broadcasted_iota(jnp.int32, (LANES, LANES), 0) * taps
    column = lax.broadcasted_iota(jnp.int32, (LANES, LANES), 1)
    turned = []
    for group in range(LANES // 8):
        piece = line[8 * group : 8 * (group + 1)]
        rest = 8 * group * taps % LANES
        for step in range(3):
            turn = rest // (3 - step)
            rest -= turn
            piece = pltpu.roll(piece, turn, 1, stride=taps // 3, stride_axis=0)
        turned.append(piece)
    line = jnp.concatenate(turned, axis=0)
    start = number & (LANES - 1)
    line = jnp.concatenate(
        [jnp.where(column >= start, line, 0.0), jnp.where(column < start, line, 0.0)], axis=0
    )
    target = lax.broadcasted_iota(jnp.int32, (32, 2 * LANES), 0)
    source = lax.broadcasted_iota(jnp.int32, (32, 2 * LANES), 1)
    goes = lax.shift_right_logical((source & (LANES - 1)) * taps, 7)
    goes = goes + jnp.where(source < LANES, 0, 1)
    pick = jnp.where(goes == target, 1.0, 0.0).astype(BF16)
    parts = []
    for _ in range(3):
        parts.append(line.astype(BF16))
        line = line - parts[-1].astype(F32)
    return jnp.dot(
        jnp.concatenate([pick] * 3, axis=1),
        jnp.concatenate(parts, axis=0),
        preferred_element_type=F32,
    )[:taps]


def adam_kernel(parts_ref, master_ref, first_ref, second_ref, *refs):
    out_refs, scratch = refs[:4], refs[4:]
    total = parts_ref[0].astype(F32)
    for source in range(1, parts_ref.shape[0]):
        total = total + parts_ref[source].astype(F32)
    weight_grad = in_flat_order(total, *scratch)
    results = adam_step(master_ref[...], first_ref[...], second_ref[...], weight_grad)
    for out_ref, result in zip(out_refs, (weight_grad, *results)):
        out_ref[...] = result


def adam(parts, *states):
    share = states[0].shape[0]
    tiled = [state.reshape(share // LANES, LANES) for state in states]
    result = jax.ShapeDtypeStruct(tiled[0].shape, F32)
    outs = pl.pallas_call(
        adam_kernel,
        in_specs=[VMEM] * 4,
        out_specs=[VMEM] * 4,
        out_shape=[result] * 4,
        scratch_shapes=[
            pltpu.VMEM((32, LANES), F32),
            pltpu.VMEM((LANES, LANES), F32),
            pltpu.VMEM((3, 16, LANES), F32),
        ],
        compiler_params=params(),
        cost_estimate=cost(2**22, 2**19),
        name="adam",
    )(parts, *tiled)
    return tuple(out.reshape(share) for out in outs)


def spread_kernel(rows, w_ref, weights_ref, turned, chunks):
    count = w_ref.shape[0]
    height = chunks.shape[0] // count
    taps = 27 * rows * count
    quads = [
        w_ref[:, :, k * LANES : (k + 1) * LANES].astype(F32)
        for k in range(w_ref.shape[2] // LANES)
    ]
    spare = jnp.zeros((count, height - QUAD * len(quads), LANES), F32)
    chunks[...] = jnp.concatenate(quads + [spare], axis=1).reshape(chunks.shape)
    line = jnp.concatenate(
        [chunks[pl.ds(k, count, stride=height), :] for k in range(rows * taps // LANES)], axis=1
    )
    whole = jnp.concatenate([line[:, r * taps : (r + 1) * taps] for r in range(rows)], axis=0)
    spread_weights(whole, turned, weights_ref)


def spread(kernel, channels, rows):
    return pl.pallas_call(
        functools.partial(spread_kernel, rows),
        in_specs=[VMEM],
        out_specs=VMEM,
        out_shape=jax.ShapeDtypeStruct((3, 2 * channels, 12 * channels), BF16),
        scratch_shapes=[
            flat_scratch(channels),
            pltpu.VMEM((kernel.shape[0] * 32, LANES), F32),
        ],
        compiler_params=params(),
        cost_estimate=cost(2**20, 2**21),
        name="spread",
    )(kernel)


def pair_dgrad_kernel(*refs):
    weights_ref, out_ref, g3, tile = refs[9:]
    _, size_x, size_y, size_z = out_ref.shape
    halo = pair_z_halo(refs[7], refs[8], size_x + 2, size_y, size_z)
    input_products(refs, halo, g3, weights_ref, tile, out_ref)


def pair_dgrad(sources, weights, shape):
    channels, _, size_y, size_z = shape
    return pl.pallas_call(
        pair_dgrad_kernel,
        in_specs=[VMEM] * 10,
        out_specs=VMEM,
        out_shape=jax.ShapeDtypeStruct(shape, BF16),
        scratch_shapes=[g3_scratch(*shape), pltpu.VMEM((2, channels * size_y, size_z), F32)],
        compiler_params=params(32 * 2**20),
        cost_estimate=dgrad_cost(*shape),
        name="dgrad",
    )(*sources, weights)


def pair_program(activations, preact, upstream, master, first_moment, second_moment, scale):
    shape = activations.shape
    channels, size_x, size_y, _ = shape
    devices = math.prod(lax.axis_size(a) for a in AXES)
    rows = channels // devices
    used = master.shape[0] // LANES
    block = (devices, QUAD, -(-used // QUAD) * LANES)
    first, last, odd_sent = faces(preact, upstream, "gx", rows)
    odd_halves = swapped(odd_sent, "gx", 1)
    inner, own, even_sent, sent = pair_inner(
        preact, upstream, first, last, master.reshape(used, LANES), block, rows
    )
    even_halves = swapped(even_sent, "gx", 0)
    kernel = lax.all_to_all(sent, AXES, 0, 0, tiled=True)
    own, xlo, xhi = side((odd_halves, even_halves), own)
    planes = (xlo, first, inner, last, xhi)
    own, activations = lax.optimization_barrier((own, activations))
    other = shifted(own, {"gy": "swap"})
    planes_x, columns = input_planes(activations, True)
    z_sent = join(own, other, columns, size_x * size_y)
    from_odd = swapped(z_sent[1], "gz", 1)
    from_even = swapped(z_sent[0], "gz", 0)
    sources = (*planes, other, other)
    acc = pair_wgrad(sources, planes_x, shape)
    z_received = (from_odd, from_even)
    part = finish(acc, columns, z_sent, z_received, scale, rows, (size_x, size_y), block)
    part, kernel = lax.optimization_barrier((part, kernel))
    parts = lax.all_to_all(part, AXES, 0, 0, tiled=True)
    weights = spread(kernel, channels, rows)
    grad_input = pair_dgrad((*sources, *z_received), weights, shape)
    return grad_input, *adam(parts, master, first_moment, second_moment)


def yface_kernel(*refs):
    low_ref, high_ref = refs[5:]
    size_z = low_ref.shape[-1]
    for index in range(low_ref.shape[0]):
        body = body_of(refs[:5], index)
        plane = body.shape[-1]
        low_ref[index] = body[:, :size_z]
        high_ref[index] = body[:, plane - size_z :]


def y_faces(planes, size_z):
    inner, channels, _ = planes[2].shape
    face = jax.ShapeDtypeStruct((inner + 4, channels, size_z), BF16)
    return pl.pallas_call(
        yface_kernel,
        in_specs=[VMEM] * 5,
        out_specs=[VMEM] * 2,
        out_shape=[face] * 2,
        compiler_params=params(),
        cost_estimate=cost(0, 2**19),
        name="yfaces",
    )(*planes)


def zface_kernel(*refs):
    zlo_ref, zhi_ref = refs[7:]
    size_z = refs[5].shape[-1]
    whole = []
    for index in range(refs[5].shape[0]):
        low, high = y_halo(refs[5:7], index)
        body = body_of(refs[:5], index)[...]
        whole.append(jnp.concatenate([low.astype(BF16), body, high.astype(BF16)], axis=1))
    low, high = z_tiles(whole, whole[0].shape[1] // size_z, size_z, range(len(whole)))
    zlo_ref[...] = low.astype(BF16)
    zhi_ref[...] = high.astype(BF16)


def z_faces(planes, y_halos):
    face = jax.ShapeDtypeStruct((planes[0].shape[0], LANES), BF16)
    return pl.pallas_call(
        zface_kernel,
        in_specs=[VMEM] * 7,
        out_specs=[VMEM] * 2,
        out_shape=[face, face],
        compiler_params=params(),
        cost_estimate=cost(2**27, 2**21),
        name="zfaces",
    )(*planes, *y_halos)


def wgrad_kernel(scale, *refs):
    x_ref, part_ref, g3, x3, acc, flat = refs[9:]
    size_x, channels, plane = x_ref.shape
    size_z = refs[5].shape[-1]
    halo = z_halo(refs[7], refs[8], size_x + 2, plane // size_z + 2, size_z)
    weight_products(refs, halo, x_ref, g3, x3, acc)
    whole = to_flat(acc[...] * scale, channels, channels, flat)
    part_ref[...] = whole[:, : part_ref.shape[1]].astype(BF16)


def wgrad(sources, planes_x, shape, scale):
    channels = shape[0]
    return pl.pallas_call(
        functools.partial(wgrad_kernel, scale),
        in_specs=[VMEM] * 10,
        out_specs=VMEM,
        out_shape=jax.ShapeDtypeStruct((channels, 27 * channels), BF16),
        scratch_shapes=[
            g3_scratch(*shape),
            x3_scratch(*shape),
            acc_scratch(channels),
            flat_scratch(channels),
        ],
        compiler_params=params(32 * 2**20),
        cost_estimate=wgrad_cost(*shape),
        name="wgrad",
    )(*sources, planes_x)


def dgrad_kernel(*refs):
    w_ref, out_ref, g3, turned, weights, tile = refs[9:]
    _, size_x, size_y, size_z = out_ref.shape
    spread_weights(w_ref[...].astype(F32), turned, weights)
    halo = z_halo(refs[7], refs[8], size_x + 2, size_y + 2, size_z)
    input_products(refs, halo, g3, weights, tile, out_ref)


def dgrad(sources, kernel, shape):
    return pl.pallas_call(
        dgrad_kernel,
        in_specs=[VMEM] * 10,
        out_specs=VMEM,
        out_shape=jax.ShapeDtypeStruct(shape, BF16),
        scratch_shapes=dgrad_scratch(*shape),
        compiler_params=params(32 * 2**20),
        cost_estimate=dgrad_cost(*shape),
        name="dgrad",
    )(*sources, kernel)


def general_program(activations, preact, upstream, master, first_moment, second_moment, scale):
    shape = activations.shape
    channels, _, _, size_z = shape
    devices = math.prod(lax.axis_size(a) for a in AXES)
    share = master.shape[0]
    first, last = faces(preact, upstream)
    x_halos = (shifted(last, {"gx": 1}), shifted(first, {"gx": -1}))
    inner = inner_planes(preact, upstream)
    (planes_x,) = input_planes(activations, False)
    sent = jnp.broadcast_to(master.astype(BF16).reshape(1, 1, share), (devices, 1, share))
    kernel = lax.all_to_all(sent, AXES, 0, 0, tiled=True).reshape(channels, 27 * channels)
    planes = (x_halos[0], first, inner, last, x_halos[1])
    y_sent = y_faces(planes, size_z)
    y_halos = (shifted(y_sent[1], {"gy": 1}), shifted(y_sent[0], {"gy": -1}))
    zlo, zhi = z_faces(planes, y_halos)
    z_halos = (shifted(zhi, {"gz": 1}), shifted(zlo, {"gz": -1}))
    sources = (*planes, *y_halos, *z_halos)
    part = wgrad(sources, planes_x, shape, scale)
    part, kernel = lax.optimization_barrier((part, kernel))
    parts = lax.all_to_all(part.reshape(devices, 1, share), AXES, 0, 0, tiled=True)
    grad_input = dgrad(sources, kernel, shape)
    weight_grad = jnp.sum(parts.astype(F32), axis=0).reshape(-1)
    results = adam_step(master, first_moment, second_moment, weight_grad)
    return grad_input, weight_grad, *results


def shifted(value, moves):
    names = tuple(moves)
    sizes = [lax.axis_size(name) for name in names]
    pairs = []
    for source in range(math.prod(sizes)):
        rest, coords = source, []
        for size in reversed(sizes):
            coords.insert(0, rest % size)
            rest //= size
        coords = [
            (at + moves[name]) if moves[name] != "swap" else 1 - at
            for at, name in zip(coords, names)
        ]
        if all(0 <= at < size for at, size in zip(coords, sizes)):
            target = 0
            for at, size in zip(coords, sizes):
                target = target * size + at
            pairs.append((source, target))
    return lax.ppermute(value, names if len(names) > 1 else names[0], pairs)


def swapped(value, axis, start):
    pairs = []
    for low in range(start, lax.axis_size(axis) - 1, 2):
        pairs += [(low, low + 1), (low + 1, low)]
    return lax.ppermute(value, axis, pairs)


def local(activations, preact, upstream, master, first_moment, second_moment):
    channels, size_x, size_y, size_z = activations.shape
    devices = math.prod(lax.axis_size(a) for a in AXES)
    share = master.shape[0]
    scale = 1.0 / math.sqrt(size_x * size_y * size_z * devices)
    in_pairs = (
        lax.axis_size("gy") == 2
        and channels % devices == 0
        and share % LANES == 0
        and channels // devices * channels == LANES
        and 2 * size_x * size_y <= LANES
        and (size_x + 2) * size_y <= LANES
    )
    program = pair_program if in_pairs else general_program
    return program(
        activations, preact, upstream, master, first_moment, second_moment, scale
    )


def solution(mesh):
    volume = P(None, "gx", "gy", "gz")
    flat = P(AXES)
    return jax.shard_map(
        local,
        mesh=mesh,
        in_specs=(volume, volume, volume, flat, flat, flat),
        out_specs=(volume, flat, flat, flat, flat),
        check_vma=False,
    )
```

```python
import functools
import math

import jax
import jax.numpy as jnp
from jax import lax
from jax.experimental import pallas as pl
from jax.experimental.pallas import tpu as pltpu
from jax.sharding import PartitionSpec as P

AXES = ("gx", "gy", "gz")
LANES = 128
VMEM = pl.BlockSpec(memory_space=pltpu.VMEM)
HBM = pl.BlockSpec(memory_space=pltpu.HBM)
F32 = jnp.float32
BF16 = jnp.bfloat16
FACES_VMEM = 55_900_000
INNER_VMEM = 54_800_000
ENDS_VMEM = 54_800_000
MIDDLES_VMEM = 54_600_000


def params(limit=24 * 2**20):
    return pltpu.CompilerParams(vmem_limit_bytes=limit)


def cost(flops, moved):
    return pl.CostEstimate(flops=flops, bytes_accessed=moved, transcendentals=0)


def to_planes(value, tile, write, rows=1):
    channels, size_y, size_z = value.shape
    count = channels // rows
    tile[...] = value.astype(F32).reshape(channels * size_y, size_z)
    for y in range(size_y):
        for r in range(rows):
            picked = tile[pl.ds(r * size_y + y, count, stride=rows * size_y), :]
            write(slice(r * count, (r + 1) * count), y, picked.astype(BF16))


QUAD = 4


def to_quads(rows, write):
    for k in range(rows.shape[-2] // QUAD):
        write(slice(k * LANES, (k + 1) * LANES), rows[..., k * QUAD : (k + 1) * QUAD, :])


def masked(p, u):
    return jnp.where(p.astype(F32) > 0, u.astype(F32), 0.0)


def choose(condition, out_ref, first_ref, second_ref):
    @pl.when(condition)
    def _():
        out_ref[...] = first_ref[...]

    @pl.when(jnp.logical_not(condition))
    def _():
        out_ref[...] = second_ref[...]


def face_kernel(axis, rows, p_ref, u_ref, *refs):
    p_buf, u_buf, tile, sems = refs[-4:]
    out_refs, swap_refs = refs[:2], refs[2:-4]
    size_x, size_z = p_ref.shape[1], p_ref.shape[3]
    copies = []
    for k, x in enumerate((0, size_x - 1)):
        pair = (
            pltpu.make_async_copy(p_ref.at[:, x], p_buf.at[k], sems.at[2 * k]),
            pltpu.make_async_copy(u_ref.at[:, x], u_buf.at[k], sems.at[2 * k + 1]),
        )
        for copy in pair:
            copy.start()
        copies.append(pair)
    for k, out_ref in enumerate(out_refs):
        for copy in copies[k]:
            copy.wait()

        def write(at, y, value):
            out_ref[at, y * size_z : (y + 1) * size_z] = value

        to_planes(masked(p_buf[k], u_buf[k]), tile.at[k], write, rows)
    if axis is not None:
        choose(is_odd(axis), swap_refs[0], out_refs[1], out_refs[0])


def faces(preact, upstream, axis=None, rows=1):
    channels, size_x, size_y, size_z = preact.shape
    face = jax.ShapeDtypeStruct((channels, size_y * size_z), BF16)
    buffer = pltpu.VMEM((2, channels, size_y, size_z), BF16)
    count = 2 if axis is None else 3
    return pl.pallas_call(
        functools.partial(face_kernel, axis, rows),
        in_specs=[HBM, HBM],
        out_specs=[VMEM] * count,
        out_shape=[face] * count,
        scratch_shapes=[
            buffer,
            buffer,
            pltpu.VMEM((2, channels * size_y, size_z), F32),
            pltpu.SemaphoreType.DMA((4,)),
        ],
        compiler_params=params(FACES_VMEM),
        cost_estimate=cost(0, 2**20),
        name="faces",
    )(preact, upstream)


def fetches(planes, p_ref, u_ref, p_buf, u_buf, sems):
    return [
        (
            pltpu.make_async_copy(p_ref.at[:, x + 1], p_buf.at[x], sems.at[2 * x]),
            pltpu.make_async_copy(u_ref.at[:, x + 1], u_buf.at[x], sems.at[2 * x + 1]),
        )
        for x in planes
    ]


def start(copies):
    for pair in copies:
        for copy in pair:
            copy.start()


def settle(order, planes, copies, g_ref, p_buf, u_buf, tile):
    size_z = p_buf.shape[-1]
    for x, pair in zip(planes, copies):
        for copy in pair:
            copy.wait()

        def write(at, y, value):
            g_ref[x, at, y * size_z : (y + 1) * size_z] = value

        to_planes(masked(p_buf[x], u_buf[x]), tile.at[x % 2], write, order)


def read_inner(order, planes, p_ref, u_ref, g_ref, p_buf, u_buf, tile, sems):
    copies = fetches(planes, p_ref, u_ref, p_buf, u_buf, sems)
    start(copies)
    settle(order, planes, copies, g_ref, p_buf, u_buf, tile)


def inner_kernel(*refs):
    read_inner(1, range(refs[2].shape[0]), *refs)


def inner_output(channels, size_x, size_y, size_z):
    return jax.ShapeDtypeStruct((size_x - 2, channels, size_y * size_z), BF16)


def inner_scratch(channels, size_x, size_y, size_z):
    return [
        pltpu.VMEM((size_x - 2, channels, size_y, size_z), BF16),
        pltpu.VMEM((size_x - 2, channels, size_y, size_z), BF16),
        pltpu.VMEM((2, channels * size_y, size_z), F32),
        pltpu.SemaphoreType.DMA((2 * size_x - 4,)),
    ]


def inner_planes(preact, upstream):
    shape = preact.shape
    return pl.pallas_call(
        inner_kernel,
        in_specs=[HBM] * 2,
        out_specs=VMEM,
        out_shape=inner_output(*shape),
        scratch_shapes=inner_scratch(*shape),
        compiler_params=params(INNER_VMEM),
        cost_estimate=cost(0, 4 * 2**20),
        name="inner",
    )(preact, upstream)


def input_kernel(a_ref, x_ref, *refs):
    tile = refs[-1]
    channels, size_x, size_y, size_z = a_ref.shape
    for x in range(size_x):

        def write(at, y, value):
            x_ref[x, at, y * size_z : (y + 1) * size_z] = value

        to_planes(a_ref[:, x], tile.at[x % 2], write)
    if len(refs) > 1:
        low, high = z_tiles([x_ref[x] for x in range(size_x)], size_y, size_z, range(size_x))
        refs[0][...] = (low + pltpu.roll(high, size_x * size_y, 1)).astype(BF16)


def input_planes(activations, with_columns):
    channels, size_x, size_y, size_z = activations.shape
    outs = [jax.ShapeDtypeStruct((size_x, channels, size_y * size_z), BF16)]
    if with_columns:
        outs.append(jax.ShapeDtypeStruct((channels, LANES), BF16))
    return pl.pallas_call(
        input_kernel,
        in_specs=[VMEM],
        out_specs=[VMEM] * len(outs),
        out_shape=outs,
        scratch_shapes=[pltpu.VMEM((2, channels * size_y, size_z), F32)],
        compiler_params=params(),
        cost_estimate=cost(0, 2 * 2**20),
        name="inputs",
    )(activations)


def body_of(refs, index):
    planes = refs[2].shape[0] + 4
    if 2 <= index < planes - 2:
        return refs[2].at[index - 2]
    return refs[{0: 0, 1: 1, planes - 2: 3, planes - 1: 4}[index]]


def y_halo(refs, index):
    me = lax.axis_index("gy")
    low = jnp.where(me > 0, refs[0][index].astype(F32), 0.0)
    high = jnp.where(me < lax.axis_size("gy") - 1, refs[1][index].astype(F32), 0.0)
    return low, high


def z_picker(rows_y, size_z):
    shape = (rows_y * size_z, 2 * LANES)
    voxel = lax.broadcasted_iota(jnp.int32, shape, 0)
    lane = lax.broadcasted_iota(jnp.int32, shape, 1)
    wanted = jnp.where(lane < LANES, lane * size_z, (lane - LANES) * size_z + size_z - 1)
    return (voxel == wanted).astype(F32).astype(BF16)


def z_tiles(planes, rows_y, size_z, numbers):
    channels = planes[0].shape[0]
    columns = jnp.dot(
        jnp.concatenate(planes, axis=0), z_picker(rows_y, size_z), preferred_element_type=F32
    )
    low = jnp.zeros((channels, LANES), F32)
    high = jnp.zeros((channels, LANES), F32)
    for index, number in enumerate(numbers):
        rows = columns[index * channels : (index + 1) * channels]
        low = low + pltpu.roll(rows[:, :LANES], number * rows_y, 1)
        high = high + pltpu.roll(rows[:, LANES:], number * rows_y, 1)
    return low, high


def put_columns(columns, row_of, rows_y, size_z):
    shape = (2 * LANES, rows_y * size_z)
    source = lax.broadcasted_iota(jnp.int32, shape, 0)
    voxel = lax.broadcasted_iota(jnp.int32, shape, 1)
    number = source % LANES
    place = row_of(number) * size_z + jnp.where(source < LANES, 0, size_z - 1)
    place = jnp.where(number < rows_y, place, -1)
    put = (voxel == place).astype(F32).astype(BF16)
    rows = [jnp.concatenate(pair, axis=1) for pair in columns]
    return jnp.dot(
        jnp.concatenate(rows, axis=0).astype(BF16), put, preferred_element_type=F32
    ).astype(BF16)


def z_halo(low_ref, high_ref, planes, rows_y, size_z):
    columns = []
    for index in range(planes):
        shift = -index * rows_y % LANES
        columns.append(
            [pltpu.roll(ref[...].astype(F32), shift, 1) for ref in (low_ref, high_ref)]
        )
    return put_columns(columns, lambda number: number, rows_y, size_z)


def pair_z_halo(odd_ref, even_ref, planes, size_y, size_z):
    me, odd = lax.axis_index("gy"), is_odd("gz")
    sides = []
    for low, high in ((even_ref, odd_ref), (odd_ref, even_ref)):
        first, second = (either(odd, low[k], high[k]) for k in range(2))
        lane = lax.broadcasted_iota(jnp.int32, first.shape, 1)
        own = jnp.where(me == 0, first, second)
        before = jnp.where(me == 0, 0.0, first)
        after = jnp.where(me == 0, second, 0.0)
        columns = []
        for index in range(planes):
            start = index * size_y
            columns.append(
                jnp.where(
                    lane < size_y,
                    pltpu.roll(own, -start % LANES, 1),
                    jnp.where(
                        lane == size_y,
                        pltpu.roll(before, (1 - start) % LANES, 1),
                        pltpu.roll(after, (size_y + 1 - start) % LANES, 1),
                    ),
                )
            )
        sides.append(columns)

    def row_of(number):
        return jnp.where(number < size_y, number + 1, jnp.where(number == size_y, 0, size_y + 1))

    return put_columns(list(zip(*sides)), row_of, size_y + 2, size_z)


def shifted_plane(index, refs, halo, g3):
    channels, plane = refs[0].shape
    size_z = refs[5].shape[-1]
    rows_y = plane // size_z + 2
    base = 3 * channels * index
    lane = lax.broadcasted_iota(jnp.int32, (channels, size_z), 1)
    is_first, is_last = lane == 0, lane == size_z - 1
    low, high = y_halo(refs[5:7], index)
    body = body_of(refs[:5], index)
    for row in range(rows_y):
        cols = slice(row * size_z, (row + 1) * size_z)
        if row == 0:
            value = low.astype(BF16)
        elif row == rows_y - 1:
            value = high.astype(BF16)
        else:
            value = body[:, (row - 1) * size_z : row * size_z]
        if halo is None:
            edge = jnp.zeros_like(value)
        else:
            edge = halo[index * channels : (index + 1) * channels, cols]
        before = jnp.where(is_first, edge, pltpu.roll(value, 1, 1))
        after = jnp.where(is_last, edge, pltpu.roll(value, size_z - 1, 1))
        g3[base : base + channels, cols] = before
        g3[base + channels : base + 2 * channels, cols] = value
        g3[base + 2 * channels : base + 3 * channels, cols] = after


def weight_products(refs, halo, x_ref, g3, x3, acc):
    size_x, channels, plane = x_ref.shape
    size_z = refs[5].shape[-1]
    group = 3 * channels
    zero = jnp.zeros((channels, 2 * size_z), BF16)
    done = 0
    for x in range(0, size_x, 2):
        while done < x + 4:
            shifted_plane(done, refs, halo, g3)
            done += 1
        for plane_x in (x, x + 1):
            value = x_ref[plane_x]
            for b in range(3):
                at = slice(b * channels, (b + 1) * channels)
                start = (2 - b) * size_z
                x3[plane_x, at, start : start + plane] = value
                if start:
                    x3[plane_x, at, :start] = zero[:, :start]
                if start < 2 * size_z:
                    x3[plane_x, at, start + plane :] = zero[:, start:]
        product = lax.dot_general(
            jnp.concatenate(
                [g3[x * group : (x + 3) * group, :], g3[(x + 1) * group : (x + 4) * group, :]],
                axis=1,
            ),
            jnp.concatenate([x3[x], x3[x + 1]], axis=1),
            (((1,), (1,)), ((), ())),
            preferred_element_type=F32,
        )
        if x == 0:
            acc[...] = product
        else:
            acc[...] += product


def to_flat(value, count, channels, flat):
    height, width = value.shape
    wide = value
    if height % LANES:
        wide = jnp.concatenate([wide, jnp.zeros((-height % LANES, width), F32)], axis=0)
    if width % LANES:
        wide = jnp.concatenate([wide, jnp.zeros((wide.shape[0], -width % LANES), F32)], axis=1)
    turned = wide.T
    for b in range(3):
        rows = turned[b * channels : (b + 1) * channels]
        for block in range(9):
            start = block * count
            cell = rows[:, start // LANES * LANES : (start // LANES + 1) * LANES]
            tap = (2 - block // 3) * 9 + b * 3 + 2 - block % 3
            shift = -start % LANES
            flat[pl.ds(tap, channels, stride=27), :] = pltpu.roll(cell, shift, 1) if shift else cell
    return flat[...].T[:count]


def spread_weights(whole, turned, weights):
    channels, taps = whole.shape
    group = 3 * channels
    whole = jnp.concatenate([whole, jnp.zeros((LANES - channels, taps), F32)], axis=0)
    whole = jnp.concatenate([whole, jnp.zeros((LANES, -taps % LANES), F32)], axis=1)
    turned[...] = whole.T
    for b in range(3):
        blocks = []
        for a in range(3):
            for c in range(3):
                tap = (2 - a) * 9 + (2 - b) * 3 + 2 - c
                blocks.append(turned[pl.ds(tap, channels, stride=27), :][:, :channels])
        zero = jnp.zeros((channels, group), F32)
        weights[b, :channels] = jnp.concatenate(blocks + [zero], axis=1).astype(BF16)
        weights[b, channels:] = jnp.concatenate([zero] + blocks, axis=1).astype(BF16)


def input_products(refs, halo, g3, weights, tile, out_ref):
    channels, size_x, size_y, size_z = out_ref.shape
    group = 3 * channels
    plane = size_y * size_z
    done = 0
    for pair in range(size_x // 2):
        while done < 2 * pair + 4:
            shifted_plane(done, refs, halo, g3)
            done += 1
        at = slice(2 * pair * group, (2 * pair + 4) * group)
        total = None
        for b in range(3):
            product = jnp.dot(
                weights[b],
                g3[at, b * size_z : b * size_z + plane],
                preferred_element_type=F32,
            )
            total = product if total is None else total + product
        for half in range(2):
            for y in range(size_y):
                tile[half, pl.ds(y, channels, stride=size_y), :] = total[
                    half * channels : (half + 1) * channels, y * size_z : (y + 1) * size_z
                ]
            out_ref[:, 2 * pair + half] = (
                tile[half].reshape(channels, size_y, size_z).astype(BF16)
            )


def g3_scratch(channels, size_x, size_y, size_z):
    return pltpu.VMEM(((size_x + 2) * 3 * channels, (size_y + 2) * size_z), BF16)


def x3_scratch(channels, size_x, size_y, size_z):
    return pltpu.VMEM((size_x, 3 * channels, (size_y + 2) * size_z), BF16)


def acc_scratch(channels):
    return pltpu.VMEM((9 * channels, 3 * channels), F32)


def flat_scratch(channels):
    return pltpu.VMEM((-(-27 * channels // LANES) * LANES, LANES), F32)


def dgrad_scratch(channels, size_x, size_y, size_z):
    return [
        g3_scratch(channels, size_x, size_y, size_z),
        flat_scratch(channels),
        pltpu.VMEM((3, 2 * channels, 12 * channels), BF16),
        pltpu.VMEM((2, channels * size_y, size_z), F32),
    ]


def wgrad_cost(channels, size_x, size_y, size_z):
    return cost(54 * channels * channels * size_x * (size_y + 2) * size_z, 4 * 2**20)


def dgrad_cost(channels, size_x, size_y, size_z):
    return cost(72 * channels * channels * size_x * size_y * size_z, 4 * 2**20)


def row_for_other(body, size_z):
    plane = body.shape[-1]
    low, high = body[:, :size_z].astype(F32), body[:, plane - size_z :].astype(F32)
    return jnp.where(lax.axis_index("gy") == 0, high, low).astype(BF16)


def in_odd_swaps(axis):
    me, count = lax.axis_index(axis), lax.axis_size(axis)
    return (me > 0) & (me < count - 1 + count % 2)


def ends_kernel(order, *refs):
    choose(is_odd("gx"), refs[5], refs[2], refs[3])

    @pl.when(jnp.logical_not(in_odd_swaps("gx")))
    def _():
        read_inner(order, range(refs[4].shape[0]), *refs[:2], refs[4], *refs[6:])


def middles_kernel(order, *refs):
    p_ref, u_ref, first_ref, last_ref, m_ref, before_ref, g_ref, side_ref, sent_ref = refs[:9]
    p_buf, u_buf, tile, sems, sent_buf, sent_sem = refs[9:]
    half = before_ref.shape[0]
    inner, _, plane = g_ref.shape
    later = range(half, inner)
    middle = in_odd_swaps("gx")
    first_copies = fetches(range(half), p_ref, u_ref, p_buf, u_buf, sems)
    later_copies = fetches(later, p_ref, u_ref, p_buf, u_buf, sems)

    @pl.when(middle)
    def _():
        start(first_copies)

    start(later_copies)
    share = m_ref[...]
    share = jnp.concatenate(
        [share, jnp.zeros((-share.shape[0] % QUAD, share.shape[1]), F32)], axis=0
    )

    def write(at, quad):
        quad = quad.astype(BF16)
        sent_buf[:, :, at] = jnp.broadcast_to(quad[None], (sent_buf.shape[0], *quad.shape))

    to_quads(share, write)
    send = pltpu.make_async_copy(sent_buf, sent_ref, sent_sem)
    send.start()

    @pl.when(middle)
    def _():
        settle(order, range(half), first_copies, g_ref, p_buf, u_buf, tile)

    @pl.when(jnp.logical_not(middle))
    def _():
        g_ref[:half] = before_ref[...]

    settle(order, later, later_copies, g_ref, p_buf, u_buf, tile)
    size_z = side_ref.shape[-1]
    size_x = inner + 2
    bodies = [first_ref] + [g_ref.at[x] for x in range(inner)] + [last_ref]
    for x, body in enumerate(bodies):
        side_ref[x] = row_for_other(body, size_z)
    low, high = z_tiles(
        [body[...] for body in bodies], plane // size_z, size_z, range(1, size_x + 1)
    )
    side_ref[size_x] = low.astype(BF16)
    side_ref[size_x + 1] = high.astype(BF16)
    send.wait()


def pair_inner(preact, upstream, first, last, share, sent_shape, order):
    shape = preact.shape
    channels, size_x, _, size_z = shape
    made = [
        inner_output(*shape),
        jax.ShapeDtypeStruct((size_x + 2, channels, size_z), BF16),
    ]
    half = jax.ShapeDtypeStruct((made[0].shape[0] * 2 // 3, *made[0].shape[1:]), BF16)
    before, swap = pl.pallas_call(
        functools.partial(ends_kernel, order),
        in_specs=[HBM] * 2 + [VMEM] * 2,
        out_specs=[VMEM] * 2,
        out_shape=[half, jax.ShapeDtypeStruct(first.shape, BF16)],
        scratch_shapes=inner_scratch(*shape),
        compiler_params=params(ENDS_VMEM),
        cost_estimate=cost(0, 2**20),
        name="ends",
    )(preact, upstream, first, last)
    g, side_rows, sent = pl.pallas_call(
        functools.partial(middles_kernel, order),
        in_specs=[HBM] * 2 + [VMEM] * 4,
        out_specs=[VMEM] * 2 + [HBM],
        out_shape=made + [jax.ShapeDtypeStruct(sent_shape, BF16)],
        scratch_shapes=inner_scratch(*shape)
        + [pltpu.VMEM(sent_shape, BF16), pltpu.SemaphoreType.DMA(())],
        compiler_params=params(MIDDLES_VMEM),
        cost_estimate=cost(0, 4 * 2**20),
        name="middles",
    )(preact, upstream, first, last, share, before)
    return g, side_rows, swap, sent


def is_odd(axis):
    return lax.rem(lax.axis_index(axis), 2) == 1


def either(condition, first, second):
    return jnp.where(condition, first.astype(F32), second.astype(F32))


def side_kernel(odd_ref, even_ref, own_ref, sent_ref, xlo_ref, xhi_ref):
    size_x = own_ref.shape[0] - 2
    size_z = own_ref.shape[-1]
    size_y = xlo_ref.shape[-1] // size_z
    odd = is_odd("gx")
    low = either(odd, even_ref[...], odd_ref[...]).astype(BF16)
    high = either(odd, odd_ref[...], even_ref[...]).astype(BF16)
    xlo_ref[...] = low
    xhi_ref[...] = high
    sent_ref[0] = row_for_other(low, size_z)
    for x in range(size_x):
        sent_ref[x + 1] = own_ref[x]
    sent_ref[size_x + 1] = row_for_other(high, size_z)
    lane = lax.broadcasted_iota(jnp.int32, (low.shape[0], LANES), 1)
    first, second = own_ref[size_x], own_ref[size_x + 1]
    for number, plane in ((0, low), (size_x + 1, high)):
        for y in range(size_y):
            at = number * size_y + y
            head = plane[:, y * size_z : y * size_z + LANES]
            tail = plane[:, (y + 1) * size_z - LANES : (y + 1) * size_z]
            first = jnp.where(lane == at, pltpu.roll(head, at, 1), first)
            second = jnp.where(lane == at, pltpu.roll(tail, at + 1, 1), second)
    sent_ref[size_x + 2] = first
    sent_ref[size_x + 3] = second


def side(halves, own):
    plane = jax.ShapeDtypeStruct(halves[0].shape, BF16)
    return pl.pallas_call(
        side_kernel,
        in_specs=[VMEM] * 3,
        out_specs=[VMEM] * 3,
        out_shape=[
            jax.ShapeDtypeStruct((own.shape[0] + 2, *own.shape[1:]), BF16),
            plane,
            plane,
        ],
        compiler_params=params(),
        cost_estimate=cost(2**25, 2**19),
        name="side",
    )(*halves, own)


def own_columns(columns, number, area):
    me = lax.axis_index("gy")
    value = columns.astype(F32)
    lane = lax.broadcasted_iota(jnp.int32, value.shape, 1)
    first = pltpu.roll(value, -number * area % LANES, 1)
    second = pltpu.roll(value, (1 - number) * area % LANES, 1)
    first = jnp.where(lane < area, first, 0.0)
    second = jnp.where((lane >= area) & (lane < 2 * area), second, 0.0)
    return jnp.where(me == 0, first, second)


def join_kernel(area, own_ref, other_ref, columns_ref, even_ref, odd_ref):
    at = own_ref.shape[0] - 2
    me = lax.axis_index("gy")
    last = own_columns(columns_ref[...], 1, area).astype(BF16)

    def fill(up_ref, down_ref):
        for k, out_ref in enumerate((down_ref, up_ref)):
            out_ref[me] = own_ref[at + k]
            out_ref[1 - me] = other_ref[at + k]
        up_ref[2] = last
        down_ref[2] = last

    odd = is_odd("gz")

    @pl.when(odd)
    def _():
        fill(odd_ref, even_ref)

    @pl.when(jnp.logical_not(odd))
    def _():
        fill(even_ref, odd_ref)


def join(own, other, columns, area):
    return pl.pallas_call(
        functools.partial(join_kernel, area),
        in_specs=[VMEM] * 3,
        out_specs=[VMEM] * 2,
        out_shape=[jax.ShapeDtypeStruct((3, *own.shape[1:]), BF16)] * 2,
        compiler_params=params(),
        cost_estimate=cost(0, 2**17),
        name="join",
    )(own, other, columns)


def pair_wgrad_kernel(*refs):
    x_ref, acc_ref, g3, x3 = refs[7:]
    weight_products(refs, None, x_ref, g3, x3, acc_ref)


def pair_wgrad(sources, planes_x, shape):
    channels = shape[0]
    return pl.pallas_call(
        pair_wgrad_kernel,
        in_specs=[VMEM] * 8,
        out_specs=VMEM,
        out_shape=jax.ShapeDtypeStruct((9 * channels, 3 * channels), F32),
        scratch_shapes=[g3_scratch(*shape), x3_scratch(*shape)],
        compiler_params=params(32 * 2**20),
        cost_estimate=wgrad_cost(*shape),
        name="wgrad",
    )(*sources, planes_x)


def finish_kernel(scale, rows, sizes, *refs):
    acc_ref, columns_ref, even_ref, odd_ref, from_odd_ref, from_even_ref = refs[:6]
    part_ref, chunks = refs[6:]
    size_x, size_y = sizes
    channels = columns_ref.shape[0]
    area = size_x * size_y
    odd = is_odd("gz")
    lane = lax.broadcasted_iota(jnp.int32, (channels, LANES), 1)
    row = lane % size_y
    jump = area - size_y + 1
    below = [either(odd, from_even_ref[k], from_odd_ref[k]) for k in range(3)]
    own = [either(odd, even_ref[k], odd_ref[k]) for k in range(2)]
    pairs = ((below[:2], own_columns(columns_ref[...], 0, area)), (own, below[2]))
    edges = []
    for tiles, value in pairs:
        before = jnp.where(lane >= area, pltpu.roll(value, jump, 1), 0.0)
        after = jnp.where(lane < area, pltpu.roll(value, LANES - jump, 1), 0.0)
        right = jnp.concatenate(
            [
                jnp.where(row > 0, pltpu.roll(value, 1, 1), before),
                value,
                jnp.where(row < size_y - 1, pltpu.roll(value, LANES - 1, 1), after),
            ],
            axis=0,
        )
        left = []
        for a in range(3):
            first = pltpu.roll(tiles[0], -a * size_y % LANES, 1)
            second = pltpu.roll(tiles[1], (area - a * size_y) % LANES, 1)
            left.append(jnp.where(lane < area, first, jnp.where(lane < 2 * area, second, 0.0)))
        edges.append(
            lax.dot_general(
                jnp.concatenate(left, axis=0).astype(BF16),
                right.astype(BF16),
                (((1,), (1,)), ((), ())),
                preferred_element_type=F32,
            )
        )
    count = part_ref.shape[0]
    height, width = chunks.shape[0] // count, LANES
    chunks[...] = jnp.zeros_like(chunks)
    pieces = rows * acc_ref.shape[1] // width
    for a in range(3):
        for c in range(3):
            at = 3 * a + c
            block = acc_ref[at * channels : (at + 1) * channels, :]
            if c != 1:
                block = block + edges[c // 2][a * channels : (a + 1) * channels]
            block = block * scale
            line = jnp.concatenate(
                [block[r * count : (r + 1) * count] for r in range(rows)], axis=1
            )
            for k in range(pieces):
                chunks[pl.ds(at * pieces + k, count, stride=height), :] = line[
                    :, k * width : (k + 1) * width
                ]

    def write(at, quads):
        part_ref[:, :, at] = quads.astype(BF16)

    whole = chunks[...].reshape(count, height, width)
    to_quads(whole[:, : part_ref.shape[2] // LANES * QUAD], write)


def finish(acc, columns, sent, received, scale, rows, sizes, part_shape):
    channels = columns.shape[0]
    return pl.pallas_call(
        functools.partial(finish_kernel, scale, rows, sizes),
        in_specs=[VMEM] * 6,
        out_specs=VMEM,
        out_shape=jax.ShapeDtypeStruct(part_shape, BF16),
        scratch_shapes=[
            pltpu.VMEM((part_shape[0] * -(-part_shape[2] // LANES * QUAD // 8) * 8, LANES), F32),
        ],
        compiler_params=params(),
        cost_estimate=cost(2**27, 2**21),
        name="finish",
    )(acc, columns, *sent, *received)


def adam_step(master, first, second, weight_grad):
    new_first = 0.9 * first + 0.1 * weight_grad
    new_second = 0.999 * second + 0.001 * weight_grad * weight_grad
    corr_first = 1.0 - (0.9**10) ** 10
    corr_second = 1.0 - (0.999**10) ** 10
    update = new_first / corr_first / (jnp.sqrt(new_second / corr_second) + 1e-08) + 0.01 * master
    return master - 0.05 * update, new_first, new_second


def in_flat_order(value, rows, places, spread_rows):
    taps = 27
    lane = lax.broadcasted_iota(jnp.int32, (9, LANES), 1)
    for k in range(value.shape[1] // LANES):
        rows[k * QUAD : (k + 1) * QUAD, :] = value[:, k * LANES : (k + 1) * LANES]
    thirds = [rows[pl.ds(k, 9, stride=3), :] for k in range(3)]
    half = LANES // 2
    by_y = (
        jnp.where(lane < half, thirds[0], thirds[1]),
        jnp.where(lane < half, pltpu.roll(thirds[0], half, 1), pltpu.roll(thirds[2], half, 1)),
        jnp.where(lane < half, thirds[1], thirds[2]),
    )
    places[...] = jnp.zeros_like(places)
    for b in range(3):
        spread_rows[b, :9, :] = by_y[b]
        for block in range(9):
            tap = (2 - block // 3) * 9 + b * 3 + 2 - block % 3
            places[tap : tap + 1, :] = spread_rows[b, block : block + 1, :]
    line = places[...].T
    number = lax.broadcasted_iota(jnp.int32, (LANES, LANES), 0) * taps
    column = lax.broadcasted_iota(jnp.int32, (LANES, LANES), 1)
    turned = []
    for group in range(LANES // 8):
        piece = line[8 * group : 8 * (group + 1)]
        rest = 8 * group * taps % LANES
        for step in range(3):
            turn = rest // (3 - step)
            rest -= turn
            piece = pltpu.roll(piece, turn, 1, stride=taps // 3, stride_axis=0)
        turned.append(piece)
    line = jnp.concatenate(turned, axis=0)
    start = number & (LANES - 1)
    line = jnp.concatenate(
        [jnp.where(column >= start, line, 0.0), jnp.where(column < start, line, 0.0)], axis=0
    )
    target = lax.broadcasted_iota(jnp.int32, (32, 2 * LANES), 0)
    source = lax.broadcasted_iota(jnp.int32, (32, 2 * LANES), 1)
    goes = lax.shift_right_logical((source & (LANES - 1)) * taps, 7)
    goes = goes + jnp.where(source < LANES, 0, 1)
    pick = jnp.where(goes == target, 1.0, 0.0).astype(BF16)
    parts = []
    for _ in range(3):
        parts.append(line.astype(BF16))
        line = line - parts[-1].astype(F32)
    return jnp.dot(
        jnp.concatenate([pick] * 3, axis=1),
        jnp.concatenate(parts, axis=0),
        preferred_element_type=F32,
    )[:taps]


def adam_kernel(parts_ref, master_ref, first_ref, second_ref, *refs):
    out_refs, scratch = refs[:4], refs[4:]
    total = parts_ref[0].astype(F32)
    for source in range(1, parts_ref.shape[0]):
        total = total + parts_ref[source].astype(F32)
    weight_grad = in_flat_order(total, *scratch)
    results = adam_step(master_ref[...], first_ref[...], second_ref[...], weight_grad)
    for out_ref, result in zip(out_refs, (weight_grad, *results)):
        out_ref[...] = result


def adam(parts, *states):
    share = states[0].shape[0]
    tiled = [state.reshape(share // LANES, LANES) for state in states]
    result = jax.ShapeDtypeStruct(tiled[0].shape, F32)
    outs = pl.pallas_call(
        adam_kernel,
        in_specs=[VMEM] * 4,
        out_specs=[VMEM] * 4,
        out_shape=[result] * 4,
        scratch_shapes=[
            pltpu.VMEM((32, LANES), F32),
            pltpu.VMEM((LANES, LANES), F32),
            pltpu.VMEM((3, 16, LANES), F32),
        ],
        compiler_params=params(),
        cost_estimate=cost(2**22, 2**19),
        name="adam",
    )(parts, *tiled)
    return tuple(out.reshape(share) for out in outs)


def spread_kernel(rows, w_ref, weights_ref, turned, chunks):
    count = w_ref.shape[0]
    height = chunks.shape[0] // count
    taps = 27 * rows * count
    quads = [
        w_ref[:, :, k * LANES : (k + 1) * LANES].astype(F32)
        for k in range(w_ref.shape[2] // LANES)
    ]
    spare = jnp.zeros((count, height - QUAD * len(quads), LANES), F32)
    chunks[...] = jnp.concatenate(quads + [spare], axis=1).reshape(chunks.shape)
    line = jnp.concatenate(
        [chunks[pl.ds(k, count, stride=height), :] for k in range(rows * taps // LANES)], axis=1
    )
    whole = jnp.concatenate([line[:, r * taps : (r + 1) * taps] for r in range(rows)], axis=0)
    spread_weights(whole, turned, weights_ref)


def spread(kernel, channels, rows):
    return pl.pallas_call(
        functools.partial(spread_kernel, rows),
        in_specs=[VMEM],
        out_specs=VMEM,
        out_shape=jax.ShapeDtypeStruct((3, 2 * channels, 12 * channels), BF16),
        scratch_shapes=[
            flat_scratch(channels),
            pltpu.VMEM((kernel.shape[0] * 32, LANES), F32),
        ],
        compiler_params=params(),
        cost_estimate=cost(2**20, 2**21),
        name="spread",
    )(kernel)


def pair_dgrad_kernel(*refs):
    weights_ref, out_ref, g3, tile = refs[9:]
    _, size_x, size_y, size_z = out_ref.shape
    halo = pair_z_halo(refs[7], refs[8], size_x + 2, size_y, size_z)
    input_products(refs, halo, g3, weights_ref, tile, out_ref)


def pair_dgrad(sources, weights, shape):
    channels, _, size_y, size_z = shape
    return pl.pallas_call(
        pair_dgrad_kernel,
        in_specs=[VMEM] * 10,
        out_specs=VMEM,
        out_shape=jax.ShapeDtypeStruct(shape, BF16),
        scratch_shapes=[g3_scratch(*shape), pltpu.VMEM((2, channels * size_y, size_z), F32)],
        compiler_params=params(32 * 2**20),
        cost_estimate=dgrad_cost(*shape),
        name="dgrad",
    )(*sources, weights)


def pair_program(activations, preact, upstream, master, first_moment, second_moment, scale):
    shape = activations.shape
    channels, size_x, size_y, _ = shape
    devices = math.prod(lax.axis_size(a) for a in AXES)
    rows = channels // devices
    used = master.shape[0] // LANES
    block = (devices, QUAD, -(-used // QUAD) * LANES)
    first, last, odd_sent = faces(preact, upstream, "gx", rows)
    odd_halves = swapped(odd_sent, "gx", 1)
    inner, own, even_sent, sent = pair_inner(
        preact, upstream, first, last, master.reshape(used, LANES), block, rows
    )
    even_halves = swapped(even_sent, "gx", 0)
    kernel = lax.all_to_all(sent, AXES, 0, 0, tiled=True)
    own, xlo, xhi = side((odd_halves, even_halves), own)
    planes = (xlo, first, inner, last, xhi)
    own, activations = lax.optimization_barrier((own, activations))
    other = shifted(own, {"gy": "swap"})
    planes_x, columns = input_planes(activations, True)
    z_sent = join(own, other, columns, size_x * size_y)
    from_odd = swapped(z_sent[1], "gz", 1)
    from_even = swapped(z_sent[0], "gz", 0)
    sources = (*planes, other, other)
    acc = pair_wgrad(sources, planes_x, shape)
    z_received = (from_odd, from_even)
    part = finish(acc, columns, z_sent, z_received, scale, rows, (size_x, size_y), block)
    part, kernel = lax.optimization_barrier((part, kernel))
    parts = lax.all_to_all(part, AXES, 0, 0, tiled=True)
    weights = spread(kernel, channels, rows)
    grad_input = pair_dgrad((*sources, *z_received), weights, shape)
    return grad_input, *adam(parts, master, first_moment, second_moment)


def yface_kernel(*refs):
    low_ref, high_ref = refs[5:]
    size_z = low_ref.shape[-1]
    for index in range(low_ref.shape[0]):
        body = body_of(refs[:5], index)
        plane = body.shape[-1]
        low_ref[index] = body[:, :size_z]
        high_ref[index] = body[:, plane - size_z :]


def y_faces(planes, size_z):
    inner, channels, _ = planes[2].shape
    face = jax.ShapeDtypeStruct((inner + 4, channels, size_z), BF16)
    return pl.pallas_call(
        yface_kernel,
        in_specs=[VMEM] * 5,
        out_specs=[VMEM] * 2,
        out_shape=[face] * 2,
        compiler_params=params(),
        cost_estimate=cost(0, 2**19),
        name="yfaces",
    )(*planes)


def zface_kernel(*refs):
    zlo_ref, zhi_ref = refs[7:]
    size_z = refs[5].shape[-1]
    whole = []
    for index in range(refs[5].shape[0]):
        low, high = y_halo(refs[5:7], index)
        body = body_of(refs[:5], index)[...]
        whole.append(jnp.concatenate([low.astype(BF16), body, high.astype(BF16)], axis=1))
    low, high = z_tiles(whole, whole[0].shape[1] // size_z, size_z, range(len(whole)))
    zlo_ref[...] = low.astype(BF16)
    zhi_ref[...] = high.astype(BF16)


def z_faces(planes, y_halos):
    face = jax.ShapeDtypeStruct((planes[0].shape[0], LANES), BF16)
    return pl.pallas_call(
        zface_kernel,
        in_specs=[VMEM] * 7,
        out_specs=[VMEM] * 2,
        out_shape=[face, face],
        compiler_params=params(),
        cost_estimate=cost(2**27, 2**21),
        name="zfaces",
    )(*planes, *y_halos)


def wgrad_kernel(scale, *refs):
    x_ref, part_ref, g3, x3, acc, flat = refs[9:]
    size_x, channels, plane = x_ref.shape
    size_z = refs[5].shape[-1]
    halo = z_halo(refs[7], refs[8], size_x + 2, plane // size_z + 2, size_z)
    weight_products(refs, halo, x_ref, g3, x3, acc)
    whole = to_flat(acc[...] * scale, channels, channels, flat)
    part_ref[...] = whole[:, : part_ref.shape[1]].astype(BF16)


def wgrad(sources, planes_x, shape, scale):
    channels = shape[0]
    return pl.pallas_call(
        functools.partial(wgrad_kernel, scale),
        in_specs=[VMEM] * 10,
        out_specs=VMEM,
        out_shape=jax.ShapeDtypeStruct((channels, 27 * channels), BF16),
        scratch_shapes=[
            g3_scratch(*shape),
            x3_scratch(*shape),
            acc_scratch(channels),
            flat_scratch(channels),
        ],
        compiler_params=params(32 * 2**20),
        cost_estimate=wgrad_cost(*shape),
        name="wgrad",
    )(*sources, planes_x)


def dgrad_kernel(*refs):
    w_ref, out_ref, g3, turned, weights, tile = refs[9:]
    _, size_x, size_y, size_z = out_ref.shape
    spread_weights(w_ref[...].astype(F32), turned, weights)
    halo = z_halo(refs[7], refs[8], size_x + 2, size_y + 2, size_z)
    input_products(refs, halo, g3, weights, tile, out_ref)


def dgrad(sources, kernel, shape):
    return pl.pallas_call(
        dgrad_kernel,
        in_specs=[VMEM] * 10,
        out_specs=VMEM,
        out_shape=jax.ShapeDtypeStruct(shape, BF16),
        scratch_shapes=dgrad_scratch(*shape),
        compiler_params=params(32 * 2**20),
        cost_estimate=dgrad_cost(*shape),
        name="dgrad",
    )(*sources, kernel)


def general_program(activations, preact, upstream, master, first_moment, second_moment, scale):
    shape = activations.shape
    channels, _, _, size_z = shape
    devices = math.prod(lax.axis_size(a) for a in AXES)
    share = master.shape[0]
    first, last = faces(preact, upstream)
    x_halos = (shifted(last, {"gx": 1}), shifted(first, {"gx": -1}))
    inner = inner_planes(preact, upstream)
    (planes_x,) = input_planes(activations, False)
    sent = jnp.broadcast_to(master.astype(BF16).reshape(1, 1, share), (devices, 1, share))
    kernel = lax.all_to_all(sent, AXES, 0, 0, tiled=True).reshape(channels, 27 * channels)
    planes = (x_halos[0], first, inner, last, x_halos[1])
    y_sent = y_faces(planes, size_z)
    y_halos = (shifted(y_sent[1], {"gy": 1}), shifted(y_sent[0], {"gy": -1}))
    zlo, zhi = z_faces(planes, y_halos)
    z_halos = (shifted(zhi, {"gz": 1}), shifted(zlo, {"gz": -1}))
    sources = (*planes, *y_halos, *z_halos)
    part = wgrad(sources, planes_x, shape, scale)
    part, kernel = lax.optimization_barrier((part, kernel))
    parts = lax.all_to_all(part.reshape(devices, 1, share), AXES, 0, 0, tiled=True)
    grad_input = dgrad(sources, kernel, shape)
    weight_grad = jnp.sum(parts.astype(F32), axis=0).reshape(-1)
    results = adam_step(master, first_moment, second_moment, weight_grad)
    return grad_input, weight_grad, *results


def shifted(value, moves):
    names = tuple(moves)
    sizes = [lax.axis_size(name) for name in names]
    pairs = []
    for source in range(math.prod(sizes)):
        rest, coords = source, []
        for size in reversed(sizes):
            coords.insert(0, rest % size)
            rest //= size
        coords = [
            (at + moves[name]) if moves[name] != "swap" else 1 - at
            for at, name in zip(coords, names)
        ]
        if all(0 <= at < size for at, size in zip(coords, sizes)):
            target = 0
            for at, size in zip(coords, sizes):
                target = target * size + at
            pairs.append((source, target))
    return lax.ppermute(value, names if len(names) > 1 else names[0], pairs)


def swapped(value, axis, start):
    pairs = []
    for low in range(start, lax.axis_size(axis) - 1, 2):
        pairs += [(low, low + 1), (low + 1, low)]
    return lax.ppermute(value, axis, pairs)


def local(activations, preact, upstream, master, first_moment, second_moment):
    channels, size_x, size_y, size_z = activations.shape
    devices = math.prod(lax.axis_size(a) for a in AXES)
    share = master.shape[0]
    scale = 1.0 / math.sqrt(size_x * size_y * size_z * devices)
    in_pairs = (
        lax.axis_size("gy") == 2
        and channels % devices == 0
        and share % LANES == 0
        and channels // devices * channels == LANES
        and 2 * size_x * size_y <= LANES
        and (size_x + 2) * size_y <= LANES
    )
    program = pair_program if in_pairs else general_program
    return program(
        activations, preact, upstream, master, first_moment, second_moment, scale
    )


def solution(mesh):
    volume = P(None, "gx", "gy", "gz")
    flat = P(AXES)
    return jax.shard_map(
        local,
        mesh=mesh,
        in_specs=(volume, volume, volume, flat, flat, flat),
        out_specs=(volume, flat, flat, flat, flat),
        check_vma=False,
    )
```

```python
import functools
import math

import jax
import jax.numpy as jnp
from jax import lax
from jax.experimental import pallas as pl
from jax.experimental.pallas import tpu as pltpu
from jax.sharding import PartitionSpec as P

AXES = ("gx", "gy", "gz")
LANES = 128
VMEM = pl.BlockSpec(memory_space=pltpu.VMEM)
HBM = pl.BlockSpec(memory_space=pltpu.HBM)
F32 = jnp.float32
BF16 = jnp.bfloat16
FACES_VMEM = 55_900_000
INNER_VMEM = 54_800_000
ENDS_VMEM = 54_800_000
MIDDLES_VMEM = 54_300_000


def params(limit=24 * 2**20):
    return pltpu.CompilerParams(vmem_limit_bytes=limit)


def cost(flops, moved):
    return pl.CostEstimate(flops=flops, bytes_accessed=moved, transcendentals=0)


def to_planes(value, tile, write, rows=1):
    channels, size_y, size_z = value.shape
    count = channels // rows
    tile[...] = value.astype(F32).reshape(channels * size_y, size_z)
    for y in range(size_y):
        for r in range(rows):
            picked = tile[pl.ds(r * size_y + y, count, stride=rows * size_y), :]
            write(slice(r * count, (r + 1) * count), y, picked.astype(BF16))


QUAD = 4


def to_quads(rows, write):
    for k in range(rows.shape[-2] // QUAD):
        write(slice(k * LANES, (k + 1) * LANES), rows[..., k * QUAD : (k + 1) * QUAD, :])


def masked(p, u):
    return jnp.where(p.astype(F32) > 0, u.astype(F32), 0.0)


def choose(condition, out_ref, first_ref, second_ref):
    @pl.when(condition)
    def _():
        out_ref[...] = first_ref[...]

    @pl.when(jnp.logical_not(condition))
    def _():
        out_ref[...] = second_ref[...]


def face_kernel(axis, rows, p_ref, u_ref, *refs):
    p_buf, u_buf, tile, sems = refs[-4:]
    out_refs, swap_refs = refs[:2], refs[2:-4]
    size_x, size_z = p_ref.shape[1], p_ref.shape[3]
    copies = []
    for k, x in enumerate((0, size_x - 1)):
        pair = (
            pltpu.make_async_copy(p_ref.at[:, x], p_buf.at[k], sems.at[2 * k]),
            pltpu.make_async_copy(u_ref.at[:, x], u_buf.at[k], sems.at[2 * k + 1]),
        )
        for copy in pair:
            copy.start()
        copies.append(pair)
    for k, out_ref in enumerate(out_refs):
        for copy in copies[k]:
            copy.wait()

        def write(at, y, value):
            out_ref[at, y * size_z : (y + 1) * size_z] = value

        to_planes(masked(p_buf[k], u_buf[k]), tile.at[k], write, rows)
    if axis is not None:
        choose(is_odd(axis), swap_refs[0], out_refs[1], out_refs[0])


def faces(preact, upstream, axis=None, rows=1):
    channels, size_x, size_y, size_z = preact.shape
    face = jax.ShapeDtypeStruct((channels, size_y * size_z), BF16)
    buffer = pltpu.VMEM((2, channels, size_y, size_z), BF16)
    count = 2 if axis is None else 3
    return pl.pallas_call(
        functools.partial(face_kernel, axis, rows),
        in_specs=[HBM, HBM],
        out_specs=[VMEM] * count,
        out_shape=[face] * count,
        scratch_shapes=[
            buffer,
            buffer,
            pltpu.VMEM((2, channels * size_y, size_z), F32),
            pltpu.SemaphoreType.DMA((4,)),
        ],
        compiler_params=params(FACES_VMEM),
        cost_estimate=cost(0, 2**20),
        name="faces",
    )(preact, upstream)


def fetches(planes, p_ref, u_ref, p_buf, u_buf, sems):
    return [
        (
            pltpu.make_async_copy(p_ref.at[:, x + 1], p_buf.at[x], sems.at[2 * x]),
            pltpu.make_async_copy(u_ref.at[:, x + 1], u_buf.at[x], sems.at[2 * x + 1]),
        )
        for x in planes
    ]


def start(copies):
    for pair in copies:
        for copy in pair:
            copy.start()


def settle(order, planes, copies, g_ref, p_buf, u_buf, tile):
    size_z = p_buf.shape[-1]
    for x, pair in zip(planes, copies):
        for copy in pair:
            copy.wait()

        def write(at, y, value):
            g_ref[x, at, y * size_z : (y + 1) * size_z] = value

        to_planes(masked(p_buf[x], u_buf[x]), tile.at[x % 2], write, order)


def read_inner(order, planes, p_ref, u_ref, g_ref, p_buf, u_buf, tile, sems):
    copies = fetches(planes, p_ref, u_ref, p_buf, u_buf, sems)
    start(copies)
    settle(order, planes, copies, g_ref, p_buf, u_buf, tile)


def inner_kernel(*refs):
    read_inner(1, range(refs[2].shape[0]), *refs)


def inner_output(channels, size_x, size_y, size_z):
    return jax.ShapeDtypeStruct((size_x - 2, channels, size_y * size_z), BF16)


def inner_scratch(channels, size_x, size_y, size_z):
    return [
        pltpu.VMEM((size_x - 2, channels, size_y, size_z), BF16),
        pltpu.VMEM((size_x - 2, channels, size_y, size_z), BF16),
        pltpu.VMEM((2, channels * size_y, size_z), F32),
        pltpu.SemaphoreType.DMA((2 * size_x - 4,)),
    ]


def inner_planes(preact, upstream):
    shape = preact.shape
    return pl.pallas_call(
        inner_kernel,
        in_specs=[HBM] * 2,
        out_specs=VMEM,
        out_shape=inner_output(*shape),
        scratch_shapes=inner_scratch(*shape),
        compiler_params=params(INNER_VMEM),
        cost_estimate=cost(0, 4 * 2**20),
        name="inner",
    )(preact, upstream)


def input_kernel(a_ref, x_ref, *refs):
    tile = refs[-1]
    channels, size_x, size_y, size_z = a_ref.shape
    for x in range(size_x):

        def write(at, y, value):
            x_ref[x, at, y * size_z : (y + 1) * size_z] = value

        to_planes(a_ref[:, x], tile.at[x % 2], write)
    if len(refs) > 1:
        low, high = z_tiles([x_ref[x] for x in range(size_x)], size_y, size_z, range(size_x))
        refs[0][...] = (low + pltpu.roll(high, size_x * size_y, 1)).astype(BF16)


def input_planes(activations, with_columns):
    channels, size_x, size_y, size_z = activations.shape
    outs = [jax.ShapeDtypeStruct((size_x, channels, size_y * size_z), BF16)]
    if with_columns:
        outs.append(jax.ShapeDtypeStruct((channels, LANES), BF16))
    return pl.pallas_call(
        input_kernel,
        in_specs=[VMEM],
        out_specs=[VMEM] * len(outs),
        out_shape=outs,
        scratch_shapes=[pltpu.VMEM((2, channels * size_y, size_z), F32)],
        compiler_params=params(),
        cost_estimate=cost(0, 2 * 2**20),
        name="inputs",
    )(activations)


def body_of(refs, index):
    planes = refs[2].shape[0] + 4
    if 2 <= index < planes - 2:
        return refs[2].at[index - 2]
    return refs[{0: 0, 1: 1, planes - 2: 3, planes - 1: 4}[index]]


def y_halo(refs, index):
    me = lax.axis_index("gy")
    low = jnp.where(me > 0, refs[0][index].astype(F32), 0.0)
    high = jnp.where(me < lax.axis_size("gy") - 1, refs[1][index].astype(F32), 0.0)
    return low, high


def z_picker(rows_y, size_z):
    shape = (rows_y * size_z, 2 * LANES)
    voxel = lax.broadcasted_iota(jnp.int32, shape, 0)
    lane = lax.broadcasted_iota(jnp.int32, shape, 1)
    wanted = jnp.where(lane < LANES, lane * size_z, (lane - LANES) * size_z + size_z - 1)
    return (voxel == wanted).astype(F32).astype(BF16)


def z_tiles(planes, rows_y, size_z, numbers):
    channels = planes[0].shape[0]
    columns = jnp.dot(
        jnp.concatenate(planes, axis=0), z_picker(rows_y, size_z), preferred_element_type=F32
    )
    low = jnp.zeros((channels, LANES), F32)
    high = jnp.zeros((channels, LANES), F32)
    for index, number in enumerate(numbers):
        rows = columns[index * channels : (index + 1) * channels]
        low = low + pltpu.roll(rows[:, :LANES], number * rows_y, 1)
        high = high + pltpu.roll(rows[:, LANES:], number * rows_y, 1)
    return low, high


def put_columns(columns, row_of, rows_y, size_z):
    shape = (2 * LANES, rows_y * size_z)
    source = lax.broadcasted_iota(jnp.int32, shape, 0)
    voxel = lax.broadcasted_iota(jnp.int32, shape, 1)
    number = source % LANES
    place = row_of(number) * size_z + jnp.where(source < LANES, 0, size_z - 1)
    place = jnp.where(number < rows_y, place, -1)
    put = (voxel == place).astype(F32).astype(BF16)
    rows = [jnp.concatenate(pair, axis=1) for pair in columns]
    return jnp.dot(
        jnp.concatenate(rows, axis=0).astype(BF16), put, preferred_element_type=F32
    ).astype(BF16)


def z_halo(low_ref, high_ref, planes, rows_y, size_z):
    columns = []
    for index in range(planes):
        shift = -index * rows_y % LANES
        columns.append(
            [pltpu.roll(ref[...].astype(F32), shift, 1) for ref in (low_ref, high_ref)]
        )
    return put_columns(columns, lambda number: number, rows_y, size_z)


def pair_z_halo(odd_ref, even_ref, planes, size_y, size_z):
    me, odd = lax.axis_index("gy"), is_odd("gz")
    sides = []
    for low, high in ((even_ref, odd_ref), (odd_ref, even_ref)):
        first, second = (either(odd, low[k], high[k]) for k in range(2))
        lane = lax.broadcasted_iota(jnp.int32, first.shape, 1)
        own = jnp.where(me == 0, first, second)
        before = jnp.where(me == 0, 0.0, first)
        after = jnp.where(me == 0, second, 0.0)
        columns = []
        for index in range(planes):
            start = index * size_y
            columns.append(
                jnp.where(
                    lane < size_y,
                    pltpu.roll(own, -start % LANES, 1),
                    jnp.where(
                        lane == size_y,
                        pltpu.roll(before, (1 - start) % LANES, 1),
                        pltpu.roll(after, (size_y + 1 - start) % LANES, 1),
                    ),
                )
            )
        sides.append(columns)

    def row_of(number):
        return jnp.where(number < size_y, number + 1, jnp.where(number == size_y, 0, size_y + 1))

    return put_columns(list(zip(*sides)), row_of, size_y + 2, size_z)


def shifted_plane(index, refs, halo, g3):
    channels, plane = refs[0].shape
    size_z = refs[5].shape[-1]
    rows_y = plane // size_z + 2
    base = 3 * channels * index
    lane = lax.broadcasted_iota(jnp.int32, (channels, size_z), 1)
    is_first, is_last = lane == 0, lane == size_z - 1
    low, high = y_halo(refs[5:7], index)
    body = body_of(refs[:5], index)
    for row in range(rows_y):
        cols = slice(row * size_z, (row + 1) * size_z)
        if row == 0:
            value = low.astype(BF16)
        elif row == rows_y - 1:
            value = high.astype(BF16)
        else:
            value = body[:, (row - 1) * size_z : row * size_z]
        if halo is None:
            edge = jnp.zeros_like(value)
        else:
            edge = halo[index * channels : (index + 1) * channels, cols]
        before = jnp.where(is_first, edge, pltpu.roll(value, 1, 1))
        after = jnp.where(is_last, edge, pltpu.roll(value, size_z - 1, 1))
        g3[base : base + channels, cols] = before
        g3[base + channels : base + 2 * channels, cols] = value
        g3[base + 2 * channels : base + 3 * channels, cols] = after


def weight_products(refs, halo, x_ref, g3, x3, acc):
    size_x, channels, plane = x_ref.shape
    size_z = refs[5].shape[-1]
    group = 3 * channels
    zero = jnp.zeros((channels, 2 * size_z), BF16)
    done = 0
    for x in range(0, size_x, 2):
        while done < x + 4:
            shifted_plane(done, refs, halo, g3)
            done += 1
        for plane_x in (x, x + 1):
            value = x_ref[plane_x]
            for b in range(3):
                at = slice(b * channels, (b + 1) * channels)
                start = (2 - b) * size_z
                x3[plane_x, at, start : start + plane] = value
                if start:
                    x3[plane_x, at, :start] = zero[:, :start]
                if start < 2 * size_z:
                    x3[plane_x, at, start + plane :] = zero[:, start:]
        product = lax.dot_general(
            jnp.concatenate(
                [g3[x * group : (x + 3) * group, :], g3[(x + 1) * group : (x + 4) * group, :]],
                axis=1,
            ),
            jnp.concatenate([x3[x], x3[x + 1]], axis=1),
            (((1,), (1,)), ((), ())),
            preferred_element_type=F32,
        )
        if x == 0:
            acc[...] = product
        else:
            acc[...] += product


def to_flat(value, count, channels, flat):
    height, width = value.shape
    wide = value
    if height % LANES:
        wide = jnp.concatenate([wide, jnp.zeros((-height % LANES, width), F32)], axis=0)
    if width % LANES:
        wide = jnp.concatenate([wide, jnp.zeros((wide.shape[0], -width % LANES), F32)], axis=1)
    turned = wide.T
    for b in range(3):
        rows = turned[b * channels : (b + 1) * channels]
        for block in range(9):
            start = block * count
            cell = rows[:, start // LANES * LANES : (start // LANES + 1) * LANES]
            tap = (2 - block // 3) * 9 + b * 3 + 2 - block % 3
            shift = -start % LANES
            flat[pl.ds(tap, channels, stride=27), :] = pltpu.roll(cell, shift, 1) if shift else cell
    return flat[...].T[:count]


def spread_weights(whole, turned, weights):
    channels, taps = whole.shape
    group = 3 * channels
    whole = jnp.concatenate([whole, jnp.zeros((LANES - channels, taps), F32)], axis=0)
    whole = jnp.concatenate([whole, jnp.zeros((LANES, -taps % LANES), F32)], axis=1)
    turned[...] = whole.T
    for b in range(3):
        blocks = []
        for a in range(3):
            for c in range(3):
                tap = (2 - a) * 9 + (2 - b) * 3 + 2 - c
                blocks.append(turned[pl.ds(tap, channels, stride=27), :][:, :channels])
        zero = jnp.zeros((channels, group), F32)
        weights[b, :channels] = jnp.concatenate(blocks + [zero], axis=1).astype(BF16)
        weights[b, channels:] = jnp.concatenate([zero] + blocks, axis=1).astype(BF16)


def input_products(refs, halo, g3, weights, tile, out_ref):
    channels, size_x, size_y, size_z = out_ref.shape
    group = 3 * channels
    plane = size_y * size_z
    done = 0
    for pair in range(size_x // 2):
        while done < 2 * pair + 4:
            shifted_plane(done, refs, halo, g3)
            done += 1
        at = slice(2 * pair * group, (2 * pair + 4) * group)
        total = None
        for b in range(3):
            product = jnp.dot(
                weights[b],
                g3[at, b * size_z : b * size_z + plane],
                preferred_element_type=F32,
            )
            total = product if total is None else total + product
        for half in range(2):
            for y in range(size_y):
                tile[half, pl.ds(y, channels, stride=size_y), :] = total[
                    half * channels : (half + 1) * channels, y * size_z : (y + 1) * size_z
                ]
            out_ref[:, 2 * pair + half] = (
                tile[half].reshape(channels, size_y, size_z).astype(BF16)
            )


def g3_scratch(channels, size_x, size_y, size_z):
    return pltpu.VMEM(((size_x + 2) * 3 * channels, (size_y + 2) * size_z), BF16)


def x3_scratch(channels, size_x, size_y, size_z):
    return pltpu.VMEM((size_x, 3 * channels, (size_y + 2) * size_z), BF16)


def acc_scratch(channels):
    return pltpu.VMEM((9 * channels, 3 * channels), F32)


def flat_scratch(channels):
    return pltpu.VMEM((-(-27 * channels // LANES) * LANES, LANES), F32)


def dgrad_scratch(channels, size_x, size_y, size_z):
    return [
        g3_scratch(channels, size_x, size_y, size_z),
        flat_scratch(channels),
        pltpu.VMEM((3, 2 * channels, 12 * channels), BF16),
        pltpu.VMEM((2, channels * size_y, size_z), F32),
    ]


def wgrad_cost(channels, size_x, size_y, size_z):
    return cost(54 * channels * channels * size_x * (size_y + 2) * size_z, 4 * 2**20)


def dgrad_cost(channels, size_x, size_y, size_z):
    return cost(72 * channels * channels * size_x * size_y * size_z, 4 * 2**20)


def row_for_other(body, size_z):
    plane = body.shape[-1]
    low, high = body[:, :size_z].astype(F32), body[:, plane - size_z :].astype(F32)
    return jnp.where(lax.axis_index("gy") == 0, high, low).astype(BF16)


def in_odd_swaps(axis):
    me, count = lax.axis_index(axis), lax.axis_size(axis)
    return (me > 0) & (me < count - 1 + count % 2)


def ends_kernel(order, *refs):
    choose(is_odd("gx"), refs[5], refs[2], refs[3])

    @pl.when(jnp.logical_not(in_odd_swaps("gx")))
    def _():
        read_inner(order, range(refs[4].shape[0]), *refs[:2], refs[4], *refs[6:])


def middles_kernel(order, *refs):
    p_ref, u_ref, first_ref, last_ref, m_ref, before_ref, g_ref, side_ref, sent_ref = refs[:9]
    p_buf, u_buf, tile, sems, sent_buf, sent_sem = refs[9:]
    half = before_ref.shape[0]
    inner, _, plane = g_ref.shape
    later = range(half, inner)
    middle = in_odd_swaps("gx")
    first_copies = fetches(range(half), p_ref, u_ref, p_buf, u_buf, sems)
    later_copies = fetches(later, p_ref, u_ref, p_buf, u_buf, sems)

    @pl.when(middle)
    def _():
        start(first_copies)

    start(later_copies)
    share = m_ref[...]
    share = jnp.concatenate(
        [share, jnp.zeros((-share.shape[0] % QUAD, share.shape[1]), F32)], axis=0
    )

    def write(at, quad):
        quad = quad.astype(BF16)
        sent_buf[:, :, at] = jnp.broadcast_to(quad[None], (sent_buf.shape[0], *quad.shape))

    to_quads(share, write)
    send = pltpu.make_async_copy(sent_buf, sent_ref, sent_sem)
    send.start()

    @pl.when(middle)
    def _():
        settle(order, range(half), first_copies, g_ref, p_buf, u_buf, tile)

    @pl.when(jnp.logical_not(middle))
    def _():
        g_ref[:half] = before_ref[...]

    settle(order, later, later_copies, g_ref, p_buf, u_buf, tile)
    size_z = side_ref.shape[-1]
    size_x = inner + 2
    bodies = [first_ref] + [g_ref.at[x] for x in range(inner)] + [last_ref]
    for x, body in enumerate(bodies):
        side_ref[x] = row_for_other(body, size_z)
    low, high = z_tiles(
        [body[...] for body in bodies], plane // size_z, size_z, range(1, size_x + 1)
    )
    side_ref[size_x] = low.astype(BF16)
    side_ref[size_x + 1] = high.astype(BF16)
    send.wait()


def pair_inner(preact, upstream, first, last, share, sent_shape, order):
    shape = preact.shape
    channels, size_x, _, size_z = shape
    made = [
        inner_output(*shape),
        jax.ShapeDtypeStruct((size_x + 2, channels, size_z), BF16),
    ]
    half = jax.ShapeDtypeStruct((made[0].shape[0] * 2 // 3, *made[0].shape[1:]), BF16)
    before, swap = pl.pallas_call(
        functools.partial(ends_kernel, order),
        in_specs=[HBM] * 2 + [VMEM] * 2,
        out_specs=[VMEM] * 2,
        out_shape=[half, jax.ShapeDtypeStruct(first.shape, BF16)],
        scratch_shapes=inner_scratch(*shape),
        compiler_params=params(ENDS_VMEM),
        cost_estimate=cost(0, 2**20),
        name="ends",
    )(preact, upstream, first, last)
    g, side_rows, sent = pl.pallas_call(
        functools.partial(middles_kernel, order),
        in_specs=[HBM] * 2 + [VMEM] * 4,
        out_specs=[VMEM] * 2 + [HBM],
        out_shape=made + [jax.ShapeDtypeStruct(sent_shape, BF16)],
        scratch_shapes=inner_scratch(*shape)
        + [pltpu.VMEM(sent_shape, BF16), pltpu.SemaphoreType.DMA(())],
        compiler_params=params(MIDDLES_VMEM),
        cost_estimate=cost(0, 4 * 2**20),
        name="middles",
    )(preact, upstream, first, last, share, before)
    return g, side_rows, swap, sent


def is_odd(axis):
    return lax.rem(lax.axis_index(axis), 2) == 1


def either(condition, first, second):
    return jnp.where(condition, first.astype(F32), second.astype(F32))


def side_kernel(odd_ref, even_ref, own_ref, sent_ref, xlo_ref, xhi_ref):
    size_x = own_ref.shape[0] - 2
    size_z = own_ref.shape[-1]
    size_y = xlo_ref.shape[-1] // size_z
    odd = is_odd("gx")
    low = either(odd, even_ref[...], odd_ref[...]).astype(BF16)
    high = either(odd, odd_ref[...], even_ref[...]).astype(BF16)
    xlo_ref[...] = low
    xhi_ref[...] = high
    sent_ref[0] = row_for_other(low, size_z)
    for x in range(size_x):
        sent_ref[x + 1] = own_ref[x]
    sent_ref[size_x + 1] = row_for_other(high, size_z)
    lane = lax.broadcasted_iota(jnp.int32, (low.shape[0], LANES), 1)
    first, second = own_ref[size_x], own_ref[size_x + 1]
    for number, plane in ((0, low), (size_x + 1, high)):
        for y in range(size_y):
            at = number * size_y + y
            head = plane[:, y * size_z : y * size_z + LANES]
            tail = plane[:, (y + 1) * size_z - LANES : (y + 1) * size_z]
            first = jnp.where(lane == at, pltpu.roll(head, at, 1), first)
            second = jnp.where(lane == at, pltpu.roll(tail, at + 1, 1), second)
    sent_ref[size_x + 2] = first
    sent_ref[size_x + 3] = second


def side(halves, own):
    plane = jax.ShapeDtypeStruct(halves[0].shape, BF16)
    return pl.pallas_call(
        side_kernel,
        in_specs=[VMEM] * 3,
        out_specs=[VMEM] * 3,
        out_shape=[
            jax.ShapeDtypeStruct((own.shape[0] + 2, *own.shape[1:]), BF16),
            plane,
            plane,
        ],
        compiler_params=params(),
        cost_estimate=cost(2**25, 2**19),
        name="side",
    )(*halves, own)


def own_columns(columns, number, area):
    me = lax.axis_index("gy")
    value = columns.astype(F32)
    lane = lax.broadcasted_iota(jnp.int32, value.shape, 1)
    first = pltpu.roll(value, -number * area % LANES, 1)
    second = pltpu.roll(value, (1 - number) * area % LANES, 1)
    first = jnp.where(lane < area, first, 0.0)
    second = jnp.where((lane >= area) & (lane < 2 * area), second, 0.0)
    return jnp.where(me == 0, first, second)


def join_kernel(area, own_ref, other_ref, columns_ref, even_ref, odd_ref):
    at = own_ref.shape[0] - 2
    me = lax.axis_index("gy")
    last = own_columns(columns_ref[...], 1, area).astype(BF16)

    def fill(up_ref, down_ref):
        for k, out_ref in enumerate((down_ref, up_ref)):
            out_ref[me] = own_ref[at + k]
            out_ref[1 - me] = other_ref[at + k]
        up_ref[2] = last
        down_ref[2] = last

    odd = is_odd("gz")

    @pl.when(odd)
    def _():
        fill(odd_ref, even_ref)

    @pl.when(jnp.logical_not(odd))
    def _():
        fill(even_ref, odd_ref)


def join(own, other, columns, area):
    return pl.pallas_call(
        functools.partial(join_kernel, area),
        in_specs=[VMEM] * 3,
        out_specs=[VMEM] * 2,
        out_shape=[jax.ShapeDtypeStruct((3, *own.shape[1:]), BF16)] * 2,
        compiler_params=params(),
        cost_estimate=cost(0, 2**17),
        name="join",
    )(own, other, columns)


def pair_wgrad_kernel(*refs):
    x_ref, acc_ref, g3, x3 = refs[7:]
    weight_products(refs, None, x_ref, g3, x3, acc_ref)


def pair_wgrad(sources, planes_x, shape):
    channels = shape[0]
    return pl.pallas_call(
        pair_wgrad_kernel,
        in_specs=[VMEM] * 8,
        out_specs=VMEM,
        out_shape=jax.ShapeDtypeStruct((9 * channels, 3 * channels), F32),
        scratch_shapes=[g3_scratch(*shape), x3_scratch(*shape)],
        compiler_params=params(32 * 2**20),
        cost_estimate=wgrad_cost(*shape),
        name="wgrad",
    )(*sources, planes_x)


def finish_kernel(scale, rows, sizes, *refs):
    acc_ref, columns_ref, even_ref, odd_ref, from_odd_ref, from_even_ref = refs[:6]
    part_ref, chunks = refs[6:]
    size_x, size_y = sizes
    channels = columns_ref.shape[0]
    area = size_x * size_y
    odd = is_odd("gz")
    lane = lax.broadcasted_iota(jnp.int32, (channels, LANES), 1)
    row = lane % size_y
    jump = area - size_y + 1
    below = [either(odd, from_even_ref[k], from_odd_ref[k]) for k in range(3)]
    own = [either(odd, even_ref[k], odd_ref[k]) for k in range(2)]
    pairs = ((below[:2], own_columns(columns_ref[...], 0, area)), (own, below[2]))
    edges = []
    for tiles, value in pairs:
        before = jnp.where(lane >= area, pltpu.roll(value, jump, 1), 0.0)
        after = jnp.where(lane < area, pltpu.roll(value, LANES - jump, 1), 0.0)
        right = jnp.concatenate(
            [
                jnp.where(row > 0, pltpu.roll(value, 1, 1), before),
                value,
                jnp.where(row < size_y - 1, pltpu.roll(value, LANES - 1, 1), after),
            ],
            axis=0,
        )
        left = []
        for a in range(3):
            first = pltpu.roll(tiles[0], -a * size_y % LANES, 1)
            second = pltpu.roll(tiles[1], (area - a * size_y) % LANES, 1)
            left.append(jnp.where(lane < area, first, jnp.where(lane < 2 * area, second, 0.0)))
        edges.append(
            lax.dot_general(
                jnp.concatenate(left, axis=0).astype(BF16),
                right.astype(BF16),
                (((1,), (1,)), ((), ())),
                preferred_element_type=F32,
            )
        )
    count = part_ref.shape[0]
    height, width = chunks.shape[0] // count, LANES
    chunks[...] = jnp.zeros_like(chunks)
    pieces = rows * acc_ref.shape[1] // width
    for a in range(3):
        for c in range(3):
            at = 3 * a + c
            block = acc_ref[at * channels : (at + 1) * channels, :]
            if c != 1:
                block = block + edges[c // 2][a * channels : (a + 1) * channels]
            block = block * scale
            line = jnp.concatenate(
                [block[r * count : (r + 1) * count] for r in range(rows)], axis=1
            )
            for k in range(pieces):
                chunks[pl.ds(at * pieces + k, count, stride=height), :] = line[
                    :, k * width : (k + 1) * width
                ]

    def write(at, quads):
        part_ref[:, :, at] = quads.astype(BF16)

    whole = chunks[...].reshape(count, height, width)
    to_quads(whole[:, : part_ref.shape[2] // LANES * QUAD], write)


def finish(acc, columns, sent, received, scale, rows, sizes, part_shape):
    channels = columns.shape[0]
    return pl.pallas_call(
        functools.partial(finish_kernel, scale, rows, sizes),
        in_specs=[VMEM] * 6,
        out_specs=VMEM,
        out_shape=jax.ShapeDtypeStruct(part_shape, BF16),
        scratch_shapes=[
            pltpu.VMEM((part_shape[0] * -(-part_shape[2] // LANES * QUAD // 8) * 8, LANES), F32),
        ],
        compiler_params=params(),
        cost_estimate=cost(2**27, 2**21),
        name="finish",
    )(acc, columns, *sent, *received)


def adam_step(master, first, second, weight_grad):
    new_first = 0.9 * first + 0.1 * weight_grad
    new_second = 0.999 * second + 0.001 * weight_grad * weight_grad
    corr_first = 1.0 - (0.9**10) ** 10
    corr_second = 1.0 - (0.999**10) ** 10
    update = new_first / corr_first / (jnp.sqrt(new_second / corr_second) + 1e-08) + 0.01 * master
    return master - 0.05 * update, new_first, new_second


def in_flat_order(value, rows, places, spread_rows):
    taps = 27
    lane = lax.broadcasted_iota(jnp.int32, (9, LANES), 1)
    for k in range(value.shape[1] // LANES):
        rows[k * QUAD : (k + 1) * QUAD, :] = value[:, k * LANES : (k + 1) * LANES]
    thirds = [rows[pl.ds(k, 9, stride=3), :] for k in range(3)]
    half = LANES // 2
    by_y = (
        jnp.where(lane < half, thirds[0], thirds[1]),
        jnp.where(lane < half, pltpu.roll(thirds[0], half, 1), pltpu.roll(thirds[2], half, 1)),
        jnp.where(lane < half, thirds[1], thirds[2]),
    )
    places[...] = jnp.zeros_like(places)
    for b in range(3):
        spread_rows[b, :9, :] = by_y[b]
        for block in range(9):
            tap = (2 - block // 3) * 9 + b * 3 + 2 - block % 3
            places[tap : tap + 1, :] = spread_rows[b, block : block + 1, :]
    line = places[...].T
    number = lax.broadcasted_iota(jnp.int32, (LANES, LANES), 0) * taps
    column = lax.broadcasted_iota(jnp.int32, (LANES, LANES), 1)
    turned = []
    for group in range(LANES // 8):
        piece = line[8 * group : 8 * (group + 1)]
        rest = 8 * group * taps % LANES
        for step in range(3):
            turn = rest // (3 - step)
            rest -= turn
            piece = pltpu.roll(piece, turn, 1, stride=taps // 3, stride_axis=0)
        turned.append(piece)
    line = jnp.concatenate(turned, axis=0)
    start = number & (LANES - 1)
    line = jnp.concatenate(
        [jnp.where(column >= start, line, 0.0), jnp.where(column < start, line, 0.0)], axis=0
    )
    target = lax.broadcasted_iota(jnp.int32, (32, 2 * LANES), 0)
    source = lax.broadcasted_iota(jnp.int32, (32, 2 * LANES), 1)
    goes = lax.shift_right_logical((source & (LANES - 1)) * taps, 7)
    goes = goes + jnp.where(source < LANES, 0, 1)
    pick = jnp.where(goes == target, 1.0, 0.0).astype(BF16)
    parts = []
    for _ in range(3):
        parts.append(line.astype(BF16))
        line = line - parts[-1].astype(F32)
    return jnp.dot(
        jnp.concatenate([pick] * 3, axis=1),
        jnp.concatenate(parts, axis=0),
        preferred_element_type=F32,
    )[:taps]


def adam_kernel(parts_ref, master_ref, first_ref, second_ref, *refs):
    out_refs, scratch = refs[:4], refs[4:]
    total = parts_ref[0].astype(F32)
    for source in range(1, parts_ref.shape[0]):
        total = total + parts_ref[source].astype(F32)
    weight_grad = in_flat_order(total, *scratch)
    results = adam_step(master_ref[...], first_ref[...], second_ref[...], weight_grad)
    for out_ref, result in zip(out_refs, (weight_grad, *results)):
        out_ref[...] = result


def adam(parts, *states):
    share = states[0].shape[0]
    tiled = [state.reshape(share // LANES, LANES) for state in states]
    result = jax.ShapeDtypeStruct(tiled[0].shape, F32)
    outs = pl.pallas_call(
        adam_kernel,
        in_specs=[VMEM] * 4,
        out_specs=[VMEM] * 4,
        out_shape=[result] * 4,
        scratch_shapes=[
            pltpu.VMEM((32, LANES), F32),
            pltpu.VMEM((LANES, LANES), F32),
            pltpu.VMEM((3, 16, LANES), F32),
        ],
        compiler_params=params(),
        cost_estimate=cost(2**22, 2**19),
        name="adam",
    )(parts, *tiled)
    return tuple(out.reshape(share) for out in outs)


def spread_kernel(rows, w_ref, weights_ref, turned, chunks):
    count = w_ref.shape[0]
    height = chunks.shape[0] // count
    taps = 27 * rows * count
    quads = [
        w_ref[:, :, k * LANES : (k + 1) * LANES].astype(F32)
        for k in range(w_ref.shape[2] // LANES)
    ]
    spare = jnp.zeros((count, height - QUAD * len(quads), LANES), F32)
    chunks[...] = jnp.concatenate(quads + [spare], axis=1).reshape(chunks.shape)
    line = jnp.concatenate(
        [chunks[pl.ds(k, count, stride=height), :] for k in range(rows * taps // LANES)], axis=1
    )
    whole = jnp.concatenate([line[:, r * taps : (r + 1) * taps] for r in range(rows)], axis=0)
    spread_weights(whole, turned, weights_ref)


def spread(kernel, channels, rows):
    return pl.pallas_call(
        functools.partial(spread_kernel, rows),
        in_specs=[VMEM],
        out_specs=VMEM,
        out_shape=jax.ShapeDtypeStruct((3, 2 * channels, 12 * channels), BF16),
        scratch_shapes=[
            flat_scratch(channels),
            pltpu.VMEM((kernel.shape[0] * 32, LANES), F32),
        ],
        compiler_params=params(),
        cost_estimate=cost(2**20, 2**21),
        name="spread",
    )(kernel)


def pair_dgrad_kernel(*refs):
    weights_ref, out_ref, g3, tile = refs[9:]
    _, size_x, size_y, size_z = out_ref.shape
    halo = pair_z_halo(refs[7], refs[8], size_x + 2, size_y, size_z)
    input_products(refs, halo, g3, weights_ref, tile, out_ref)


def pair_dgrad(sources, weights, shape):
    channels, _, size_y, size_z = shape
    return pl.pallas_call(
        pair_dgrad_kernel,
        in_specs=[VMEM] * 10,
        out_specs=VMEM,
        out_shape=jax.ShapeDtypeStruct(shape, BF16),
        scratch_shapes=[g3_scratch(*shape), pltpu.VMEM((2, channels * size_y, size_z), F32)],
        compiler_params=params(32 * 2**20),
        cost_estimate=dgrad_cost(*shape),
        name="dgrad",
    )(*sources, weights)


def pair_program(activations, preact, upstream, master, first_moment, second_moment, scale):
    shape = activations.shape
    channels, size_x, size_y, _ = shape
    devices = math.prod(lax.axis_size(a) for a in AXES)
    rows = channels // devices
    used = master.shape[0] // LANES
    block = (devices, QUAD, -(-used // QUAD) * LANES)
    first, last, odd_sent = faces(preact, upstream, "gx", rows)
    odd_halves = swapped(odd_sent, "gx", 1)
    inner, own, even_sent, sent = pair_inner(
        preact, upstream, first, last, master.reshape(used, LANES), block, rows
    )
    even_halves = swapped(even_sent, "gx", 0)
    kernel = lax.all_to_all(sent, AXES, 0, 0, tiled=True)
    own, xlo, xhi = side((odd_halves, even_halves), own)
    planes = (xlo, first, inner, last, xhi)
    own, activations = lax.optimization_barrier((own, activations))
    other = shifted(own, {"gy": "swap"})
    planes_x, columns = input_planes(activations, True)
    z_sent = join(own, other, columns, size_x * size_y)
    from_odd = swapped(z_sent[1], "gz", 1)
    from_even = swapped(z_sent[0], "gz", 0)
    sources = (*planes, other, other)
    acc = pair_wgrad(sources, planes_x, shape)
    z_received = (from_odd, from_even)
    part = finish(acc, columns, z_sent, z_received, scale, rows, (size_x, size_y), block)
    part, kernel = lax.optimization_barrier((part, kernel))
    parts = lax.all_to_all(part, AXES, 0, 0, tiled=True)
    weights = spread(kernel, channels, rows)
    grad_input = pair_dgrad((*sources, *z_received), weights, shape)
    return grad_input, *adam(parts, master, first_moment, second_moment)


def yface_kernel(*refs):
    low_ref, high_ref = refs[5:]
    size_z = low_ref.shape[-1]
    for index in range(low_ref.shape[0]):
        body = body_of(refs[:5], index)
        plane = body.shape[-1]
        low_ref[index] = body[:, :size_z]
        high_ref[index] = body[:, plane - size_z :]


def y_faces(planes, size_z):
    inner, channels, _ = planes[2].shape
    face = jax.ShapeDtypeStruct((inner + 4, channels, size_z), BF16)
    return pl.pallas_call(
        yface_kernel,
        in_specs=[VMEM] * 5,
        out_specs=[VMEM] * 2,
        out_shape=[face] * 2,
        compiler_params=params(),
        cost_estimate=cost(0, 2**19),
        name="yfaces",
    )(*planes)


def zface_kernel(*refs):
    zlo_ref, zhi_ref = refs[7:]
    size_z = refs[5].shape[-1]
    whole = []
    for index in range(refs[5].shape[0]):
        low, high = y_halo(refs[5:7], index)
        body = body_of(refs[:5], index)[...]
        whole.append(jnp.concatenate([low.astype(BF16), body, high.astype(BF16)], axis=1))
    low, high = z_tiles(whole, whole[0].shape[1] // size_z, size_z, range(len(whole)))
    zlo_ref[...] = low.astype(BF16)
    zhi_ref[...] = high.astype(BF16)


def z_faces(planes, y_halos):
    face = jax.ShapeDtypeStruct((planes[0].shape[0], LANES), BF16)
    return pl.pallas_call(
        zface_kernel,
        in_specs=[VMEM] * 7,
        out_specs=[VMEM] * 2,
        out_shape=[face, face],
        compiler_params=params(),
        cost_estimate=cost(2**27, 2**21),
        name="zfaces",
    )(*planes, *y_halos)


def wgrad_kernel(scale, *refs):
    x_ref, part_ref, g3, x3, acc, flat = refs[9:]
    size_x, channels, plane = x_ref.shape
    size_z = refs[5].shape[-1]
    halo = z_halo(refs[7], refs[8], size_x + 2, plane // size_z + 2, size_z)
    weight_products(refs, halo, x_ref, g3, x3, acc)
    whole = to_flat(acc[...] * scale, channels, channels, flat)
    part_ref[...] = whole[:, : part_ref.shape[1]].astype(BF16)


def wgrad(sources, planes_x, shape, scale):
    channels = shape[0]
    return pl.pallas_call(
        functools.partial(wgrad_kernel, scale),
        in_specs=[VMEM] * 10,
        out_specs=VMEM,
        out_shape=jax.ShapeDtypeStruct((channels, 27 * channels), BF16),
        scratch_shapes=[
            g3_scratch(*shape),
            x3_scratch(*shape),
            acc_scratch(channels),
            flat_scratch(channels),
        ],
        compiler_params=params(32 * 2**20),
        cost_estimate=wgrad_cost(*shape),
        name="wgrad",
    )(*sources, planes_x)


def dgrad_kernel(*refs):
    w_ref, out_ref, g3, turned, weights, tile = refs[9:]
    _, size_x, size_y, size_z = out_ref.shape
    spread_weights(w_ref[...].astype(F32), turned, weights)
    halo = z_halo(refs[7], refs[8], size_x + 2, size_y + 2, size_z)
    input_products(refs, halo, g3, weights, tile, out_ref)


def dgrad(sources, kernel, shape):
    return pl.pallas_call(
        dgrad_kernel,
        in_specs=[VMEM] * 10,
        out_specs=VMEM,
        out_shape=jax.ShapeDtypeStruct(shape, BF16),
        scratch_shapes=dgrad_scratch(*shape),
        compiler_params=params(32 * 2**20),
        cost_estimate=dgrad_cost(*shape),
        name="dgrad",
    )(*sources, kernel)


def general_program(activations, preact, upstream, master, first_moment, second_moment, scale):
    shape = activations.shape
    channels, _, _, size_z = shape
    devices = math.prod(lax.axis_size(a) for a in AXES)
    share = master.shape[0]
    first, last = faces(preact, upstream)
    x_halos = (shifted(last, {"gx": 1}), shifted(first, {"gx": -1}))
    inner = inner_planes(preact, upstream)
    (planes_x,) = input_planes(activations, False)
    sent = jnp.broadcast_to(master.astype(BF16).reshape(1, 1, share), (devices, 1, share))
    kernel = lax.all_to_all(sent, AXES, 0, 0, tiled=True).reshape(channels, 27 * channels)
    planes = (x_halos[0], first, inner, last, x_halos[1])
    y_sent = y_faces(planes, size_z)
    y_halos = (shifted(y_sent[1], {"gy": 1}), shifted(y_sent[0], {"gy": -1}))
    zlo, zhi = z_faces(planes, y_halos)
    z_halos = (shifted(zhi, {"gz": 1}), shifted(zlo, {"gz": -1}))
    sources = (*planes, *y_halos, *z_halos)
    part = wgrad(sources, planes_x, shape, scale)
    part, kernel = lax.optimization_barrier((part, kernel))
    parts = lax.all_to_all(part.reshape(devices, 1, share), AXES, 0, 0, tiled=True)
    grad_input = dgrad(sources, kernel, shape)
    weight_grad = jnp.sum(parts.astype(F32), axis=0).reshape(-1)
    results = adam_step(master, first_moment, second_moment, weight_grad)
    return grad_input, weight_grad, *results


def shifted(value, moves):
    names = tuple(moves)
    sizes = [lax.axis_size(name) for name in names]
    pairs = []
    for source in range(math.prod(sizes)):
        rest, coords = source, []
        for size in reversed(sizes):
            coords.insert(0, rest % size)
            rest //= size
        coords = [
            (at + moves[name]) if moves[name] != "swap" else 1 - at
            for at, name in zip(coords, names)
        ]
        if all(0 <= at < size for at, size in zip(coords, sizes)):
            target = 0
            for at, size in zip(coords, sizes):
                target = target * size + at
            pairs.append((source, target))
    return lax.ppermute(value, names if len(names) > 1 else names[0], pairs)


def swapped(value, axis, start):
    pairs = []
    for low in range(start, lax.axis_size(axis) - 1, 2):
        pairs += [(low, low + 1), (low + 1, low)]
    return lax.ppermute(value, axis, pairs)


def local(activations, preact, upstream, master, first_moment, second_moment):
    channels, size_x, size_y, size_z = activations.shape
    devices = math.prod(lax.axis_size(a) for a in AXES)
    share = master.shape[0]
    scale = 1.0 / math.sqrt(size_x * size_y * size_z * devices)
    in_pairs = (
        lax.axis_size("gy") == 2
        and channels % devices == 0
        and share % LANES == 0
        and channels // devices * channels == LANES
        and 2 * size_x * size_y <= LANES
        and (size_x + 2) * size_y <= LANES
    )
    program = pair_program if in_pairs else general_program
    return program(
        activations, preact, upstream, master, first_moment, second_moment, scale
    )


def solution(mesh):
    volume = P(None, "gx", "gy", "gz")
    flat = P(AXES)
    return jax.shard_map(
        local,
        mesh=mesh,
        in_specs=(volume, volume, volume, flat, flat, flat),
        out_specs=(volume, flat, flat, flat, flat),
        check_vma=False,
    )
```

```python
import functools
import math

import jax
import jax.numpy as jnp
from jax import lax
from jax.experimental import pallas as pl
from jax.experimental.pallas import tpu as pltpu
from jax.sharding import PartitionSpec as P

AXES = ("gx", "gy", "gz")
LANES = 128
VMEM = pl.BlockSpec(memory_space=pltpu.VMEM)
HBM = pl.BlockSpec(memory_space=pltpu.HBM)
F32 = jnp.float32
BF16 = jnp.bfloat16
FACES_VMEM = 55_900_000
INNER_VMEM = 54_800_000
ENDS_VMEM = 54_800_000
MIDDLES_VMEM = 54_000_000


def params(limit=24 * 2**20):
    return pltpu.CompilerParams(vmem_limit_bytes=limit)


def cost(flops, moved):
    return pl.CostEstimate(flops=flops, bytes_accessed=moved, transcendentals=0)


def to_planes(value, tile, write, rows=1):
    channels, size_y, size_z = value.shape
    count = channels // rows
    tile[...] = value.astype(F32).reshape(channels * size_y, size_z)
    for y in range(size_y):
        for r in range(rows):
            picked = tile[pl.ds(r * size_y + y, count, stride=rows * size_y), :]
            write(slice(r * count, (r + 1) * count), y, picked.astype(BF16))


QUAD = 4


def to_quads(rows, write):
    for k in range(rows.shape[-2] // QUAD):
        write(slice(k * LANES, (k + 1) * LANES), rows[..., k * QUAD : (k + 1) * QUAD, :])


def masked(p, u):
    return jnp.where(p.astype(F32) > 0, u.astype(F32), 0.0)


def choose(condition, out_ref, first_ref, second_ref):
    @pl.when(condition)
    def _():
        out_ref[...] = first_ref[...]

    @pl.when(jnp.logical_not(condition))
    def _():
        out_ref[...] = second_ref[...]


def face_kernel(axis, rows, p_ref, u_ref, *refs):
    p_buf, u_buf, tile, sems = refs[-4:]
    out_refs, swap_refs = refs[:2], refs[2:-4]
    size_x, size_z = p_ref.shape[1], p_ref.shape[3]
    copies = []
    for k, x in enumerate((0, size_x - 1)):
        pair = (
            pltpu.make_async_copy(p_ref.at[:, x], p_buf.at[k], sems.at[2 * k]),
            pltpu.make_async_copy(u_ref.at[:, x], u_buf.at[k], sems.at[2 * k + 1]),
        )
        for copy in pair:
            copy.start()
        copies.append(pair)
    for k, out_ref in enumerate(out_refs):
        for copy in copies[k]:
            copy.wait()

        def write(at, y, value):
            out_ref[at, y * size_z : (y + 1) * size_z] = value

        to_planes(masked(p_buf[k], u_buf[k]), tile.at[k], write, rows)
    if axis is not None:
        choose(is_odd(axis), swap_refs[0], out_refs[1], out_refs[0])


def faces(preact, upstream, axis=None, rows=1):
    channels, size_x, size_y, size_z = preact.shape
    face = jax.ShapeDtypeStruct((channels, size_y * size_z), BF16)
    buffer = pltpu.VMEM((2, channels, size_y, size_z), BF16)
    count = 2 if axis is None else 3
    return pl.pallas_call(
        functools.partial(face_kernel, axis, rows),
        in_specs=[HBM, HBM],
        out_specs=[VMEM] * count,
        out_shape=[face] * count,
        scratch_shapes=[
            buffer,
            buffer,
            pltpu.VMEM((2, channels * size_y, size_z), F32),
            pltpu.SemaphoreType.DMA((4,)),
        ],
        compiler_params=params(FACES_VMEM),
        cost_estimate=cost(0, 2**20),
        name="faces",
    )(preact, upstream)


def fetches(planes, p_ref, u_ref, p_buf, u_buf, sems):
    return [
        (
            pltpu.make_async_copy(p_ref.at[:, x + 1], p_buf.at[x], sems.at[2 * x]),
            pltpu.make_async_copy(u_ref.at[:, x + 1], u_buf.at[x], sems.at[2 * x + 1]),
        )
        for x in planes
    ]


def start(copies):
    for pair in copies:
        for copy in pair:
            copy.start()


def settle(order, planes, copies, g_ref, p_buf, u_buf, tile):
    size_z = p_buf.shape[-1]
    for x, pair in zip(planes, copies):
        for copy in pair:
            copy.wait()

        def write(at, y, value):
            g_ref[x, at, y * size_z : (y + 1) * size_z] = value

        to_planes(masked(p_buf[x], u_buf[x]), tile.at[x % 2], write, order)


def read_inner(order, planes, p_ref, u_ref, g_ref, p_buf, u_buf, tile, sems):
    copies = fetches(planes, p_ref, u_ref, p_buf, u_buf, sems)
    start(copies)
    settle(order, planes, copies, g_ref, p_buf, u_buf, tile)


def inner_kernel(*refs):
    read_inner(1, range(refs[2].shape[0]), *refs)


def inner_output(channels, size_x, size_y, size_z):
    return jax.ShapeDtypeStruct((size_x - 2, channels, size_y * size_z), BF16)


def inner_scratch(channels, size_x, size_y, size_z):
    return [
        pltpu.VMEM((size_x - 2, channels, size_y, size_z), BF16),
        pltpu.VMEM((size_x - 2, channels, size_y, size_z), BF16),
        pltpu.VMEM((2, channels * size_y, size_z), F32),
        pltpu.SemaphoreType.DMA((2 * size_x - 4,)),
    ]


def inner_planes(preact, upstream):
    shape = preact.shape
    return pl.pallas_call(
        inner_kernel,
        in_specs=[HBM] * 2,
        out_specs=VMEM,
        out_shape=inner_output(*shape),
        scratch_shapes=inner_scratch(*shape),
        compiler_params=params(INNER_VMEM),
        cost_estimate=cost(0, 4 * 2**20),
        name="inner",
    )(preact, upstream)


def input_kernel(a_ref, x_ref, *refs):
    tile = refs[-1]
    channels, size_x, size_y, size_z = a_ref.shape
    for x in range(size_x):

        def write(at, y, value):
            x_ref[x, at, y * size_z : (y + 1) * size_z] = value

        to_planes(a_ref[:, x], tile.at[x % 2], write)
    if len(refs) > 1:
        low, high = z_tiles([x_ref[x] for x in range(size_x)], size_y, size_z, range(size_x))
        refs[0][...] = (low + pltpu.roll(high, size_x * size_y, 1)).astype(BF16)


def input_planes(activations, with_columns):
    channels, size_x, size_y, size_z = activations.shape
    outs = [jax.ShapeDtypeStruct((size_x, channels, size_y * size_z), BF16)]
    if with_columns:
        outs.append(jax.ShapeDtypeStruct((channels, LANES), BF16))
    return pl.pallas_call(
        input_kernel,
        in_specs=[VMEM],
        out_specs=[VMEM] * len(outs),
        out_shape=outs,
        scratch_shapes=[pltpu.VMEM((2, channels * size_y, size_z), F32)],
        compiler_params=params(),
        cost_estimate=cost(0, 2 * 2**20),
        name="inputs",
    )(activations)


def body_of(refs, index):
    planes = refs[2].shape[0] + 4
    if 2 <= index < planes - 2:
        return refs[2].at[index - 2]
    return refs[{0: 0, 1: 1, planes - 2: 3, planes - 1: 4}[index]]


def y_halo(refs, index):
    me = lax.axis_index("gy")
    low = jnp.where(me > 0, refs[0][index].astype(F32), 0.0)
    high = jnp.where(me < lax.axis_size("gy") - 1, refs[1][index].astype(F32), 0.0)
    return low, high


def z_picker(rows_y, size_z):
    shape = (rows_y * size_z, 2 * LANES)
    voxel = lax.broadcasted_iota(jnp.int32, shape, 0)
    lane = lax.broadcasted_iota(jnp.int32, shape, 1)
    wanted = jnp.where(lane < LANES, lane * size_z, (lane - LANES) * size_z + size_z - 1)
    return (voxel == wanted).astype(F32).astype(BF16)


def z_tiles(planes, rows_y, size_z, numbers):
    channels = planes[0].shape[0]
    columns = jnp.dot(
        jnp.concatenate(planes, axis=0), z_picker(rows_y, size_z), preferred_element_type=F32
    )
    low = jnp.zeros((channels, LANES), F32)
    high = jnp.zeros((channels, LANES), F32)
    for index, number in enumerate(numbers):
        rows = columns[index * channels : (index + 1) * channels]
        low = low + pltpu.roll(rows[:, :LANES], number * rows_y, 1)
        high = high + pltpu.roll(rows[:, LANES:], number * rows_y, 1)
    return low, high


def put_columns(columns, row_of, rows_y, size_z):
    shape = (2 * LANES, rows_y * size_z)
    source = lax.broadcasted_iota(jnp.int32, shape, 0)
    voxel = lax.broadcasted_iota(jnp.int32, shape, 1)
    number = source % LANES
    place = row_of(number) * size_z + jnp.where(source < LANES, 0, size_z - 1)
    place = jnp.where(number < rows_y, place, -1)
    put = (voxel == place).astype(F32).astype(BF16)
    rows = [jnp.concatenate(pair, axis=1) for pair in columns]
    return jnp.dot(
        jnp.concatenate(rows, axis=0).astype(BF16), put, preferred_element_type=F32
    ).astype(BF16)


def z_halo(low_ref, high_ref, planes, rows_y, size_z):
    columns = []
    for index in range(planes):
        shift = -index * rows_y % LANES
        columns.append(
            [pltpu.roll(ref[...].astype(F32), shift, 1) for ref in (low_ref, high_ref)]
        )
    return put_columns(columns, lambda number: number, rows_y, size_z)


def pair_z_halo(odd_ref, even_ref, planes, size_y, size_z):
    me, odd = lax.axis_index("gy"), is_odd("gz")
    sides = []
    for low, high in ((even_ref, odd_ref), (odd_ref, even_ref)):
        first, second = (either(odd, low[k], high[k]) for k in range(2))
        lane = lax.broadcasted_iota(jnp.int32, first.shape, 1)
        own = jnp.where(me == 0, first, second)
        before = jnp.where(me == 0, 0.0, first)
        after = jnp.where(me == 0, second, 0.0)
        columns = []
        for index in range(planes):
            start = index * size_y
            columns.append(
                jnp.where(
                    lane < size_y,
                    pltpu.roll(own, -start % LANES, 1),
                    jnp.where(
                        lane == size_y,
                        pltpu.roll(before, (1 - start) % LANES, 1),
                        pltpu.roll(after, (size_y + 1 - start) % LANES, 1),
                    ),
                )
            )
        sides.append(columns)

    def row_of(number):
        return jnp.where(number < size_y, number + 1, jnp.where(number == size_y, 0, size_y + 1))

    return put_columns(list(zip(*sides)), row_of, size_y + 2, size_z)


def shifted_plane(index, refs, halo, g3):
    channels, plane = refs[0].shape
    size_z = refs[5].shape[-1]
    rows_y = plane // size_z + 2
    base = 3 * channels * index
    lane = lax.broadcasted_iota(jnp.int32, (channels, size_z), 1)
    is_first, is_last = lane == 0, lane == size_z - 1
    low, high = y_halo(refs[5:7], index)
    body = body_of(refs[:5], index)
    for row in range(rows_y):
        cols = slice(row * size_z, (row + 1) * size_z)
        if row == 0:
            value = low.astype(BF16)
        elif row == rows_y - 1:
            value = high.astype(BF16)
        else:
            value = body[:, (row - 1) * size_z : row * size_z]
        if halo is None:
            edge = jnp.zeros_like(value)
        else:
            edge = halo[index * channels : (index + 1) * channels, cols]
        before = jnp.where(is_first, edge, pltpu.roll(value, 1, 1))
        after = jnp.where(is_last, edge, pltpu.roll(value, size_z - 1, 1))
        g3[base : base + channels, cols] = before
        g3[base + channels : base + 2 * channels, cols] = value
        g3[base + 2 * channels : base + 3 * channels, cols] = after


def weight_products(refs, halo, x_ref, g3, x3, acc):
    size_x, channels, plane = x_ref.shape
    size_z = refs[5].shape[-1]
    group = 3 * channels
    zero = jnp.zeros((channels, 2 * size_z), BF16)
    done = 0
    for x in range(0, size_x, 2):
        while done < x + 4:
            shifted_plane(done, refs, halo, g3)
            done += 1
        for plane_x in (x, x + 1):
            value = x_ref[plane_x]
            for b in range(3):
                at = slice(b * channels, (b + 1) * channels)
                start = (2 - b) * size_z
                x3[plane_x, at, start : start + plane] = value
                if start:
                    x3[plane_x, at, :start] = zero[:, :start]
                if start < 2 * size_z:
                    x3[plane_x, at, start + plane :] = zero[:, start:]
        product = lax.dot_general(
            jnp.concatenate(
                [g3[x * group : (x + 3) * group, :], g3[(x + 1) * group : (x + 4) * group, :]],
                axis=1,
            ),
            jnp.concatenate([x3[x], x3[x + 1]], axis=1),
            (((1,), (1,)), ((), ())),
            preferred_element_type=F32,
        )
        if x == 0:
            acc[...] = product
        else:
            acc[...] += product


def to_flat(value, count, channels, flat):
    height, width = value.shape
    wide = value
    if height % LANES:
        wide = jnp.concatenate([wide, jnp.zeros((-height % LANES, width), F32)], axis=0)
    if width % LANES:
        wide = jnp.concatenate([wide, jnp.zeros((wide.shape[0], -width % LANES), F32)], axis=1)
    turned = wide.T
    for b in range(3):
        rows = turned[b * channels : (b + 1) * channels]
        for block in range(9):
            start = block * count
            cell = rows[:, start // LANES * LANES : (start // LANES + 1) * LANES]
            tap = (2 - block // 3) * 9 + b * 3 + 2 - block % 3
            shift = -start % LANES
            flat[pl.ds(tap, channels, stride=27), :] = pltpu.roll(cell, shift, 1) if shift else cell
    return flat[...].T[:count]


def spread_weights(whole, turned, weights):
    channels, taps = whole.shape
    group = 3 * channels
    whole = jnp.concatenate([whole, jnp.zeros((LANES - channels, taps), F32)], axis=0)
    whole = jnp.concatenate([whole, jnp.zeros((LANES, -taps % LANES), F32)], axis=1)
    turned[...] = whole.T
    for b in range(3):
        blocks = []
        for a in range(3):
            for c in range(3):
                tap = (2 - a) * 9 + (2 - b) * 3 + 2 - c
                blocks.append(turned[pl.ds(tap, channels, stride=27), :][:, :channels])
        zero = jnp.zeros((channels, group), F32)
        weights[b, :channels] = jnp.concatenate(blocks + [zero], axis=1).astype(BF16)
        weights[b, channels:] = jnp.concatenate([zero] + blocks, axis=1).astype(BF16)


def input_products(refs, halo, g3, weights, tile, out_ref):
    channels, size_x, size_y, size_z = out_ref.shape
    group = 3 * channels
    plane = size_y * size_z
    done = 0
    for pair in range(size_x // 2):
        while done < 2 * pair + 4:
            shifted_plane(done, refs, halo, g3)
            done += 1
        at = slice(2 * pair * group, (2 * pair + 4) * group)
        total = None
        for b in range(3):
            product = jnp.dot(
                weights[b],
                g3[at, b * size_z : b * size_z + plane],
                preferred_element_type=F32,
            )
            total = product if total is None else total + product
        for half in range(2):
            for y in range(size_y):
                tile[half, pl.ds(y, channels, stride=size_y), :] = total[
                    half * channels : (half + 1) * channels, y * size_z : (y + 1) * size_z
                ]
            out_ref[:, 2 * pair + half] = (
                tile[half].reshape(channels, size_y, size_z).astype(BF16)
            )


def g3_scratch(channels, size_x, size_y, size_z):
    return pltpu.VMEM(((size_x + 2) * 3 * channels, (size_y + 2) * size_z), BF16)


def x3_scratch(channels, size_x, size_y, size_z):
    return pltpu.VMEM((size_x, 3 * channels, (size_y + 2) * size_z), BF16)


def acc_scratch(channels):
    return pltpu.VMEM((9 * channels, 3 * channels), F32)


def flat_scratch(channels):
    return pltpu.VMEM((-(-27 * channels // LANES) * LANES, LANES), F32)


def dgrad_scratch(channels, size_x, size_y, size_z):
    return [
        g3_scratch(channels, size_x, size_y, size_z),
        flat_scratch(channels),
        pltpu.VMEM((3, 2 * channels, 12 * channels), BF16),
        pltpu.VMEM((2, channels * size_y, size_z), F32),
    ]


def wgrad_cost(channels, size_x, size_y, size_z):
    return cost(54 * channels * channels * size_x * (size_y + 2) * size_z, 4 * 2**20)


def dgrad_cost(channels, size_x, size_y, size_z):
    return cost(72 * channels * channels * size_x * size_y * size_z, 4 * 2**20)


def row_for_other(body, size_z):
    plane = body.shape[-1]
    low, high = body[:, :size_z].astype(F32), body[:, plane - size_z :].astype(F32)
    return jnp.where(lax.axis_index("gy") == 0, high, low).astype(BF16)


def in_odd_swaps(axis):
    me, count = lax.axis_index(axis), lax.axis_size(axis)
    return (me > 0) & (me < count - 1 + count % 2)


def ends_kernel(order, *refs):
    choose(is_odd("gx"), refs[5], refs[2], refs[3])

    @pl.when(jnp.logical_not(in_odd_swaps("gx")))
    def _():
        read_inner(order, range(refs[4].shape[0]), *refs[:2], refs[4], *refs[6:])


def middles_kernel(order, *refs):
    p_ref, u_ref, first_ref, last_ref, m_ref, before_ref, g_ref, side_ref, sent_ref = refs[:9]
    p_buf, u_buf, tile, sems, sent_buf, sent_sem = refs[9:]
    half = before_ref.shape[0]
    inner, _, plane = g_ref.shape
    later = range(half, inner)
    middle = in_odd_swaps("gx")
    first_copies = fetches(range(half), p_ref, u_ref, p_buf, u_buf, sems)
    later_copies = fetches(later, p_ref, u_ref, p_buf, u_buf, sems)

    @pl.when(middle)
    def _():
        start(first_copies)

    start(later_copies)
    share = m_ref[...]
    share = jnp.concatenate(
        [share, jnp.zeros((-share.shape[0] % QUAD, share.shape[1]), F32)], axis=0
    )

    def write(at, quad):
        quad = quad.astype(BF16)
        sent_buf[:, :, at] = jnp.broadcast_to(quad[None], (sent_buf.shape[0], *quad.shape))

    to_quads(share, write)
    send = pltpu.make_async_copy(sent_buf, sent_ref, sent_sem)
    send.start()

    @pl.when(middle)
    def _():
        settle(order, range(half), first_copies, g_ref, p_buf, u_buf, tile)

    @pl.when(jnp.logical_not(middle))
    def _():
        g_ref[:half] = before_ref[...]

    settle(order, later, later_copies, g_ref, p_buf, u_buf, tile)
    size_z = side_ref.shape[-1]
    size_x = inner + 2
    bodies = [first_ref] + [g_ref.at[x] for x in range(inner)] + [last_ref]
    for x, body in enumerate(bodies):
        side_ref[x] = row_for_other(body, size_z)
    low, high = z_tiles(
        [body[...] for body in bodies], plane // size_z, size_z, range(1, size_x + 1)
    )
    side_ref[size_x] = low.astype(BF16)
    side_ref[size_x + 1] = high.astype(BF16)
    send.wait()


def pair_inner(preact, upstream, first, last, share, sent_shape, order):
    shape = preact.shape
    channels, size_x, _, size_z = shape
    made = [
        inner_output(*shape),
        jax.ShapeDtypeStruct((size_x + 2, channels, size_z), BF16),
    ]
    half = jax.ShapeDtypeStruct((made[0].shape[0], *made[0].shape[1:]), BF16)
    before, swap = pl.pallas_call(
        functools.partial(ends_kernel, order),
        in_specs=[HBM] * 2 + [VMEM] * 2,
        out_specs=[VMEM] * 2,
        out_shape=[half, jax.ShapeDtypeStruct(first.shape, BF16)],
        scratch_shapes=inner_scratch(*shape),
        compiler_params=params(ENDS_VMEM),
        cost_estimate=cost(0, 2**20),
        name="ends",
    )(preact, upstream, first, last)
    g, side_rows, sent = pl.pallas_call(
        functools.partial(middles_kernel, order),
        in_specs=[HBM] * 2 + [VMEM] * 4,
        out_specs=[VMEM] * 2 + [HBM],
        out_shape=made + [jax.ShapeDtypeStruct(sent_shape, BF16)],
        scratch_shapes=inner_scratch(*shape)
        + [pltpu.VMEM(sent_shape, BF16), pltpu.SemaphoreType.DMA(())],
        compiler_params=params(MIDDLES_VMEM),
        cost_estimate=cost(0, 4 * 2**20),
        name="middles",
    )(preact, upstream, first, last, share, before)
    return g, side_rows, swap, sent


def is_odd(axis):
    return lax.rem(lax.axis_index(axis), 2) == 1


def either(condition, first, second):
    return jnp.where(condition, first.astype(F32), second.astype(F32))


def side_kernel(odd_ref, even_ref, own_ref, sent_ref, xlo_ref, xhi_ref):
    size_x = own_ref.shape[0] - 2
    size_z = own_ref.shape[-1]
    size_y = xlo_ref.shape[-1] // size_z
    odd = is_odd("gx")
    low = either(odd, even_ref[...], odd_ref[...]).astype(BF16)
    high = either(odd, odd_ref[...], even_ref[...]).astype(BF16)
    xlo_ref[...] = low
    xhi_ref[...] = high
    sent_ref[0] = row_for_other(low, size_z)
    for x in range(size_x):
        sent_ref[x + 1] = own_ref[x]
    sent_ref[size_x + 1] = row_for_other(high, size_z)
    lane = lax.broadcasted_iota(jnp.int32, (low.shape[0], LANES), 1)
    first, second = own_ref[size_x], own_ref[size_x + 1]
    for number, plane in ((0, low), (size_x + 1, high)):
        for y in range(size_y):
            at = number * size_y + y
            head = plane[:, y * size_z : y * size_z + LANES]
            tail = plane[:, (y + 1) * size_z - LANES : (y + 1) * size_z]
            first = jnp.where(lane == at, pltpu.roll(head, at, 1), first)
            second = jnp.where(lane == at, pltpu.roll(tail, at + 1, 1), second)
    sent_ref[size_x + 2] = first
    sent_ref[size_x + 3] = second


def side(halves, own):
    plane = jax.ShapeDtypeStruct(halves[0].shape, BF16)
    return pl.pallas_call(
        side_kernel,
        in_specs=[VMEM] * 3,
        out_specs=[VMEM] * 3,
        out_shape=[
            jax.ShapeDtypeStruct((own.shape[0] + 2, *own.shape[1:]), BF16),
            plane,
            plane,
        ],
        compiler_params=params(),
        cost_estimate=cost(2**25, 2**19),
        name="side",
    )(*halves, own)


def own_columns(columns, number, area):
    me = lax.axis_index("gy")
    value = columns.astype(F32)
    lane = lax.broadcasted_iota(jnp.int32, value.shape, 1)
    first = pltpu.roll(value, -number * area % LANES, 1)
    second = pltpu.roll(value, (1 - number) * area % LANES, 1)
    first = jnp.where(lane < area, first, 0.0)
    second = jnp.where((lane >= area) & (lane < 2 * area), second, 0.0)
    return jnp.where(me == 0, first, second)


def join_kernel(area, own_ref, other_ref, columns_ref, even_ref, odd_ref):
    at = own_ref.shape[0] - 2
    me = lax.axis_index("gy")
    last = own_columns(columns_ref[...], 1, area).astype(BF16)

    def fill(up_ref, down_ref):
        for k, out_ref in enumerate((down_ref, up_ref)):
            out_ref[me] = own_ref[at + k]
            out_ref[1 - me] = other_ref[at + k]
        up_ref[2] = last
        down_ref[2] = last

    odd = is_odd("gz")

    @pl.when(odd)
    def _():
        fill(odd_ref, even_ref)

    @pl.when(jnp.logical_not(odd))
    def _():
        fill(even_ref, odd_ref)


def join(own, other, columns, area):
    return pl.pallas_call(
        functools.partial(join_kernel, area),
        in_specs=[VMEM] * 3,
        out_specs=[VMEM] * 2,
        out_shape=[jax.ShapeDtypeStruct((3, *own.shape[1:]), BF16)] * 2,
        compiler_params=params(),
        cost_estimate=cost(0, 2**17),
        name="join",
    )(own, other, columns)


def pair_wgrad_kernel(*refs):
    x_ref, acc_ref, g3, x3 = refs[7:]
    weight_products(refs, None, x_ref, g3, x3, acc_ref)


def pair_wgrad(sources, planes_x, shape):
    channels = shape[0]
    return pl.pallas_call(
        pair_wgrad_kernel,
        in_specs=[VMEM] * 8,
        out_specs=VMEM,
        out_shape=jax.ShapeDtypeStruct((9 * channels, 3 * channels), F32),
        scratch_shapes=[g3_scratch(*shape), x3_scratch(*shape)],
        compiler_params=params(32 * 2**20),
        cost_estimate=wgrad_cost(*shape),
        name="wgrad",
    )(*sources, planes_x)


def finish_kernel(scale, rows, sizes, *refs):
    acc_ref, columns_ref, even_ref, odd_ref, from_odd_ref, from_even_ref = refs[:6]
    part_ref, chunks = refs[6:]
    size_x, size_y = sizes
    channels = columns_ref.shape[0]
    area = size_x * size_y
    odd = is_odd("gz")
    lane = lax.broadcasted_iota(jnp.int32, (channels, LANES), 1)
    row = lane % size_y
    jump = area - size_y + 1
    below = [either(odd, from_even_ref[k], from_odd_ref[k]) for k in range(3)]
    own = [either(odd, even_ref[k], odd_ref[k]) for k in range(2)]
    pairs = ((below[:2], own_columns(columns_ref[...], 0, area)), (own, below[2]))
    edges = []
    for tiles, value in pairs:
        before = jnp.where(lane >= area, pltpu.roll(value, jump, 1), 0.0)
        after = jnp.where(lane < area, pltpu.roll(value, LANES - jump, 1), 0.0)
        right = jnp.concatenate(
            [
                jnp.where(row > 0, pltpu.roll(value, 1, 1), before),
                value,
                jnp.where(row < size_y - 1, pltpu.roll(value, LANES - 1, 1), after),
            ],
            axis=0,
        )
        left = []
        for a in range(3):
            first = pltpu.roll(tiles[0], -a * size_y % LANES, 1)
            second = pltpu.roll(tiles[1], (area - a * size_y) % LANES, 1)
            left.append(jnp.where(lane < area, first, jnp.where(lane < 2 * area, second, 0.0)))
        edges.append(
            lax.dot_general(
                jnp.concatenate(left, axis=0).astype(BF16),
                right.astype(BF16),
                (((1,), (1,)), ((), ())),
                preferred_element_type=F32,
            )
        )
    count = part_ref.shape[0]
    height, width = chunks.shape[0] // count, LANES
    chunks[...] = jnp.zeros_like(chunks)
    pieces = rows * acc_ref.shape[1] // width
    for a in range(3):
        for c in range(3):
            at = 3 * a + c
            block = acc_ref[at * channels : (at + 1) * channels, :]
            if c != 1:
                block = block + edges[c // 2][a * channels : (a + 1) * channels]
            block = block * scale
            line = jnp.concatenate(
                [block[r * count : (r + 1) * count] for r in range(rows)], axis=1
            )
            for k in range(pieces):
                chunks[pl.ds(at * pieces + k, count, stride=height), :] = line[
                    :, k * width : (k + 1) * width
                ]

    def write(at, quads):
        part_ref[:, :, at] = quads.astype(BF16)

    whole = chunks[...].reshape(count, height, width)
    to_quads(whole[:, : part_ref.shape[2] // LANES * QUAD], write)


def finish(acc, columns, sent, received, scale, rows, sizes, part_shape):
    channels = columns.shape[0]
    return pl.pallas_call(
        functools.partial(finish_kernel, scale, rows, sizes),
        in_specs=[VMEM] * 6,
        out_specs=VMEM,
        out_shape=jax.ShapeDtypeStruct(part_shape, BF16),
        scratch_shapes=[
            pltpu.VMEM((part_shape[0] * -(-part_shape[2] // LANES * QUAD // 8) * 8, LANES), F32),
        ],
        compiler_params=params(),
        cost_estimate=cost(2**27, 2**21),
        name="finish",
    )(acc, columns, *sent, *received)


def adam_step(master, first, second, weight_grad):
    new_first = 0.9 * first + 0.1 * weight_grad
    new_second = 0.999 * second + 0.001 * weight_grad * weight_grad
    corr_first = 1.0 - (0.9**10) ** 10
    corr_second = 1.0 - (0.999**10) ** 10
    update = new_first / corr_first / (jnp.sqrt(new_second / corr_second) + 1e-08) + 0.01 * master
    return master - 0.05 * update, new_first, new_second


def in_flat_order(value, rows, places, spread_rows):
    taps = 27
    lane = lax.broadcasted_iota(jnp.int32, (9, LANES), 1)
    for k in range(value.shape[1] // LANES):
        rows[k * QUAD : (k + 1) * QUAD, :] = value[:, k * LANES : (k + 1) * LANES]
    thirds = [rows[pl.ds(k, 9, stride=3), :] for k in range(3)]
    half = LANES // 2
    by_y = (
        jnp.where(lane < half, thirds[0], thirds[1]),
        jnp.where(lane < half, pltpu.roll(thirds[0], half, 1), pltpu.roll(thirds[2], half, 1)),
        jnp.where(lane < half, thirds[1], thirds[2]),
    )
    places[...] = jnp.zeros_like(places)
    for b in range(3):
        spread_rows[b, :9, :] = by_y[b]
        for block in range(9):
            tap = (2 - block // 3) * 9 + b * 3 + 2 - block % 3
            places[tap : tap + 1, :] = spread_rows[b, block : block + 1, :]
    line = places[...].T
    number = lax.broadcasted_iota(jnp.int32, (LANES, LANES), 0) * taps
    column = lax.broadcasted_iota(jnp.int32, (LANES, LANES), 1)
    turned = []
    for group in range(LANES // 8):
        piece = line[8 * group : 8 * (group + 1)]
        rest = 8 * group * taps % LANES
        for step in range(3):
            turn = rest // (3 - step)
            rest -= turn
            piece = pltpu.roll(piece, turn, 1, stride=taps // 3, stride_axis=0)
        turned.append(piece)
    line = jnp.concatenate(turned, axis=0)
    start = number & (LANES - 1)
    line = jnp.concatenate(
        [jnp.where(column >= start, line, 0.0), jnp.where(column < start, line, 0.0)], axis=0
    )
    target = lax.broadcasted_iota(jnp.int32, (32, 2 * LANES), 0)
    source = lax.broadcasted_iota(jnp.int32, (32, 2 * LANES), 1)
    goes = lax.shift_right_logical((source & (LANES - 1)) * taps, 7)
    goes = goes + jnp.where(source < LANES, 0, 1)
    pick = jnp.where(goes == target, 1.0, 0.0).astype(BF16)
    parts = []
    for _ in range(3):
        parts.append(line.astype(BF16))
        line = line - parts[-1].astype(F32)
    return jnp.dot(
        jnp.concatenate([pick] * 3, axis=1),
        jnp.concatenate(parts, axis=0),
        preferred_element_type=F32,
    )[:taps]


def adam_kernel(parts_ref, master_ref, first_ref, second_ref, *refs):
    out_refs, scratch = refs[:4], refs[4:]
    total = parts_ref[0].astype(F32)
    for source in range(1, parts_ref.shape[0]):
        total = total + parts_ref[source].astype(F32)
    weight_grad = in_flat_order(total, *scratch)
    results = adam_step(master_ref[...], first_ref[...], second_ref[...], weight_grad)
    for out_ref, result in zip(out_refs, (weight_grad, *results)):
        out_ref[...] = result


def adam(parts, *states):
    share = states[0].shape[0]
    tiled = [state.reshape(share // LANES, LANES) for state in states]
    result = jax.ShapeDtypeStruct(tiled[0].shape, F32)
    outs = pl.pallas_call(
        adam_kernel,
        in_specs=[VMEM] * 4,
        out_specs=[VMEM] * 4,
        out_shape=[result] * 4,
        scratch_shapes=[
            pltpu.VMEM((32, LANES), F32),
            pltpu.VMEM((LANES, LANES), F32),
            pltpu.VMEM((3, 16, LANES), F32),
        ],
        compiler_params=params(),
        cost_estimate=cost(2**22, 2**19),
        name="adam",
    )(parts, *tiled)
    return tuple(out.reshape(share) for out in outs)


def spread_kernel(rows, w_ref, weights_ref, turned, chunks):
    count = w_ref.shape[0]
    height = chunks.shape[0] // count
    taps = 27 * rows * count
    quads = [
        w_ref[:, :, k * LANES : (k + 1) * LANES].astype(F32)
        for k in range(w_ref.shape[2] // LANES)
    ]
    spare = jnp.zeros((count, height - QUAD * len(quads), LANES), F32)
    chunks[...] = jnp.concatenate(quads + [spare], axis=1).reshape(chunks.shape)
    line = jnp.concatenate(
        [chunks[pl.ds(k, count, stride=height), :] for k in range(rows * taps // LANES)], axis=1
    )
    whole = jnp.concatenate([line[:, r * taps : (r + 1) * taps] for r in range(rows)], axis=0)
    spread_weights(whole, turned, weights_ref)


def spread(kernel, channels, rows):
    return pl.pallas_call(
        functools.partial(spread_kernel, rows),
        in_specs=[VMEM],
        out_specs=VMEM,
        out_shape=jax.ShapeDtypeStruct((3, 2 * channels, 12 * channels), BF16),
        scratch_shapes=[
            flat_scratch(channels),
            pltpu.VMEM((kernel.shape[0] * 32, LANES), F32),
        ],
        compiler_params=params(),
        cost_estimate=cost(2**20, 2**21),
        name="spread",
    )(kernel)


def pair_dgrad_kernel(*refs):
    weights_ref, out_ref, g3, tile = refs[9:]
    _, size_x, size_y, size_z = out_ref.shape
    halo = pair_z_halo(refs[7], refs[8], size_x + 2, size_y, size_z)
    input_products(refs, halo, g3, weights_ref, tile, out_ref)


def pair_dgrad(sources, weights, shape):
    channels, _, size_y, size_z = shape
    return pl.pallas_call(
        pair_dgrad_kernel,
        in_specs=[VMEM] * 10,
        out_specs=VMEM,
        out_shape=jax.ShapeDtypeStruct(shape, BF16),
        scratch_shapes=[g3_scratch(*shape), pltpu.VMEM((2, channels * size_y, size_z), F32)],
        compiler_params=params(32 * 2**20),
        cost_estimate=dgrad_cost(*shape),
        name="dgrad",
    )(*sources, weights)


def pair_program(activations, preact, upstream, master, first_moment, second_moment, scale):
    shape = activations.shape
    channels, size_x, size_y, _ = shape
    devices = math.prod(lax.axis_size(a) for a in AXES)
    rows = channels // devices
    used = master.shape[0] // LANES
    block = (devices, QUAD, -(-used // QUAD) * LANES)
    first, last, odd_sent = faces(preact, upstream, "gx", rows)
    odd_halves = swapped(odd_sent, "gx", 1)
    inner, own, even_sent, sent = pair_inner(
        preact, upstream, first, last, master.reshape(used, LANES), block, rows
    )
    even_halves = swapped(even_sent, "gx", 0)
    kernel = lax.all_to_all(sent, AXES, 0, 0, tiled=True)
    own, xlo, xhi = side((odd_halves, even_halves), own)
    planes = (xlo, first, inner, last, xhi)
    own, activations = lax.optimization_barrier((own, activations))
    other = shifted(own, {"gy": "swap"})
    planes_x, columns = input_planes(activations, True)
    z_sent = join(own, other, columns, size_x * size_y)
    from_odd = swapped(z_sent[1], "gz", 1)
    from_even = swapped(z_sent[0], "gz", 0)
    sources = (*planes, other, other)
    acc = pair_wgrad(sources, planes_x, shape)
    z_received = (from_odd, from_even)
    part = finish(acc, columns, z_sent, z_received, scale, rows, (size_x, size_y), block)
    part, kernel = lax.optimization_barrier((part, kernel))
    parts = lax.all_to_all(part, AXES, 0, 0, tiled=True)
    weights = spread(kernel, channels, rows)
    grad_input = pair_dgrad((*sources, *z_received), weights, shape)
    return grad_input, *adam(parts, master, first_moment, second_moment)


def yface_kernel(*refs):
    low_ref, high_ref = refs[5:]
    size_z = low_ref.shape[-1]
    for index in range(low_ref.shape[0]):
        body = body_of(refs[:5], index)
        plane = body.shape[-1]
        low_ref[index] = body[:, :size_z]
        high_ref[index] = body[:, plane - size_z :]


def y_faces(planes, size_z):
    inner, channels, _ = planes[2].shape
    face = jax.ShapeDtypeStruct((inner + 4, channels, size_z), BF16)
    return pl.pallas_call(
        yface_kernel,
        in_specs=[VMEM] * 5,
        out_specs=[VMEM] * 2,
        out_shape=[face] * 2,
        compiler_params=params(),
        cost_estimate=cost(0, 2**19),
        name="yfaces",
    )(*planes)


def zface_kernel(*refs):
    zlo_ref, zhi_ref = refs[7:]
    size_z = refs[5].shape[-1]
    whole = []
    for index in range(refs[5].shape[0]):
        low, high = y_halo(refs[5:7], index)
        body = body_of(refs[:5], index)[...]
        whole.append(jnp.concatenate([low.astype(BF16), body, high.astype(BF16)], axis=1))
    low, high = z_tiles(whole, whole[0].shape[1] // size_z, size_z, range(len(whole)))
    zlo_ref[...] = low.astype(BF16)
    zhi_ref[...] = high.astype(BF16)


def z_faces(planes, y_halos):
    face = jax.ShapeDtypeStruct((planes[0].shape[0], LANES), BF16)
    return pl.pallas_call(
        zface_kernel,
        in_specs=[VMEM] * 7,
        out_specs=[VMEM] * 2,
        out_shape=[face, face],
        compiler_params=params(),
        cost_estimate=cost(2**27, 2**21),
        name="zfaces",
    )(*planes, *y_halos)


def wgrad_kernel(scale, *refs):
    x_ref, part_ref, g3, x3, acc, flat = refs[9:]
    size_x, channels, plane = x_ref.shape
    size_z = refs[5].shape[-1]
    halo = z_halo(refs[7], refs[8], size_x + 2, plane // size_z + 2, size_z)
    weight_products(refs, halo, x_ref, g3, x3, acc)
    whole = to_flat(acc[...] * scale, channels, channels, flat)
    part_ref[...] = whole[:, : part_ref.shape[1]].astype(BF16)


def wgrad(sources, planes_x, shape, scale):
    channels = shape[0]
    return pl.pallas_call(
        functools.partial(wgrad_kernel, scale),
        in_specs=[VMEM] * 10,
        out_specs=VMEM,
        out_shape=jax.ShapeDtypeStruct((channels, 27 * channels), BF16),
        scratch_shapes=[
            g3_scratch(*shape),
            x3_scratch(*shape),
            acc_scratch(channels),
            flat_scratch(channels),
        ],
        compiler_params=params(32 * 2**20),
        cost_estimate=wgrad_cost(*shape),
        name="wgrad",
    )(*sources, planes_x)


def dgrad_kernel(*refs):
    w_ref, out_ref, g3, turned, weights, tile = refs[9:]
    _, size_x, size_y, size_z = out_ref.shape
    spread_weights(w_ref[...].astype(F32), turned, weights)
    halo = z_halo(refs[7], refs[8], size_x + 2, size_y + 2, size_z)
    input_products(refs, halo, g3, weights, tile, out_ref)


def dgrad(sources, kernel, shape):
    return pl.pallas_call(
        dgrad_kernel,
        in_specs=[VMEM] * 10,
        out_specs=VMEM,
        out_shape=jax.ShapeDtypeStruct(shape, BF16),
        scratch_shapes=dgrad_scratch(*shape),
        compiler_params=params(32 * 2**20),
        cost_estimate=dgrad_cost(*shape),
        name="dgrad",
    )(*sources, kernel)


def general_program(activations, preact, upstream, master, first_moment, second_moment, scale):
    shape = activations.shape
    channels, _, _, size_z = shape
    devices = math.prod(lax.axis_size(a) for a in AXES)
    share = master.shape[0]
    first, last = faces(preact, upstream)
    x_halos = (shifted(last, {"gx": 1}), shifted(first, {"gx": -1}))
    inner = inner_planes(preact, upstream)
    (planes_x,) = input_planes(activations, False)
    sent = jnp.broadcast_to(master.astype(BF16).reshape(1, 1, share), (devices, 1, share))
    kernel = lax.all_to_all(sent, AXES, 0, 0, tiled=True).reshape(channels, 27 * channels)
    planes = (x_halos[0], first, inner, last, x_halos[1])
    y_sent = y_faces(planes, size_z)
    y_halos = (shifted(y_sent[1], {"gy": 1}), shifted(y_sent[0], {"gy": -1}))
    zlo, zhi = z_faces(planes, y_halos)
    z_halos = (shifted(zhi, {"gz": 1}), shifted(zlo, {"gz": -1}))
    sources = (*planes, *y_halos, *z_halos)
    part = wgrad(sources, planes_x, shape, scale)
    part, kernel = lax.optimization_barrier((part, kernel))
    parts = lax.all_to_all(part.reshape(devices, 1, share), AXES, 0, 0, tiled=True)
    grad_input = dgrad(sources, kernel, shape)
    weight_grad = jnp.sum(parts.astype(F32), axis=0).reshape(-1)
    results = adam_step(master, first_moment, second_moment, weight_grad)
    return grad_input, weight_grad, *results


def shifted(value, moves):
    names = tuple(moves)
    sizes = [lax.axis_size(name) for name in names]
    pairs = []
    for source in range(math.prod(sizes)):
        rest, coords = source, []
        for size in reversed(sizes):
            coords.insert(0, rest % size)
            rest //= size
        coords = [
            (at + moves[name]) if moves[name] != "swap" else 1 - at
            for at, name in zip(coords, names)
        ]
        if all(0 <= at < size for at, size in zip(coords, sizes)):
            target = 0
            for at, size in zip(coords, sizes):
                target = target * size + at
            pairs.append((source, target))
    return lax.ppermute(value, names if len(names) > 1 else names[0], pairs)


def swapped(value, axis, start):
    pairs = []
    for low in range(start, lax.axis_size(axis) - 1, 2):
        pairs += [(low, low + 1), (low + 1, low)]
    return lax.ppermute(value, axis, pairs)


def local(activations, preact, upstream, master, first_moment, second_moment):
    channels, size_x, size_y, size_z = activations.shape
    devices = math.prod(lax.axis_size(a) for a in AXES)
    share = master.shape[0]
    scale = 1.0 / math.sqrt(size_x * size_y * size_z * devices)
    in_pairs = (
        lax.axis_size("gy") == 2
        and channels % devices == 0
        and share % LANES == 0
        and channels // devices * channels == LANES
        and 2 * size_x * size_y <= LANES
        and (size_x + 2) * size_y <= LANES
    )
    program = pair_program if in_pairs else general_program
    return program(
        activations, preact, upstream, master, first_moment, second_moment, scale
    )


def solution(mesh):
    volume = P(None, "gx", "gy", "gz")
    flat = P(AXES)
    return jax.shard_map(
        local,
        mesh=mesh,
        in_specs=(volume, volume, volume, flat, flat, flat),
        out_specs=(volume, flat, flat, flat, flat),
        check_vma=False,
    )
```

```python
import functools
import math

import jax
import jax.numpy as jnp
from jax import lax
from jax.experimental import pallas as pl
from jax.experimental.pallas import tpu as pltpu
from jax.sharding import PartitionSpec as P

AXES = ("gx", "gy", "gz")
LANES = 128
VMEM = pl.BlockSpec(memory_space=pltpu.VMEM)
HBM = pl.BlockSpec(memory_space=pltpu.HBM)
F32 = jnp.float32
BF16 = jnp.bfloat16
FACES_VMEM = 55_900_000
INNER_VMEM = 54_800_000
ENDS_VMEM = 54_800_000
MIDDLES_VMEM = 54_000_000


def params(limit=24 * 2**20):
    return pltpu.CompilerParams(vmem_limit_bytes=limit)


def cost(flops, moved):
    return pl.CostEstimate(flops=flops, bytes_accessed=moved, transcendentals=0)


def to_planes(value, tile, write, rows=1):
    channels, size_y, size_z = value.shape
    count = channels // rows
    tile[...] = value.astype(F32).reshape(channels * size_y, size_z)
    for y in range(size_y):
        for r in range(rows):
            picked = tile[pl.ds(r * size_y + y, count, stride=rows * size_y), :]
            write(slice(r * count, (r + 1) * count), y, picked.astype(BF16))


QUAD = 4


def to_quads(rows, write):
    for k in range(rows.shape[-2] // QUAD):
        write(slice(k * LANES, (k + 1) * LANES), rows[..., k * QUAD : (k + 1) * QUAD, :])


def masked(p, u):
    return jnp.where(p.astype(F32) > 0, u.astype(F32), 0.0)


def choose(condition, out_ref, first_ref, second_ref):
    @pl.when(condition)
    def _():
        out_ref[...] = first_ref[...]

    @pl.when(jnp.logical_not(condition))
    def _():
        out_ref[...] = second_ref[...]


def face_kernel(axis, rows, p_ref, u_ref, *refs):
    p_buf, u_buf, tile, sems = refs[-4:]
    out_refs, swap_refs = refs[:2], refs[2:-4]
    size_x, size_z = p_ref.shape[1], p_ref.shape[3]
    copies = []
    for k, x in enumerate((0, size_x - 1)):
        pair = (
            pltpu.make_async_copy(p_ref.at[:, x], p_buf.at[k], sems.at[2 * k]),
            pltpu.make_async_copy(u_ref.at[:, x], u_buf.at[k], sems.at[2 * k + 1]),
        )
        for copy in pair:
            copy.start()
        copies.append(pair)
    for k, out_ref in enumerate(out_refs):
        for copy in copies[k]:
            copy.wait()

        def write(at, y, value):
            out_ref[at, y * size_z : (y + 1) * size_z] = value

        to_planes(masked(p_buf[k], u_buf[k]), tile.at[k], write, rows)
    if axis is not None:
        choose(is_odd(axis), swap_refs[0], out_refs[1], out_refs[0])


def faces(preact, upstream, axis=None, rows=1):
    channels, size_x, size_y, size_z = preact.shape
    face = jax.ShapeDtypeStruct((channels, size_y * size_z), BF16)
    buffer = pltpu.VMEM((2, channels, size_y, size_z), BF16)
    count = 2 if axis is None else 3
    return pl.pallas_call(
        functools.partial(face_kernel, axis, rows),
        in_specs=[HBM, HBM],
        out_specs=[VMEM] * count,
        out_shape=[face] * count,
        scratch_shapes=[
            buffer,
            buffer,
            pltpu.VMEM((2, channels * size_y, size_z), F32),
            pltpu.SemaphoreType.DMA((4,)),
        ],
        compiler_params=params(FACES_VMEM),
        cost_estimate=cost(0, 2**20),
        name="faces",
    )(preact, upstream)


def fetches(planes, p_ref, u_ref, p_buf, u_buf, sems):
    return [
        (
            pltpu.make_async_copy(p_ref.at[:, x + 1], p_buf.at[x], sems.at[2 * x]),
            pltpu.make_async_copy(u_ref.at[:, x + 1], u_buf.at[x], sems.at[2 * x + 1]),
        )
        for x in planes
    ]


def start(copies):
    for pair in copies:
        for copy in pair:
            copy.start()


def settle(order, planes, copies, g_ref, p_buf, u_buf, tile):
    size_z = p_buf.shape[-1]
    for x, pair in zip(planes, copies):
        for copy in pair:
            copy.wait()

        def write(at, y, value):
            g_ref[x, at, y * size_z : (y + 1) * size_z] = value

        to_planes(masked(p_buf[x], u_buf[x]), tile.at[x % 2], write, order)


def read_inner(order, planes, p_ref, u_ref, g_ref, p_buf, u_buf, tile, sems):
    copies = fetches(planes, p_ref, u_ref, p_buf, u_buf, sems)
    start(copies)
    settle(order, planes, copies, g_ref, p_buf, u_buf, tile)


def inner_kernel(*refs):
    read_inner(1, range(refs[2].shape[0]), *refs)


def inner_output(channels, size_x, size_y, size_z):
    return jax.ShapeDtypeStruct((size_x - 2, channels, size_y * size_z), BF16)


def inner_scratch(channels, size_x, size_y, size_z):
    return [
        pltpu.VMEM((size_x - 2, channels, size_y, size_z), BF16),
        pltpu.VMEM((size_x - 2, channels, size_y, size_z), BF16),
        pltpu.VMEM((2, channels * size_y, size_z), F32),
        pltpu.SemaphoreType.DMA((2 * size_x - 4,)),
    ]


def inner_planes(preact, upstream):
    shape = preact.shape
    return pl.pallas_call(
        inner_kernel,
        in_specs=[HBM] * 2,
        out_specs=VMEM,
        out_shape=inner_output(*shape),
        scratch_shapes=inner_scratch(*shape),
        compiler_params=params(INNER_VMEM),
        cost_estimate=cost(0, 4 * 2**20),
        name="inner",
    )(preact, upstream)


def input_kernel(a_ref, x_ref, *refs):
    tile = refs[-1]
    channels, size_x, size_y, size_z = a_ref.shape
    for x in range(size_x):

        def write(at, y, value):
            x_ref[x, at, y * size_z : (y + 1) * size_z] = value

        to_planes(a_ref[:, x], tile.at[x % 2], write)
    if len(refs) > 1:
        low, high = z_tiles([x_ref[x] for x in range(size_x)], size_y, size_z, range(size_x))
        refs[0][...] = (low + pltpu.roll(high, size_x * size_y, 1)).astype(BF16)


def input_planes(activations, with_columns):
    channels, size_x, size_y, size_z = activations.shape
    outs = [jax.ShapeDtypeStruct((size_x, channels, size_y * size_z), BF16)]
    if with_columns:
        outs.append(jax.ShapeDtypeStruct((channels, LANES), BF16))
    return pl.pallas_call(
        input_kernel,
        in_specs=[VMEM],
        out_specs=[VMEM] * len(outs),
        out_shape=outs,
        scratch_shapes=[pltpu.VMEM((2, channels * size_y, size_z), F32)],
        compiler_params=params(),
        cost_estimate=cost(0, 2 * 2**20),
        name="inputs",
    )(activations)


def body_of(refs, index):
    planes = refs[2].shape[0] + 4
    if 2 <= index < planes - 2:
        return refs[2].at[index - 2]
    return refs[{0: 0, 1: 1, planes - 2: 3, planes - 1: 4}[index]]


def y_halo(refs, index):
    me = lax.axis_index("gy")
    low = jnp.where(me > 0, refs[0][index].astype(F32), 0.0)
    high = jnp.where(me < lax.axis_size("gy") - 1, refs[1][index].astype(F32), 0.0)
    return low, high


def z_picker(rows_y, size_z):
    shape = (rows_y * size_z, 2 * LANES)
    voxel = lax.broadcasted_iota(jnp.int32, shape, 0)
    lane = lax.broadcasted_iota(jnp.int32, shape, 1)
    wanted = jnp.where(lane < LANES, lane * size_z, (lane - LANES) * size_z + size_z - 1)
    return (voxel == wanted).astype(F32).astype(BF16)


def z_tiles(planes, rows_y, size_z, numbers):
    channels = planes[0].shape[0]
    columns = jnp.dot(
        jnp.concatenate(planes, axis=0), z_picker(rows_y, size_z), preferred_element_type=F32
    )
    low = jnp.zeros((channels, LANES), F32)
    high = jnp.zeros((channels, LANES), F32)
    for index, number in enumerate(numbers):
        rows = columns[index * channels : (index + 1) * channels]
        low = low + pltpu.roll(rows[:, :LANES], number * rows_y, 1)
        high = high + pltpu.roll(rows[:, LANES:], number * rows_y, 1)
    return low, high


def put_columns(columns, row_of, rows_y, size_z):
    shape = (2 * LANES, rows_y * size_z)
    source = lax.broadcasted_iota(jnp.int32, shape, 0)
    voxel = lax.broadcasted_iota(jnp.int32, shape, 1)
    number = source % LANES
    place = row_of(number) * size_z + jnp.where(source < LANES, 0, size_z - 1)
    place = jnp.where(number < rows_y, place, -1)
    put = (voxel == place).astype(F32).astype(BF16)
    rows = [jnp.concatenate(pair, axis=1) for pair in columns]
    return jnp.dot(
        jnp.concatenate(rows, axis=0).astype(BF16), put, preferred_element_type=F32
    ).astype(BF16)


def z_halo(low_ref, high_ref, planes, rows_y, size_z):
    columns = []
    for index in range(planes):
        shift = -index * rows_y % LANES
        columns.append(
            [pltpu.roll(ref[...].astype(F32), shift, 1) for ref in (low_ref, high_ref)]
        )
    return put_columns(columns, lambda number: number, rows_y, size_z)


def pair_z_halo(odd_ref, even_ref, planes, size_y, size_z):
    me, odd = lax.axis_index("gy"), is_odd("gz")
    sides = []
    for low, high in ((even_ref, odd_ref), (odd_ref, even_ref)):
        first, second = (either(odd, low[k], high[k]) for k in range(2))
        lane = lax.broadcasted_iota(jnp.int32, first.shape, 1)
        own = jnp.where(me == 0, first, second)
        before = jnp.where(me == 0, 0.0, first)
        after = jnp.where(me == 0, second, 0.0)
        columns = []
        for index in range(planes):
            start = index * size_y
            columns.append(
                jnp.where(
                    lane < size_y,
                    pltpu.roll(own, -start % LANES, 1),
                    jnp.where(
                        lane == size_y,
                        pltpu.roll(before, (1 - start) % LANES, 1),
                        pltpu.roll(after, (size_y + 1 - start) % LANES, 1),
                    ),
                )
            )
        sides.append(columns)

    def row_of(number):
        return jnp.where(number < size_y, number + 1, jnp.where(number == size_y, 0, size_y + 1))

    return put_columns(list(zip(*sides)), row_of, size_y + 2, size_z)


def shifted_plane(index, refs, halo, g3):
    channels, plane = refs[0].shape
    size_z = refs[5].shape[-1]
    rows_y = plane // size_z + 2
    base = 3 * channels * index
    lane = lax.broadcasted_iota(jnp.int32, (channels, size_z), 1)
    is_first, is_last = lane == 0, lane == size_z - 1
    low, high = y_halo(refs[5:7], index)
    body = body_of(refs[:5], index)
    for row in range(rows_y):
        cols = slice(row * size_z, (row + 1) * size_z)
        if row == 0:
            value = low.astype(BF16)
        elif row == rows_y - 1:
            value = high.astype(BF16)
        else:
            value = body[:, (row - 1) * size_z : row * size_z]
        if halo is None:
            edge = jnp.zeros_like(value)
        else:
            edge = halo[index * channels : (index + 1) * channels, cols]
        before = jnp.where(is_first, edge, pltpu.roll(value, 1, 1))
        after = jnp.where(is_last, edge, pltpu.roll(value, size_z - 1, 1))
        g3[base : base + channels, cols] = before
        g3[base + channels : base + 2 * channels, cols] = value
        g3[base + 2 * channels : base + 3 * channels, cols] = after


def weight_products(refs, halo, x_ref, g3, x3, acc):
    size_x, channels, plane = x_ref.shape
    size_z = refs[5].shape[-1]
    group = 3 * channels
    zero = jnp.zeros((channels, 2 * size_z), BF16)
    done = 0
    for x in range(0, size_x, 2):
        while done < x + 4:
            shifted_plane(done, refs, halo, g3)
            done += 1
        for plane_x in (x, x + 1):
            value = x_ref[plane_x]
            for b in range(3):
                at = slice(b * channels, (b + 1) * channels)
                start = (2 - b) * size_z
                x3[plane_x, at, start : start + plane] = value
                if start:
                    x3[plane_x, at, :start] = zero[:, :start]
                if start < 2 * size_z:
                    x3[plane_x, at, start + plane :] = zero[:, start:]
        product = lax.dot_general(
            jnp.concatenate(
                [g3[x * group : (x + 3) * group, :], g3[(x + 1) * group : (x + 4) * group, :]],
                axis=1,
            ),
            jnp.concatenate([x3[x], x3[x + 1]], axis=1),
            (((1,), (1,)), ((), ())),
            preferred_element_type=F32,
        )
        if x == 0:
            acc[...] = product
        else:
            acc[...] += product


def to_flat(value, count, channels, flat):
    height, width = value.shape
    wide = value
    if height % LANES:
        wide = jnp.concatenate([wide, jnp.zeros((-height % LANES, width), F32)], axis=0)
    if width % LANES:
        wide = jnp.concatenate([wide, jnp.zeros((wide.shape[0], -width % LANES), F32)], axis=1)
    turned = wide.T
    for b in range(3):
        rows = turned[b * channels : (b + 1) * channels]
        for block in range(9):
            start = block * count
            cell = rows[:, start // LANES * LANES : (start // LANES + 1) * LANES]
            tap = (2 - block // 3) * 9 + b * 3 + 2 - block % 3
            shift = -start % LANES
            flat[pl.ds(tap, channels, stride=27), :] = pltpu.roll(cell, shift, 1) if shift else cell
    return flat[...].T[:count]


def spread_weights(whole, turned, weights):
    channels, taps = whole.shape
    group = 3 * channels
    whole = jnp.concatenate([whole, jnp.zeros((LANES - channels, taps), F32)], axis=0)
    whole = jnp.concatenate([whole, jnp.zeros((LANES, -taps % LANES), F32)], axis=1)
    turned[...] = whole.T
    for b in range(3):
        blocks = []
        for a in range(3):
            for c in range(3):
                tap = (2 - a) * 9 + (2 - b) * 3 + 2 - c
                blocks.append(turned[pl.ds(tap, channels, stride=27), :][:, :channels])
        zero = jnp.zeros((channels, group), F32)
        weights[b, :channels] = jnp.concatenate(blocks + [zero], axis=1).astype(BF16)
        weights[b, channels:] = jnp.concatenate([zero] + blocks, axis=1).astype(BF16)


def input_products(refs, halo, g3, weights, tile, out_ref):
    channels, size_x, size_y, size_z = out_ref.shape
    group = 3 * channels
    plane = size_y * size_z
    done = 0
    for pair in range(size_x // 2):
        while done < 2 * pair + 4:
            shifted_plane(done, refs, halo, g3)
            done += 1
        at = slice(2 * pair * group, (2 * pair + 4) * group)
        total = None
        for b in range(3):
            product = jnp.dot(
                weights[b],
                g3[at, b * size_z : b * size_z + plane],
                preferred_element_type=F32,
            )
            total = product if total is None else total + product
        for half in range(2):
            for y in range(size_y):
                tile[half, pl.ds(y, channels, stride=size_y), :] = total[
                    half * channels : (half + 1) * channels, y * size_z : (y + 1) * size_z
                ]
            out_ref[:, 2 * pair + half] = (
                tile[half].reshape(channels, size_y, size_z).astype(BF16)
            )


def g3_scratch(channels, size_x, size_y, size_z):
    return pltpu.VMEM(((size_x + 2) * 3 * channels, (size_y + 2) * size_z), BF16)


def x3_scratch(channels, size_x, size_y, size_z):
    return pltpu.VMEM((size_x, 3 * channels, (size_y + 2) * size_z), BF16)


def acc_scratch(channels):
    return pltpu.VMEM((9 * channels, 3 * channels), F32)


def flat_scratch(channels):
    return pltpu.VMEM((-(-27 * channels // LANES) * LANES, LANES), F32)


def dgrad_scratch(channels, size_x, size_y, size_z):
    return [
        g3_scratch(channels, size_x, size_y, size_z),
        flat_scratch(channels),
        pltpu.VMEM((3, 2 * channels, 12 * channels), BF16),
        pltpu.VMEM((2, channels * size_y, size_z), F32),
    ]


def wgrad_cost(channels, size_x, size_y, size_z):
    return cost(54 * channels * channels * size_x * (size_y + 2) * size_z, 4 * 2**20)


def dgrad_cost(channels, size_x, size_y, size_z):
    return cost(72 * channels * channels * size_x * size_y * size_z, 4 * 2**20)


def row_for_other(body, size_z):
    plane = body.shape[-1]
    low, high = body[:, :size_z].astype(F32), body[:, plane - size_z :].astype(F32)
    return jnp.where(lax.axis_index("gy") == 0, high, low).astype(BF16)


def in_odd_swaps(axis):
    me, count = lax.axis_index(axis), lax.axis_size(axis)
    return (me > 0) & (me < count - 1 + count % 2)


def ends_kernel(order, *refs):
    choose(is_odd("gx"), refs[5], refs[2], refs[3])

    @pl.when(jnp.logical_not(in_odd_swaps("gx")))
    def _():
        read_inner(order, range(refs[4].shape[0]), *refs[:2], refs[4], *refs[6:])


def middles_kernel(order, *refs):
    p_ref, u_ref, first_ref, last_ref, m_ref, before_ref, g_ref, side_ref, sent_ref = refs[:9]
    p_buf, u_buf, tile, sems, sent_buf, sent_sem = refs[9:]
    half = before_ref.shape[0]
    inner, _, plane = g_ref.shape
    later = range(half, inner)
    middle = in_odd_swaps("gx")
    first_copies = fetches(range(half), p_ref, u_ref, p_buf, u_buf, sems)
    later_copies = fetches(later, p_ref, u_ref, p_buf, u_buf, sems)

    @pl.when(middle)
    def _():
        start(first_copies)

    start(later_copies)
    share = m_ref[...]
    share = jnp.concatenate(
        [share, jnp.zeros((-share.shape[0] % QUAD, share.shape[1]), F32)], axis=0
    )

    def write(at, quad):
        quad = quad.astype(BF16)
        sent_buf[:, :, at] = jnp.broadcast_to(quad[None], (sent_buf.shape[0], *quad.shape))

    to_quads(share, write)
    send = pltpu.make_async_copy(sent_buf, sent_ref, sent_sem)
    send.start()

    @pl.when(middle)
    def _():
        settle(order, range(half), first_copies, g_ref, p_buf, u_buf, tile)

    @pl.when(jnp.logical_not(middle))
    def _():
        g_ref[:half] = before_ref[...]

    settle(order, later, later_copies, g_ref, p_buf, u_buf, tile)
    size_z = side_ref.shape[-1]
    size_x = inner + 2
    bodies = [first_ref] + [g_ref.at[x] for x in range(inner)] + [last_ref]
    for x, body in enumerate(bodies):
        side_ref[x] = row_for_other(body, size_z)
    low, high = z_tiles(
        [body[...] for body in bodies], plane // size_z, size_z, range(1, size_x + 1)
    )
    side_ref[size_x] = low.astype(BF16)
    side_ref[size_x + 1] = high.astype(BF16)
    send.wait()


def pair_inner(preact, upstream, first, last, share, sent_shape, order):
    shape = preact.shape
    channels, size_x, _, size_z = shape
    made = [
        inner_output(*shape),
        jax.ShapeDtypeStruct((size_x + 2, channels, size_z), BF16),
    ]
    half = jax.ShapeDtypeStruct((made[0].shape[0], *made[0].shape[1:]), BF16)
    before, swap = pl.pallas_call(
        functools.partial(ends_kernel, order),
        in_specs=[HBM] * 2 + [VMEM] * 2,
        out_specs=[VMEM] * 2,
        out_shape=[half, jax.ShapeDtypeStruct(first.shape, BF16)],
        scratch_shapes=inner_scratch(*shape),
        compiler_params=params(ENDS_VMEM),
        cost_estimate=cost(0, 2**20),
        name="ends",
    )(preact, upstream, first, last)
    g, side_rows, sent = pl.pallas_call(
        functools.partial(middles_kernel, order),
        in_specs=[HBM] * 2 + [VMEM] * 4,
        out_specs=[VMEM] * 2 + [HBM],
        out_shape=made + [jax.ShapeDtypeStruct(sent_shape, BF16)],
        scratch_shapes=inner_scratch(*shape)
        + [pltpu.VMEM(sent_shape, BF16), pltpu.SemaphoreType.DMA(())],
        compiler_params=params(MIDDLES_VMEM),
        cost_estimate=cost(0, 4 * 2**20),
        name="middles",
    )(preact, upstream, first, last, share, before)
    return g, side_rows, swap, sent


def is_odd(axis):
    return lax.rem(lax.axis_index(axis), 2) == 1


def either(condition, first, second):
    return jnp.where(condition, first.astype(F32), second.astype(F32))


def side_kernel(odd_ref, even_ref, own_ref, sent_ref, xlo_ref, xhi_ref):
    size_x = own_ref.shape[0] - 2
    size_z = own_ref.shape[-1]
    size_y = xlo_ref.shape[-1] // size_z
    odd = is_odd("gx")
    low = either(odd, even_ref[...], odd_ref[...]).astype(BF16)
    high = either(odd, odd_ref[...], even_ref[...]).astype(BF16)
    xlo_ref[...] = low
    xhi_ref[...] = high
    sent_ref[0] = row_for_other(low, size_z)
    for x in range(size_x):
        sent_ref[x + 1] = own_ref[x]
    sent_ref[size_x + 1] = row_for_other(high, size_z)
    lane = lax.broadcasted_iota(jnp.int32, (low.shape[0], LANES), 1)
    first, second = own_ref[size_x], own_ref[size_x + 1]
    for number, plane in ((0, low), (size_x + 1, high)):
        for y in range(size_y):
            at = number * size_y + y
            head = plane[:, y * size_z : y * size_z + LANES]
            tail = plane[:, (y + 1) * size_z - LANES : (y + 1) * size_z]
            first = jnp.where(lane == at, pltpu.roll(head, at, 1), first)
            second = jnp.where(lane == at, pltpu.roll(tail, at + 1, 1), second)
    sent_ref[size_x + 2] = first
    sent_ref[size_x + 3] = second


def side(halves, own):
    plane = jax.ShapeDtypeStruct(halves[0].shape, BF16)
    return pl.pallas_call(
        side_kernel,
        in_specs=[VMEM] * 3,
        out_specs=[VMEM] * 3,
        out_shape=[
            jax.ShapeDtypeStruct((own.shape[0] + 2, *own.shape[1:]), BF16),
            plane,
            plane,
        ],
        compiler_params=params(),
        cost_estimate=cost(2**25, 2**19),
        name="side",
    )(*halves, own)


def own_columns(columns, number, area):
    me = lax.axis_index("gy")
    value = columns.astype(F32)
    lane = lax.broadcasted_iota(jnp.int32, value.shape, 1)
    first = pltpu.roll(value, -number * area % LANES, 1)
    second = pltpu.roll(value, (1 - number) * area % LANES, 1)
    first = jnp.where(lane < area, first, 0.0)
    second = jnp.where((lane >= area) & (lane < 2 * area), second, 0.0)
    return jnp.where(me == 0, first, second)


def join_kernel(area, own_ref, other_ref, columns_ref, even_ref, odd_ref):
    at = own_ref.shape[0] - 2
    me = lax.axis_index("gy")
    last = own_columns(columns_ref[...], 1, area).astype(BF16)

    def fill(up_ref, down_ref):
        for k, out_ref in enumerate((down_ref, up_ref)):
            out_ref[me] = own_ref[at + k]
            out_ref[1 - me] = other_ref[at + k]
        up_ref[2] = last
        down_ref[2] = last

    odd = is_odd("gz")

    @pl.when(odd)
    def _():
        fill(odd_ref, even_ref)

    @pl.when(jnp.logical_not(odd))
    def _():
        fill(even_ref, odd_ref)


def join(own, other, columns, area):
    return pl.pallas_call(
        functools.partial(join_kernel, area),
        in_specs=[VMEM] * 3,
        out_specs=[VMEM] * 2,
        out_shape=[jax.ShapeDtypeStruct((3, *own.shape[1:]), BF16)] * 2,
        compiler_params=params(),
        cost_estimate=cost(0, 2**17),
        name="join",
    )(own, other, columns)


def pair_wgrad_kernel(*refs):
    x_ref, acc_ref, g3, x3 = refs[7:]
    weight_products(refs, None, x_ref, g3, x3, acc_ref)


def pair_wgrad(sources, planes_x, shape):
    channels = shape[0]
    return pl.pallas_call(
        pair_wgrad_kernel,
        in_specs=[VMEM] * 8,
        out_specs=VMEM,
        out_shape=jax.ShapeDtypeStruct((9 * channels, 3 * channels), F32),
        scratch_shapes=[g3_scratch(*shape), x3_scratch(*shape)],
        compiler_params=params(32 * 2**20),
        cost_estimate=wgrad_cost(*shape),
        name="wgrad",
    )(*sources, planes_x)


def finish_kernel(scale, rows, sizes, *refs):
    acc_ref, columns_ref, even_ref, odd_ref, from_odd_ref, from_even_ref = refs[:6]
    part_ref, chunks = refs[6:]
    size_x, size_y = sizes
    channels = columns_ref.shape[0]
    area = size_x * size_y
    odd = is_odd("gz")
    lane = lax.broadcasted_iota(jnp.int32, (channels, LANES), 1)
    row = lane % size_y
    jump = area - size_y + 1
    below = [either(odd, from_even_ref[k], from_odd_ref[k]) for k in range(3)]
    own = [either(odd, even_ref[k], odd_ref[k]) for k in range(2)]
    pairs = ((below[:2], own_columns(columns_ref[...], 0, area)), (own, below[2]))
    edges = []
    for tiles, value in pairs:
        before = jnp.where(lane >= area, pltpu.roll(value, jump, 1), 0.0)
        after = jnp.where(lane < area, pltpu.roll(value, LANES - jump, 1), 0.0)
        right = jnp.concatenate(
            [
                jnp.where(row > 0, pltpu.roll(value, 1, 1), before),
                value,
                jnp.where(row < size_y - 1, pltpu.roll(value, LANES - 1, 1), after),
            ],
            axis=0,
        )
        left = []
        for a in range(3):
            first = pltpu.roll(tiles[0], -a * size_y % LANES, 1)
            second = pltpu.roll(tiles[1], (area - a * size_y) % LANES, 1)
            left.append(jnp.where(lane < area, first, jnp.where(lane < 2 * area, second, 0.0)))
        edges.append(
            lax.dot_general(
                jnp.concatenate(left, axis=0).astype(BF16),
                right.astype(BF16),
                (((1,), (1,)), ((), ())),
                preferred_element_type=F32,
            )
        )
    count = part_ref.shape[0]
    height, width = chunks.shape[0] // count, LANES
    pieces = rows * acc_ref.shape[1] // width
    for k in range(9 * pieces, part_ref.shape[2] // LANES * QUAD):
        chunks[pl.ds(k, count, stride=height), :] = jnp.zeros((count, width), F32)
    for a in range(3):
        for c in range(3):
            at = 3 * a + c
            block = acc_ref[at * channels : (at + 1) * channels, :]
            if c != 1:
                block = block + edges[c // 2][a * channels : (a + 1) * channels]
            block = block * scale
            line = jnp.concatenate(
                [block[r * count : (r + 1) * count] for r in range(rows)], axis=1
            )
            for k in range(pieces):
                chunks[pl.ds(at * pieces + k, count, stride=height), :] = line[
                    :, k * width : (k + 1) * width
                ]

    def write(at, quads):
        part_ref[:, :, at] = quads.astype(BF16)

    whole = chunks[...].reshape(count, height, width)
    to_quads(whole[:, : part_ref.shape[2] // LANES * QUAD], write)


def finish(acc, columns, sent, received, scale, rows, sizes, part_shape):
    channels = columns.shape[0]
    return pl.pallas_call(
        functools.partial(finish_kernel, scale, rows, sizes),
        in_specs=[VMEM] * 6,
        out_specs=VMEM,
        out_shape=jax.ShapeDtypeStruct(part_shape, BF16),
        scratch_shapes=[
            pltpu.VMEM((part_shape[0] * -(-part_shape[2] // LANES * QUAD // 8) * 8, LANES), F32),
        ],
        compiler_params=params(),
        cost_estimate=cost(2**27, 2**21),
        name="finish",
    )(acc, columns, *sent, *received)


def adam_step(master, first, second, weight_grad):
    new_first = 0.9 * first + 0.1 * weight_grad
    new_second = 0.999 * second + 0.001 * weight_grad * weight_grad
    corr_first = 1.0 - (0.9**10) ** 10
    corr_second = 1.0 - (0.999**10) ** 10
    update = new_first / corr_first / (jnp.sqrt(new_second / corr_second) + 1e-08) + 0.01 * master
    return master - 0.05 * update, new_first, new_second


def in_flat_order(value, rows, places, spread_rows):
    taps = 27
    lane = lax.broadcasted_iota(jnp.int32, (9, LANES), 1)
    for k in range(value.shape[1] // LANES):
        rows[k * QUAD : (k + 1) * QUAD, :] = value[:, k * LANES : (k + 1) * LANES]
    thirds = [rows[pl.ds(k, 9, stride=3), :] for k in range(3)]
    half = LANES // 2
    by_y = (
        jnp.where(lane < half, thirds[0], thirds[1]),
        jnp.where(lane < half, pltpu.roll(thirds[0], half, 1), pltpu.roll(thirds[2], half, 1)),
        jnp.where(lane < half, thirds[1], thirds[2]),
    )
    places[...] = jnp.zeros_like(places)
    for b in range(3):
        spread_rows[b, :9, :] = by_y[b]
        for block in range(9):
            tap = (2 - block // 3) * 9 + b * 3 + 2 - block % 3
            places[tap : tap + 1, :] = spread_rows[b, block : block + 1, :]
    line = places[...].T
    number = lax.broadcasted_iota(jnp.int32, (LANES, LANES), 0) * taps
    column = lax.broadcasted_iota(jnp.int32, (LANES, LANES), 1)
    turned = []
    for group in range(LANES // 8):
        piece = line[8 * group : 8 * (group + 1)]
        rest = 8 * group * taps % LANES
        for step in range(3):
            turn = rest // (3 - step)
            rest -= turn
            piece = pltpu.roll(piece, turn, 1, stride=taps // 3, stride_axis=0)
        turned.append(piece)
    line = jnp.concatenate(turned, axis=0)
    start = number & (LANES - 1)
    line = jnp.concatenate(
        [jnp.where(column >= start, line, 0.0), jnp.where(column < start, line, 0.0)], axis=0
    )
    target = lax.broadcasted_iota(jnp.int32, (32, 2 * LANES), 0)
    source = lax.broadcasted_iota(jnp.int32, (32, 2 * LANES), 1)
    goes = lax.shift_right_logical((source & (LANES - 1)) * taps, 7)
    goes = goes + jnp.where(source < LANES, 0, 1)
    pick = jnp.where(goes == target, 1.0, 0.0).astype(BF16)
    parts = []
    for _ in range(3):
        parts.append(line.astype(BF16))
        line = line - parts[-1].astype(F32)
    return jnp.dot(
        jnp.concatenate([pick] * 3, axis=1),
        jnp.concatenate(parts, axis=0),
        preferred_element_type=F32,
    )[:taps]


def adam_kernel(parts_ref, master_ref, first_ref, second_ref, *refs):
    out_refs, scratch = refs[:4], refs[4:]
    sums = [parts_ref[source].astype(F32) for source in range(parts_ref.shape[0])]
    while len(sums) > 1:
        sums = [sum(sums[k : k + 2][1:], sums[k]) for k in range(0, len(sums), 2)]
    weight_grad = in_flat_order(sums[0], *scratch)
    results = adam_step(master_ref[...], first_ref[...], second_ref[...], weight_grad)
    for out_ref, result in zip(out_refs, (weight_grad, *results)):
        out_ref[...] = result


def adam(parts, *states):
    share = states[0].shape[0]
    tiled = [state.reshape(share // LANES, LANES) for state in states]
    result = jax.ShapeDtypeStruct(tiled[0].shape, F32)
    outs = pl.pallas_call(
        adam_kernel,
        in_specs=[VMEM] * 4,
        out_specs=[VMEM] * 4,
        out_shape=[result] * 4,
        scratch_shapes=[
            pltpu.VMEM((32, LANES), F32),
            pltpu.VMEM((LANES, LANES), F32),
            pltpu.VMEM((3, 16, LANES), F32),
        ],
        compiler_params=params(),
        cost_estimate=cost(2**22, 2**19),
        name="adam",
    )(parts, *tiled)
    return tuple(out.reshape(share) for out in outs)


def spread_kernel(rows, w_ref, weights_ref, turned, chunks):
    count = w_ref.shape[0]
    height = chunks.shape[0] // count
    taps = 27 * rows * count
    quads = [
        w_ref[:, :, k * LANES : (k + 1) * LANES].astype(F32)
        for k in range(w_ref.shape[2] // LANES)
    ]
    spare = jnp.zeros((count, height - QUAD * len(quads), LANES), F32)
    chunks[...] = jnp.concatenate(quads + [spare], axis=1).reshape(chunks.shape)
    line = jnp.concatenate(
        [chunks[pl.ds(k, count, stride=height), :] for k in range(rows * taps // LANES)], axis=1
    )
    whole = jnp.concatenate([line[:, r * taps : (r + 1) * taps] for r in range(rows)], axis=0)
    spread_weights(whole, turned, weights_ref)


def spread(kernel, channels, rows):
    return pl.pallas_call(
        functools.partial(spread_kernel, rows),
        in_specs=[VMEM],
        out_specs=VMEM,
        out_shape=jax.ShapeDtypeStruct((3, 2 * channels, 12 * channels), BF16),
        scratch_shapes=[
            flat_scratch(channels),
            pltpu.VMEM((kernel.shape[0] * 32, LANES), F32),
        ],
        compiler_params=params(),
        cost_estimate=cost(2**20, 2**21),
        name="spread",
    )(kernel)


def pair_dgrad_kernel(*refs):
    weights_ref, out_ref, g3, tile = refs[9:]
    _, size_x, size_y, size_z = out_ref.shape
    halo = pair_z_halo(refs[7], refs[8], size_x + 2, size_y, size_z)
    input_products(refs, halo, g3, weights_ref, tile, out_ref)


def pair_dgrad(sources, weights, shape):
    channels, _, size_y, size_z = shape
    return pl.pallas_call(
        pair_dgrad_kernel,
        in_specs=[VMEM] * 10,
        out_specs=VMEM,
        out_shape=jax.ShapeDtypeStruct(shape, BF16),
        scratch_shapes=[g3_scratch(*shape), pltpu.VMEM((2, channels * size_y, size_z), F32)],
        compiler_params=params(32 * 2**20),
        cost_estimate=dgrad_cost(*shape),
        name="dgrad",
    )(*sources, weights)


def pair_program(activations, preact, upstream, master, first_moment, second_moment, scale):
    shape = activations.shape
    channels, size_x, size_y, _ = shape
    devices = math.prod(lax.axis_size(a) for a in AXES)
    rows = channels // devices
    used = master.shape[0] // LANES
    block = (devices, QUAD, -(-used // QUAD) * LANES)
    first, last, odd_sent = faces(preact, upstream, "gx", rows)
    odd_halves = swapped(odd_sent, "gx", 1)
    inner, own, even_sent, sent = pair_inner(
        preact, upstream, first, last, master.reshape(used, LANES), block, rows
    )
    even_halves = swapped(even_sent, "gx", 0)
    kernel = lax.all_to_all(sent, AXES, 0, 0, tiled=True)
    own, xlo, xhi = side((odd_halves, even_halves), own)
    planes = (xlo, first, inner, last, xhi)
    own, activations = lax.optimization_barrier((own, activations))
    other = shifted(own, {"gy": "swap"})
    planes_x, columns = input_planes(activations, True)
    z_sent = join(own, other, columns, size_x * size_y)
    from_odd = swapped(z_sent[1], "gz", 1)
    from_even = swapped(z_sent[0], "gz", 0)
    sources = (*planes, other, other)
    acc = pair_wgrad(sources, planes_x, shape)
    z_received = (from_odd, from_even)
    part = finish(acc, columns, z_sent, z_received, scale, rows, (size_x, size_y), block)
    part, kernel = lax.optimization_barrier((part, kernel))
    parts = lax.all_to_all(part, AXES, 0, 0, tiled=True)
    weights = spread(kernel, channels, rows)
    grad_input = pair_dgrad((*sources, *z_received), weights, shape)
    return grad_input, *adam(parts, master, first_moment, second_moment)


def yface_kernel(*refs):
    low_ref, high_ref = refs[5:]
    size_z = low_ref.shape[-1]
    for index in range(low_ref.shape[0]):
        body = body_of(refs[:5], index)
        plane = body.shape[-1]
        low_ref[index] = body[:, :size_z]
        high_ref[index] = body[:, plane - size_z :]


def y_faces(planes, size_z):
    inner, channels, _ = planes[2].shape
    face = jax.ShapeDtypeStruct((inner + 4, channels, size_z), BF16)
    return pl.pallas_call(
        yface_kernel,
        in_specs=[VMEM] * 5,
        out_specs=[VMEM] * 2,
        out_shape=[face] * 2,
        compiler_params=params(),
        cost_estimate=cost(0, 2**19),
        name="yfaces",
    )(*planes)


def zface_kernel(*refs):
    zlo_ref, zhi_ref = refs[7:]
    size_z = refs[5].shape[-1]
    whole = []
    for index in range(refs[5].shape[0]):
        low, high = y_halo(refs[5:7], index)
        body = body_of(refs[:5], index)[...]
        whole.append(jnp.concatenate([low.astype(BF16), body, high.astype(BF16)], axis=1))
    low, high = z_tiles(whole, whole[0].shape[1] // size_z, size_z, range(len(whole)))
    zlo_ref[...] = low.astype(BF16)
    zhi_ref[...] = high.astype(BF16)


def z_faces(planes, y_halos):
    face = jax.ShapeDtypeStruct((planes[0].shape[0], LANES), BF16)
    return pl.pallas_call(
        zface_kernel,
        in_specs=[VMEM] * 7,
        out_specs=[VMEM] * 2,
        out_shape=[face, face],
        compiler_params=params(),
        cost_estimate=cost(2**27, 2**21),
        name="zfaces",
    )(*planes, *y_halos)


def wgrad_kernel(scale, *refs):
    x_ref, part_ref, g3, x3, acc, flat = refs[9:]
    size_x, channels, plane = x_ref.shape
    size_z = refs[5].shape[-1]
    halo = z_halo(refs[7], refs[8], size_x + 2, plane // size_z + 2, size_z)
    weight_products(refs, halo, x_ref, g3, x3, acc)
    whole = to_flat(acc[...] * scale, channels, channels, flat)
    part_ref[...] = whole[:, : part_ref.shape[1]].astype(BF16)


def wgrad(sources, planes_x, shape, scale):
    channels = shape[0]
    return pl.pallas_call(
        functools.partial(wgrad_kernel, scale),
        in_specs=[VMEM] * 10,
        out_specs=VMEM,
        out_shape=jax.ShapeDtypeStruct((channels, 27 * channels), BF16),
        scratch_shapes=[
            g3_scratch(*shape),
            x3_scratch(*shape),
            acc_scratch(channels),
            flat_scratch(channels),
        ],
        compiler_params=params(32 * 2**20),
        cost_estimate=wgrad_cost(*shape),
        name="wgrad",
    )(*sources, planes_x)


def dgrad_kernel(*refs):
    w_ref, out_ref, g3, turned, weights, tile = refs[9:]
    _, size_x, size_y, size_z = out_ref.shape
    spread_weights(w_ref[...].astype(F32), turned, weights)
    halo = z_halo(refs[7], refs[8], size_x + 2, size_y + 2, size_z)
    input_products(refs, halo, g3, weights, tile, out_ref)


def dgrad(sources, kernel, shape):
    return pl.pallas_call(
        dgrad_kernel,
        in_specs=[VMEM] * 10,
        out_specs=VMEM,
        out_shape=jax.ShapeDtypeStruct(shape, BF16),
        scratch_shapes=dgrad_scratch(*shape),
        compiler_params=params(32 * 2**20),
        cost_estimate=dgrad_cost(*shape),
        name="dgrad",
    )(*sources, kernel)


def general_program(activations, preact, upstream, master, first_moment, second_moment, scale):
    shape = activations.shape
    channels, _, _, size_z = shape
    devices = math.prod(lax.axis_size(a) for a in AXES)
    share = master.shape[0]
    first, last = faces(preact, upstream)
    x_halos = (shifted(last, {"gx": 1}), shifted(first, {"gx": -1}))
    inner = inner_planes(preact, upstream)
    (planes_x,) = input_planes(activations, False)
    sent = jnp.broadcast_to(master.astype(BF16).reshape(1, 1, share), (devices, 1, share))
    kernel = lax.all_to_all(sent, AXES, 0, 0, tiled=True).reshape(channels, 27 * channels)
    planes = (x_halos[0], first, inner, last, x_halos[1])
    y_sent = y_faces(planes, size_z)
    y_halos = (shifted(y_sent[1], {"gy": 1}), shifted(y_sent[0], {"gy": -1}))
    zlo, zhi = z_faces(planes, y_halos)
    z_halos = (shifted(zhi, {"gz": 1}), shifted(zlo, {"gz": -1}))
    sources = (*planes, *y_halos, *z_halos)
    part = wgrad(sources, planes_x, shape, scale)
    part, kernel = lax.optimization_barrier((part, kernel))
    parts = lax.all_to_all(part.reshape(devices, 1, share), AXES, 0, 0, tiled=True)
    grad_input = dgrad(sources, kernel, shape)
    weight_grad = jnp.sum(parts.astype(F32), axis=0).reshape(-1)
    results = adam_step(master, first_moment, second_moment, weight_grad)
    return grad_input, weight_grad, *results


def shifted(value, moves):
    names = tuple(moves)
    sizes = [lax.axis_size(name) for name in names]
    pairs = []
    for source in range(math.prod(sizes)):
        rest, coords = source, []
        for size in reversed(sizes):
            coords.insert(0, rest % size)
            rest //= size
        coords = [
            (at + moves[name]) if moves[name] != "swap" else 1 - at
            for at, name in zip(coords, names)
        ]
        if all(0 <= at < size for at, size in zip(coords, sizes)):
            target = 0
            for at, size in zip(coords, sizes):
                target = target * size + at
            pairs.append((source, target))
    return lax.ppermute(value, names if len(names) > 1 else names[0], pairs)


def swapped(value, axis, start):
    pairs = []
    for low in range(start, lax.axis_size(axis) - 1, 2):
        pairs += [(low, low + 1), (low + 1, low)]
    return lax.ppermute(value, axis, pairs)


def local(activations, preact, upstream, master, first_moment, second_moment):
    channels, size_x, size_y, size_z = activations.shape
    devices = math.prod(lax.axis_size(a) for a in AXES)
    share = master.shape[0]
    scale = 1.0 / math.sqrt(size_x * size_y * size_z * devices)
    in_pairs = (
        lax.axis_size("gy") == 2
        and channels % devices == 0
        and share % LANES == 0
        and channels // devices * channels == LANES
        and 2 * size_x * size_y <= LANES
        and (size_x + 2) * size_y <= LANES
    )
    program = pair_program if in_pairs else general_program
    return program(
        activations, preact, upstream, master, first_moment, second_moment, scale
    )


def solution(mesh):
    volume = P(None, "gx", "gy", "gz")
    flat = P(AXES)
    return jax.shard_map(
        local,
        mesh=mesh,
        in_specs=(volume, volume, volume, flat, flat, flat),
        out_specs=(volume, flat, flat, flat, flat),
        check_vma=False,
    )
```
